32 devices in a mesh: seq: 4 (over x, core), blk: 8 (over z, y).
Axes of the slice: x: 2, y: 2, z: 4, core: 2. Of those that a mesh axis runs over, the one named last changes fastest.
Arguments:
- tokens: bfloat16 [4, 128, 16, 1152], P('seq', 'blk'), may hold values from -6 to 6
- segments: int32 [4, 16], P('seq'), may hold values from 0 to 1, never falling along the last dimension, each value on 1 to 9 neighbouring positions
- timesteps: int32 [4, 2], P('seq'), may hold values from 0 to 999
- caption: bfloat16 [4, 2, 120, 4096], P('seq'), may hold values from -6 to 6
- cotangent: bfloat16 [4, 128, 16, 1152], P('seq', 'blk'), may hold values from -6 to 6
- ada_weight: bfloat16 [1152, 10368], P(None, 'blk'), may hold values from -0.1875 to 0.1875
- ada_bias: bfloat16 [10368], P('blk'), may hold values from -3 to 3
- spatial_in: bfloat16 [1152, 3456], P(('seq', 'blk')), may hold values from -0.1875 to 0.1875
- spatial_out: bfloat16 [1152, 1152], P(('seq', 'blk')), may hold values from -1 to 1
- temporal_in: bfloat16 [1152, 3456], P(('seq', 'blk')), may hold values from -0.1875 to 0.1875
- temporal_out: bfloat16 [1152, 1152], P(('seq', 'blk')), may hold values from -0.5 to 0.5
- cross_gain: bfloat16 [1152], P(('seq', 'blk')), may hold values from 0.25 to 1.75
- cross_query: bfloat16 [1152, 1152], P(('seq', 'blk')), may hold values from -0.1875 to 0.1875
- caption_proj: bfloat16 [4096, 2304], P(None, 'blk'), may hold values from -0.09375 to 0.09375
- cross_out: bfloat16 [1152, 1152], P(('seq', 'blk')), may hold values from -1.25 to 1.25
- hidden_in: bfloat16 [1152, 4608], P(('seq', 'blk')), may hold values from -0.1875 to 0.1875
- hidden_out: bfloat16 [4608, 1152], P(('seq', 'blk')), may hold values from -0.09375 to 0.09375
Outputs:
- out: bfloat16 [4, 128, 16, 1152], P('seq', 'blk')
- grad_tokens: bfloat16 [4, 128, 16, 1152], P('seq', 'blk')
- grad_ada_weight: float32 [1152, 10368], P(None, 'blk')
- grad_ada_bias: float32 [10368], P('blk')
- grad_spatial_in: float32 [1152, 3456], P(('seq', 'blk'))
- grad_spatial_out: float32 [1152, 1152], P(('seq', 'blk'))
- grad_temporal_in: float32 [1152, 3456], P(('seq', 'blk'))
- grad_temporal_out: float32 [1152, 1152], P(('seq', 'blk'))
- grad_cross_gain: float32 [1152], P(('seq', 'blk'))
- grad_cross_query: float32 [1152, 1152], P(('seq', 'blk'))
- grad_caption_proj: float32 [4096, 2304], P(None, 'blk')
- grad_cross_out: float32 [1152, 1152], P(('seq', 'blk'))
- grad_hidden_in: float32 [1152, 4608], P(('seq', 'blk'))
- grad_hidden_out: float32 [4608, 1152], P(('seq', 'blk'))
The draws below stay inside these ranges and needn't reach their ends.
Inputs may be any that keep to these rules, and one draw needn't show every extreme that they name: `segments`: along the 16 frames of a pack the video number never falls; each of the 2 videos holds at least 7 and at most 9 frames.
All inputs are finite; a program needn't handle non-finite values.
Results may differ from the reference program's by a relative error of at most 0.035.
Values may be sent and summed in bfloat16 or wider, within the bound.
A program may use at most 384 MiB of HBM per device.

```python
import math
import jax
import jax.numpy as jnp
import numpy as np
from jax import lax

D = 1152
H = 16
E = 72
FF = 4608
TD = 4096
L = 120
FRAMES = 16
SEGS = 2
MOST = 9
PATCHES = 128
N_SEQ = 4


def place_ends(entries, key, smallest, high):
    place = [jax.random.randint(jax.random.fold_in(key, axis), (), 0, length) for axis, length in enumerate(entries.shape)]
    widest = entries.shape.index(max(entries.shape))
    beside = place[:widest] + [(place[widest] + 1) % entries.shape[widest]] + place[widest + 1:]
    return entries.at[tuple(place)].set(smallest).at[tuple(beside)].set(high)


def levels(key, shape, shards, least, largest):
    gain = 1.0
    for axis_at, shards_of in shards:
        heights = jax.random.uniform(jax.random.fold_in(jax.random.fold_in(key, 6), axis_at), (shards_of,), jnp.float32, least / len(shards), largest / len(shards))
        gain = gain * jnp.repeat(jnp.exp(heights), shape[axis_at] // shards_of).reshape((-1,) + (1,) * (len(shape) - 1 - axis_at))
    return gain


def length_profile(count, total, bound, skew):
    weights = [(1 << 20) // math.isqrt(rank ** skew) + 1 for rank in range(2, count + 1)]
    rest, holding = total - bound - (count - 1), [1] * (count - 1)
    while rest > 0:
        movable = [i for i in range(count - 1) if holding[i] < bound]
        pool, remaining = sum([weights[i] for i in movable]), rest
        for i in movable:
            extra = min(bound - holding[i], max(1, remaining * weights[i] // pool), rest)
            holding[i] = holding[i] + extra
            rest = rest - extra
    return np.array([bound] + holding)


def ragged_sizes(own_key, number_of, total, limit, slope):
    if number_of == 2:
        one = jax.random.randint(own_key, (), max(1, total - limit), min(limit, total - 1) + 1)
        return jnp.stack([one, total - one])
    sizes = jnp.asarray(length_profile(number_of, total, limit, slope), jnp.int32)
    pairs = (number_of - 1) // 2
    source_of, receiver = sizes[1:1 + 2 * pairs:2], sizes[2:2 + 2 * pairs:2]
    slack = jnp.minimum(source_of - 1, limit - receiver)
    passed = jax.random.randint(jax.random.fold_in(own_key, 1), (pairs,), 0, 1 << 20) % (slack + 1)
    sizes = sizes.at[1:1 + 2 * pairs:2].set(source_of - passed).at[2:2 + 2 * pairs:2].set(receiver + passed)
    return sizes[jax.random.permutation(jax.random.fold_in(own_key, 2), number_of)]


def scatter_about(key, extent, width, limit, split=(), kind=jnp.bfloat16):
    values = jax.random.normal(key, extent, jnp.float32) * width
    if len(split) > 0:
        values = levels(key, extent, split, -0.22, 0.18) * values
    return jnp.clip(values, min=-limit, max=limit).astype(kind)


def setup_inputs(seed: int = 0) -> dict:
    key_list = jax.random.split(jax.random.key(seed), 18)
    return {
        "tokens": scatter_about(key_list[0], (N_SEQ, PATCHES, FRAMES, D), 1.0, 6.0, ((0, 4), (1, 8))),
        "segments": jax.vmap(lambda own: jnp.searchsorted(jnp.cumsum(ragged_sizes(own, SEGS, FRAMES, MOST, 0)), jnp.arange(FRAMES), side="right"))(jax.random.split(key_list[1], N_SEQ)).reshape((N_SEQ, FRAMES)).astype(jnp.int32),
        "timesteps": place_ends(jax.random.randint(key_list[2], (N_SEQ, SEGS), 0, 1000), jax.random.fold_in(key_list[2], 1), 0, 999).astype(jnp.int32),
        "caption": scatter_about(key_list[3], (N_SEQ, SEGS, L, TD), 1.0, 6.0, ((0, 4),)),
        "cotangent": scatter_about(key_list[4], (N_SEQ, PATCHES, FRAMES, D), 1.0, 6.0, ((0, 4), (1, 8))),
        "ada_weight": scatter_about(key_list[5], (D, 9 * D), D ** -0.5, 0.1875, ((1, 8),)),
        "ada_bias": scatter_about(key_list[6], (9 * D,), 0.5, 3.0, ((0, 8),)),
        "spatial_in": scatter_about(key_list[7], (D, 3 * D), D ** -0.5, 0.1875, ((0, 32),)),
        "spatial_out": scatter_about(key_list[8], (D, D), (4 * D // PATCHES) ** -0.5, 1.0, ((0, 32),)),
        "temporal_in": scatter_about(key_list[9], (D, 3 * D), D ** -0.5, 0.1875, ((0, 32),)),
        "temporal_out": scatter_about(key_list[10], (D, D), (D // 8) ** -0.5, 0.5, ((0, 32),)),
        "cross_gain": jnp.clip(1.0 + 0.15 * jax.random.normal(key_list[11], (D,), jnp.float32), 0.25, 1.75).astype(jnp.bfloat16),
        "cross_query": scatter_about(key_list[12], (D, D), D ** -0.5, 0.1875, ((0, 32),)),
        "caption_proj": scatter_about(key_list[13], (TD, 2 * D), TD ** -0.5, 0.09375, ((1, 8),)),
        "cross_out": scatter_about(key_list[14], (D, D), (2 * D // L) ** -0.5, 1.25, ((0, 32),)),
        "hidden_in": scatter_about(key_list[15], (D, FF), D ** -0.5, 0.1875, ((0, 32),)),
        "hidden_out": scatter_about(key_list[16], (FF, D), FF ** -0.5, 0.09375, ((0, 32),)),
    }


@jax.custom_vjp
def low(v):
    return lax.optimization_barrier(v.astype(jnp.bfloat16)).astype(jnp.float32)

@jax.custom_vjp
def low_back(v):
    return v

def low_keep(v):
    return (low(v), None)

def low_pass(kept, grad):
    return (grad,)

def back_keep(v):
    return (v, None)

def back_low(kept, grad):
    return (low(grad),)
low.defvjp(low_keep, low_pass)
low_back.defvjp(back_keep, back_low)
HIGHEST = lax.Precision.HIGHEST
EPSILON = 1e-06
MASKED = -1e+30

def matmul(left, right):
    return jnp.dot(left, right, precision=HIGHEST)

def normalize(values):
    center = values - lax.optimization_barrier(jnp.mean(values, axis=-1, keepdims=True))
    return center * lax.rsqrt(lax.optimization_barrier(jnp.mean(center * center, axis=-1, keepdims=True)) + EPSILON)

def softmax_rows(scores):
    shifted = jnp.exp(scores - lax.optimization_barrier(jnp.max(scores, axis=-1, keepdims=True)))
    return shifted / lax.optimization_barrier(jnp.sum(shifted, axis=-1, keepdims=True))

def time_embedding(step_ids, model_width):
    half_width = model_width // 2
    frequency = jnp.exp(-math.log(10000.0) * jnp.arange(half_width).astype(jnp.float32) / half_width)
    angles = step_ids.astype(jnp.float32)[:, None] * frequency[None, :]
    return jnp.concatenate([jnp.cos(angles), jnp.sin(angles)], axis=1)

def spatial_frame(parts):
    query_f, key_f, value_f = parts
    scores = low_back(jnp.einsum('phe,qhe->hpq', query_f, key_f, precision=HIGHEST) * E ** (-0.5))
    weights = softmax_rows(scores)
    return jnp.einsum('hpq,qhe->phe', low(weights), value_f, precision=HIGHEST)

def video_block(tokens, frame_seg, step_ids, caption, ada_weight, ada_bias, spatial_in, spatial_out, temporal_in, temporal_out, cross_gain, cross_query, caption_proj, cross_out, hidden_in, hidden_out):
    patches, frames, model_width = tokens.shape
    token_rows = patches * frames
    score_scale = E ** (-0.5)
    conditioning = low(jax.nn.silu(time_embedding(step_ids, model_width)))
    modulation = low_back(low(matmul(conditioning, ada_weight) + ada_bias))
    choose = (frame_seg[:, None] == jnp.arange(SEGS, dtype=jnp.int32)[None, :]).astype(jnp.float32)
    frame_mod = matmul(choose, modulation)
    pieces = [frame_mod[:, index * model_width:(index + 1) * model_width] for index in range(9)]
    shift_one, scale_one, gate_one, shift_two, scale_two, gate_two, shift_three, scale_three, gate_three = pieces
    spatial_input = low(normalize(tokens) * (1.0 + scale_one) + shift_one)
    spatial_qkv = low_back(low(matmul(spatial_input.reshape(token_rows, model_width), spatial_in)))
    spatial_qkv = spatial_qkv.reshape(patches, frames, 3, H, E).transpose(1, 0, 2, 3, 4)
    spatial_attn = lax.map(jax.checkpoint(spatial_frame), (spatial_qkv[:, :, 0], spatial_qkv[:, :, 1], spatial_qkv[:, :, 2]))
    spatial_attn = low_back(low(spatial_attn.transpose(1, 0, 2, 3).reshape(token_rows, model_width)))
    branch_one = low_back(matmul(spatial_attn, spatial_out)).reshape(patches, frames, model_width)
    after_one = tokens + gate_one * branch_one
    temporal_input = low(normalize(after_one) * (1.0 + scale_two) + shift_two)
    temporal_qkv = low_back(low(matmul(temporal_input.reshape(token_rows, model_width), temporal_in)))
    temporal_qkv = temporal_qkv.reshape(patches, frames, 3, H, E)
    same_seg = frame_seg[:, None] == frame_seg[None, :]
    scores = low_back(jnp.einsum('pfhe,pghe->phfg', temporal_qkv[:, :, 0], temporal_qkv[:, :, 1], precision=HIGHEST) * score_scale)
    weights = softmax_rows(jnp.where(same_seg[None, None], scores, MASKED))
    temporal_attn = jnp.einsum('phfg,pghe->pfhe', low(weights), temporal_qkv[:, :, 2], precision=HIGHEST)
    temporal_attn = low_back(low(temporal_attn.reshape(token_rows, model_width)))
    branch_two = low_back(matmul(temporal_attn, temporal_out)).reshape(patches, frames, model_width)
    after_two = after_one + gate_two * branch_two
    cross_input = low(normalize(after_two) * cross_gain)
    cross_q = low_back(low(matmul(cross_input.reshape(token_rows, model_width), cross_query)))
    cross_q = cross_q.reshape(patches, frames, H, E).transpose(1, 0, 2, 3)
    text_keys = SEGS * L
    memory = low_back(low(matmul(caption.reshape(text_keys, TD), caption_proj))).reshape(text_keys, 2, H, E)
    key_seg = jnp.arange(text_keys, dtype=jnp.int32) // L
    allowed = frame_seg[:, None] == key_seg[None, :]

    def cross_frame(parts):
        query_f, allow_f = parts
        cross_scores = low_back(jnp.einsum('phe,khe->phk', query_f, memory[:, 0], precision=HIGHEST) * score_scale)
        cross_weights = softmax_rows(jnp.where(allow_f[None, None, :], cross_scores, MASKED))
        return jnp.einsum('phk,khe->phe', low(cross_weights), memory[:, 1], precision=HIGHEST)
    cross_attn = lax.map(jax.checkpoint(cross_frame), (cross_q, allowed))
    cross_attn = low_back(low(cross_attn.transpose(1, 0, 2, 3).reshape(token_rows, model_width)))
    branch_three = low_back(matmul(cross_attn, cross_out)).reshape(patches, frames, model_width)
    after_three = after_two + branch_three
    mlp_input = low(normalize(after_three) * (1.0 + scale_three) + shift_three)
    pre_act = low_back(matmul(mlp_input.reshape(token_rows, model_width), hidden_in))
    post_act = low(jax.nn.gelu(pre_act, approximate=True))
    branch_four = low_back(matmul(post_act, hidden_out)).reshape(patches, frames, model_width)
    return after_three + gate_three * branch_four

def reference(tokens, segments, timesteps, caption, cotangent, ada_weight, ada_bias, spatial_in, spatial_out, temporal_in, temporal_out, cross_gain, cross_query, caption_proj, cross_out, hidden_in, hidden_out):
    params = tuple((weight.astype(jnp.float32) for weight in (ada_weight, ada_bias, spatial_in, spatial_out, temporal_in, temporal_out, cross_gain, cross_query, caption_proj, cross_out, hidden_in, hidden_out)))

    def one_pack(totals, group):
        pack_tokens, pack_seg, pack_steps, pack_caption, pack_cot = group
        caption_f = pack_caption.astype(jnp.float32)

        def forward(inputs, *weight_list):
            return video_block(inputs, pack_seg, pack_steps, caption_f, *weight_list)
        result, pull = jax.vjp(forward, pack_tokens.astype(jnp.float32), *params)
        grads = pull(pack_cot.astype(jnp.float32))
        totals = tuple((total + grad for total, grad in zip(totals, grads[1:])))
        return (totals, (result.astype(jnp.bfloat16), grads[0].astype(jnp.bfloat16)))
    zeros = tuple((jnp.zeros(weight.shape, jnp.float32) for weight in params))
    totals, (outputs, grad_inputs) = lax.scan(one_pack, zeros, (tokens, segments, timesteps, caption, cotangent))
    return (outputs, grad_inputs) + totals
```

```python
import math

import jax
import jax.numpy as jnp
import numpy as np
from jax import lax
from jax.experimental import pallas as pl
from jax.experimental.pallas import tpu as pltpu
from jax.sharding import PartitionSpec as P

H = 16
E = 72


EPSILON = 1e-06
MASKED = -1e30


def to_low(values):
    return values.astype(jnp.bfloat16)


def linear(left, right):
    return jnp.dot(left, right, preferred_element_type=jnp.float32)


def left_product(left, right):
    return lax.dot_general(
        left, right, (((0,), (0,)), ((), ())), preferred_element_type=jnp.float32
    )


def right_product(left, right):
    return lax.dot_general(
        left, right, (((1,), (1,)), ((), ())), preferred_element_type=jnp.float32
    )


def normalize(values):
    center = values - jnp.mean(values, axis=-1, keepdims=True)
    return center * lax.rsqrt(jnp.mean(center * center, axis=-1, keepdims=True) + EPSILON)


def modulate(values, shift_rows, scale_rows):
    return normalize(values) * (1.0 + scale_rows) + shift_rows


def gain_norm(values, gain_row):
    return normalize(values) * gain_row


def gelu_tanh(values):
    return jax.nn.gelu(values, approximate=True)


def softmax_rows(scores):
    shifted = jnp.exp(scores - jnp.max(scores, axis=-1, keepdims=True))
    return shifted / jnp.sum(shifted, axis=-1, keepdims=True)


def softmax_with_total(scores):
    top = jnp.max(scores, axis=-1, keepdims=True)
    shifted = jnp.exp(scores - top)
    total = jnp.sum(shifted, axis=-1, keepdims=True)
    return (shifted / total, (top + jnp.log(total))[..., 0])


def softmax_back(probs, grad_probs):
    return probs * (grad_probs - jnp.sum(grad_probs * probs, axis=-1, keepdims=True))


def time_embedding(step_ids, model_width):
    half_width = model_width // 2
    frequency = jnp.exp(
        -math.log(10000.0) * jnp.arange(half_width).astype(jnp.float32) / half_width
    )
    angles = step_ids.astype(jnp.float32)[:, None] * frequency[None, :]
    return jnp.concatenate([jnp.cos(angles), jnp.sin(angles)], axis=1)


def general_shards(
    tokens,
    segments,
    timesteps,
    caption,
    cotangent,
    ada_weight,
    ada_bias,
    spatial_in,
    spatial_out,
    temporal_in,
    temporal_out,
    cross_gain,
    cross_query,
    caption_proj,
    cross_out,
    hidden_in,
    hidden_out,
):
    inputs = tokens[0].astype(jnp.float32)
    patch_dev, frames, model_width = inputs.shape
    token_rows = patch_dev * frames
    head_count = H
    head_size = E
    score_scale = E ** (-0.5)
    frame_seg = segments[0]
    step_ids = timesteps[0]
    seg_count, text_len, text_width = caption.shape[1:]
    text_keys = seg_count * text_len
    caption_rows = caption[0].reshape(text_keys, text_width)
    grad_out = cotangent[0].astype(jnp.float32)
    gathered = (
        lax.all_gather(spatial_in, ("seq", "blk"), axis=0, tiled=True),
        lax.all_gather(spatial_out, ("seq", "blk"), axis=0, tiled=True),
        lax.all_gather(temporal_in, ("seq", "blk"), axis=0, tiled=True),
        lax.all_gather(temporal_out, ("seq", "blk"), axis=0, tiled=True),
        lax.all_gather(cross_gain, ("seq", "blk"), axis=0, tiled=True),
        lax.all_gather(cross_query, ("seq", "blk"), axis=0, tiled=True),
        lax.all_gather(cross_out, ("seq", "blk"), axis=0, tiled=True),
        lax.all_gather(hidden_in, ("seq", "blk"), axis=0, tiled=True),
        lax.all_gather(hidden_out, ("seq", "blk"), axis=0, tiled=True),
    )
    (
        wide_sin,
        wide_sout,
        wide_tin,
        wide_tout,
        gain_low,
        wide_query,
        wide_cout,
        wide_hin,
        wide_hout,
    ) = gathered
    gain_row = gain_low.astype(jnp.float32)
    conditioning = to_low(jax.nn.silu(time_embedding(step_ids, model_width)))
    mod_part = to_low(linear(conditioning, ada_weight) + ada_bias.astype(jnp.float32))
    text_part = to_low(linear(caption_rows, caption_proj))
    modulation, memory = (
        lax.all_gather(mod_part, "blk", axis=1, tiled=True),
        lax.all_gather(text_part, "blk", axis=1, tiled=True),
    )
    choose = frame_seg[:, None] == jnp.arange(seg_count, dtype=jnp.int32)[None, :]
    frame_mod = linear(choose.astype(jnp.bfloat16), modulation)
    pieces = [frame_mod[:, index * model_width : (index + 1) * model_width] for index in range(9)]
    (
        shift_one,
        scale_one,
        gate_one,
        shift_two,
        scale_two,
        gate_two,
        shift_three,
        scale_three,
        gate_three,
    ) = pieces
    spatial_input = to_low(modulate(inputs, shift_one, scale_one)).reshape(token_rows, model_width)
    spatial_qkv = to_low(linear(spatial_input, wide_sin)).reshape(
        patch_dev, frames, 3 * model_width
    )
    query_s = spatial_qkv[..., :model_width].reshape(patch_dev, frames, head_count, head_size)
    local_kv = spatial_qkv[..., model_width:]
    whole_kv = lax.all_gather(local_kv, "blk", axis=0, tiled=True)

    def split_kv(both):
        count = both.shape[0]
        return (
            both[..., :model_width].reshape(count, frames, head_count, head_size),
            both[..., model_width:].reshape(count, frames, head_count, head_size),
        )

    def spatial_probs(key_all):
        scores = jnp.einsum("pfhe,qfhe->fhpq", query_s, key_all, preferred_element_type=jnp.float32)
        return softmax_with_total(scores * score_scale)

    key_s, value_s = split_kv(whole_kv)
    probs_s, log_total_s = spatial_probs(key_s)
    probs_s_low = to_low(probs_s)
    attn_s = to_low(
        jnp.einsum(
            "fhpq,qfhe->pfhe", probs_s_low, value_s, preferred_element_type=jnp.float32
        ).reshape(token_rows, model_width)
    )
    branch_s = linear(attn_s, wide_sout).reshape(patch_dev, frames, model_width)
    after_one = inputs + gate_one * branch_s
    temporal_input = to_low(modulate(after_one, shift_two, scale_two)).reshape(
        token_rows, model_width
    )
    temporal_qkv = to_low(linear(temporal_input, wide_tin)).reshape(
        patch_dev, frames, 3, head_count, head_size
    )
    query_t = temporal_qkv[:, :, 0]
    key_t = temporal_qkv[:, :, 1]
    value_t = temporal_qkv[:, :, 2]
    same_seg = frame_seg[:, None] == frame_seg[None, :]
    scores_t = (
        jnp.einsum("pfhe,pghe->phfg", query_t, key_t, preferred_element_type=jnp.float32)
        * score_scale
    )
    probs_t = softmax_rows(jnp.where(same_seg[None, None], scores_t, MASKED))
    probs_t_low = to_low(probs_t)
    attn_t = to_low(
        jnp.einsum(
            "phfg,pghe->pfhe", probs_t_low, value_t, preferred_element_type=jnp.float32
        ).reshape(token_rows, model_width)
    )
    branch_t = linear(attn_t, wide_tout).reshape(patch_dev, frames, model_width)
    after_two = after_one + gate_two * branch_t
    cross_input = to_low(gain_norm(after_two, gain_row)).reshape(token_rows, model_width)
    query_c = to_low(linear(cross_input, wide_query)).reshape(
        patch_dev, frames, head_count, head_size
    )
    key_c = memory[:, :model_width].reshape(text_keys, head_count, head_size)
    value_c = memory[:, model_width:].reshape(text_keys, head_count, head_size)
    key_seg = jnp.arange(text_keys, dtype=jnp.int32) // text_len
    allowed = frame_seg[:, None] == key_seg[None, :]
    scores_c = (
        jnp.einsum("pfhe,khe->pfhk", query_c, key_c, preferred_element_type=jnp.float32)
        * score_scale
    )
    probs_c = softmax_rows(jnp.where(allowed[None, :, None, :], scores_c, MASKED))
    probs_c_low = to_low(probs_c)
    attn_c = to_low(
        jnp.einsum(
            "pfhk,khe->pfhe", probs_c_low, value_c, preferred_element_type=jnp.float32
        ).reshape(token_rows, model_width)
    )
    branch_c = linear(attn_c, wide_cout).reshape(patch_dev, frames, model_width)
    after_three = after_two + branch_c
    mlp_input = to_low(modulate(after_three, shift_three, scale_three)).reshape(
        token_rows, model_width
    )
    pre_act = linear(mlp_input, wide_hin)
    post_act = to_low(gelu_tanh(pre_act))
    branch_m = linear(post_act, wide_hout).reshape(patch_dev, frames, model_width)
    result = after_three + gate_three * branch_m
    grad_gate_three = jnp.sum(grad_out * branch_m, axis=0)
    grad_four = to_low(grad_out * gate_three).reshape(token_rows, model_width)
    grad_hout = left_product(post_act, grad_four)
    grad_post = right_product(grad_four, wide_hout)
    gelu_pull = jax.vjp(gelu_tanh, pre_act)[1]
    grad_pre = to_low(gelu_pull(grad_post)[0])
    grad_hin = left_product(mlp_input, grad_pre)
    grad_mlp_in = right_product(grad_pre, wide_hin).reshape(patch_dev, frames, model_width)
    mlp_pull = jax.vjp(modulate, after_three, shift_three, scale_three)[1]
    back_three, grad_shift_three, grad_scale_three = mlp_pull(grad_mlp_in)
    grad_three = grad_out + back_three
    grad_cross_branch = to_low(grad_three).reshape(token_rows, model_width)
    grad_cout = left_product(attn_c, grad_cross_branch)
    grad_attn_c = to_low(right_product(grad_cross_branch, wide_cout)).reshape(
        patch_dev, frames, head_count, head_size
    )
    grad_probs_c = jnp.einsum(
        "pfhe,khe->pfhk", grad_attn_c, value_c, preferred_element_type=jnp.float32
    )
    grad_scores_c = to_low(softmax_back(probs_c, grad_probs_c))
    grad_query_c = to_low(
        jnp.einsum("pfhk,khe->pfhe", grad_scores_c, key_c, preferred_element_type=jnp.float32)
        * score_scale
    ).reshape(token_rows, model_width)
    grad_key_c = (
        jnp.einsum("pfhk,pfhe->khe", grad_scores_c, query_c, preferred_element_type=jnp.float32)
        * score_scale
    )
    grad_value_c = jnp.einsum(
        "pfhk,pfhe->khe", probs_c_low, grad_attn_c, preferred_element_type=jnp.float32
    )
    grad_memory = jnp.concatenate(
        [grad_key_c.reshape(text_keys, model_width), grad_value_c.reshape(text_keys, model_width)],
        axis=1,
    )
    grad_wquery = left_product(cross_input, grad_query_c)
    grad_cross_in = right_product(grad_query_c, wide_query).reshape(patch_dev, frames, model_width)
    cross_pull = jax.vjp(gain_norm, after_two, gain_row)[1]
    back_two, grad_gain = cross_pull(grad_cross_in)
    grad_two = grad_three + back_two
    grad_gate_two = jnp.sum(grad_two * branch_t, axis=0)
    grad_temporal_branch = to_low(grad_two * gate_two).reshape(token_rows, model_width)
    grad_tout = left_product(attn_t, grad_temporal_branch)
    grad_attn_t = to_low(right_product(grad_temporal_branch, wide_tout)).reshape(
        patch_dev, frames, head_count, head_size
    )
    grad_probs_t = jnp.einsum(
        "pfhe,pghe->phfg", grad_attn_t, value_t, preferred_element_type=jnp.float32
    )
    grad_scores_t = to_low(softmax_back(probs_t, grad_probs_t))
    grad_query_t = (
        jnp.einsum("phfg,pghe->pfhe", grad_scores_t, key_t, preferred_element_type=jnp.float32)
        * score_scale
    )
    grad_key_t = (
        jnp.einsum("phfg,pfhe->pghe", grad_scores_t, query_t, preferred_element_type=jnp.float32)
        * score_scale
    )
    grad_value_t = jnp.einsum(
        "phfg,pfhe->pghe", probs_t_low, grad_attn_t, preferred_element_type=jnp.float32
    )
    grad_qkv_t = to_low(jnp.stack([grad_query_t, grad_key_t, grad_value_t], axis=2)).reshape(
        token_rows, 3 * model_width
    )
    grad_tin = left_product(temporal_input, grad_qkv_t)
    grad_temporal_in = right_product(grad_qkv_t, wide_tin).reshape(patch_dev, frames, model_width)
    temporal_pull = jax.vjp(modulate, after_one, shift_two, scale_two)[1]
    back_one, grad_shift_two, grad_scale_two = temporal_pull(grad_temporal_in)
    grad_one = grad_two + back_one
    grad_gate_one = jnp.sum(grad_one * branch_s, axis=0)
    grad_spatial_branch = to_low(grad_one * gate_one).reshape(token_rows, model_width)
    grad_sout = left_product(attn_s, grad_spatial_branch)
    grad_attn_s = to_low(right_product(grad_spatial_branch, wide_sout)).reshape(
        patch_dev, frames, head_count, head_size
    )
    back_kv = lax.all_gather(local_kv, "blk", axis=0, tiled=True)
    back_key, back_value = split_kv(back_kv)
    back_probs = spatial_probs(back_key)[0]
    back_probs_low = to_low(back_probs)
    grad_probs_s = jnp.einsum(
        "pfhe,qfhe->fhpq", grad_attn_s, back_value, preferred_element_type=jnp.float32
    )
    row_delta = jnp.sum(grad_probs_s * back_probs, axis=-1, keepdims=True)
    grad_scores_s = to_low(back_probs * (grad_probs_s - row_delta))
    grad_query_s = (
        jnp.einsum("fhpq,qfhe->pfhe", grad_scores_s, back_key, preferred_element_type=jnp.float32)
        * score_scale
    )
    count = lax.axis_size("blk") * patch_dev
    grad_key = (
        jnp.einsum("fhpq,pfhe->qfhe", grad_scores_s, query_s, preferred_element_type=jnp.float32)
        * score_scale
    )
    grad_value = jnp.einsum(
        "fhpq,pfhe->qfhe", back_probs_low, grad_attn_s, preferred_element_type=jnp.float32
    )
    grad_kv = to_low(
        lax.psum_scatter(
            jnp.concatenate(
                [
                    grad_key.reshape(count, frames, model_width),
                    grad_value.reshape(count, frames, model_width),
                ],
                axis=2,
            ).astype(jnp.bfloat16),
            "blk",
            scatter_dimension=0,
            tiled=True,
        ).astype(jnp.float32)
    )
    grad_qkv_s = jnp.concatenate(
        [to_low(grad_query_s).reshape(patch_dev, frames, model_width), grad_kv], axis=2
    ).reshape(token_rows, 3 * model_width)
    grad_sin = left_product(spatial_input, grad_qkv_s)
    grad_spatial_in = right_product(grad_qkv_s, wide_sin).reshape(patch_dev, frames, model_width)
    spatial_pull = jax.vjp(modulate, inputs, shift_one, scale_one)[1]
    back_zero, grad_shift_one, grad_scale_one = spatial_pull(grad_spatial_in)
    grad_input = grad_one + back_zero
    grad_frame_mod = jnp.concatenate(
        [
            grad_shift_one,
            grad_scale_one,
            grad_gate_one,
            grad_shift_two,
            grad_scale_two,
            grad_gate_two,
            grad_shift_three,
            grad_scale_three,
            grad_gate_three,
        ],
        axis=1,
    )
    grad_mod_local = lax.dot_general(
        choose.astype(jnp.float32),
        grad_frame_mod,
        (((0,), (0,)), ((), ())),
        precision=lax.Precision.HIGHEST,
    )
    grad_mod_part, grad_memory_part = (
        lax.psum_scatter(
            grad_mod_local.astype(jnp.bfloat16), "blk", scatter_dimension=1, tiled=True
        ).astype(jnp.float32),
        lax.psum_scatter(
            grad_memory.astype(jnp.bfloat16), "blk", scatter_dimension=1, tiled=True
        ).astype(jnp.float32),
    )
    grad_mod_low = to_low(grad_mod_part)
    grad_ada_w = left_product(conditioning, grad_mod_low)
    grad_ada_b = jnp.sum(grad_mod_low.astype(jnp.float32), axis=0)
    grad_caption = left_product(caption_rows, to_low(grad_memory_part))
    grad_ada_w, grad_ada_b, grad_caption = (
        lax.psum(grad_ada_w.astype(jnp.bfloat16), "seq").astype(jnp.float32),
        lax.psum(grad_ada_b.astype(jnp.bfloat16), "seq").astype(jnp.float32),
        lax.psum(grad_caption.astype(jnp.bfloat16), "seq").astype(jnp.float32),
    )
    shares = (
        lax.psum_scatter(grad_sin, ("seq", "blk"), scatter_dimension=0, tiled=True),
        lax.psum_scatter(grad_sout, ("seq", "blk"), scatter_dimension=0, tiled=True),
        lax.psum_scatter(grad_tin, ("seq", "blk"), scatter_dimension=0, tiled=True),
        lax.psum_scatter(grad_tout, ("seq", "blk"), scatter_dimension=0, tiled=True),
        lax.psum_scatter(grad_gain, ("seq", "blk"), scatter_dimension=0, tiled=True),
        lax.psum_scatter(grad_wquery, ("seq", "blk"), scatter_dimension=0, tiled=True),
        lax.psum_scatter(grad_cout, ("seq", "blk"), scatter_dimension=0, tiled=True),
        lax.psum_scatter(grad_hin, ("seq", "blk"), scatter_dimension=0, tiled=True),
        lax.psum_scatter(grad_hout, ("seq", "blk"), scatter_dimension=0, tiled=True),
    )
    (
        share_sin,
        share_sout,
        share_tin,
        share_tout,
        share_gain,
        share_query,
        share_cout,
        share_hin,
        share_hout,
    ) = shares
    return (
        to_low(result)[None],
        to_low(grad_input)[None],
        grad_ada_w,
        grad_ada_b,
        share_sin,
        share_sout,
        share_tin,
        share_tout,
        share_gain,
        share_query,
        grad_caption,
        share_cout,
        share_hin,
        share_hout,
    )


MESH = pl.DeviceIdType.MESH
BLOCKS = 18
LINES = 8
SHARD = 36
LINE = 4 * SHARD
WINDOW = 48
WIDE = LINES * LINE
MIB = 2**20


def place():
    seq = lax.axis_index("seq")
    blk = lax.axis_index("blk")
    x, c = seq // 2, seq % 2
    z, y = blk // 2, blk % 2
    x1, y1 = x + (1 - 2 * x) * (1 - c), y + (1 - 2 * y) * c
    x2, y2 = x + (1 - 2 * x) * c, y + (1 - 2 * y) * (1 - c)
    return x, c, y, z, x1, y1, x2, y2


def device(x, c, y, z):
    return {"seq": x * 2 + c, "blk": z * 2 + y}


def line_of(c, x, y):
    return (c * 2 + x) * 2 + y


def remote(src, dst, send_sem, recv_sem, where):
    return pltpu.make_async_remote_copy(
        src_ref=src,
        dst_ref=dst,
        send_sem=send_sem,
        recv_sem=recv_sem,
        device_id=where,
        device_id_type=MESH,
    )


def greet(others):
    barrier = pltpu.get_barrier_semaphore()
    for other in others:
        pl.semaphore_signal(barrier, inc=1, device_id=other, device_id_type=MESH)
    pl.semaphore_wait(barrier, len(others))


def gather_kernel(src, wide, parts, lines, z_send, z_recv, l_send, l_recv, own_sem):
    x, c, y, z, x1, y1, x2, y2 = place()
    near = [device(x, c, y, (z + k) % 4) for k in (1, 2, 3)]
    first, second, twin = device(x1, c, y1, z), device(x2, c, y2, z), device(x, 1 - c, y, z)
    greet(near + [first, second, twin])
    mine, line1 = line_of(c, x, y), line_of(c, x1, y1)
    line2, line3 = line_of(c, x2, y2), line_of(c, 1 - x, 1 - y)
    other = [line_of(1 - c, x, y), line_of(1 - c, x2, y2), line_of(1 - c, x1, y1), line_of(1 - c, 1 - x, 1 - y)]

    def z_copy(t, k):
        return remote(src.at[t], parts.at[t, z], z_send.at[t, k - 1], z_recv.at[t, k - 1], near[k - 1])

    def z_wait(t, k):
        return remote(src.at[t], parts.at[t, (z + 4 - k) % 4], z_send.at[t, k - 1], z_recv.at[t, k - 1], near[k - 1])

    def own(t):
        return pltpu.make_async_copy(lines.at[t], wide.at[t, mine], own_sem.at[t])

    def out(t, to, line, place_at, where):
        return remote(to, wide.at[t, line], l_send.at[t, place_at], l_recv.at[t, place_at], where)

    def sends(t, index):
        line, where = (
            (mine, first),
            (mine, second),
            (mine, twin),
            (line1, second),
            (line1, twin),
            (line2, twin),
            (line3, twin),
        )[index]
        from_here = lines.at[t] if index < 3 else wide.at[t, line]
        return out(t, from_here, line, index, where)

    def arrives(t, line, place_at):
        return out(t, wide.at[t, line], line, place_at, first).wait_recv()

    def step(t, carry):
        @pl.when(t < BLOCKS)
        def _():
            for k in (1, 2, 3):
                z_copy(t, k).start()
            parts[t, z] = src[t]

        @pl.when((t >= 2) & (t < BLOCKS + 2))
        def _():
            b = t - 2
            for k in (1, 2, 3):
                z_wait(b, k).wait_recv()
            w0, w1, w2, w3 = [parts[b, k] for k in range(4)]
            lines[b, 0:32] = w0[0:32]
            lines[b, 32:48] = w0[32:48] + w1[0:16]
            lines[b, 48:64] = w1[16:32]
            lines[b, 64:80] = w1[32:48] + w2[0:16]
            lines[b, 80:96] = w2[16:32]
            lines[b, 96:112] = w2[32:48] + w3[0:16]
            lines[b, 112:144] = w3[16:48]
            for index in range(3):
                sends(b, index).start()
            own(b).start()

        @pl.when((t >= 3) & (t < BLOCKS + 3))
        def _():
            b = t - 3
            arrives(b, line1, 0)
            for index in (3, 4):
                sends(b, index).start()

        @pl.when(t >= 4)
        def _():
            b = t - 4
            arrives(b, line2, 1)
            sends(b, 5).start()
            arrives(b, line3, 3)
            sends(b, 6).start()

        return carry

    lax.fori_loop(0, BLOCKS + 4, step, 0)

    def finish(t, carry):
        for line, place_at in zip(other, (2, 4, 5, 6)):
            arrives(t, line, place_at)
        for k in (1, 2, 3):
            z_copy(t, k).wait_send()
        for index in range(7):
            sends(t, index).wait_send()
        own(t).wait()
        return carry

    lax.fori_loop(0, BLOCKS, finish, 0)


def gather_weights(src):
    return pl.pallas_call(
        gather_kernel,
        out_shape=jax.ShapeDtypeStruct((BLOCKS, LINES, LINE, WIDE), jnp.bfloat16),
        in_specs=[pl.BlockSpec(memory_space=pltpu.VMEM)],
        out_specs=pl.BlockSpec(memory_space=pl.ANY),
        scratch_shapes=[
            pltpu.VMEM((BLOCKS, 4, WINDOW, WIDE), jnp.bfloat16),
            pltpu.VMEM((BLOCKS, LINE, WIDE), jnp.bfloat16),
            pltpu.SemaphoreType.DMA((BLOCKS, 3)),
            pltpu.SemaphoreType.DMA((BLOCKS, 3)),
            pltpu.SemaphoreType.DMA((BLOCKS, 7)),
            pltpu.SemaphoreType.DMA((BLOCKS, 7)),
            pltpu.SemaphoreType.DMA((BLOCKS,)),
        ],
        compiler_params=pltpu.CompilerParams(
            collective_id=0, has_side_effects=True, vmem_limit_bytes=40 * MIB
        ),
        name="gather_weights",
    )(src)


def left_at(t):
    at = jnp.minimum(t, 4)
    for first in (8, 9, 10, 11, 14, 15):
        at = at + jnp.where(t >= first, 1, 0)
    return at


def right_at(t):
    return jnp.maximum(t - 3, 0)


def scatter_kernel(
    left, right, total,
    s0, r0, s1, r1, k1, s2, r2, k2, s3, r3, k3,
    s0_sem, r0_sem, s1_sem, r1_sem, s2_sem, r2_sem, s3_sem, r3_sem,
):
    x, c, y, z, x1, y1, x2, y2 = place()
    near = [device(x, c, y, (z + k) % 4) for k in (1, 2, 3)]
    first, second, twin = device(x1, c, y1, z), device(x2, c, y2, z), device(x, 1 - c, y, z)
    greet(near + [first, second, twin])

    def product(t, core, xl, yl):
        rows = pl.ds(pl.multiple_of(line_of(core, xl, yl) * LINE, 16), LINE)
        return jnp.dot(
            left[left_at(t), rows, :], right[right_at(t)], preferred_element_type=jnp.float32
        )

    order = [(1 - x, 1 - y), (x2, y2), (x1, y1), (x, y)]
    twin_order = [(1 - x, 1 - y), (x1, y1), (x2, y2), (x, y)]

    def copy0(t, l):
        return remote(s0.at[t % 2, l], r0.at[t % 4, l], s0_sem.at[t % 2, l], r0_sem.at[t % 4, l], twin)

    def copy1(t, l):
        return remote(s1.at[t % 2, l], r1.at[t % 4, l], s1_sem.at[t % 2, l], r1_sem.at[t % 4, l], second)

    def copy2(t):
        return remote(s2.at[t % 2], r2.at[t % 4], s2_sem.at[t % 2], r2_sem.at[t % 4], first)

    def copy3(t, k):
        part = pl.ds(pl.multiple_of(32 * ((z + k) % 4), 16), WINDOW)
        return remote(s3.at[t % 2, part], r3.at[t % 4, k - 1], s3_sem.at[t % 2, k - 1], r3_sem.at[t % 4, k - 1], near[k - 1])

    def wide(values):
        return values.astype(jnp.float32)

    def step(t, carry):
        @pl.when(t < BLOCKS)
        def _():
            for l, (xl, yl) in enumerate(twin_order):
                @pl.when(t >= 2)
                def _():
                    copy0(t - 2, l).wait_send()
                s0[t % 2, l] = product(t, 1 - c, xl, yl).astype(jnp.bfloat16)
                copy0(t, l).start()

        @pl.when((t >= 1) & (t < BLOCKS + 1))
        def _():
            b = t - 1
            for l, (xl, yl) in enumerate(order):
                copy0(b, l).wait_recv()
                value = product(b, c, xl, yl) + wide(r0[b % 4, l])
                if l < 2:
                    @pl.when(b >= 2)
                    def _():
                        copy1(b - 2, l).wait_send()
                    s1[b % 2, l] = value.astype(jnp.bfloat16)
                    copy1(b, l).start()
                else:
                    k1[b % 2, l - 2] = value

        @pl.when((t >= 2) & (t < BLOCKS + 2))
        def _():
            b = t - 2
            copy1(b, 0).wait_recv()

            @pl.when(b >= 2)
            def _():
                copy2(b - 2).wait_send()
            s2[b % 2] = (k1[b % 2, 0] + wide(r1[b % 4, 0])).astype(jnp.bfloat16)
            copy2(b).start()
            copy1(b, 1).wait_recv()
            k2[b % 2] = k1[b % 2, 1] + wide(r1[b % 4, 1])

        @pl.when((t >= 3) & (t < BLOCKS + 3))
        def _():
            b = t - 3
            copy2(b).wait_recv()

            @pl.when(b >= 2)
            def _():
                for k in (1, 2, 3):
                    copy3(b - 2, k).wait_send()
            value = k2[b % 2] + wide(r2[b % 4])
            k3[b % 2] = value
            s3[b % 2] = value.astype(jnp.bfloat16)
            for k in (1, 2, 3):
                copy3(b, k).start()

        @pl.when(t >= 4)
        def _():
            b = t - 4
            value = k3[b % 2, pl.ds(pl.multiple_of(32 * z, 16), WINDOW)]
            for k in (1, 2, 3):
                copy3(b, k).wait_recv()
                value = value + wide(r3[b % 4, k - 1])
            total[b] = value

        return carry

    lax.fori_loop(0, BLOCKS + 4, step, 0)
    for b in (BLOCKS - 2, BLOCKS - 1):
        for l in range(4):
            copy0(b, l).wait_send()
        for l in range(2):
            copy1(b, l).wait_send()
        copy2(b).wait_send()
        for k in (1, 2, 3):
            copy3(b, k).wait_send()


def scatter_weights(left, right):
    low, full = jnp.bfloat16, jnp.float32
    return pl.pallas_call(
        scatter_kernel,
        out_shape=jax.ShapeDtypeStruct((BLOCKS, WINDOW, WIDE), full),
        in_specs=[pl.BlockSpec(memory_space=pltpu.VMEM)] * 2,
        out_specs=pl.BlockSpec(memory_space=pltpu.VMEM),
        scratch_shapes=[
            pltpu.VMEM((2, 4, LINE, WIDE), low),
            pltpu.VMEM((4, 4, LINE, WIDE), low),
            pltpu.VMEM((2, 2, LINE, WIDE), low),
            pltpu.VMEM((4, 2, LINE, WIDE), low),
            pltpu.VMEM((2, 2, LINE, WIDE), full),
            pltpu.VMEM((2, LINE, WIDE), low),
            pltpu.VMEM((4, LINE, WIDE), low),
            pltpu.VMEM((2, LINE, WIDE), full),
            pltpu.VMEM((2, LINE, WIDE), low),
            pltpu.VMEM((4, 3, WINDOW, WIDE), low),
            pltpu.VMEM((2, LINE, WIDE), full),
            pltpu.SemaphoreType.DMA((2, 4)),
            pltpu.SemaphoreType.DMA((4, 4)),
            pltpu.SemaphoreType.DMA((2, 2)),
            pltpu.SemaphoreType.DMA((4, 2)),
            pltpu.SemaphoreType.DMA((2,)),
            pltpu.SemaphoreType.DMA((4,)),
            pltpu.SemaphoreType.DMA((2, 3)),
            pltpu.SemaphoreType.DMA((4, 3)),
        ],
        compiler_params=pltpu.CompilerParams(
            collective_id=1, has_side_effects=True, vmem_limit_bytes=60 * MIB
        ),
        name="scatter_weights",
    )(left, right)


ORDER = (
    np.arange(WIDE).reshape(2, 2, 4, 2, SHARD).transpose(1, 0, 3, 2, 4).reshape(-1)
)


def hidden_order(values):
    rows = values.shape[0]
    cut = values.reshape(rows, 2, 2, 4, 2, 4, SHARD)
    return cut.transpose(0, 5, 2, 1, 4, 3, 6).reshape(rows, 4 * WIDE)


def hidden_back(values):
    rows = values.shape[0]
    cut = values.reshape(rows, 4, 2, 2, 2, 4, SHARD)
    return cut.transpose(0, 3, 2, 5, 4, 1, 6).reshape(rows, 4 * WIDE)


def by_block(values):
    rows = values.shape[0]
    return values.reshape(rows, -1, WIDE).transpose(1, 0, 2)


def shards(
    tokens,
    segments,
    timesteps,
    caption,
    cotangent,
    ada_weight,
    ada_bias,
    spatial_in,
    spatial_out,
    temporal_in,
    temporal_out,
    cross_gain,
    cross_query,
    caption_proj,
    cross_out,
    hidden_in,
    hidden_out,
):
    inputs = tokens[0].astype(jnp.float32)
    patch_dev, frames, model_width = inputs.shape
    token_rows = patch_dev * frames
    head_count = H
    head_size = E
    score_scale = E ** (-0.5)
    frame_seg = segments[0]
    step_ids = timesteps[0]
    seg_count, text_len, text_width = caption.shape[1:]
    text_keys = seg_count * text_len
    caption_rows = caption[0].reshape(text_keys, text_width)
    grad_out = cotangent[0].astype(jnp.float32)
    zplace = lax.axis_index("blk") // 2
    stack = jnp.concatenate(
        [
            by_block(spatial_in),
            spatial_out[None],
            by_block(temporal_in),
            temporal_out[None],
            cross_query[None],
            cross_out[None],
            by_block(hidden_order(hidden_in)),
            hidden_out.reshape(4, SHARD, WIDE),
        ]
    )
    windows = lax.dynamic_update_slice(
        jnp.zeros((BLOCKS, WINDOW, WIDE), jnp.bfloat16), stack, (0, 4 * zplace, 0)
    )
    weight = gather_weights(windows).reshape(BLOCKS, WIDE, WIDE)
    turn = (jnp.arange(WIDE)[:, None] == ORDER[None, :]).astype(jnp.bfloat16)

    def turned(values):
        return to_low(linear(values, turn))

    def turned_back(values):
        return to_low(right_product(values, turn))

    def forth(values, first, count):
        return jnp.concatenate(
            [linear(values, weight[first + k]) for k in range(count)], axis=1
        )

    def back(values, first, count):
        return sum(
            right_product(values[:, k * WIDE : (k + 1) * WIDE], weight[first + k])
            for k in range(count)
        )

    gain_low = lax.all_gather(cross_gain, ("seq", "blk"), axis=0, tiled=True)
    gain_row = gain_low.astype(jnp.float32)
    conditioning = to_low(jax.nn.silu(time_embedding(step_ids, model_width)))
    mod_part = to_low(linear(conditioning, ada_weight) + ada_bias.astype(jnp.float32))
    text_part = to_low(linear(caption_rows, caption_proj))
    modulation, memory = (
        lax.all_gather(mod_part, "blk", axis=1, tiled=True),
        lax.all_gather(text_part, "blk", axis=1, tiled=True),
    )
    choose = frame_seg[:, None] == jnp.arange(seg_count, dtype=jnp.int32)[None, :]
    frame_mod = linear(choose.astype(jnp.bfloat16), modulation)
    pieces = [frame_mod[:, index * model_width : (index + 1) * model_width] for index in range(9)]
    (
        shift_one,
        scale_one,
        gate_one,
        shift_two,
        scale_two,
        gate_two,
        shift_three,
        scale_three,
        gate_three,
    ) = pieces
    spatial_input = turned(
        to_low(modulate(inputs, shift_one, scale_one)).reshape(token_rows, model_width)
    )
    spatial_qkv = to_low(forth(spatial_input, 0, 3)).reshape(patch_dev, frames, 3 * model_width)
    query_s = spatial_qkv[..., :model_width].reshape(patch_dev, frames, head_count, head_size)
    local_kv = spatial_qkv[..., model_width:]
    whole_kv = lax.all_gather(local_kv, "blk", axis=0, tiled=True)

    def split_kv(both):
        count = both.shape[0]
        return (
            both[..., :model_width].reshape(count, frames, head_count, head_size),
            both[..., model_width:].reshape(count, frames, head_count, head_size),
        )

    def spatial_probs(key_all):
        scores = jnp.einsum("pfhe,qfhe->fhpq", query_s, key_all, preferred_element_type=jnp.float32)
        return softmax_with_total(scores * score_scale)

    key_s, value_s = split_kv(whole_kv)
    probs_s, log_total_s = spatial_probs(key_s)
    probs_s_low = to_low(probs_s)
    attn_s = turned(
        to_low(
            jnp.einsum(
                "fhpq,qfhe->pfhe", probs_s_low, value_s, preferred_element_type=jnp.float32
            ).reshape(token_rows, model_width)
        )
    )
    branch_s = forth(attn_s, 3, 1).reshape(patch_dev, frames, model_width)
    after_one = inputs + gate_one * branch_s
    temporal_input = turned(
        to_low(modulate(after_one, shift_two, scale_two)).reshape(token_rows, model_width)
    )
    temporal_qkv = to_low(forth(temporal_input, 4, 3)).reshape(
        patch_dev, frames, 3, head_count, head_size
    )
    query_t = temporal_qkv[:, :, 0]
    key_t = temporal_qkv[:, :, 1]
    value_t = temporal_qkv[:, :, 2]
    same_seg = frame_seg[:, None] == frame_seg[None, :]
    scores_t = (
        jnp.einsum("pfhe,pghe->phfg", query_t, key_t, preferred_element_type=jnp.float32)
        * score_scale
    )
    probs_t = softmax_rows(jnp.where(same_seg[None, None], scores_t, MASKED))
    probs_t_low = to_low(probs_t)
    attn_t = turned(
        to_low(
            jnp.einsum(
                "phfg,pghe->pfhe", probs_t_low, value_t, preferred_element_type=jnp.float32
            ).reshape(token_rows, model_width)
        )
    )
    branch_t = forth(attn_t, 7, 1).reshape(patch_dev, frames, model_width)
    after_two = after_one + gate_two * branch_t
    cross_input = turned(to_low(gain_norm(after_two, gain_row)).reshape(token_rows, model_width))
    query_c = to_low(forth(cross_input, 8, 1)).reshape(patch_dev, frames, head_count, head_size)
    key_c = memory[:, :model_width].reshape(text_keys, head_count, head_size)
    value_c = memory[:, model_width:].reshape(text_keys, head_count, head_size)
    key_seg = jnp.arange(text_keys, dtype=jnp.int32) // text_len
    allowed = frame_seg[:, None] == key_seg[None, :]
    scores_c = (
        jnp.einsum("pfhe,khe->pfhk", query_c, key_c, preferred_element_type=jnp.float32)
        * score_scale
    )
    probs_c = softmax_rows(jnp.where(allowed[None, :, None, :], scores_c, MASKED))
    probs_c_low = to_low(probs_c)
    attn_c = turned(
        to_low(
            jnp.einsum(
                "pfhk,khe->pfhe", probs_c_low, value_c, preferred_element_type=jnp.float32
            ).reshape(token_rows, model_width)
        )
    )
    branch_c = forth(attn_c, 9, 1).reshape(patch_dev, frames, model_width)
    after_three = after_two + branch_c
    mlp_input = turned(
        to_low(modulate(after_three, shift_three, scale_three)).reshape(token_rows, model_width)
    )
    pre_act = forth(mlp_input, 10, 4)
    post_act = to_low(gelu_tanh(pre_act))
    branch_m = sum(
        linear(post_act[:, k * WIDE : (k + 1) * WIDE], weight[14 + k]) for k in range(4)
    ).reshape(patch_dev, frames, model_width)
    result = after_three + gate_three * branch_m
    grad_gate_three = jnp.sum(grad_out * branch_m, axis=0)
    grad_four = to_low(grad_out * gate_three).reshape(token_rows, model_width)
    grad_post = jnp.concatenate(
        [right_product(grad_four, weight[14 + k]) for k in range(4)], axis=1
    )
    gelu_pull = jax.vjp(gelu_tanh, pre_act)[1]
    grad_pre = to_low(gelu_pull(grad_post)[0])
    grad_mlp_in = turned_back(back(grad_pre, 10, 4)).astype(jnp.float32).reshape(
        patch_dev, frames, model_width
    )
    mlp_pull = jax.vjp(modulate, after_three, shift_three, scale_three)[1]
    back_three, grad_shift_three, grad_scale_three = mlp_pull(grad_mlp_in)
    grad_three = grad_out + back_three
    grad_cross_branch = to_low(grad_three).reshape(token_rows, model_width)
    grad_attn_c = turned_back(back(grad_cross_branch, 9, 1)).reshape(
        patch_dev, frames, head_count, head_size
    )
    grad_probs_c = jnp.einsum(
        "pfhe,khe->pfhk", grad_attn_c, value_c, preferred_element_type=jnp.float32
    )
    grad_scores_c = to_low(softmax_back(probs_c, grad_probs_c))
    grad_query_c = to_low(
        jnp.einsum("pfhk,khe->pfhe", grad_scores_c, key_c, preferred_element_type=jnp.float32)
        * score_scale
    ).reshape(token_rows, model_width)
    grad_key_c = (
        jnp.einsum("pfhk,pfhe->khe", grad_scores_c, query_c, preferred_element_type=jnp.float32)
        * score_scale
    )
    grad_value_c = jnp.einsum(
        "pfhk,pfhe->khe", probs_c_low, grad_attn_c, preferred_element_type=jnp.float32
    )
    grad_memory = jnp.concatenate(
        [grad_key_c.reshape(text_keys, model_width), grad_value_c.reshape(text_keys, model_width)],
        axis=1,
    )
    grad_cross_in = turned_back(back(grad_query_c, 8, 1)).astype(jnp.float32).reshape(
        patch_dev, frames, model_width
    )
    cross_pull = jax.vjp(gain_norm, after_two, gain_row)[1]
    back_two, grad_gain = cross_pull(grad_cross_in)
    grad_two = grad_three + back_two
    grad_gate_two = jnp.sum(grad_two * branch_t, axis=0)
    grad_temporal_branch = to_low(grad_two * gate_two).reshape(token_rows, model_width)
    grad_attn_t = turned_back(back(grad_temporal_branch, 7, 1)).reshape(
        patch_dev, frames, head_count, head_size
    )
    grad_probs_t = jnp.einsum(
        "pfhe,pghe->phfg", grad_attn_t, value_t, preferred_element_type=jnp.float32
    )
    grad_scores_t = to_low(softmax_back(probs_t, grad_probs_t))
    grad_query_t = (
        jnp.einsum("phfg,pghe->pfhe", grad_scores_t, key_t, preferred_element_type=jnp.float32)
        * score_scale
    )
    grad_key_t = (
        jnp.einsum("phfg,pfhe->pghe", grad_scores_t, query_t, preferred_element_type=jnp.float32)
        * score_scale
    )
    grad_value_t = jnp.einsum(
        "phfg,pfhe->pghe", probs_t_low, grad_attn_t, preferred_element_type=jnp.float32
    )
    grad_qkv_t = to_low(jnp.stack([grad_query_t, grad_key_t, grad_value_t], axis=2)).reshape(
        token_rows, 3 * model_width
    )
    grad_temporal_in = turned_back(back(grad_qkv_t, 4, 3)).astype(jnp.float32).reshape(
        patch_dev, frames, model_width
    )
    temporal_pull = jax.vjp(modulate, after_one, shift_two, scale_two)[1]
    back_one, grad_shift_two, grad_scale_two = temporal_pull(grad_temporal_in)
    grad_one = grad_two + back_one
    grad_gate_one = jnp.sum(grad_one * branch_s, axis=0)
    grad_spatial_branch = to_low(grad_one * gate_one).reshape(token_rows, model_width)
    grad_attn_s = turned_back(back(grad_spatial_branch, 3, 1)).reshape(
        patch_dev, frames, head_count, head_size
    )
    grad_probs_s = jnp.einsum(
        "pfhe,qfhe->fhpq", grad_attn_s, value_s, preferred_element_type=jnp.float32
    )
    row_delta = jnp.sum(grad_probs_s * probs_s, axis=-1, keepdims=True)
    grad_scores_s = to_low(probs_s * (grad_probs_s - row_delta))
    grad_query_s = (
        jnp.einsum("fhpq,qfhe->pfhe", grad_scores_s, key_s, preferred_element_type=jnp.float32)
        * score_scale
    )
    count = lax.axis_size("blk") * patch_dev
    grad_key = (
        jnp.einsum("fhpq,pfhe->qfhe", grad_scores_s, query_s, preferred_element_type=jnp.float32)
        * score_scale
    )
    grad_value = jnp.einsum(
        "fhpq,pfhe->qfhe", probs_s_low, grad_attn_s, preferred_element_type=jnp.float32
    )
    grad_kv = lax.psum_scatter(
        jnp.concatenate(
            [
                grad_key.reshape(count, frames, model_width),
                grad_value.reshape(count, frames, model_width),
            ],
            axis=2,
        ).astype(jnp.bfloat16),
        "blk",
        scatter_dimension=0,
        tiled=True,
    )
    grad_qkv_s = jnp.concatenate(
        [to_low(grad_query_s).reshape(patch_dev, frames, model_width), grad_kv], axis=2
    ).reshape(token_rows, 3 * model_width)
    grad_spatial_in = turned_back(back(grad_qkv_s, 0, 3)).astype(jnp.float32).reshape(
        patch_dev, frames, model_width
    )
    spatial_pull = jax.vjp(modulate, inputs, shift_one, scale_one)[1]
    back_zero, grad_shift_one, grad_scale_one = spatial_pull(grad_spatial_in)
    grad_input = grad_one + back_zero
    grad_frame_mod = jnp.concatenate(
        [
            grad_shift_one,
            grad_scale_one,
            grad_gate_one,
            grad_shift_two,
            grad_scale_two,
            grad_gate_two,
            grad_shift_three,
            grad_scale_three,
            grad_gate_three,
        ],
        axis=1,
    )
    grad_mod_local = lax.dot_general(
        choose.astype(jnp.float32),
        grad_frame_mod,
        (((0,), (0,)), ((), ())),
        precision=lax.Precision.HIGHEST,
    )
    grad_mod_part, grad_memory_part = (
        lax.psum_scatter(
            grad_mod_local.astype(jnp.bfloat16), "blk", scatter_dimension=1, tiled=True
        ).astype(jnp.float32),
        lax.psum_scatter(
            grad_memory.astype(jnp.bfloat16), "blk", scatter_dimension=1, tiled=True
        ).astype(jnp.float32),
    )
    grad_mod_low = to_low(grad_mod_part)
    grad_caption = left_product(caption_rows, to_low(grad_memory_part))
    all_cond = lax.all_gather(conditioning, "seq", axis=0, tiled=True)
    all_mod = lax.all_gather(grad_mod_low, "seq", axis=0, tiled=True)
    grad_ada_w = left_product(all_cond, all_mod)
    grad_ada_b = jnp.sum(all_mod.astype(jnp.float32), axis=0)
    grad_caption = lax.psum(grad_caption.astype(jnp.bfloat16), "seq").astype(jnp.float32)
    share_gain = lax.psum_scatter(grad_gain, ("seq", "blk"), scatter_dimension=0, tiled=True)
    left = jnp.stack(
        [post_act[:, k * WIDE : (k + 1) * WIDE].T for k in range(4)]
        + [
            values.T
            for values in (
                mlp_input, attn_c, cross_input, attn_t, temporal_input, attn_s, spatial_input,
            )
        ]
    )
    right = jnp.concatenate(
        [
            by_block(values)
            for values in (
                grad_four, grad_pre, grad_cross_branch, grad_query_c, grad_temporal_branch,
                grad_qkv_t, grad_spatial_branch, grad_qkv_s,
            )
        ]
    )
    spread = scatter_weights(left, right)
    shares = lax.dynamic_slice(spread, (0, 4 * zplace, 0), (BLOCKS, SHARD, WIDE))

    def joined(first, count):
        return shares[first : first + count].transpose(1, 0, 2).reshape(SHARD, count * WIDE)

    return (
        to_low(result)[None],
        to_low(grad_input)[None],
        grad_ada_w,
        grad_ada_b,
        joined(15, 3),
        shares[14],
        joined(11, 3),
        shares[10],
        share_gain,
        shares[9],
        grad_caption,
        shares[8],
        hidden_back(joined(4, 4)),
        shares[0:4].reshape(4 * SHARD, WIDE),
    )


def solution(mesh):
    fast = dict(mesh.shape) == {"seq": 4, "blk": 8}
    return jax.shard_map(
        shards if fast else general_shards,
        mesh=mesh,
        in_specs=(
            P("seq", "blk", None, None),
            P("seq", None),
            P("seq", None),
            P("seq", None, None, None),
            P("seq", "blk", None, None),
            P(None, "blk"),
            P("blk"),
            P(("seq", "blk"), None),
            P(("seq", "blk"), None),
            P(("seq", "blk"), None),
            P(("seq", "blk"), None),
            P(("seq", "blk")),
            P(("seq", "blk"), None),
            P(None, "blk"),
            P(("seq", "blk"), None),
            P(("seq", "blk"), None),
            P(("seq", "blk"), None),
        ),
        out_specs=(
            P("seq", "blk", None, None),
            P("seq", "blk", None, None),
            P(None, "blk"),
            P("blk"),
            P(("seq", "blk"), None),
            P(("seq", "blk"), None),
            P(("seq", "blk"), None),
            P(("seq", "blk"), None),
            P(("seq", "blk")),
            P(("seq", "blk"), None),
            P(None, "blk"),
            P(("seq", "blk"), None),
            P(("seq", "blk"), None),
            P(("seq", "blk"), None),
        ),
        check_vma=False,
    )
```

```python
import math

import jax
import jax.numpy as jnp
import numpy as np
from jax import lax
from jax.experimental import pallas as pl
from jax.experimental.pallas import tpu as pltpu
from jax.sharding import PartitionSpec as P

H = 16
E = 72
L = 120


EPSILON = 1e-06
MASKED = -1e30


def to_low(values):
    return values.astype(jnp.bfloat16)


def linear(left, right):
    return jnp.dot(left, right, preferred_element_type=jnp.float32)


def left_product(left, right):
    return lax.dot_general(
        left, right, (((0,), (0,)), ((), ())), preferred_element_type=jnp.float32
    )


def right_product(left, right):
    return lax.dot_general(
        left, right, (((1,), (1,)), ((), ())), preferred_element_type=jnp.float32
    )


def normalize(values):
    center = values - jnp.mean(values, axis=-1, keepdims=True)
    return center * lax.rsqrt(jnp.mean(center * center, axis=-1, keepdims=True) + EPSILON)


def modulate(values, shift_rows, scale_rows):
    return normalize(values) * (1.0 + scale_rows) + shift_rows


def gain_norm(values, gain_row):
    return normalize(values) * gain_row


def gelu_tanh(values):
    return jax.nn.gelu(values, approximate=True)


def softmax_rows(scores):
    shifted = jnp.exp(scores - jnp.max(scores, axis=-1, keepdims=True))
    return shifted / jnp.sum(shifted, axis=-1, keepdims=True)


def softmax_with_total(scores):
    top = jnp.max(scores, axis=-1, keepdims=True)
    shifted = jnp.exp(scores - top)
    total = jnp.sum(shifted, axis=-1, keepdims=True)
    return (shifted / total, (top + jnp.log(total))[..., 0])


def softmax_back(probs, grad_probs):
    return probs * (grad_probs - jnp.sum(grad_probs * probs, axis=-1, keepdims=True))


def time_embedding(step_ids, model_width):
    half_width = model_width // 2
    frequency = jnp.exp(
        -math.log(10000.0) * jnp.arange(half_width).astype(jnp.float32) / half_width
    )
    angles = step_ids.astype(jnp.float32)[:, None] * frequency[None, :]
    return jnp.concatenate([jnp.cos(angles), jnp.sin(angles)], axis=1)


def general_shards(
    tokens,
    segments,
    timesteps,
    caption,
    cotangent,
    ada_weight,
    ada_bias,
    spatial_in,
    spatial_out,
    temporal_in,
    temporal_out,
    cross_gain,
    cross_query,
    caption_proj,
    cross_out,
    hidden_in,
    hidden_out,
):
    inputs = tokens[0].astype(jnp.float32)
    patch_dev, frames, model_width = inputs.shape
    token_rows = patch_dev * frames
    head_count = H
    head_size = E
    score_scale = E ** (-0.5)
    frame_seg = segments[0]
    step_ids = timesteps[0]
    seg_count, text_len, text_width = caption.shape[1:]
    text_keys = seg_count * text_len
    caption_rows = caption[0].reshape(text_keys, text_width)
    grad_out = cotangent[0].astype(jnp.float32)
    gathered = (
        lax.all_gather(spatial_in, ("seq", "blk"), axis=0, tiled=True),
        lax.all_gather(spatial_out, ("seq", "blk"), axis=0, tiled=True),
        lax.all_gather(temporal_in, ("seq", "blk"), axis=0, tiled=True),
        lax.all_gather(temporal_out, ("seq", "blk"), axis=0, tiled=True),
        lax.all_gather(cross_gain, ("seq", "blk"), axis=0, tiled=True),
        lax.all_gather(cross_query, ("seq", "blk"), axis=0, tiled=True),
        lax.all_gather(cross_out, ("seq", "blk"), axis=0, tiled=True),
        lax.all_gather(hidden_in, ("seq", "blk"), axis=0, tiled=True),
        lax.all_gather(hidden_out, ("seq", "blk"), axis=0, tiled=True),
    )
    (
        wide_sin,
        wide_sout,
        wide_tin,
        wide_tout,
        gain_low,
        wide_query,
        wide_cout,
        wide_hin,
        wide_hout,
    ) = gathered
    gain_row = gain_low.astype(jnp.float32)
    conditioning = to_low(jax.nn.silu(time_embedding(step_ids, model_width)))
    mod_part = to_low(linear(conditioning, ada_weight) + ada_bias.astype(jnp.float32))
    text_part = to_low(linear(caption_rows, caption_proj))
    modulation, memory = (
        lax.all_gather(mod_part, "blk", axis=1, tiled=True),
        lax.all_gather(text_part, "blk", axis=1, tiled=True),
    )
    choose = frame_seg[:, None] == jnp.arange(seg_count, dtype=jnp.int32)[None, :]
    frame_mod = linear(choose.astype(jnp.bfloat16), modulation)
    pieces = [frame_mod[:, index * model_width : (index + 1) * model_width] for index in range(9)]
    (
        shift_one,
        scale_one,
        gate_one,
        shift_two,
        scale_two,
        gate_two,
        shift_three,
        scale_three,
        gate_three,
    ) = pieces
    spatial_input = to_low(modulate(inputs, shift_one, scale_one)).reshape(token_rows, model_width)
    spatial_qkv = to_low(linear(spatial_input, wide_sin)).reshape(
        patch_dev, frames, 3 * model_width
    )
    query_s = spatial_qkv[..., :model_width].reshape(patch_dev, frames, head_count, head_size)
    local_kv = spatial_qkv[..., model_width:]
    whole_kv = lax.all_gather(local_kv, "blk", axis=0, tiled=True)

    def split_kv(both):
        count = both.shape[0]
        return (
            both[..., :model_width].reshape(count, frames, head_count, head_size),
            both[..., model_width:].reshape(count, frames, head_count, head_size),
        )

    def spatial_probs(key_all):
        scores = jnp.einsum("pfhe,qfhe->fhpq", query_s, key_all, preferred_element_type=jnp.float32)
        return softmax_with_total(scores * score_scale)

    key_s, value_s = split_kv(whole_kv)
    probs_s, log_total_s = spatial_probs(key_s)
    probs_s_low = to_low(probs_s)
    attn_s = to_low(
        jnp.einsum(
            "fhpq,qfhe->pfhe", probs_s_low, value_s, preferred_element_type=jnp.float32
        ).reshape(token_rows, model_width)
    )
    branch_s = linear(attn_s, wide_sout).reshape(patch_dev, frames, model_width)
    after_one = inputs + gate_one * branch_s
    temporal_input = to_low(modulate(after_one, shift_two, scale_two)).reshape(
        token_rows, model_width
    )
    temporal_qkv = to_low(linear(temporal_input, wide_tin)).reshape(
        patch_dev, frames, 3, head_count, head_size
    )
    query_t = temporal_qkv[:, :, 0]
    key_t = temporal_qkv[:, :, 1]
    value_t = temporal_qkv[:, :, 2]
    same_seg = frame_seg[:, None] == frame_seg[None, :]
    scores_t = (
        jnp.einsum("pfhe,pghe->phfg", query_t, key_t, preferred_element_type=jnp.float32)
        * score_scale
    )
    probs_t = softmax_rows(jnp.where(same_seg[None, None], scores_t, MASKED))
    probs_t_low = to_low(probs_t)
    attn_t = to_low(
        jnp.einsum(
            "phfg,pghe->pfhe", probs_t_low, value_t, preferred_element_type=jnp.float32
        ).reshape(token_rows, model_width)
    )
    branch_t = linear(attn_t, wide_tout).reshape(patch_dev, frames, model_width)
    after_two = after_one + gate_two * branch_t
    cross_input = to_low(gain_norm(after_two, gain_row)).reshape(token_rows, model_width)
    query_c = to_low(linear(cross_input, wide_query)).reshape(
        patch_dev, frames, head_count, head_size
    )
    key_c = memory[:, :model_width].reshape(text_keys, head_count, head_size)
    value_c = memory[:, model_width:].reshape(text_keys, head_count, head_size)
    key_seg = jnp.arange(text_keys, dtype=jnp.int32) // text_len
    allowed = frame_seg[:, None] == key_seg[None, :]
    scores_c = (
        jnp.einsum("pfhe,khe->pfhk", query_c, key_c, preferred_element_type=jnp.float32)
        * score_scale
    )
    probs_c = softmax_rows(jnp.where(allowed[None, :, None, :], scores_c, MASKED))
    probs_c_low = to_low(probs_c)
    attn_c = to_low(
        jnp.einsum(
            "pfhk,khe->pfhe", probs_c_low, value_c, preferred_element_type=jnp.float32
        ).reshape(token_rows, model_width)
    )
    branch_c = linear(attn_c, wide_cout).reshape(patch_dev, frames, model_width)
    after_three = after_two + branch_c
    mlp_input = to_low(modulate(after_three, shift_three, scale_three)).reshape(
        token_rows, model_width
    )
    pre_act = linear(mlp_input, wide_hin)
    post_act = to_low(gelu_tanh(pre_act))
    branch_m = linear(post_act, wide_hout).reshape(patch_dev, frames, model_width)
    result = after_three + gate_three * branch_m
    grad_gate_three = jnp.sum(grad_out * branch_m, axis=0)
    grad_four = to_low(grad_out * gate_three).reshape(token_rows, model_width)
    grad_hout = left_product(post_act, grad_four)
    grad_post = right_product(grad_four, wide_hout)
    gelu_pull = jax.vjp(gelu_tanh, pre_act)[1]
    grad_pre = to_low(gelu_pull(grad_post)[0])
    grad_hin = left_product(mlp_input, grad_pre)
    grad_mlp_in = right_product(grad_pre, wide_hin).reshape(patch_dev, frames, model_width)
    mlp_pull = jax.vjp(modulate, after_three, shift_three, scale_three)[1]
    back_three, grad_shift_three, grad_scale_three = mlp_pull(grad_mlp_in)
    grad_three = grad_out + back_three
    grad_cross_branch = to_low(grad_three).reshape(token_rows, model_width)
    grad_cout = left_product(attn_c, grad_cross_branch)
    grad_attn_c = to_low(right_product(grad_cross_branch, wide_cout)).reshape(
        patch_dev, frames, head_count, head_size
    )
    grad_probs_c = jnp.einsum(
        "pfhe,khe->pfhk", grad_attn_c, value_c, preferred_element_type=jnp.float32
    )
    grad_scores_c = to_low(softmax_back(probs_c, grad_probs_c))
    grad_query_c = to_low(
        jnp.einsum("pfhk,khe->pfhe", grad_scores_c, key_c, preferred_element_type=jnp.float32)
        * score_scale
    ).reshape(token_rows, model_width)
    grad_key_c = (
        jnp.einsum("pfhk,pfhe->khe", grad_scores_c, query_c, preferred_element_type=jnp.float32)
        * score_scale
    )
    grad_value_c = jnp.einsum(
        "pfhk,pfhe->khe", probs_c_low, grad_attn_c, preferred_element_type=jnp.float32
    )
    grad_memory = jnp.concatenate(
        [grad_key_c.reshape(text_keys, model_width), grad_value_c.reshape(text_keys, model_width)],
        axis=1,
    )
    grad_wquery = left_product(cross_input, grad_query_c)
    grad_cross_in = right_product(grad_query_c, wide_query).reshape(patch_dev, frames, model_width)
    cross_pull = jax.vjp(gain_norm, after_two, gain_row)[1]
    back_two, grad_gain = cross_pull(grad_cross_in)
    grad_two = grad_three + back_two
    grad_gate_two = jnp.sum(grad_two * branch_t, axis=0)
    grad_temporal_branch = to_low(grad_two * gate_two).reshape(token_rows, model_width)
    grad_tout = left_product(attn_t, grad_temporal_branch)
    grad_attn_t = to_low(right_product(grad_temporal_branch, wide_tout)).reshape(
        patch_dev, frames, head_count, head_size
    )
    grad_probs_t = jnp.einsum(
        "pfhe,pghe->phfg", grad_attn_t, value_t, preferred_element_type=jnp.float32
    )
    grad_scores_t = to_low(softmax_back(probs_t, grad_probs_t))
    grad_query_t = (
        jnp.einsum("phfg,pghe->pfhe", grad_scores_t, key_t, preferred_element_type=jnp.float32)
        * score_scale
    )
    grad_key_t = (
        jnp.einsum("phfg,pfhe->pghe", grad_scores_t, query_t, preferred_element_type=jnp.float32)
        * score_scale
    )
    grad_value_t = jnp.einsum(
        "phfg,pfhe->pghe", probs_t_low, grad_attn_t, preferred_element_type=jnp.float32
    )
    grad_qkv_t = to_low(jnp.stack([grad_query_t, grad_key_t, grad_value_t], axis=2)).reshape(
        token_rows, 3 * model_width
    )
    grad_tin = left_product(temporal_input, grad_qkv_t)
    grad_temporal_in = right_product(grad_qkv_t, wide_tin).reshape(patch_dev, frames, model_width)
    temporal_pull = jax.vjp(modulate, after_one, shift_two, scale_two)[1]
    back_one, grad_shift_two, grad_scale_two = temporal_pull(grad_temporal_in)
    grad_one = grad_two + back_one
    grad_gate_one = jnp.sum(grad_one * branch_s, axis=0)
    grad_spatial_branch = to_low(grad_one * gate_one).reshape(token_rows, model_width)
    grad_sout = left_product(attn_s, grad_spatial_branch)
    grad_attn_s = to_low(right_product(grad_spatial_branch, wide_sout)).reshape(
        patch_dev, frames, head_count, head_size
    )
    back_kv = lax.all_gather(local_kv, "blk", axis=0, tiled=True)
    back_key, back_value = split_kv(back_kv)
    back_probs = spatial_probs(back_key)[0]
    back_probs_low = to_low(back_probs)
    grad_probs_s = jnp.einsum(
        "pfhe,qfhe->fhpq", grad_attn_s, back_value, preferred_element_type=jnp.float32
    )
    row_delta = jnp.sum(grad_probs_s * back_probs, axis=-1, keepdims=True)
    grad_scores_s = to_low(back_probs * (grad_probs_s - row_delta))
    grad_query_s = (
        jnp.einsum("fhpq,qfhe->pfhe", grad_scores_s, back_key, preferred_element_type=jnp.float32)
        * score_scale
    )
    count = lax.axis_size("blk") * patch_dev
    grad_key = (
        jnp.einsum("fhpq,pfhe->qfhe", grad_scores_s, query_s, preferred_element_type=jnp.float32)
        * score_scale
    )
    grad_value = jnp.einsum(
        "fhpq,pfhe->qfhe", back_probs_low, grad_attn_s, preferred_element_type=jnp.float32
    )
    grad_kv = to_low(
        lax.psum_scatter(
            jnp.concatenate(
                [
                    grad_key.reshape(count, frames, model_width),
                    grad_value.reshape(count, frames, model_width),
                ],
                axis=2,
            ).astype(jnp.bfloat16),
            "blk",
            scatter_dimension=0,
            tiled=True,
        ).astype(jnp.float32)
    )
    grad_qkv_s = jnp.concatenate(
        [to_low(grad_query_s).reshape(patch_dev, frames, model_width), grad_kv], axis=2
    ).reshape(token_rows, 3 * model_width)
    grad_sin = left_product(spatial_input, grad_qkv_s)
    grad_spatial_in = right_product(grad_qkv_s, wide_sin).reshape(patch_dev, frames, model_width)
    spatial_pull = jax.vjp(modulate, inputs, shift_one, scale_one)[1]
    back_zero, grad_shift_one, grad_scale_one = spatial_pull(grad_spatial_in)
    grad_input = grad_one + back_zero
    grad_frame_mod = jnp.concatenate(
        [
            grad_shift_one,
            grad_scale_one,
            grad_gate_one,
            grad_shift_two,
            grad_scale_two,
            grad_gate_two,
            grad_shift_three,
            grad_scale_three,
            grad_gate_three,
        ],
        axis=1,
    )
    grad_mod_local = lax.dot_general(
        choose.astype(jnp.float32),
        grad_frame_mod,
        (((0,), (0,)), ((), ())),
        precision=lax.Precision.HIGHEST,
    )
    grad_mod_part, grad_memory_part = (
        lax.psum_scatter(
            grad_mod_local.astype(jnp.bfloat16), "blk", scatter_dimension=1, tiled=True
        ).astype(jnp.float32),
        lax.psum_scatter(
            grad_memory.astype(jnp.bfloat16), "blk", scatter_dimension=1, tiled=True
        ).astype(jnp.float32),
    )
    grad_mod_low = to_low(grad_mod_part)
    grad_ada_w = left_product(conditioning, grad_mod_low)
    grad_ada_b = jnp.sum(grad_mod_low.astype(jnp.float32), axis=0)
    grad_caption = left_product(caption_rows, to_low(grad_memory_part))
    grad_ada_w, grad_ada_b, grad_caption = (
        lax.psum(grad_ada_w.astype(jnp.bfloat16), "seq").astype(jnp.float32),
        lax.psum(grad_ada_b.astype(jnp.bfloat16), "seq").astype(jnp.float32),
        lax.psum(grad_caption.astype(jnp.bfloat16), "seq").astype(jnp.float32),
    )
    shares = (
        lax.psum_scatter(grad_sin, ("seq", "blk"), scatter_dimension=0, tiled=True),
        lax.psum_scatter(grad_sout, ("seq", "blk"), scatter_dimension=0, tiled=True),
        lax.psum_scatter(grad_tin, ("seq", "blk"), scatter_dimension=0, tiled=True),
        lax.psum_scatter(grad_tout, ("seq", "blk"), scatter_dimension=0, tiled=True),
        lax.psum_scatter(grad_gain, ("seq", "blk"), scatter_dimension=0, tiled=True),
        lax.psum_scatter(grad_wquery, ("seq", "blk"), scatter_dimension=0, tiled=True),
        lax.psum_scatter(grad_cout, ("seq", "blk"), scatter_dimension=0, tiled=True),
        lax.psum_scatter(grad_hin, ("seq", "blk"), scatter_dimension=0, tiled=True),
        lax.psum_scatter(grad_hout, ("seq", "blk"), scatter_dimension=0, tiled=True),
    )
    (
        share_sin,
        share_sout,
        share_tin,
        share_tout,
        share_gain,
        share_query,
        share_cout,
        share_hin,
        share_hout,
    ) = shares
    return (
        to_low(result)[None],
        to_low(grad_input)[None],
        grad_ada_w,
        grad_ada_b,
        share_sin,
        share_sout,
        share_tin,
        share_tout,
        share_gain,
        share_query,
        grad_caption,
        share_cout,
        share_hin,
        share_hout,
    )


MESH = pl.DeviceIdType.MESH
BLOCKS = 18
LINES = 8
SHARD = 36
LINE = 4 * SHARD
WINDOW = 48
WIDE = LINES * LINE
MIB = 2**20


def place():
    seq = lax.axis_index("seq")
    blk = lax.axis_index("blk")
    x, c = seq // 2, seq % 2
    z, y = blk // 2, blk % 2
    x1, y1 = x + (1 - 2 * x) * (1 - c), y + (1 - 2 * y) * c
    x2, y2 = x + (1 - 2 * x) * c, y + (1 - 2 * y) * (1 - c)
    return x, c, y, z, x1, y1, x2, y2


def device(x, c, y, z):
    return {"seq": x * 2 + c, "blk": z * 2 + y}


def line_of(c, x, y):
    return (c * 2 + x) * 2 + y


def remote(src, dst, send_sem, recv_sem, where):
    return pltpu.make_async_remote_copy(
        src_ref=src,
        dst_ref=dst,
        send_sem=send_sem,
        recv_sem=recv_sem,
        device_id=where,
        device_id_type=MESH,
    )


def greet(others):
    barrier = pltpu.get_barrier_semaphore()
    for other in others:
        pl.semaphore_signal(barrier, inc=1, device_id=other, device_id_type=MESH)
    pl.semaphore_wait(barrier, len(others))


def left_at(t):
    at = jnp.minimum(t, 4)
    for first in (8, 9, 10, 11, 14, 15):
        at = at + jnp.where(t >= first, 1, 0)
    return at


def right_at(t):
    return jnp.maximum(t - 3, 0)


ROWS = 256
TEXT = 240
TEXT_WIN = 384
MOD = 9 * WIDE
MOD_WIN = 1408
LEFT_SEM, SLOPE_SEM, SAVE_SEMS = 40, 42, 44
TILE = 384
SCALE = E ** (-0.5)


def nt(left, right):
    return lax.dot_general(
        left, right, (((1,), (1,)), ((), ())), preferred_element_type=jnp.float32
    )


def wide32(values):
    return values.astype(jnp.float32)


def loop(count, body):
    def step(index, carry):
        body(index)
        return carry

    lax.fori_loop(0, count, step, 0)


def each_rows(size, body, total=ROWS):
    loop(total // size, lambda i: body(pl.ds(pl.multiple_of(i * size, size), size)))


def each_cols(body):
    loop(WIDE // TILE, lambda i: body(pl.ds(pl.multiple_of(i * TILE, TILE), TILE)))


def swap_rows():
    row = lax.broadcasted_iota(jnp.int32, (ROWS, ROWS), 0)
    col = lax.broadcasted_iota(jnp.int32, (ROWS, ROWS), 1)
    return ((row % 16) * 16 + row // 16 == col).astype(jnp.float32).astype(jnp.bfloat16)


def head_window(h):
    base = h * E
    start = jnp.minimum(base // 128, 7) * 128
    lane = lax.broadcasted_iota(jnp.int32, (1, 256), 1)
    on = (lane >= base - start) & (lane < base - start + E)
    return pl.ds(pl.multiple_of(start, 128), 256), on.astype(jnp.float32)


def soft(scores, allowed):
    scores = scores * SCALE
    if allowed is not None:
        scores = jnp.where(allowed, scores, MASKED)
    powers = jnp.exp(scores - jnp.max(scores, axis=-1, keepdims=True))
    return powers * (1.0 / jnp.sum(powers, axis=-1, keepdims=True))


def head_forward(h, query, key, value, attn, allowed):
    lanes, on = head_window(h)
    low_on = to_low(on)
    scores = nt(query[:, lanes] * low_on, key[:, lanes])
    probs = to_low(soft(scores, allowed))
    part = linear(probs, value[:, lanes]) * on
    attn[:, lanes] = attn[:, lanes] + to_low(part)


def blk_peers(x, c, b):
    return [device(x, c, (b + k) % 2, ((b + k) % 8) // 2) for k in range(1, 8)]


def forward_kernel(
    src, tok, cot, gain_in, mod_in, text_in, seg_in, seg_row, turn,
    wide, out, left_o, qkvs_o, qkvt_o, qc_o, mem_o, xhat_o, rstd_o, branch_o, slope_o, gfour_o, cot_o, mods_o, gate_o, gain_o,
    parts, lines, weights, tokp, cotp, tokf, xin, xp, left, qkvs, qkvt, qc, mem, text, mod, mods, xhat, rstd, branch, branchw,
    stream, attnf, attnp, post, slope, gfour, gains, gain_at, gate,
    z_send, z_recv, l_send, l_recv, own_sem, w_sem, t_send, t_recv, a_send, a_recv, m_send, m_recv, x_send, x_recv,
    g_send, g_recv, save_sem,
):
    x, c, y, z, x1, y1, x2, y2 = place()
    b = z * 2 + y
    near = [device(x, c, y, (z + k) % 4) for k in (1, 2, 3)]
    first, second, twin = device(x1, c, y1, z), device(x2, c, y2, z), device(x, 1 - c, y, z)
    peers = blk_peers(x, c, b)
    greet(peers + [device(1 - x, c, y, z), twin])
    mine, line1 = line_of(c, x, y), line_of(c, x1, y1)
    line2, line3 = line_of(c, x2, y2), line_of(c, 1 - x, 1 - y)
    other = [line_of(1 - c, x, y), line_of(1 - c, x2, y2), line_of(1 - c, x1, y1), line_of(1 - c, 1 - x, 1 - y)]

    def z_copy(t, k):
        return remote(src.at[t], parts.at[t, z], z_send.at[t, k - 1], z_recv.at[t, k - 1], near[k - 1])

    def z_wait(t, k):
        return remote(src.at[t], parts.at[t, (z + 4 - k) % 4], z_send.at[t, k - 1], z_recv.at[t, k - 1], near[k - 1])

    def wide_line(t, line):
        return wide.at[t, pl.ds(pl.multiple_of(line * LINE, 16), LINE)]

    def own(t):
        return pltpu.make_async_copy(lines.at[t], wide_line(t, mine), own_sem.at[t])

    def line_copy(t, to, line, index, where):
        return remote(to, wide_line(t, line), l_send.at[t, index], l_recv.at[t, index], where)

    def sends(t, index):
        line, where = (
            (mine, first), (mine, second), (mine, twin), (line1, second),
            (line1, twin), (line2, twin), (line3, twin),
        )[index]
        from_here = lines.at[t] if index < 3 else wide_line(t, line)
        return line_copy(t, from_here, line, index, where)

    def arrives(t, line, index):
        line_copy(t, wide_line(t, line), line, index, first).wait_recv()

    def tick(t):
        @pl.when(t < BLOCKS)
        def _():
            for k in (1, 2, 3):
                z_copy(t, k).start()
            parts[t, z] = src[t]

        @pl.when((t >= 2) & (t < BLOCKS + 2))
        def _():
            now = t - 2
            for k in (1, 2, 3):
                z_wait(now, k).wait_recv()
            w0, w1, w2, w3 = [parts[now, k] for k in range(4)]
            lines[now, 0:32] = w0[0:32]
            lines[now, 32:48] = w0[32:48] + w1[0:16]
            lines[now, 48:64] = w1[16:32]
            lines[now, 64:80] = w1[32:48] + w2[0:16]
            lines[now, 80:96] = w2[16:32]
            lines[now, 96:112] = w2[32:48] + w3[0:16]
            lines[now, 112:144] = w3[16:48]
            for index in range(3):
                sends(now, index).start()
            own(now).start()

        @pl.when((t >= 3) & (t < BLOCKS + 3))
        def _():
            now = t - 3
            arrives(now, line1, 0)
            for index in (3, 4):
                sends(now, index).start()

        @pl.when(t >= 4)
        def _():
            now = t - 4
            arrives(now, line2, 1)
            sends(now, 5).start()
            arrives(now, line3, 3)
            sends(now, 6).start()

    done = [0]

    def pump(until):
        until = min(until, BLOCKS + 4)
        if until > done[0]:
            start = done[0]
            loop(until - start, lambda i: tick(i + start))
            done[0] = until

    def load(block):
        pump(block + 5)
        for line, index in zip(other, (2, 4, 5, 6)):
            arrives(block, line, index)
        own(block).wait()
        copy = pltpu.make_async_copy(wide.at[block], weights.at[block % 2], w_sem.at[block % 2])
        copy.start()
        copy.wait()

    def times(values, block, emit):
        def tile(cols):
            emit(cols, linear(values[...], weights[block % 2, :, cols]))

        each_cols(tile)

    saves = []
    held = {}

    def save(from_ref, to_ref, name=None):
        if name is None:
            name = len(saves)
            saves.append(name)
        held[name] = pltpu.make_async_copy(from_ref, to_ref, save_sem.at[name])
        held[name].start()

    def settle(name):
        if name in held:
            held.pop(name).wait()

    def turned(values, index):
        slot = index % 2
        settle(LEFT_SEM + slot)

        def tile(cols):
            xp[:, cols] = to_low(nt(values[...], turn[cols, :]))
            left[slot, cols, :] = to_low(nt(turn[cols, :], values[...]))

        each_cols(tile)
        save(left.at[slot], left_o.at[index], LEFT_SEM + slot)

    swap = swap_rows()
    tokp[...] = to_low(linear(swap, tok[...]))
    cotp[...] = to_low(linear(swap, cot[...]))

    def t_copy(k):
        to = (b + k) % 8
        part = tokp.at[pl.ds(pl.multiple_of(32 * to, 32), 32)]
        return remote(part, tokf.at[b], t_send.at[k - 1], t_recv.at[k - 1], peers[k - 1])

    def t_wait(k):
        of = (b + 8 - k) % 8
        remote(tokp.at[pl.ds(0, 32)], tokf.at[of], t_send.at[k - 1], t_recv.at[k - 1], peers[k - 1]).wait_recv()

    def m_copy(k, at):
        return remote(mod_in, mod.at[at], m_send.at[k - 1], m_recv.at[k - 1], peers[k - 1])

    def x_copy(k, at):
        return remote(text_in, text.at[at], x_send.at[k - 1], x_recv.at[k - 1], peers[k - 1])

    for k in range(1, 8):
        t_copy(k).start()
        m_copy(k, b).start()
        x_copy(k, b).start()
    tokf[b] = tokp[pl.ds(pl.multiple_of(32 * b, 32), 32)]
    mod[b] = mod_in[...]
    text[b] = text_in[...]

    def g_copy(at, from_at, to):
        return remote(gains.at[from_at], gain_at.at[at], g_send.at[at], g_recv.at[at], to)

    gains[0] = gain_in[...]
    g_copy(0, 0, twin).start()
    save(cotp, cot_o)
    pump(3)

    for k in range(1, 8):
        m_copy(k, (b + 8 - k) % 8).wait_recv()
    mods[...] = jnp.zeros_like(mods)
    for k in range(8):
        lanes = slice(1280 * k, 1280 * k + MOD_WIN)
        mods[:, lanes] = mods[:, lanes] + wide32(mod[k])[0:8]
    save(mods, mods_o)

    g_copy(0, 0, twin).wait_recv()
    gains[1] = gains[0] + gain_at[0]
    g_copy(1, 1, first).start()

    def pick(piece, seg):
        lanes = slice(WIDE * piece, WIDE * piece + WIDE)
        return jnp.where(seg > 0.5, mods[1:2, lanes], mods[0:1, lanes])

    def normal(values, rows, index):
        center = values - jnp.mean(values, axis=-1, keepdims=True)
        factor = lax.rsqrt(jnp.mean(center * center, axis=-1, keepdims=True) + EPSILON)
        scaled = center * factor
        xhat[index, rows, :] = to_low(scaled)
        rstd[index, rows, :] = jnp.broadcast_to(factor, (factor.shape[0], 128))
        return scaled

    for k in range(1, 8):
        t_wait(k)
    g_copy(1, 1, first).wait_recv()
    gains[2] = gains[1] + gain_at[1]
    g_copy(2, 2, second).start()

    def spatial_rows(i):
        seg = jnp.concatenate([seg_in[1, 0:16, 0:1], seg_in[1, 128:144, 0:1]])
        values = wide32(tokf[i])
        center = values - jnp.mean(values, axis=-1, keepdims=True)
        factor = lax.rsqrt(jnp.mean(center * center, axis=-1, keepdims=True) + EPSILON)
        scaled = center * factor
        ready = to_low(scaled * (1.0 + pick(1, seg)) + pick(0, seg))
        low = to_low(scaled)
        spread = jnp.broadcast_to(factor, (32, 128))
        for f in range(2):
            rows = pl.ds(pl.multiple_of(128 * f + 16 * i, 16), 16)
            part = slice(16 * f, 16 * f + 16)
            xhat[0, rows, :] = low[part]
            rstd[0, rows, :] = spread[part]
            xin[rows, :] = ready[part]

    loop(8, spatial_rows)
    save(xhat.at[0], xhat_o.at[0])
    save(rstd.at[0], rstd_o.at[0])
    turned(xin, 10)
    for j in range(3):
        load(j)

        def emit(cols, value, j=j):
            qkvs[j, :, cols] = to_low(value)

        times(xp, j, emit)
    save(qkvs, qkvs_o)
    g_copy(2, 2, second).wait_recv()
    gains[3] = gains[2] + gain_at[2]
    for k in (1, 2, 3):
        remote(gains.at[3], gain_at.at[2 + k], g_send.at[2 + k], g_recv.at[2 + k], near[k - 1]).start()
    attnf[...] = jnp.zeros_like(attnf)

    def spatial_heads(frame, start):
        rows = slice(128 * frame, 128 * frame + 128)

        def body(h):
            head_forward(
                h + start, qkvs.at[0, rows], qkvs.at[1, rows], qkvs.at[2, rows], attnf.at[rows], None
            )

        loop(8, body)

    spatial_heads(0, 0)
    spatial_heads(0, 8)
    pump(8)
    spatial_heads(1, 0)
    spatial_heads(1, 8)
    for k in (1, 2, 3):
        remote(gains.at[3], gain_at.at[2 + k], g_send.at[2 + k], g_recv.at[2 + k], near[k - 1]).wait_recv()
    gains[0 + 4] = gains[3] + gain_at[3] + gain_at[4] + gain_at[5]
    save(gains.at[4], gain_o)

    def a_copy(k, f):
        to = (b + k) % 8
        part = attnf.at[pl.ds(pl.multiple_of(128 * f + 16 * to, 16), 16)]
        return remote(part, attnp.at[2 * b + f], a_send.at[k - 1, f], a_recv.at[k - 1, f], peers[k - 1])

    def a_wait(k, f):
        of = (b + 8 - k) % 8
        part = attnf.at[pl.ds(0, 16)]
        remote(part, attnp.at[2 * of + f], a_send.at[k - 1, f], a_recv.at[k - 1, f], peers[k - 1]).wait_recv()

    for k in range(1, 8):
        for f in range(2):
            a_copy(k, f).start()
    for f in range(2):
        attnp[2 * b + f] = attnf[pl.ds(pl.multiple_of(128 * f + 16 * b, 16), 16)]
    pump(9)
    for k in range(1, 8):
        for f in range(2):
            a_wait(k, f)
    xin[...] = attnp[...].reshape(ROWS, WIDE)
    turned(xin, 9)
    load(3)

    def emit_branch(cols, value):
        branchw[:, cols] = value

    times(xp, 3, emit_branch)

    def after_spatial(rows):
        seg = seg_in[0, rows, 0:1]
        value = branchw[rows, :]
        branch[0, rows, :] = to_low(value)
        value = wide32(tokp[rows, :]) + pick(2, seg) * value
        stream[rows, :] = value
        xin[rows, :] = to_low(normal(value, rows, 1) * (1.0 + pick(4, seg)) + pick(3, seg))

    each_rows(32, after_spatial)
    save(branch.at[0], branch_o.at[0])
    save(xhat.at[1], xhat_o.at[1])
    save(rstd.at[1], rstd_o.at[1])

    turned(xin, 8)
    for j in range(3):
        load(4 + j)

        def emit(cols, value, j=j):
            qkvt[j, :, cols] = to_low(value)

        times(xp, 4 + j, emit)
    save(qkvt, qkvt_o)
    for k in range(1, 8):
        for f in range(2):
            a_copy(k, f).wait_send()
    attnf[...] = jnp.zeros_like(attnf)

    def temporal_mask():
        row = lax.broadcasted_iota(jnp.int32, (ROWS, ROWS), 0)
        col = lax.broadcasted_iota(jnp.int32, (ROWS, ROWS), 1)
        return (row % 16 == col % 16) & (seg_in[0, :, 0:1] == seg_row[0:1, :])

    def temporal_head(h):
        head_forward(h, qkvt.at[0], qkvt.at[1], qkvt.at[2], attnf, temporal_mask())

    loop(8, temporal_head)
    pump(12)
    loop(8, lambda h: temporal_head(h + 8))
    xin[...] = attnf[...]
    turned(xin, 7)
    load(7)
    times(xp, 7, emit_branch)

    def after_temporal(rows):
        seg = seg_in[0, rows, 0:1]
        value = branchw[rows, :]
        branch[1, rows, :] = to_low(value)
        value = stream[rows, :] + pick(5, seg) * value
        stream[rows, :] = value
        xin[rows, :] = to_low(normal(value, rows, 2) * gains[4, 0:1, :])

    each_rows(32, after_temporal)
    save(branch.at[1], branch_o.at[1])
    save(xhat.at[2], xhat_o.at[2])
    save(rstd.at[2], rstd_o.at[2])

    turned(xin, 6)
    load(8)

    def emit_query(cols, value):
        qc[:, cols] = to_low(value)

    times(xp, 8, emit_query)
    save(qc, qc_o)
    for k in range(1, 8):
        x_copy(k, (b + 8 - k) % 8).wait_recv()
    mem[...] = jnp.zeros_like(mem)
    for k in range(8):
        start = 288 * (k % 4) // 128 * 128
        lanes = slice(start, start + TEXT_WIN)
        mem[k // 4, :, lanes] = mem[k // 4, :, lanes] + text[k]
    save(mem, mem_o)
    attnf[...] = jnp.zeros_like(attnf)

    def cross_mask():
        col = lax.broadcasted_iota(jnp.int32, (ROWS, TEXT), 1)
        return (col >= L) == (seg_in[0, :, 0:1] > 0.5)

    def cross_head(h):
        head_forward(h, qc, mem.at[0], mem.at[1], attnf, cross_mask())

    loop(8, cross_head)
    pump(14)
    loop(8, lambda h: cross_head(h + 8))
    xin[...] = attnf[...]
    turned(xin, 5)
    load(9)
    times(xp, 9, emit_branch)

    def after_cross(rows):
        seg = seg_in[0, rows, 0:1]
        value = stream[rows, :] + branchw[rows, :]
        stream[rows, :] = value
        xin[rows, :] = to_low(normal(value, rows, 3) * (1.0 + pick(7, seg)) + pick(6, seg))
        gfour[rows, :] = to_low(wide32(cotp[rows, :]) * pick(8, seg))

    each_rows(32, after_cross)
    save(xhat.at[3], xhat_o.at[3])
    save(rstd.at[3], rstd_o.at[3])
    save(gfour, gfour_o)

    turned(xin, 4)
    same = (
        lax.broadcasted_iota(jnp.int32, (TILE, TILE), 0) == lax.broadcasted_iota(jnp.int32, (TILE, TILE), 1)
    ).astype(jnp.float32).astype(jnp.bfloat16)
    for k in range(4):
        slot = k % 2
        load(10 + 2 * k)
        settle(SLOPE_SEM + slot)
        settle(LEFT_SEM + slot)

        def emit_hidden(cols, value, slot=slot):
            inner = math.sqrt(2.0 / math.pi) * (value + 0.044715 * value * value * value)
            bent = jnp.tanh(inner)
            half = 0.5 * (1.0 + bent)
            tilt = math.sqrt(2.0 / math.pi) * (1.0 + 3 * 0.044715 * value * value)
            slope[slot, :, cols] = to_low(half + 0.5 * value * (1.0 - bent * bent) * tilt)
            low = to_low(value * half)
            post[:, cols] = low
            left[slot, cols, :] = to_low(nt(same, low))

        times(xp, 10 + 2 * k, emit_hidden)
        save(slope.at[slot], slope_o.at[k], SLOPE_SEM + slot)
        save(left.at[slot], left_o.at[k], LEFT_SEM + slot)
        load(11 + 2 * k)

        def emit_out(cols, value, k=k):
            branchw[:, cols] = value if k == 0 else branchw[:, cols] + value

        times(post, 11 + 2 * k, emit_out)

    gate[...] = jnp.zeros_like(gate)

    def last(rows):
        seg = seg_in[0, rows, 0:1]
        value = branchw[rows, :]
        xin[rows, :] = to_low(stream[rows, :] + pick(8, seg) * value)
        value = wide32(cotp[rows, :]) * value
        later = jnp.sum(value * seg, axis=0, keepdims=True)
        every = jnp.sum(value, axis=0, keepdims=True)
        gate[0:1, :] = gate[0:1, :] + (every - later)
        gate[1:2, :] = gate[1:2, :] + later

    each_rows(32, last)
    save(gate, gate_o)
    out[...] = to_low(linear(swap_rows(), xin[...]))

    for copy in held.values():
        copy.wait()
    for k in range(1, 8):
        t_copy(k).wait_send()
        m_copy(k, b).wait_send()
        x_copy(k, b).wait_send()
    for at, to in ((0, twin), (1, first), (2, second)):
        g_copy(at, at, to).wait_send()
    for k in (1, 2, 3):
        remote(gains.at[3], gain_at.at[2 + k], g_send.at[2 + k], g_recv.at[2 + k], near[k - 1]).wait_send()

    def finish(t):
        for k in (1, 2, 3):
            z_copy(t, k).wait_send()
        for index in range(7):
            sends(t, index).wait_send()

    loop(BLOCKS, finish)


ANY = pl.BlockSpec(memory_space=pl.ANY)
IN_VMEM = pl.BlockSpec(memory_space=pltpu.VMEM)


def forward(src, tok, cot, gain_in, mod_in, text_in, seg_in, seg_row, turn):
    low, full = jnp.bfloat16, jnp.float32
    dma = pltpu.SemaphoreType.DMA
    hbm = [
        ((BLOCKS, WIDE, WIDE), low),
        ((ROWS, WIDE), low),
        ((11, WIDE, ROWS), low),
        ((3, ROWS, WIDE), low),
        ((3, ROWS, WIDE), low),
        ((ROWS, WIDE), low),
        ((2, TEXT, WIDE), low),
        ((4, ROWS, WIDE), low),
        ((4, ROWS, 128), full),
        ((2, ROWS, WIDE), low),
        ((4, ROWS, WIDE), low),
        ((ROWS, WIDE), low),
        ((ROWS, WIDE), low),
        ((8, MOD), full),
        ((8, WIDE), full),
        ((8, WIDE), full),
    ]
    vmem = [
        ((BLOCKS, 4, WINDOW, WIDE), low),
        ((BLOCKS, LINE, WIDE), low),
        ((2, WIDE, WIDE), low),
        ((ROWS, WIDE), low),
        ((ROWS, WIDE), low),
        ((8, 32, WIDE), low),
        ((ROWS, WIDE), low),
        ((ROWS, WIDE), low),
        ((2, WIDE, ROWS), low),
        ((3, ROWS, WIDE), low),
        ((3, ROWS, WIDE), low),
        ((ROWS, WIDE), low),
        ((2, TEXT, WIDE), low),
        ((8, TEXT, TEXT_WIN), low),
        ((8, 16, MOD_WIN), low),
        ((8, MOD), full),
        ((4, ROWS, WIDE), low),
        ((4, ROWS, 128), full),
        ((2, ROWS, WIDE), low),
        ((ROWS, WIDE), full),
        ((ROWS, WIDE), full),
        ((ROWS, WIDE), low),
        ((16, 16, WIDE), low),
        ((ROWS, WIDE), low),
        ((2, ROWS, WIDE), low),
        ((ROWS, WIDE), low),
        ((5, 8, WIDE), full),
        ((6, 8, WIDE), full),
        ((8, WIDE), full),
    ]
    return pl.pallas_call(
        forward_kernel,
        out_shape=[jax.ShapeDtypeStruct(*shape) for shape in hbm],
        in_specs=[IN_VMEM] * 9,
        out_specs=[ANY, IN_VMEM] + [ANY] * 14,
        scratch_shapes=[pltpu.VMEM(*shape) for shape in vmem]
        + [
            dma((BLOCKS, 3)), dma((BLOCKS, 3)), dma((BLOCKS, 7)), dma((BLOCKS, 7)), dma((BLOCKS,)), dma((2,)),
            dma((7,)), dma((7,)), dma((7, 2)), dma((7, 2)), dma((7,)), dma((7,)), dma((7,)), dma((7,)),
            dma((6,)), dma((6,)), dma((SAVE_SEMS,)),
        ],
        compiler_params=pltpu.CompilerParams(
            collective_id=0, has_side_effects=True, vmem_limit_bytes=60 * MIB
        ),
        name="forward",
    )(src, tok, cot, gain_in, mod_in, text_in, seg_in, seg_row, turn)


def tn(left, right):
    return lax.dot_general(
        left, right, (((0,), (0,)), ((), ())), preferred_element_type=jnp.float32
    )


def head_backward(h, query, key, value, grad, dquery, dkey, dvalue, allowed):
    lanes, on = head_window(h)
    low_on = to_low(on)
    qw, kw, vw, gw = query[:, lanes], key[:, lanes], value[:, lanes], grad[:, lanes]
    probs = soft(nt(qw * low_on, kw), allowed)
    grad_probs = nt(gw * low_on, vw)
    delta = jnp.sum(grad_probs * probs, axis=-1, keepdims=True)
    scores = to_low(probs * (grad_probs - delta))
    dquery[:, lanes] = dquery[:, lanes] + to_low(linear(scores, kw) * (on * SCALE))
    dkey[:, lanes] = dkey[:, lanes] + to_low(tn(scores, qw) * (on * SCALE))
    dvalue[:, lanes] = dvalue[:, lanes] + to_low(tn(to_low(probs), gw) * on)


def backward_kernel(
    wide, left_i, qkvs_i, qkvt_i, qc_i, mem_i, xhat_i, rstd_i, branch_i, slope_i, gfour_i, cot_i, mods_i, gate_i, gain_i,
    seg_in, seg_row, turn,
    total, gtok, gain_o, text_o, mod_o,
    weights, left, right, qkv, xhat, rstd, branch, slope, mods, gain, stream, work, grad, xin, gm, dmem, text, mod_out, mod,
    seqs, gains, gain_at, gframe, back, backp,
    s0, r0, s1, r1, k1, s2, r2, k2, s3, r3, k3, share,
    in_sem, w_sem, s0_sem, r0_sem, s1_sem, r1_sem, s2_sem, r2_sem, s3_sem, r3_sem, share_sem,
    a_send, a_recv, u_send, u_recv, x_send, x_recv, m_send, m_recv, q_send, q_recv, g_send, g_recv,
):
    x, c, y, z, x1, y1, x2, y2 = place()
    b = z * 2 + y
    near = [device(x, c, y, (z + k) % 4) for k in (1, 2, 3)]
    first, second, twin = device(x1, c, y1, z), device(x2, c, y2, z), device(x, 1 - c, y, z)
    peers = blk_peers(x, c, b)
    across = [twin, device(1 - x, c, y, z), device(1 - x, 1 - c, y, z)]
    greet(peers + across)

    fetches = {}

    def fetch(name, from_ref, to_ref):
        fetches[name] = pltpu.make_async_copy(from_ref, to_ref, in_sem.at[name])
        fetches[name].start()

    def have(name):
        if name in fetches:
            fetches.pop(name).wait()

    fetch(0, gfour_i, right.at[0])
    for k in range(11):
        fetch(1 + k, left_i.at[k], left.at[k])
    fetch(12, mods_i, mods)
    fetch(13, gain_i, gain)
    fetch(14, slope_i.at[0], slope.at[0])
    fetch(15, slope_i.at[1], slope.at[1])
    fetch(16, xhat_i.at[3], xhat.at[1])
    fetch(17, rstd_i.at[3], rstd.at[1])
    fetch(18, cot_i, xin)
    fetch(19, gate_i, work.at[0:8])

    def weight(block):
        slot = WEIGHT_ORDER.index(block) % 2
        return weights.at[slot]

    def prefetch(at):
        if at < len(WEIGHT_ORDER):
            copy = pltpu.make_async_copy(wide.at[WEIGHT_ORDER[at]], weights.at[at % 2], w_sem.at[at % 2])
            copy.start()
            fetches["w", WEIGHT_ORDER[at]] = copy

    def release(block):
        prefetch(WEIGHT_ORDER.index(block) + 2)

    prefetch(0)
    prefetch(1)

    order = [(1 - x, 1 - y), (x2, y2), (x1, y1), (x, y)]
    twin_order = [(1 - x, 1 - y), (x1, y1), (x2, y2), (x, y)]

    def product(t, core, xl, yl):
        rows = pl.ds(pl.multiple_of(line_of(core, xl, yl) * LINE, 16), LINE)
        return linear(left[left_at(t), rows, :], right[right_at(t)])

    def copy0(t, l):
        return remote(s0.at[t % 2, l], r0.at[t % 4, l], s0_sem.at[t % 2, l], r0_sem.at[t % 4, l], twin)

    def copy1(t, l):
        return remote(s1.at[t % 2, l], r1.at[t % 4, l], s1_sem.at[t % 2, l], r1_sem.at[t % 4, l], second)

    def copy2(t):
        return remote(s2.at[t % 2], r2.at[t % 4], s2_sem.at[t % 2], r2_sem.at[t % 4], first)

    def copy3(t, k):
        part = pl.ds(pl.multiple_of(32 * ((z + k) % 4), 16), WINDOW)
        return remote(s3.at[t % 2, part], r3.at[t % 4, k - 1], s3_sem.at[t % 2, k - 1], r3_sem.at[t % 4, k - 1], near[k - 1])

    def share_copy(t):
        return pltpu.make_async_copy(share.at[t % 2], total.at[t], share_sem.at[t % 2])

    def tick(t):
        @pl.when(t < BLOCKS)
        def _():
            for l, (xl, yl) in enumerate(twin_order):
                @pl.when(t >= 2)
                def _():
                    copy0(t - 2, l).wait_send()
                s0[t % 2, l] = to_low(product(t, 1 - c, xl, yl))
                copy0(t, l).start()

        @pl.when((t >= 1) & (t < BLOCKS + 1))
        def _():
            now = t - 1
            for l, (xl, yl) in enumerate(order):
                copy0(now, l).wait_recv()
                value = product(now, c, xl, yl) + wide32(r0[now % 4, l])
                if l < 2:
                    @pl.when(now >= 2)
                    def _():
                        copy1(now - 2, l).wait_send()
                    s1[now % 2, l] = to_low(value)
                    copy1(now, l).start()
                else:
                    k1[now % 2, l - 2] = to_low(value)

        @pl.when((t >= 2) & (t < BLOCKS + 2))
        def _():
            now = t - 2
            copy1(now, 0).wait_recv()

            @pl.when(now >= 2)
            def _():
                copy2(now - 2).wait_send()
            s2[now % 2] = to_low(wide32(k1[now % 2, 0]) + wide32(r1[now % 4, 0]))
            copy2(now).start()
            copy1(now, 1).wait_recv()
            k2[now % 2] = wide32(k1[now % 2, 1]) + wide32(r1[now % 4, 1])

        @pl.when((t >= 3) & (t < BLOCKS + 3))
        def _():
            now = t - 3
            copy2(now).wait_recv()

            @pl.when(now >= 2)
            def _():
                for k in (1, 2, 3):
                    copy3(now - 2, k).wait_send()
            value = k2[now % 2] + wide32(r2[now % 4])
            k3[now % 2] = value
            s3[now % 2] = to_low(value)
            for k in (1, 2, 3):
                copy3(now, k).start()

        @pl.when(t >= 4)
        def _():
            now = t - 4
            value = k3[now % 2, pl.ds(pl.multiple_of(32 * z, 16), WINDOW)]
            for k in (1, 2, 3):
                copy3(now, k).wait_recv()
                value = value + wide32(r3[now % 4, k - 1])

            @pl.when(now >= 2)
            def _():
                share_copy(now - 2).wait()
            share[now % 2] = value
            share_copy(now).start()

    done = [0]

    def pump(until):
        if until > done[0]:
            start = done[0]
            loop(until - start, lambda i: tick(i + start))
            done[0] = until

    def pick(piece, seg):
        lanes = slice(WIDE * piece, WIDE * piece + WIDE)
        return jnp.where(seg > 0.5, mods[1:2, lanes], mods[0:1, lanes])

    def by_video(piece, value, seg):
        lanes = slice(WIDE * piece, WIDE * piece + WIDE)
        later = jnp.sum(value * seg, axis=0, keepdims=True)
        every = jnp.sum(value, axis=0, keepdims=True)
        gm[0:1, lanes] = gm[0:1, lanes] + (every - later)
        gm[1:2, lanes] = gm[1:2, lanes] + later

    def through(values_at, blocks, emit):
        for n, (values, block) in enumerate(zip(values_at, blocks)):
            have(("w", block))

            def tile(cols, n=n, values=values, block=block):
                part = nt(values[...], weight(block)[cols, :])
                if n > 0:
                    part = part + work[:, cols]
                if n == len(blocks) - 1:
                    xin[:, cols] = to_low(part)
                else:
                    work[:, cols] = part

            each_cols(tile)
            release(block)
        turn_back(emit)

    def turn_back(emit):
        each_cols(lambda cols: emit(cols, linear(xin[...], turn[:, cols])))

    def emit_work(cols, value):
        work[:, cols] = value

    def emit_grad(cols, value):
        grad[:, cols] = to_low(value)

    def norm_back(grad_in, tilt, at, rows):
        slope_in = grad_in * tilt
        hat = wide32(xhat[at, rows, :])
        first_mean = jnp.mean(slope_in, axis=-1, keepdims=True)
        second_mean = jnp.mean(slope_in * hat, axis=-1, keepdims=True)
        return rstd[at, rows, 0:1] * (slope_in - first_mean - hat * second_mean)

    gm[...] = jnp.zeros_like(gm)
    have(0)
    have(12)
    have(18)
    have(19)
    gm[0:8, 8 * WIDE : 9 * WIDE] = work[0:8]
    stream[...] = wide32(xin[...])
    for k in range(11):
        have(1 + k)
    pump(1)
    for k in range(4):
        have(14 + k % 2 if k < 2 else ("slope", k))
        have(("w", 11 + 2 * k))

        def tile(cols, k=k):
            value = nt(right[0], weight(11 + 2 * k)[cols, :]) * wide32(slope[k % 2, :, cols])
            right[1 + k, :, cols] = to_low(value)

        each_cols(tile)
        release(11 + 2 * k)
        if k < 2:
            copy = pltpu.make_async_copy(slope_i.at[k + 2], slope.at[k % 2], in_sem.at[14 + k])
            copy.start()
            fetches["slope", k + 2] = copy
        have(("w", 10 + 2 * k))

        def tile(cols, k=k):
            part = nt(right[1 + k], weight(10 + 2 * k)[cols, :])
            if k > 0:
                part = part + work[:, cols]
            if k < 3:
                work[:, cols] = part
            else:
                xin[:, cols] = to_low(part)

        each_cols(tile)
        release(10 + 2 * k)
        pump(k + 2)
    turn_back(emit_work)
    have(16)
    have(17)
    fetch(20, qc_i, qkv.at[0])
    fetch(21, mem_i.at[0], qkv.at[1, 0:TEXT])
    fetch(22, mem_i.at[1], qkv.at[2, 0:TEXT])
    fetch(23, xhat_i.at[2], xhat.at[0])
    fetch(24, rstd_i.at[2], rstd.at[0])

    def after_mlp(rows):
        seg = seg_in[0, rows, 0:1]
        value = work[rows, :]
        by_video(6, value, seg)
        by_video(7, value * wide32(xhat[1, rows, :]), seg)
        value = stream[rows, :] + norm_back(value, 1.0 + pick(7, seg), 1, rows)
        stream[rows, :] = value
        right[5, rows, :] = to_low(value)

    each_rows(32, after_mlp)

    fetch(25, xhat_i.at[1], xhat.at[1])
    fetch(26, rstd_i.at[1], rstd.at[1])
    through([right.at[5]], [9], emit_grad)
    right[6] = jnp.zeros_like(right[6])
    dmem[...] = jnp.zeros_like(dmem)
    for name in (13, 20, 21, 22, 23, 24):
        have(name)

    def cross_head(h):
        col = lax.broadcasted_iota(jnp.int32, (ROWS, TEXT), 1)
        allowed = (col >= L) == (seg_in[0, :, 0:1] > 0.5)
        head_backward(
            h, qkv.at[0], qkv.at[1, 0:TEXT], qkv.at[2, 0:TEXT], grad, right.at[6], dmem.at[0], dmem.at[1], allowed
        )

    for part in range(4):
        loop(4, lambda h: cross_head(h + 4 * part))
        pump(6 + part if part < 3 else 8)

    def x_copy(k):
        to = (b + k) % 8
        lanes = pl.ds(pl.multiple_of((288 * (to % 4)) // 128 * 128, 128), TEXT_WIN)
        return remote(dmem.at[to // 4, :, lanes], text.at[b], x_send.at[k - 1], x_recv.at[k - 1], peers[k - 1])

    def x_wait(k):
        of = (b + 8 - k) % 8
        remote(dmem.at[0, :, pl.ds(0, TEXT_WIN)], text.at[of], x_send.at[k - 1], x_recv.at[k - 1], peers[k - 1]).wait_recv()

    for k in range(1, 8):
        x_copy(k).start()
    text[b] = dmem[b // 4, :, pl.ds(pl.multiple_of((288 * (b % 4)) // 128 * 128, 128), TEXT_WIN)]
    fetch(27, qkvt_i.at[0], qkv.at[0])
    fetch(28, qkvt_i.at[1], qkv.at[1])
    fetch(29, qkvt_i.at[2], qkv.at[2])
    fetch(30, branch_i.at[1], branch)
    through([right.at[6]], [8], emit_work)
    gains[0] = jnp.zeros_like(gains[0])
    have(30)

    def after_cross(rows):
        seg = seg_in[0, rows, 0:1]
        value = work[rows, :]
        gains[0, 0:1, :] = gains[0, 0:1, :] + jnp.sum(value * wide32(xhat[0, rows, :]), axis=0, keepdims=True)
        value = stream[rows, :] + norm_back(value, gain[0:1, :], 0, rows)
        stream[rows, :] = value
        by_video(5, value * wide32(branch[rows, :]), seg)
        right[7, rows, :] = to_low(value * pick(5, seg))

    each_rows(32, after_cross)

    def g_copy(at, to):
        return remote(gains.at[min(at, 3)], gain_at.at[at], g_send.at[at], g_recv.at[at], to)

    g_copy(0, twin).start()
    fetch(31, branch_i.at[0], branch)
    fetch(32, xhat_i.at[0], xhat.at[0])
    fetch(33, rstd_i.at[0], rstd.at[0])
    pump(9)

    through([right.at[7]], [7], emit_grad)
    for j in range(3):
        right[8 + j] = jnp.zeros_like(right[8 + j])
    for name in (25, 26, 27, 28, 29):
        have(name)

    def temporal_head(h):
        row = lax.broadcasted_iota(jnp.int32, (ROWS, ROWS), 0)
        col = lax.broadcasted_iota(jnp.int32, (ROWS, ROWS), 1)
        allowed = (row % 16 == col % 16) & (seg_in[0, :, 0:1] == seg_row[0:1, :])
        head_backward(
            h, qkv.at[0], qkv.at[1], qkv.at[2], grad, right.at[8], right.at[9], right.at[10], allowed
        )

    loop(8, temporal_head)
    pump(10)
    g_copy(0, twin).wait_recv()
    gains[1] = gains[0] + gain_at[0]
    g_copy(1, first).start()
    loop(8, lambda h: temporal_head(h + 8))
    pump(11)
    g_copy(1, first).wait_recv()
    gains[2] = gains[1] + gain_at[1]
    g_copy(2, second).start()
    for k in range(1, 8):
        x_wait(k)
    summed = wide32(text[0])
    for k in range(1, 8):
        summed = summed + wide32(text[k])
    text_o[...] = to_low(summed)
    for j in range(3):
        fetch(34 + j, qkvs_i.at[j], qkv.at[j])
    through([right.at[8], right.at[9], right.at[10]], [4, 5, 6], emit_work)
    have(31)

    def after_temporal(rows):
        seg = seg_in[0, rows, 0:1]
        value = work[rows, :]
        by_video(3, value, seg)
        by_video(4, value * wide32(xhat[1, rows, :]), seg)
        value = stream[rows, :] + norm_back(value, 1.0 + pick(4, seg), 1, rows)
        stream[rows, :] = value
        by_video(2, value * wide32(branch[rows, :]), seg)
        right[11, rows, :] = to_low(value * pick(2, seg))

    each_rows(32, after_temporal)

    through([right.at[11]], [3], emit_grad)

    def a_copy(k):
        to = (b + k) % 8
        part = grad.at[pl.ds(pl.multiple_of(32 * to, 32), 32)]
        return remote(part, back.at[b], a_send.at[k - 1], a_recv.at[k - 1], peers[k - 1])

    def a_wait(k):
        of = (b + 8 - k) % 8
        remote(grad.at[pl.ds(0, 32)], back.at[of], a_send.at[k - 1], a_recv.at[k - 1], peers[k - 1]).wait_recv()

    for k in range(1, 8):
        a_copy(k).start()
    back[b] = grad[pl.ds(pl.multiple_of(32 * b, 32), 32)]
    pump(12)
    g_copy(2, second).wait_recv()
    gains[3] = gains[2] + gain_at[2]
    for k in (1, 2, 3):
        g_copy(2 + k, near[k - 1]).start()
    for j in range(3):
        right[12 + j] = jnp.zeros_like(right[12 + j])
    for name in (32, 33, 34, 35, 36):
        have(name)
    for k in range(1, 8):
        a_wait(k)
    for k in range(8):
        for f in range(2):
            gframe[128 * f + 16 * k : 128 * f + 16 * k + 16, :] = back[k, 16 * f : 16 * f + 16, :]

    def spatial_heads(frame, start):
        rows = slice(128 * frame, 128 * frame + 128)

        def body(h):
            head_backward(
                h + start, qkv.at[0, rows], qkv.at[1, rows], qkv.at[2, rows], gframe.at[rows],
                right.at[12, rows], right.at[13, rows], right.at[14, rows], None,
            )

        loop(8, body)

    spatial_heads(0, 0)
    spatial_heads(0, 8)
    pump(14)
    spatial_heads(1, 0)
    spatial_heads(1, 8)
    pump(15)
    through([right.at[12], right.at[13], right.at[14]], [0, 1, 2], emit_work)
    pump(16)
    for k in range(1, 8):
        a_copy(k).wait_send()

    def after_spatial(i):
        rows = pl.ds(pl.multiple_of(16 * i, 16), 16)
        seg = seg_in[1, rows, 0:1]
        value = work[rows, :]
        by_video(0, value, seg)
        by_video(1, value * wide32(xhat[0, rows, :]), seg)
        value = to_low(norm_back(value, 1.0 + pick(1, seg), 0, rows))
        back[i % 8, pl.ds(pl.multiple_of(16 * (i // 8), 16), 16), :] = value

    loop(16, after_spatial)

    def u_copy(k):
        to = (b + k) % 8
        return remote(back.at[to], backp.at[b], u_send.at[k - 1], u_recv.at[k - 1], peers[k - 1])

    def u_wait(k):
        of = (b + 8 - k) % 8
        remote(back.at[0], backp.at[of], u_send.at[k - 1], u_recv.at[k - 1], peers[k - 1]).wait_recv()

    def m_copy(k):
        to = (b + k) % 8
        return remote(mod_out.at[to], mod.at[b], m_send.at[k - 1], m_recv.at[k - 1], peers[k - 1])

    def m_wait(k):
        of = (b + 8 - k) % 8
        remote(mod_out.at[0], mod.at[of], m_send.at[k - 1], m_recv.at[k - 1], peers[k - 1]).wait_recv()

    for k in range(1, 8):
        u_copy(k).start()
    backp[b] = back[b]
    for k in range(8):
        mod_out[k] = to_low(gm[:, 1280 * k : 1280 * k + MOD_WIN])
    for k in range(1, 8):
        m_copy(k).start()
    mod[b] = mod_out[b]
    pump(18)
    for k in range(1, 8):
        m_wait(k)
    summed = wide32(mod[0])
    for k in range(1, 8):
        summed = summed + wide32(mod[k])
    own = x * 2 + c
    seqs[own] = to_low(summed)
    places = [x * 2 + 1 - c, (1 - x) * 2 + c, (1 - x) * 2 + 1 - c]

    def q_copy(k, at):
        return remote(seqs.at[own], seqs.at[at], q_send.at[k], q_recv.at[k], across[k])

    for k in range(3):
        q_copy(k, own).start()
    for k in range(1, 8):
        u_wait(k)
    xin[...] = to_low(stream[...] + wide32(backp[...].reshape(ROWS, WIDE)))
    gtok[...] = to_low(linear(swap_rows(), xin[...]))
    for k in (1, 2, 3):
        g_copy(2 + k, near[k - 1]).wait_recv()
    gain_o[...] = gains[3] + gain_at[3] + gain_at[4] + gain_at[5]
    pump(BLOCKS + 4)
    for k in range(3):
        q_copy(k, places[k]).wait_recv()
    mod_o[...] = seqs[...]

    for now in (BLOCKS - 2, BLOCKS - 1):
        for l in range(4):
            copy0(now, l).wait_send()
        for l in range(2):
            copy1(now, l).wait_send()
        copy2(now).wait_send()
        for k in (1, 2, 3):
            copy3(now, k).wait_send()
        share_copy(now).wait()
    for k in range(1, 8):
        x_copy(k).wait_send()
        u_copy(k).wait_send()
        m_copy(k).wait_send()
    for k in range(3):
        q_copy(k, own).wait_send()
    for at, to in enumerate([twin, first, second] + near):
        g_copy(at, to).wait_send()


WEIGHT_ORDER = (11, 10, 13, 12, 15, 14, 17, 16, 9, 8, 7, 4, 5, 6, 3, 0, 1, 2)


def backward(*operands):
    low, full = jnp.bfloat16, jnp.float32
    dma = pltpu.SemaphoreType.DMA
    outs = [
        ((BLOCKS, WINDOW, WIDE), full),
        ((ROWS, WIDE), low),
        ((8, WIDE), full),
        ((TEXT, TEXT_WIN), low),
        ((4, 16, MOD_WIN), low),
    ]
    vmem = [
        ((2, WIDE, WIDE), low),
        ((11, WIDE, ROWS), low),
        ((15, ROWS, WIDE), low),
        ((3, ROWS, WIDE), low),
        ((2, ROWS, WIDE), low),
        ((2, ROWS, 128), full),
        ((ROWS, WIDE), low),
        ((2, ROWS, WIDE), low),
        ((8, MOD), full),
        ((8, WIDE), full),
        ((ROWS, WIDE), full),
        ((ROWS, WIDE), full),
        ((ROWS, WIDE), low),
        ((ROWS, WIDE), low),
        ((16, MOD), full),
        ((2, TEXT, WIDE), low),
        ((8, TEXT, TEXT_WIN), low),
        ((8, 16, MOD_WIN), low),
        ((8, 16, MOD_WIN), low),
        ((4, 16, MOD_WIN), low),
        ((4, 8, WIDE), full),
        ((6, 8, WIDE), full),
        ((ROWS, WIDE), low),
        ((8, 32, WIDE), low),
        ((8, 32, WIDE), low),
        ((2, 4, LINE, WIDE), low),
        ((4, 4, LINE, WIDE), low),
        ((2, 2, LINE, WIDE), low),
        ((4, 2, LINE, WIDE), low),
        ((2, 2, LINE, WIDE), low),
        ((2, LINE, WIDE), low),
        ((4, LINE, WIDE), low),
        ((2, LINE, WIDE), full),
        ((2, LINE, WIDE), low),
        ((4, 3, WINDOW, WIDE), low),
        ((2, LINE, WIDE), full),
        ((2, WINDOW, WIDE), full),
    ]
    return pl.pallas_call(
        backward_kernel,
        out_shape=[jax.ShapeDtypeStruct(*shape) for shape in outs],
        in_specs=[ANY] * 15 + [IN_VMEM] * 3,
        out_specs=[ANY] + [IN_VMEM] * 4,
        scratch_shapes=[pltpu.VMEM(*shape) for shape in vmem]
        + [
            dma((40,)), dma((2,)), dma((2, 4)), dma((4, 4)), dma((2, 2)), dma((4, 2)), dma((2,)), dma((4,)),
            dma((2, 3)), dma((4, 3)), dma((2,)), dma((7,)), dma((7,)), dma((7,)), dma((7,)), dma((7,)), dma((7,)),
            dma((7,)), dma((7,)), dma((3,)), dma((3,)), dma((6,)), dma((6,)),
        ],
        compiler_params=pltpu.CompilerParams(
            collective_id=1, has_side_effects=True, vmem_limit_bytes=63 * MIB
        ),
        name="backward",
    )(*operands)


TURN = np.arange(WIDE)[None, :] == (
    np.arange(WIDE).reshape(2, 2, 4, 2, SHARD).transpose(1, 0, 3, 2, 4).reshape(-1)
)[:, None]


def hidden_order(values):
    rows = values.shape[0]
    cut = values.reshape(rows, 2, 2, 4, 2, 4, SHARD)
    return cut.transpose(0, 5, 2, 1, 4, 3, 6).reshape(rows, 4 * WIDE)


def hidden_back(values):
    rows = values.shape[0]
    cut = values.reshape(rows, 4, 2, 2, 2, 4, SHARD)
    return cut.transpose(0, 3, 2, 5, 4, 1, 6).reshape(rows, 4 * WIDE)


def by_block(values):
    rows = values.shape[0]
    return values.reshape(rows, -1, WIDE).transpose(1, 0, 2)


def shards(
    tokens,
    segments,
    timesteps,
    caption,
    cotangent,
    ada_weight,
    ada_bias,
    spatial_in,
    spatial_out,
    temporal_in,
    temporal_out,
    cross_gain,
    cross_query,
    caption_proj,
    cross_out,
    hidden_in,
    hidden_out,
):
    frame_seg = segments[0]
    text_width = caption.shape[-1]
    caption_rows = caption[0].reshape(TEXT, text_width)
    blk = lax.axis_index("blk")
    seq = lax.axis_index("seq")
    zplace = blk // 2
    hidden_blocks = by_block(hidden_order(hidden_in))
    hidden_rows = hidden_out.reshape(4, SHARD, WIDE)
    stack = jnp.concatenate(
        [
            by_block(spatial_in),
            spatial_out[None],
            by_block(temporal_in),
            temporal_out[None],
            cross_query[None],
            cross_out[None],
        ]
        + [part[k][None] for k in range(4) for part in (hidden_blocks, hidden_rows)]
    )
    windows = lax.dynamic_update_slice(
        jnp.zeros((BLOCKS, WINDOW, WIDE), jnp.bfloat16), stack, (0, 4 * zplace, 0)
    )
    gain_in = lax.dynamic_update_slice(
        jnp.zeros((8, WIDE), jnp.float32),
        cross_gain.astype(jnp.float32)[None],
        (0, SHARD * (seq * 8 + blk)),
    )
    conditioning = to_low(jax.nn.silu(time_embedding(timesteps[0], WIDE)))
    mod_part = to_low(linear(conditioning, ada_weight) + ada_bias.astype(jnp.float32))
    mod_in = lax.dynamic_update_slice(
        jnp.zeros((16, MOD_WIN), jnp.bfloat16), mod_part, (0, 16 * blk)
    )
    text_part = to_low(linear(caption_rows, caption_proj))
    text_in = lax.dynamic_update_slice(
        jnp.zeros((TEXT, TEXT_WIN), jnp.bfloat16), text_part, (0, 32 * (blk % 4))
    )
    frames = frame_seg.astype(jnp.float32)
    own_frames = lax.dynamic_slice(frames, (2 * blk,), (2,))
    seg_in = jnp.broadcast_to(
        jnp.stack([jnp.repeat(frames, 16), jnp.repeat(own_frames, 128)])[:, :, None],
        (2, ROWS, 128),
    )
    seg_row = jnp.broadcast_to(jnp.repeat(frames, 16)[None], (8, ROWS))
    turn = jnp.asarray(TURN, jnp.bfloat16)
    wide, out, *kept = forward(
        windows,
        tokens.reshape(ROWS, WIDE),
        cotangent.reshape(ROWS, WIDE),
        gain_in,
        mod_in,
        text_in,
        seg_in,
        seg_row,
        turn,
    )
    spread, grad_tokens, grad_gain, grad_text, grad_mod = backward(
        wide, *kept, seg_in, seg_row, turn
    )
    shares = lax.dynamic_slice(spread, (0, 4 * zplace, 0), (BLOCKS, SHARD, WIDE))
    share_gain = lax.dynamic_slice(grad_gain, (0, SHARD * (seq * 8 + blk)), (1, SHARD))[0]
    text_low = lax.dynamic_slice(grad_text, (0, 32 * (blk % 4)), (TEXT, 2 * WIDE // 8))
    grad_caption = left_product(caption_rows, text_low)
    grad_caption = lax.psum(grad_caption.astype(jnp.bfloat16), "seq").astype(jnp.float32)
    all_mod = lax.dynamic_slice(grad_mod, (0, 0, 16 * blk), (4, 2, MOD // 8)).reshape(8, MOD // 8)
    all_steps = lax.all_gather(timesteps[0], "seq", axis=0, tiled=True)
    all_cond = to_low(jax.nn.silu(time_embedding(all_steps, WIDE)))
    grad_ada_w = left_product(all_cond, all_mod)
    grad_ada_b = jnp.sum(all_mod.astype(jnp.float32), axis=0)

    def joined(first, count):
        return shares[first : first + count].transpose(1, 0, 2).reshape(SHARD, count * WIDE)

    return (
        out.reshape(tokens.shape),
        grad_tokens.reshape(tokens.shape),
        grad_ada_w,
        grad_ada_b,
        joined(15, 3),
        shares[14],
        joined(11, 3),
        shares[10],
        share_gain,
        shares[9],
        grad_caption,
        shares[8],
        hidden_back(joined(4, 4)),
        shares[0:4].reshape(4 * SHARD, WIDE),
    )


def solution(mesh):
    fast = dict(mesh.shape) == {"seq": 4, "blk": 8}
    return jax.shard_map(
        shards if fast else general_shards,
        mesh=mesh,
        in_specs=(
            P("seq", "blk", None, None),
            P("seq", None),
            P("seq", None),
            P("seq", None, None, None),
            P("seq", "blk", None, None),
            P(None, "blk"),
            P("blk"),
            P(("seq", "blk"), None),
            P(("seq", "blk"), None),
            P(("seq", "blk"), None),
            P(("seq", "blk"), None),
            P(("seq", "blk")),
            P(("seq", "blk"), None),
            P(None, "blk"),
            P(("seq", "blk"), None),
            P(("seq", "blk"), None),
            P(("seq", "blk"), None),
        ),
        out_specs=(
            P("seq", "blk", None, None),
            P("seq", "blk", None, None),
            P(None, "blk"),
            P("blk"),
            P(("seq", "blk"), None),
            P(("seq", "blk"), None),
            P(("seq", "blk"), None),
            P(("seq", "blk"), None),
            P(("seq", "blk")),
            P(("seq", "blk"), None),
            P(None, "blk"),
            P(("seq", "blk"), None),
            P(("seq", "blk"), None),
            P(("seq", "blk"), None),
        ),
        check_vma=False,
    )
```

```python
import math

import jax
import jax.numpy as jnp
import numpy as np
from jax import lax
from jax.experimental import pallas as pl
from jax.experimental.pallas import tpu as pltpu
from jax.sharding import PartitionSpec as P

H = 16
E = 72
L = 120


EPSILON = 1e-06
MASKED = -1e30


def to_low(values):
    return values.astype(jnp.bfloat16)


def linear(left, right):
    return jnp.dot(left, right, preferred_element_type=jnp.float32)


def left_product(left, right):
    return lax.dot_general(
        left, right, (((0,), (0,)), ((), ())), preferred_element_type=jnp.float32
    )


def right_product(left, right):
    return lax.dot_general(
        left, right, (((1,), (1,)), ((), ())), preferred_element_type=jnp.float32
    )


def normalize(values):
    center = values - jnp.mean(values, axis=-1, keepdims=True)
    return center * lax.rsqrt(jnp.mean(center * center, axis=-1, keepdims=True) + EPSILON)


def modulate(values, shift_rows, scale_rows):
    return normalize(values) * (1.0 + scale_rows) + shift_rows


def gain_norm(values, gain_row):
    return normalize(values) * gain_row


def gelu_tanh(values):
    return jax.nn.gelu(values, approximate=True)


def softmax_rows(scores):
    shifted = jnp.exp(scores - jnp.max(scores, axis=-1, keepdims=True))
    return shifted / jnp.sum(shifted, axis=-1, keepdims=True)


def softmax_with_total(scores):
    top = jnp.max(scores, axis=-1, keepdims=True)
    shifted = jnp.exp(scores - top)
    total = jnp.sum(shifted, axis=-1, keepdims=True)
    return (shifted / total, (top + jnp.log(total))[..., 0])


def softmax_back(probs, grad_probs):
    return probs * (grad_probs - jnp.sum(grad_probs * probs, axis=-1, keepdims=True))


def time_embedding(step_ids, model_width):
    half_width = model_width // 2
    frequency = jnp.exp(
        -math.log(10000.0) * jnp.arange(half_width).astype(jnp.float32) / half_width
    )
    angles = step_ids.astype(jnp.float32)[:, None] * frequency[None, :]
    return jnp.concatenate([jnp.cos(angles), jnp.sin(angles)], axis=1)


def general_shards(
    tokens,
    segments,
    timesteps,
    caption,
    cotangent,
    ada_weight,
    ada_bias,
    spatial_in,
    spatial_out,
    temporal_in,
    temporal_out,
    cross_gain,
    cross_query,
    caption_proj,
    cross_out,
    hidden_in,
    hidden_out,
):
    inputs = tokens[0].astype(jnp.float32)
    patch_dev, frames, model_width = inputs.shape
    token_rows = patch_dev * frames
    head_count = H
    head_size = E
    score_scale = E ** (-0.5)
    frame_seg = segments[0]
    step_ids = timesteps[0]
    seg_count, text_len, text_width = caption.shape[1:]
    text_keys = seg_count * text_len
    caption_rows = caption[0].reshape(text_keys, text_width)
    grad_out = cotangent[0].astype(jnp.float32)
    gathered = (
        lax.all_gather(spatial_in, ("seq", "blk"), axis=0, tiled=True),
        lax.all_gather(spatial_out, ("seq", "blk"), axis=0, tiled=True),
        lax.all_gather(temporal_in, ("seq", "blk"), axis=0, tiled=True),
        lax.all_gather(temporal_out, ("seq", "blk"), axis=0, tiled=True),
        lax.all_gather(cross_gain, ("seq", "blk"), axis=0, tiled=True),
        lax.all_gather(cross_query, ("seq", "blk"), axis=0, tiled=True),
        lax.all_gather(cross_out, ("seq", "blk"), axis=0, tiled=True),
        lax.all_gather(hidden_in, ("seq", "blk"), axis=0, tiled=True),
        lax.all_gather(hidden_out, ("seq", "blk"), axis=0, tiled=True),
    )
    (
        wide_sin,
        wide_sout,
        wide_tin,
        wide_tout,
        gain_low,
        wide_query,
        wide_cout,
        wide_hin,
        wide_hout,
    ) = gathered
    gain_row = gain_low.astype(jnp.float32)
    conditioning = to_low(jax.nn.silu(time_embedding(step_ids, model_width)))
    mod_part = to_low(linear(conditioning, ada_weight) + ada_bias.astype(jnp.float32))
    text_part = to_low(linear(caption_rows, caption_proj))
    modulation, memory = (
        lax.all_gather(mod_part, "blk", axis=1, tiled=True),
        lax.all_gather(text_part, "blk", axis=1, tiled=True),
    )
    choose = frame_seg[:, None] == jnp.arange(seg_count, dtype=jnp.int32)[None, :]
    frame_mod = linear(choose.astype(jnp.bfloat16), modulation)
    pieces = [frame_mod[:, index * model_width : (index + 1) * model_width] for index in range(9)]
    (
        shift_one,
        scale_one,
        gate_one,
        shift_two,
        scale_two,
        gate_two,
        shift_three,
        scale_three,
        gate_three,
    ) = pieces
    spatial_input = to_low(modulate(inputs, shift_one, scale_one)).reshape(token_rows, model_width)
    spatial_qkv = to_low(linear(spatial_input, wide_sin)).reshape(
        patch_dev, frames, 3 * model_width
    )
    query_s = spatial_qkv[..., :model_width].reshape(patch_dev, frames, head_count, head_size)
    local_kv = spatial_qkv[..., model_width:]
    whole_kv = lax.all_gather(local_kv, "blk", axis=0, tiled=True)

    def split_kv(both):
        count = both.shape[0]
        return (
            both[..., :model_width].reshape(count, frames, head_count, head_size),
            both[..., model_width:].reshape(count, frames, head_count, head_size),
        )

    def spatial_probs(key_all):
        scores = jnp.einsum("pfhe,qfhe->fhpq", query_s, key_all, preferred_element_type=jnp.float32)
        return softmax_with_total(scores * score_scale)

    key_s, value_s = split_kv(whole_kv)
    probs_s, log_total_s = spatial_probs(key_s)
    probs_s_low = to_low(probs_s)
    attn_s = to_low(
        jnp.einsum(
            "fhpq,qfhe->pfhe", probs_s_low, value_s, preferred_element_type=jnp.float32
        ).reshape(token_rows, model_width)
    )
    branch_s = linear(attn_s, wide_sout).reshape(patch_dev, frames, model_width)
    after_one = inputs + gate_one * branch_s
    temporal_input = to_low(modulate(after_one, shift_two, scale_two)).reshape(
        token_rows, model_width
    )
    temporal_qkv = to_low(linear(temporal_input, wide_tin)).reshape(
        patch_dev, frames, 3, head_count, head_size
    )
    query_t = temporal_qkv[:, :, 0]
    key_t = temporal_qkv[:, :, 1]
    value_t = temporal_qkv[:, :, 2]
    same_seg = frame_seg[:, None] == frame_seg[None, :]
    scores_t = (
        jnp.einsum("pfhe,pghe->phfg", query_t, key_t, preferred_element_type=jnp.float32)
        * score_scale
    )
    probs_t = softmax_rows(jnp.where(same_seg[None, None], scores_t, MASKED))
    probs_t_low = to_low(probs_t)
    attn_t = to_low(
        jnp.einsum(
            "phfg,pghe->pfhe", probs_t_low, value_t, preferred_element_type=jnp.float32
        ).reshape(token_rows, model_width)
    )
    branch_t = linear(attn_t, wide_tout).reshape(patch_dev, frames, model_width)
    after_two = after_one + gate_two * branch_t
    cross_input = to_low(gain_norm(after_two, gain_row)).reshape(token_rows, model_width)
    query_c = to_low(linear(cross_input, wide_query)).reshape(
        patch_dev, frames, head_count, head_size
    )
    key_c = memory[:, :model_width].reshape(text_keys, head_count, head_size)
    value_c = memory[:, model_width:].reshape(text_keys, head_count, head_size)
    key_seg = jnp.arange(text_keys, dtype=jnp.int32) // text_len
    allowed = frame_seg[:, None] == key_seg[None, :]
    scores_c = (
        jnp.einsum("pfhe,khe->pfhk", query_c, key_c, preferred_element_type=jnp.float32)
        * score_scale
    )
    probs_c = softmax_rows(jnp.where(allowed[None, :, None, :], scores_c, MASKED))
    probs_c_low = to_low(probs_c)
    attn_c = to_low(
        jnp.einsum(
            "pfhk,khe->pfhe", probs_c_low, value_c, preferred_element_type=jnp.float32
        ).reshape(token_rows, model_width)
    )
    branch_c = linear(attn_c, wide_cout).reshape(patch_dev, frames, model_width)
    after_three = after_two + branch_c
    mlp_input = to_low(modulate(after_three, shift_three, scale_three)).reshape(
        token_rows, model_width
    )
    pre_act = linear(mlp_input, wide_hin)
    post_act = to_low(gelu_tanh(pre_act))
    branch_m = linear(post_act, wide_hout).reshape(patch_dev, frames, model_width)
    result = after_three + gate_three * branch_m
    grad_gate_three = jnp.sum(grad_out * branch_m, axis=0)
    grad_four = to_low(grad_out * gate_three).reshape(token_rows, model_width)
    grad_hout = left_product(post_act, grad_four)
    grad_post = right_product(grad_four, wide_hout)
    gelu_pull = jax.vjp(gelu_tanh, pre_act)[1]
    grad_pre = to_low(gelu_pull(grad_post)[0])
    grad_hin = left_product(mlp_input, grad_pre)
    grad_mlp_in = right_product(grad_pre, wide_hin).reshape(patch_dev, frames, model_width)
    mlp_pull = jax.vjp(modulate, after_three, shift_three, scale_three)[1]
    back_three, grad_shift_three, grad_scale_three = mlp_pull(grad_mlp_in)
    grad_three = grad_out + back_three
    grad_cross_branch = to_low(grad_three).reshape(token_rows, model_width)
    grad_cout = left_product(attn_c, grad_cross_branch)
    grad_attn_c = to_low(right_product(grad_cross_branch, wide_cout)).reshape(
        patch_dev, frames, head_count, head_size
    )
    grad_probs_c = jnp.einsum(
        "pfhe,khe->pfhk", grad_attn_c, value_c, preferred_element_type=jnp.float32
    )
    grad_scores_c = to_low(softmax_back(probs_c, grad_probs_c))
    grad_query_c = to_low(
        jnp.einsum("pfhk,khe->pfhe", grad_scores_c, key_c, preferred_element_type=jnp.float32)
        * score_scale
    ).reshape(token_rows, model_width)
    grad_key_c = (
        jnp.einsum("pfhk,pfhe->khe", grad_scores_c, query_c, preferred_element_type=jnp.float32)
        * score_scale
    )
    grad_value_c = jnp.einsum(
        "pfhk,pfhe->khe", probs_c_low, grad_attn_c, preferred_element_type=jnp.float32
    )
    grad_memory = jnp.concatenate(
        [grad_key_c.reshape(text_keys, model_width), grad_value_c.reshape(text_keys, model_width)],
        axis=1,
    )
    grad_wquery = left_product(cross_input, grad_query_c)
    grad_cross_in = right_product(grad_query_c, wide_query).reshape(patch_dev, frames, model_width)
    cross_pull = jax.vjp(gain_norm, after_two, gain_row)[1]
    back_two, grad_gain = cross_pull(grad_cross_in)
    grad_two = grad_three + back_two
    grad_gate_two = jnp.sum(grad_two * branch_t, axis=0)
    grad_temporal_branch = to_low(grad_two * gate_two).reshape(token_rows, model_width)
    grad_tout = left_product(attn_t, grad_temporal_branch)
    grad_attn_t = to_low(right_product(grad_temporal_branch, wide_tout)).reshape(
        patch_dev, frames, head_count, head_size
    )
    grad_probs_t = jnp.einsum(
        "pfhe,pghe->phfg", grad_attn_t, value_t, preferred_element_type=jnp.float32
    )
    grad_scores_t = to_low(softmax_back(probs_t, grad_probs_t))
    grad_query_t = (
        jnp.einsum("phfg,pghe->pfhe", grad_scores_t, key_t, preferred_element_type=jnp.float32)
        * score_scale
    )
    grad_key_t = (
        jnp.einsum("phfg,pfhe->pghe", grad_scores_t, query_t, preferred_element_type=jnp.float32)
        * score_scale
    )
    grad_value_t = jnp.einsum(
        "phfg,pfhe->pghe", probs_t_low, grad_attn_t, preferred_element_type=jnp.float32
    )
    grad_qkv_t = to_low(jnp.stack([grad_query_t, grad_key_t, grad_value_t], axis=2)).reshape(
        token_rows, 3 * model_width
    )
    grad_tin = left_product(temporal_input, grad_qkv_t)
    grad_temporal_in = right_product(grad_qkv_t, wide_tin).reshape(patch_dev, frames, model_width)
    temporal_pull = jax.vjp(modulate, after_one, shift_two, scale_two)[1]
    back_one, grad_shift_two, grad_scale_two = temporal_pull(grad_temporal_in)
    grad_one = grad_two + back_one
    grad_gate_one = jnp.sum(grad_one * branch_s, axis=0)
    grad_spatial_branch = to_low(grad_one * gate_one).reshape(token_rows, model_width)
    grad_sout = left_product(attn_s, grad_spatial_branch)
    grad_attn_s = to_low(right_product(grad_spatial_branch, wide_sout)).reshape(
        patch_dev, frames, head_count, head_size
    )
    back_kv = lax.all_gather(local_kv, "blk", axis=0, tiled=True)
    back_key, back_value = split_kv(back_kv)
    back_probs = spatial_probs(back_key)[0]
    back_probs_low = to_low(back_probs)
    grad_probs_s = jnp.einsum(
        "pfhe,qfhe->fhpq", grad_attn_s, back_value, preferred_element_type=jnp.float32
    )
    row_delta = jnp.sum(grad_probs_s * back_probs, axis=-1, keepdims=True)
    grad_scores_s = to_low(back_probs * (grad_probs_s - row_delta))
    grad_query_s = (
        jnp.einsum("fhpq,qfhe->pfhe", grad_scores_s, back_key, preferred_element_type=jnp.float32)
        * score_scale
    )
    count = lax.axis_size("blk") * patch_dev
    grad_key = (
        jnp.einsum("fhpq,pfhe->qfhe", grad_scores_s, query_s, preferred_element_type=jnp.float32)
        * score_scale
    )
    grad_value = jnp.einsum(
        "fhpq,pfhe->qfhe", back_probs_low, grad_attn_s, preferred_element_type=jnp.float32
    )
    grad_kv = to_low(
        lax.psum_scatter(
            jnp.concatenate(
                [
                    grad_key.reshape(count, frames, model_width),
                    grad_value.reshape(count, frames, model_width),
                ],
                axis=2,
            ).astype(jnp.bfloat16),
            "blk",
            scatter_dimension=0,
            tiled=True,
        ).astype(jnp.float32)
    )
    grad_qkv_s = jnp.concatenate(
        [to_low(grad_query_s).reshape(patch_dev, frames, model_width), grad_kv], axis=2
    ).reshape(token_rows, 3 * model_width)
    grad_sin = left_product(spatial_input, grad_qkv_s)
    grad_spatial_in = right_product(grad_qkv_s, wide_sin).reshape(patch_dev, frames, model_width)
    spatial_pull = jax.vjp(modulate, inputs, shift_one, scale_one)[1]
    back_zero, grad_shift_one, grad_scale_one = spatial_pull(grad_spatial_in)
    grad_input = grad_one + back_zero
    grad_frame_mod = jnp.concatenate(
        [
            grad_shift_one,
            grad_scale_one,
            grad_gate_one,
            grad_shift_two,
            grad_scale_two,
            grad_gate_two,
            grad_shift_three,
            grad_scale_three,
            grad_gate_three,
        ],
        axis=1,
    )
    grad_mod_local = lax.dot_general(
        choose.astype(jnp.float32),
        grad_frame_mod,
        (((0,), (0,)), ((), ())),
        precision=lax.Precision.HIGHEST,
    )
    grad_mod_part, grad_memory_part = (
        lax.psum_scatter(
            grad_mod_local.astype(jnp.bfloat16), "blk", scatter_dimension=1, tiled=True
        ).astype(jnp.float32),
        lax.psum_scatter(
            grad_memory.astype(jnp.bfloat16), "blk", scatter_dimension=1, tiled=True
        ).astype(jnp.float32),
    )
    grad_mod_low = to_low(grad_mod_part)
    grad_ada_w = left_product(conditioning, grad_mod_low)
    grad_ada_b = jnp.sum(grad_mod_low.astype(jnp.float32), axis=0)
    grad_caption = left_product(caption_rows, to_low(grad_memory_part))
    grad_ada_w, grad_ada_b, grad_caption = (
        lax.psum(grad_ada_w.astype(jnp.bfloat16), "seq").astype(jnp.float32),
        lax.psum(grad_ada_b.astype(jnp.bfloat16), "seq").astype(jnp.float32),
        lax.psum(grad_caption.astype(jnp.bfloat16), "seq").astype(jnp.float32),
    )
    shares = (
        lax.psum_scatter(grad_sin, ("seq", "blk"), scatter_dimension=0, tiled=True),
        lax.psum_scatter(grad_sout, ("seq", "blk"), scatter_dimension=0, tiled=True),
        lax.psum_scatter(grad_tin, ("seq", "blk"), scatter_dimension=0, tiled=True),
        lax.psum_scatter(grad_tout, ("seq", "blk"), scatter_dimension=0, tiled=True),
        lax.psum_scatter(grad_gain, ("seq", "blk"), scatter_dimension=0, tiled=True),
        lax.psum_scatter(grad_wquery, ("seq", "blk"), scatter_dimension=0, tiled=True),
        lax.psum_scatter(grad_cout, ("seq", "blk"), scatter_dimension=0, tiled=True),
        lax.psum_scatter(grad_hin, ("seq", "blk"), scatter_dimension=0, tiled=True),
        lax.psum_scatter(grad_hout, ("seq", "blk"), scatter_dimension=0, tiled=True),
    )
    (
        share_sin,
        share_sout,
        share_tin,
        share_tout,
        share_gain,
        share_query,
        share_cout,
        share_hin,
        share_hout,
    ) = shares
    return (
        to_low(result)[None],
        to_low(grad_input)[None],
        grad_ada_w,
        grad_ada_b,
        share_sin,
        share_sout,
        share_tin,
        share_tout,
        share_gain,
        share_query,
        grad_caption,
        share_cout,
        share_hin,
        share_hout,
    )


MESH = pl.DeviceIdType.MESH
BLOCKS = 18
LINES = 8
SHARD = 36
LINE = 4 * SHARD
WINDOW = 48
WIDE = LINES * LINE
MIB = 2**20


def place():
    seq = lax.axis_index("seq")
    blk = lax.axis_index("blk")
    x, c = seq // 2, seq % 2
    z, y = blk // 2, blk % 2
    x1, y1 = x + (1 - 2 * x) * (1 - c), y + (1 - 2 * y) * c
    x2, y2 = x + (1 - 2 * x) * c, y + (1 - 2 * y) * (1 - c)
    return x, c, y, z, x1, y1, x2, y2


def device(x, c, y, z):
    return {"seq": x * 2 + c, "blk": z * 2 + y}


def line_of(c, x, y):
    return (c * 2 + x) * 2 + y


def remote(src, dst, send_sem, recv_sem, where):
    return pltpu.make_async_remote_copy(
        src_ref=src,
        dst_ref=dst,
        send_sem=send_sem,
        recv_sem=recv_sem,
        device_id=where,
        device_id_type=MESH,
    )


def greet(others):
    barrier = pltpu.get_barrier_semaphore()
    for other in others:
        pl.semaphore_signal(barrier, inc=1, device_id=other, device_id_type=MESH)
    pl.semaphore_wait(barrier, len(others))


def left_at(t):
    at = jnp.minimum(t, 4)
    for first in (8, 9, 10, 11, 14, 15):
        at = at + jnp.where(t >= first, 1, 0)
    return at


def right_at(t):
    return jnp.maximum(t - 3, 0)


ROWS = 256
TEXT = 256
TEXT_WIN = 384
MOD = 9 * WIDE
MOD_WIN = 1408
LEFT_SEM, SLOPE_SEM, SAVE_SEMS = 40, 42, 44
TILE = 384
SCALE = E ** (-0.5)


def nt(left, right):
    return lax.dot_general(
        left, right, (((1,), (1,)), ((), ())), preferred_element_type=jnp.float32
    )


def wide32(values):
    return values.astype(jnp.float32)


def loop(count, body):
    def step(index, carry):
        body(index)
        return carry

    lax.fori_loop(0, count, step, 0)


def each_rows(size, body, total=ROWS):
    loop(total // size, lambda i: body(pl.ds(pl.multiple_of(i * size, size), size)))


def each_cols(body):
    loop(WIDE // TILE, lambda i: body(pl.ds(pl.multiple_of(i * TILE, TILE), TILE)))


def swap_rows():
    row = lax.broadcasted_iota(jnp.int32, (ROWS, ROWS), 0)
    col = lax.broadcasted_iota(jnp.int32, (ROWS, ROWS), 1)
    return to_low((((row & 15) << 4) + (row >> 4) == col).astype(jnp.float32))


def head_window(h):
    base = h * E
    start = jnp.minimum(base // 128, 7) * 128
    lane = lax.broadcasted_iota(jnp.int32, (1, 256), 1)
    on = (lane >= base - start) & (lane < base - start + E)
    return pl.ds(pl.multiple_of(start, 128), 256), on.astype(jnp.float32)


def soft(scores, bias, mask):
    scores = scores * SCALE
    if bias is not None:
        scores = scores + bias
    powers = jnp.exp(scores - jnp.max(scores, axis=-1, keepdims=True))
    probs = powers * (1.0 / jnp.sum(powers, axis=-1, keepdims=True))
    return probs if mask is None else probs * mask


def chains(h, groups):
    return [(window, rows, keys) for window in (head_window(h), head_window(h + H // 2)) for rows, keys in groups]


def split_rows(values, jobs):
    start = 0
    parts = []
    for _, rows, _ in jobs:
        size = rows.stop - rows.start
        parts.append(values[start : start + size])
        start += size
    return parts


def heads_forward(h, query, key, value, attn, groups, bias, mask):
    jobs = chains(h, groups)
    scores = [nt(query[rows, lanes] * to_low(on), key[keys, lanes]) for (lanes, on), rows, keys in jobs]
    probs = split_rows(to_low(soft(jnp.concatenate(scores), bias, mask)), jobs)
    parts = [linear(prob, value[keys, lanes]) * on for prob, ((lanes, on), rows, keys) in zip(probs, jobs)]
    for part, ((lanes, on), rows, keys) in zip(parts, jobs):
        attn[rows, lanes] = attn[rows, lanes] + to_low(part)


HALVES = [(slice(0, 128), slice(0, 128)), (slice(128, 256), slice(128, 256))]
VIDEOS = [(slice(0, 144), slice(0, 128)), (slice(112, 256), slice(128, 256))]


def regroup(back):
    row = lax.broadcasted_iota(jnp.int32, (ROWS, ROWS), 0)
    col = lax.broadcasted_iota(jnp.int32, (ROWS, ROWS), 1)
    if back:
        source = (((row >> 3) & 1) << 7) + ((row >> 4) << 3) + (row & 7)
    else:
        source = (((row >> 3) & 15) << 4) + ((row >> 7) << 3) + (row & 7)
    return to_low((source == col).astype(jnp.float32))


def temporal_bias(seg_in, seg_row):
    row = lax.broadcasted_iota(jnp.int32, (128, 128), 0)
    col = lax.broadcasted_iota(jnp.int32, (128, 128), 1)
    allowed = ((row & 7) == (col & 7)) & (seg_in[2, 0:128, 0:1] == seg_row[0:1, 0:128])
    return jnp.where(allowed, 0.0, MASKED)


def cross_bias():
    col = lax.broadcasted_iota(jnp.int32, (1, 128), 1)
    return jnp.where(col < L, 0.0, MASKED)


def cross_rows(seg_in):
    both = [1.0 - seg_in[0, 0:144, 0:1], seg_in[0, 112:256, 0:1]]
    return jnp.concatenate(both + both)


def blk_peers(x, c, b):
    return [device(x, c, (b + k) % 2, ((b + k) % 8) // 2) for k in range(1, 8)]


def forward_kernel(
    src, tok, cot, gain_in, mod_in, text_in, seg_in, seg_row, turn,
    wide, out, left_o, qkvs_o, qkvt_o, qc_o, mem_o, xhat_o, rstd_o, branch_o, slope_o, gfour_o, cot_o, mods_o, gate_o, gain_o,
    parts, lines, weights, tokp, cotp, tokf, xin, xp, left, qkvs, qkvt, qc, mem, text, mod, mods, xhat, rstd, branch, branchw, bias,
    stream, attnf, attnp, post, slope, gfour, gains, gain_at, gate,
    z_send, z_recv, l_send, l_recv, own_sem, w_sem, t_send, t_recv, a_send, a_recv, m_send, m_recv, x_send, x_recv,
    g_send, g_recv, save_sem,
):
    x, c, y, z, x1, y1, x2, y2 = place()
    b = z * 2 + y
    near = [device(x, c, y, (z + k) % 4) for k in (1, 2, 3)]
    first, second, twin = device(x1, c, y1, z), device(x2, c, y2, z), device(x, 1 - c, y, z)
    peers = blk_peers(x, c, b)
    greet(peers + [device(1 - x, c, y, z), twin])
    mine, line1 = line_of(c, x, y), line_of(c, x1, y1)
    line2, line3 = line_of(c, x2, y2), line_of(c, 1 - x, 1 - y)
    other = [line_of(1 - c, x, y), line_of(1 - c, x2, y2), line_of(1 - c, x1, y1), line_of(1 - c, 1 - x, 1 - y)]

    def z_copy(t, k):
        return remote(src.at[t], parts.at[t, z], z_send.at[t, k - 1], z_recv.at[t, k - 1], near[k - 1])

    def z_wait(t, k):
        return remote(src.at[t], parts.at[t, (z + 4 - k) % 4], z_send.at[t, k - 1], z_recv.at[t, k - 1], near[k - 1])

    def wide_line(t, line):
        return wide.at[t, pl.ds(pl.multiple_of(line * LINE, 16), LINE)]

    def own(t):
        return pltpu.make_async_copy(lines.at[t], wide_line(t, mine), own_sem.at[t])

    def line_copy(t, to, line, index, where):
        return remote(to, wide_line(t, line), l_send.at[t, index], l_recv.at[t, index], where)

    def sends(t, index):
        line, where = (
            (mine, first), (mine, second), (mine, twin), (line1, second),
            (line1, twin), (line2, twin), (line3, twin),
        )[index]
        from_here = lines.at[t] if index < 3 else wide_line(t, line)
        return line_copy(t, from_here, line, index, where)

    def arrives(t, line, index):
        line_copy(t, wide_line(t, line), line, index, first).wait_recv()

    def tick(t):
        @pl.when(t < BLOCKS)
        def _():
            for k in (1, 2, 3):
                z_copy(t, k).start()
            parts[t, z] = src[t]

        @pl.when((t >= 2) & (t < BLOCKS + 2))
        def _():
            now = t - 2
            for k in (1, 2, 3):
                z_wait(now, k).wait_recv()
            w0, w1, w2, w3 = [parts[now, k] for k in range(4)]
            lines[now, 0:32] = w0[0:32]
            lines[now, 32:48] = w0[32:48] + w1[0:16]
            lines[now, 48:64] = w1[16:32]
            lines[now, 64:80] = w1[32:48] + w2[0:16]
            lines[now, 80:96] = w2[16:32]
            lines[now, 96:112] = w2[32:48] + w3[0:16]
            lines[now, 112:144] = w3[16:48]
            for index in range(3):
                sends(now, index).start()
            own(now).start()

        @pl.when((t >= 4) & (t < BLOCKS + 4))
        def _():
            now = t - 4
            arrives(now, line1, 0)
            for index in (3, 4):
                sends(now, index).start()

        @pl.when(t >= 5)
        def _():
            now = t - 5
            arrives(now, line2, 1)
            sends(now, 5).start()
            arrives(now, line3, 3)
            sends(now, 6).start()

    done = [0]

    def pump(until):
        until = min(until, BLOCKS + 5)
        if until > done[0]:
            start = done[0]
            loop(until - start, lambda i: tick(i + start))
            done[0] = until

    def poke():
        pump(done[0] + 1)

    def load(block):
        pump(block + 6)
        for line, index in zip(other, (2, 4, 5, 6)):
            arrives(block, line, index)
        own(block).wait()
        copy = pltpu.make_async_copy(wide.at[block], weights.at[block % 2], w_sem.at[block % 2])
        copy.start()
        copy.wait()

    def times(values, block, emit):
        def tile(cols):
            emit(cols, linear(values[...], weights[block % 2, :, cols]))

        each_cols(tile)

    saves = []
    held = {}

    def save(from_ref, to_ref, name=None):
        if name is None:
            name = len(saves)
            saves.append(name)
        held[name] = pltpu.make_async_copy(from_ref, to_ref, save_sem.at[name])
        held[name].start()

    def settle(name):
        if name in held:
            held.pop(name).wait()

    def turned(values, index):
        slot = index % 2
        settle(LEFT_SEM + slot)

        def tile(cols):
            xp[:, cols] = to_low(nt(values[...], turn[cols, :]))
            left[slot, cols, :] = to_low(nt(turn[cols, :], values[...]))

        each_cols(tile)
        save(left.at[slot], left_o.at[index], LEFT_SEM + slot)

    swap = swap_rows()
    tokp[...] = to_low(linear(swap, tok[...]))
    cotp[...] = to_low(linear(swap, cot[...]))

    def t_copy(k):
        to = (b + k) % 8
        part = tokp.at[pl.ds(pl.multiple_of(32 * to, 32), 32)]
        return remote(part, tokf.at[b], t_send.at[k - 1], t_recv.at[k - 1], peers[k - 1])

    def t_wait(k):
        of = (b + 8 - k) % 8
        remote(tokp.at[pl.ds(0, 32)], tokf.at[of], t_send.at[k - 1], t_recv.at[k - 1], peers[k - 1]).wait_recv()

    def m_copy(k, at):
        return remote(mod_in, mod.at[at], m_send.at[k - 1], m_recv.at[k - 1], peers[k - 1])

    def x_copy(k, at):
        return remote(text_in, text.at[at], x_send.at[k - 1], x_recv.at[k - 1], peers[k - 1])

    for k in range(1, 8):
        t_copy(k).start()
        m_copy(k, b).start()
        x_copy(k, b).start()
    tokf[b] = tokp[pl.ds(pl.multiple_of(32 * b, 32), 32)]
    mod[b] = mod_in[...]
    text[b] = text_in[...]

    def g_copy(at, from_at, to):
        return remote(gains.at[from_at], gain_at.at[at], g_send.at[at], g_recv.at[at], to)

    gains[0] = gain_in[...]
    g_copy(0, 0, twin).start()
    save(cotp, cot_o)
    pump(3)

    for k in range(1, 8):
        m_copy(k, (b + 8 - k) % 8).wait_recv()
    mods[...] = jnp.zeros_like(mods)
    for k in range(8):
        lanes = slice(1280 * k, 1280 * k + MOD_WIN)
        mods[:, lanes] = mods[:, lanes] + wide32(mod[k])[0:8]
    save(mods, mods_o)

    g_copy(0, 0, twin).wait_recv()
    gains[1] = gains[0] + gain_at[0]
    g_copy(1, 1, first).start()

    def pick(piece, seg):
        lanes = slice(WIDE * piece, WIDE * piece + WIDE)
        return jnp.where(seg > 0.5, mods[1:2, lanes], mods[0:1, lanes])

    def normal(values, rows, index):
        center = values - jnp.mean(values, axis=-1, keepdims=True)
        factor = lax.rsqrt(jnp.mean(center * center, axis=-1, keepdims=True) + EPSILON)
        scaled = center * factor
        xhat[index, rows, :] = to_low(scaled)
        rstd[index, rows, :] = jnp.broadcast_to(factor, (factor.shape[0], 128))
        return scaled

    for k in range(1, 8):
        t_wait(k)
    g_copy(1, 1, first).wait_recv()
    gains[2] = gains[1] + gain_at[1]
    g_copy(2, 2, second).start()

    def spatial_rows(i):
        seg = jnp.concatenate([seg_in[1, 0:16, 0:1], seg_in[1, 128:144, 0:1]])
        values = wide32(tokf[i])
        center = values - jnp.mean(values, axis=-1, keepdims=True)
        factor = lax.rsqrt(jnp.mean(center * center, axis=-1, keepdims=True) + EPSILON)
        scaled = center * factor
        ready = to_low(scaled * (1.0 + pick(1, seg)) + pick(0, seg))
        low = to_low(scaled)
        spread = jnp.broadcast_to(factor, (32, 128))
        for f in range(2):
            rows = pl.ds(pl.multiple_of(128 * f + 16 * i, 16), 16)
            part = slice(16 * f, 16 * f + 16)
            xhat[0, rows, :] = low[part]
            rstd[0, rows, :] = spread[part]
            xin[rows, :] = ready[part]

    loop(8, spatial_rows)
    save(xhat.at[0], xhat_o.at[0])
    save(rstd.at[0], rstd_o.at[0])
    turned(xin, 10)
    for j in range(3):
        load(j)

        def emit(cols, value, j=j):
            qkvs[j, :, cols] = to_low(value)

        times(xp, j, emit)
    save(qkvs, qkvs_o)
    g_copy(2, 2, second).wait_recv()
    gains[3] = gains[2] + gain_at[2]
    for k in (1, 2, 3):
        remote(gains.at[3], gain_at.at[2 + k], g_send.at[2 + k], g_recv.at[2 + k], near[k - 1]).start()
    attnf[...] = jnp.zeros_like(attnf)

    def spatial_heads(h):
        heads_forward(h, qkvs.at[0], qkvs.at[1], qkvs.at[2], attnf, HALVES, None, None)

    loop(4, spatial_heads)
    poke()
    loop(4, lambda h: spatial_heads(h + 4))
    for k in (1, 2, 3):
        remote(gains.at[3], gain_at.at[2 + k], g_send.at[2 + k], g_recv.at[2 + k], near[k - 1]).wait_recv()
    gains[0 + 4] = gains[3] + gain_at[3] + gain_at[4] + gain_at[5]
    save(gains.at[4], gain_o)

    def a_copy(k, f):
        to = (b + k) % 8
        part = attnf.at[pl.ds(pl.multiple_of(128 * f + 16 * to, 16), 16)]
        return remote(part, attnp.at[2 * b + f], a_send.at[k - 1, f], a_recv.at[k - 1, f], peers[k - 1])

    def a_wait(k, f):
        of = (b + 8 - k) % 8
        part = attnf.at[pl.ds(0, 16)]
        remote(part, attnp.at[2 * of + f], a_send.at[k - 1, f], a_recv.at[k - 1, f], peers[k - 1]).wait_recv()

    for k in range(1, 8):
        for f in range(2):
            a_copy(k, f).start()
    for f in range(2):
        attnp[2 * b + f] = attnf[pl.ds(pl.multiple_of(128 * f + 16 * b, 16), 16)]
    poke()
    for k in range(1, 8):
        for f in range(2):
            a_wait(k, f)
    xin[...] = attnp[...].reshape(ROWS, WIDE)
    turned(xin, 9)
    load(3)

    def emit_branch(cols, value):
        branchw[:, cols] = value

    times(xp, 3, emit_branch)

    def after_spatial(rows):
        seg = seg_in[0, rows, 0:1]
        value = branchw[rows, :]
        branch[0, rows, :] = to_low(value)
        value = wide32(tokp[rows, :]) + pick(2, seg) * value
        stream[rows, :] = value
        xin[rows, :] = to_low(normal(value, rows, 1) * (1.0 + pick(4, seg)) + pick(3, seg))

    each_rows(32, after_spatial)
    save(branch.at[0], branch_o.at[0])
    save(xhat.at[1], xhat_o.at[1])
    save(rstd.at[1], rstd_o.at[1])

    for k in range(1, 8):
        for f in range(2):
            a_copy(k, f).wait_send()
    attnf[...] = to_low(linear(regroup(False), xin[...]))
    turned(attnf, 8)
    for j in range(3):
        load(4 + j)

        def emit(cols, value, j=j):
            qkvt[j, :, cols] = to_low(value)

        times(xp, 4 + j, emit)
    save(qkvt, qkvt_o)
    attnf[...] = jnp.zeros_like(attnf)

    bias[...] = temporal_bias(seg_in, seg_row)

    def temporal_heads(h):
        heads_forward(
            h, qkvt.at[0], qkvt.at[1], qkvt.at[2], attnf, HALVES, jnp.concatenate([bias[...]] * 4), None
        )

    loop(4, temporal_heads)
    poke()
    loop(4, lambda h: temporal_heads(h + 4))
    xin[...] = to_low(linear(regroup(True), attnf[...]))
    turned(xin, 7)
    load(7)
    times(xp, 7, emit_branch)

    def after_temporal(rows):
        seg = seg_in[0, rows, 0:1]
        value = branchw[rows, :]
        branch[1, rows, :] = to_low(value)
        value = stream[rows, :] + pick(5, seg) * value
        stream[rows, :] = value
        xin[rows, :] = to_low(normal(value, rows, 2) * gains[4, 0:1, :])

    each_rows(32, after_temporal)
    save(branch.at[1], branch_o.at[1])
    save(xhat.at[2], xhat_o.at[2])
    save(rstd.at[2], rstd_o.at[2])

    turned(xin, 6)
    load(8)

    def emit_query(cols, value):
        qc[:, cols] = to_low(value)

    times(xp, 8, emit_query)
    save(qc, qc_o)
    for k in range(1, 8):
        x_copy(k, (b + 8 - k) % 8).wait_recv()
    mem[...] = jnp.zeros_like(mem)
    for k in range(8):
        start = 288 * (k % 4) // 128 * 128
        lanes = slice(start, start + TEXT_WIN)
        mem[k // 4, :, lanes] = mem[k // 4, :, lanes] + text[k]
    save(mem, mem_o)
    attnf[...] = jnp.zeros_like(attnf)

    def cross_heads(h):
        heads_forward(h, qc, mem.at[0], mem.at[1], attnf, VIDEOS, cross_bias(), cross_rows(seg_in))

    loop(4, cross_heads)
    poke()
    loop(4, lambda h: cross_heads(h + 4))
    xin[...] = attnf[...]
    turned(xin, 5)
    load(9)
    times(xp, 9, emit_branch)

    def after_cross(rows):
        seg = seg_in[0, rows, 0:1]
        value = stream[rows, :] + branchw[rows, :]
        stream[rows, :] = value
        xin[rows, :] = to_low(normal(value, rows, 3) * (1.0 + pick(7, seg)) + pick(6, seg))
        gfour[rows, :] = to_low(wide32(cotp[rows, :]) * pick(8, seg))

    each_rows(32, after_cross)
    save(xhat.at[3], xhat_o.at[3])
    save(rstd.at[3], rstd_o.at[3])
    save(gfour, gfour_o)

    turned(xin, 4)
    same = (
        lax.broadcasted_iota(jnp.int32, (TILE, TILE), 0) == lax.broadcasted_iota(jnp.int32, (TILE, TILE), 1)
    ).astype(jnp.float32).astype(jnp.bfloat16)
    for k in range(4):
        slot = k % 2
        load(10 + 2 * k)
        settle(SLOPE_SEM + slot)
        settle(LEFT_SEM + slot)

        def emit_hidden(cols, value, slot=slot):
            inner = math.sqrt(2.0 / math.pi) * (value + 0.044715 * value * value * value)
            bent = jnp.tanh(inner)
            half = 0.5 * (1.0 + bent)
            tilt = math.sqrt(2.0 / math.pi) * (1.0 + 3 * 0.044715 * value * value)
            slope[slot, :, cols] = to_low(half + 0.5 * value * (1.0 - bent * bent) * tilt)
            low = to_low(value * half)
            post[:, cols] = low
            left[slot, cols, :] = to_low(nt(same, low))

        times(xp, 10 + 2 * k, emit_hidden)
        save(slope.at[slot], slope_o.at[k], SLOPE_SEM + slot)
        save(left.at[slot], left_o.at[k], LEFT_SEM + slot)
        load(11 + 2 * k)

        def emit_out(cols, value, k=k):
            branchw[:, cols] = value if k == 0 else branchw[:, cols] + value

        times(post, 11 + 2 * k, emit_out)

    gate[...] = jnp.zeros_like(gate)

    def last(rows):
        seg = seg_in[0, rows, 0:1]
        value = branchw[rows, :]
        xin[rows, :] = to_low(stream[rows, :] + pick(8, seg) * value)
        value = wide32(cotp[rows, :]) * value
        later = jnp.sum(value * seg, axis=0, keepdims=True)
        every = jnp.sum(value, axis=0, keepdims=True)
        gate[0:1, :] = gate[0:1, :] + (every - later)
        gate[1:2, :] = gate[1:2, :] + later

    each_rows(32, last)
    save(gate, gate_o)
    out[...] = to_low(linear(swap_rows(), xin[...]))

    for copy in held.values():
        copy.wait()
    for k in range(1, 8):
        t_copy(k).wait_send()
        m_copy(k, b).wait_send()
        x_copy(k, b).wait_send()
    for at, to in ((0, twin), (1, first), (2, second)):
        g_copy(at, at, to).wait_send()
    for k in (1, 2, 3):
        remote(gains.at[3], gain_at.at[2 + k], g_send.at[2 + k], g_recv.at[2 + k], near[k - 1]).wait_send()

    def finish(t):
        for k in (1, 2, 3):
            z_copy(t, k).wait_send()
        for index in range(7):
            sends(t, index).wait_send()

    loop(BLOCKS, finish)


ANY = pl.BlockSpec(memory_space=pl.ANY)
IN_VMEM = pl.BlockSpec(memory_space=pltpu.VMEM)


def forward(src, tok, cot, gain_in, mod_in, text_in, seg_in, seg_row, turn):
    low, full = jnp.bfloat16, jnp.float32
    dma = pltpu.SemaphoreType.DMA
    hbm = [
        ((BLOCKS, WIDE, WIDE), low),
        ((ROWS, WIDE), low),
        ((11, WIDE, ROWS), low),
        ((3, ROWS, WIDE), low),
        ((3, ROWS, WIDE), low),
        ((ROWS, WIDE), low),
        ((2, TEXT, WIDE), low),
        ((4, ROWS, WIDE), low),
        ((4, ROWS, 128), full),
        ((2, ROWS, WIDE), low),
        ((4, ROWS, WIDE), low),
        ((ROWS, WIDE), low),
        ((ROWS, WIDE), low),
        ((8, MOD), full),
        ((8, WIDE), full),
        ((8, WIDE), full),
    ]
    vmem = [
        ((BLOCKS, 4, WINDOW, WIDE), low),
        ((BLOCKS, LINE, WIDE), low),
        ((2, WIDE, WIDE), low),
        ((ROWS, WIDE), low),
        ((ROWS, WIDE), low),
        ((8, 32, WIDE), low),
        ((ROWS, WIDE), low),
        ((ROWS, WIDE), low),
        ((2, WIDE, ROWS), low),
        ((3, ROWS, WIDE), low),
        ((3, ROWS, WIDE), low),
        ((ROWS, WIDE), low),
        ((2, TEXT, WIDE), low),
        ((8, TEXT, TEXT_WIN), low),
        ((8, 16, MOD_WIN), low),
        ((8, MOD), full),
        ((4, ROWS, WIDE), low),
        ((4, ROWS, 128), full),
        ((2, ROWS, WIDE), low),
        ((ROWS, WIDE), full),
        ((128, 128), full),
        ((ROWS, WIDE), full),
        ((ROWS, WIDE), low),
        ((16, 16, WIDE), low),
        ((ROWS, WIDE), low),
        ((2, ROWS, WIDE), low),
        ((ROWS, WIDE), low),
        ((5, 8, WIDE), full),
        ((6, 8, WIDE), full),
        ((8, WIDE), full),
    ]
    return pl.pallas_call(
        forward_kernel,
        out_shape=[jax.ShapeDtypeStruct(*shape) for shape in hbm],
        in_specs=[IN_VMEM] * 9,
        out_specs=[ANY, IN_VMEM] + [ANY] * 14,
        scratch_shapes=[pltpu.VMEM(*shape) for shape in vmem]
        + [
            dma((BLOCKS, 3)), dma((BLOCKS, 3)), dma((BLOCKS, 7)), dma((BLOCKS, 7)), dma((BLOCKS,)), dma((2,)),
            dma((7,)), dma((7,)), dma((7, 2)), dma((7, 2)), dma((7,)), dma((7,)), dma((7,)), dma((7,)),
            dma((6,)), dma((6,)), dma((SAVE_SEMS,)),
        ],
        compiler_params=pltpu.CompilerParams(
            collective_id=0, has_side_effects=True, vmem_limit_bytes=60 * MIB
        ),
        name="forward",
    )(src, tok, cot, gain_in, mod_in, text_in, seg_in, seg_row, turn)


def tn(left, right):
    return lax.dot_general(
        left, right, (((0,), (0,)), ((), ())), preferred_element_type=jnp.float32
    )


def heads_backward(h, query, key, value, grad, dquery, dkey, dvalue, groups, bias, mask):
    jobs = chains(h, groups)
    scores, grads = [], []
    for (lanes, on), rows, keys in jobs:
        low_on = to_low(on)
        scores.append(nt(query[rows, lanes] * low_on, key[keys, lanes]))
        grads.append(nt(grad[rows, lanes] * low_on, value[keys, lanes]))
    probs = soft(jnp.concatenate(scores), bias, mask)
    grad_probs = jnp.concatenate(grads)
    delta = jnp.sum(grad_probs * probs, axis=-1, keepdims=True)
    slopes = split_rows(to_low(probs * (grad_probs - delta)), jobs)
    probs = split_rows(to_low(probs), jobs)
    parts = []
    for slope, prob, ((lanes, on), rows, keys) in zip(slopes, probs, jobs):
        parts.append(
            (
                to_low(linear(slope, key[keys, lanes]) * (on * SCALE)),
                to_low(tn(slope, query[rows, lanes]) * (on * SCALE)),
                to_low(tn(prob, grad[rows, lanes]) * on),
            )
        )
    for (by_query, by_key, by_value), ((lanes, on), rows, keys) in zip(parts, jobs):
        dquery[rows, lanes] = dquery[rows, lanes] + by_query
        dkey[keys, lanes] = dkey[keys, lanes] + by_key
        dvalue[keys, lanes] = dvalue[keys, lanes] + by_value


def backward_kernel(
    wide, left_i, qkvs_i, qkvt_i, qc_i, mem_i, xhat_i, rstd_i, branch_i, slope_i, gfour_i, cot_i, mods_i, gate_i, gain_i,
    seg_in, seg_row, turn,
    total, gtok, gain_o, text_o, mod_o,
    weights, left, right, qkv, xhat, rstd, branch, slope, mods, gain, bias, stream, work, grad, xin, gm, dmem, text, mod_out, mod,
    seqs, gains, gain_at, gframe, back, backp,
    s0, r0, s1, r1, s2, r2, k2, s3, r3, share,
    in_sem, w_sem, s0_sem, r0_sem, s1_sem, r1_sem, s2_sem, r2_sem, s3_sem, r3_sem, share_sem,
    a_send, a_recv, u_send, u_recv, x_send, x_recv, m_send, m_recv, q_send, q_recv, g_send, g_recv,
):
    x, c, y, z, x1, y1, x2, y2 = place()
    b = z * 2 + y
    near = [device(x, c, y, (z + k) % 4) for k in (1, 2, 3)]
    first, second, twin = device(x1, c, y1, z), device(x2, c, y2, z), device(x, 1 - c, y, z)
    peers = blk_peers(x, c, b)
    across = [twin, device(1 - x, c, y, z), device(1 - x, 1 - c, y, z)]
    greet(peers + across)

    fetches = {}

    def fetch(name, from_ref, to_ref):
        fetches[name] = pltpu.make_async_copy(from_ref, to_ref, in_sem.at[name])
        fetches[name].start()

    def have(name):
        if name in fetches:
            fetches.pop(name).wait()

    fetch(0, gfour_i, right.at[0])
    for k in range(11):
        fetch(1 + k, left_i.at[k], left.at[k])
    fetch(12, mods_i, mods)
    fetch(13, gain_i, gain)
    fetch(14, slope_i.at[0], slope.at[0])
    fetch(15, slope_i.at[1], slope.at[1])
    fetch(16, xhat_i.at[3], xhat.at[1])
    fetch(17, rstd_i.at[3], rstd.at[1])
    fetch(18, cot_i, xin)
    fetch(19, gate_i, work.at[0:8])

    def weight(block):
        slot = WEIGHT_ORDER.index(block) % 2
        return weights.at[slot]

    def prefetch(at):
        if at < len(WEIGHT_ORDER):
            copy = pltpu.make_async_copy(wide.at[WEIGHT_ORDER[at]], weights.at[at % 2], w_sem.at[at % 2])
            copy.start()
            fetches["w", WEIGHT_ORDER[at]] = copy

    def release(block):
        prefetch(WEIGHT_ORDER.index(block) + 2)

    prefetch(0)
    prefetch(1)

    away = [(1 - x) * 2 + 1 - y, x2 * 2 + y2]
    stay = [x1 * 2 + y1, x * 2 + y]

    def product(t, core, xl):
        rows = pl.ds(pl.multiple_of(line_of(core, xl, 0) * LINE, 16), 2 * LINE)
        return linear(left[left_at(t), rows, :], right[right_at(t)])

    def copy0(t, l):
        pair = pl.ds(2 * l, 2)
        return remote(s0.at[t % 2, pair], r0.at[t % 4, pair], s0_sem.at[t % 2, l], r0_sem.at[t % 4, l], twin)

    def copy1(t, l):
        return remote(s1.at[t % 2, away[l]], r1.at[t % 4, l], s1_sem.at[t % 2, l], r1_sem.at[t % 4, l], second)

    def copy2(t):
        return remote(s2.at[t % 2], r2.at[t % 4], s2_sem.at[t % 2], r2_sem.at[t % 4], first)

    def copy3(t, k):
        part = pl.ds(pl.multiple_of(32 * ((z + k) % 4), 16), WINDOW)
        return remote(s3.at[t % 2, part], r3.at[t % 4, k - 1], s3_sem.at[t % 2, k - 1], r3_sem.at[t % 4, k - 1], near[k - 1])

    def share_copy(t):
        return pltpu.make_async_copy(share.at[t % 2], total.at[t], share_sem.at[t % 2])

    def tick(t):
        @pl.when(t < BLOCKS)
        def _():
            for l in range(2):
                @pl.when(t >= 2)
                def _():
                    copy0(t - 2, l).wait_send()
                value = to_low(product(t, 1 - c, l))
                s0[t % 2, 2 * l] = value[:LINE]
                s0[t % 2, 2 * l + 1] = value[LINE:]
                copy0(t, l).start()

        @pl.when((t >= 1) & (t < BLOCKS + 1))
        def _():
            now = t - 1

            @pl.when(now >= 2)
            def _():
                for l in range(2):
                    copy1(now - 2, l).wait_send()
            for l in range(2):
                copy0(now, l).wait_recv()
                value = product(now, c, l)
                for part in range(2):
                    line = 2 * l + part
                    summed = value[part * LINE : part * LINE + LINE] + wide32(r0[now % 4, line])
                    s1[now % 2, line] = to_low(summed)
            for l in range(2):
                copy1(now, l).start()

        @pl.when((t >= 2) & (t < BLOCKS + 2))
        def _():
            now = t - 2
            copy1(now, 0).wait_recv()

            @pl.when(now >= 2)
            def _():
                copy2(now - 2).wait_send()
            s2[now % 2] = to_low(wide32(s1[now % 2, stay[0]]) + wide32(r1[now % 4, 0]))
            copy2(now).start()
            copy1(now, 1).wait_recv()
            k2[now % 2] = wide32(s1[now % 2, stay[1]]) + wide32(r1[now % 4, 1])

        @pl.when((t >= 3) & (t < BLOCKS + 3))
        def _():
            now = t - 3
            copy2(now).wait_recv()

            @pl.when(now >= 2)
            def _():
                for k in (1, 2, 3):
                    copy3(now - 2, k).wait_send()
            value = k2[now % 2] + wide32(r2[now % 4])
            s3[now % 2] = to_low(value)
            for k in (1, 2, 3):
                copy3(now, k).start()

        @pl.when(t >= 4)
        def _():
            now = t - 4
            value = wide32(s3[now % 2, pl.ds(pl.multiple_of(32 * z, 16), WINDOW)])
            for k in (1, 2, 3):
                copy3(now, k).wait_recv()
                value = value + wide32(r3[now % 4, k - 1])

            @pl.when(now >= 2)
            def _():
                share_copy(now - 2).wait()
            share[now % 2] = value
            share_copy(now).start()

    done = [0]

    def pump(until):
        if until > done[0]:
            start = done[0]
            loop(until - start, lambda i: tick(i + start))
            done[0] = until

    def pick(piece, seg):
        lanes = slice(WIDE * piece, WIDE * piece + WIDE)
        return jnp.where(seg > 0.5, mods[1:2, lanes], mods[0:1, lanes])

    def by_video(piece, value, seg):
        lanes = slice(WIDE * piece, WIDE * piece + WIDE)
        later = jnp.sum(value * seg, axis=0, keepdims=True)
        every = jnp.sum(value, axis=0, keepdims=True)
        gm[0:1, lanes] = gm[0:1, lanes] + (every - later)
        gm[1:2, lanes] = gm[1:2, lanes] + later

    def through(values_at, blocks, emit, grouped=False):
        for n, (values, block) in enumerate(zip(values_at, blocks)):
            have(("w", block))

            def tile(cols, n=n, values=values, block=block):
                part = nt(values[...], weight(block)[cols, :])
                if n > 0:
                    part = part + work[:, cols]
                if n == len(blocks) - 1:
                    xin[:, cols] = to_low(part)
                else:
                    work[:, cols] = part

            each_cols(tile)
            release(block)
        if grouped:
            xin[...] = to_low(linear(regroup(True), xin[...]))
        turn_back(emit)

    def turn_back(emit):
        each_cols(lambda cols: emit(cols, linear(xin[...], turn[:, cols])))

    def emit_work(cols, value):
        work[:, cols] = value

    def emit_grad(cols, value):
        grad[:, cols] = to_low(value)

    def norm_back(grad_in, tilt, at, rows):
        slope_in = grad_in * tilt
        hat = wide32(xhat[at, rows, :])
        first_mean = jnp.mean(slope_in, axis=-1, keepdims=True)
        second_mean = jnp.mean(slope_in * hat, axis=-1, keepdims=True)
        return rstd[at, rows, 0:1] * (slope_in - first_mean - hat * second_mean)

    gm[...] = jnp.zeros_like(gm)
    have(0)
    have(12)
    have(18)
    have(19)
    gm[0:8, 8 * WIDE : 9 * WIDE] = work[0:8]
    stream[...] = wide32(xin[...])
    for k in range(5):
        have(1 + k)
    pump(1)
    for k in range(4):
        have(14 + k % 2 if k < 2 else ("slope", k))
        have(("w", 11 + 2 * k))

        def tile(cols, k=k):
            value = nt(right[0], weight(11 + 2 * k)[cols, :]) * wide32(slope[k % 2, :, cols])
            right[1 + k, :, cols] = to_low(value)

        each_cols(tile)
        release(11 + 2 * k)
        if k < 2:
            copy = pltpu.make_async_copy(slope_i.at[k + 2], slope.at[k % 2], in_sem.at[14 + k])
            copy.start()
            fetches["slope", k + 2] = copy
        have(("w", 10 + 2 * k))

        def tile(cols, k=k):
            part = nt(right[1 + k], weight(10 + 2 * k)[cols, :])
            if k > 0:
                part = part + work[:, cols]
            if k < 3:
                work[:, cols] = part
            else:
                xin[:, cols] = to_low(part)

        each_cols(tile)
        release(10 + 2 * k)
        pump(k + 2)
    turn_back(emit_work)
    for k in range(5, 11):
        have(1 + k)
    have(16)
    have(17)
    fetch(20, qc_i, qkv.at[0])
    fetch(21, mem_i.at[0], qkv.at[1])
    fetch(22, mem_i.at[1], qkv.at[2])
    fetch(23, xhat_i.at[2], xhat.at[0])
    fetch(24, rstd_i.at[2], rstd.at[0])

    def after_mlp(rows):
        seg = seg_in[0, rows, 0:1]
        value = work[rows, :]
        by_video(6, value, seg)
        by_video(7, value * wide32(xhat[1, rows, :]), seg)
        value = stream[rows, :] + norm_back(value, 1.0 + pick(7, seg), 1, rows)
        stream[rows, :] = value
        right[5, rows, :] = to_low(value)

    each_rows(32, after_mlp)

    fetch(25, xhat_i.at[1], xhat.at[1])
    fetch(26, rstd_i.at[1], rstd.at[1])
    through([right.at[5]], [9], emit_grad)
    right[6] = jnp.zeros_like(right[6])
    dmem[...] = jnp.zeros_like(dmem)
    for name in (13, 20, 21, 22, 23, 24):
        have(name)

    def cross_heads(h):
        heads_backward(
            h, qkv.at[0], qkv.at[1], qkv.at[2], grad, right.at[6], dmem.at[0], dmem.at[1],
            VIDEOS, cross_bias(), cross_rows(seg_in),
        )

    for part in range(4):
        loop(2, lambda h: cross_heads(h + 2 * part))
        pump(6 + part if part < 3 else 8)

    def x_copy(k):
        to = (b + k) % 8
        lanes = pl.ds(pl.multiple_of((288 * (to % 4)) // 128 * 128, 128), TEXT_WIN)
        return remote(dmem.at[to // 4, :, lanes], text.at[b], x_send.at[k - 1], x_recv.at[k - 1], peers[k - 1])

    def x_wait(k):
        of = (b + 8 - k) % 8
        remote(dmem.at[0, :, pl.ds(0, TEXT_WIN)], text.at[of], x_send.at[k - 1], x_recv.at[k - 1], peers[k - 1]).wait_recv()

    for k in range(1, 8):
        x_copy(k).start()
    text[b] = dmem[b // 4, :, pl.ds(pl.multiple_of((288 * (b % 4)) // 128 * 128, 128), TEXT_WIN)]
    fetch(27, qkvt_i.at[0], qkv.at[0])
    fetch(28, qkvt_i.at[1], qkv.at[1])
    fetch(29, qkvt_i.at[2], qkv.at[2])
    fetch(30, branch_i.at[1], branch)
    through([right.at[6]], [8], emit_work)
    gains[0] = jnp.zeros_like(gains[0])
    have(30)

    def after_cross(rows):
        seg = seg_in[0, rows, 0:1]
        value = work[rows, :]
        gains[0, 0:1, :] = gains[0, 0:1, :] + jnp.sum(value * wide32(xhat[0, rows, :]), axis=0, keepdims=True)
        value = stream[rows, :] + norm_back(value, gain[0:1, :], 0, rows)
        stream[rows, :] = value
        by_video(5, value * wide32(branch[rows, :]), seg)
        right[7, rows, :] = to_low(value * pick(5, seg))

    each_rows(32, after_cross)

    def g_copy(at, to):
        return remote(gains.at[min(at, 3)], gain_at.at[at], g_send.at[at], g_recv.at[at], to)

    g_copy(0, twin).start()
    fetch(31, branch_i.at[0], branch)
    fetch(32, xhat_i.at[0], xhat.at[0])
    fetch(33, rstd_i.at[0], rstd.at[0])
    pump(9)

    through([right.at[7]], [7], emit_grad)
    grad[...] = to_low(linear(regroup(False), grad[...]))
    bias[...] = temporal_bias(seg_in, seg_row)
    for j in range(3):
        right[8 + j] = jnp.zeros_like(right[8 + j])
    for name in (25, 26, 27, 28, 29):
        have(name)

    def temporal_heads(h):
        heads_backward(
            h, qkv.at[0], qkv.at[1], qkv.at[2], grad, right.at[8], right.at[9], right.at[10],
            HALVES, jnp.concatenate([bias[...]] * 4), None,
        )

    loop(4, temporal_heads)
    pump(10)
    g_copy(0, twin).wait_recv()
    gains[1] = gains[0] + gain_at[0]
    g_copy(1, first).start()
    loop(4, lambda h: temporal_heads(h + 4))
    pump(11)
    g_copy(1, first).wait_recv()
    gains[2] = gains[1] + gain_at[1]
    g_copy(2, second).start()
    for k in range(1, 8):
        x_wait(k)
    summed = wide32(text[0])
    for k in range(1, 8):
        summed = summed + wide32(text[k])
    text_o[...] = to_low(summed)
    for j in range(3):
        fetch(34 + j, qkvs_i.at[j], qkv.at[j])
    through([right.at[8], right.at[9], right.at[10]], [4, 5, 6], emit_work, True)
    have(31)

    def after_temporal(rows):
        seg = seg_in[0, rows, 0:1]
        value = work[rows, :]
        by_video(3, value, seg)
        by_video(4, value * wide32(xhat[1, rows, :]), seg)
        value = stream[rows, :] + norm_back(value, 1.0 + pick(4, seg), 1, rows)
        stream[rows, :] = value
        by_video(2, value * wide32(branch[rows, :]), seg)
        right[11, rows, :] = to_low(value * pick(2, seg))

    each_rows(32, after_temporal)

    through([right.at[11]], [3], emit_grad)

    def a_copy(k):
        to = (b + k) % 8
        part = grad.at[pl.ds(pl.multiple_of(32 * to, 32), 32)]
        return remote(part, back.at[b], a_send.at[k - 1], a_recv.at[k - 1], peers[k - 1])

    def a_wait(k):
        of = (b + 8 - k) % 8
        remote(grad.at[pl.ds(0, 32)], back.at[of], a_send.at[k - 1], a_recv.at[k - 1], peers[k - 1]).wait_recv()

    for k in range(1, 8):
        a_copy(k).start()
    back[b] = grad[pl.ds(pl.multiple_of(32 * b, 32), 32)]
    pump(12)
    g_copy(2, second).wait_recv()
    gains[3] = gains[2] + gain_at[2]
    for k in (1, 2, 3):
        g_copy(2 + k, near[k - 1]).start()
    for j in range(3):
        right[12 + j] = jnp.zeros_like(right[12 + j])
    for name in (32, 33, 34, 35, 36):
        have(name)
    for k in range(1, 8):
        a_wait(k)
    for k in range(8):
        for f in range(2):
            gframe[128 * f + 16 * k : 128 * f + 16 * k + 16, :] = back[k, 16 * f : 16 * f + 16, :]

    def spatial_heads(h):
        heads_backward(
            h, qkv.at[0], qkv.at[1], qkv.at[2], gframe, right.at[12], right.at[13], right.at[14], HALVES, None, None
        )

    loop(4, spatial_heads)
    pump(14)
    loop(4, lambda h: spatial_heads(h + 4))
    pump(15)
    through([right.at[12], right.at[13], right.at[14]], [0, 1, 2], emit_work)
    pump(16)
    for k in range(1, 8):
        a_copy(k).wait_send()

    def after_spatial(i):
        rows = pl.ds(pl.multiple_of(16 * i, 16), 16)
        seg = seg_in[1, rows, 0:1]
        value = work[rows, :]
        by_video(0, value, seg)
        by_video(1, value * wide32(xhat[0, rows, :]), seg)
        value = to_low(norm_back(value, 1.0 + pick(1, seg), 0, rows))
        back[i % 8, pl.ds(pl.multiple_of(16 * (i // 8), 16), 16), :] = value

    loop(16, after_spatial)

    def u_copy(k):
        to = (b + k) % 8
        return remote(back.at[to], backp.at[b], u_send.at[k - 1], u_recv.at[k - 1], peers[k - 1])

    def u_wait(k):
        of = (b + 8 - k) % 8
        remote(back.at[0], backp.at[of], u_send.at[k - 1], u_recv.at[k - 1], peers[k - 1]).wait_recv()

    def m_copy(k):
        to = (b + k) % 8
        return remote(mod_out.at[to], mod.at[b], m_send.at[k - 1], m_recv.at[k - 1], peers[k - 1])

    def m_wait(k):
        of = (b + 8 - k) % 8
        remote(mod_out.at[0], mod.at[of], m_send.at[k - 1], m_recv.at[k - 1], peers[k - 1]).wait_recv()

    for k in range(1, 8):
        u_copy(k).start()
    backp[b] = back[b]
    for k in range(8):
        mod_out[k] = to_low(gm[:, 1280 * k : 1280 * k + MOD_WIN])
    for k in range(1, 8):
        m_copy(k).start()
    mod[b] = mod_out[b]
    pump(18)
    for k in range(1, 8):
        m_wait(k)
    summed = wide32(mod[0])
    for k in range(1, 8):
        summed = summed + wide32(mod[k])
    own = x * 2 + c
    seqs[own] = to_low(summed)
    places = [x * 2 + 1 - c, (1 - x) * 2 + c, (1 - x) * 2 + 1 - c]

    def q_copy(k, at):
        return remote(seqs.at[own], seqs.at[at], q_send.at[k], q_recv.at[k], across[k])

    for k in range(3):
        q_copy(k, own).start()
    for k in range(1, 8):
        u_wait(k)
    xin[...] = to_low(stream[...] + wide32(backp[...].reshape(ROWS, WIDE)))
    gtok[...] = to_low(linear(swap_rows(), xin[...]))
    for k in (1, 2, 3):
        g_copy(2 + k, near[k - 1]).wait_recv()
    gain_o[...] = gains[3] + gain_at[3] + gain_at[4] + gain_at[5]
    pump(BLOCKS + 4)
    for k in range(3):
        q_copy(k, places[k]).wait_recv()
    mod_o[...] = seqs[...]

    for now in (BLOCKS - 2, BLOCKS - 1):
        for l in range(2):
            copy0(now, l).wait_send()
            copy1(now, l).wait_send()
        copy2(now).wait_send()
        for k in (1, 2, 3):
            copy3(now, k).wait_send()
        share_copy(now).wait()
    for k in range(1, 8):
        x_copy(k).wait_send()
        u_copy(k).wait_send()
        m_copy(k).wait_send()
    for k in range(3):
        q_copy(k, own).wait_send()
    for at, to in enumerate([twin, first, second] + near):
        g_copy(at, to).wait_send()


WEIGHT_ORDER = (11, 10, 13, 12, 15, 14, 17, 16, 9, 8, 7, 4, 5, 6, 3, 0, 1, 2)


def backward(*operands):
    low, full = jnp.bfloat16, jnp.float32
    dma = pltpu.SemaphoreType.DMA
    outs = [
        ((BLOCKS, WINDOW, WIDE), full),
        ((ROWS, WIDE), low),
        ((8, WIDE), full),
        ((TEXT, TEXT_WIN), low),
        ((4, 16, MOD_WIN), low),
    ]
    vmem = [
        ((2, WIDE, WIDE), low),
        ((11, WIDE, ROWS), low),
        ((15, ROWS, WIDE), low),
        ((3, ROWS, WIDE), low),
        ((2, ROWS, WIDE), low),
        ((2, ROWS, 128), full),
        ((ROWS, WIDE), low),
        ((2, ROWS, WIDE), low),
        ((8, MOD), full),
        ((8, WIDE), full),
        ((128, 128), full),
        ((ROWS, WIDE), full),
        ((ROWS, WIDE), full),
        ((ROWS, WIDE), low),
        ((ROWS, WIDE), low),
        ((16, MOD), full),
        ((2, TEXT, WIDE), low),
        ((8, TEXT, TEXT_WIN), low),
        ((8, 16, MOD_WIN), low),
        ((8, 16, MOD_WIN), low),
        ((4, 16, MOD_WIN), low),
        ((4, 8, WIDE), full),
        ((6, 8, WIDE), full),
        ((ROWS, WIDE), low),
        ((8, 32, WIDE), low),
        ((8, 32, WIDE), low),
        ((2, 4, LINE, WIDE), low),
        ((4, 4, LINE, WIDE), low),
        ((2, 4, LINE, WIDE), low),
        ((4, 2, LINE, WIDE), low),
        ((2, LINE, WIDE), low),
        ((4, LINE, WIDE), low),
        ((2, LINE, WIDE), full),
        ((2, LINE, WIDE), low),
        ((4, 3, WINDOW, WIDE), low),
        ((2, WINDOW, WIDE), full),
    ]
    return pl.pallas_call(
        backward_kernel,
        out_shape=[jax.ShapeDtypeStruct(*shape) for shape in outs],
        in_specs=[ANY] * 15 + [IN_VMEM] * 3,
        out_specs=[ANY] + [IN_VMEM] * 4,
        scratch_shapes=[pltpu.VMEM(*shape) for shape in vmem]
        + [
            dma((40,)), dma((2,)), dma((2, 4)), dma((4, 4)), dma((2, 2)), dma((4, 2)), dma((2,)), dma((4,)),
            dma((2, 3)), dma((4, 3)), dma((2,)), dma((7,)), dma((7,)), dma((7,)), dma((7,)), dma((7,)), dma((7,)),
            dma((7,)), dma((7,)), dma((3,)), dma((3,)), dma((6,)), dma((6,)),
        ],
        compiler_params=pltpu.CompilerParams(
            collective_id=1, has_side_effects=True, vmem_limit_bytes=63 * MIB
        ),
        name="backward",
    )(*operands)


TURN = np.arange(WIDE)[None, :] == (
    np.arange(WIDE).reshape(2, 2, 4, 2, SHARD).transpose(1, 0, 3, 2, 4).reshape(-1)
)[:, None]


def hidden_order(values):
    rows = values.shape[0]
    cut = values.reshape(rows, 2, 2, 4, 2, 4, SHARD)
    return cut.transpose(0, 5, 2, 1, 4, 3, 6).reshape(rows, 4 * WIDE)


def hidden_back(values):
    rows = values.shape[0]
    cut = values.reshape(rows, 4, 2, 2, 2, 4, SHARD)
    return cut.transpose(0, 3, 2, 5, 4, 1, 6).reshape(rows, 4 * WIDE)


def by_block(values):
    rows = values.shape[0]
    return values.reshape(rows, -1, WIDE).transpose(1, 0, 2)


def shards(
    tokens,
    segments,
    timesteps,
    caption,
    cotangent,
    ada_weight,
    ada_bias,
    spatial_in,
    spatial_out,
    temporal_in,
    temporal_out,
    cross_gain,
    cross_query,
    caption_proj,
    cross_out,
    hidden_in,
    hidden_out,
):
    frame_seg = segments[0]
    text_width = caption.shape[-1]
    caption_rows = caption[0].reshape(2 * L, text_width)
    blk = lax.axis_index("blk")
    seq = lax.axis_index("seq")
    zplace = blk // 2
    hidden_blocks = by_block(hidden_order(hidden_in))
    hidden_rows = hidden_out.reshape(4, SHARD, WIDE)
    stack = jnp.concatenate(
        [
            by_block(spatial_in),
            spatial_out[None],
            by_block(temporal_in),
            temporal_out[None],
            cross_query[None],
            cross_out[None],
        ]
        + [part[k][None] for k in range(4) for part in (hidden_blocks, hidden_rows)]
    )
    windows = lax.dynamic_update_slice(
        jnp.zeros((BLOCKS, WINDOW, WIDE), jnp.bfloat16), stack, (0, 4 * zplace, 0)
    )
    gain_in = lax.dynamic_update_slice(
        jnp.zeros((8, WIDE), jnp.float32),
        cross_gain.astype(jnp.float32)[None],
        (0, SHARD * (seq * 8 + blk)),
    )
    conditioning = to_low(jax.nn.silu(time_embedding(timesteps[0], WIDE)))
    mod_part = to_low(linear(conditioning, ada_weight) + ada_bias.astype(jnp.float32))
    mod_in = lax.dynamic_update_slice(
        jnp.zeros((16, MOD_WIN), jnp.bfloat16), mod_part, (0, 16 * blk)
    )
    text_part = to_low(linear(caption_rows, caption_proj))
    text_in = lax.dynamic_update_slice(
        jnp.zeros((2, 128, TEXT_WIN), jnp.bfloat16), text_part.reshape(2, L, -1), (0, 0, 32 * (blk % 4))
    ).reshape(TEXT, TEXT_WIN)
    frames = frame_seg.astype(jnp.float32)
    own_frames = lax.dynamic_slice(frames, (2 * blk,), (2,))
    seg_in = jnp.broadcast_to(
        jnp.stack(
            [jnp.repeat(frames, 16), jnp.repeat(own_frames, 128), jnp.tile(jnp.repeat(frames, 8), 2)]
        )[:, :, None],
        (3, ROWS, 128),
    )
    seg_row = jnp.broadcast_to(jnp.repeat(frames, 8)[None], (8, 128))
    turn = jnp.asarray(TURN, jnp.bfloat16)
    wide, out, *kept = forward(
        windows,
        tokens.reshape(ROWS, WIDE),
        cotangent.reshape(ROWS, WIDE),
        gain_in,
        mod_in,
        text_in,
        seg_in,
        seg_row,
        turn,
    )
    spread, grad_tokens, grad_gain, grad_text, grad_mod = backward(
        wide, *kept, seg_in, seg_row, turn
    )
    shares = lax.dynamic_slice(spread, (0, 4 * zplace, 0), (BLOCKS, SHARD, WIDE))
    share_gain = lax.dynamic_slice(grad_gain, (0, SHARD * (seq * 8 + blk)), (1, SHARD))[0]
    text_low = lax.dynamic_slice(
        grad_text.reshape(2, 128, TEXT_WIN), (0, 0, 32 * (blk % 4)), (2, L, 2 * WIDE // 8)
    ).reshape(2 * L, -1)
    grad_caption = left_product(caption_rows, text_low)
    grad_caption = lax.psum(grad_caption.astype(jnp.bfloat16), "seq").astype(jnp.float32)
    all_mod = lax.dynamic_slice(grad_mod, (0, 0, 16 * blk), (4, 2, MOD // 8)).reshape(8, MOD // 8)
    all_steps = lax.all_gather(timesteps[0], "seq", axis=0, tiled=True)
    all_cond = to_low(jax.nn.silu(time_embedding(all_steps, WIDE)))
    grad_ada_w = left_product(all_cond, all_mod)
    grad_ada_b = jnp.sum(all_mod.astype(jnp.float32), axis=0)

    def joined(first, count):
        return shares[first : first + count].transpose(1, 0, 2).reshape(SHARD, count * WIDE)

    return (
        out.reshape(tokens.shape),
        grad_tokens.reshape(tokens.shape),
        grad_ada_w,
        grad_ada_b,
        joined(15, 3),
        shares[14],
        joined(11, 3),
        shares[10],
        share_gain,
        shares[9],
        grad_caption,
        shares[8],
        hidden_back(joined(4, 4)),
        shares[0:4].reshape(4 * SHARD, WIDE),
    )


def solution(mesh):
    fast = dict(mesh.shape) == {"seq": 4, "blk": 8}
    return jax.shard_map(
        shards if fast else general_shards,
        mesh=mesh,
        in_specs=(
            P("seq", "blk", None, None),
            P("seq", None),
            P("seq", None),
            P("seq", None, None, None),
            P("seq", "blk", None, None),
            P(None, "blk"),
            P("blk"),
            P(("seq", "blk"), None),
            P(("seq", "blk"), None),
            P(("seq", "blk"), None),
            P(("seq", "blk"), None),
            P(("seq", "blk")),
            P(("seq", "blk"), None),
            P(None, "blk"),
            P(("seq", "blk"), None),
            P(("seq", "blk"), None),
            P(("seq", "blk"), None),
        ),
        out_specs=(
            P("seq", "blk", None, None),
            P("seq", "blk", None, None),
            P(None, "blk"),
            P("blk"),
            P(("seq", "blk"), None),
            P(("seq", "blk"), None),
            P(("seq", "blk"), None),
            P(("seq", "blk"), None),
            P(("seq", "blk")),
            P(("seq", "blk"), None),
            P(None, "blk"),
            P(("seq", "blk"), None),
            P(("seq", "blk"), None),
            P(("seq", "blk"), None),
        ),
        check_vma=False,
    )
```

```python
import math

import jax
import jax.numpy as jnp
import numpy as np
from jax import lax
from jax.experimental import pallas as pl
from jax.experimental.pallas import tpu as pltpu
from jax.sharding import PartitionSpec as P

H = 16
E = 72
L = 120


EPSILON = 1e-06
MASKED = -1e30


def to_low(values):
    return values.astype(jnp.bfloat16)


def linear(left, right):
    return jnp.dot(left, right, preferred_element_type=jnp.float32)


def left_product(left, right):
    return lax.dot_general(
        left, right, (((0,), (0,)), ((), ())), preferred_element_type=jnp.float32
    )


def right_product(left, right):
    return lax.dot_general(
        left, right, (((1,), (1,)), ((), ())), preferred_element_type=jnp.float32
    )


def normalize(values):
    center = values - jnp.mean(values, axis=-1, keepdims=True)
    return center * lax.rsqrt(jnp.mean(center * center, axis=-1, keepdims=True) + EPSILON)


def modulate(values, shift_rows, scale_rows):
    return normalize(values) * (1.0 + scale_rows) + shift_rows


def gain_norm(values, gain_row):
    return normalize(values) * gain_row


def gelu_tanh(values):
    return jax.nn.gelu(values, approximate=True)


def softmax_rows(scores):
    shifted = jnp.exp(scores - jnp.max(scores, axis=-1, keepdims=True))
    return shifted / jnp.sum(shifted, axis=-1, keepdims=True)


def softmax_with_total(scores):
    top = jnp.max(scores, axis=-1, keepdims=True)
    shifted = jnp.exp(scores - top)
    total = jnp.sum(shifted, axis=-1, keepdims=True)
    return (shifted / total, (top + jnp.log(total))[..., 0])


def softmax_back(probs, grad_probs):
    return probs * (grad_probs - jnp.sum(grad_probs * probs, axis=-1, keepdims=True))


def time_embedding(step_ids, model_width):
    half_width = model_width // 2
    frequency = jnp.exp(
        -math.log(10000.0) * jnp.arange(half_width).astype(jnp.float32) / half_width
    )
    angles = step_ids.astype(jnp.float32)[:, None] * frequency[None, :]
    return jnp.concatenate([jnp.cos(angles), jnp.sin(angles)], axis=1)


def general_shards(
    tokens,
    segments,
    timesteps,
    caption,
    cotangent,
    ada_weight,
    ada_bias,
    spatial_in,
    spatial_out,
    temporal_in,
    temporal_out,
    cross_gain,
    cross_query,
    caption_proj,
    cross_out,
    hidden_in,
    hidden_out,
):
    inputs = tokens[0].astype(jnp.float32)
    patch_dev, frames, model_width = inputs.shape
    token_rows = patch_dev * frames
    head_count = H
    head_size = E
    score_scale = E ** (-0.5)
    frame_seg = segments[0]
    step_ids = timesteps[0]
    seg_count, text_len, text_width = caption.shape[1:]
    text_keys = seg_count * text_len
    caption_rows = caption[0].reshape(text_keys, text_width)
    grad_out = cotangent[0].astype(jnp.float32)
    gathered = (
        lax.all_gather(spatial_in, ("seq", "blk"), axis=0, tiled=True),
        lax.all_gather(spatial_out, ("seq", "blk"), axis=0, tiled=True),
        lax.all_gather(temporal_in, ("seq", "blk"), axis=0, tiled=True),
        lax.all_gather(temporal_out, ("seq", "blk"), axis=0, tiled=True),
        lax.all_gather(cross_gain, ("seq", "blk"), axis=0, tiled=True),
        lax.all_gather(cross_query, ("seq", "blk"), axis=0, tiled=True),
        lax.all_gather(cross_out, ("seq", "blk"), axis=0, tiled=True),
        lax.all_gather(hidden_in, ("seq", "blk"), axis=0, tiled=True),
        lax.all_gather(hidden_out, ("seq", "blk"), axis=0, tiled=True),
    )
    (
        wide_sin,
        wide_sout,
        wide_tin,
        wide_tout,
        gain_low,
        wide_query,
        wide_cout,
        wide_hin,
        wide_hout,
    ) = gathered
    gain_row = gain_low.astype(jnp.float32)
    conditioning = to_low(jax.nn.silu(time_embedding(step_ids, model_width)))
    mod_part = to_low(linear(conditioning, ada_weight) + ada_bias.astype(jnp.float32))
    text_part = to_low(linear(caption_rows, caption_proj))
    modulation, memory = (
        lax.all_gather(mod_part, "blk", axis=1, tiled=True),
        lax.all_gather(text_part, "blk", axis=1, tiled=True),
    )
    choose = frame_seg[:, None] == jnp.arange(seg_count, dtype=jnp.int32)[None, :]
    frame_mod = linear(choose.astype(jnp.bfloat16), modulation)
    pieces = [frame_mod[:, index * model_width : (index + 1) * model_width] for index in range(9)]
    (
        shift_one,
        scale_one,
        gate_one,
        shift_two,
        scale_two,
        gate_two,
        shift_three,
        scale_three,
        gate_three,
    ) = pieces
    spatial_input = to_low(modulate(inputs, shift_one, scale_one)).reshape(token_rows, model_width)
    spatial_qkv = to_low(linear(spatial_input, wide_sin)).reshape(
        patch_dev, frames, 3 * model_width
    )
    query_s = spatial_qkv[..., :model_width].reshape(patch_dev, frames, head_count, head_size)
    local_kv = spatial_qkv[..., model_width:]
    whole_kv = lax.all_gather(local_kv, "blk", axis=0, tiled=True)

    def split_kv(both):
        count = both.shape[0]
        return (
            both[..., :model_width].reshape(count, frames, head_count, head_size),
            both[..., model_width:].reshape(count, frames, head_count, head_size),
        )

    def spatial_probs(key_all):
        scores = jnp.einsum("pfhe,qfhe->fhpq", query_s, key_all, preferred_element_type=jnp.float32)
        return softmax_with_total(scores * score_scale)

    key_s, value_s = split_kv(whole_kv)
    probs_s, log_total_s = spatial_probs(key_s)
    probs_s_low = to_low(probs_s)
    attn_s = to_low(
        jnp.einsum(
            "fhpq,qfhe->pfhe", probs_s_low, value_s, preferred_element_type=jnp.float32
        ).reshape(token_rows, model_width)
    )
    branch_s = linear(attn_s, wide_sout).reshape(patch_dev, frames, model_width)
    after_one = inputs + gate_one * branch_s
    temporal_input = to_low(modulate(after_one, shift_two, scale_two)).reshape(
        token_rows, model_width
    )
    temporal_qkv = to_low(linear(temporal_input, wide_tin)).reshape(
        patch_dev, frames, 3, head_count, head_size
    )
    query_t = temporal_qkv[:, :, 0]
    key_t = temporal_qkv[:, :, 1]
    value_t = temporal_qkv[:, :, 2]
    same_seg = frame_seg[:, None] == frame_seg[None, :]
    scores_t = (
        jnp.einsum("pfhe,pghe->phfg", query_t, key_t, preferred_element_type=jnp.float32)
        * score_scale
    )
    probs_t = softmax_rows(jnp.where(same_seg[None, None], scores_t, MASKED))
    probs_t_low = to_low(probs_t)
    attn_t = to_low(
        jnp.einsum(
            "phfg,pghe->pfhe", probs_t_low, value_t, preferred_element_type=jnp.float32
        ).reshape(token_rows, model_width)
    )
    branch_t = linear(attn_t, wide_tout).reshape(patch_dev, frames, model_width)
    after_two = after_one + gate_two * branch_t
    cross_input = to_low(gain_norm(after_two, gain_row)).reshape(token_rows, model_width)
    query_c = to_low(linear(cross_input, wide_query)).reshape(
        patch_dev, frames, head_count, head_size
    )
    key_c = memory[:, :model_width].reshape(text_keys, head_count, head_size)
    value_c = memory[:, model_width:].reshape(text_keys, head_count, head_size)
    key_seg = jnp.arange(text_keys, dtype=jnp.int32) // text_len
    allowed = frame_seg[:, None] == key_seg[None, :]
    scores_c = (
        jnp.einsum("pfhe,khe->pfhk", query_c, key_c, preferred_element_type=jnp.float32)
        * score_scale
    )
    probs_c = softmax_rows(jnp.where(allowed[None, :, None, :], scores_c, MASKED))
    probs_c_low = to_low(probs_c)
    attn_c = to_low(
        jnp.einsum(
            "pfhk,khe->pfhe", probs_c_low, value_c, preferred_element_type=jnp.float32
        ).reshape(token_rows, model_width)
    )
    branch_c = linear(attn_c, wide_cout).reshape(patch_dev, frames, model_width)
    after_three = after_two + branch_c
    mlp_input = to_low(modulate(after_three, shift_three, scale_three)).reshape(
        token_rows, model_width
    )
    pre_act = linear(mlp_input, wide_hin)
    post_act = to_low(gelu_tanh(pre_act))
    branch_m = linear(post_act, wide_hout).reshape(patch_dev, frames, model_width)
    result = after_three + gate_three * branch_m
    grad_gate_three = jnp.sum(grad_out * branch_m, axis=0)
    grad_four = to_low(grad_out * gate_three).reshape(token_rows, model_width)
    grad_hout = left_product(post_act, grad_four)
    grad_post = right_product(grad_four, wide_hout)
    gelu_pull = jax.vjp(gelu_tanh, pre_act)[1]
    grad_pre = to_low(gelu_pull(grad_post)[0])
    grad_hin = left_product(mlp_input, grad_pre)
    grad_mlp_in = right_product(grad_pre, wide_hin).reshape(patch_dev, frames, model_width)
    mlp_pull = jax.vjp(modulate, after_three, shift_three, scale_three)[1]
    back_three, grad_shift_three, grad_scale_three = mlp_pull(grad_mlp_in)
    grad_three = grad_out + back_three
    grad_cross_branch = to_low(grad_three).reshape(token_rows, model_width)
    grad_cout = left_product(attn_c, grad_cross_branch)
    grad_attn_c = to_low(right_product(grad_cross_branch, wide_cout)).reshape(
        patch_dev, frames, head_count, head_size
    )
    grad_probs_c = jnp.einsum(
        "pfhe,khe->pfhk", grad_attn_c, value_c, preferred_element_type=jnp.float32
    )
    grad_scores_c = to_low(softmax_back(probs_c, grad_probs_c))
    grad_query_c = to_low(
        jnp.einsum("pfhk,khe->pfhe", grad_scores_c, key_c, preferred_element_type=jnp.float32)
        * score_scale
    ).reshape(token_rows, model_width)
    grad_key_c = (
        jnp.einsum("pfhk,pfhe->khe", grad_scores_c, query_c, preferred_element_type=jnp.float32)
        * score_scale
    )
    grad_value_c = jnp.einsum(
        "pfhk,pfhe->khe", probs_c_low, grad_attn_c, preferred_element_type=jnp.float32
    )
    grad_memory = jnp.concatenate(
        [grad_key_c.reshape(text_keys, model_width), grad_value_c.reshape(text_keys, model_width)],
        axis=1,
    )
    grad_wquery = left_product(cross_input, grad_query_c)
    grad_cross_in = right_product(grad_query_c, wide_query).reshape(patch_dev, frames, model_width)
    cross_pull = jax.vjp(gain_norm, after_two, gain_row)[1]
    back_two, grad_gain = cross_pull(grad_cross_in)
    grad_two = grad_three + back_two
    grad_gate_two = jnp.sum(grad_two * branch_t, axis=0)
    grad_temporal_branch = to_low(grad_two * gate_two).reshape(token_rows, model_width)
    grad_tout = left_product(attn_t, grad_temporal_branch)
    grad_attn_t = to_low(right_product(grad_temporal_branch, wide_tout)).reshape(
        patch_dev, frames, head_count, head_size
    )
    grad_probs_t = jnp.einsum(
        "pfhe,pghe->phfg", grad_attn_t, value_t, preferred_element_type=jnp.float32
    )
    grad_scores_t = to_low(softmax_back(probs_t, grad_probs_t))
    grad_query_t = (
        jnp.einsum("phfg,pghe->pfhe", grad_scores_t, key_t, preferred_element_type=jnp.float32)
        * score_scale
    )
    grad_key_t = (
        jnp.einsum("phfg,pfhe->pghe", grad_scores_t, query_t, preferred_element_type=jnp.float32)
        * score_scale
    )
    grad_value_t = jnp.einsum(
        "phfg,pfhe->pghe", probs_t_low, grad_attn_t, preferred_element_type=jnp.float32
    )
    grad_qkv_t = to_low(jnp.stack([grad_query_t, grad_key_t, grad_value_t], axis=2)).reshape(
        token_rows, 3 * model_width
    )
    grad_tin = left_product(temporal_input, grad_qkv_t)
    grad_temporal_in = right_product(grad_qkv_t, wide_tin).reshape(patch_dev, frames, model_width)
    temporal_pull = jax.vjp(modulate, after_one, shift_two, scale_two)[1]
    back_one, grad_shift_two, grad_scale_two = temporal_pull(grad_temporal_in)
    grad_one = grad_two + back_one
    grad_gate_one = jnp.sum(grad_one * branch_s, axis=0)
    grad_spatial_branch = to_low(grad_one * gate_one).reshape(token_rows, model_width)
    grad_sout = left_product(attn_s, grad_spatial_branch)
    grad_attn_s = to_low(right_product(grad_spatial_branch, wide_sout)).reshape(
        patch_dev, frames, head_count, head_size
    )
    back_kv = lax.all_gather(local_kv, "blk", axis=0, tiled=True)
    back_key, back_value = split_kv(back_kv)
    back_probs = spatial_probs(back_key)[0]
    back_probs_low = to_low(back_probs)
    grad_probs_s = jnp.einsum(
        "pfhe,qfhe->fhpq", grad_attn_s, back_value, preferred_element_type=jnp.float32
    )
    row_delta = jnp.sum(grad_probs_s * back_probs, axis=-1, keepdims=True)
    grad_scores_s = to_low(back_probs * (grad_probs_s - row_delta))
    grad_query_s = (
        jnp.einsum("fhpq,qfhe->pfhe", grad_scores_s, back_key, preferred_element_type=jnp.float32)
        * score_scale
    )
    count = lax.axis_size("blk") * patch_dev
    grad_key = (
        jnp.einsum("fhpq,pfhe->qfhe", grad_scores_s, query_s, preferred_element_type=jnp.float32)
        * score_scale
    )
    grad_value = jnp.einsum(
        "fhpq,pfhe->qfhe", back_probs_low, grad_attn_s, preferred_element_type=jnp.float32
    )
    grad_kv = to_low(
        lax.psum_scatter(
            jnp.concatenate(
                [
                    grad_key.reshape(count, frames, model_width),
                    grad_value.reshape(count, frames, model_width),
                ],
                axis=2,
            ).astype(jnp.bfloat16),
            "blk",
            scatter_dimension=0,
            tiled=True,
        ).astype(jnp.float32)
    )
    grad_qkv_s = jnp.concatenate(
        [to_low(grad_query_s).reshape(patch_dev, frames, model_width), grad_kv], axis=2
    ).reshape(token_rows, 3 * model_width)
    grad_sin = left_product(spatial_input, grad_qkv_s)
    grad_spatial_in = right_product(grad_qkv_s, wide_sin).reshape(patch_dev, frames, model_width)
    spatial_pull = jax.vjp(modulate, inputs, shift_one, scale_one)[1]
    back_zero, grad_shift_one, grad_scale_one = spatial_pull(grad_spatial_in)
    grad_input = grad_one + back_zero
    grad_frame_mod = jnp.concatenate(
        [
            grad_shift_one,
            grad_scale_one,
            grad_gate_one,
            grad_shift_two,
            grad_scale_two,
            grad_gate_two,
            grad_shift_three,
            grad_scale_three,
            grad_gate_three,
        ],
        axis=1,
    )
    grad_mod_local = lax.dot_general(
        choose.astype(jnp.float32),
        grad_frame_mod,
        (((0,), (0,)), ((), ())),
        precision=lax.Precision.HIGHEST,
    )
    grad_mod_part, grad_memory_part = (
        lax.psum_scatter(
            grad_mod_local.astype(jnp.bfloat16), "blk", scatter_dimension=1, tiled=True
        ).astype(jnp.float32),
        lax.psum_scatter(
            grad_memory.astype(jnp.bfloat16), "blk", scatter_dimension=1, tiled=True
        ).astype(jnp.float32),
    )
    grad_mod_low = to_low(grad_mod_part)
    grad_ada_w = left_product(conditioning, grad_mod_low)
    grad_ada_b = jnp.sum(grad_mod_low.astype(jnp.float32), axis=0)
    grad_caption = left_product(caption_rows, to_low(grad_memory_part))
    grad_ada_w, grad_ada_b, grad_caption = (
        lax.psum(grad_ada_w.astype(jnp.bfloat16), "seq").astype(jnp.float32),
        lax.psum(grad_ada_b.astype(jnp.bfloat16), "seq").astype(jnp.float32),
        lax.psum(grad_caption.astype(jnp.bfloat16), "seq").astype(jnp.float32),
    )
    shares = (
        lax.psum_scatter(grad_sin, ("seq", "blk"), scatter_dimension=0, tiled=True),
        lax.psum_scatter(grad_sout, ("seq", "blk"), scatter_dimension=0, tiled=True),
        lax.psum_scatter(grad_tin, ("seq", "blk"), scatter_dimension=0, tiled=True),
        lax.psum_scatter(grad_tout, ("seq", "blk"), scatter_dimension=0, tiled=True),
        lax.psum_scatter(grad_gain, ("seq", "blk"), scatter_dimension=0, tiled=True),
        lax.psum_scatter(grad_wquery, ("seq", "blk"), scatter_dimension=0, tiled=True),
        lax.psum_scatter(grad_cout, ("seq", "blk"), scatter_dimension=0, tiled=True),
        lax.psum_scatter(grad_hin, ("seq", "blk"), scatter_dimension=0, tiled=True),
        lax.psum_scatter(grad_hout, ("seq", "blk"), scatter_dimension=0, tiled=True),
    )
    (
        share_sin,
        share_sout,
        share_tin,
        share_tout,
        share_gain,
        share_query,
        share_cout,
        share_hin,
        share_hout,
    ) = shares
    return (
        to_low(result)[None],
        to_low(grad_input)[None],
        grad_ada_w,
        grad_ada_b,
        share_sin,
        share_sout,
        share_tin,
        share_tout,
        share_gain,
        share_query,
        grad_caption,
        share_cout,
        share_hin,
        share_hout,
    )


MESH = pl.DeviceIdType.MESH
BLOCKS = 18
LINES = 8
SHARD = 36
LINE = 4 * SHARD
WINDOW = 48
WIDE = LINES * LINE
MIB = 2**20


def place():
    seq = lax.axis_index("seq")
    blk = lax.axis_index("blk")
    x, c = seq // 2, seq % 2
    z, y = blk // 2, blk % 2
    x1, y1 = x + (1 - 2 * x) * (1 - c), y + (1 - 2 * y) * c
    x2, y2 = x + (1 - 2 * x) * c, y + (1 - 2 * y) * (1 - c)
    return x, c, y, z, x1, y1, x2, y2


def device(x, c, y, z):
    return {"seq": x * 2 + c, "blk": z * 2 + y}


def line_of(c, x, y):
    return (c * 2 + x) * 2 + y


def remote(src, dst, send_sem, recv_sem, where):
    return pltpu.make_async_remote_copy(
        src_ref=src,
        dst_ref=dst,
        send_sem=send_sem,
        recv_sem=recv_sem,
        device_id=where,
        device_id_type=MESH,
    )


def greet(others):
    barrier = pltpu.get_barrier_semaphore()
    for other in others:
        pl.semaphore_signal(barrier, inc=1, device_id=other, device_id_type=MESH)
    pl.semaphore_wait(barrier, len(others))


def left_at(t):
    at = jnp.minimum(t, 4)
    for first in (8, 9, 10, 11, 14, 15):
        at = at + jnp.where(t >= first, 1, 0)
    return at


def right_at(t):
    return jnp.maximum(t - 3, 0)


ROWS = 256
KEYS = 256
TEXT = 288
MOD = 9 * WIDE
MOD_TILES = 11
MOD_WIN = 128 * MOD_TILES
LEFT_SEM, SLOPE_SEM, SAVE_SEMS = 40, 42, 44
TILE = 384
SCALE = E ** (-0.5)


def nt(left, right):
    return lax.dot_general(
        left, right, (((1,), (1,)), ((), ())), preferred_element_type=jnp.float32
    )


def wide32(values):
    return values.astype(jnp.float32)


def loop(count, body):
    def step(index, carry):
        body(index)
        return carry

    lax.fori_loop(0, count, step, 0)


def each_rows(size, body, total=ROWS):
    loop(total // size, lambda i: body(pl.ds(pl.multiple_of(i * size, size), size)))


def each_cols(body):
    loop(WIDE // TILE, lambda i: body(pl.ds(pl.multiple_of(i * TILE, TILE), TILE)))


def swap_rows():
    row = lax.broadcasted_iota(jnp.int32, (ROWS, ROWS), 0)
    col = lax.broadcasted_iota(jnp.int32, (ROWS, ROWS), 1)
    return to_low((((row & 15) << 4) + (row >> 4) == col).astype(jnp.float32))


def head_window(h):
    base = h * E
    start = jnp.minimum(base // 128, 7) * 128
    lane = lax.broadcasted_iota(jnp.int32, (1, 256), 1)
    on = (lane >= base - start) & (lane < base - start + E)
    return pl.ds(pl.multiple_of(start, 128), 256), on.astype(jnp.float32)


def soft(scores, bias, mask):
    scores = scores * SCALE
    if bias is not None:
        scores = scores + bias
    powers = jnp.exp(scores - jnp.max(scores, axis=-1, keepdims=True))
    probs = powers * (1.0 / jnp.sum(powers, axis=-1, keepdims=True))
    return probs if mask is None else probs * mask


def chains(h, groups):
    return [(window, rows, keys) for window in (head_window(h), head_window(h + H // 2)) for rows, keys in groups]


def split_rows(values, jobs):
    start = 0
    parts = []
    for _, rows, _ in jobs:
        size = rows.stop - rows.start
        parts.append(values[start : start + size])
        start += size
    return parts


def heads_forward(h, query, key, value, attn, groups, bias, mask):
    jobs = chains(h, groups)
    scores = [nt(query[rows, lanes] * to_low(on), key[keys, lanes]) for (lanes, on), rows, keys in jobs]
    probs = split_rows(to_low(soft(jnp.concatenate(scores), bias, mask)), jobs)
    parts = [linear(prob, value[keys, lanes]) * on for prob, ((lanes, on), rows, keys) in zip(probs, jobs)]
    for part, ((lanes, on), rows, keys) in zip(parts, jobs):
        attn[rows, lanes] = attn[rows, lanes] + to_low(part)


def text_heads_forward(h, query, key, value, attn, bias, mask):
    jobs = chains(h, VIDEOS)
    scores = [linear(query[rows, lanes] * to_low(on), key[lanes, keys]) for (lanes, on), rows, keys in jobs]
    probs = split_rows(to_low(soft(jnp.concatenate(scores), bias, mask)), jobs)
    parts = [nt(prob, value[lanes, keys]) * on for prob, ((lanes, on), rows, keys) in zip(probs, jobs)]
    for part, ((lanes, on), rows, keys) in zip(parts, jobs):
        attn[rows, lanes] = attn[rows, lanes] + to_low(part)


HALVES = [(slice(0, 128), slice(0, 128)), (slice(128, 256), slice(128, 256))]
VIDEOS = [(slice(0, 144), slice(0, 128)), (slice(112, 256), slice(128, 256))]


def regroup(back):
    row = lax.broadcasted_iota(jnp.int32, (ROWS, ROWS), 0)
    col = lax.broadcasted_iota(jnp.int32, (ROWS, ROWS), 1)
    if back:
        source = (((row >> 3) & 1) << 7) + ((row >> 4) << 3) + (row & 7)
    else:
        source = (((row >> 3) & 15) << 4) + ((row >> 7) << 3) + (row & 7)
    return to_low((source == col).astype(jnp.float32))


def temporal_bias(seg_in, seg_row):
    row = lax.broadcasted_iota(jnp.int32, (128, 128), 0)
    col = lax.broadcasted_iota(jnp.int32, (128, 128), 1)
    allowed = ((row & 7) == (col & 7)) & (seg_in[2, 0:128, 0:1] == seg_row[0:1, 0:128])
    return jnp.where(allowed, 0.0, MASKED)


def cross_bias():
    col = lax.broadcasted_iota(jnp.int32, (1, 128), 1)
    return jnp.where(col < L, 0.0, MASKED)


def cross_rows(seg_in):
    both = [1.0 - seg_in[0, 0:144, 0:1], seg_in[0, 112:256, 0:1]]
    return jnp.concatenate(both + both)


def blk_peers(x, c, b):
    return [device(x, c, (b + k) % 2, ((b + k) % 8) // 2) for k in range(1, 8)]


def forward_kernel(
    src, tok, cot, gain_in, mod_in, text_in, seg_in, seg_row, turn,
    wide, out, left_o, qkvs_o, qkvt_o, qc_o, mem_o, xhat_o, rstd_o, branch_o, slope_o, gfour_o, cot_o, mods_o, gate_o, gain_o,
    parts, lines, weights, tokp, cotp, tokf, xin, xp, left, qkvs, qkvt, qc, mem, text, mod, mods, xhat, rstd, branch, branchw, bias,
    stream, attnf, attnp, post, slope, gfour, gains, gain_at, gate,
    z_send, z_recv, l_send, l_recv, own_sem, w_sem, t_send, t_recv, a_send, a_recv, m_send, m_recv, x_send, x_recv,
    g_send, g_recv, save_sem,
):
    x, c, y, z, x1, y1, x2, y2 = place()
    b = z * 2 + y
    near = [device(x, c, y, (z + k) % 4) for k in (1, 2, 3)]
    first, second, twin = device(x1, c, y1, z), device(x2, c, y2, z), device(x, 1 - c, y, z)
    peers = blk_peers(x, c, b)
    greet(peers + [device(1 - x, c, y, z), twin])
    mine, line1 = line_of(c, x, y), line_of(c, x1, y1)
    line2, line3 = line_of(c, x2, y2), line_of(c, 1 - x, 1 - y)
    other = [line_of(1 - c, x, y), line_of(1 - c, x2, y2), line_of(1 - c, x1, y1), line_of(1 - c, 1 - x, 1 - y)]

    def z_copy(t, k):
        return remote(src.at[t], parts.at[t, z], z_send.at[t, k - 1], z_recv.at[t, k - 1], near[k - 1])

    def z_wait(t, k):
        return remote(src.at[t], parts.at[t, (z + 4 - k) % 4], z_send.at[t, k - 1], z_recv.at[t, k - 1], near[k - 1])

    def wide_line(t, line):
        return wide.at[t, pl.ds(pl.multiple_of(line * LINE, 16), LINE)]

    def own(t):
        return pltpu.make_async_copy(lines.at[t], wide_line(t, mine), own_sem.at[t])

    def line_copy(t, to, line, index, where):
        return remote(to, wide_line(t, line), l_send.at[t, index], l_recv.at[t, index], where)

    def sends(t, index):
        line, where = (
            (mine, first), (mine, second), (mine, twin), (line1, second),
            (line1, twin), (line2, twin), (line3, twin),
        )[index]
        from_here = lines.at[t] if index < 3 else wide_line(t, line)
        return line_copy(t, from_here, line, index, where)

    def arrives(t, line, index):
        line_copy(t, wide_line(t, line), line, index, first).wait_recv()

    def tick(t):
        @pl.when(t < BLOCKS)
        def _():
            for k in (1, 2, 3):
                z_copy(t, k).start()
            parts[t, z] = src[t]

        @pl.when((t >= 2) & (t < BLOCKS + 2))
        def _():
            now = t - 2
            for k in (1, 2, 3):
                z_wait(now, k).wait_recv()
            w0, w1, w2, w3 = [parts[now, k] for k in range(4)]
            lines[now, 0:32] = w0[0:32]
            lines[now, 32:48] = w0[32:48] + w1[0:16]
            lines[now, 48:64] = w1[16:32]
            lines[now, 64:80] = w1[32:48] + w2[0:16]
            lines[now, 80:96] = w2[16:32]
            lines[now, 96:112] = w2[32:48] + w3[0:16]
            lines[now, 112:144] = w3[16:48]
            for index in range(3):
                sends(now, index).start()
            own(now).start()

        @pl.when((t >= 4) & (t < BLOCKS + 4))
        def _():
            now = t - 4
            arrives(now, line1, 0)
            for index in (3, 4):
                sends(now, index).start()

        @pl.when(t >= 5)
        def _():
            now = t - 5
            arrives(now, line2, 1)
            sends(now, 5).start()
            arrives(now, line3, 3)
            sends(now, 6).start()

    done = [0]

    def pump(until):
        until = min(until, BLOCKS + 5)
        if until > done[0]:
            start = done[0]
            loop(until - start, lambda i: tick(i + start))
            done[0] = until

    def poke():
        pump(done[0] + 1)

    def load(block):
        pump(block + 6)
        for line, index in zip(other, (2, 4, 5, 6)):
            arrives(block, line, index)
        own(block).wait()
        copy = pltpu.make_async_copy(wide.at[block], weights.at[block % 2], w_sem.at[block % 2])
        copy.start()
        copy.wait()

    def times(values, block, emit):
        def tile(cols):
            emit(cols, linear(values[...], weights[block % 2, :, cols]))

        each_cols(tile)

    saves = []
    held = {}

    def save(from_ref, to_ref, name=None):
        if name is None:
            name = len(saves)
            saves.append(name)
        held[name] = pltpu.make_async_copy(from_ref, to_ref, save_sem.at[name])
        held[name].start()

    def settle(name):
        if name in held:
            held.pop(name).wait()

    def turned(values, index):
        slot = index % 2
        settle(LEFT_SEM + slot)

        def tile(cols):
            xp[:, cols] = to_low(nt(values[...], turn[cols, :]))
            left[slot, cols, :] = to_low(nt(turn[cols, :], values[...]))

        each_cols(tile)
        save(left.at[slot], left_o.at[index], LEFT_SEM + slot)

    pump(2)

    def m_copy(k, at):
        return remote(mod_in, mod.at[at], m_send.at[k - 1], m_recv.at[k - 1], peers[k - 1])

    for k in range(1, 8):
        m_copy(k, b).start()
    mod[b] = mod_in[...]
    swap = swap_rows()
    tokp[...] = to_low(linear(swap, tok[...]))

    def t_copy(k):
        to = (b + k) % 8
        part = tokp.at[pl.ds(pl.multiple_of(32 * to, 32), 32)]
        return remote(part, tokf.at[b], t_send.at[k - 1], t_recv.at[k - 1], peers[k - 1])

    def t_wait(k):
        of = (b + 8 - k) % 8
        remote(tokp.at[pl.ds(0, 32)], tokf.at[of], t_send.at[k - 1], t_recv.at[k - 1], peers[k - 1]).wait_recv()

    for k in range(1, 8):
        t_copy(k).start()
    tokf[b] = tokp[pl.ds(pl.multiple_of(32 * b, 32), 32)]

    def g_copy(at, from_at, to):
        return remote(gains.at[from_at], gain_at.at[at], g_send.at[at], g_recv.at[at], to)

    gains[0] = gain_in[...]
    g_copy(0, 0, twin).start()
    cotp[...] = to_low(linear(swap, cot[...]))
    save(cotp, cot_o)
    pump(3)

    def x_copy(k, at):
        return remote(text_in, text.at[at, y], x_send.at[k - 1], x_recv.at[k - 1], near[k - 1])

    def x_over(at):
        return remote(text.at[:, at], text.at[:, at], x_send.at[3], x_recv.at[3], device(x, c, 1 - y, z))

    for k in range(1, 8):
        m_copy(k, (b + 8 - k) % 8).wait_recv()
    mods[...] = jnp.zeros_like(mods)
    for k in range(8):
        part = wide32(mod[k])
        for row in range(2):
            for tile in range(MOD_TILES):
                lanes = slice(1280 * k + 128 * tile, 1280 * k + 128 * tile + 128)
                at = row * MOD_TILES + tile
                mods[row : row + 1, lanes] = mods[row : row + 1, lanes] + part[at : at + 1]
    save(mods, mods_o)
    g_copy(0, 0, twin).wait_recv()
    gains[1] = gains[0] + gain_at[0]
    g_copy(1, 1, first).start()
    pump(5)
    for k in (1, 2, 3):
        x_copy(k, z).start()
    text[z, y] = text_in[...]

    def pick(piece, seg):
        lanes = slice(WIDE * piece, WIDE * piece + WIDE)
        return jnp.where(seg > 0.5, mods[1:2, lanes], mods[0:1, lanes])

    def normal(values, rows, index):
        center = values - jnp.mean(values, axis=-1, keepdims=True)
        factor = lax.rsqrt(jnp.mean(center * center, axis=-1, keepdims=True) + EPSILON)
        scaled = center * factor
        xhat[index, rows, :] = to_low(scaled)
        rstd[index, rows, :] = jnp.broadcast_to(factor, (factor.shape[0], 128))
        return scaled

    for k in range(1, 8):
        t_wait(k)
    g_copy(1, 1, first).wait_recv()
    gains[2] = gains[1] + gain_at[1]
    g_copy(2, 2, second).start()

    def spatial_rows(i):
        seg = jnp.concatenate([seg_in[1, 0:16, 0:1], seg_in[1, 128:144, 0:1]])
        values = wide32(tokf[i])
        center = values - jnp.mean(values, axis=-1, keepdims=True)
        factor = lax.rsqrt(jnp.mean(center * center, axis=-1, keepdims=True) + EPSILON)
        scaled = center * factor
        ready = to_low(scaled * (1.0 + pick(1, seg)) + pick(0, seg))
        low = to_low(scaled)
        spread = jnp.broadcast_to(factor, (32, 128))
        for f in range(2):
            rows = pl.ds(pl.multiple_of(128 * f + 16 * i, 16), 16)
            part = slice(16 * f, 16 * f + 16)
            xhat[0, rows, :] = low[part]
            rstd[0, rows, :] = spread[part]
            xin[rows, :] = ready[part]

    loop(8, spatial_rows)
    save(xhat.at[0], xhat_o.at[0])
    save(rstd.at[0], rstd_o.at[0])
    turned(xin, 10)
    for j in range(3):
        load(j)

        def emit(cols, value, j=j):
            qkvs[j, :, cols] = to_low(value)

        times(xp, j, emit)
    save(qkvs, qkvs_o)
    g_copy(2, 2, second).wait_recv()
    gains[3] = gains[2] + gain_at[2]
    for k in (1, 2, 3):
        remote(gains.at[3], gain_at.at[2 + k], g_send.at[2 + k], g_recv.at[2 + k], near[k - 1]).start()
    for k in (1, 2, 3):
        x_copy(k, (z + 4 - k) % 4).wait_recv()
    x_over(y).start()
    attnf[...] = jnp.zeros_like(attnf)

    def spatial_heads(h):
        heads_forward(h, qkvs.at[0], qkvs.at[1], qkvs.at[2], attnf, HALVES, None, None)

    loop(4, spatial_heads)
    poke()
    loop(4, lambda h: spatial_heads(h + 4))
    for k in (1, 2, 3):
        remote(gains.at[3], gain_at.at[2 + k], g_send.at[2 + k], g_recv.at[2 + k], near[k - 1]).wait_recv()
    gains[0 + 4] = gains[3] + gain_at[3] + gain_at[4] + gain_at[5]
    save(gains.at[4], gain_o)

    def a_copy(k, f):
        to = (b + k) % 8
        part = attnf.at[pl.ds(pl.multiple_of(128 * f + 16 * to, 16), 16)]
        return remote(part, attnp.at[2 * b + f], a_send.at[k - 1, f], a_recv.at[k - 1, f], peers[k - 1])

    def a_wait(k, f):
        of = (b + 8 - k) % 8
        part = attnf.at[pl.ds(0, 16)]
        remote(part, attnp.at[2 * of + f], a_send.at[k - 1, f], a_recv.at[k - 1, f], peers[k - 1]).wait_recv()

    for k in range(1, 8):
        for f in range(2):
            a_copy(k, f).start()
    for f in range(2):
        attnp[2 * b + f] = attnf[pl.ds(pl.multiple_of(128 * f + 16 * b, 16), 16)]
    poke()
    for k in range(1, 8):
        for f in range(2):
            a_wait(k, f)
    xin[...] = attnp[...].reshape(ROWS, WIDE)
    turned(xin, 9)
    load(3)

    def emit_branch(cols, value):
        branchw[:, cols] = value

    times(xp, 3, emit_branch)

    def after_spatial(rows):
        seg = seg_in[0, rows, 0:1]
        value = branchw[rows, :]
        branch[0, rows, :] = to_low(value)
        value = wide32(tokp[rows, :]) + pick(2, seg) * value
        stream[rows, :] = value
        xin[rows, :] = to_low(normal(value, rows, 1) * (1.0 + pick(4, seg)) + pick(3, seg))

    each_rows(32, after_spatial)
    save(branch.at[0], branch_o.at[0])
    save(xhat.at[1], xhat_o.at[1])
    save(rstd.at[1], rstd_o.at[1])

    for k in range(1, 8):
        for f in range(2):
            a_copy(k, f).wait_send()
    attnf[...] = to_low(linear(regroup(False), xin[...]))
    turned(attnf, 8)
    for j in range(3):
        load(4 + j)

        def emit(cols, value, j=j):
            qkvt[j, :, cols] = to_low(value)

        times(xp, 4 + j, emit)
    save(qkvt, qkvt_o)
    attnf[...] = jnp.zeros_like(attnf)

    bias[...] = temporal_bias(seg_in, seg_row)

    def temporal_heads(h):
        heads_forward(
            h, qkvt.at[0], qkvt.at[1], qkvt.at[2], attnf, HALVES, jnp.concatenate([bias[...]] * 4), None
        )

    loop(4, temporal_heads)
    poke()
    loop(4, lambda h: temporal_heads(h + 4))
    xin[...] = to_low(linear(regroup(True), attnf[...]))
    turned(xin, 7)
    load(7)
    times(xp, 7, emit_branch)

    def after_temporal(rows):
        seg = seg_in[0, rows, 0:1]
        value = branchw[rows, :]
        branch[1, rows, :] = to_low(value)
        value = stream[rows, :] + pick(5, seg) * value
        stream[rows, :] = value
        xin[rows, :] = to_low(normal(value, rows, 2) * gains[4, 0:1, :])

    each_rows(32, after_temporal)
    save(branch.at[1], branch_o.at[1])
    save(xhat.at[2], xhat_o.at[2])
    save(rstd.at[2], rstd_o.at[2])

    turned(xin, 6)
    load(8)

    def emit_query(cols, value):
        qc[:, cols] = to_low(value)

    times(xp, 8, emit_query)
    save(qc, qc_o)
    x_over(1 - y).wait_recv()
    for k in range(8):
        mem[k // 4, TEXT * (k % 4) : TEXT * (k % 4) + TEXT, :] = text[k // 2, k % 2]
    save(mem, mem_o)
    attnf[...] = jnp.zeros_like(attnf)

    def cross_heads(h):
        text_heads_forward(h, qc, mem.at[0], mem.at[1], attnf, cross_bias(), cross_rows(seg_in))

    loop(4, cross_heads)
    poke()
    loop(4, lambda h: cross_heads(h + 4))
    xin[...] = attnf[...]
    turned(xin, 5)
    load(9)
    times(xp, 9, emit_branch)

    def after_cross(rows):
        seg = seg_in[0, rows, 0:1]
        value = stream[rows, :] + branchw[rows, :]
        stream[rows, :] = value
        xin[rows, :] = to_low(normal(value, rows, 3) * (1.0 + pick(7, seg)) + pick(6, seg))
        gfour[rows, :] = to_low(wide32(cotp[rows, :]) * pick(8, seg))

    each_rows(32, after_cross)
    save(xhat.at[3], xhat_o.at[3])
    save(rstd.at[3], rstd_o.at[3])
    save(gfour, gfour_o)

    turned(xin, 4)
    same = (
        lax.broadcasted_iota(jnp.int32, (TILE, TILE), 0) == lax.broadcasted_iota(jnp.int32, (TILE, TILE), 1)
    ).astype(jnp.float32).astype(jnp.bfloat16)
    for k in range(4):
        slot = k % 2
        load(10 + 2 * k)
        settle(SLOPE_SEM + slot)
        settle(LEFT_SEM + slot)

        def emit_hidden(cols, value, slot=slot):
            inner = math.sqrt(2.0 / math.pi) * (value + 0.044715 * value * value * value)
            bent = jnp.tanh(inner)
            half = 0.5 * (1.0 + bent)
            tilt = math.sqrt(2.0 / math.pi) * (1.0 + 3 * 0.044715 * value * value)
            slope[slot, :, cols] = to_low(half + 0.5 * value * (1.0 - bent * bent) * tilt)
            low = to_low(value * half)
            post[:, cols] = low
            left[slot, cols, :] = to_low(nt(same, low))

        times(xp, 10 + 2 * k, emit_hidden)
        save(slope.at[slot], slope_o.at[k], SLOPE_SEM + slot)
        save(left.at[slot], left_o.at[k], LEFT_SEM + slot)
        load(11 + 2 * k)

        def emit_out(cols, value, k=k):
            branchw[:, cols] = value if k == 0 else branchw[:, cols] + value

        times(post, 11 + 2 * k, emit_out)

    gate[...] = jnp.zeros_like(gate)

    def last(rows):
        seg = seg_in[0, rows, 0:1]
        value = branchw[rows, :]
        xin[rows, :] = to_low(stream[rows, :] + pick(8, seg) * value)
        value = wide32(cotp[rows, :]) * value
        later = jnp.sum(value * seg, axis=0, keepdims=True)
        every = jnp.sum(value, axis=0, keepdims=True)
        gate[0:1, :] = gate[0:1, :] + (every - later)
        gate[1:2, :] = gate[1:2, :] + later

    each_rows(32, last)
    save(gate, gate_o)
    out[...] = to_low(linear(swap_rows(), xin[...]))

    for copy in held.values():
        copy.wait()
    for k in range(1, 8):
        t_copy(k).wait_send()
        m_copy(k, b).wait_send()
    for k in (1, 2, 3):
        x_copy(k, z).wait_send()
    x_over(y).wait_send()
    for at, to in ((0, twin), (1, first), (2, second)):
        g_copy(at, at, to).wait_send()
    for k in (1, 2, 3):
        remote(gains.at[3], gain_at.at[2 + k], g_send.at[2 + k], g_recv.at[2 + k], near[k - 1]).wait_send()

    def finish(t):
        for k in (1, 2, 3):
            z_copy(t, k).wait_send()
        for index in range(7):
            sends(t, index).wait_send()

    loop(BLOCKS, finish)


ANY = pl.BlockSpec(memory_space=pl.ANY)
IN_VMEM = pl.BlockSpec(memory_space=pltpu.VMEM)


def forward(src, tok, cot, gain_in, mod_in, text_in, seg_in, seg_row, turn):
    low, full = jnp.bfloat16, jnp.float32
    dma = pltpu.SemaphoreType.DMA
    hbm = [
        ((BLOCKS, WIDE, WIDE), low),
        ((ROWS, WIDE), low),
        ((11, WIDE, ROWS), low),
        ((3, ROWS, WIDE), low),
        ((3, ROWS, WIDE), low),
        ((ROWS, WIDE), low),
        ((2, WIDE, KEYS), low),
        ((4, ROWS, WIDE), low),
        ((4, ROWS, 128), full),
        ((2, ROWS, WIDE), low),
        ((4, ROWS, WIDE), low),
        ((ROWS, WIDE), low),
        ((ROWS, WIDE), low),
        ((8, MOD), full),
        ((8, WIDE), full),
        ((8, WIDE), full),
    ]
    vmem = [
        ((BLOCKS, 4, WINDOW, WIDE), low),
        ((BLOCKS, LINE, WIDE), low),
        ((2, WIDE, WIDE), low),
        ((ROWS, WIDE), low),
        ((ROWS, WIDE), low),
        ((8, 32, WIDE), low),
        ((ROWS, WIDE), low),
        ((ROWS, WIDE), low),
        ((2, WIDE, ROWS), low),
        ((3, ROWS, WIDE), low),
        ((3, ROWS, WIDE), low),
        ((ROWS, WIDE), low),
        ((2, WIDE, KEYS), low),
        ((4, 2, TEXT, KEYS), low),
        ((8, 32, 128), low),
        ((8, MOD), full),
        ((4, ROWS, WIDE), low),
        ((4, ROWS, 128), full),
        ((2, ROWS, WIDE), low),
        ((ROWS, WIDE), full),
        ((128, 128), full),
        ((ROWS, WIDE), full),
        ((ROWS, WIDE), low),
        ((16, 16, WIDE), low),
        ((ROWS, WIDE), low),
        ((2, ROWS, WIDE), low),
        ((ROWS, WIDE), low),
        ((5, 8, WIDE), full),
        ((6, 8, WIDE), full),
        ((8, WIDE), full),
    ]
    return pl.pallas_call(
        forward_kernel,
        out_shape=[jax.ShapeDtypeStruct(*shape) for shape in hbm],
        in_specs=[IN_VMEM] * 9,
        out_specs=[ANY, IN_VMEM] + [ANY] * 14,
        scratch_shapes=[pltpu.VMEM(*shape) for shape in vmem]
        + [
            dma((BLOCKS, 3)), dma((BLOCKS, 3)), dma((BLOCKS, 7)), dma((BLOCKS, 7)), dma((BLOCKS,)), dma((2,)),
            dma((7,)), dma((7,)), dma((7, 2)), dma((7, 2)), dma((7,)), dma((7,)), dma((4,)), dma((4,)),
            dma((6,)), dma((6,)), dma((SAVE_SEMS,)),
        ],
        compiler_params=pltpu.CompilerParams(
            collective_id=0, has_side_effects=True, vmem_limit_bytes=60 * MIB
        ),
        name="forward",
    )(src, tok, cot, gain_in, mod_in, text_in, seg_in, seg_row, turn)


def tn(left, right):
    return lax.dot_general(
        left, right, (((0,), (0,)), ((), ())), preferred_element_type=jnp.float32
    )


def text_heads_backward(h, query, key, value, grad, dquery, dkey, dvalue, bias, mask):
    jobs = chains(h, VIDEOS)
    scores, grads = [], []
    for (lanes, on), rows, keys in jobs:
        low_on = to_low(on)
        scores.append(linear(query[rows, lanes] * low_on, key[lanes, keys]))
        grads.append(linear(grad[rows, lanes] * low_on, value[lanes, keys]))
    probs = soft(jnp.concatenate(scores), bias, mask)
    grad_probs = jnp.concatenate(grads)
    delta = jnp.sum(grad_probs * probs, axis=-1, keepdims=True)
    slopes = split_rows(to_low(probs * (grad_probs - delta)), jobs)
    probs = split_rows(to_low(probs), jobs)
    parts = []
    for slope, prob, ((lanes, on), rows, keys) in zip(slopes, probs, jobs):
        low_on = to_low(on)
        parts.append(
            (
                to_low(nt(slope, key[lanes, keys]) * (on * SCALE)),
                to_low(tn(query[rows, lanes] * low_on, slope) * SCALE),
                to_low(tn(grad[rows, lanes] * low_on, prob)),
            )
        )
    for (by_query, by_key, by_value), ((lanes, on), rows, keys) in zip(parts, jobs):
        dquery[rows, lanes] = dquery[rows, lanes] + by_query
        dkey[lanes, keys] = dkey[lanes, keys] + by_key
        dvalue[lanes, keys] = dvalue[lanes, keys] + by_value


def heads_backward(h, query, key, value, grad, dquery, dkey, dvalue, groups, bias, mask):
    jobs = chains(h, groups)
    scores, grads = [], []
    for (lanes, on), rows, keys in jobs:
        low_on = to_low(on)
        scores.append(nt(query[rows, lanes] * low_on, key[keys, lanes]))
        grads.append(nt(grad[rows, lanes] * low_on, value[keys, lanes]))
    probs = soft(jnp.concatenate(scores), bias, mask)
    grad_probs = jnp.concatenate(grads)
    delta = jnp.sum(grad_probs * probs, axis=-1, keepdims=True)
    slopes = split_rows(to_low(probs * (grad_probs - delta)), jobs)
    probs = split_rows(to_low(probs), jobs)
    parts = []
    for slope, prob, ((lanes, on), rows, keys) in zip(slopes, probs, jobs):
        parts.append(
            (
                to_low(linear(slope, key[keys, lanes]) * (on * SCALE)),
                to_low(tn(slope, query[rows, lanes]) * (on * SCALE)),
                to_low(tn(prob, grad[rows, lanes]) * on),
            )
        )
    for (by_query, by_key, by_value), ((lanes, on), rows, keys) in zip(parts, jobs):
        dquery[rows, lanes] = dquery[rows, lanes] + by_query
        dkey[keys, lanes] = dkey[keys, lanes] + by_key
        dvalue[keys, lanes] = dvalue[keys, lanes] + by_value


def backward_kernel(
    wide, left_i, qkvs_i, qkvt_i, qc_i, mem_i, xhat_i, rstd_i, branch_i, slope_i, gfour_i, cot_i, mods_i, gate_i, gain_i,
    seg_in, seg_row, turn, cond_in,
    total, gtok, gain_o, text_o, mod_o,
    weights, left, right, qkv, xhat, rstd, branch, slope, mods, gain, bias, stream, work, grad, xin, gm, mem, dmem, text, texts, text_at, mod_out, mod,
    seqs, gains, gain_at, gframe, back, backp,
    s0, r0, s1, r1, s2, r2, k2, s3, r3, share,
    in_sem, w_sem, s0_sem, r0_sem, s1_sem, r1_sem, s2_sem, r2_sem, s3_sem, r3_sem, share_sem,
    a_send, a_recv, u_send, u_recv, x_send, x_recv, m_send, m_recv, q_send, q_recv, g_send, g_recv,
):
    x, c, y, z, x1, y1, x2, y2 = place()
    b = z * 2 + y
    near = [device(x, c, y, (z + k) % 4) for k in (1, 2, 3)]
    first, second, twin = device(x1, c, y1, z), device(x2, c, y2, z), device(x, 1 - c, y, z)
    peers = blk_peers(x, c, b)
    across = [twin, device(1 - x, c, y, z), device(1 - x, 1 - c, y, z)]
    greet(peers + across)

    fetches = {}

    def fetch(name, from_ref, to_ref):
        fetches[name] = pltpu.make_async_copy(from_ref, to_ref, in_sem.at[name])
        fetches[name].start()

    def have(name):
        if name in fetches:
            fetches.pop(name).wait()

    fetch(0, gfour_i, right.at[0])
    for k in range(11):
        fetch(1 + k, left_i.at[k], left.at[k])
    fetch(12, mods_i, mods)
    fetch(13, gain_i, gain)
    fetch(14, slope_i.at[0], slope.at[0])
    fetch(15, slope_i.at[1], slope.at[1])
    fetch(16, xhat_i.at[3], xhat.at[1])
    fetch(17, rstd_i.at[3], rstd.at[1])
    fetch(18, cot_i, xin)
    fetch(19, gate_i, work.at[0:8])

    def weight(block):
        slot = WEIGHT_ORDER.index(block) % 2
        return weights.at[slot]

    def prefetch(at):
        if at < len(WEIGHT_ORDER):
            copy = pltpu.make_async_copy(wide.at[WEIGHT_ORDER[at]], weights.at[at % 2], w_sem.at[at % 2])
            copy.start()
            fetches["w", WEIGHT_ORDER[at]] = copy

    def release(block):
        prefetch(WEIGHT_ORDER.index(block) + 2)

    prefetch(0)
    prefetch(1)

    away = [(1 - x) * 2 + 1 - y, x2 * 2 + y2]
    stay = [x1 * 2 + y1, x * 2 + y]

    def product(t, core, xl):
        rows = pl.ds(pl.multiple_of(line_of(core, xl, 0) * LINE, 16), 2 * LINE)
        return linear(left[left_at(t), rows, :], right[right_at(t)])

    def copy0(t, l):
        pair = pl.ds(2 * l, 2)
        return remote(s0.at[t % 2, pair], r0.at[t % 4, pair], s0_sem.at[t % 2, l], r0_sem.at[t % 4, l], twin)

    def copy1(t, l):
        return remote(s1.at[t % 2, away[l]], r1.at[t % 4, l], s1_sem.at[t % 2, l], r1_sem.at[t % 4, l], second)

    def copy2(t):
        return remote(s2.at[t % 2], r2.at[t % 4], s2_sem.at[t % 2], r2_sem.at[t % 4], first)

    def copy3(t, k):
        part = pl.ds(pl.multiple_of(32 * ((z + k) % 4), 16), WINDOW)
        return remote(s3.at[t % 2, part], r3.at[t % 4, k - 1], s3_sem.at[t % 2, k - 1], r3_sem.at[t % 4, k - 1], near[k - 1])

    def share_copy(t):
        return pltpu.make_async_copy(share.at[t % 2], total.at[t], share_sem.at[t % 2])

    def tick(t):
        @pl.when(t < BLOCKS)
        def _():
            for l in range(2):
                @pl.when(t >= 2)
                def _():
                    copy0(t - 2, l).wait_send()
                value = to_low(product(t, 1 - c, l))
                s0[t % 2, 2 * l] = value[:LINE]
                s0[t % 2, 2 * l + 1] = value[LINE:]
                copy0(t, l).start()

        @pl.when((t >= 1) & (t < BLOCKS + 1))
        def _():
            now = t - 1

            @pl.when(now >= 2)
            def _():
                for l in range(2):
                    copy1(now - 2, l).wait_send()
            for l in range(2):
                copy0(now, l).wait_recv()
                value = product(now, c, l)
                for part in range(2):
                    line = 2 * l + part
                    summed = value[part * LINE : part * LINE + LINE] + wide32(r0[now % 4, line])
                    s1[now % 2, line] = to_low(summed)
            for l in range(2):
                copy1(now, l).start()

        @pl.when((t >= 2) & (t < BLOCKS + 2))
        def _():
            now = t - 2
            copy1(now, 0).wait_recv()

            @pl.when(now >= 2)
            def _():
                copy2(now - 2).wait_send()
            s2[now % 2] = to_low(wide32(s1[now % 2, stay[0]]) + wide32(r1[now % 4, 0]))
            copy2(now).start()
            copy1(now, 1).wait_recv()
            k2[now % 2] = wide32(s1[now % 2, stay[1]]) + wide32(r1[now % 4, 1])

        @pl.when((t >= 3) & (t < BLOCKS + 3))
        def _():
            now = t - 3
            copy2(now).wait_recv()

            @pl.when(now >= 2)
            def _():
                for k in (1, 2, 3):
                    copy3(now - 2, k).wait_send()
            value = k2[now % 2] + wide32(r2[now % 4])
            s3[now % 2] = to_low(value)
            for k in (1, 2, 3):
                copy3(now, k).start()

        @pl.when(t >= 4)
        def _():
            now = t - 4
            value = wide32(s3[now % 2, pl.ds(pl.multiple_of(32 * z, 16), WINDOW)])
            for k in (1, 2, 3):
                copy3(now, k).wait_recv()
                value = value + wide32(r3[now % 4, k - 1])

            @pl.when(now >= 2)
            def _():
                share_copy(now - 2).wait()
            share[now % 2] = value
            share_copy(now).start()

    done = [0]

    def pump(until):
        if until > done[0]:
            start = done[0]
            loop(until - start, lambda i: tick(i + start))
            done[0] = until

    def pick(piece, seg):
        lanes = slice(WIDE * piece, WIDE * piece + WIDE)
        return jnp.where(seg > 0.5, mods[1:2, lanes], mods[0:1, lanes])

    def by_video(piece, value, seg):
        lanes = slice(WIDE * piece, WIDE * piece + WIDE)
        later = jnp.sum(value * seg, axis=0, keepdims=True)
        every = jnp.sum(value, axis=0, keepdims=True)
        gm[0:1, lanes] = gm[0:1, lanes] + (every - later)
        gm[1:2, lanes] = gm[1:2, lanes] + later

    def through(values_at, blocks, emit, grouped=False):
        for n, (values, block) in enumerate(zip(values_at, blocks)):
            have(("w", block))

            def tile(cols, n=n, values=values, block=block):
                part = nt(values[...], weight(block)[cols, :])
                if n > 0:
                    part = part + work[:, cols]
                if n == len(blocks) - 1:
                    xin[:, cols] = to_low(part)
                else:
                    work[:, cols] = part

            each_cols(tile)
            release(block)
        if grouped:
            xin[...] = to_low(linear(regroup(True), xin[...]))
        turn_back(emit)

    def turn_back(emit):
        each_cols(lambda cols: emit(cols, linear(xin[...], turn[:, cols])))

    def emit_work(cols, value):
        work[:, cols] = value

    def emit_grad(cols, value):
        grad[:, cols] = to_low(value)

    def norm_back(grad_in, tilt, at, rows):
        slope_in = grad_in * tilt
        hat = wide32(xhat[at, rows, :])
        first_mean = jnp.mean(slope_in, axis=-1, keepdims=True)
        second_mean = jnp.mean(slope_in * hat, axis=-1, keepdims=True)
        return rstd[at, rows, 0:1] * (slope_in - first_mean - hat * second_mean)

    gm[...] = jnp.zeros_like(gm)
    have(0)
    have(12)
    have(18)
    have(19)
    gm[0:8, 8 * WIDE : 9 * WIDE] = work[0:8]
    stream[...] = wide32(xin[...])
    for k in range(5):
        have(1 + k)
    pump(1)
    for k in range(4):
        have(14 + k % 2 if k < 2 else ("slope", k))
        have(("w", 11 + 2 * k))

        def tile(cols, k=k):
            value = nt(right[0], weight(11 + 2 * k)[cols, :]) * wide32(slope[k % 2, :, cols])
            right[1 + k, :, cols] = to_low(value)

        each_cols(tile)
        release(11 + 2 * k)
        if k < 2:
            copy = pltpu.make_async_copy(slope_i.at[k + 2], slope.at[k % 2], in_sem.at[14 + k])
            copy.start()
            fetches["slope", k + 2] = copy
        have(("w", 10 + 2 * k))

        def tile(cols, k=k):
            part = nt(right[1 + k], weight(10 + 2 * k)[cols, :])
            if k > 0:
                part = part + work[:, cols]
            if k < 3:
                work[:, cols] = part
            else:
                xin[:, cols] = to_low(part)

        each_cols(tile)
        release(10 + 2 * k)
        pump(k + 2)
    turn_back(emit_work)
    for k in range(5, 11):
        have(1 + k)
    have(16)
    have(17)
    fetch(20, qc_i, qkv.at[0])
    fetch(21, mem_i.at[0], mem.at[0])
    fetch(22, mem_i.at[1], mem.at[1])
    fetch(23, xhat_i.at[2], xhat.at[0])
    fetch(24, rstd_i.at[2], rstd.at[0])

    def after_mlp(rows):
        seg = seg_in[0, rows, 0:1]
        value = work[rows, :]
        by_video(6, value, seg)
        by_video(7, value * wide32(xhat[1, rows, :]), seg)
        value = stream[rows, :] + norm_back(value, 1.0 + pick(7, seg), 1, rows)
        stream[rows, :] = value
        right[5, rows, :] = to_low(value)

    each_rows(32, after_mlp)

    fetch(25, xhat_i.at[1], xhat.at[1])
    fetch(26, rstd_i.at[1], rstd.at[1])
    through([right.at[5]], [9], emit_grad)
    right[6] = jnp.zeros_like(right[6])
    dmem[...] = jnp.zeros_like(dmem)
    for name in (13, 20, 21, 22, 23, 24):
        have(name)

    def cross_heads(h):
        text_heads_backward(
            h, qkv.at[0], mem.at[0], mem.at[1], grad, right.at[6], dmem.at[0], dmem.at[1],
            cross_bias(), cross_rows(seg_in),
        )

    for part in range(4):
        loop(2, lambda h: cross_heads(h + 2 * part))
        pump(6 + part if part < 3 else 8)

    def dmem_part(zp, yp):
        return dmem.at[zp // 2, pl.ds(pl.multiple_of(TEXT * (zp % 2 * 2 + yp), 16), TEXT)]

    def x_over(zp):
        return remote(dmem_part(zp, 1 - y), text.at[zp], x_send.at[zp], x_recv.at[zp], device(x, c, 1 - y, z))

    def x_copy(k):
        return remote(texts.at[(z + k) % 4], text_at.at[k - 1], x_send.at[3 + k], x_recv.at[3 + k], near[k - 1])

    for zp in range(4):
        x_over(zp).start()
    fetch(27, qkvt_i.at[0], qkv.at[0])
    fetch(28, qkvt_i.at[1], qkv.at[1])
    fetch(29, qkvt_i.at[2], qkv.at[2])
    fetch(30, branch_i.at[1], branch)
    through([right.at[6]], [8], emit_work)
    gains[0] = jnp.zeros_like(gains[0])
    have(30)

    def after_cross(rows):
        seg = seg_in[0, rows, 0:1]
        value = work[rows, :]
        gains[0, 0:1, :] = gains[0, 0:1, :] + jnp.sum(value * wide32(xhat[0, rows, :]), axis=0, keepdims=True)
        value = stream[rows, :] + norm_back(value, gain[0:1, :], 0, rows)
        stream[rows, :] = value
        by_video(5, value * wide32(branch[rows, :]), seg)
        right[7, rows, :] = to_low(value * pick(5, seg))

    each_rows(32, after_cross)

    def g_copy(at, to):
        return remote(gains.at[min(at, 3)], gain_at.at[at], g_send.at[at], g_recv.at[at], to)

    g_copy(0, twin).start()
    fetch(31, branch_i.at[0], branch)
    fetch(32, xhat_i.at[0], xhat.at[0])
    fetch(33, rstd_i.at[0], rstd.at[0])
    pump(9)

    through([right.at[7]], [7], emit_grad)
    grad[...] = to_low(linear(regroup(False), grad[...]))
    bias[...] = temporal_bias(seg_in, seg_row)
    for j in range(3):
        right[8 + j] = jnp.zeros_like(right[8 + j])
    for name in (25, 26, 27, 28, 29):
        have(name)

    def temporal_heads(h):
        heads_backward(
            h, qkv.at[0], qkv.at[1], qkv.at[2], grad, right.at[8], right.at[9], right.at[10],
            HALVES, jnp.concatenate([bias[...]] * 4), None,
        )

    loop(4, temporal_heads)
    pump(10)
    g_copy(0, twin).wait_recv()
    gains[1] = gains[0] + gain_at[0]
    g_copy(1, first).start()
    loop(4, lambda h: temporal_heads(h + 4))
    pump(11)
    g_copy(1, first).wait_recv()
    gains[2] = gains[1] + gain_at[1]
    g_copy(2, second).start()
    for zp in range(4):
        x_over(zp).wait_recv()
        texts[zp] = to_low(wide32(dmem_part(zp, y)[...]) + wide32(text[zp]))
    for k in (1, 2, 3):
        x_copy(k).start()
    for j in range(3):
        fetch(34 + j, qkvs_i.at[j], qkv.at[j])
    through([right.at[8], right.at[9], right.at[10]], [4, 5, 6], emit_work, True)
    have(31)

    def after_temporal(rows):
        seg = seg_in[0, rows, 0:1]
        value = work[rows, :]
        by_video(3, value, seg)
        by_video(4, value * wide32(xhat[1, rows, :]), seg)
        value = stream[rows, :] + norm_back(value, 1.0 + pick(4, seg), 1, rows)
        stream[rows, :] = value
        by_video(2, value * wide32(branch[rows, :]), seg)
        right[11, rows, :] = to_low(value * pick(2, seg))

    each_rows(32, after_temporal)

    through([right.at[11]], [3], emit_grad)

    def a_copy(k):
        to = (b + k) % 8
        part = grad.at[pl.ds(pl.multiple_of(32 * to, 32), 32)]
        return remote(part, back.at[b], a_send.at[k - 1], a_recv.at[k - 1], peers[k - 1])

    def a_wait(k):
        of = (b + 8 - k) % 8
        remote(grad.at[pl.ds(0, 32)], back.at[of], a_send.at[k - 1], a_recv.at[k - 1], peers[k - 1]).wait_recv()

    for k in (1, 2, 3):
        x_copy(k).wait_recv()
    text_o[...] = to_low(wide32(texts[z]) + wide32(text_at[0]) + wide32(text_at[1]) + wide32(text_at[2]))
    for k in range(1, 8):
        a_copy(k).start()
    back[b] = grad[pl.ds(pl.multiple_of(32 * b, 32), 32)]
    pump(12)
    g_copy(2, second).wait_recv()
    gains[3] = gains[2] + gain_at[2]
    for k in (1, 2, 3):
        g_copy(2 + k, near[k - 1]).start()
    for j in range(3):
        right[12 + j] = jnp.zeros_like(right[12 + j])
    for name in (32, 33, 34, 35, 36):
        have(name)
    for k in range(1, 8):
        a_wait(k)
    for k in range(8):
        for f in range(2):
            gframe[128 * f + 16 * k : 128 * f + 16 * k + 16, :] = back[k, 16 * f : 16 * f + 16, :]

    def spatial_heads(h):
        heads_backward(
            h, qkv.at[0], qkv.at[1], qkv.at[2], gframe, right.at[12], right.at[13], right.at[14], HALVES, None, None
        )

    loop(4, spatial_heads)
    pump(14)
    loop(4, lambda h: spatial_heads(h + 4))
    pump(15)
    through([right.at[12], right.at[13], right.at[14]], [0, 1, 2], emit_work)
    pump(16)
    for k in range(1, 8):
        a_copy(k).wait_send()

    def after_spatial(i):
        rows = pl.ds(pl.multiple_of(16 * i, 16), 16)
        seg = seg_in[1, rows, 0:1]
        value = work[rows, :]
        by_video(0, value, seg)
        by_video(1, value * wide32(xhat[0, rows, :]), seg)
        value = to_low(norm_back(value, 1.0 + pick(1, seg), 0, rows))
        back[i % 8, pl.ds(pl.multiple_of(16 * (i // 8), 16), 16), :] = value

    loop(16, after_spatial)

    def u_copy(k):
        to = (b + k) % 8
        return remote(back.at[to], backp.at[b], u_send.at[k - 1], u_recv.at[k - 1], peers[k - 1])

    def u_wait(k):
        of = (b + 8 - k) % 8
        remote(back.at[0], backp.at[of], u_send.at[k - 1], u_recv.at[k - 1], peers[k - 1]).wait_recv()

    def m_copy(k):
        to = (b + k) % 8
        return remote(mod_out.at[to], mod.at[b], m_send.at[k - 1], m_recv.at[k - 1], peers[k - 1])

    def m_wait(k):
        of = (b + 8 - k) % 8
        remote(mod_out.at[0], mod.at[of], m_send.at[k - 1], m_recv.at[k - 1], peers[k - 1]).wait_recv()

    for k in range(1, 8):
        u_copy(k).start()
    backp[b] = back[b]
    for k in range(8):
        tiles = [
            gm[row : row + 1, 1280 * k + 128 * tile : 1280 * k + 128 * tile + 128]
            for row in range(2)
            for tile in range(MOD_TILES)
        ]
        mod_out[k] = to_low(jnp.concatenate(tiles + [jnp.zeros((32 - 2 * MOD_TILES, 128), jnp.float32)]))
    for k in range(1, 8):
        m_copy(k).start()
    mod[b] = mod_out[b]
    pump(18)
    for k in range(1, 8):
        m_wait(k)
    summed = wide32(mod[0])
    for k in range(1, 8):
        summed = summed + wide32(mod[k])
    own = x * 2 + c
    seqs[own, 0:32] = to_low(summed)
    seqs[own, 32:64] = cond_in[...]
    places = [x * 2 + 1 - c, (1 - x) * 2 + c, (1 - x) * 2 + 1 - c]

    def q_copy(k, at):
        return remote(seqs.at[own], seqs.at[at], q_send.at[k], q_recv.at[k], across[k])

    for k in range(3):
        q_copy(k, own).start()
    for k in range(1, 8):
        u_wait(k)
    xin[...] = to_low(stream[...] + wide32(backp[...].reshape(ROWS, WIDE)))
    gtok[...] = to_low(linear(swap_rows(), xin[...]))
    for k in (1, 2, 3):
        g_copy(2 + k, near[k - 1]).wait_recv()
    gain_o[...] = gains[3] + gain_at[3] + gain_at[4] + gain_at[5]
    pump(BLOCKS + 4)
    for k in range(3):
        q_copy(k, places[k]).wait_recv()
    mod_o[...] = seqs[...]

    for now in (BLOCKS - 2, BLOCKS - 1):
        for l in range(2):
            copy0(now, l).wait_send()
            copy1(now, l).wait_send()
        copy2(now).wait_send()
        for k in (1, 2, 3):
            copy3(now, k).wait_send()
        share_copy(now).wait()
    for k in range(1, 8):
        u_copy(k).wait_send()
        m_copy(k).wait_send()
        x_over(k - 1).wait_send() if k < 5 else x_copy(k - 4).wait_send()
    for k in range(3):
        q_copy(k, own).wait_send()
    for at, to in enumerate([twin, first, second] + near):
        g_copy(at, to).wait_send()


WEIGHT_ORDER = (11, 10, 13, 12, 15, 14, 17, 16, 9, 8, 7, 4, 5, 6, 3, 0, 1, 2)


def backward(*operands):
    low, full = jnp.bfloat16, jnp.float32
    dma = pltpu.SemaphoreType.DMA
    outs = [
        ((BLOCKS, WINDOW, WIDE), full),
        ((ROWS, WIDE), low),
        ((8, WIDE), full),
        ((TEXT, KEYS), low),
        ((4, 64, 128), low),
    ]
    vmem = [
        ((2, WIDE, WIDE), low),
        ((11, WIDE, ROWS), low),
        ((15, ROWS, WIDE), low),
        ((3, ROWS, WIDE), low),
        ((2, ROWS, WIDE), low),
        ((2, ROWS, 128), full),
        ((ROWS, WIDE), low),
        ((2, ROWS, WIDE), low),
        ((8, MOD), full),
        ((8, WIDE), full),
        ((128, 128), full),
        ((ROWS, WIDE), full),
        ((ROWS, WIDE), full),
        ((ROWS, WIDE), low),
        ((ROWS, WIDE), low),
        ((8, MOD), full),
        ((2, WIDE, KEYS), low),
        ((2, WIDE, KEYS), low),
        ((4, TEXT, KEYS), low),
        ((4, TEXT, KEYS), low),
        ((3, TEXT, KEYS), low),
        ((8, 32, 128), low),
        ((8, 32, 128), low),
        ((4, 64, 128), low),
        ((4, 8, WIDE), full),
        ((6, 8, WIDE), full),
        ((ROWS, WIDE), low),
        ((8, 32, WIDE), low),
        ((8, 32, WIDE), low),
        ((2, 4, LINE, WIDE), low),
        ((4, 4, LINE, WIDE), low),
        ((2, 4, LINE, WIDE), low),
        ((4, 2, LINE, WIDE), low),
        ((2, LINE, WIDE), low),
        ((4, LINE, WIDE), low),
        ((2, LINE, WIDE), full),
        ((2, LINE, WIDE), low),
        ((4, 3, WINDOW, WIDE), low),
        ((2, WINDOW, WIDE), full),
    ]
    return pl.pallas_call(
        backward_kernel,
        out_shape=[jax.ShapeDtypeStruct(*shape) for shape in outs],
        in_specs=[ANY] * 15 + [IN_VMEM] * 4,
        out_specs=[ANY] + [IN_VMEM] * 4,
        scratch_shapes=[pltpu.VMEM(*shape) for shape in vmem]
        + [
            dma((40,)), dma((2,)), dma((2, 4)), dma((4, 4)), dma((2, 2)), dma((4, 2)), dma((2,)), dma((4,)),
            dma((2, 3)), dma((4, 3)), dma((2,)), dma((7,)), dma((7,)), dma((7,)), dma((7,)), dma((7,)), dma((7,)),
            dma((7,)), dma((7,)), dma((3,)), dma((3,)), dma((6,)), dma((6,)),
        ],
        compiler_params=pltpu.CompilerParams(
            collective_id=1, has_side_effects=True, vmem_limit_bytes=63 * MIB
        ),
        name="backward",
    )(*operands)


TURN = np.arange(WIDE)[None, :] == (
    np.arange(WIDE).reshape(2, 2, 4, 2, SHARD).transpose(1, 0, 3, 2, 4).reshape(-1)
)[:, None]


def hidden_order(values):
    rows = values.shape[0]
    cut = values.reshape(rows, 2, 2, 4, 2, 4, SHARD)
    return cut.transpose(0, 5, 2, 1, 4, 3, 6).reshape(rows, 4 * WIDE)


def hidden_back(values):
    rows = values.shape[0]
    cut = values.reshape(rows, 4, 2, 2, 2, 4, SHARD)
    return cut.transpose(0, 3, 2, 5, 4, 1, 6).reshape(rows, 4 * WIDE)


def by_block(values):
    rows = values.shape[0]
    return values.reshape(rows, -1, WIDE).transpose(1, 0, 2)


def shards(
    tokens,
    segments,
    timesteps,
    caption,
    cotangent,
    ada_weight,
    ada_bias,
    spatial_in,
    spatial_out,
    temporal_in,
    temporal_out,
    cross_gain,
    cross_query,
    caption_proj,
    cross_out,
    hidden_in,
    hidden_out,
):
    frame_seg = segments[0]
    text_width = caption.shape[-1]
    caption_rows = caption[0].reshape(2 * L, text_width)
    blk = lax.axis_index("blk")
    seq = lax.axis_index("seq")
    zplace = blk // 2
    hidden_blocks = by_block(hidden_order(hidden_in))
    hidden_rows = hidden_out.reshape(4, SHARD, WIDE)
    stack = jnp.concatenate(
        [
            by_block(spatial_in),
            spatial_out[None],
            by_block(temporal_in),
            temporal_out[None],
            cross_query[None],
            cross_out[None],
        ]
        + [part[k][None] for k in range(4) for part in (hidden_blocks, hidden_rows)]
    )
    windows = lax.dynamic_update_slice(
        jnp.zeros((BLOCKS, WINDOW, WIDE), jnp.bfloat16), stack, (0, 4 * zplace, 0)
    )
    gain_in = lax.dynamic_update_slice(
        jnp.zeros((8, WIDE), jnp.float32),
        cross_gain.astype(jnp.float32)[None],
        (0, SHARD * (seq * 8 + blk)),
    )
    conditioning = to_low(jax.nn.silu(time_embedding(timesteps[0], WIDE)))
    mod_part = to_low(linear(conditioning, ada_weight) + ada_bias.astype(jnp.float32))
    mod_in = lax.dynamic_update_slice(
        jnp.zeros((2, MOD_WIN), jnp.bfloat16), mod_part, (0, 16 * blk)
    ).reshape(2 * MOD_TILES, 128)
    mod_in = jnp.pad(mod_in, ((0, 32 - 2 * MOD_TILES), (0, 0)))
    cond_in = jnp.pad(conditioning.reshape(2 * WIDE // 128, 128), ((0, 32 - 2 * WIDE // 128), (0, 0)))
    text_part = to_low(
        lax.dot_general(
            caption_proj, caption_rows, (((0,), (1,)), ((), ())), preferred_element_type=jnp.float32
        )
    )
    text_in = jnp.pad(text_part.reshape(TEXT, 2, L), ((0, 0), (0, 0), (0, 128 - L))).reshape(TEXT, KEYS)
    frames = frame_seg.astype(jnp.float32)
    own_frames = lax.dynamic_slice(frames, (2 * blk,), (2,))
    seg_in = jnp.broadcast_to(
        jnp.stack(
            [jnp.repeat(frames, 16), jnp.repeat(own_frames, 128), jnp.tile(jnp.repeat(frames, 8), 2)]
        )[:, :, None],
        (3, ROWS, 128),
    )
    seg_row = jnp.broadcast_to(jnp.repeat(frames, 8)[None], (8, 128))
    turn = jnp.asarray(TURN, jnp.bfloat16)
    wide, out, *kept = forward(
        windows,
        tokens.reshape(ROWS, WIDE),
        cotangent.reshape(ROWS, WIDE),
        gain_in,
        mod_in,
        text_in,
        seg_in,
        seg_row,
        turn,
    )
    spread, grad_tokens, grad_gain, grad_text, grad_mod = backward(
        wide, *kept, seg_in, seg_row, turn, cond_in
    )
    shares = lax.dynamic_slice(spread, (0, 4 * zplace, 0), (BLOCKS, SHARD, WIDE))
    share_gain = lax.dynamic_slice(grad_gain, (0, SHARD * (seq * 8 + blk)), (1, SHARD))[0]
    text_low = grad_text.reshape(TEXT, 2, 128)[:, :, :L].reshape(TEXT, 2 * L)
    grad_caption = lax.dot_general(
        caption_rows, text_low, (((0,), (1,)), ((), ())), preferred_element_type=jnp.float32
    )
    grad_caption = lax.psum(grad_caption.astype(jnp.bfloat16), "seq").astype(jnp.float32)
    all_mod = lax.dynamic_slice(
        grad_mod[:, : 2 * MOD_TILES].reshape(8, MOD_WIN), (0, 16 * blk), (8, MOD // 8)
    )
    all_cond = grad_mod[:, 32 : 32 + 2 * WIDE // 128].reshape(8, WIDE)
    grad_ada_w = left_product(all_cond, all_mod)
    grad_ada_b = jnp.sum(all_mod.astype(jnp.float32), axis=0)

    def joined(first, count):
        return shares[first : first + count].transpose(1, 0, 2).reshape(SHARD, count * WIDE)

    return (
        out.reshape(tokens.shape),
        grad_tokens.reshape(tokens.shape),
        grad_ada_w,
        grad_ada_b,
        joined(15, 3),
        shares[14],
        joined(11, 3),
        shares[10],
        share_gain,
        shares[9],
        grad_caption,
        shares[8],
        hidden_back(joined(4, 4)),
        shares[0:4].reshape(4 * SHARD, WIDE),
    )


def solution(mesh):
    fast = dict(mesh.shape) == {"seq": 4, "blk": 8}
    return jax.shard_map(
        shards if fast else general_shards,
        mesh=mesh,
        in_specs=(
            P("seq", "blk", None, None),
            P("seq", None),
            P("seq", None),
            P("seq", None, None, None),
            P("seq", "blk", None, None),
            P(None, "blk"),
            P("blk"),
            P(("seq", "blk"), None),
            P(("seq", "blk"), None),
            P(("seq", "blk"), None),
            P(("seq", "blk"), None),
            P(("seq", "blk")),
            P(("seq", "blk"), None),
            P(None, "blk"),
            P(("seq", "blk"), None),
            P(("seq", "blk"), None),
            P(("seq", "blk"), None),
        ),
        out_specs=(
            P("seq", "blk", None, None),
            P("seq", "blk", None, None),
            P(None, "blk"),
            P("blk"),
            P(("seq", "blk"), None),
            P(("seq", "blk"), None),
            P(("seq", "blk"), None),
            P(("seq", "blk"), None),
            P(("seq", "blk")),
            P(("seq", "blk"), None),
            P(None, "blk"),
            P(("seq", "blk"), None),
            P(("seq", "blk"), None),
            P(("seq", "blk"), None),
        ),
        check_vma=False,
    )
```

```python
import math

import jax
import jax.numpy as jnp
import numpy as np
from jax import lax
from jax.experimental import pallas as pl
from jax.experimental.pallas import tpu as pltpu
from jax.sharding import PartitionSpec as P

H = 16
E = 72
L = 120


EPSILON = 1e-06
MASKED = -1e30


def to_low(values):
    return values.astype(jnp.bfloat16)


def linear(left, right):
    return jnp.dot(left, right, preferred_element_type=jnp.float32)


def left_product(left, right):
    return lax.dot_general(
        left, right, (((0,), (0,)), ((), ())), preferred_element_type=jnp.float32
    )


def right_product(left, right):
    return lax.dot_general(
        left, right, (((1,), (1,)), ((), ())), preferred_element_type=jnp.float32
    )


def normalize(values):
    center = values - jnp.mean(values, axis=-1, keepdims=True)
    return center * lax.rsqrt(jnp.mean(center * center, axis=-1, keepdims=True) + EPSILON)


def modulate(values, shift_rows, scale_rows):
    return normalize(values) * (1.0 + scale_rows) + shift_rows


def gain_norm(values, gain_row):
    return normalize(values) * gain_row


def gelu_tanh(values):
    return jax.nn.gelu(values, approximate=True)


def softmax_rows(scores):
    shifted = jnp.exp(scores - jnp.max(scores, axis=-1, keepdims=True))
    return shifted / jnp.sum(shifted, axis=-1, keepdims=True)


def softmax_with_total(scores):
    top = jnp.max(scores, axis=-1, keepdims=True)
    shifted = jnp.exp(scores - top)
    total = jnp.sum(shifted, axis=-1, keepdims=True)
    return (shifted / total, (top + jnp.log(total))[..., 0])


def softmax_back(probs, grad_probs):
    return probs * (grad_probs - jnp.sum(grad_probs * probs, axis=-1, keepdims=True))


def time_embedding(step_ids, model_width):
    half_width = model_width // 2
    frequency = jnp.exp(
        -math.log(10000.0) * jnp.arange(half_width).astype(jnp.float32) / half_width
    )
    angles = step_ids.astype(jnp.float32)[:, None] * frequency[None, :]
    return jnp.concatenate([jnp.cos(angles), jnp.sin(angles)], axis=1)


def general_shards(
    tokens,
    segments,
    timesteps,
    caption,
    cotangent,
    ada_weight,
    ada_bias,
    spatial_in,
    spatial_out,
    temporal_in,
    temporal_out,
    cross_gain,
    cross_query,
    caption_proj,
    cross_out,
    hidden_in,
    hidden_out,
):
    inputs = tokens[0].astype(jnp.float32)
    patch_dev, frames, model_width = inputs.shape
    token_rows = patch_dev * frames
    head_count = H
    head_size = E
    score_scale = E ** (-0.5)
    frame_seg = segments[0]
    step_ids = timesteps[0]
    seg_count, text_len, text_width = caption.shape[1:]
    text_keys = seg_count * text_len
    caption_rows = caption[0].reshape(text_keys, text_width)
    grad_out = cotangent[0].astype(jnp.float32)
    gathered = (
        lax.all_gather(spatial_in, ("seq", "blk"), axis=0, tiled=True),
        lax.all_gather(spatial_out, ("seq", "blk"), axis=0, tiled=True),
        lax.all_gather(temporal_in, ("seq", "blk"), axis=0, tiled=True),
        lax.all_gather(temporal_out, ("seq", "blk"), axis=0, tiled=True),
        lax.all_gather(cross_gain, ("seq", "blk"), axis=0, tiled=True),
        lax.all_gather(cross_query, ("seq", "blk"), axis=0, tiled=True),
        lax.all_gather(cross_out, ("seq", "blk"), axis=0, tiled=True),
        lax.all_gather(hidden_in, ("seq", "blk"), axis=0, tiled=True),
        lax.all_gather(hidden_out, ("seq", "blk"), axis=0, tiled=True),
    )
    (
        wide_sin,
        wide_sout,
        wide_tin,
        wide_tout,
        gain_low,
        wide_query,
        wide_cout,
        wide_hin,
        wide_hout,
    ) = gathered
    gain_row = gain_low.astype(jnp.float32)
    conditioning = to_low(jax.nn.silu(time_embedding(step_ids, model_width)))
    mod_part = to_low(linear(conditioning, ada_weight) + ada_bias.astype(jnp.float32))
    text_part = to_low(linear(caption_rows, caption_proj))
    modulation, memory = (
        lax.all_gather(mod_part, "blk", axis=1, tiled=True),
        lax.all_gather(text_part, "blk", axis=1, tiled=True),
    )
    choose = frame_seg[:, None] == jnp.arange(seg_count, dtype=jnp.int32)[None, :]
    frame_mod = linear(choose.astype(jnp.bfloat16), modulation)
    pieces = [frame_mod[:, index * model_width : (index + 1) * model_width] for index in range(9)]
    (
        shift_one,
        scale_one,
        gate_one,
        shift_two,
        scale_two,
        gate_two,
        shift_three,
        scale_three,
        gate_three,
    ) = pieces
    spatial_input = to_low(modulate(inputs, shift_one, scale_one)).reshape(token_rows, model_width)
    spatial_qkv = to_low(linear(spatial_input, wide_sin)).reshape(
        patch_dev, frames, 3 * model_width
    )
    query_s = spatial_qkv[..., :model_width].reshape(patch_dev, frames, head_count, head_size)
    local_kv = spatial_qkv[..., model_width:]
    whole_kv = lax.all_gather(local_kv, "blk", axis=0, tiled=True)

    def split_kv(both):
        count = both.shape[0]
        return (
            both[..., :model_width].reshape(count, frames, head_count, head_size),
            both[..., model_width:].reshape(count, frames, head_count, head_size),
        )

    def spatial_probs(key_all):
        scores = jnp.einsum("pfhe,qfhe->fhpq", query_s, key_all, preferred_element_type=jnp.float32)
        return softmax_with_total(scores * score_scale)

    key_s, value_s = split_kv(whole_kv)
    probs_s, log_total_s = spatial_probs(key_s)
    probs_s_low = to_low(probs_s)
    attn_s = to_low(
        jnp.einsum(
            "fhpq,qfhe->pfhe", probs_s_low, value_s, preferred_element_type=jnp.float32
        ).reshape(token_rows, model_width)
    )
    branch_s = linear(attn_s, wide_sout).reshape(patch_dev, frames, model_width)
    after_one = inputs + gate_one * branch_s
    temporal_input = to_low(modulate(after_one, shift_two, scale_two)).reshape(
        token_rows, model_width
    )
    temporal_qkv = to_low(linear(temporal_input, wide_tin)).reshape(
        patch_dev, frames, 3, head_count, head_size
    )
    query_t = temporal_qkv[:, :, 0]
    key_t = temporal_qkv[:, :, 1]
    value_t = temporal_qkv[:, :, 2]
    same_seg = frame_seg[:, None] == frame_seg[None, :]
    scores_t = (
        jnp.einsum("pfhe,pghe->phfg", query_t, key_t, preferred_element_type=jnp.float32)
        * score_scale
    )
    probs_t = softmax_rows(jnp.where(same_seg[None, None], scores_t, MASKED))
    probs_t_low = to_low(probs_t)
    attn_t = to_low(
        jnp.einsum(
            "phfg,pghe->pfhe", probs_t_low, value_t, preferred_element_type=jnp.float32
        ).reshape(token_rows, model_width)
    )
    branch_t = linear(attn_t, wide_tout).reshape(patch_dev, frames, model_width)
    after_two = after_one + gate_two * branch_t
    cross_input = to_low(gain_norm(after_two, gain_row)).reshape(token_rows, model_width)
    query_c = to_low(linear(cross_input, wide_query)).reshape(
        patch_dev, frames, head_count, head_size
    )
    key_c = memory[:, :model_width].reshape(text_keys, head_count, head_size)
    value_c = memory[:, model_width:].reshape(text_keys, head_count, head_size)
    key_seg = jnp.arange(text_keys, dtype=jnp.int32) // text_len
    allowed = frame_seg[:, None] == key_seg[None, :]
    scores_c = (
        jnp.einsum("pfhe,khe->pfhk", query_c, key_c, preferred_element_type=jnp.float32)
        * score_scale
    )
    probs_c = softmax_rows(jnp.where(allowed[None, :, None, :], scores_c, MASKED))
    probs_c_low = to_low(probs_c)
    attn_c = to_low(
        jnp.einsum(
            "pfhk,khe->pfhe", probs_c_low, value_c, preferred_element_type=jnp.float32
        ).reshape(token_rows, model_width)
    )
    branch_c = linear(attn_c, wide_cout).reshape(patch_dev, frames, model_width)
    after_three = after_two + branch_c
    mlp_input = to_low(modulate(after_three, shift_three, scale_three)).reshape(
        token_rows, model_width
    )
    pre_act = linear(mlp_input, wide_hin)
    post_act = to_low(gelu_tanh(pre_act))
    branch_m = linear(post_act, wide_hout).reshape(patch_dev, frames, model_width)
    result = after_three + gate_three * branch_m
    grad_gate_three = jnp.sum(grad_out * branch_m, axis=0)
    grad_four = to_low(grad_out * gate_three).reshape(token_rows, model_width)
    grad_hout = left_product(post_act, grad_four)
    grad_post = right_product(grad_four, wide_hout)
    gelu_pull = jax.vjp(gelu_tanh, pre_act)[1]
    grad_pre = to_low(gelu_pull(grad_post)[0])
    grad_hin = left_product(mlp_input, grad_pre)
    grad_mlp_in = right_product(grad_pre, wide_hin).reshape(patch_dev, frames, model_width)
    mlp_pull = jax.vjp(modulate, after_three, shift_three, scale_three)[1]
    back_three, grad_shift_three, grad_scale_three = mlp_pull(grad_mlp_in)
    grad_three = grad_out + back_three
    grad_cross_branch = to_low(grad_three).reshape(token_rows, model_width)
    grad_cout = left_product(attn_c, grad_cross_branch)
    grad_attn_c = to_low(right_product(grad_cross_branch, wide_cout)).reshape(
        patch_dev, frames, head_count, head_size
    )
    grad_probs_c = jnp.einsum(
        "pfhe,khe->pfhk", grad_attn_c, value_c, preferred_element_type=jnp.float32
    )
    grad_scores_c = to_low(softmax_back(probs_c, grad_probs_c))
    grad_query_c = to_low(
        jnp.einsum("pfhk,khe->pfhe", grad_scores_c, key_c, preferred_element_type=jnp.float32)
        * score_scale
    ).reshape(token_rows, model_width)
    grad_key_c = (
        jnp.einsum("pfhk,pfhe->khe", grad_scores_c, query_c, preferred_element_type=jnp.float32)
        * score_scale
    )
    grad_value_c = jnp.einsum(
        "pfhk,pfhe->khe", probs_c_low, grad_attn_c, preferred_element_type=jnp.float32
    )
    grad_memory = jnp.concatenate(
        [grad_key_c.reshape(text_keys, model_width), grad_value_c.reshape(text_keys, model_width)],
        axis=1,
    )
    grad_wquery = left_product(cross_input, grad_query_c)
    grad_cross_in = right_product(grad_query_c, wide_query).reshape(patch_dev, frames, model_width)
    cross_pull = jax.vjp(gain_norm, after_two, gain_row)[1]
    back_two, grad_gain = cross_pull(grad_cross_in)
    grad_two = grad_three + back_two
    grad_gate_two = jnp.sum(grad_two * branch_t, axis=0)
    grad_temporal_branch = to_low(grad_two * gate_two).reshape(token_rows, model_width)
    grad_tout = left_product(attn_t, grad_temporal_branch)
    grad_attn_t = to_low(right_product(grad_temporal_branch, wide_tout)).reshape(
        patch_dev, frames, head_count, head_size
    )
    grad_probs_t = jnp.einsum(
        "pfhe,pghe->phfg", grad_attn_t, value_t, preferred_element_type=jnp.float32
    )
    grad_scores_t = to_low(softmax_back(probs_t, grad_probs_t))
    grad_query_t = (
        jnp.einsum("phfg,pghe->pfhe", grad_scores_t, key_t, preferred_element_type=jnp.float32)
        * score_scale
    )
    grad_key_t = (
        jnp.einsum("phfg,pfhe->pghe", grad_scores_t, query_t, preferred_element_type=jnp.float32)
        * score_scale
    )
    grad_value_t = jnp.einsum(
        "phfg,pfhe->pghe", probs_t_low, grad_attn_t, preferred_element_type=jnp.float32
    )
    grad_qkv_t = to_low(jnp.stack([grad_query_t, grad_key_t, grad_value_t], axis=2)).reshape(
        token_rows, 3 * model_width
    )
    grad_tin = left_product(temporal_input, grad_qkv_t)
    grad_temporal_in = right_product(grad_qkv_t, wide_tin).reshape(patch_dev, frames, model_width)
    temporal_pull = jax.vjp(modulate, after_one, shift_two, scale_two)[1]
    back_one, grad_shift_two, grad_scale_two = temporal_pull(grad_temporal_in)
    grad_one = grad_two + back_one
    grad_gate_one = jnp.sum(grad_one * branch_s, axis=0)
    grad_spatial_branch = to_low(grad_one * gate_one).reshape(token_rows, model_width)
    grad_sout = left_product(attn_s, grad_spatial_branch)
    grad_attn_s = to_low(right_product(grad_spatial_branch, wide_sout)).reshape(
        patch_dev, frames, head_count, head_size
    )
    back_kv = lax.all_gather(local_kv, "blk", axis=0, tiled=True)
    back_key, back_value = split_kv(back_kv)
    back_probs = spatial_probs(back_key)[0]
    back_probs_low = to_low(back_probs)
    grad_probs_s = jnp.einsum(
        "pfhe,qfhe->fhpq", grad_attn_s, back_value, preferred_element_type=jnp.float32
    )
    row_delta = jnp.sum(grad_probs_s * back_probs, axis=-1, keepdims=True)
    grad_scores_s = to_low(back_probs * (grad_probs_s - row_delta))
    grad_query_s = (
        jnp.einsum("fhpq,qfhe->pfhe", grad_scores_s, back_key, preferred_element_type=jnp.float32)
        * score_scale
    )
    count = lax.axis_size("blk") * patch_dev
    grad_key = (
        jnp.einsum("fhpq,pfhe->qfhe", grad_scores_s, query_s, preferred_element_type=jnp.float32)
        * score_scale
    )
    grad_value = jnp.einsum(
        "fhpq,pfhe->qfhe", back_probs_low, grad_attn_s, preferred_element_type=jnp.float32
    )
    grad_kv = to_low(
        lax.psum_scatter(
            jnp.concatenate(
                [
                    grad_key.reshape(count, frames, model_width),
                    grad_value.reshape(count, frames, model_width),
                ],
                axis=2,
            ).astype(jnp.bfloat16),
            "blk",
            scatter_dimension=0,
            tiled=True,
        ).astype(jnp.float32)
    )
    grad_qkv_s = jnp.concatenate(
        [to_low(grad_query_s).reshape(patch_dev, frames, model_width), grad_kv], axis=2
    ).reshape(token_rows, 3 * model_width)
    grad_sin = left_product(spatial_input, grad_qkv_s)
    grad_spatial_in = right_product(grad_qkv_s, wide_sin).reshape(patch_dev, frames, model_width)
    spatial_pull = jax.vjp(modulate, inputs, shift_one, scale_one)[1]
    back_zero, grad_shift_one, grad_scale_one = spatial_pull(grad_spatial_in)
    grad_input = grad_one + back_zero
    grad_frame_mod = jnp.concatenate(
        [
            grad_shift_one,
            grad_scale_one,
            grad_gate_one,
            grad_shift_two,
            grad_scale_two,
            grad_gate_two,
            grad_shift_three,
            grad_scale_three,
            grad_gate_three,
        ],
        axis=1,
    )
    grad_mod_local = lax.dot_general(
        choose.astype(jnp.float32),
        grad_frame_mod,
        (((0,), (0,)), ((), ())),
        precision=lax.Precision.HIGHEST,
    )
    grad_mod_part, grad_memory_part = (
        lax.psum_scatter(
            grad_mod_local.astype(jnp.bfloat16), "blk", scatter_dimension=1, tiled=True
        ).astype(jnp.float32),
        lax.psum_scatter(
            grad_memory.astype(jnp.bfloat16), "blk", scatter_dimension=1, tiled=True
        ).astype(jnp.float32),
    )
    grad_mod_low = to_low(grad_mod_part)
    grad_ada_w = left_product(conditioning, grad_mod_low)
    grad_ada_b = jnp.sum(grad_mod_low.astype(jnp.float32), axis=0)
    grad_caption = left_product(caption_rows, to_low(grad_memory_part))
    grad_ada_w, grad_ada_b, grad_caption = (
        lax.psum(grad_ada_w.astype(jnp.bfloat16), "seq").astype(jnp.float32),
        lax.psum(grad_ada_b.astype(jnp.bfloat16), "seq").astype(jnp.float32),
        lax.psum(grad_caption.astype(jnp.bfloat16), "seq").astype(jnp.float32),
    )
    shares = (
        lax.psum_scatter(grad_sin, ("seq", "blk"), scatter_dimension=0, tiled=True),
        lax.psum_scatter(grad_sout, ("seq", "blk"), scatter_dimension=0, tiled=True),
        lax.psum_scatter(grad_tin, ("seq", "blk"), scatter_dimension=0, tiled=True),
        lax.psum_scatter(grad_tout, ("seq", "blk"), scatter_dimension=0, tiled=True),
        lax.psum_scatter(grad_gain, ("seq", "blk"), scatter_dimension=0, tiled=True),
        lax.psum_scatter(grad_wquery, ("seq", "blk"), scatter_dimension=0, tiled=True),
        lax.psum_scatter(grad_cout, ("seq", "blk"), scatter_dimension=0, tiled=True),
        lax.psum_scatter(grad_hin, ("seq", "blk"), scatter_dimension=0, tiled=True),
        lax.psum_scatter(grad_hout, ("seq", "blk"), scatter_dimension=0, tiled=True),
    )
    (
        share_sin,
        share_sout,
        share_tin,
        share_tout,
        share_gain,
        share_query,
        share_cout,
        share_hin,
        share_hout,
    ) = shares
    return (
        to_low(result)[None],
        to_low(grad_input)[None],
        grad_ada_w,
        grad_ada_b,
        share_sin,
        share_sout,
        share_tin,
        share_tout,
        share_gain,
        share_query,
        grad_caption,
        share_cout,
        share_hin,
        share_hout,
    )


MESH = pl.DeviceIdType.MESH
BLOCKS = 18
LINES = 8
SHARD = 36
LINE = 4 * SHARD
WINDOW = 48
WIDE = LINES * LINE
MIB = 2**20


def place():
    seq = lax.axis_index("seq")
    blk = lax.axis_index("blk")
    x, c = seq // 2, seq % 2
    z, y = blk // 2, blk % 2
    x1, y1 = x + (1 - 2 * x) * (1 - c), y + (1 - 2 * y) * c
    x2, y2 = x + (1 - 2 * x) * c, y + (1 - 2 * y) * (1 - c)
    return x, c, y, z, x1, y1, x2, y2


def device(x, c, y, z):
    return {"seq": x * 2 + c, "blk": z * 2 + y}


def line_of(c, x, y):
    return (c * 2 + x) * 2 + y


def remote(src, dst, send_sem, recv_sem, where):
    return pltpu.make_async_remote_copy(
        src_ref=src,
        dst_ref=dst,
        send_sem=send_sem,
        recv_sem=recv_sem,
        device_id=where,
        device_id_type=MESH,
    )


def greet(others):
    barrier = pltpu.get_barrier_semaphore()
    for other in others:
        pl.semaphore_signal(barrier, inc=1, device_id=other, device_id_type=MESH)
    pl.semaphore_wait(barrier, len(others))


def left_at(t):
    at = jnp.minimum(t, 4)
    for first in (8, 9, 10, 11, 14, 15):
        at = at + jnp.where(t >= first, 1, 0)
    return at


def right_at(t):
    return jnp.maximum(t - 3, 0)


ROWS = 256
KEYS = 256
TEXT = 288
MOD = 9 * WIDE
MOD_TILES = 11
MOD_WIN = 128 * MOD_TILES
PARTS, HELD, LAST = 6, 4, 8
LEFT_SEM, SLOPE_SEM, SAVE_SEMS = 40, 42, 44
TILE = 384
SCALE = E ** (-0.5)


def nt(left, right):
    return lax.dot_general(
        left, right, (((1,), (1,)), ((), ())), preferred_element_type=jnp.float32
    )


def wide32(values):
    return values.astype(jnp.float32)


def loop(count, body):
    def step(index, carry):
        body(index)
        return carry

    lax.fori_loop(0, count, step, 0)


def each_rows(size, body, total=ROWS):
    loop(total // size, lambda i: body(pl.ds(pl.multiple_of(i * size, size), size)))


def each_cols(body):
    loop(WIDE // TILE, lambda i: body(pl.ds(pl.multiple_of(i * TILE, TILE), TILE)))


def swap_rows():
    row = lax.broadcasted_iota(jnp.int32, (ROWS, ROWS), 0)
    col = lax.broadcasted_iota(jnp.int32, (ROWS, ROWS), 1)
    return to_low((((row & 15) << 4) + (row >> 4) == col).astype(jnp.float32))


def head_window(h):
    base = h * E
    start = jnp.minimum(base // 128, 7) * 128
    lane = lax.broadcasted_iota(jnp.int32, (1, 256), 1)
    on = (lane >= base - start) & (lane < base - start + E)
    return pl.ds(pl.multiple_of(start, 128), 256), on.astype(jnp.float32)


def soft(scores, bias, mask):
    scores = scores * SCALE
    if bias is not None:
        scores = scores + bias
    powers = jnp.exp(scores - jnp.max(scores, axis=-1, keepdims=True))
    probs = powers * (1.0 / jnp.sum(powers, axis=-1, keepdims=True))
    return probs if mask is None else probs * mask


def chains(h, groups):
    return [(window, rows, keys) for window in (head_window(h), head_window(h + H // 2)) for rows, keys in groups]


def split_rows(values, jobs):
    start = 0
    parts = []
    for _, rows, _ in jobs:
        size = rows.stop - rows.start
        parts.append(values[start : start + size])
        start += size
    return parts


def heads_forward(h, query, key, value, attn, groups, bias, mask):
    jobs = chains(h, groups)
    scores = [nt(query[rows, lanes] * to_low(on), key[keys, lanes]) for (lanes, on), rows, keys in jobs]
    probs = split_rows(to_low(soft(jnp.concatenate(scores), bias, mask)), jobs)
    parts = [linear(prob, value[keys, lanes]) * on for prob, ((lanes, on), rows, keys) in zip(probs, jobs)]
    for part, ((lanes, on), rows, keys) in zip(parts, jobs):
        attn[rows, lanes] = attn[rows, lanes] + to_low(part)


def text_heads_forward(h, query, key, value, attn, bias, mask):
    jobs = chains(h, VIDEOS)
    scores = [linear(query[rows, lanes] * to_low(on), key[lanes, keys]) for (lanes, on), rows, keys in jobs]
    probs = split_rows(to_low(soft(jnp.concatenate(scores), bias, mask)), jobs)
    parts = [nt(prob, value[lanes, keys]) * on for prob, ((lanes, on), rows, keys) in zip(probs, jobs)]
    for part, ((lanes, on), rows, keys) in zip(parts, jobs):
        attn[rows, lanes] = attn[rows, lanes] + to_low(part)


HALVES = [(slice(0, 128), slice(0, 128)), (slice(128, 256), slice(128, 256))]
VIDEOS = [(slice(0, 144), slice(0, 128)), (slice(112, 256), slice(128, 256))]


def regroup(back):
    row = lax.broadcasted_iota(jnp.int32, (ROWS, ROWS), 0)
    col = lax.broadcasted_iota(jnp.int32, (ROWS, ROWS), 1)
    if back:
        source = (((row >> 3) & 1) << 7) + ((row >> 4) << 3) + (row & 7)
    else:
        source = (((row >> 3) & 15) << 4) + ((row >> 7) << 3) + (row & 7)
    return to_low((source == col).astype(jnp.float32))


def temporal_bias(seg_in, seg_row):
    row = lax.broadcasted_iota(jnp.int32, (128, 128), 0)
    col = lax.broadcasted_iota(jnp.int32, (128, 128), 1)
    allowed = ((row & 7) == (col & 7)) & (seg_in[2, 0:128, 0:1] == seg_row[0:1, 0:128])
    return jnp.where(allowed, 0.0, MASKED)


def cross_bias():
    col = lax.broadcasted_iota(jnp.int32, (1, 128), 1)
    return jnp.where(col < L, 0.0, MASKED)


def cross_rows(seg_in):
    both = [1.0 - seg_in[0, 0:144, 0:1], seg_in[0, 112:256, 0:1]]
    return jnp.concatenate(both + both)


def blk_peers(x, c, b):
    return [device(x, c, (b + k) % 2, ((b + k) % 8) // 2) for k in range(1, 8)]


def forward_kernel(
    spatial_in, spatial_out, temporal_in, temporal_out, cross_query, cross_out, hidden_in, hidden_out,
    tok, gain_one, cond, ada_bias, seg_in, seg_row, pick_in, cot_i, turn_i, ada_i, caption_i, proj_i,
    wide, out, left_o, qkvs_o, qkvt_o, qc_o, mem_o, xhat_o, rstd_o, branch_o, slope_o, gfour_o, cot_o, mods_o, gate_o, gain_o,
    parts, lines, weights, tokp, cotp, tokf, xin, xp, left, qkvs, qkvt, qc, mem, text, mod, mods, xhat, rstd, branch, branchw, bias,
    stream, attnf, attnp, post, slope, gfour, gains, gain_at, gate,
    src, cot, turn, ada, caption, proj, mod_in, text_in, hidden,
    z_send, z_recv, l_send, l_recv, own_sem, w_sem, t_send, t_recv, a_send, a_recv, m_send, m_recv, x_send, x_recv,
    g_send, g_recv, save_sem, in_sem,
):
    x, c, y, z, x1, y1, x2, y2 = place()
    b = z * 2 + y
    near = [device(x, c, y, (z + k) % 4) for k in (1, 2, 3)]
    first, second, twin = device(x1, c, y1, z), device(x2, c, y2, z), device(x, 1 - c, y, z)
    peers = blk_peers(x, c, b)
    greet(peers + [device(1 - x, c, y, z), twin])
    mine, line1 = line_of(c, x, y), line_of(c, x1, y1)
    line2, line3 = line_of(c, x2, y2), line_of(c, 1 - x, 1 - y)
    other = [line_of(1 - c, x, y), line_of(1 - c, x2, y2), line_of(1 - c, x1, y1), line_of(1 - c, 1 - x, 1 - y)]

    def z_copy(t, k):
        return remote(src.at[t], parts.at[t % PARTS, z], z_send.at[t, k - 1], z_recv.at[t, k - 1], near[k - 1])

    def z_wait(t, k):
        from_z = (z + 4 - k) % 4
        return remote(src.at[t], parts.at[t % PARTS, from_z], z_send.at[t, k - 1], z_recv.at[t, k - 1], near[k - 1])

    def wide_line(t, line):
        return wide.at[t, pl.ds(pl.multiple_of(line * LINE, 16), LINE)]

    def own(t):
        return pltpu.make_async_copy(lines.at[t % HELD], wide_line(t, mine), own_sem.at[t])

    def line_copy(t, to, line, index, where):
        return remote(to, wide_line(t, line), l_send.at[t, index], l_recv.at[t, index], where)

    def sends(t, index):
        line, where = (
            (mine, first), (mine, second), (mine, twin), (line1, second),
            (line1, twin), (line2, twin), (line3, twin),
        )[index]
        from_here = lines.at[t % HELD] if index < 3 else wide_line(t, line)
        return line_copy(t, from_here, line, index, where)

    def arrives(t, line, index):
        line_copy(t, wide_line(t, line), line, index, first).wait_recv()

    def tick(t):
        @pl.when((t >= 3) & (t < BLOCKS + 3))
        def _():
            now = t - 3
            for k in (1, 2, 3):
                z_wait(now, k).wait_recv()

            @pl.when(now >= HELD)
            def _():
                for index in range(3):
                    sends(now - HELD, index).wait_send()
                own(now - HELD).wait()

            at = now % HELD
            w0, w1, w2, w3 = [parts[now % PARTS, k] for k in range(4)]
            lines[at, 0:32] = w0[0:32]
            lines[at, 32:48] = w0[32:48] + w1[0:16]
            lines[at, 48:64] = w1[16:32]
            lines[at, 64:80] = w1[32:48] + w2[0:16]
            lines[at, 80:96] = w2[16:32]
            lines[at, 96:112] = w2[32:48] + w3[0:16]
            lines[at, 112:144] = w3[16:48]
            for index in range(3):
                sends(now, index).start()
            own(now).start()

        @pl.when(t < BLOCKS)
        def _():
            for k in (1, 2, 3):
                z_copy(t, k).start()
            parts[t % PARTS, z] = src[t]

        @pl.when((t >= 5) & (t < BLOCKS + 5))
        def _():
            now = t - 5
            arrives(now, line1, 0)
            for index in (3, 4):
                sends(now, index).start()

        @pl.when(t >= LAST)
        def _():
            now = t - LAST
            arrives(now, line2, 1)
            sends(now, 5).start()
            arrives(now, line3, 3)
            sends(now, 6).start()

    done = [0]

    def pump(until):
        until = min(until, BLOCKS + LAST)
        if until > done[0]:
            start = done[0]
            loop(until - start, lambda i: tick(i + start))
            done[0] = until

    def poke():
        pump(done[0] + 1)

    def load(block):
        pump(block + LAST + 1)
        for line, index in zip(other, (2, 4, 5, 6)):
            arrives(block, line, index)
        if block >= BLOCKS - HELD:
            own(block).wait()
        copy = pltpu.make_async_copy(wide.at[block], weights.at[block % 2], w_sem.at[block % 2])
        copy.start()
        copy.wait()

    def times(values, block, emit):
        def tile(cols):
            emit(cols, linear(values[...], weights[block % 2, :, cols]))

        each_cols(tile)

    saves = []
    held = {}

    def save(from_ref, to_ref, name=None):
        if name is None:
            name = len(saves)
            saves.append(name)
        held[name] = pltpu.make_async_copy(from_ref, to_ref, save_sem.at[name])
        held[name].start()

    def settle(name):
        if name in held:
            held.pop(name).wait()

    def turned(values, index):
        slot = index % 2
        settle(LEFT_SEM + slot)

        def tile(cols):
            xp[:, cols] = to_low(nt(values[...], turn[cols, :]))
            left[slot, cols, :] = to_low(nt(turn[cols, :], values[...]))

        each_cols(tile)
        save(left.at[slot], left_o.at[index], LEFT_SEM + slot)

    fetches = [
        pltpu.make_async_copy(from_ref, to_ref, in_sem.at[at])
        for at, (from_ref, to_ref) in enumerate(
            ((ada_i, ada), (turn_i, turn), (cot_i, cot), (caption_i, caption), (proj_i, proj))
        )
    ]
    for copy in fetches:
        copy.start()

    def shift(rows, first):
        row = lax.broadcasted_iota(jnp.int32, (WINDOW, rows), 0) - 4 * z
        col = lax.broadcasted_iota(jnp.int32, (WINDOW, rows), 1)
        return to_low(((row >= 0) & (row < SHARD) & (row + first == col)).astype(jnp.float32))

    def window(at, values):
        src[at] = to_low(linear(shift(SHARD, 0), values))

    for j in range(3):
        window(j, spatial_in[:, WIDE * j : WIDE * j + WIDE])
    pump(3)
    window(3, spatial_out[...])
    for j in range(3):
        window(4 + j, temporal_in[:, WIDE * j : WIDE * j + WIDE])
    window(7, temporal_out[...])
    window(8, cross_query[...])
    window(9, cross_out[...])

    def m_copy(k, at):
        return remote(mod_in, mod.at[at], m_send.at[k - 1], m_recv.at[k - 1], peers[k - 1])

    fetches[0].wait()
    part = wide32(to_low(linear(cond[...], ada[...]) + wide32(ada_bias[...])))[0:8]
    part = jnp.concatenate([part, jnp.zeros((8, MOD_WIN - MOD // 8), jnp.float32)], axis=1)
    part = pltpu.roll(part, 16 * b, 1)
    tiles = [part[row : row + 1, 128 * tile : 128 * tile + 128] for row in range(2) for tile in range(MOD_TILES)]
    mod_in[...] = to_low(jnp.concatenate(tiles + [jnp.zeros((32 - 2 * MOD_TILES, 128), jnp.float32)]))
    for k in range(1, 8):
        m_copy(k, b).start()
    mod[b] = mod_in[...]
    swap = swap_rows()
    tokp[...] = to_low(linear(swap, tok[...]))

    def t_copy(k):
        to = (b + k) % 8
        part = tokp.at[pl.ds(pl.multiple_of(32 * to, 32), 32)]
        return remote(part, tokf.at[b], t_send.at[k - 1], t_recv.at[k - 1], peers[k - 1])

    def t_wait(k):
        of = (b + 8 - k) % 8
        remote(tokp.at[pl.ds(0, 32)], tokf.at[of], t_send.at[k - 1], t_recv.at[k - 1], peers[k - 1]).wait_recv()

    for k in range(1, 8):
        t_copy(k).start()
    tokf[b] = tokp[pl.ds(pl.multiple_of(32 * b, 32), 32)]

    def g_copy(at, from_at, to):
        return remote(gains.at[from_at], gain_at.at[at], g_send.at[at], g_recv.at[at], to)

    spread = jnp.concatenate([wide32(gain_one[...]), jnp.zeros((8, WIDE - SHARD), jnp.float32)], axis=1)
    gains[0] = pltpu.roll(spread, SHARD * ((x * 2 + c) * 8 + b), 1)
    g_copy(0, 0, twin).start()
    pump(5)
    fetches[2].wait()
    cotp[...] = to_low(linear(swap, cot[...]))
    save(cotp, cot_o)

    def x_copy(k, at):
        return remote(text_in, text.at[at, y], x_send.at[k - 1], x_recv.at[k - 1], near[k - 1])

    def x_over(at):
        return remote(text.at[:, at], text.at[:, at], x_send.at[3], x_recv.at[3], device(x, c, 1 - y, z))

    for k in range(1, 8):
        m_copy(k, (b + 8 - k) % 8).wait_recv()
    mods[...] = jnp.zeros_like(mods)
    for k in range(8):
        part = wide32(mod[k])
        for row in range(2):
            for tile in range(MOD_TILES):
                lanes = slice(1280 * k + 128 * tile, 1280 * k + 128 * tile + 128)
                at = row * MOD_TILES + tile
                mods[row : row + 1, lanes] = mods[row : row + 1, lanes] + part[at : at + 1]
    save(mods, mods_o)
    g_copy(0, 0, twin).wait_recv()
    gains[1] = gains[0] + gain_at[0]
    g_copy(1, 1, first).start()
    pump(6)
    fetches[3].wait()
    fetches[4].wait()
    text_in[...] = jnp.zeros_like(text_in)
    row = lax.broadcasted_iota(jnp.int32, (TEXT, TEXT), 0)
    col = lax.broadcasted_iota(jnp.int32, (TEXT, TEXT), 1)
    same = to_low((row == col).astype(jnp.float32))
    for v in range(2):
        part = to_low(linear(caption[v], proj[...]))
        text_in[:, 128 * v : 128 * v + L] = to_low(nt(same, part))
    for k in (1, 2, 3):
        x_copy(k, z).start()
    text[z, y] = text_in[...]
    hidden[...] = jnp.zeros_like(hidden)
    rows = lax.broadcasted_iota(jnp.int32, (WIDE, TILE), 0)
    for j in range(4):
        at = 2 * (j % 2) + j // 2
        lanes = slice(256 * at, 256 * at + TILE)
        for k in range(4):
            chosen = to_low((rows == pick_in[4 * k + at : 4 * k + at + 1, :]).astype(jnp.float32))
            part = to_low(linear(hidden_in[:, WIDE * j : WIDE * j + WIDE], chosen))
            hidden[k, 0:SHARD, lanes] = hidden[k, 0:SHARD, lanes] + part
    for k in range(4):
        window(10 + 2 * k, hidden[k, 0:SHARD])
        src[11 + 2 * k] = to_low(linear(shift(4 * SHARD, SHARD * k), hidden_out[...]))
    fetches[1].wait()

    def pick(piece, seg):
        lanes = slice(WIDE * piece, WIDE * piece + WIDE)
        return jnp.where(seg > 0.5, mods[1:2, lanes], mods[0:1, lanes])

    def normal(values, rows, index):
        center = values - jnp.mean(values, axis=-1, keepdims=True)
        factor = lax.rsqrt(jnp.mean(center * center, axis=-1, keepdims=True) + EPSILON)
        scaled = center * factor
        xhat[index, rows, :] = to_low(scaled)
        rstd[index, rows, :] = jnp.broadcast_to(factor, (factor.shape[0], 128))
        return scaled

    for k in range(1, 8):
        t_wait(k)
    g_copy(1, 1, first).wait_recv()
    gains[2] = gains[1] + gain_at[1]
    g_copy(2, 2, second).start()

    def spatial_rows(i):
        seg = jnp.concatenate([seg_in[1, 0:16, 0:1], seg_in[1, 128:144, 0:1]])
        values = wide32(tokf[i])
        center = values - jnp.mean(values, axis=-1, keepdims=True)
        factor = lax.rsqrt(jnp.mean(center * center, axis=-1, keepdims=True) + EPSILON)
        scaled = center * factor
        ready = to_low(scaled * (1.0 + pick(1, seg)) + pick(0, seg))
        low = to_low(scaled)
        spread = jnp.broadcast_to(factor, (32, 128))
        for f in range(2):
            rows = pl.ds(pl.multiple_of(128 * f + 16 * i, 16), 16)
            part = slice(16 * f, 16 * f + 16)
            xhat[0, rows, :] = low[part]
            rstd[0, rows, :] = spread[part]
            xin[rows, :] = ready[part]

    loop(8, spatial_rows)
    save(xhat.at[0], xhat_o.at[0])
    save(rstd.at[0], rstd_o.at[0])
    turned(xin, 10)
    for j in range(3):
        load(j)

        def emit(cols, value, j=j):
            qkvs[j, :, cols] = to_low(value)

        times(xp, j, emit)
    save(qkvs, qkvs_o)
    g_copy(2, 2, second).wait_recv()
    gains[3] = gains[2] + gain_at[2]
    for k in (1, 2, 3):
        remote(gains.at[3], gain_at.at[2 + k], g_send.at[2 + k], g_recv.at[2 + k], near[k - 1]).start()
    for k in (1, 2, 3):
        x_copy(k, (z + 4 - k) % 4).wait_recv()
    x_over(y).start()
    attnf[...] = jnp.zeros_like(attnf)

    def spatial_heads(h):
        heads_forward(h, qkvs.at[0], qkvs.at[1], qkvs.at[2], attnf, HALVES, None, None)

    loop(4, spatial_heads)
    poke()
    loop(4, lambda h: spatial_heads(h + 4))
    for k in (1, 2, 3):
        remote(gains.at[3], gain_at.at[2 + k], g_send.at[2 + k], g_recv.at[2 + k], near[k - 1]).wait_recv()
    gains[0 + 4] = gains[3] + gain_at[3] + gain_at[4] + gain_at[5]
    save(gains.at[4], gain_o)

    def a_copy(k, f):
        to = (b + k) % 8
        part = attnf.at[pl.ds(pl.multiple_of(128 * f + 16 * to, 16), 16)]
        return remote(part, attnp.at[2 * b + f], a_send.at[k - 1, f], a_recv.at[k - 1, f], peers[k - 1])

    def a_wait(k, f):
        of = (b + 8 - k) % 8
        part = attnf.at[pl.ds(0, 16)]
        remote(part, attnp.at[2 * of + f], a_send.at[k - 1, f], a_recv.at[k - 1, f], peers[k - 1]).wait_recv()

    for k in range(1, 8):
        for f in range(2):
            a_copy(k, f).start()
    for f in range(2):
        attnp[2 * b + f] = attnf[pl.ds(pl.multiple_of(128 * f + 16 * b, 16), 16)]
    poke()
    for k in range(1, 8):
        for f in range(2):
            a_wait(k, f)
    xin[...] = attnp[...].reshape(ROWS, WIDE)
    turned(xin, 9)
    load(3)

    def emit_branch(cols, value):
        branchw[:, cols] = value

    times(xp, 3, emit_branch)

    def after_spatial(rows):
        seg = seg_in[0, rows, 0:1]
        value = branchw[rows, :]
        branch[0, rows, :] = to_low(value)
        value = wide32(tokp[rows, :]) + pick(2, seg) * value
        stream[rows, :] = value
        xin[rows, :] = to_low(normal(value, rows, 1) * (1.0 + pick(4, seg)) + pick(3, seg))

    each_rows(32, after_spatial)
    save(branch.at[0], branch_o.at[0])
    save(xhat.at[1], xhat_o.at[1])
    save(rstd.at[1], rstd_o.at[1])

    for k in range(1, 8):
        for f in range(2):
            a_copy(k, f).wait_send()
    attnf[...] = to_low(linear(regroup(False), xin[...]))
    turned(attnf, 8)
    for j in range(3):
        load(4 + j)

        def emit(cols, value, j=j):
            qkvt[j, :, cols] = to_low(value)

        times(xp, 4 + j, emit)
    save(qkvt, qkvt_o)
    attnf[...] = jnp.zeros_like(attnf)

    bias[...] = temporal_bias(seg_in, seg_row)

    def temporal_heads(h):
        heads_forward(
            h, qkvt.at[0], qkvt.at[1], qkvt.at[2], attnf, HALVES, jnp.concatenate([bias[...]] * 4), None
        )

    loop(4, temporal_heads)
    poke()
    loop(4, lambda h: temporal_heads(h + 4))
    xin[...] = to_low(linear(regroup(True), attnf[...]))
    turned(xin, 7)
    load(7)
    times(xp, 7, emit_branch)

    def after_temporal(rows):
        seg = seg_in[0, rows, 0:1]
        value = branchw[rows, :]
        branch[1, rows, :] = to_low(value)
        value = stream[rows, :] + pick(5, seg) * value
        stream[rows, :] = value
        xin[rows, :] = to_low(normal(value, rows, 2) * gains[4, 0:1, :])

    each_rows(32, after_temporal)
    save(branch.at[1], branch_o.at[1])
    save(xhat.at[2], xhat_o.at[2])
    save(rstd.at[2], rstd_o.at[2])

    turned(xin, 6)
    load(8)

    def emit_query(cols, value):
        qc[:, cols] = to_low(value)

    times(xp, 8, emit_query)
    save(qc, qc_o)
    x_over(1 - y).wait_recv()
    for k in range(8):
        mem[k // 4, TEXT * (k % 4) : TEXT * (k % 4) + TEXT, :] = text[k // 2, k % 2]
    save(mem, mem_o)
    attnf[...] = jnp.zeros_like(attnf)

    def cross_heads(h):
        text_heads_forward(h, qc, mem.at[0], mem.at[1], attnf, cross_bias(), cross_rows(seg_in))

    loop(4, cross_heads)
    poke()
    loop(4, lambda h: cross_heads(h + 4))
    xin[...] = attnf[...]
    turned(xin, 5)
    load(9)
    times(xp, 9, emit_branch)

    def after_cross(rows):
        seg = seg_in[0, rows, 0:1]
        value = stream[rows, :] + branchw[rows, :]
        stream[rows, :] = value
        xin[rows, :] = to_low(normal(value, rows, 3) * (1.0 + pick(7, seg)) + pick(6, seg))
        gfour[rows, :] = to_low(wide32(cotp[rows, :]) * pick(8, seg))

    each_rows(32, after_cross)
    save(xhat.at[3], xhat_o.at[3])
    save(rstd.at[3], rstd_o.at[3])
    save(gfour, gfour_o)

    turned(xin, 4)
    same = (
        lax.broadcasted_iota(jnp.int32, (TILE, TILE), 0) == lax.broadcasted_iota(jnp.int32, (TILE, TILE), 1)
    ).astype(jnp.float32).astype(jnp.bfloat16)
    for k in range(4):
        slot = k % 2
        load(10 + 2 * k)
        settle(SLOPE_SEM + slot)
        settle(LEFT_SEM + slot)

        def emit_hidden(cols, value, slot=slot):
            inner = math.sqrt(2.0 / math.pi) * (value + 0.044715 * value * value * value)
            bent = jnp.tanh(inner)
            half = 0.5 * (1.0 + bent)
            tilt = math.sqrt(2.0 / math.pi) * (1.0 + 3 * 0.044715 * value * value)
            slope[slot, :, cols] = to_low(half + 0.5 * value * (1.0 - bent * bent) * tilt)
            low = to_low(value * half)
            post[:, cols] = low
            left[slot, cols, :] = to_low(nt(same, low))

        times(xp, 10 + 2 * k, emit_hidden)
        save(slope.at[slot], slope_o.at[k], SLOPE_SEM + slot)
        save(left.at[slot], left_o.at[k], LEFT_SEM + slot)
        load(11 + 2 * k)

        def emit_out(cols, value, k=k):
            branchw[:, cols] = value if k == 0 else branchw[:, cols] + value

        times(post, 11 + 2 * k, emit_out)

    gate[...] = jnp.zeros_like(gate)

    def last(rows):
        seg = seg_in[0, rows, 0:1]
        value = branchw[rows, :]
        xin[rows, :] = to_low(stream[rows, :] + pick(8, seg) * value)
        value = wide32(cotp[rows, :]) * value
        later = jnp.sum(value * seg, axis=0, keepdims=True)
        every = jnp.sum(value, axis=0, keepdims=True)
        gate[0:1, :] = gate[0:1, :] + (every - later)
        gate[1:2, :] = gate[1:2, :] + later

    each_rows(32, last)
    save(gate, gate_o)
    out[...] = to_low(linear(swap_rows(), xin[...]))

    for copy in held.values():
        copy.wait()
    for k in range(1, 8):
        t_copy(k).wait_send()
        m_copy(k, b).wait_send()
    for k in (1, 2, 3):
        x_copy(k, z).wait_send()
    x_over(y).wait_send()
    for at, to in ((0, twin), (1, first), (2, second)):
        g_copy(at, at, to).wait_send()
    for k in (1, 2, 3):
        remote(gains.at[3], gain_at.at[2 + k], g_send.at[2 + k], g_recv.at[2 + k], near[k - 1]).wait_send()

    for t in range(BLOCKS - HELD, BLOCKS):
        for index in range(3):
            sends(t, index).wait_send()

    def finish(t):
        for k in (1, 2, 3):
            z_copy(t, k).wait_send()
        for index in range(3, 7):
            sends(t, index).wait_send()

    loop(BLOCKS, finish)


ANY = pl.BlockSpec(memory_space=pl.ANY)
IN_VMEM = pl.BlockSpec(memory_space=pltpu.VMEM)


def forward(*operands):
    low, full = jnp.bfloat16, jnp.float32
    dma = pltpu.SemaphoreType.DMA
    hbm = [
        ((BLOCKS, WIDE, WIDE), low),
        ((ROWS, WIDE), low),
        ((11, WIDE, ROWS), low),
        ((3, ROWS, WIDE), low),
        ((3, ROWS, WIDE), low),
        ((ROWS, WIDE), low),
        ((2, WIDE, KEYS), low),
        ((4, ROWS, WIDE), low),
        ((4, ROWS, 128), full),
        ((2, ROWS, WIDE), low),
        ((4, ROWS, WIDE), low),
        ((ROWS, WIDE), low),
        ((ROWS, WIDE), low),
        ((8, MOD), full),
        ((8, WIDE), full),
        ((8, WIDE), full),
    ]
    vmem = [
        ((PARTS, 4, WINDOW, WIDE), low),
        ((HELD, LINE, WIDE), low),
        ((2, WIDE, WIDE), low),
        ((ROWS, WIDE), low),
        ((ROWS, WIDE), low),
        ((8, 32, WIDE), low),
        ((ROWS, WIDE), low),
        ((ROWS, WIDE), low),
        ((2, WIDE, ROWS), low),
        ((3, ROWS, WIDE), low),
        ((3, ROWS, WIDE), low),
        ((ROWS, WIDE), low),
        ((2, WIDE, KEYS), low),
        ((4, 2, TEXT, KEYS), low),
        ((8, 32, 128), low),
        ((8, MOD), full),
        ((4, ROWS, WIDE), low),
        ((4, ROWS, 128), full),
        ((2, ROWS, WIDE), low),
        ((ROWS, WIDE), full),
        ((128, 128), full),
        ((ROWS, WIDE), full),
        ((ROWS, WIDE), low),
        ((16, 16, WIDE), low),
        ((ROWS, WIDE), low),
        ((2, ROWS, WIDE), low),
        ((ROWS, WIDE), low),
        ((5, 8, WIDE), full),
        ((6, 8, WIDE), full),
        ((8, WIDE), full),
        ((BLOCKS, WINDOW, WIDE), low),
        ((ROWS, WIDE), low),
        ((WIDE, WIDE), low),
        ((WIDE, MOD // 8), low),
        ((2, L, 4096), low),
        ((4096, TEXT), low),
        ((32, 128), low),
        ((TEXT, KEYS), low),
        ((4, WINDOW, WIDE), low),
    ]
    return pl.pallas_call(
        forward_kernel,
        out_shape=[jax.ShapeDtypeStruct(*shape) for shape in hbm],
        in_specs=[IN_VMEM] * 15 + [ANY] * 5,
        out_specs=[ANY, IN_VMEM] + [ANY] * 14,
        scratch_shapes=[pltpu.VMEM(*shape) for shape in vmem]
        + [
            dma((BLOCKS, 3)), dma((BLOCKS, 3)), dma((BLOCKS, 7)), dma((BLOCKS, 7)), dma((BLOCKS,)), dma((2,)),
            dma((7,)), dma((7,)), dma((7, 2)), dma((7, 2)), dma((7,)), dma((7,)), dma((4,)), dma((4,)),
            dma((6,)), dma((6,)), dma((SAVE_SEMS,)), dma((5,)),
        ],
        compiler_params=pltpu.CompilerParams(
            collective_id=0, has_side_effects=True, vmem_limit_bytes=60 * MIB
        ),
        name="forward",
    )(*operands)


def tn(left, right):
    return lax.dot_general(
        left, right, (((0,), (0,)), ((), ())), preferred_element_type=jnp.float32
    )


def text_heads_backward(h, query, key, value, grad, dquery, dkey, dvalue, bias, mask):
    jobs = chains(h, VIDEOS)
    scores, grads = [], []
    for (lanes, on), rows, keys in jobs:
        low_on = to_low(on)
        scores.append(linear(query[rows, lanes] * low_on, key[lanes, keys]))
        grads.append(linear(grad[rows, lanes] * low_on, value[lanes, keys]))
    probs = soft(jnp.concatenate(scores), bias, mask)
    grad_probs = jnp.concatenate(grads)
    delta = jnp.sum(grad_probs * probs, axis=-1, keepdims=True)
    slopes = split_rows(to_low(probs * (grad_probs - delta)), jobs)
    probs = split_rows(to_low(probs), jobs)
    parts = []
    for slope, prob, ((lanes, on), rows, keys) in zip(slopes, probs, jobs):
        low_on = to_low(on)
        parts.append(
            (
                to_low(nt(slope, key[lanes, keys]) * (on * SCALE)),
                to_low(tn(query[rows, lanes] * low_on, slope) * SCALE),
                to_low(tn(grad[rows, lanes] * low_on, prob)),
            )
        )
    for (by_query, by_key, by_value), ((lanes, on), rows, keys) in zip(parts, jobs):
        dquery[rows, lanes] = dquery[rows, lanes] + by_query
        dkey[lanes, keys] = dkey[lanes, keys] + by_key
        dvalue[lanes, keys] = dvalue[lanes, keys] + by_value


def heads_backward(h, query, key, value, grad, dquery, dkey, dvalue, groups, bias, mask):
    jobs = chains(h, groups)
    scores, grads = [], []
    for (lanes, on), rows, keys in jobs:
        low_on = to_low(on)
        scores.append(nt(query[rows, lanes] * low_on, key[keys, lanes]))
        grads.append(nt(grad[rows, lanes] * low_on, value[keys, lanes]))
    probs = soft(jnp.concatenate(scores), bias, mask)
    grad_probs = jnp.concatenate(grads)
    delta = jnp.sum(grad_probs * probs, axis=-1, keepdims=True)
    slopes = split_rows(to_low(probs * (grad_probs - delta)), jobs)
    probs = split_rows(to_low(probs), jobs)
    parts = []
    for slope, prob, ((lanes, on), rows, keys) in zip(slopes, probs, jobs):
        parts.append(
            (
                to_low(linear(slope, key[keys, lanes]) * (on * SCALE)),
                to_low(tn(slope, query[rows, lanes]) * (on * SCALE)),
                to_low(tn(prob, grad[rows, lanes]) * on),
            )
        )
    for (by_query, by_key, by_value), ((lanes, on), rows, keys) in zip(parts, jobs):
        dquery[rows, lanes] = dquery[rows, lanes] + by_query
        dkey[keys, lanes] = dkey[keys, lanes] + by_key
        dvalue[keys, lanes] = dvalue[keys, lanes] + by_value


def backward_kernel(
    wide, left_i, qkvs_i, qkvt_i, qc_i, mem_i, xhat_i, rstd_i, branch_i, slope_i, gfour_i, cot_i, mods_i, gate_i, gain_i,
    seg_in, seg_row, turn, cond_in,
    total, gtok, gain_o, text_o, mod_o,
    weights, left, right, qkv, xhat, rstd, branch, slope, mods, gain, bias, stream, work, grad, xin, gm, mem, dmem, text, texts, text_at, mod_out, mod,
    seqs, gains, gain_at, gframe, back, backp,
    s0, r0, s1, r1, s2, r2, k2, s3, r3, share,
    in_sem, w_sem, s0_sem, r0_sem, s1_sem, r1_sem, s2_sem, r2_sem, s3_sem, r3_sem, share_sem,
    a_send, a_recv, u_send, u_recv, x_send, x_recv, m_send, m_recv, q_send, q_recv, g_send, g_recv,
):
    x, c, y, z, x1, y1, x2, y2 = place()
    b = z * 2 + y
    near = [device(x, c, y, (z + k) % 4) for k in (1, 2, 3)]
    first, second, twin = device(x1, c, y1, z), device(x2, c, y2, z), device(x, 1 - c, y, z)
    peers = blk_peers(x, c, b)
    across = [twin, device(1 - x, c, y, z), device(1 - x, 1 - c, y, z)]
    greet(peers + across)

    fetches = {}

    def fetch(name, from_ref, to_ref):
        fetches[name] = pltpu.make_async_copy(from_ref, to_ref, in_sem.at[name])
        fetches[name].start()

    def have(name):
        if name in fetches:
            fetches.pop(name).wait()

    fetch(0, gfour_i, right.at[0])
    for k in range(11):
        fetch(1 + k, left_i.at[k], left.at[k])
    fetch(12, mods_i, mods)
    fetch(13, gain_i, gain)
    fetch(14, slope_i.at[0], slope.at[0])
    fetch(15, slope_i.at[1], slope.at[1])
    fetch(16, xhat_i.at[3], xhat.at[1])
    fetch(17, rstd_i.at[3], rstd.at[1])
    fetch(18, cot_i, xin)
    fetch(19, gate_i, work.at[0:8])

    def weight(block):
        slot = WEIGHT_ORDER.index(block) % 2
        return weights.at[slot]

    def prefetch(at):
        if at < len(WEIGHT_ORDER):
            copy = pltpu.make_async_copy(wide.at[WEIGHT_ORDER[at]], weights.at[at % 2], w_sem.at[at % 2])
            copy.start()
            fetches["w", WEIGHT_ORDER[at]] = copy

    def release(block):
        prefetch(WEIGHT_ORDER.index(block) + 2)

    prefetch(0)
    prefetch(1)

    away = [(1 - x) * 2 + 1 - y, x2 * 2 + y2]
    stay = [x1 * 2 + y1, x * 2 + y]

    def product(t, core, xl):
        rows = pl.ds(pl.multiple_of(line_of(core, xl, 0) * LINE, 16), 2 * LINE)
        return linear(left[left_at(t), rows, :], right[right_at(t)])

    def copy0(t, l):
        pair = pl.ds(2 * l, 2)
        return remote(s0.at[t % 2, pair], r0.at[t % 4, pair], s0_sem.at[t % 2, l], r0_sem.at[t % 4, l], twin)

    def copy1(t, l):
        return remote(s1.at[t % 2, away[l]], r1.at[t % 4, l], s1_sem.at[t % 2, l], r1_sem.at[t % 4, l], second)

    def copy2(t):
        return remote(s2.at[t % 2], r2.at[t % 4], s2_sem.at[t % 2], r2_sem.at[t % 4], first)

    def copy3(t, k):
        part = pl.ds(pl.multiple_of(32 * ((z + k) % 4), 16), WINDOW)
        return remote(s3.at[t % 2, part], r3.at[t % 4, k - 1], s3_sem.at[t % 2, k - 1], r3_sem.at[t % 4, k - 1], near[k - 1])

    def share_copy(t):
        return pltpu.make_async_copy(share.at[t % 2], total.at[t], share_sem.at[t % 2])

    def tick(t):
        @pl.when(t >= 8)
        def _():
            now = t - 8
            value = wide32(s3[now % 2, pl.ds(pl.multiple_of(32 * z, 16), WINDOW)])
            for k in (1, 2, 3):
                copy3(now, k).wait_recv()
                value = value + wide32(r3[now % 4, k - 1])

            @pl.when(now >= 2)
            def _():
                share_copy(now - 2).wait()
            share[now % 2] = value
            share_copy(now).start()

        @pl.when((t >= 6) & (t < BLOCKS + 6))
        def _():
            now = t - 6
            copy2(now).wait_recv()

            @pl.when(now >= 2)
            def _():
                for k in (1, 2, 3):
                    copy3(now - 2, k).wait_send()
            value = k2[now % 2] + wide32(r2[now % 4])
            s3[now % 2] = to_low(value)
            for k in (1, 2, 3):
                copy3(now, k).start()

        @pl.when((t >= 4) & (t < BLOCKS + 4))
        def _():
            now = t - 4
            copy1(now, 0).wait_recv()

            @pl.when(now >= 2)
            def _():
                copy2(now - 2).wait_send()
            s2[now % 2] = to_low(wide32(s1[now % 2, stay[0]]) + wide32(r1[now % 4, 0]))
            copy2(now).start()
            copy1(now, 1).wait_recv()
            k2[now % 2] = wide32(s1[now % 2, stay[1]]) + wide32(r1[now % 4, 1])

        @pl.when((t >= 2) & (t < BLOCKS + 2))
        def _():
            now = t - 2

            @pl.when(now >= 2)
            def _():
                for l in range(2):
                    copy1(now - 2, l).wait_send()
            for l in range(2):
                copy0(now, l).wait_recv()
                value = product(now, c, l)
                for part in range(2):
                    line = 2 * l + part
                    summed = value[part * LINE : part * LINE + LINE] + wide32(r0[now % 4, line])
                    s1[now % 2, line] = to_low(summed)
            for l in range(2):
                copy1(now, l).start()

        @pl.when(t < BLOCKS)
        def _():
            for l in range(2):
                @pl.when(t >= 2)
                def _():
                    copy0(t - 2, l).wait_send()
                value = to_low(product(t, 1 - c, l))
                s0[t % 2, 2 * l] = value[:LINE]
                s0[t % 2, 2 * l + 1] = value[LINE:]
                copy0(t, l).start()

    done = [0]

    def pump(until):
        if until > done[0]:
            start = done[0]
            loop(until - start, lambda i: tick(i + start))
            done[0] = until

    def pick(piece, seg):
        lanes = slice(WIDE * piece, WIDE * piece + WIDE)
        return jnp.where(seg > 0.5, mods[1:2, lanes], mods[0:1, lanes])

    def by_video(piece, value, seg):
        lanes = slice(WIDE * piece, WIDE * piece + WIDE)
        later = jnp.sum(value * seg, axis=0, keepdims=True)
        every = jnp.sum(value, axis=0, keepdims=True)
        gm[0:1, lanes] = gm[0:1, lanes] + (every - later)
        gm[1:2, lanes] = gm[1:2, lanes] + later

    def through(values_at, blocks, emit, grouped=False):
        for n, (values, block) in enumerate(zip(values_at, blocks)):
            have(("w", block))

            def tile(cols, n=n, values=values, block=block):
                part = nt(values[...], weight(block)[cols, :])
                if n > 0:
                    part = part + work[:, cols]
                if n == len(blocks) - 1:
                    xin[:, cols] = to_low(part)
                else:
                    work[:, cols] = part

            each_cols(tile)
            release(block)
        if grouped:
            xin[...] = to_low(linear(regroup(True), xin[...]))
        turn_back(emit)

    def turn_back(emit):
        each_cols(lambda cols: emit(cols, linear(xin[...], turn[:, cols])))

    def emit_work(cols, value):
        work[:, cols] = value

    def emit_grad(cols, value):
        grad[:, cols] = to_low(value)

    def norm_back(grad_in, tilt, at, rows):
        slope_in = grad_in * tilt
        hat = wide32(xhat[at, rows, :])
        first_mean = jnp.mean(slope_in, axis=-1, keepdims=True)
        second_mean = jnp.mean(slope_in * hat, axis=-1, keepdims=True)
        return rstd[at, rows, 0:1] * (slope_in - first_mean - hat * second_mean)

    gm[...] = jnp.zeros_like(gm)
    have(0)
    have(12)
    have(18)
    have(19)
    gm[0:8, 8 * WIDE : 9 * WIDE] = work[0:8]
    stream[...] = wide32(xin[...])
    for k in range(5):
        have(1 + k)
    pump(2)
    for k in range(4):
        have(14 + k % 2 if k < 2 else ("slope", k))
        have(("w", 11 + 2 * k))

        def tile(cols, k=k):
            value = nt(right[0], weight(11 + 2 * k)[cols, :]) * wide32(slope[k % 2, :, cols])
            right[1 + k, :, cols] = to_low(value)

        each_cols(tile)
        release(11 + 2 * k)
        if k < 2:
            copy = pltpu.make_async_copy(slope_i.at[k + 2], slope.at[k % 2], in_sem.at[14 + k])
            copy.start()
            fetches["slope", k + 2] = copy
        have(("w", 10 + 2 * k))

        def tile(cols, k=k):
            part = nt(right[1 + k], weight(10 + 2 * k)[cols, :])
            if k > 0:
                part = part + work[:, cols]
            if k < 3:
                work[:, cols] = part
            else:
                xin[:, cols] = to_low(part)

        each_cols(tile)
        release(10 + 2 * k)
        pump(k + 3)
    turn_back(emit_work)
    for k in range(5, 11):
        have(1 + k)
    have(16)
    have(17)
    fetch(20, qc_i, qkv.at[0])
    fetch(21, mem_i.at[0], mem.at[0])
    fetch(22, mem_i.at[1], mem.at[1])
    fetch(23, xhat_i.at[2], xhat.at[0])
    fetch(24, rstd_i.at[2], rstd.at[0])

    def after_mlp(rows):
        seg = seg_in[0, rows, 0:1]
        value = work[rows, :]
        by_video(6, value, seg)
        by_video(7, value * wide32(xhat[1, rows, :]), seg)
        value = stream[rows, :] + norm_back(value, 1.0 + pick(7, seg), 1, rows)
        stream[rows, :] = value
        right[5, rows, :] = to_low(value)

    each_rows(32, after_mlp)

    fetch(25, xhat_i.at[1], xhat.at[1])
    fetch(26, rstd_i.at[1], rstd.at[1])
    through([right.at[5]], [9], emit_grad)
    right[6] = jnp.zeros_like(right[6])
    dmem[...] = jnp.zeros_like(dmem)
    for name in (13, 20, 21, 22, 23, 24):
        have(name)

    def cross_heads(h):
        text_heads_backward(
            h, qkv.at[0], mem.at[0], mem.at[1], grad, right.at[6], dmem.at[0], dmem.at[1],
            cross_bias(), cross_rows(seg_in),
        )

    for part in range(4):
        loop(2, lambda h: cross_heads(h + 2 * part))
        pump(7 + (part + 1) // 2)

    def dmem_part(zp, yp):
        return dmem.at[zp // 2, pl.ds(pl.multiple_of(TEXT * (zp % 2 * 2 + yp), 16), TEXT)]

    def x_over(zp):
        return remote(dmem_part(zp, 1 - y), text.at[zp], x_send.at[zp], x_recv.at[zp], device(x, c, 1 - y, z))

    def x_copy(k):
        return remote(texts.at[(z + k) % 4], text_at.at[k - 1], x_send.at[3 + k], x_recv.at[3 + k], near[k - 1])

    for zp in range(4):
        x_over(zp).start()
    fetch(27, qkvt_i.at[0], qkv.at[0])
    fetch(28, qkvt_i.at[1], qkv.at[1])
    fetch(29, qkvt_i.at[2], qkv.at[2])
    fetch(30, branch_i.at[1], branch)
    through([right.at[6]], [8], emit_work)
    gains[0] = jnp.zeros_like(gains[0])
    have(30)

    def after_cross(rows):
        seg = seg_in[0, rows, 0:1]
        value = work[rows, :]
        gains[0, 0:1, :] = gains[0, 0:1, :] + jnp.sum(value * wide32(xhat[0, rows, :]), axis=0, keepdims=True)
        value = stream[rows, :] + norm_back(value, gain[0:1, :], 0, rows)
        stream[rows, :] = value
        by_video(5, value * wide32(branch[rows, :]), seg)
        right[7, rows, :] = to_low(value * pick(5, seg))

    each_rows(32, after_cross)

    def g_copy(at, to):
        return remote(gains.at[min(at, 3)], gain_at.at[at], g_send.at[at], g_recv.at[at], to)

    g_copy(0, twin).start()
    fetch(31, branch_i.at[0], branch)
    fetch(32, xhat_i.at[0], xhat.at[0])
    fetch(33, rstd_i.at[0], rstd.at[0])
    pump(10)

    through([right.at[7]], [7], emit_grad)
    grad[...] = to_low(linear(regroup(False), grad[...]))
    bias[...] = temporal_bias(seg_in, seg_row)
    for j in range(3):
        right[8 + j] = jnp.zeros_like(right[8 + j])
    for name in (25, 26, 27, 28, 29):
        have(name)

    def temporal_heads(h):
        heads_backward(
            h, qkv.at[0], qkv.at[1], qkv.at[2], grad, right.at[8], right.at[9], right.at[10],
            HALVES, jnp.concatenate([bias[...]] * 4), None,
        )

    loop(4, temporal_heads)
    pump(11)
    g_copy(0, twin).wait_recv()
    gains[1] = gains[0] + gain_at[0]
    g_copy(1, first).start()
    loop(4, lambda h: temporal_heads(h + 4))
    pump(12)
    g_copy(1, first).wait_recv()
    gains[2] = gains[1] + gain_at[1]
    g_copy(2, second).start()
    for zp in range(4):
        x_over(zp).wait_recv()
        texts[zp] = to_low(wide32(dmem_part(zp, y)[...]) + wide32(text[zp]))
    for k in (1, 2, 3):
        x_copy(k).start()
    for j in range(3):
        fetch(34 + j, qkvs_i.at[j], qkv.at[j])
    through([right.at[8], right.at[9], right.at[10]], [4, 5, 6], emit_work, True)
    have(31)

    def after_temporal(rows):
        seg = seg_in[0, rows, 0:1]
        value = work[rows, :]
        by_video(3, value, seg)
        by_video(4, value * wide32(xhat[1, rows, :]), seg)
        value = stream[rows, :] + norm_back(value, 1.0 + pick(4, seg), 1, rows)
        stream[rows, :] = value
        by_video(2, value * wide32(branch[rows, :]), seg)
        right[11, rows, :] = to_low(value * pick(2, seg))

    each_rows(32, after_temporal)

    through([right.at[11]], [3], emit_grad)

    def a_copy(k):
        to = (b + k) % 8
        part = grad.at[pl.ds(pl.multiple_of(32 * to, 32), 32)]
        return remote(part, back.at[b], a_send.at[k - 1], a_recv.at[k - 1], peers[k - 1])

    def a_wait(k):
        of = (b + 8 - k) % 8
        remote(grad.at[pl.ds(0, 32)], back.at[of], a_send.at[k - 1], a_recv.at[k - 1], peers[k - 1]).wait_recv()

    for k in (1, 2, 3):
        x_copy(k).wait_recv()
    text_o[...] = to_low(wide32(texts[z]) + wide32(text_at[0]) + wide32(text_at[1]) + wide32(text_at[2]))
    for k in range(1, 8):
        a_copy(k).start()
    back[b] = grad[pl.ds(pl.multiple_of(32 * b, 32), 32)]
    pump(13)
    g_copy(2, second).wait_recv()
    gains[3] = gains[2] + gain_at[2]
    for k in (1, 2, 3):
        g_copy(2 + k, near[k - 1]).start()
    for j in range(3):
        right[12 + j] = jnp.zeros_like(right[12 + j])
    for name in (32, 33, 34, 35, 36):
        have(name)
    for k in range(1, 8):
        a_wait(k)
    for k in range(8):
        for f in range(2):
            gframe[128 * f + 16 * k : 128 * f + 16 * k + 16, :] = back[k, 16 * f : 16 * f + 16, :]

    def spatial_heads(h):
        heads_backward(
            h, qkv.at[0], qkv.at[1], qkv.at[2], gframe, right.at[12], right.at[13], right.at[14], HALVES, None, None
        )

    loop(4, spatial_heads)
    pump(14)
    loop(4, lambda h: spatial_heads(h + 4))
    pump(15)
    through([right.at[12], right.at[13], right.at[14]], [0, 1, 2], emit_work)
    pump(16)
    for k in range(1, 8):
        a_copy(k).wait_send()

    def after_spatial(i):
        rows = pl.ds(pl.multiple_of(16 * i, 16), 16)
        seg = seg_in[1, rows, 0:1]
        value = work[rows, :]
        by_video(0, value, seg)
        by_video(1, value * wide32(xhat[0, rows, :]), seg)
        value = to_low(norm_back(value, 1.0 + pick(1, seg), 0, rows))
        back[i % 8, pl.ds(pl.multiple_of(16 * (i // 8), 16), 16), :] = value

    loop(16, after_spatial)

    def u_copy(k):
        to = (b + k) % 8
        return remote(back.at[to], backp.at[b], u_send.at[k - 1], u_recv.at[k - 1], peers[k - 1])

    def u_wait(k):
        of = (b + 8 - k) % 8
        remote(back.at[0], backp.at[of], u_send.at[k - 1], u_recv.at[k - 1], peers[k - 1]).wait_recv()

    def m_copy(k):
        to = (b + k) % 8
        return remote(mod_out.at[to], mod.at[b], m_send.at[k - 1], m_recv.at[k - 1], peers[k - 1])

    def m_wait(k):
        of = (b + 8 - k) % 8
        remote(mod_out.at[0], mod.at[of], m_send.at[k - 1], m_recv.at[k - 1], peers[k - 1]).wait_recv()

    for k in range(1, 8):
        u_copy(k).start()
    backp[b] = back[b]
    for k in range(8):
        tiles = [
            gm[row : row + 1, 1280 * k + 128 * tile : 1280 * k + 128 * tile + 128]
            for row in range(2)
            for tile in range(MOD_TILES)
        ]
        mod_out[k] = to_low(jnp.concatenate(tiles + [jnp.zeros((32 - 2 * MOD_TILES, 128), jnp.float32)]))
    for k in range(1, 8):
        m_copy(k).start()
    mod[b] = mod_out[b]
    pump(18)
    for k in range(1, 8):
        m_wait(k)
    summed = wide32(mod[0])
    for k in range(1, 8):
        summed = summed + wide32(mod[k])
    own = x * 2 + c
    seqs[own, 0:32] = to_low(summed)
    seqs[own, 32:64] = cond_in[...]
    places = [x * 2 + 1 - c, (1 - x) * 2 + c, (1 - x) * 2 + 1 - c]

    def q_copy(k, at):
        return remote(seqs.at[own], seqs.at[at], q_send.at[k], q_recv.at[k], across[k])

    for k in range(3):
        q_copy(k, own).start()
    for k in range(1, 8):
        u_wait(k)
    xin[...] = to_low(stream[...] + wide32(backp[...].reshape(ROWS, WIDE)))
    gtok[...] = to_low(linear(swap_rows(), xin[...]))
    for k in (1, 2, 3):
        g_copy(2 + k, near[k - 1]).wait_recv()
    gain_o[...] = gains[3] + gain_at[3] + gain_at[4] + gain_at[5]
    pump(BLOCKS + 8)
    for k in range(3):
        q_copy(k, places[k]).wait_recv()
    mod_o[...] = seqs[...]

    for now in (BLOCKS - 2, BLOCKS - 1):
        for l in range(2):
            copy0(now, l).wait_send()
            copy1(now, l).wait_send()
        copy2(now).wait_send()
        for k in (1, 2, 3):
            copy3(now, k).wait_send()
        share_copy(now).wait()
    for k in range(1, 8):
        u_copy(k).wait_send()
        m_copy(k).wait_send()
        x_over(k - 1).wait_send() if k < 5 else x_copy(k - 4).wait_send()
    for k in range(3):
        q_copy(k, own).wait_send()
    for at, to in enumerate([twin, first, second] + near):
        g_copy(at, to).wait_send()


WEIGHT_ORDER = (11, 10, 13, 12, 15, 14, 17, 16, 9, 8, 7, 4, 5, 6, 3, 0, 1, 2)


def backward(*operands):
    low, full = jnp.bfloat16, jnp.float32
    dma = pltpu.SemaphoreType.DMA
    outs = [
        ((BLOCKS, WINDOW, WIDE), full),
        ((ROWS, WIDE), low),
        ((8, WIDE), full),
        ((TEXT, KEYS), low),
        ((4, 64, 128), low),
    ]
    vmem = [
        ((2, WIDE, WIDE), low),
        ((11, WIDE, ROWS), low),
        ((15, ROWS, WIDE), low),
        ((3, ROWS, WIDE), low),
        ((2, ROWS, WIDE), low),
        ((2, ROWS, 128), full),
        ((ROWS, WIDE), low),
        ((2, ROWS, WIDE), low),
        ((8, MOD), full),
        ((8, WIDE), full),
        ((128, 128), full),
        ((ROWS, WIDE), full),
        ((ROWS, WIDE), full),
        ((ROWS, WIDE), low),
        ((ROWS, WIDE), low),
        ((8, MOD), full),
        ((2, WIDE, KEYS), low),
        ((2, WIDE, KEYS), low),
        ((4, TEXT, KEYS), low),
        ((4, TEXT, KEYS), low),
        ((3, TEXT, KEYS), low),
        ((8, 32, 128), low),
        ((8, 32, 128), low),
        ((4, 64, 128), low),
        ((4, 8, WIDE), full),
        ((6, 8, WIDE), full),
        ((ROWS, WIDE), low),
        ((8, 32, WIDE), low),
        ((8, 32, WIDE), low),
        ((2, 4, LINE, WIDE), low),
        ((4, 4, LINE, WIDE), low),
        ((2, 4, LINE, WIDE), low),
        ((4, 2, LINE, WIDE), low),
        ((2, LINE, WIDE), low),
        ((4, LINE, WIDE), low),
        ((2, LINE, WIDE), full),
        ((2, LINE, WIDE), low),
        ((4, 3, WINDOW, WIDE), low),
        ((2, WINDOW, WIDE), full),
    ]
    return pl.pallas_call(
        backward_kernel,
        out_shape=[jax.ShapeDtypeStruct(*shape) for shape in outs],
        in_specs=[ANY] * 15 + [IN_VMEM] * 4,
        out_specs=[ANY] + [IN_VMEM] * 4,
        scratch_shapes=[pltpu.VMEM(*shape) for shape in vmem]
        + [
            dma((40,)), dma((2,)), dma((2, 4)), dma((4, 4)), dma((2, 2)), dma((4, 2)), dma((2,)), dma((4,)),
            dma((2, 3)), dma((4, 3)), dma((2,)), dma((7,)), dma((7,)), dma((7,)), dma((7,)), dma((7,)), dma((7,)),
            dma((7,)), dma((7,)), dma((3,)), dma((3,)), dma((6,)), dma((6,)),
        ],
        compiler_params=pltpu.CompilerParams(
            collective_id=1, has_side_effects=True, vmem_limit_bytes=63 * MIB
        ),
        name="backward",
    )(*operands)


TURN = np.arange(WIDE)[None, :] == (
    np.arange(WIDE).reshape(2, 2, 4, 2, SHARD).transpose(1, 0, 3, 2, 4).reshape(-1)
)[:, None]


def hidden_pick():
    pick = np.full((16, TILE), -1, np.int32)
    for k in range(4):
        for g in range(4):
            for at in range(8 * SHARD):
                yp, rest = divmod(at, 4 * SHARD)
                zp, r = divmod(rest, SHARD)
                pick[4 * k + g, 32 * g + at] = (2 * zp + yp) * 4 * SHARD + SHARD * k + r
    return pick


HIDDEN_PICK = hidden_pick()


def hidden_back(values):
    rows = values.shape[0]
    cut = values.reshape(rows, 4, 2, 2, 2, 4, SHARD)
    return cut.transpose(0, 3, 2, 5, 4, 1, 6).reshape(rows, 4 * WIDE)


def shards(
    tokens,
    segments,
    timesteps,
    caption,
    cotangent,
    ada_weight,
    ada_bias,
    spatial_in,
    spatial_out,
    temporal_in,
    temporal_out,
    cross_gain,
    cross_query,
    caption_proj,
    cross_out,
    hidden_in,
    hidden_out,
):
    frame_seg = segments[0]
    text_width = caption.shape[-1]
    caption_rows = caption[0].reshape(2 * L, text_width)
    blk = lax.axis_index("blk")
    seq = lax.axis_index("seq")
    zplace = blk // 2
    conditioning = to_low(jax.nn.silu(time_embedding(timesteps[0], WIDE)))
    cond_in = jnp.pad(conditioning.reshape(2 * WIDE // 128, 128), ((0, 32 - 2 * WIDE // 128), (0, 0)))
    frames = frame_seg.astype(jnp.float32)
    own_frames = lax.dynamic_slice(frames, (2 * blk,), (2,))
    seg_in = jnp.broadcast_to(
        jnp.stack(
            [jnp.repeat(frames, 16), jnp.repeat(own_frames, 128), jnp.tile(jnp.repeat(frames, 8), 2)]
        )[:, :, None],
        (3, ROWS, 128),
    )
    seg_row = jnp.broadcast_to(jnp.repeat(frames, 8)[None], (8, 128))
    turn = jnp.asarray(TURN, jnp.bfloat16)
    wide, out, *kept = forward(
        spatial_in,
        spatial_out,
        temporal_in,
        temporal_out,
        cross_query,
        cross_out,
        hidden_in,
        hidden_out,
        tokens.reshape(ROWS, WIDE),
        jnp.pad(cross_gain[None], ((0, 7), (0, 0))),
        jnp.pad(conditioning, ((0, 14), (0, 0))),
        ada_bias[None],
        seg_in,
        seg_row,
        jnp.asarray(HIDDEN_PICK),
        cotangent.reshape(ROWS, WIDE),
        turn,
        ada_weight,
        caption[0],
        caption_proj,
    )
    spread, grad_tokens, grad_gain, grad_text, grad_mod = backward(
        wide, *kept, seg_in, seg_row, turn, cond_in
    )
    shares = lax.dynamic_slice(spread, (0, 4 * zplace, 0), (BLOCKS, SHARD, WIDE))
    share_gain = lax.dynamic_slice(grad_gain, (0, SHARD * (seq * 8 + blk)), (1, SHARD))[0]
    text_low = grad_text.reshape(TEXT, 2, 128)[:, :, :L].reshape(TEXT, 2 * L)
    grad_caption = lax.dot_general(
        caption_rows, text_low, (((0,), (1,)), ((), ())), preferred_element_type=jnp.float32
    )
    grad_caption = lax.psum(grad_caption.astype(jnp.bfloat16), "seq").astype(jnp.float32)
    all_mod = lax.dynamic_slice(
        grad_mod[:, : 2 * MOD_TILES].reshape(8, MOD_WIN), (0, 16 * blk), (8, MOD // 8)
    )
    all_cond = grad_mod[:, 32 : 32 + 2 * WIDE // 128].reshape(8, WIDE)
    grad_ada_w = left_product(all_cond, all_mod)
    grad_ada_b = jnp.sum(all_mod.astype(jnp.float32), axis=0)

    def joined(first, count):
        return shares[first : first + count].transpose(1, 0, 2).reshape(SHARD, count * WIDE)

    return (
        out.reshape(tokens.shape),
        grad_tokens.reshape(tokens.shape),
        grad_ada_w,
        grad_ada_b,
        joined(15, 3),
        shares[14],
        joined(11, 3),
        shares[10],
        share_gain,
        shares[9],
        grad_caption,
        shares[8],
        hidden_back(joined(4, 4)),
        shares[0:4].reshape(4 * SHARD, WIDE),
    )


def solution(mesh):
    fast = dict(mesh.shape) == {"seq": 4, "blk": 8}
    return jax.shard_map(
        shards if fast else general_shards,
        mesh=mesh,
        in_specs=(
            P("seq", "blk", None, None),
            P("seq", None),
            P("seq", None),
            P("seq", None, None, None),
            P("seq", "blk", None, None),
            P(None, "blk"),
            P("blk"),
            P(("seq", "blk"), None),
            P(("seq", "blk"), None),
            P(("seq", "blk"), None),
            P(("seq", "blk"), None),
            P(("seq", "blk")),
            P(("seq", "blk"), None),
            P(None, "blk"),
            P(("seq", "blk"), None),
            P(("seq", "blk"), None),
            P(("seq", "blk"), None),
        ),
        out_specs=(
            P("seq", "blk", None, None),
            P("seq", "blk", None, None),
            P(None, "blk"),
            P("blk"),
            P(("seq", "blk"), None),
            P(("seq", "blk"), None),
            P(("seq", "blk"), None),
            P(("seq", "blk"), None),
            P(("seq", "blk")),
            P(("seq", "blk"), None),
            P(None, "blk"),
            P(("seq", "blk"), None),
            P(("seq", "blk"), None),
            P(("seq", "blk"), None),
        ),
        check_vma=False,
    )
```

```python
import math

import jax
import jax.numpy as jnp
import numpy as np
from jax import lax
from jax.experimental import pallas as pl
from jax.experimental.pallas import tpu as pltpu
from jax.sharding import PartitionSpec as P

H = 16
E = 72
L = 120


EPSILON = 1e-06
MASKED = -1e30


def to_low(values):
    return values.astype(jnp.bfloat16)


def linear(left, right):
    return jnp.dot(left, right, preferred_element_type=jnp.float32)


def left_product(left, right):
    return lax.dot_general(
        left, right, (((0,), (0,)), ((), ())), preferred_element_type=jnp.float32
    )


def right_product(left, right):
    return lax.dot_general(
        left, right, (((1,), (1,)), ((), ())), preferred_element_type=jnp.float32
    )


def normalize(values):
    center = values - jnp.mean(values, axis=-1, keepdims=True)
    return center * lax.rsqrt(jnp.mean(center * center, axis=-1, keepdims=True) + EPSILON)


def modulate(values, shift_rows, scale_rows):
    return normalize(values) * (1.0 + scale_rows) + shift_rows


def gain_norm(values, gain_row):
    return normalize(values) * gain_row


def gelu_tanh(values):
    return jax.nn.gelu(values, approximate=True)


def softmax_rows(scores):
    shifted = jnp.exp(scores - jnp.max(scores, axis=-1, keepdims=True))
    return shifted / jnp.sum(shifted, axis=-1, keepdims=True)


def softmax_with_total(scores):
    top = jnp.max(scores, axis=-1, keepdims=True)
    shifted = jnp.exp(scores - top)
    total = jnp.sum(shifted, axis=-1, keepdims=True)
    return (shifted / total, (top + jnp.log(total))[..., 0])


def softmax_back(probs, grad_probs):
    return probs * (grad_probs - jnp.sum(grad_probs * probs, axis=-1, keepdims=True))


def time_embedding(step_ids, model_width):
    half_width = model_width // 2
    frequency = jnp.exp(
        -math.log(10000.0) * jnp.arange(half_width).astype(jnp.float32) / half_width
    )
    angles = step_ids.astype(jnp.float32)[:, None] * frequency[None, :]
    return jnp.concatenate([jnp.cos(angles), jnp.sin(angles)], axis=1)


def general_shards(
    tokens,
    segments,
    timesteps,
    caption,
    cotangent,
    ada_weight,
    ada_bias,
    spatial_in,
    spatial_out,
    temporal_in,
    temporal_out,
    cross_gain,
    cross_query,
    caption_proj,
    cross_out,
    hidden_in,
    hidden_out,
):
    inputs = tokens[0].astype(jnp.float32)
    patch_dev, frames, model_width = inputs.shape
    token_rows = patch_dev * frames
    head_count = H
    head_size = E
    score_scale = E ** (-0.5)
    frame_seg = segments[0]
    step_ids = timesteps[0]
    seg_count, text_len, text_width = caption.shape[1:]
    text_keys = seg_count * text_len
    caption_rows = caption[0].reshape(text_keys, text_width)
    grad_out = cotangent[0].astype(jnp.float32)
    gathered = (
        lax.all_gather(spatial_in, ("seq", "blk"), axis=0, tiled=True),
        lax.all_gather(spatial_out, ("seq", "blk"), axis=0, tiled=True),
        lax.all_gather(temporal_in, ("seq", "blk"), axis=0, tiled=True),
        lax.all_gather(temporal_out, ("seq", "blk"), axis=0, tiled=True),
        lax.all_gather(cross_gain, ("seq", "blk"), axis=0, tiled=True),
        lax.all_gather(cross_query, ("seq", "blk"), axis=0, tiled=True),
        lax.all_gather(cross_out, ("seq", "blk"), axis=0, tiled=True),
        lax.all_gather(hidden_in, ("seq", "blk"), axis=0, tiled=True),
        lax.all_gather(hidden_out, ("seq", "blk"), axis=0, tiled=True),
    )
    (
        wide_sin,
        wide_sout,
        wide_tin,
        wide_tout,
        gain_low,
        wide_query,
        wide_cout,
        wide_hin,
        wide_hout,
    ) = gathered
    gain_row = gain_low.astype(jnp.float32)
    conditioning = to_low(jax.nn.silu(time_embedding(step_ids, model_width)))
    mod_part = to_low(linear(conditioning, ada_weight) + ada_bias.astype(jnp.float32))
    text_part = to_low(linear(caption_rows, caption_proj))
    modulation, memory = (
        lax.all_gather(mod_part, "blk", axis=1, tiled=True),
        lax.all_gather(text_part, "blk", axis=1, tiled=True),
    )
    choose = frame_seg[:, None] == jnp.arange(seg_count, dtype=jnp.int32)[None, :]
    frame_mod = linear(choose.astype(jnp.bfloat16), modulation)
    pieces = [frame_mod[:, index * model_width : (index + 1) * model_width] for index in range(9)]
    (
        shift_one,
        scale_one,
        gate_one,
        shift_two,
        scale_two,
        gate_two,
        shift_three,
        scale_three,
        gate_three,
    ) = pieces
    spatial_input = to_low(modulate(inputs, shift_one, scale_one)).reshape(token_rows, model_width)
    spatial_qkv = to_low(linear(spatial_input, wide_sin)).reshape(
        patch_dev, frames, 3 * model_width
    )
    query_s = spatial_qkv[..., :model_width].reshape(patch_dev, frames, head_count, head_size)
    local_kv = spatial_qkv[..., model_width:]
    whole_kv = lax.all_gather(local_kv, "blk", axis=0, tiled=True)

    def split_kv(both):
        count = both.shape[0]
        return (
            both[..., :model_width].reshape(count, frames, head_count, head_size),
            both[..., model_width:].reshape(count, frames, head_count, head_size),
        )

    def spatial_probs(key_all):
        scores = jnp.einsum("pfhe,qfhe->fhpq", query_s, key_all, preferred_element_type=jnp.float32)
        return softmax_with_total(scores * score_scale)

    key_s, value_s = split_kv(whole_kv)
    probs_s, log_total_s = spatial_probs(key_s)
    probs_s_low = to_low(probs_s)
    attn_s = to_low(
        jnp.einsum(
            "fhpq,qfhe->pfhe", probs_s_low, value_s, preferred_element_type=jnp.float32
        ).reshape(token_rows, model_width)
    )
    branch_s = linear(attn_s, wide_sout).reshape(patch_dev, frames, model_width)
    after_one = inputs + gate_one * branch_s
    temporal_input = to_low(modulate(after_one, shift_two, scale_two)).reshape(
        token_rows, model_width
    )
    temporal_qkv = to_low(linear(temporal_input, wide_tin)).reshape(
        patch_dev, frames, 3, head_count, head_size
    )
    query_t = temporal_qkv[:, :, 0]
    key_t = temporal_qkv[:, :, 1]
    value_t = temporal_qkv[:, :, 2]
    same_seg = frame_seg[:, None] == frame_seg[None, :]
    scores_t = (
        jnp.einsum("pfhe,pghe->phfg", query_t, key_t, preferred_element_type=jnp.float32)
        * score_scale
    )
    probs_t = softmax_rows(jnp.where(same_seg[None, None], scores_t, MASKED))
    probs_t_low = to_low(probs_t)
    attn_t = to_low(
        jnp.einsum(
            "phfg,pghe->pfhe", probs_t_low, value_t, preferred_element_type=jnp.float32
        ).reshape(token_rows, model_width)
    )
    branch_t = linear(attn_t, wide_tout).reshape(patch_dev, frames, model_width)
    after_two = after_one + gate_two * branch_t
    cross_input = to_low(gain_norm(after_two, gain_row)).reshape(token_rows, model_width)
    query_c = to_low(linear(cross_input, wide_query)).reshape(
        patch_dev, frames, head_count, head_size
    )
    key_c = memory[:, :model_width].reshape(text_keys, head_count, head_size)
    value_c = memory[:, model_width:].reshape(text_keys, head_count, head_size)
    key_seg = jnp.arange(text_keys, dtype=jnp.int32) // text_len
    allowed = frame_seg[:, None] == key_seg[None, :]
    scores_c = (
        jnp.einsum("pfhe,khe->pfhk", query_c, key_c, preferred_element_type=jnp.float32)
        * score_scale
    )
    probs_c = softmax_rows(jnp.where(allowed[None, :, None, :], scores_c, MASKED))
    probs_c_low = to_low(probs_c)
    attn_c = to_low(
        jnp.einsum(
            "pfhk,khe->pfhe", probs_c_low, value_c, preferred_element_type=jnp.float32
        ).reshape(token_rows, model_width)
    )
    branch_c = linear(attn_c, wide_cout).reshape(patch_dev, frames, model_width)
    after_three = after_two + branch_c
    mlp_input = to_low(modulate(after_three, shift_three, scale_three)).reshape(
        token_rows, model_width
    )
    pre_act = linear(mlp_input, wide_hin)
    post_act = to_low(gelu_tanh(pre_act))
    branch_m = linear(post_act, wide_hout).reshape(patch_dev, frames, model_width)
    result = after_three + gate_three * branch_m
    grad_gate_three = jnp.sum(grad_out * branch_m, axis=0)
    grad_four = to_low(grad_out * gate_three).reshape(token_rows, model_width)
    grad_hout = left_product(post_act, grad_four)
    grad_post = right_product(grad_four, wide_hout)
    gelu_pull = jax.vjp(gelu_tanh, pre_act)[1]
    grad_pre = to_low(gelu_pull(grad_post)[0])
    grad_hin = left_product(mlp_input, grad_pre)
    grad_mlp_in = right_product(grad_pre, wide_hin).reshape(patch_dev, frames, model_width)
    mlp_pull = jax.vjp(modulate, after_three, shift_three, scale_three)[1]
    back_three, grad_shift_three, grad_scale_three = mlp_pull(grad_mlp_in)
    grad_three = grad_out + back_three
    grad_cross_branch = to_low(grad_three).reshape(token_rows, model_width)
    grad_cout = left_product(attn_c, grad_cross_branch)
    grad_attn_c = to_low(right_product(grad_cross_branch, wide_cout)).reshape(
        patch_dev, frames, head_count, head_size
    )
    grad_probs_c = jnp.einsum(
        "pfhe,khe->pfhk", grad_attn_c, value_c, preferred_element_type=jnp.float32
    )
    grad_scores_c = to_low(softmax_back(probs_c, grad_probs_c))
    grad_query_c = to_low(
        jnp.einsum("pfhk,khe->pfhe", grad_scores_c, key_c, preferred_element_type=jnp.float32)
        * score_scale
    ).reshape(token_rows, model_width)
    grad_key_c = (
        jnp.einsum("pfhk,pfhe->khe", grad_scores_c, query_c, preferred_element_type=jnp.float32)
        * score_scale
    )
    grad_value_c = jnp.einsum(
        "pfhk,pfhe->khe", probs_c_low, grad_attn_c, preferred_element_type=jnp.float32
    )
    grad_memory = jnp.concatenate(
        [grad_key_c.reshape(text_keys, model_width), grad_value_c.reshape(text_keys, model_width)],
        axis=1,
    )
    grad_wquery = left_product(cross_input, grad_query_c)
    grad_cross_in = right_product(grad_query_c, wide_query).reshape(patch_dev, frames, model_width)
    cross_pull = jax.vjp(gain_norm, after_two, gain_row)[1]
    back_two, grad_gain = cross_pull(grad_cross_in)
    grad_two = grad_three + back_two
    grad_gate_two = jnp.sum(grad_two * branch_t, axis=0)
    grad_temporal_branch = to_low(grad_two * gate_two).reshape(token_rows, model_width)
    grad_tout = left_product(attn_t, grad_temporal_branch)
    grad_attn_t = to_low(right_product(grad_temporal_branch, wide_tout)).reshape(
        patch_dev, frames, head_count, head_size
    )
    grad_probs_t = jnp.einsum(
        "pfhe,pghe->phfg", grad_attn_t, value_t, preferred_element_type=jnp.float32
    )
    grad_scores_t = to_low(softmax_back(probs_t, grad_probs_t))
    grad_query_t = (
        jnp.einsum("phfg,pghe->pfhe", grad_scores_t, key_t, preferred_element_type=jnp.float32)
        * score_scale
    )
    grad_key_t = (
        jnp.einsum("phfg,pfhe->pghe", grad_scores_t, query_t, preferred_element_type=jnp.float32)
        * score_scale
    )
    grad_value_t = jnp.einsum(
        "phfg,pfhe->pghe", probs_t_low, grad_attn_t, preferred_element_type=jnp.float32
    )
    grad_qkv_t = to_low(jnp.stack([grad_query_t, grad_key_t, grad_value_t], axis=2)).reshape(
        token_rows, 3 * model_width
    )
    grad_tin = left_product(temporal_input, grad_qkv_t)
    grad_temporal_in = right_product(grad_qkv_t, wide_tin).reshape(patch_dev, frames, model_width)
    temporal_pull = jax.vjp(modulate, after_one, shift_two, scale_two)[1]
    back_one, grad_shift_two, grad_scale_two = temporal_pull(grad_temporal_in)
    grad_one = grad_two + back_one
    grad_gate_one = jnp.sum(grad_one * branch_s, axis=0)
    grad_spatial_branch = to_low(grad_one * gate_one).reshape(token_rows, model_width)
    grad_sout = left_product(attn_s, grad_spatial_branch)
    grad_attn_s = to_low(right_product(grad_spatial_branch, wide_sout)).reshape(
        patch_dev, frames, head_count, head_size
    )
    back_kv = lax.all_gather(local_kv, "blk", axis=0, tiled=True)
    back_key, back_value = split_kv(back_kv)
    back_probs = spatial_probs(back_key)[0]
    back_probs_low = to_low(back_probs)
    grad_probs_s = jnp.einsum(
        "pfhe,qfhe->fhpq", grad_attn_s, back_value, preferred_element_type=jnp.float32
    )
    row_delta = jnp.sum(grad_probs_s * back_probs, axis=-1, keepdims=True)
    grad_scores_s = to_low(back_probs * (grad_probs_s - row_delta))
    grad_query_s = (
        jnp.einsum("fhpq,qfhe->pfhe", grad_scores_s, back_key, preferred_element_type=jnp.float32)
        * score_scale
    )
    count = lax.axis_size("blk") * patch_dev
    grad_key = (
        jnp.einsum("fhpq,pfhe->qfhe", grad_scores_s, query_s, preferred_element_type=jnp.float32)
        * score_scale
    )
    grad_value = jnp.einsum(
        "fhpq,pfhe->qfhe", back_probs_low, grad_attn_s, preferred_element_type=jnp.float32
    )
    grad_kv = to_low(
        lax.psum_scatter(
            jnp.concatenate(
                [
                    grad_key.reshape(count, frames, model_width),
                    grad_value.reshape(count, frames, model_width),
                ],
                axis=2,
            ).astype(jnp.bfloat16),
            "blk",
            scatter_dimension=0,
            tiled=True,
        ).astype(jnp.float32)
    )
    grad_qkv_s = jnp.concatenate(
        [to_low(grad_query_s).reshape(patch_dev, frames, model_width), grad_kv], axis=2
    ).reshape(token_rows, 3 * model_width)
    grad_sin = left_product(spatial_input, grad_qkv_s)
    grad_spatial_in = right_product(grad_qkv_s, wide_sin).reshape(patch_dev, frames, model_width)
    spatial_pull = jax.vjp(modulate, inputs, shift_one, scale_one)[1]
    back_zero, grad_shift_one, grad_scale_one = spatial_pull(grad_spatial_in)
    grad_input = grad_one + back_zero
    grad_frame_mod = jnp.concatenate(
        [
            grad_shift_one,
            grad_scale_one,
            grad_gate_one,
            grad_shift_two,
            grad_scale_two,
            grad_gate_two,
            grad_shift_three,
            grad_scale_three,
            grad_gate_three,
        ],
        axis=1,
    )
    grad_mod_local = lax.dot_general(
        choose.astype(jnp.float32),
        grad_frame_mod,
        (((0,), (0,)), ((), ())),
        precision=lax.Precision.HIGHEST,
    )
    grad_mod_part, grad_memory_part = (
        lax.psum_scatter(
            grad_mod_local.astype(jnp.bfloat16), "blk", scatter_dimension=1, tiled=True
        ).astype(jnp.float32),
        lax.psum_scatter(
            grad_memory.astype(jnp.bfloat16), "blk", scatter_dimension=1, tiled=True
        ).astype(jnp.float32),
    )
    grad_mod_low = to_low(grad_mod_part)
    grad_ada_w = left_product(conditioning, grad_mod_low)
    grad_ada_b = jnp.sum(grad_mod_low.astype(jnp.float32), axis=0)
    grad_caption = left_product(caption_rows, to_low(grad_memory_part))
    grad_ada_w, grad_ada_b, grad_caption = (
        lax.psum(grad_ada_w.astype(jnp.bfloat16), "seq").astype(jnp.float32),
        lax.psum(grad_ada_b.astype(jnp.bfloat16), "seq").astype(jnp.float32),
        lax.psum(grad_caption.astype(jnp.bfloat16), "seq").astype(jnp.float32),
    )
    shares = (
        lax.psum_scatter(grad_sin, ("seq", "blk"), scatter_dimension=0, tiled=True),
        lax.psum_scatter(grad_sout, ("seq", "blk"), scatter_dimension=0, tiled=True),
        lax.psum_scatter(grad_tin, ("seq", "blk"), scatter_dimension=0, tiled=True),
        lax.psum_scatter(grad_tout, ("seq", "blk"), scatter_dimension=0, tiled=True),
        lax.psum_scatter(grad_gain, ("seq", "blk"), scatter_dimension=0, tiled=True),
        lax.psum_scatter(grad_wquery, ("seq", "blk"), scatter_dimension=0, tiled=True),
        lax.psum_scatter(grad_cout, ("seq", "blk"), scatter_dimension=0, tiled=True),
        lax.psum_scatter(grad_hin, ("seq", "blk"), scatter_dimension=0, tiled=True),
        lax.psum_scatter(grad_hout, ("seq", "blk"), scatter_dimension=0, tiled=True),
    )
    (
        share_sin,
        share_sout,
        share_tin,
        share_tout,
        share_gain,
        share_query,
        share_cout,
        share_hin,
        share_hout,
    ) = shares
    return (
        to_low(result)[None],
        to_low(grad_input)[None],
        grad_ada_w,
        grad_ada_b,
        share_sin,
        share_sout,
        share_tin,
        share_tout,
        share_gain,
        share_query,
        grad_caption,
        share_cout,
        share_hin,
        share_hout,
    )


MESH = pl.DeviceIdType.MESH
BLOCKS = 18
LINES = 8
SHARD = 36
LINE = 4 * SHARD
WINDOW = 48
WIDE = LINES * LINE
MIB = 2**20


def place():
    seq = lax.axis_index("seq")
    blk = lax.axis_index("blk")
    x, c = seq // 2, seq % 2
    z, y = blk // 2, blk % 2
    x1, y1 = x + (1 - 2 * x) * (1 - c), y + (1 - 2 * y) * c
    x2, y2 = x + (1 - 2 * x) * c, y + (1 - 2 * y) * (1 - c)
    return x, c, y, z, x1, y1, x2, y2


def device(x, c, y, z):
    return {"seq": x * 2 + c, "blk": z * 2 + y}


def line_of(c, x, y):
    return (c * 2 + x) * 2 + y


def remote(src, dst, send_sem, recv_sem, where):
    return pltpu.make_async_remote_copy(
        src_ref=src,
        dst_ref=dst,
        send_sem=send_sem,
        recv_sem=recv_sem,
        device_id=where,
        device_id_type=MESH,
    )


def greet(others):
    barrier = pltpu.get_barrier_semaphore()
    for other in others:
        pl.semaphore_signal(barrier, inc=1, device_id=other, device_id_type=MESH)
    pl.semaphore_wait(barrier, len(others))


def left_at(t):
    at = jnp.minimum(t, 4)
    for first in (8, 9, 10, 11, 14, 15):
        at = at + jnp.where(t >= first, 1, 0)
    return at


def right_at(t):
    return jnp.maximum(t - 3, 0)


ROWS = 256
KEYS = 256
TEXT = 288
MOD = 9 * WIDE
MOD_TILES = 11
MOD_WIN = 128 * MOD_TILES
PARTS, HELD, LAST = 4, 4, 8
PAIR = 80
LEFT_SEM, SLOPE_SEM, SAVE_SEMS = 40, 42, 44
TILE = 384
SCALE = E ** (-0.5)


def nt(left, right):
    return lax.dot_general(
        left, right, (((1,), (1,)), ((), ())), preferred_element_type=jnp.float32
    )


def wide32(values):
    return values.astype(jnp.float32)


def loop(count, body):
    def step(index, carry):
        body(index)
        return carry

    lax.fori_loop(0, count, step, 0)


def each_rows(size, body, total=ROWS):
    loop(total // size, lambda i: body(pl.ds(pl.multiple_of(i * size, size), size)))


def each_cols(body):
    loop(WIDE // TILE, lambda i: body(pl.ds(pl.multiple_of(i * TILE, TILE), TILE)))


def swap_rows():
    row = lax.broadcasted_iota(jnp.int32, (ROWS, ROWS), 0)
    col = lax.broadcasted_iota(jnp.int32, (ROWS, ROWS), 1)
    return to_low((((row & 15) << 4) + (row >> 4) == col).astype(jnp.float32))


def head_window(h):
    base = h * E
    start = jnp.minimum(base // 128, 7) * 128
    lane = lax.broadcasted_iota(jnp.int32, (1, 256), 1)
    on = (lane >= base - start) & (lane < base - start + E)
    return pl.ds(pl.multiple_of(start, 128), 256), on.astype(jnp.float32)


def soft(scores, bias, mask):
    scores = scores * SCALE
    if bias is not None:
        scores = scores + bias
    powers = jnp.exp(scores - jnp.max(scores, axis=-1, keepdims=True))
    probs = powers * (1.0 / jnp.sum(powers, axis=-1, keepdims=True))
    return probs if mask is None else probs * mask


def chains(h, groups):
    return [(window, rows, keys) for window in (head_window(h), head_window(h + H // 2)) for rows, keys in groups]


def split_rows(values, jobs):
    start = 0
    parts = []
    for _, rows, _ in jobs:
        size = rows.stop - rows.start
        parts.append(values[start : start + size])
        start += size
    return parts


def heads_forward(h, query, key, value, attn, groups, bias, mask):
    jobs = chains(h, groups)
    scores = [nt(query[rows, lanes] * to_low(on), key[keys, lanes]) for (lanes, on), rows, keys in jobs]
    probs = split_rows(to_low(soft(jnp.concatenate(scores), bias, mask)), jobs)
    parts = [linear(prob, value[keys, lanes]) * on for prob, ((lanes, on), rows, keys) in zip(probs, jobs)]
    for part, ((lanes, on), rows, keys) in zip(parts, jobs):
        attn[rows, lanes] = attn[rows, lanes] + to_low(part)


def text_heads_forward(h, query, key, value, attn, bias, mask):
    jobs = chains(h, VIDEOS)
    scores = [linear(query[rows, lanes] * to_low(on), key[lanes, keys]) for (lanes, on), rows, keys in jobs]
    probs = split_rows(to_low(soft(jnp.concatenate(scores), bias, mask)), jobs)
    parts = [nt(prob, value[lanes, keys]) * on for prob, ((lanes, on), rows, keys) in zip(probs, jobs)]
    for part, ((lanes, on), rows, keys) in zip(parts, jobs):
        attn[rows, lanes] = attn[rows, lanes] + to_low(part)


HALVES = [(slice(0, 128), slice(0, 128)), (slice(128, 256), slice(128, 256))]
VIDEOS = [(slice(0, 144), slice(0, 128)), (slice(112, 256), slice(128, 256))]


def regroup(back):
    row = lax.broadcasted_iota(jnp.int32, (ROWS, ROWS), 0)
    col = lax.broadcasted_iota(jnp.int32, (ROWS, ROWS), 1)
    if back:
        source = (((row >> 3) & 1) << 7) + ((row >> 4) << 3) + (row & 7)
    else:
        source = (((row >> 3) & 15) << 4) + ((row >> 7) << 3) + (row & 7)
    return to_low((source == col).astype(jnp.float32))


def temporal_bias(seg_in, seg_row):
    row = lax.broadcasted_iota(jnp.int32, (128, 128), 0)
    col = lax.broadcasted_iota(jnp.int32, (128, 128), 1)
    allowed = ((row & 7) == (col & 7)) & (seg_in[2, 0:128, 0:1] == seg_row[0:1, 0:128])
    return jnp.where(allowed, 0.0, MASKED)


def cross_bias():
    col = lax.broadcasted_iota(jnp.int32, (1, 128), 1)
    return jnp.where(col < L, 0.0, MASKED)


def cross_rows(seg_in):
    both = [1.0 - seg_in[0, 0:144, 0:1], seg_in[0, 112:256, 0:1]]
    return jnp.concatenate(both + both)


def blk_peers(x, c, b):
    return [device(x, c, (b + k) % 2, ((b + k) % 8) // 2) for k in range(1, 8)]


def forward_kernel(
    spatial_in, spatial_out, temporal_in, temporal_out, cross_query, cross_out, hidden_in, hidden_out,
    tok, gain_one, cond, ada_bias, seg_in, seg_row, pick_in, cot_i, turn_i, ada_i, caption_i, proj_i,
    wide, out, left_o, qkvs_o, qkvt_o, qc_o, mem_o, xhat_o, rstd_o, branch_o, slope_o, gfour_o, cot_o, mods_o, gate_o, gain_o,
    win, pair, far, lines, weights, tokp, cotp, tokf, xin, xp, left, qkvs, qkvt, qc, mem, text, mod, mods, xhat, rstd, branch, branchw, bias,
    stream, attnf, attnp, post, slope, gfour, gains, gain_at, gate,
    src, cot, turn, ada, caption, proj, mod_in, text_in, hidden,
    z_send, z_recv, l_send, l_recv, own_sem, w_sem, t_send, t_recv, a_send, a_recv, m_send, m_recv, x_send, x_recv,
    g_send, g_recv, save_sem, in_sem,
):
    x, c, y, z, x1, y1, x2, y2 = place()
    b = z * 2 + y
    near = [device(x, c, y, (z + k) % 4) for k in (1, 2, 3)]
    beside, across = device(x, c, y, z + 1 - 2 * (z % 2)), device(x, c, y, 3 - z)
    middle = (z == 1) | (z == 2)
    first, second, twin = device(x1, c, y1, z), device(x2, c, y2, z), device(x, 1 - c, y, z)
    peers = blk_peers(x, c, b)
    greet(peers + [device(1 - x, c, y, z), twin])
    mine, line3 = line_of(c, x, y), line_of(c, 1 - x, 1 - y)

    def hops(t, core):
        turn_round = core + (1 - core) * (t % 4 == 2)
        xa, ya = x + (1 - 2 * x) * (1 - turn_round), y + (1 - 2 * y) * turn_round
        xb, yb = x + (1 - 2 * x) * turn_round, y + (1 - 2 * y) * (1 - turn_round)
        return (xa, ya), (xb, yb)

    def z_one(t):
        return remote(src.at[t], win.at[t % PARTS], z_send.at[t, 0], z_recv.at[t, 0], beside)

    def z_two(t):
        return remote(pair.at[t % PARTS], far.at[t % PARTS], z_send.at[t, 1], z_recv.at[t, 1], across)

    def z_three(t):
        return remote(far.at[t % PARTS], far.at[t % PARTS], z_send.at[t, 2], z_recv.at[t, 2], beside)

    def wide_line(t, line):
        return wide.at[t, pl.ds(pl.multiple_of(line * LINE, 16), LINE)]

    def own(t):
        return pltpu.make_async_copy(lines.at[t % HELD], wide_line(t, mine), own_sem.at[t])

    def line_copy(t, to, line, index, where):
        return remote(to, wide_line(t, line), l_send.at[t, index], l_recv.at[t, index], where)

    def sends(t, index):
        (xa, ya), (xb, yb) = hops(t, c)
        one, two = device(xa, c, ya, z), device(xb, c, yb, z)
        line1, line2 = line_of(c, xa, ya), line_of(c, xb, yb)
        line, where = (
            (mine, one), (mine, two), (mine, twin), (line1, two),
            (line1, twin), (line2, twin), (line3, twin),
        )[index]
        from_here = lines.at[t % HELD] if index < 3 else wide_line(t, line)
        return line_copy(t, from_here, line, index, where)

    def arrives(t, line, index):
        line_copy(t, wide_line(t, line), line, index, first).wait_recv()

    def tick(t):
        @pl.when((t >= 4) & (t < BLOCKS + 4))
        def _():
            now = t - 4

            @pl.when(middle)
            def _():
                z_two(now).wait_send()
                z_three(now).wait_send()

            @pl.when(jnp.logical_not(middle))
            def _():
                z_three(now).wait_recv()

            @pl.when(now >= HELD)
            def _():
                for index in range(3):
                    sends(now - HELD, index).wait_send()
                own(now - HELD).wait()

            def line_from(low, high):
                at = now % HELD
                lines[at, 0:64] = low[0:64]
                lines[at, 64:80] = low[64:80] + high[0:16]
                lines[at, 80:144] = high[16:80]

            @pl.when(z < 2)
            def _():
                line_from(pair[now % PARTS], far[now % PARTS])

            @pl.when(z >= 2)
            def _():
                line_from(far[now % PARTS], pair[now % PARTS])

            for index in range(3):
                sends(now, index).start()
            own(now).start()

        @pl.when((t >= 2) & (t < BLOCKS + 2) & middle)
        def _():
            z_two(t - 2).wait_recv()
            z_three(t - 2).start()

        @pl.when((t >= 1) & (t < BLOCKS + 1))
        def _():
            now = t - 1
            z_one(now).wait_recv()

            def pair_from(even, odd):
                at = now % PARTS
                pair[at, 0:32] = even[0:32]
                pair[at, 32:48] = even[32:48] + odd[0:16]
                pair[at, 48:80] = odd[16:48]

            @pl.when(z % 2 == 0)
            def _():
                pair_from(src[now], win[now % PARTS])

            @pl.when(z % 2 == 1)
            def _():
                pair_from(win[now % PARTS], src[now])

            @pl.when(middle)
            def _():
                z_two(now).start()

        @pl.when(t < BLOCKS)
        def _():
            z_one(t).start()

        @pl.when((t >= 6) & (t < BLOCKS + 6))
        def _():
            now = t - 6
            xa, ya = hops(now, c)[0]
            arrives(now, line_of(c, xa, ya), 0)
            for index in (3, 4):
                sends(now, index).start()

        @pl.when(t >= LAST)
        def _():
            now = t - LAST
            xb, yb = hops(now, c)[1]
            arrives(now, line_of(c, xb, yb), 1)
            sends(now, 5).start()
            arrives(now, line3, 3)
            sends(now, 6).start()

    done = [0]

    def pump(until):
        until = min(until, BLOCKS + LAST)
        if until > done[0]:
            start = done[0]
            loop(until - start, lambda i: tick(i + start))
            done[0] = until

    def poke():
        pump(done[0] + 1)

    def load(block):
        pump(block + LAST + 1)
        near_at, far_at = hops(block, 1 - c)
        places = [(x, y), near_at, far_at, (1 - x, 1 - y)]
        for (xl, yl), index in zip(places, (2, 4, 5, 6)):
            arrives(block, line_of(1 - c, xl, yl), index)
        if block >= BLOCKS - HELD:
            own(block).wait()
        copy = pltpu.make_async_copy(wide.at[block], weights.at[block % 2], w_sem.at[block % 2])
        copy.start()
        copy.wait()

    def times(values, block, emit):
        def tile(cols):
            emit(cols, linear(values[...], weights[block % 2, :, cols]))

        each_cols(tile)

    saves = []
    held = {}

    def save(from_ref, to_ref, name=None):
        if name is None:
            name = len(saves)
            saves.append(name)
        held[name] = pltpu.make_async_copy(from_ref, to_ref, save_sem.at[name])
        held[name].start()

    def settle(name):
        if name in held:
            held.pop(name).wait()

    def turned(values, index):
        slot = index % 2
        settle(LEFT_SEM + slot)

        def tile(cols):
            xp[:, cols] = to_low(nt(values[...], turn[cols, :]))
            left[slot, cols, :] = to_low(nt(turn[cols, :], values[...]))

        each_cols(tile)
        save(left.at[slot], left_o.at[index], LEFT_SEM + slot)

    fetches = [
        pltpu.make_async_copy(from_ref, to_ref, in_sem.at[at])
        for at, (from_ref, to_ref) in enumerate(
            ((ada_i, ada), (turn_i, turn), (cot_i, cot), (caption_i, caption), (proj_i, proj))
        )
    ]
    for copy in fetches:
        copy.start()

    def shift(rows, first):
        row = lax.broadcasted_iota(jnp.int32, (WINDOW, rows), 0) - 4 * z
        col = lax.broadcasted_iota(jnp.int32, (WINDOW, rows), 1)
        return to_low(((row >= 0) & (row < SHARD) & (row + first == col)).astype(jnp.float32))

    def window(at, values):
        src[at] = to_low(linear(shift(SHARD, 0), values))

    for j in range(3):
        window(j, spatial_in[:, WIDE * j : WIDE * j + WIDE])
    pump(3)
    window(3, spatial_out[...])
    for j in range(3):
        window(4 + j, temporal_in[:, WIDE * j : WIDE * j + WIDE])
    window(7, temporal_out[...])
    window(8, cross_query[...])
    window(9, cross_out[...])

    def m_copy(k, at):
        return remote(mod_in, mod.at[at], m_send.at[k - 1], m_recv.at[k - 1], peers[k - 1])

    fetches[0].wait()
    part = wide32(to_low(linear(cond[...], ada[...]) + wide32(ada_bias[...])))[0:8]
    part = jnp.concatenate([part, jnp.zeros((8, MOD_WIN - MOD // 8), jnp.float32)], axis=1)
    part = pltpu.roll(part, 16 * b, 1)
    tiles = [part[row : row + 1, 128 * tile : 128 * tile + 128] for row in range(2) for tile in range(MOD_TILES)]
    mod_in[...] = to_low(jnp.concatenate(tiles + [jnp.zeros((32 - 2 * MOD_TILES, 128), jnp.float32)]))
    for k in range(1, 8):
        m_copy(k, b).start()
    mod[b] = mod_in[...]
    swap = swap_rows()
    tokp[...] = to_low(linear(swap, tok[...]))

    def t_copy(k):
        to = (b + k) % 8
        part = tokp.at[pl.ds(pl.multiple_of(32 * to, 32), 32)]
        return remote(part, tokf.at[b], t_send.at[k - 1], t_recv.at[k - 1], peers[k - 1])

    def t_wait(k):
        of = (b + 8 - k) % 8
        remote(tokp.at[pl.ds(0, 32)], tokf.at[of], t_send.at[k - 1], t_recv.at[k - 1], peers[k - 1]).wait_recv()

    for k in range(1, 8):
        t_copy(k).start()
    tokf[b] = tokp[pl.ds(pl.multiple_of(32 * b, 32), 32)]

    def g_copy(at, from_at, to):
        return remote(gains.at[from_at], gain_at.at[at], g_send.at[at], g_recv.at[at], to)

    spread = jnp.concatenate([wide32(gain_one[...]), jnp.zeros((8, WIDE - SHARD), jnp.float32)], axis=1)
    gains[0] = pltpu.roll(spread, SHARD * ((x * 2 + c) * 8 + b), 1)
    g_copy(0, 0, twin).start()
    pump(5)
    fetches[2].wait()
    cotp[...] = to_low(linear(swap, cot[...]))
    save(cotp, cot_o)

    def x_copy(k, at):
        return remote(text_in, text.at[at, y], x_send.at[k - 1], x_recv.at[k - 1], near[k - 1])

    def x_over(at):
        return remote(text.at[:, at], text.at[:, at], x_send.at[3], x_recv.at[3], device(x, c, 1 - y, z))

    for k in range(1, 8):
        m_copy(k, (b + 8 - k) % 8).wait_recv()
    mods[...] = jnp.zeros_like(mods)
    for k in range(8):
        part = wide32(mod[k])
        for row in range(2):
            for tile in range(MOD_TILES):
                lanes = slice(1280 * k + 128 * tile, 1280 * k + 128 * tile + 128)
                at = row * MOD_TILES + tile
                mods[row : row + 1, lanes] = mods[row : row + 1, lanes] + part[at : at + 1]
    save(mods, mods_o)
    g_copy(0, 0, twin).wait_recv()
    gains[1] = gains[0] + gain_at[0]
    g_copy(1, 1, first).start()
    pump(6)
    fetches[3].wait()
    fetches[4].wait()
    text_in[...] = jnp.zeros_like(text_in)
    row = lax.broadcasted_iota(jnp.int32, (TEXT, TEXT), 0)
    col = lax.broadcasted_iota(jnp.int32, (TEXT, TEXT), 1)
    same = to_low((row == col).astype(jnp.float32))
    for v in range(2):
        part = to_low(linear(caption[v], proj[...]))
        text_in[:, 128 * v : 128 * v + L] = to_low(nt(same, part))
    for k in (1, 2, 3):
        x_copy(k, z).start()
    text[z, y] = text_in[...]
    hidden[...] = jnp.zeros_like(hidden)
    rows = lax.broadcasted_iota(jnp.int32, (WIDE, TILE), 0)
    for j in range(4):
        at = 2 * (j % 2) + j // 2
        lanes = slice(256 * at, 256 * at + TILE)
        for k in range(4):
            chosen = to_low((rows == pick_in[4 * k + at : 4 * k + at + 1, :]).astype(jnp.float32))
            part = to_low(linear(hidden_in[:, WIDE * j : WIDE * j + WIDE], chosen))
            hidden[k, 0:SHARD, lanes] = hidden[k, 0:SHARD, lanes] + part
    for k in range(4):
        window(10 + 2 * k, hidden[k, 0:SHARD])
        src[11 + 2 * k] = to_low(linear(shift(4 * SHARD, SHARD * k), hidden_out[...]))
    fetches[1].wait()

    def pick(piece, seg):
        lanes = slice(WIDE * piece, WIDE * piece + WIDE)
        return jnp.where(seg > 0.5, mods[1:2, lanes], mods[0:1, lanes])

    def normal(values, rows, index):
        center = values - jnp.mean(values, axis=-1, keepdims=True)
        factor = lax.rsqrt(jnp.mean(center * center, axis=-1, keepdims=True) + EPSILON)
        scaled = center * factor
        xhat[index, rows, :] = to_low(scaled)
        rstd[index, rows, :] = jnp.broadcast_to(factor, (factor.shape[0], 128))
        return scaled

    for k in range(1, 8):
        t_wait(k)
    g_copy(1, 1, first).wait_recv()
    gains[2] = gains[1] + gain_at[1]
    g_copy(2, 2, second).start()

    def spatial_rows(i):
        seg = jnp.concatenate([seg_in[1, 0:16, 0:1], seg_in[1, 128:144, 0:1]])
        values = wide32(tokf[i])
        center = values - jnp.mean(values, axis=-1, keepdims=True)
        factor = lax.rsqrt(jnp.mean(center * center, axis=-1, keepdims=True) + EPSILON)
        scaled = center * factor
        ready = to_low(scaled * (1.0 + pick(1, seg)) + pick(0, seg))
        low = to_low(scaled)
        spread = jnp.broadcast_to(factor, (32, 128))
        for f in range(2):
            rows = pl.ds(pl.multiple_of(128 * f + 16 * i, 16), 16)
            part = slice(16 * f, 16 * f + 16)
            xhat[0, rows, :] = low[part]
            rstd[0, rows, :] = spread[part]
            xin[rows, :] = ready[part]

    loop(8, spatial_rows)
    save(xhat.at[0], xhat_o.at[0])
    save(rstd.at[0], rstd_o.at[0])
    turned(xin, 10)
    for j in range(3):
        load(j)

        def emit(cols, value, j=j):
            qkvs[j, :, cols] = to_low(value)

        times(xp, j, emit)
    save(qkvs, qkvs_o)
    g_copy(2, 2, second).wait_recv()
    gains[3] = gains[2] + gain_at[2]
    for k in (1, 2, 3):
        remote(gains.at[3], gain_at.at[2 + k], g_send.at[2 + k], g_recv.at[2 + k], near[k - 1]).start()
    for k in (1, 2, 3):
        x_copy(k, (z + 4 - k) % 4).wait_recv()
    x_over(y).start()
    attnf[...] = jnp.zeros_like(attnf)

    def spatial_heads(h):
        heads_forward(h, qkvs.at[0], qkvs.at[1], qkvs.at[2], attnf, HALVES, None, None)

    loop(4, spatial_heads)
    poke()
    loop(4, lambda h: spatial_heads(h + 4))
    for k in (1, 2, 3):
        remote(gains.at[3], gain_at.at[2 + k], g_send.at[2 + k], g_recv.at[2 + k], near[k - 1]).wait_recv()
    gains[0 + 4] = gains[3] + gain_at[3] + gain_at[4] + gain_at[5]
    save(gains.at[4], gain_o)

    def a_copy(k, f):
        to = (b + k) % 8
        part = attnf.at[pl.ds(pl.multiple_of(128 * f + 16 * to, 16), 16)]
        return remote(part, attnp.at[2 * b + f], a_send.at[k - 1, f], a_recv.at[k - 1, f], peers[k - 1])

    def a_wait(k, f):
        of = (b + 8 - k) % 8
        part = attnf.at[pl.ds(0, 16)]
        remote(part, attnp.at[2 * of + f], a_send.at[k - 1, f], a_recv.at[k - 1, f], peers[k - 1]).wait_recv()

    for k in range(1, 8):
        for f in range(2):
            a_copy(k, f).start()
    for f in range(2):
        attnp[2 * b + f] = attnf[pl.ds(pl.multiple_of(128 * f + 16 * b, 16), 16)]
    poke()
    for k in range(1, 8):
        for f in range(2):
            a_wait(k, f)
    xin[...] = attnp[...].reshape(ROWS, WIDE)
    turned(xin, 9)
    load(3)

    def emit_branch(cols, value):
        branchw[:, cols] = value

    times(xp, 3, emit_branch)

    def after_spatial(rows):
        seg = seg_in[0, rows, 0:1]
        value = branchw[rows, :]
        branch[0, rows, :] = to_low(value)
        value = wide32(tokp[rows, :]) + pick(2, seg) * value
        stream[rows, :] = value
        xin[rows, :] = to_low(normal(value, rows, 1) * (1.0 + pick(4, seg)) + pick(3, seg))

    each_rows(32, after_spatial)
    save(branch.at[0], branch_o.at[0])
    save(xhat.at[1], xhat_o.at[1])
    save(rstd.at[1], rstd_o.at[1])

    for k in range(1, 8):
        for f in range(2):
            a_copy(k, f).wait_send()
    attnf[...] = to_low(linear(regroup(False), xin[...]))
    turned(attnf, 8)
    for j in range(3):
        load(4 + j)

        def emit(cols, value, j=j):
            qkvt[j, :, cols] = to_low(value)

        times(xp, 4 + j, emit)
    save(qkvt, qkvt_o)
    attnf[...] = jnp.zeros_like(attnf)

    bias[...] = temporal_bias(seg_in, seg_row)

    def temporal_heads(h):
        heads_forward(
            h, qkvt.at[0], qkvt.at[1], qkvt.at[2], attnf, HALVES, jnp.concatenate([bias[...]] * 4), None
        )

    loop(4, temporal_heads)
    poke()
    loop(4, lambda h: temporal_heads(h + 4))
    xin[...] = to_low(linear(regroup(True), attnf[...]))
    turned(xin, 7)
    load(7)
    times(xp, 7, emit_branch)

    def after_temporal(rows):
        seg = seg_in[0, rows, 0:1]
        value = branchw[rows, :]
        branch[1, rows, :] = to_low(value)
        value = stream[rows, :] + pick(5, seg) * value
        stream[rows, :] = value
        xin[rows, :] = to_low(normal(value, rows, 2) * gains[4, 0:1, :])

    each_rows(32, after_temporal)
    save(branch.at[1], branch_o.at[1])
    save(xhat.at[2], xhat_o.at[2])
    save(rstd.at[2], rstd_o.at[2])

    turned(xin, 6)
    load(8)

    def emit_query(cols, value):
        qc[:, cols] = to_low(value)

    times(xp, 8, emit_query)
    save(qc, qc_o)
    x_over(1 - y).wait_recv()
    for k in range(8):
        mem[k // 4, TEXT * (k % 4) : TEXT * (k % 4) + TEXT, :] = text[k // 2, k % 2]
    save(mem, mem_o)
    attnf[...] = jnp.zeros_like(attnf)

    def cross_heads(h):
        text_heads_forward(h, qc, mem.at[0], mem.at[1], attnf, cross_bias(), cross_rows(seg_in))

    loop(4, cross_heads)
    poke()
    loop(4, lambda h: cross_heads(h + 4))
    xin[...] = attnf[...]
    turned(xin, 5)
    load(9)
    times(xp, 9, emit_branch)

    def after_cross(rows):
        seg = seg_in[0, rows, 0:1]
        value = stream[rows, :] + branchw[rows, :]
        stream[rows, :] = value
        xin[rows, :] = to_low(normal(value, rows, 3) * (1.0 + pick(7, seg)) + pick(6, seg))
        gfour[rows, :] = to_low(wide32(cotp[rows, :]) * pick(8, seg))

    each_rows(32, after_cross)
    save(xhat.at[3], xhat_o.at[3])
    save(rstd.at[3], rstd_o.at[3])
    save(gfour, gfour_o)

    turned(xin, 4)
    same = (
        lax.broadcasted_iota(jnp.int32, (TILE, TILE), 0) == lax.broadcasted_iota(jnp.int32, (TILE, TILE), 1)
    ).astype(jnp.float32).astype(jnp.bfloat16)
    for k in range(4):
        slot = k % 2
        load(10 + 2 * k)
        settle(SLOPE_SEM + slot)
        settle(LEFT_SEM + slot)

        def emit_hidden(cols, value, slot=slot):
            inner = math.sqrt(2.0 / math.pi) * (value + 0.044715 * value * value * value)
            bent = jnp.tanh(inner)
            half = 0.5 * (1.0 + bent)
            tilt = math.sqrt(2.0 / math.pi) * (1.0 + 3 * 0.044715 * value * value)
            slope[slot, :, cols] = to_low(half + 0.5 * value * (1.0 - bent * bent) * tilt)
            low = to_low(value * half)
            post[:, cols] = low
            left[slot, cols, :] = to_low(nt(same, low))

        times(xp, 10 + 2 * k, emit_hidden)
        save(slope.at[slot], slope_o.at[k], SLOPE_SEM + slot)
        save(left.at[slot], left_o.at[k], LEFT_SEM + slot)
        load(11 + 2 * k)

        def emit_out(cols, value, k=k):
            branchw[:, cols] = value if k == 0 else branchw[:, cols] + value

        times(post, 11 + 2 * k, emit_out)

    gate[...] = jnp.zeros_like(gate)

    def last(rows):
        seg = seg_in[0, rows, 0:1]
        value = branchw[rows, :]
        xin[rows, :] = to_low(stream[rows, :] + pick(8, seg) * value)
        value = wide32(cotp[rows, :]) * value
        later = jnp.sum(value * seg, axis=0, keepdims=True)
        every = jnp.sum(value, axis=0, keepdims=True)
        gate[0:1, :] = gate[0:1, :] + (every - later)
        gate[1:2, :] = gate[1:2, :] + later

    each_rows(32, last)
    save(gate, gate_o)
    out[...] = to_low(linear(swap_rows(), xin[...]))

    for copy in held.values():
        copy.wait()
    for k in range(1, 8):
        t_copy(k).wait_send()
        m_copy(k, b).wait_send()
    for k in (1, 2, 3):
        x_copy(k, z).wait_send()
    x_over(y).wait_send()
    for at, to in ((0, twin), (1, first), (2, second)):
        g_copy(at, at, to).wait_send()
    for k in (1, 2, 3):
        remote(gains.at[3], gain_at.at[2 + k], g_send.at[2 + k], g_recv.at[2 + k], near[k - 1]).wait_send()

    for t in range(BLOCKS - HELD, BLOCKS):
        for index in range(3):
            sends(t, index).wait_send()

    def finish(t):
        z_one(t).wait_send()
        for index in range(3, 7):
            sends(t, index).wait_send()

    loop(BLOCKS, finish)


ANY = pl.BlockSpec(memory_space=pl.ANY)
IN_VMEM = pl.BlockSpec(memory_space=pltpu.VMEM)


def forward(*operands):
    low, full = jnp.bfloat16, jnp.float32
    dma = pltpu.SemaphoreType.DMA
    hbm = [
        ((BLOCKS, WIDE, WIDE), low),
        ((ROWS, WIDE), low),
        ((11, WIDE, ROWS), low),
        ((3, ROWS, WIDE), low),
        ((3, ROWS, WIDE), low),
        ((ROWS, WIDE), low),
        ((2, WIDE, KEYS), low),
        ((4, ROWS, WIDE), low),
        ((4, ROWS, 128), full),
        ((2, ROWS, WIDE), low),
        ((4, ROWS, WIDE), low),
        ((ROWS, WIDE), low),
        ((ROWS, WIDE), low),
        ((8, MOD), full),
        ((8, WIDE), full),
        ((8, WIDE), full),
    ]
    vmem = [
        ((PARTS, WINDOW, WIDE), low),
        ((PARTS, PAIR, WIDE), low),
        ((PARTS, PAIR, WIDE), low),
        ((HELD, LINE, WIDE), low),
        ((2, WIDE, WIDE), low),
        ((ROWS, WIDE), low),
        ((ROWS, WIDE), low),
        ((8, 32, WIDE), low),
        ((ROWS, WIDE), low),
        ((ROWS, WIDE), low),
        ((2, WIDE, ROWS), low),
        ((3, ROWS, WIDE), low),
        ((3, ROWS, WIDE), low),
        ((ROWS, WIDE), low),
        ((2, WIDE, KEYS), low),
        ((4, 2, TEXT, KEYS), low),
        ((8, 32, 128), low),
        ((8, MOD), full),
        ((4, ROWS, WIDE), low),
        ((4, ROWS, 128), full),
        ((2, ROWS, WIDE), low),
        ((ROWS, WIDE), full),
        ((128, 128), full),
        ((ROWS, WIDE), full),
        ((ROWS, WIDE), low),
        ((16, 16, WIDE), low),
        ((ROWS, WIDE), low),
        ((2, ROWS, WIDE), low),
        ((ROWS, WIDE), low),
        ((5, 8, WIDE), full),
        ((6, 8, WIDE), full),
        ((8, WIDE), full),
        ((BLOCKS, WINDOW, WIDE), low),
        ((ROWS, WIDE), low),
        ((WIDE, WIDE), low),
        ((WIDE, MOD // 8), low),
        ((2, L, 4096), low),
        ((4096, TEXT), low),
        ((32, 128), low),
        ((TEXT, KEYS), low),
        ((4, WINDOW, WIDE), low),
    ]
    return pl.pallas_call(
        forward_kernel,
        out_shape=[jax.ShapeDtypeStruct(*shape) for shape in hbm],
        in_specs=[IN_VMEM] * 15 + [ANY] * 5,
        out_specs=[ANY, IN_VMEM] + [ANY] * 14,
        scratch_shapes=[pltpu.VMEM(*shape) for shape in vmem]
        + [
            dma((BLOCKS, 3)), dma((BLOCKS, 3)), dma((BLOCKS, 7)), dma((BLOCKS, 7)), dma((BLOCKS,)), dma((2,)),
            dma((7,)), dma((7,)), dma((7, 2)), dma((7, 2)), dma((7,)), dma((7,)), dma((4,)), dma((4,)),
            dma((6,)), dma((6,)), dma((SAVE_SEMS,)), dma((5,)),
        ],
        compiler_params=pltpu.CompilerParams(
            collective_id=0, has_side_effects=True, vmem_limit_bytes=60 * MIB
        ),
        name="forward",
    )(*operands)


def tn(left, right):
    return lax.dot_general(
        left, right, (((0,), (0,)), ((), ())), preferred_element_type=jnp.float32
    )


def text_heads_backward(h, query, key, value, grad, dquery, dkey, dvalue, bias, mask):
    jobs = chains(h, VIDEOS)
    scores, grads = [], []
    for (lanes, on), rows, keys in jobs:
        low_on = to_low(on)
        scores.append(linear(query[rows, lanes] * low_on, key[lanes, keys]))
        grads.append(linear(grad[rows, lanes] * low_on, value[lanes, keys]))
    probs = soft(jnp.concatenate(scores), bias, mask)
    grad_probs = jnp.concatenate(grads)
    delta = jnp.sum(grad_probs * probs, axis=-1, keepdims=True)
    slopes = split_rows(to_low(probs * (grad_probs - delta)), jobs)
    probs = split_rows(to_low(probs), jobs)
    parts = []
    for slope, prob, ((lanes, on), rows, keys) in zip(slopes, probs, jobs):
        low_on = to_low(on)
        parts.append(
            (
                to_low(nt(slope, key[lanes, keys]) * (on * SCALE)),
                to_low(tn(query[rows, lanes] * low_on, slope) * SCALE),
                to_low(tn(grad[rows, lanes] * low_on, prob)),
            )
        )
    for (by_query, by_key, by_value), ((lanes, on), rows, keys) in zip(parts, jobs):
        dquery[rows, lanes] = dquery[rows, lanes] + by_query
        dkey[lanes, keys] = dkey[lanes, keys] + by_key
        dvalue[lanes, keys] = dvalue[lanes, keys] + by_value


def heads_backward(h, query, key, value, grad, dquery, dkey, dvalue, groups, bias, mask):
    jobs = chains(h, groups)
    scores, grads = [], []
    for (lanes, on), rows, keys in jobs:
        low_on = to_low(on)
        scores.append(nt(query[rows, lanes] * low_on, key[keys, lanes]))
        grads.append(nt(grad[rows, lanes] * low_on, value[keys, lanes]))
    probs = soft(jnp.concatenate(scores), bias, mask)
    grad_probs = jnp.concatenate(grads)
    delta = jnp.sum(grad_probs * probs, axis=-1, keepdims=True)
    slopes = split_rows(to_low(probs * (grad_probs - delta)), jobs)
    probs = split_rows(to_low(probs), jobs)
    parts = []
    for slope, prob, ((lanes, on), rows, keys) in zip(slopes, probs, jobs):
        parts.append(
            (
                to_low(linear(slope, key[keys, lanes]) * (on * SCALE)),
                to_low(tn(slope, query[rows, lanes]) * (on * SCALE)),
                to_low(tn(prob, grad[rows, lanes]) * on),
            )
        )
    for (by_query, by_key, by_value), ((lanes, on), rows, keys) in zip(parts, jobs):
        dquery[rows, lanes] = dquery[rows, lanes] + by_query
        dkey[keys, lanes] = dkey[keys, lanes] + by_key
        dvalue[keys, lanes] = dvalue[keys, lanes] + by_value


def backward_kernel(
    wide, left_i, qkvs_i, qkvt_i, qc_i, mem_i, xhat_i, rstd_i, branch_i, slope_i, gfour_i, cot_i, mods_i, gate_i, gain_i,
    seg_in, seg_row, turn, cond_in,
    total, gtok, gain_o, text_o, mod_o,
    weights, left, right, qkv, xhat, rstd, branch, slope, mods, gain, bias, stream, work, grad, xin, gm, mem, dmem, text, texts, text_at, mod_out, mod,
    seqs, gains, gain_at, gframe, back, backp,
    s0, r0, s1, r1, s2, r2, k2, s3, pass_in, pass_out, far_in, close, close_in, share,
    in_sem, w_sem, s0_sem, r0_sem, s1_sem, r1_sem, s2_sem, r2_sem, z_send, z_recv, share_sem,
    a_send, a_recv, u_send, u_recv, x_send, x_recv, m_send, m_recv, q_send, q_recv, g_send, g_recv,
):
    x, c, y, z, x1, y1, x2, y2 = place()
    b = z * 2 + y
    near = [device(x, c, y, (z + k) % 4) for k in (1, 2, 3)]
    first, second, twin = device(x1, c, y1, z), device(x2, c, y2, z), device(x, 1 - c, y, z)
    peers = blk_peers(x, c, b)
    across = [twin, device(1 - x, c, y, z), device(1 - x, 1 - c, y, z)]
    greet(peers + across)

    fetches = {}

    def fetch(name, from_ref, to_ref):
        fetches[name] = pltpu.make_async_copy(from_ref, to_ref, in_sem.at[name])
        fetches[name].start()

    def have(name):
        if name in fetches:
            fetches.pop(name).wait()

    fetch(0, gfour_i, right.at[0])
    for k in range(11):
        fetch(1 + k, left_i.at[k], left.at[k])
    fetch(12, mods_i, mods)
    fetch(13, gain_i, gain)
    fetch(14, slope_i.at[0], slope.at[0])
    fetch(15, slope_i.at[1], slope.at[1])
    fetch(16, xhat_i.at[3], xhat.at[1])
    fetch(17, rstd_i.at[3], rstd.at[1])
    fetch(18, cot_i, xin)
    fetch(19, gate_i, work.at[0:8])

    def weight(block):
        slot = WEIGHT_ORDER.index(block) % 2
        return weights.at[slot]

    def prefetch(at):
        if at < len(WEIGHT_ORDER):
            copy = pltpu.make_async_copy(wide.at[WEIGHT_ORDER[at]], weights.at[at % 2], w_sem.at[at % 2])
            copy.start()
            fetches["w", WEIGHT_ORDER[at]] = copy

    def release(block):
        prefetch(WEIGHT_ORDER.index(block) + 2)

    prefetch(0)
    prefetch(1)

    away = [(1 - x) * 2 + 1 - y, x2 * 2 + y2]
    stay = [x1 * 2 + y1, x * 2 + y]

    def product(t, core, xl):
        rows = pl.ds(pl.multiple_of(line_of(core, xl, 0) * LINE, 16), 2 * LINE)
        return linear(left[left_at(t), rows, :], right[right_at(t)])

    def copy0(t, l):
        pair = pl.ds(2 * l, 2)
        return remote(s0.at[t % 2, pair], r0.at[t % 4, pair], s0_sem.at[t % 2, l], r0_sem.at[t % 4, l], twin)

    def copy1(t, l):
        return remote(s1.at[t % 2, away[l]], r1.at[t % 4, l], s1_sem.at[t % 2, l], r1_sem.at[t % 4, l], second)

    def copy2(t):
        return remote(s2.at[t % 2], r2.at[t % 4], s2_sem.at[t % 2], r2_sem.at[t % 4], first)

    beside, opposite = device(x, c, y, z + 1 - 2 * (z % 2)), device(x, c, y, 3 - z)
    middle = (z == 1) | (z == 2)
    near_rows = pl.ds(pl.multiple_of(64 * (z // 2), 16), PAIR)
    far_rows = pl.ds(pl.multiple_of(64 - 64 * (z // 2), 16), PAIR)
    own_rows = pl.ds(pl.multiple_of(32 * (z % 2), 16), WINDOW)
    beside_rows = pl.ds(pl.multiple_of(32 - 32 * (z % 2), 16), WINDOW)

    def z_one(t):
        return remote(s3.at[t % 4, far_rows], pass_in.at[t % 4], z_send.at[0, t % 4], z_recv.at[0, t % 4], beside)

    def z_two(t):
        return remote(pass_out.at[t % 2], far_in.at[t % 4], z_send.at[1, t % 4], z_recv.at[1, t % 4], opposite)

    def z_three(t):
        return remote(
            close.at[t % 2, beside_rows], close_in.at[t % 4], z_send.at[2, t % 4], z_recv.at[2, t % 4], beside
        )

    def share_copy(t):
        return pltpu.make_async_copy(share.at[t % 2], total.at[t], share_sem.at[t % 2])

    def tick(t):
        @pl.when(t >= 10)
        def _():
            now = t - 10
            z_three(now).wait_recv()
            value = wide32(close[now % 2, own_rows]) + wide32(close_in[now % 4])

            @pl.when(jnp.logical_not(middle))
            def _():
                z_one(now).wait_send()

            @pl.when(now >= 2)
            def _():
                share_copy(now - 2).wait()
            share[now % 2] = value
            share_copy(now).start()

        @pl.when((t >= 8) & (t < BLOCKS + 8))
        def _():
            now = t - 8

            @pl.when(now >= 2)
            def _():
                z_three(now - 2).wait_send()

            @pl.when(middle)
            def _():
                z_two(now).wait_recv()
                close[now % 2] = to_low(wide32(s3[now % 4, near_rows]) + wide32(far_in[now % 4]))

            @pl.when(jnp.logical_not(middle))
            def _():
                close[now % 2] = s3[now % 4, near_rows]

            z_three(now).start()

        @pl.when((t >= 7) & (t < BLOCKS + 7) & middle)
        def _():
            now = t - 7
            z_one(now).wait_recv()

            @pl.when(now >= 2)
            def _():
                z_two(now - 2).wait_send()
            pass_out[now % 2] = to_low(wide32(s3[now % 4, far_rows]) + wide32(pass_in[now % 4]))
            z_two(now).start()

        @pl.when((t >= 6) & (t < BLOCKS + 6))
        def _():
            now = t - 6
            copy2(now).wait_recv()
            s3[now % 4] = to_low(k2[now % 2] + wide32(r2[now % 4]))

            @pl.when(jnp.logical_not(middle))
            def _():
                z_one(now).start()

        @pl.when((t >= 4) & (t < BLOCKS + 4))
        def _():
            now = t - 4
            copy1(now, 0).wait_recv()

            @pl.when(now >= 2)
            def _():
                copy2(now - 2).wait_send()
            s2[now % 2] = to_low(wide32(s1[now % 2, stay[0]]) + wide32(r1[now % 4, 0]))
            copy2(now).start()
            copy1(now, 1).wait_recv()
            k2[now % 2] = wide32(s1[now % 2, stay[1]]) + wide32(r1[now % 4, 1])

        @pl.when((t >= 2) & (t < BLOCKS + 2))
        def _():
            now = t - 2

            @pl.when(now >= 2)
            def _():
                for l in range(2):
                    copy1(now - 2, l).wait_send()
            for l in range(2):
                copy0(now, l).wait_recv()
                value = product(now, c, l)
                for part in range(2):
                    line = 2 * l + part
                    summed = value[part * LINE : part * LINE + LINE] + wide32(r0[now % 4, line])
                    s1[now % 2, line] = to_low(summed)
            for l in range(2):
                copy1(now, l).start()

        @pl.when(t < BLOCKS)
        def _():
            for l in range(2):
                @pl.when(t >= 2)
                def _():
                    copy0(t - 2, l).wait_send()
                value = to_low(product(t, 1 - c, l))
                s0[t % 2, 2 * l] = value[:LINE]
                s0[t % 2, 2 * l + 1] = value[LINE:]
                copy0(t, l).start()

    done = [0]

    def pump(until):
        if until > done[0]:
            start = done[0]
            loop(until - start, lambda i: tick(i + start))
            done[0] = until

    def pick(piece, seg):
        lanes = slice(WIDE * piece, WIDE * piece + WIDE)
        return jnp.where(seg > 0.5, mods[1:2, lanes], mods[0:1, lanes])

    def by_video(piece, value, seg):
        lanes = slice(WIDE * piece, WIDE * piece + WIDE)
        later = jnp.sum(value * seg, axis=0, keepdims=True)
        every = jnp.sum(value, axis=0, keepdims=True)
        gm[0:1, lanes] = gm[0:1, lanes] + (every - later)
        gm[1:2, lanes] = gm[1:2, lanes] + later

    def through(values_at, blocks, emit, grouped=False):
        for n, (values, block) in enumerate(zip(values_at, blocks)):
            have(("w", block))

            def tile(cols, n=n, values=values, block=block):
                part = nt(values[...], weight(block)[cols, :])
                if n > 0:
                    part = part + work[:, cols]
                if n == len(blocks) - 1:
                    xin[:, cols] = to_low(part)
                else:
                    work[:, cols] = part

            each_cols(tile)
            release(block)
        if grouped:
            xin[...] = to_low(linear(regroup(True), xin[...]))
        turn_back(emit)

    def turn_back(emit):
        each_cols(lambda cols: emit(cols, linear(xin[...], turn[:, cols])))

    def emit_work(cols, value):
        work[:, cols] = value

    def emit_grad(cols, value):
        grad[:, cols] = to_low(value)

    def norm_back(grad_in, tilt, at, rows):
        slope_in = grad_in * tilt
        hat = wide32(xhat[at, rows, :])
        first_mean = jnp.mean(slope_in, axis=-1, keepdims=True)
        second_mean = jnp.mean(slope_in * hat, axis=-1, keepdims=True)
        return rstd[at, rows, 0:1] * (slope_in - first_mean - hat * second_mean)

    gm[...] = jnp.zeros_like(gm)
    have(0)
    have(12)
    have(18)
    have(19)
    gm[0:8, 8 * WIDE : 9 * WIDE] = work[0:8]
    stream[...] = wide32(xin[...])
    for k in range(5):
        have(1 + k)
    pump(2)
    for k in range(4):
        have(14 + k % 2 if k < 2 else ("slope", k))
        have(("w", 11 + 2 * k))

        def tile(cols, k=k):
            value = nt(right[0], weight(11 + 2 * k)[cols, :]) * wide32(slope[k % 2, :, cols])
            right[1 + k, :, cols] = to_low(value)

        each_cols(tile)
        release(11 + 2 * k)
        if k < 2:
            copy = pltpu.make_async_copy(slope_i.at[k + 2], slope.at[k % 2], in_sem.at[14 + k])
            copy.start()
            fetches["slope", k + 2] = copy
        have(("w", 10 + 2 * k))

        def tile(cols, k=k):
            part = nt(right[1 + k], weight(10 + 2 * k)[cols, :])
            if k > 0:
                part = part + work[:, cols]
            if k < 3:
                work[:, cols] = part
            else:
                xin[:, cols] = to_low(part)

        each_cols(tile)
        release(10 + 2 * k)
        pump(k + 3)
    turn_back(emit_work)
    for k in range(5, 11):
        have(1 + k)
    have(16)
    have(17)
    fetch(20, qc_i, qkv.at[0])
    fetch(21, mem_i.at[0], mem.at[0])
    fetch(22, mem_i.at[1], mem.at[1])
    fetch(23, xhat_i.at[2], xhat.at[0])
    fetch(24, rstd_i.at[2], rstd.at[0])

    def after_mlp(rows):
        seg = seg_in[0, rows, 0:1]
        value = work[rows, :]
        by_video(6, value, seg)
        by_video(7, value * wide32(xhat[1, rows, :]), seg)
        value = stream[rows, :] + norm_back(value, 1.0 + pick(7, seg), 1, rows)
        stream[rows, :] = value
        right[5, rows, :] = to_low(value)

    each_rows(32, after_mlp)

    fetch(25, xhat_i.at[1], xhat.at[1])
    fetch(26, rstd_i.at[1], rstd.at[1])
    through([right.at[5]], [9], emit_grad)
    right[6] = jnp.zeros_like(right[6])
    dmem[...] = jnp.zeros_like(dmem)
    for name in (13, 20, 21, 22, 23, 24):
        have(name)

    def cross_heads(h):
        text_heads_backward(
            h, qkv.at[0], mem.at[0], mem.at[1], grad, right.at[6], dmem.at[0], dmem.at[1],
            cross_bias(), cross_rows(seg_in),
        )

    for part in range(4):
        loop(2, lambda h: cross_heads(h + 2 * part))
        pump(7 + (part + 1) // 2)

    def dmem_part(zp, yp):
        return dmem.at[zp // 2, pl.ds(pl.multiple_of(TEXT * (zp % 2 * 2 + yp), 16), TEXT)]

    def x_over(zp):
        return remote(dmem_part(zp, 1 - y), text.at[zp], x_send.at[zp], x_recv.at[zp], device(x, c, 1 - y, z))

    def x_copy(k):
        return remote(texts.at[(z + k) % 4], text_at.at[k - 1], x_send.at[3 + k], x_recv.at[3 + k], near[k - 1])

    for zp in range(4):
        x_over(zp).start()
    fetch(27, qkvt_i.at[0], qkv.at[0])
    fetch(28, qkvt_i.at[1], qkv.at[1])
    fetch(29, qkvt_i.at[2], qkv.at[2])
    fetch(30, branch_i.at[1], branch)
    through([right.at[6]], [8], emit_work)
    gains[0] = jnp.zeros_like(gains[0])
    have(30)

    def after_cross(rows):
        seg = seg_in[0, rows, 0:1]
        value = work[rows, :]
        gains[0, 0:1, :] = gains[0, 0:1, :] + jnp.sum(value * wide32(xhat[0, rows, :]), axis=0, keepdims=True)
        value = stream[rows, :] + norm_back(value, gain[0:1, :], 0, rows)
        stream[rows, :] = value
        by_video(5, value * wide32(branch[rows, :]), seg)
        right[7, rows, :] = to_low(value * pick(5, seg))

    each_rows(32, after_cross)

    def g_copy(at, to):
        return remote(gains.at[min(at, 3)], gain_at.at[at], g_send.at[at], g_recv.at[at], to)

    g_copy(0, twin).start()
    fetch(31, branch_i.at[0], branch)
    fetch(32, xhat_i.at[0], xhat.at[0])
    fetch(33, rstd_i.at[0], rstd.at[0])
    pump(10)

    through([right.at[7]], [7], emit_grad)
    grad[...] = to_low(linear(regroup(False), grad[...]))
    bias[...] = temporal_bias(seg_in, seg_row)
    for j in range(3):
        right[8 + j] = jnp.zeros_like(right[8 + j])
    for name in (25, 26, 27, 28, 29):
        have(name)

    def temporal_heads(h):
        heads_backward(
            h, qkv.at[0], qkv.at[1], qkv.at[2], grad, right.at[8], right.at[9], right.at[10],
            HALVES, jnp.concatenate([bias[...]] * 4), None,
        )

    loop(4, temporal_heads)
    pump(11)
    g_copy(0, twin).wait_recv()
    gains[1] = gains[0] + gain_at[0]
    g_copy(1, first).start()
    loop(4, lambda h: temporal_heads(h + 4))
    pump(12)
    g_copy(1, first).wait_recv()
    gains[2] = gains[1] + gain_at[1]
    g_copy(2, second).start()
    for zp in range(4):
        x_over(zp).wait_recv()
        texts[zp] = to_low(wide32(dmem_part(zp, y)[...]) + wide32(text[zp]))
    for k in (1, 2, 3):
        x_copy(k).start()
    for j in range(3):
        fetch(34 + j, qkvs_i.at[j], qkv.at[j])
    through([right.at[8], right.at[9], right.at[10]], [4, 5, 6], emit_work, True)
    have(31)

    def after_temporal(rows):
        seg = seg_in[0, rows, 0:1]
        value = work[rows, :]
        by_video(3, value, seg)
        by_video(4, value * wide32(xhat[1, rows, :]), seg)
        value = stream[rows, :] + norm_back(value, 1.0 + pick(4, seg), 1, rows)
        stream[rows, :] = value
        by_video(2, value * wide32(branch[rows, :]), seg)
        right[11, rows, :] = to_low(value * pick(2, seg))

    each_rows(32, after_temporal)

    through([right.at[11]], [3], emit_grad)

    def a_copy(k):
        to = (b + k) % 8
        part = grad.at[pl.ds(pl.multiple_of(32 * to, 32), 32)]
        return remote(part, back.at[b], a_send.at[k - 1], a_recv.at[k - 1], peers[k - 1])

    def a_wait(k):
        of = (b + 8 - k) % 8
        remote(grad.at[pl.ds(0, 32)], back.at[of], a_send.at[k - 1], a_recv.at[k - 1], peers[k - 1]).wait_recv()

    for k in (1, 2, 3):
        x_copy(k).wait_recv()
    text_o[...] = to_low(wide32(texts[z]) + wide32(text_at[0]) + wide32(text_at[1]) + wide32(text_at[2]))
    for k in range(1, 8):
        a_copy(k).start()
    back[b] = grad[pl.ds(pl.multiple_of(32 * b, 32), 32)]
    pump(13)
    g_copy(2, second).wait_recv()
    gains[3] = gains[2] + gain_at[2]
    for k in (1, 2, 3):
        g_copy(2 + k, near[k - 1]).start()
    for j in range(3):
        right[12 + j] = jnp.zeros_like(right[12 + j])
    for name in (32, 33, 34, 35, 36):
        have(name)
    for k in range(1, 8):
        a_wait(k)
    for k in range(8):
        for f in range(2):
            gframe[128 * f + 16 * k : 128 * f + 16 * k + 16, :] = back[k, 16 * f : 16 * f + 16, :]

    def spatial_heads(h):
        heads_backward(
            h, qkv.at[0], qkv.at[1], qkv.at[2], gframe, right.at[12], right.at[13], right.at[14], HALVES, None, None
        )

    loop(4, spatial_heads)
    pump(14)
    loop(4, lambda h: spatial_heads(h + 4))
    pump(15)
    through([right.at[12], right.at[13], right.at[14]], [0, 1, 2], emit_work)
    pump(16)
    for k in range(1, 8):
        a_copy(k).wait_send()

    def after_spatial(i):
        rows = pl.ds(pl.multiple_of(16 * i, 16), 16)
        seg = seg_in[1, rows, 0:1]
        value = work[rows, :]
        by_video(0, value, seg)
        by_video(1, value * wide32(xhat[0, rows, :]), seg)
        value = to_low(norm_back(value, 1.0 + pick(1, seg), 0, rows))
        back[i % 8, pl.ds(pl.multiple_of(16 * (i // 8), 16), 16), :] = value

    loop(16, after_spatial)

    def u_copy(k):
        to = (b + k) % 8
        return remote(back.at[to], backp.at[b], u_send.at[k - 1], u_recv.at[k - 1], peers[k - 1])

    def u_wait(k):
        of = (b + 8 - k) % 8
        remote(back.at[0], backp.at[of], u_send.at[k - 1], u_recv.at[k - 1], peers[k - 1]).wait_recv()

    def m_copy(k):
        to = (b + k) % 8
        return remote(mod_out.at[to], mod.at[b], m_send.at[k - 1], m_recv.at[k - 1], peers[k - 1])

    def m_wait(k):
        of = (b + 8 - k) % 8
        remote(mod_out.at[0], mod.at[of], m_send.at[k - 1], m_recv.at[k - 1], peers[k - 1]).wait_recv()

    for k in range(1, 8):
        u_copy(k).start()
    backp[b] = back[b]
    for k in range(8):
        tiles = [
            gm[row : row + 1, 1280 * k + 128 * tile : 1280 * k + 128 * tile + 128]
            for row in range(2)
            for tile in range(MOD_TILES)
        ]
        mod_out[k] = to_low(jnp.concatenate(tiles + [jnp.zeros((32 - 2 * MOD_TILES, 128), jnp.float32)]))
    for k in range(1, 8):
        m_copy(k).start()
    mod[b] = mod_out[b]
    pump(18)
    for k in range(1, 8):
        m_wait(k)
    summed = wide32(mod[0])
    for k in range(1, 8):
        summed = summed + wide32(mod[k])
    own = x * 2 + c
    seqs[own, 0:32] = to_low(summed)
    seqs[own, 32:64] = cond_in[...]
    places = [x * 2 + 1 - c, (1 - x) * 2 + c, (1 - x) * 2 + 1 - c]

    def q_copy(k, at):
        return remote(seqs.at[own], seqs.at[at], q_send.at[k], q_recv.at[k], across[k])

    for k in range(3):
        q_copy(k, own).start()
    for k in range(1, 8):
        u_wait(k)
    xin[...] = to_low(stream[...] + wide32(backp[...].reshape(ROWS, WIDE)))
    gtok[...] = to_low(linear(swap_rows(), xin[...]))
    for k in (1, 2, 3):
        g_copy(2 + k, near[k - 1]).wait_recv()
    gain_o[...] = gains[3] + gain_at[3] + gain_at[4] + gain_at[5]
    pump(BLOCKS + 10)
    for k in range(3):
        q_copy(k, places[k]).wait_recv()
    mod_o[...] = seqs[...]

    for now in (BLOCKS - 2, BLOCKS - 1):
        for l in range(2):
            copy0(now, l).wait_send()
            copy1(now, l).wait_send()
        copy2(now).wait_send()
        z_three(now).wait_send()
        share_copy(now).wait()

        @pl.when(middle)
        def _(now=now):
            z_two(now).wait_send()

    for k in range(1, 8):
        u_copy(k).wait_send()
        m_copy(k).wait_send()
        x_over(k - 1).wait_send() if k < 5 else x_copy(k - 4).wait_send()
    for k in range(3):
        q_copy(k, own).wait_send()
    for at, to in enumerate([twin, first, second] + near):
        g_copy(at, to).wait_send()


WEIGHT_ORDER = (11, 10, 13, 12, 15, 14, 17, 16, 9, 8, 7, 4, 5, 6, 3, 0, 1, 2)


def backward(*operands):
    low, full = jnp.bfloat16, jnp.float32
    dma = pltpu.SemaphoreType.DMA
    outs = [
        ((BLOCKS, WINDOW, WIDE), full),
        ((ROWS, WIDE), low),
        ((8, WIDE), full),
        ((TEXT, KEYS), low),
        ((4, 64, 128), low),
    ]
    vmem = [
        ((2, WIDE, WIDE), low),
        ((11, WIDE, ROWS), low),
        ((15, ROWS, WIDE), low),
        ((3, ROWS, WIDE), low),
        ((2, ROWS, WIDE), low),
        ((2, ROWS, 128), full),
        ((ROWS, WIDE), low),
        ((2, ROWS, WIDE), low),
        ((8, MOD), full),
        ((8, WIDE), full),
        ((128, 128), full),
        ((ROWS, WIDE), full),
        ((ROWS, WIDE), full),
        ((ROWS, WIDE), low),
        ((ROWS, WIDE), low),
        ((8, MOD), full),
        ((2, WIDE, KEYS), low),
        ((2, WIDE, KEYS), low),
        ((4, TEXT, KEYS), low),
        ((4, TEXT, KEYS), low),
        ((3, TEXT, KEYS), low),
        ((8, 32, 128), low),
        ((8, 32, 128), low),
        ((4, 64, 128), low),
        ((4, 8, WIDE), full),
        ((6, 8, WIDE), full),
        ((ROWS, WIDE), low),
        ((8, 32, WIDE), low),
        ((8, 32, WIDE), low),
        ((2, 4, LINE, WIDE), low),
        ((4, 4, LINE, WIDE), low),
        ((2, 4, LINE, WIDE), low),
        ((4, 2, LINE, WIDE), low),
        ((2, LINE, WIDE), low),
        ((4, LINE, WIDE), low),
        ((2, LINE, WIDE), full),
        ((4, LINE, WIDE), low),
        ((4, PAIR, WIDE), low),
        ((2, PAIR, WIDE), low),
        ((4, PAIR, WIDE), low),
        ((2, PAIR, WIDE), low),
        ((4, WINDOW, WIDE), low),
        ((2, WINDOW, WIDE), full),
    ]
    return pl.pallas_call(
        backward_kernel,
        out_shape=[jax.ShapeDtypeStruct(*shape) for shape in outs],
        in_specs=[ANY] * 15 + [IN_VMEM] * 4,
        out_specs=[ANY] + [IN_VMEM] * 4,
        scratch_shapes=[pltpu.VMEM(*shape) for shape in vmem]
        + [
            dma((40,)), dma((2,)), dma((2, 4)), dma((4, 4)), dma((2, 2)), dma((4, 2)), dma((2,)), dma((4,)),
            dma((3, 4)), dma((3, 4)), dma((2,)), dma((7,)), dma((7,)), dma((7,)), dma((7,)), dma((7,)), dma((7,)),
            dma((7,)), dma((7,)), dma((3,)), dma((3,)), dma((6,)), dma((6,)),
        ],
        compiler_params=pltpu.CompilerParams(
            collective_id=1, has_side_effects=True, vmem_limit_bytes=63 * MIB
        ),
        name="backward",
    )(*operands)


TURN = np.arange(WIDE)[None, :] == (
    np.arange(WIDE).reshape(2, 2, 4, 2, SHARD).transpose(1, 0, 3, 2, 4).reshape(-1)
)[:, None]


def hidden_pick():
    pick = np.full((16, TILE), -1, np.int32)
    for k in range(4):
        for g in range(4):
            for at in range(8 * SHARD):
                yp, rest = divmod(at, 4 * SHARD)
                zp, r = divmod(rest, SHARD)
                pick[4 * k + g, 32 * g + at] = (2 * zp + yp) * 4 * SHARD + SHARD * k + r
    return pick


HIDDEN_PICK = hidden_pick()


def hidden_back(values):
    rows = values.shape[0]
    cut = values.reshape(rows, 4, 2, 2, 2, 4, SHARD)
    return cut.transpose(0, 3, 2, 5, 4, 1, 6).reshape(rows, 4 * WIDE)


def shards(
    tokens,
    segments,
    timesteps,
    caption,
    cotangent,
    ada_weight,
    ada_bias,
    spatial_in,
    spatial_out,
    temporal_in,
    temporal_out,
    cross_gain,
    cross_query,
    caption_proj,
    cross_out,
    hidden_in,
    hidden_out,
):
    frame_seg = segments[0]
    text_width = caption.shape[-1]
    caption_rows = caption[0].reshape(2 * L, text_width)
    blk = lax.axis_index("blk")
    seq = lax.axis_index("seq")
    zplace = blk // 2
    conditioning = to_low(jax.nn.silu(time_embedding(timesteps[0], WIDE)))
    cond_in = jnp.pad(conditioning.reshape(2 * WIDE // 128, 128), ((0, 32 - 2 * WIDE // 128), (0, 0)))
    frames = frame_seg.astype(jnp.float32)
    own_frames = lax.dynamic_slice(frames, (2 * blk,), (2,))
    seg_in = jnp.broadcast_to(
        jnp.stack(
            [jnp.repeat(frames, 16), jnp.repeat(own_frames, 128), jnp.tile(jnp.repeat(frames, 8), 2)]
        )[:, :, None],
        (3, ROWS, 128),
    )
    seg_row = jnp.broadcast_to(jnp.repeat(frames, 8)[None], (8, 128))
    turn = jnp.asarray(TURN, jnp.bfloat16)
    wide, out, *kept = forward(
        spatial_in,
        spatial_out,
        temporal_in,
        temporal_out,
        cross_query,
        cross_out,
        hidden_in,
        hidden_out,
        tokens.reshape(ROWS, WIDE),
        jnp.pad(cross_gain[None], ((0, 7), (0, 0))),
        jnp.pad(conditioning, ((0, 14), (0, 0))),
        ada_bias[None],
        seg_in,
        seg_row,
        jnp.asarray(HIDDEN_PICK),
        cotangent.reshape(ROWS, WIDE),
        turn,
        ada_weight,
        caption[0],
        caption_proj,
    )
    spread, grad_tokens, grad_gain, grad_text, grad_mod = backward(
        wide, *kept, seg_in, seg_row, turn, cond_in
    )
    shares = lax.dynamic_slice(spread, (0, 4 * zplace, 0), (BLOCKS, SHARD, WIDE))
    share_gain = lax.dynamic_slice(grad_gain, (0, SHARD * (seq * 8 + blk)), (1, SHARD))[0]
    text_low = grad_text.reshape(TEXT, 2, 128)[:, :, :L].reshape(TEXT, 2 * L)
    grad_caption = lax.dot_general(
        caption_rows, text_low, (((0,), (1,)), ((), ())), preferred_element_type=jnp.float32
    )
    grad_caption = lax.psum(grad_caption.astype(jnp.bfloat16), "seq").astype(jnp.float32)
    all_mod = lax.dynamic_slice(
        grad_mod[:, : 2 * MOD_TILES].reshape(8, MOD_WIN), (0, 16 * blk), (8, MOD // 8)
    )
    all_cond = grad_mod[:, 32 : 32 + 2 * WIDE // 128].reshape(8, WIDE)
    grad_ada_w = left_product(all_cond, all_mod)
    grad_ada_b = jnp.sum(all_mod.astype(jnp.float32), axis=0)

    def joined(first, count):
        return shares[first : first + count].transpose(1, 0, 2).reshape(SHARD, count * WIDE)

    return (
        out.reshape(tokens.shape),
        grad_tokens.reshape(tokens.shape),
        grad_ada_w,
        grad_ada_b,
        joined(15, 3),
        shares[14],
        joined(11, 3),
        shares[10],
        share_gain,
        shares[9],
        grad_caption,
        shares[8],
        hidden_back(joined(4, 4)),
        shares[0:4].reshape(4 * SHARD, WIDE),
    )


def solution(mesh):
    fast = dict(mesh.shape) == {"seq": 4, "blk": 8}
    return jax.shard_map(
        shards if fast else general_shards,
        mesh=mesh,
        in_specs=(
            P("seq", "blk", None, None),
            P("seq", None),
            P("seq", None),
            P("seq", None, None, None),
            P("seq", "blk", None, None),
            P(None, "blk"),
            P("blk"),
            P(("seq", "blk"), None),
            P(("seq", "blk"), None),
            P(("seq", "blk"), None),
            P(("seq", "blk"), None),
            P(("seq", "blk")),
            P(("seq", "blk"), None),
            P(None, "blk"),
            P(("seq", "blk"), None),
            P(("seq", "blk"), None),
            P(("seq", "blk"), None),
        ),
        out_specs=(
            P("seq", "blk", None, None),
            P("seq", "blk", None, None),
            P(None, "blk"),
            P("blk"),
            P(("seq", "blk"), None),
            P(("seq", "blk"), None),
            P(("seq", "blk"), None),
            P(("seq", "blk"), None),
            P(("seq", "blk")),
            P(("seq", "blk"), None),
            P(None, "blk"),
            P(("seq", "blk"), None),
            P(("seq", "blk"), None),
            P(("seq", "blk"), None),
        ),
        check_vma=False,
    )
```

```python
import math

import jax
import jax.numpy as jnp
import numpy as np
from jax import lax
from jax.experimental import pallas as pl
from jax.experimental.pallas import tpu as pltpu
from jax.sharding import PartitionSpec as P

H = 16
E = 72
L = 120


EPSILON = 1e-06
MASKED = -1e30


def to_low(values):
    return values.astype(jnp.bfloat16)


def linear(left, right):
    return jnp.dot(left, right, preferred_element_type=jnp.float32)


def left_product(left, right):
    return lax.dot_general(
        left, right, (((0,), (0,)), ((), ())), preferred_element_type=jnp.float32
    )


def right_product(left, right):
    return lax.dot_general(
        left, right, (((1,), (1,)), ((), ())), preferred_element_type=jnp.float32
    )


def normalize(values):
    center = values - jnp.mean(values, axis=-1, keepdims=True)
    return center * lax.rsqrt(jnp.mean(center * center, axis=-1, keepdims=True) + EPSILON)


def modulate(values, shift_rows, scale_rows):
    return normalize(values) * (1.0 + scale_rows) + shift_rows


def gain_norm(values, gain_row):
    return normalize(values) * gain_row


def gelu_tanh(values):
    return jax.nn.gelu(values, approximate=True)


def softmax_rows(scores):
    shifted = jnp.exp(scores - jnp.max(scores, axis=-1, keepdims=True))
    return shifted / jnp.sum(shifted, axis=-1, keepdims=True)


def softmax_with_total(scores):
    top = jnp.max(scores, axis=-1, keepdims=True)
    shifted = jnp.exp(scores - top)
    total = jnp.sum(shifted, axis=-1, keepdims=True)
    return (shifted / total, (top + jnp.log(total))[..., 0])


def softmax_back(probs, grad_probs):
    return probs * (grad_probs - jnp.sum(grad_probs * probs, axis=-1, keepdims=True))


def time_embedding(step_ids, model_width):
    half_width = model_width // 2
    frequency = jnp.exp(
        -math.log(10000.0) * jnp.arange(half_width).astype(jnp.float32) / half_width
    )
    angles = step_ids.astype(jnp.float32)[:, None] * frequency[None, :]
    return jnp.concatenate([jnp.cos(angles), jnp.sin(angles)], axis=1)


def general_shards(
    tokens,
    segments,
    timesteps,
    caption,
    cotangent,
    ada_weight,
    ada_bias,
    spatial_in,
    spatial_out,
    temporal_in,
    temporal_out,
    cross_gain,
    cross_query,
    caption_proj,
    cross_out,
    hidden_in,
    hidden_out,
):
    inputs = tokens[0].astype(jnp.float32)
    patch_dev, frames, model_width = inputs.shape
    token_rows = patch_dev * frames
    head_count = H
    head_size = E
    score_scale = E ** (-0.5)
    frame_seg = segments[0]
    step_ids = timesteps[0]
    seg_count, text_len, text_width = caption.shape[1:]
    text_keys = seg_count * text_len
    caption_rows = caption[0].reshape(text_keys, text_width)
    grad_out = cotangent[0].astype(jnp.float32)
    gathered = (
        lax.all_gather(spatial_in, ("seq", "blk"), axis=0, tiled=True),
        lax.all_gather(spatial_out, ("seq", "blk"), axis=0, tiled=True),
        lax.all_gather(temporal_in, ("seq", "blk"), axis=0, tiled=True),
        lax.all_gather(temporal_out, ("seq", "blk"), axis=0, tiled=True),
        lax.all_gather(cross_gain, ("seq", "blk"), axis=0, tiled=True),
        lax.all_gather(cross_query, ("seq", "blk"), axis=0, tiled=True),
        lax.all_gather(cross_out, ("seq", "blk"), axis=0, tiled=True),
        lax.all_gather(hidden_in, ("seq", "blk"), axis=0, tiled=True),
        lax.all_gather(hidden_out, ("seq", "blk"), axis=0, tiled=True),
    )
    (
        wide_sin,
        wide_sout,
        wide_tin,
        wide_tout,
        gain_low,
        wide_query,
        wide_cout,
        wide_hin,
        wide_hout,
    ) = gathered
    gain_row = gain_low.astype(jnp.float32)
    conditioning = to_low(jax.nn.silu(time_embedding(step_ids, model_width)))
    mod_part = to_low(linear(conditioning, ada_weight) + ada_bias.astype(jnp.float32))
    text_part = to_low(linear(caption_rows, caption_proj))
    modulation, memory = (
        lax.all_gather(mod_part, "blk", axis=1, tiled=True),
        lax.all_gather(text_part, "blk", axis=1, tiled=True),
    )
    choose = frame_seg[:, None] == jnp.arange(seg_count, dtype=jnp.int32)[None, :]
    frame_mod = linear(choose.astype(jnp.bfloat16), modulation)
    pieces = [frame_mod[:, index * model_width : (index + 1) * model_width] for index in range(9)]
    (
        shift_one,
        scale_one,
        gate_one,
        shift_two,
        scale_two,
        gate_two,
        shift_three,
        scale_three,
        gate_three,
    ) = pieces
    spatial_input = to_low(modulate(inputs, shift_one, scale_one)).reshape(token_rows, model_width)
    spatial_qkv = to_low(linear(spatial_input, wide_sin)).reshape(
        patch_dev, frames, 3 * model_width
    )
    query_s = spatial_qkv[..., :model_width].reshape(patch_dev, frames, head_count, head_size)
    local_kv = spatial_qkv[..., model_width:]
    whole_kv = lax.all_gather(local_kv, "blk", axis=0, tiled=True)

    def split_kv(both):
        count = both.shape[0]
        return (
            both[..., :model_width].reshape(count, frames, head_count, head_size),
            both[..., model_width:].reshape(count, frames, head_count, head_size),
        )

    def spatial_probs(key_all):
        scores = jnp.einsum("pfhe,qfhe->fhpq", query_s, key_all, preferred_element_type=jnp.float32)
        return softmax_with_total(scores * score_scale)

    key_s, value_s = split_kv(whole_kv)
    probs_s, log_total_s = spatial_probs(key_s)
    probs_s_low = to_low(probs_s)
    attn_s = to_low(
        jnp.einsum(
            "fhpq,qfhe->pfhe", probs_s_low, value_s, preferred_element_type=jnp.float32
        ).reshape(token_rows, model_width)
    )
    branch_s = linear(attn_s, wide_sout).reshape(patch_dev, frames, model_width)
    after_one = inputs + gate_one * branch_s
    temporal_input = to_low(modulate(after_one, shift_two, scale_two)).reshape(
        token_rows, model_width
    )
    temporal_qkv = to_low(linear(temporal_input, wide_tin)).reshape(
        patch_dev, frames, 3, head_count, head_size
    )
    query_t = temporal_qkv[:, :, 0]
    key_t = temporal_qkv[:, :, 1]
    value_t = temporal_qkv[:, :, 2]
    same_seg = frame_seg[:, None] == frame_seg[None, :]
    scores_t = (
        jnp.einsum("pfhe,pghe->phfg", query_t, key_t, preferred_element_type=jnp.float32)
        * score_scale
    )
    probs_t = softmax_rows(jnp.where(same_seg[None, None], scores_t, MASKED))
    probs_t_low = to_low(probs_t)
    attn_t = to_low(
        jnp.einsum(
            "phfg,pghe->pfhe", probs_t_low, value_t, preferred_element_type=jnp.float32
        ).reshape(token_rows, model_width)
    )
    branch_t = linear(attn_t, wide_tout).reshape(patch_dev, frames, model_width)
    after_two = after_one + gate_two * branch_t
    cross_input = to_low(gain_norm(after_two, gain_row)).reshape(token_rows, model_width)
    query_c = to_low(linear(cross_input, wide_query)).reshape(
        patch_dev, frames, head_count, head_size
    )
    key_c = memory[:, :model_width].reshape(text_keys, head_count, head_size)
    value_c = memory[:, model_width:].reshape(text_keys, head_count, head_size)
    key_seg = jnp.arange(text_keys, dtype=jnp.int32) // text_len
    allowed = frame_seg[:, None] == key_seg[None, :]
    scores_c = (
        jnp.einsum("pfhe,khe->pfhk", query_c, key_c, preferred_element_type=jnp.float32)
        * score_scale
    )
    probs_c = softmax_rows(jnp.where(allowed[None, :, None, :], scores_c, MASKED))
    probs_c_low = to_low(probs_c)
    attn_c = to_low(
        jnp.einsum(
            "pfhk,khe->pfhe", probs_c_low, value_c, preferred_element_type=jnp.float32
        ).reshape(token_rows, model_width)
    )
    branch_c = linear(attn_c, wide_cout).reshape(patch_dev, frames, model_width)
    after_three = after_two + branch_c
    mlp_input = to_low(modulate(after_three, shift_three, scale_three)).reshape(
        token_rows, model_width
    )
    pre_act = linear(mlp_input, wide_hin)
    post_act = to_low(gelu_tanh(pre_act))
    branch_m = linear(post_act, wide_hout).reshape(patch_dev, frames, model_width)
    result = after_three + gate_three * branch_m
    grad_gate_three = jnp.sum(grad_out * branch_m, axis=0)
    grad_four = to_low(grad_out * gate_three).reshape(token_rows, model_width)
    grad_hout = left_product(post_act, grad_four)
    grad_post = right_product(grad_four, wide_hout)
    gelu_pull = jax.vjp(gelu_tanh, pre_act)[1]
    grad_pre = to_low(gelu_pull(grad_post)[0])
    grad_hin = left_product(mlp_input, grad_pre)
    grad_mlp_in = right_product(grad_pre, wide_hin).reshape(patch_dev, frames, model_width)
    mlp_pull = jax.vjp(modulate, after_three, shift_three, scale_three)[1]
    back_three, grad_shift_three, grad_scale_three = mlp_pull(grad_mlp_in)
    grad_three = grad_out + back_three
    grad_cross_branch = to_low(grad_three).reshape(token_rows, model_width)
    grad_cout = left_product(attn_c, grad_cross_branch)
    grad_attn_c = to_low(right_product(grad_cross_branch, wide_cout)).reshape(
        patch_dev, frames, head_count, head_size
    )
    grad_probs_c = jnp.einsum(
        "pfhe,khe->pfhk", grad_attn_c, value_c, preferred_element_type=jnp.float32
    )
    grad_scores_c = to_low(softmax_back(probs_c, grad_probs_c))
    grad_query_c = to_low(
        jnp.einsum("pfhk,khe->pfhe", grad_scores_c, key_c, preferred_element_type=jnp.float32)
        * score_scale
    ).reshape(token_rows, model_width)
    grad_key_c = (
        jnp.einsum("pfhk,pfhe->khe", grad_scores_c, query_c, preferred_element_type=jnp.float32)
        * score_scale
    )
    grad_value_c = jnp.einsum(
        "pfhk,pfhe->khe", probs_c_low, grad_attn_c, preferred_element_type=jnp.float32
    )
    grad_memory = jnp.concatenate(
        [grad_key_c.reshape(text_keys, model_width), grad_value_c.reshape(text_keys, model_width)],
        axis=1,
    )
    grad_wquery = left_product(cross_input, grad_query_c)
    grad_cross_in = right_product(grad_query_c, wide_query).reshape(patch_dev, frames, model_width)
    cross_pull = jax.vjp(gain_norm, after_two, gain_row)[1]
    back_two, grad_gain = cross_pull(grad_cross_in)
    grad_two = grad_three + back_two
    grad_gate_two = jnp.sum(grad_two * branch_t, axis=0)
    grad_temporal_branch = to_low(grad_two * gate_two).reshape(token_rows, model_width)
    grad_tout = left_product(attn_t, grad_temporal_branch)
    grad_attn_t = to_low(right_product(grad_temporal_branch, wide_tout)).reshape(
        patch_dev, frames, head_count, head_size
    )
    grad_probs_t = jnp.einsum(
        "pfhe,pghe->phfg", grad_attn_t, value_t, preferred_element_type=jnp.float32
    )
    grad_scores_t = to_low(softmax_back(probs_t, grad_probs_t))
    grad_query_t = (
        jnp.einsum("phfg,pghe->pfhe", grad_scores_t, key_t, preferred_element_type=jnp.float32)
        * score_scale
    )
    grad_key_t = (
        jnp.einsum("phfg,pfhe->pghe", grad_scores_t, query_t, preferred_element_type=jnp.float32)
        * score_scale
    )
    grad_value_t = jnp.einsum(
        "phfg,pfhe->pghe", probs_t_low, grad_attn_t, preferred_element_type=jnp.float32
    )
    grad_qkv_t = to_low(jnp.stack([grad_query_t, grad_key_t, grad_value_t], axis=2)).reshape(
        token_rows, 3 * model_width
    )
    grad_tin = left_product(temporal_input, grad_qkv_t)
    grad_temporal_in = right_product(grad_qkv_t, wide_tin).reshape(patch_dev, frames, model_width)
    temporal_pull = jax.vjp(modulate, after_one, shift_two, scale_two)[1]
    back_one, grad_shift_two, grad_scale_two = temporal_pull(grad_temporal_in)
    grad_one = grad_two + back_one
    grad_gate_one = jnp.sum(grad_one * branch_s, axis=0)
    grad_spatial_branch = to_low(grad_one * gate_one).reshape(token_rows, model_width)
    grad_sout = left_product(attn_s, grad_spatial_branch)
    grad_attn_s = to_low(right_product(grad_spatial_branch, wide_sout)).reshape(
        patch_dev, frames, head_count, head_size
    )
    back_kv = lax.all_gather(local_kv, "blk", axis=0, tiled=True)
    back_key, back_value = split_kv(back_kv)
    back_probs = spatial_probs(back_key)[0]
    back_probs_low = to_low(back_probs)
    grad_probs_s = jnp.einsum(
        "pfhe,qfhe->fhpq", grad_attn_s, back_value, preferred_element_type=jnp.float32
    )
    row_delta = jnp.sum(grad_probs_s * back_probs, axis=-1, keepdims=True)
    grad_scores_s = to_low(back_probs * (grad_probs_s - row_delta))
    grad_query_s = (
        jnp.einsum("fhpq,qfhe->pfhe", grad_scores_s, back_key, preferred_element_type=jnp.float32)
        * score_scale
    )
    count = lax.axis_size("blk") * patch_dev
    grad_key = (
        jnp.einsum("fhpq,pfhe->qfhe", grad_scores_s, query_s, preferred_element_type=jnp.float32)
        * score_scale
    )
    grad_value = jnp.einsum(
        "fhpq,pfhe->qfhe", back_probs_low, grad_attn_s, preferred_element_type=jnp.float32
    )
    grad_kv = to_low(
        lax.psum_scatter(
            jnp.concatenate(
                [
                    grad_key.reshape(count, frames, model_width),
                    grad_value.reshape(count, frames, model_width),
                ],
                axis=2,
            ).astype(jnp.bfloat16),
            "blk",
            scatter_dimension=0,
            tiled=True,
        ).astype(jnp.float32)
    )
    grad_qkv_s = jnp.concatenate(
        [to_low(grad_query_s).reshape(patch_dev, frames, model_width), grad_kv], axis=2
    ).reshape(token_rows, 3 * model_width)
    grad_sin = left_product(spatial_input, grad_qkv_s)
    grad_spatial_in = right_product(grad_qkv_s, wide_sin).reshape(patch_dev, frames, model_width)
    spatial_pull = jax.vjp(modulate, inputs, shift_one, scale_one)[1]
    back_zero, grad_shift_one, grad_scale_one = spatial_pull(grad_spatial_in)
    grad_input = grad_one + back_zero
    grad_frame_mod = jnp.concatenate(
        [
            grad_shift_one,
            grad_scale_one,
            grad_gate_one,
            grad_shift_two,
            grad_scale_two,
            grad_gate_two,
            grad_shift_three,
            grad_scale_three,
            grad_gate_three,
        ],
        axis=1,
    )
    grad_mod_local = lax.dot_general(
        choose.astype(jnp.float32),
        grad_frame_mod,
        (((0,), (0,)), ((), ())),
        precision=lax.Precision.HIGHEST,
    )
    grad_mod_part, grad_memory_part = (
        lax.psum_scatter(
            grad_mod_local.astype(jnp.bfloat16), "blk", scatter_dimension=1, tiled=True
        ).astype(jnp.float32),
        lax.psum_scatter(
            grad_memory.astype(jnp.bfloat16), "blk", scatter_dimension=1, tiled=True
        ).astype(jnp.float32),
    )
    grad_mod_low = to_low(grad_mod_part)
    grad_ada_w = left_product(conditioning, grad_mod_low)
    grad_ada_b = jnp.sum(grad_mod_low.astype(jnp.float32), axis=0)
    grad_caption = left_product(caption_rows, to_low(grad_memory_part))
    grad_ada_w, grad_ada_b, grad_caption = (
        lax.psum(grad_ada_w.astype(jnp.bfloat16), "seq").astype(jnp.float32),
        lax.psum(grad_ada_b.astype(jnp.bfloat16), "seq").astype(jnp.float32),
        lax.psum(grad_caption.astype(jnp.bfloat16), "seq").astype(jnp.float32),
    )
    shares = (
        lax.psum_scatter(grad_sin, ("seq", "blk"), scatter_dimension=0, tiled=True),
        lax.psum_scatter(grad_sout, ("seq", "blk"), scatter_dimension=0, tiled=True),
        lax.psum_scatter(grad_tin, ("seq", "blk"), scatter_dimension=0, tiled=True),
        lax.psum_scatter(grad_tout, ("seq", "blk"), scatter_dimension=0, tiled=True),
        lax.psum_scatter(grad_gain, ("seq", "blk"), scatter_dimension=0, tiled=True),
        lax.psum_scatter(grad_wquery, ("seq", "blk"), scatter_dimension=0, tiled=True),
        lax.psum_scatter(grad_cout, ("seq", "blk"), scatter_dimension=0, tiled=True),
        lax.psum_scatter(grad_hin, ("seq", "blk"), scatter_dimension=0, tiled=True),
        lax.psum_scatter(grad_hout, ("seq", "blk"), scatter_dimension=0, tiled=True),
    )
    (
        share_sin,
        share_sout,
        share_tin,
        share_tout,
        share_gain,
        share_query,
        share_cout,
        share_hin,
        share_hout,
    ) = shares
    return (
        to_low(result)[None],
        to_low(grad_input)[None],
        grad_ada_w,
        grad_ada_b,
        share_sin,
        share_sout,
        share_tin,
        share_tout,
        share_gain,
        share_query,
        grad_caption,
        share_cout,
        share_hin,
        share_hout,
    )


MESH = pl.DeviceIdType.MESH
BLOCKS = 18
LINES = 8
SHARD = 36
LINE = 4 * SHARD
WINDOW = 48
WIDE = LINES * LINE
MIB = 2**20


def place():
    seq = lax.axis_index("seq")
    blk = lax.axis_index("blk")
    x, c = seq // 2, seq % 2
    z, y = blk // 2, blk % 2
    x1, y1 = x + (1 - 2 * x) * (1 - c), y + (1 - 2 * y) * c
    x2, y2 = x + (1 - 2 * x) * c, y + (1 - 2 * y) * (1 - c)
    return x, c, y, z, x1, y1, x2, y2


def device(x, c, y, z):
    return {"seq": x * 2 + c, "blk": z * 2 + y}


def line_of(c, x, y):
    return (c * 2 + x) * 2 + y


def remote(src, dst, send_sem, recv_sem, where):
    return pltpu.make_async_remote_copy(
        src_ref=src,
        dst_ref=dst,
        send_sem=send_sem,
        recv_sem=recv_sem,
        device_id=where,
        device_id_type=MESH,
    )


def greet(others):
    barrier = pltpu.get_barrier_semaphore()
    for other in others:
        pl.semaphore_signal(barrier, inc=1, device_id=other, device_id_type=MESH)
    pl.semaphore_wait(barrier, len(others))


def left_at(t):
    at = jnp.minimum(t, 4)
    for first in (8, 9, 10, 11, 14, 15):
        at = at + jnp.where(t >= first, 1, 0)
    return at


def right_at(t):
    return jnp.where(t < 14, jnp.maximum(t - 3, 0), t - 13)


ROWS = 256
KEYS = 256
TEXT = 288
MOD = 9 * WIDE
MOD_TILES = 11
MOD_WIN = 128 * MOD_TILES
PARTS, HELD, LAST = 4, 4, 8
PAIR = 80
LEFT_SEM, SLOPE_SEM, SAVE_SEMS = 40, 42, 44
TILE = 384
SCALE = E ** (-0.5)


def nt(left, right):
    return lax.dot_general(
        left, right, (((1,), (1,)), ((), ())), preferred_element_type=jnp.float32
    )


def wide32(values):
    return values.astype(jnp.float32)


def loop(count, body):
    def step(index, carry):
        body(index)
        return carry

    lax.fori_loop(0, count, step, 0)


def each_rows(size, body, total=ROWS):
    loop(total // size, lambda i: body(pl.ds(pl.multiple_of(i * size, size), size)))


def each_cols(body):
    loop(WIDE // TILE, lambda i: body(pl.ds(pl.multiple_of(i * TILE, TILE), TILE)))


def swap_rows():
    row = lax.broadcasted_iota(jnp.int32, (ROWS, ROWS), 0)
    col = lax.broadcasted_iota(jnp.int32, (ROWS, ROWS), 1)
    return to_low((((row & 15) << 4) + (row >> 4) == col).astype(jnp.float32))


def head_window(h):
    base = h * E
    start = jnp.minimum(base // 128, 7) * 128
    lane = lax.broadcasted_iota(jnp.int32, (1, 256), 1)
    on = (lane >= base - start) & (lane < base - start + E)
    return pl.ds(pl.multiple_of(start, 128), 256), on.astype(jnp.float32)


def soft(scores, bias, mask):
    scores = scores * SCALE
    if bias is not None:
        scores = scores + bias
    powers = jnp.exp(scores - jnp.max(scores, axis=-1, keepdims=True))
    probs = powers * (1.0 / jnp.sum(powers, axis=-1, keepdims=True))
    return probs if mask is None else probs * mask


def chains(h, groups):
    return [(window, rows, keys) for window in (head_window(h), head_window(h + H // 2)) for rows, keys in groups]


def split_rows(values, jobs):
    start = 0
    parts = []
    for _, rows, _ in jobs:
        size = rows.stop - rows.start
        parts.append(values[start : start + size])
        start += size
    return parts


def heads_forward(h, query, key, value, attn, groups, bias, mask):
    jobs = chains(h, groups)
    scores = [nt(query[rows, lanes] * to_low(on), key[keys, lanes]) for (lanes, on), rows, keys in jobs]
    probs = split_rows(to_low(soft(jnp.concatenate(scores), bias, mask)), jobs)
    parts = [linear(prob, value[keys, lanes]) * on for prob, ((lanes, on), rows, keys) in zip(probs, jobs)]
    for part, ((lanes, on), rows, keys) in zip(parts, jobs):
        attn[rows, lanes] = attn[rows, lanes] + to_low(part)


def text_heads_forward(h, query, key, value, attn, bias, mask):
    jobs = chains(h, VIDEOS)
    scores = [linear(query[rows, lanes] * to_low(on), key[lanes, keys]) for (lanes, on), rows, keys in jobs]
    probs = split_rows(to_low(soft(jnp.concatenate(scores), bias, mask)), jobs)
    parts = [nt(prob, value[lanes, keys]) * on for prob, ((lanes, on), rows, keys) in zip(probs, jobs)]
    for part, ((lanes, on), rows, keys) in zip(parts, jobs):
        attn[rows, lanes] = attn[rows, lanes] + to_low(part)


HALVES = [(slice(0, 128), slice(0, 128)), (slice(128, 256), slice(128, 256))]
VIDEOS = [(slice(0, 144), slice(0, 128)), (slice(112, 256), slice(128, 256))]


def regroup(back):
    row = lax.broadcasted_iota(jnp.int32, (ROWS, ROWS), 0)
    col = lax.broadcasted_iota(jnp.int32, (ROWS, ROWS), 1)
    if back:
        source = (((row >> 3) & 1) << 7) + ((row >> 4) << 3) + (row & 7)
    else:
        source = (((row >> 3) & 15) << 4) + ((row >> 7) << 3) + (row & 7)
    return to_low((source == col).astype(jnp.float32))


def temporal_bias(seg_in, seg_row):
    row = lax.broadcasted_iota(jnp.int32, (128, 128), 0)
    col = lax.broadcasted_iota(jnp.int32, (128, 128), 1)
    allowed = ((row & 7) == (col & 7)) & (seg_in[2, 0:128, 0:1] == seg_row[0:1, 0:128])
    return jnp.where(allowed, 0.0, MASKED)


def cross_bias():
    col = lax.broadcasted_iota(jnp.int32, (1, 128), 1)
    return jnp.where(col < L, 0.0, MASKED)


def cross_rows(seg_in):
    both = [1.0 - seg_in[0, 0:144, 0:1], seg_in[0, 112:256, 0:1]]
    return jnp.concatenate(both + both)


def move_lanes(to, value, from_start, to_start, width):
    left = min(from_start // 128 * 128, value.shape[1] - 256)
    right = min(to_start // 128 * 128, width - 256)
    off = to_start - right
    part = pltpu.roll(value[:, left : left + 256], (off - (from_start - left)) % 256, 1)
    lane = lax.broadcasted_iota(jnp.int32, part.shape, 1)
    lanes = slice(right, right + 256)
    to[:, lanes] = jnp.where((lane >= off) & (lane < off + SHARD), part, to[:, lanes])


def hidden_places():
    places = []
    for d in range(32):
        xp, cp, zp, yp = d // 16, d // 8 % 2, d // 2 % 4, d % 2
        for k in range(4):
            places.append((k, (4 * d + k) * SHARD, (((cp * 2 + xp) * 2 + yp) * 4 + zp) * SHARD))
    return places


def blk_peers(x, c, b):
    return [device(x, c, (b + k) % 2, ((b + k) % 8) // 2) for k in range(1, 8)]


def forward_kernel(
    spatial_in, spatial_out, temporal_in, temporal_out, cross_query, cross_out, hidden_in, hidden_out,
    tok, gain_one, cond, ada_bias, seg_in, seg_row, cot_i, turn_i, ada_i, caption_i, proj_i,
    wide, out, left_o, qkvs_o, qkvt_o, qc_o, mem_o, xhat_o, rstd_o, branch_o, slope_o, gfour_o, cot_o, mods_o, gate_o, gain_o,
    win, pair, far, lines, weights, tokp, cotp, tokf, xin, xp, left, qkvs, qkvt, qc, mem, text, mod, mods, xhat, rstd, branch, branchw, bias,
    stream, attnf, attnp, post, slope, gfour, gains, gain_at, gate,
    src, cot, turn, ada, caption, proj, mod_in, text_in, hidden,
    z_send, z_recv, l_send, l_recv, own_sem, w_sem, t_send, t_recv, a_send, a_recv, m_send, m_recv, x_send, x_recv,
    g_send, g_recv, save_sem, in_sem,
):
    x, c, y, z, x1, y1, x2, y2 = place()
    b = z * 2 + y
    near = [device(x, c, y, (z + k) % 4) for k in (1, 2, 3)]
    beside, across = device(x, c, y, z + 1 - 2 * (z % 2)), device(x, c, y, 3 - z)
    middle = (z == 1) | (z == 2)
    first, second, twin = device(x1, c, y1, z), device(x2, c, y2, z), device(x, 1 - c, y, z)
    peers = blk_peers(x, c, b)
    greet(peers + [device(1 - x, c, y, z), twin])
    mine, line3 = line_of(c, x, y), line_of(c, 1 - x, 1 - y)

    def hops(t, core):
        turn_round = core + (1 - core) * (t % 4 == 2)
        xa, ya = x + (1 - 2 * x) * (1 - turn_round), y + (1 - 2 * y) * turn_round
        xb, yb = x + (1 - 2 * x) * turn_round, y + (1 - 2 * y) * (1 - turn_round)
        return (xa, ya), (xb, yb)

    def z_one(t):
        return remote(src.at[t], win.at[t % PARTS], z_send.at[t, 0], z_recv.at[t, 0], beside)

    def z_two(t):
        return remote(pair.at[t % PARTS], far.at[t % PARTS], z_send.at[t, 1], z_recv.at[t, 1], across)

    def z_three(t):
        return remote(far.at[t % PARTS], far.at[t % PARTS], z_send.at[t, 2], z_recv.at[t, 2], beside)

    def wide_line(t, line):
        return wide.at[t, pl.ds(pl.multiple_of(line * LINE, 16), LINE)]

    def own(t):
        return pltpu.make_async_copy(lines.at[t % HELD], wide_line(t, mine), own_sem.at[t])

    def line_copy(t, to, line, index, where):
        return remote(to, wide_line(t, line), l_send.at[t, index], l_recv.at[t, index], where)

    def sends(t, index):
        (xa, ya), (xb, yb) = hops(t, c)
        one, two = device(xa, c, ya, z), device(xb, c, yb, z)
        line1, line2 = line_of(c, xa, ya), line_of(c, xb, yb)
        line, where = (
            (mine, one), (mine, two), (mine, twin), (line1, two),
            (line1, twin), (line2, twin), (line3, twin),
        )[index]
        from_here = lines.at[t % HELD] if index < 3 else wide_line(t, line)
        return line_copy(t, from_here, line, index, where)

    def arrives(t, line, index):
        line_copy(t, wide_line(t, line), line, index, first).wait_recv()

    def tick(t):
        @pl.when((t >= 4) & (t < BLOCKS + 4))
        def _():
            now = t - 4

            @pl.when(middle)
            def _():
                z_two(now).wait_send()
                z_three(now).wait_send()

            @pl.when(jnp.logical_not(middle))
            def _():
                z_three(now).wait_recv()

            @pl.when(now >= HELD)
            def _():
                for index in range(3):
                    sends(now - HELD, index).wait_send()
                own(now - HELD).wait()

            def line_from(low, high):
                at = now % HELD
                lines[at, 0:64] = low[0:64]
                lines[at, 64:80] = low[64:80] + high[0:16]
                lines[at, 80:144] = high[16:80]

            @pl.when(z < 2)
            def _():
                line_from(pair[now % PARTS], far[now % PARTS])

            @pl.when(z >= 2)
            def _():
                line_from(far[now % PARTS], pair[now % PARTS])

            for index in range(3):
                sends(now, index).start()
            own(now).start()

        @pl.when((t >= 2) & (t < BLOCKS + 2) & middle)
        def _():
            z_two(t - 2).wait_recv()
            z_three(t - 2).start()

        @pl.when((t >= 1) & (t < BLOCKS + 1))
        def _():
            now = t - 1
            z_one(now).wait_recv()

            def pair_from(even, odd):
                at = now % PARTS
                pair[at, 0:32] = even[0:32]
                pair[at, 32:48] = even[32:48] + odd[0:16]
                pair[at, 48:80] = odd[16:48]

            @pl.when(z % 2 == 0)
            def _():
                pair_from(src[now], win[now % PARTS])

            @pl.when(z % 2 == 1)
            def _():
                pair_from(win[now % PARTS], src[now])

            @pl.when(middle)
            def _():
                z_two(now).start()

        @pl.when(t < BLOCKS)
        def _():
            z_one(t).start()

        @pl.when((t >= 6) & (t < BLOCKS + 6))
        def _():
            now = t - 6
            xa, ya = hops(now, c)[0]
            arrives(now, line_of(c, xa, ya), 0)
            for index in (3, 4):
                sends(now, index).start()

        @pl.when(t >= LAST)
        def _():
            now = t - LAST
            xb, yb = hops(now, c)[1]
            arrives(now, line_of(c, xb, yb), 1)
            sends(now, 5).start()
            arrives(now, line3, 3)
            sends(now, 6).start()

    done = [0]

    def pump(until):
        until = min(until, BLOCKS + LAST)
        if until > done[0]:
            start = done[0]
            loop(until - start, lambda i: tick(i + start))
            done[0] = until

    def poke():
        pump(done[0] + 1)

    def load(block):
        pump(block + LAST + 1)
        near_at, far_at = hops(block, 1 - c)
        places = [(x, y), near_at, far_at, (1 - x, 1 - y)]
        for (xl, yl), index in zip(places, (2, 4, 5, 6)):
            arrives(block, line_of(1 - c, xl, yl), index)
        if block >= BLOCKS - HELD:
            own(block).wait()
        copy = pltpu.make_async_copy(wide.at[block], weights.at[block % 2], w_sem.at[block % 2])
        copy.start()
        copy.wait()

    def times(values, block, emit):
        def tile(cols):
            emit(cols, linear(values[...], weights[block % 2, :, cols]))

        each_cols(tile)

    saves = []
    held = {}

    def save(from_ref, to_ref, name=None):
        if name is None:
            name = len(saves)
            saves.append(name)
        held[name] = pltpu.make_async_copy(from_ref, to_ref, save_sem.at[name])
        held[name].start()

    def settle(name):
        if name in held:
            held.pop(name).wait()

    def turned(values, index):
        slot = index % 2
        settle(LEFT_SEM + slot)

        def tile(cols):
            xp[:, cols] = to_low(nt(values[...], turn[cols, :]))
            left[slot, cols, :] = to_low(nt(turn[cols, :], values[...]))

        each_cols(tile)
        save(left.at[slot], left_o.at[index], LEFT_SEM + slot)

    fetches = [
        pltpu.make_async_copy(from_ref, to_ref, in_sem.at[at])
        for at, (from_ref, to_ref) in enumerate(
            ((ada_i, ada), (turn_i, turn), (cot_i, cot), (caption_i, caption), (proj_i, proj))
        )
    ]
    for copy in fetches:
        copy.start()

    def shift(rows, first):
        row = lax.broadcasted_iota(jnp.int32, (WINDOW, rows), 0) - 4 * z
        col = lax.broadcasted_iota(jnp.int32, (WINDOW, rows), 1)
        return to_low(((row >= 0) & (row < SHARD) & (row + first == col)).astype(jnp.float32))

    def window(at, values):
        src[at] = to_low(linear(shift(SHARD, 0), values))

    for j in range(3):
        window(j, spatial_in[:, WIDE * j : WIDE * j + WIDE])
    pump(2)
    window(3, spatial_out[...])
    for j in range(3):
        window(4 + j, temporal_in[:, WIDE * j : WIDE * j + WIDE])
    window(7, temporal_out[...])
    window(8, cross_query[...])
    window(9, cross_out[...])
    pump(4)

    def m_copy(k, at):
        return remote(mod_in, mod.at[at], m_send.at[k - 1], m_recv.at[k - 1], peers[k - 1])

    fetches[0].wait()
    part = wide32(to_low(nt(cond[...], ada[...]) + wide32(ada_bias[...])))[0:8]
    part = jnp.concatenate([part, jnp.zeros((8, MOD_WIN - MOD // 8), jnp.float32)], axis=1)
    part = pltpu.roll(part, 16 * b, 1)
    tiles = [part[row : row + 1, 128 * tile : 128 * tile + 128] for row in range(2) for tile in range(MOD_TILES)]
    mod_in[...] = to_low(jnp.concatenate(tiles + [jnp.zeros((32 - 2 * MOD_TILES, 128), jnp.float32)]))
    for k in range(1, 8):
        m_copy(k, b).start()
    mod[b] = mod_in[...]
    swap = swap_rows()
    tokp[...] = to_low(linear(swap, tok[...]))

    def t_copy(k):
        to = (b + k) % 8
        part = tokp.at[pl.ds(pl.multiple_of(32 * to, 32), 32)]
        return remote(part, tokf.at[b], t_send.at[k - 1], t_recv.at[k - 1], peers[k - 1])

    def t_wait(k):
        of = (b + 8 - k) % 8
        remote(tokp.at[pl.ds(0, 32)], tokf.at[of], t_send.at[k - 1], t_recv.at[k - 1], peers[k - 1]).wait_recv()

    pump(5)
    for k in range(1, 8):
        t_copy(k).start()
    tokf[b] = tokp[pl.ds(pl.multiple_of(32 * b, 32), 32)]

    def g_copy(at, from_at, to):
        return remote(gains.at[from_at], gain_at.at[at], g_send.at[at], g_recv.at[at], to)

    spread = jnp.concatenate([wide32(gain_one[...]), jnp.zeros((8, WIDE - SHARD), jnp.float32)], axis=1)
    gains[0] = pltpu.roll(spread, SHARD * ((x * 2 + c) * 8 + b), 1)
    g_copy(0, 0, twin).start()
    pump(6)
    fetches[2].wait()
    cotp[...] = to_low(linear(swap, cot[...]))
    save(cotp, cot_o)

    def x_copy(k, at):
        return remote(text_in, text.at[at, y], x_send.at[k - 1], x_recv.at[k - 1], near[k - 1])

    def x_over(at):
        return remote(text.at[:, at], text.at[:, at], x_send.at[3], x_recv.at[3], device(x, c, 1 - y, z))

    for k in range(1, 8):
        m_copy(k, (b + 8 - k) % 8).wait_recv()
    mods[...] = jnp.zeros_like(mods)
    for k in range(8):
        part = wide32(mod[k])
        for row in range(2):
            for tile in range(MOD_TILES):
                lanes = slice(1280 * k + 128 * tile, 1280 * k + 128 * tile + 128)
                at = row * MOD_TILES + tile
                mods[row : row + 1, lanes] = mods[row : row + 1, lanes] + part[at : at + 1]
    save(mods, mods_o)
    g_copy(0, 0, twin).wait_recv()
    gains[1] = gains[0] + gain_at[0]
    g_copy(1, 1, first).start()
    pump(7)
    fetches[3].wait()
    fetches[4].wait()
    text_in[...] = jnp.zeros_like(text_in)
    for v in range(2):
        text_in[:, 128 * v : 128 * v + L] = to_low(nt(proj[...], caption[v]))
    for k in (1, 2, 3):
        x_copy(k, z).start()
    text[z, y] = text_in[...]
    pump(8)
    hidden[...] = jnp.zeros_like(hidden)
    for k, natural, placed in hidden_places():
        start = natural // WIDE * WIDE
        move_lanes(hidden.at[k], wide32(hidden_in[:, start : start + WIDE]), natural - start, placed, WIDE)
    for k in range(4):
        window(10 + 2 * k, to_low(hidden[k]))
        src[11 + 2 * k] = to_low(linear(shift(4 * SHARD, SHARD * k), hidden_out[...]))
    fetches[1].wait()

    def pick(piece, seg):
        lanes = slice(WIDE * piece, WIDE * piece + WIDE)
        return jnp.where(seg > 0.5, mods[1:2, lanes], mods[0:1, lanes])

    def normal(values, rows, index):
        center = values - jnp.mean(values, axis=-1, keepdims=True)
        factor = lax.rsqrt(jnp.mean(center * center, axis=-1, keepdims=True) + EPSILON)
        scaled = center * factor
        xhat[index, rows, :] = to_low(scaled)
        rstd[index, rows, :] = jnp.broadcast_to(factor, (factor.shape[0], 128))
        return scaled

    for k in range(1, 8):
        t_wait(k)
    g_copy(1, 1, first).wait_recv()
    gains[2] = gains[1] + gain_at[1]
    g_copy(2, 2, second).start()

    def spatial_rows(i):
        seg = jnp.concatenate([seg_in[1, 0:16, 0:1], seg_in[1, 128:144, 0:1]])
        values = wide32(tokf[i])
        center = values - jnp.mean(values, axis=-1, keepdims=True)
        factor = lax.rsqrt(jnp.mean(center * center, axis=-1, keepdims=True) + EPSILON)
        scaled = center * factor
        ready = to_low(scaled * (1.0 + pick(1, seg)) + pick(0, seg))
        low = to_low(scaled)
        spread = jnp.broadcast_to(factor, (32, 128))
        for f in range(2):
            rows = pl.ds(pl.multiple_of(128 * f + 16 * i, 16), 16)
            part = slice(16 * f, 16 * f + 16)
            xhat[0, rows, :] = low[part]
            rstd[0, rows, :] = spread[part]
            xin[rows, :] = ready[part]

    loop(8, spatial_rows)
    save(xhat.at[0], xhat_o.at[0])
    save(rstd.at[0], rstd_o.at[0])
    turned(xin, 10)
    for j in range(3):
        load(j)

        def emit(cols, value, j=j):
            qkvs[j, :, cols] = to_low(value)

        times(xp, j, emit)
    save(qkvs, qkvs_o)
    g_copy(2, 2, second).wait_recv()
    gains[3] = gains[2] + gain_at[2]
    for k in (1, 2, 3):
        remote(gains.at[3], gain_at.at[2 + k], g_send.at[2 + k], g_recv.at[2 + k], near[k - 1]).start()
    for k in (1, 2, 3):
        x_copy(k, (z + 4 - k) % 4).wait_recv()
    x_over(y).start()
    attnf[...] = jnp.zeros_like(attnf)

    def spatial_heads(h):
        heads_forward(h, qkvs.at[0], qkvs.at[1], qkvs.at[2], attnf, HALVES, None, None)

    loop(4, spatial_heads)
    poke()
    loop(4, lambda h: spatial_heads(h + 4))
    for k in (1, 2, 3):
        remote(gains.at[3], gain_at.at[2 + k], g_send.at[2 + k], g_recv.at[2 + k], near[k - 1]).wait_recv()
    gains[0 + 4] = gains[3] + gain_at[3] + gain_at[4] + gain_at[5]
    save(gains.at[4], gain_o)

    def a_copy(k, f):
        to = (b + k) % 8
        part = attnf.at[pl.ds(pl.multiple_of(128 * f + 16 * to, 16), 16)]
        return remote(part, attnp.at[2 * b + f], a_send.at[k - 1, f], a_recv.at[k - 1, f], peers[k - 1])

    def a_wait(k, f):
        of = (b + 8 - k) % 8
        part = attnf.at[pl.ds(0, 16)]
        remote(part, attnp.at[2 * of + f], a_send.at[k - 1, f], a_recv.at[k - 1, f], peers[k - 1]).wait_recv()

    for k in range(1, 8):
        for f in range(2):
            a_copy(k, f).start()
    for f in range(2):
        attnp[2 * b + f] = attnf[pl.ds(pl.multiple_of(128 * f + 16 * b, 16), 16)]
    poke()
    for k in range(1, 8):
        for f in range(2):
            a_wait(k, f)
    xin[...] = attnp[...].reshape(ROWS, WIDE)
    turned(xin, 9)
    load(3)

    def emit_branch(cols, value):
        branchw[:, cols] = value

    times(xp, 3, emit_branch)

    def after_spatial(rows):
        seg = seg_in[0, rows, 0:1]
        value = branchw[rows, :]
        branch[0, rows, :] = to_low(value)
        value = wide32(tokp[rows, :]) + pick(2, seg) * value
        stream[rows, :] = value
        xin[rows, :] = to_low(normal(value, rows, 1) * (1.0 + pick(4, seg)) + pick(3, seg))

    each_rows(32, after_spatial)
    save(branch.at[0], branch_o.at[0])
    save(xhat.at[1], xhat_o.at[1])
    save(rstd.at[1], rstd_o.at[1])

    for k in range(1, 8):
        for f in range(2):
            a_copy(k, f).wait_send()
    attnf[...] = to_low(linear(regroup(False), xin[...]))
    turned(attnf, 8)
    for j in range(3):
        load(4 + j)

        def emit(cols, value, j=j):
            qkvt[j, :, cols] = to_low(value)

        times(xp, 4 + j, emit)
    save(qkvt, qkvt_o)
    attnf[...] = jnp.zeros_like(attnf)

    bias[...] = temporal_bias(seg_in, seg_row)

    def temporal_heads(h):
        heads_forward(
            h, qkvt.at[0], qkvt.at[1], qkvt.at[2], attnf, HALVES, jnp.concatenate([bias[...]] * 4), None
        )

    loop(4, temporal_heads)
    poke()
    loop(4, lambda h: temporal_heads(h + 4))
    xin[...] = to_low(linear(regroup(True), attnf[...]))
    turned(xin, 7)
    load(7)
    times(xp, 7, emit_branch)

    def after_temporal(rows):
        seg = seg_in[0, rows, 0:1]
        value = branchw[rows, :]
        branch[1, rows, :] = to_low(value)
        value = stream[rows, :] + pick(5, seg) * value
        stream[rows, :] = value
        xin[rows, :] = to_low(normal(value, rows, 2) * gains[4, 0:1, :])

    each_rows(32, after_temporal)
    save(branch.at[1], branch_o.at[1])
    save(xhat.at[2], xhat_o.at[2])
    save(rstd.at[2], rstd_o.at[2])

    turned(xin, 6)
    load(8)

    def emit_query(cols, value):
        qc[:, cols] = to_low(value)

    times(xp, 8, emit_query)
    save(qc, qc_o)
    x_over(1 - y).wait_recv()
    for k in range(8):
        mem[k // 4, TEXT * (k % 4) : TEXT * (k % 4) + TEXT, :] = text[k // 2, k % 2]
    save(mem, mem_o)
    attnf[...] = jnp.zeros_like(attnf)

    def cross_heads(h):
        text_heads_forward(h, qc, mem.at[0], mem.at[1], attnf, cross_bias(), cross_rows(seg_in))

    loop(4, cross_heads)
    poke()
    loop(4, lambda h: cross_heads(h + 4))
    xin[...] = attnf[...]
    turned(xin, 5)
    load(9)
    times(xp, 9, emit_branch)

    def after_cross(rows):
        seg = seg_in[0, rows, 0:1]
        value = stream[rows, :] + branchw[rows, :]
        stream[rows, :] = value
        xin[rows, :] = to_low(normal(value, rows, 3) * (1.0 + pick(7, seg)) + pick(6, seg))
        gfour[rows, :] = to_low(wide32(cotp[rows, :]) * pick(8, seg))

    each_rows(32, after_cross)
    save(xhat.at[3], xhat_o.at[3])
    save(rstd.at[3], rstd_o.at[3])
    save(gfour, gfour_o)

    turned(xin, 4)
    same = (
        lax.broadcasted_iota(jnp.int32, (TILE, TILE), 0) == lax.broadcasted_iota(jnp.int32, (TILE, TILE), 1)
    ).astype(jnp.float32).astype(jnp.bfloat16)
    for k in range(4):
        slot = k % 2
        load(10 + 2 * k)
        settle(SLOPE_SEM + slot)
        settle(LEFT_SEM + slot)

        def emit_hidden(cols, value, slot=slot):
            inner = math.sqrt(2.0 / math.pi) * (value + 0.044715 * value * value * value)
            bent = jnp.tanh(inner)
            half = 0.5 * (1.0 + bent)
            tilt = math.sqrt(2.0 / math.pi) * (1.0 + 3 * 0.044715 * value * value)
            slope[slot, :, cols] = to_low(half + 0.5 * value * (1.0 - bent * bent) * tilt)
            low = to_low(value * half)
            post[:, cols] = low
            left[slot, cols, :] = to_low(nt(same, low))

        times(xp, 10 + 2 * k, emit_hidden)
        save(slope.at[slot], slope_o.at[k], SLOPE_SEM + slot)
        save(left.at[slot], left_o.at[k], LEFT_SEM + slot)
        load(11 + 2 * k)

        def emit_out(cols, value, k=k):
            branchw[:, cols] = value if k == 0 else branchw[:, cols] + value

        times(post, 11 + 2 * k, emit_out)

    gate[...] = jnp.zeros_like(gate)

    def last(rows):
        seg = seg_in[0, rows, 0:1]
        value = branchw[rows, :]
        xin[rows, :] = to_low(stream[rows, :] + pick(8, seg) * value)
        value = wide32(cotp[rows, :]) * value
        later = jnp.sum(value * seg, axis=0, keepdims=True)
        every = jnp.sum(value, axis=0, keepdims=True)
        gate[0:1, :] = gate[0:1, :] + (every - later)
        gate[1:2, :] = gate[1:2, :] + later

    each_rows(32, last)
    save(gate, gate_o)
    out[...] = to_low(linear(swap_rows(), xin[...]))

    for copy in held.values():
        copy.wait()
    for k in range(1, 8):
        t_copy(k).wait_send()
        m_copy(k, b).wait_send()
    for k in (1, 2, 3):
        x_copy(k, z).wait_send()
    x_over(y).wait_send()
    for at, to in ((0, twin), (1, first), (2, second)):
        g_copy(at, at, to).wait_send()
    for k in (1, 2, 3):
        remote(gains.at[3], gain_at.at[2 + k], g_send.at[2 + k], g_recv.at[2 + k], near[k - 1]).wait_send()

    for t in range(BLOCKS - HELD, BLOCKS):
        for index in range(3):
            sends(t, index).wait_send()

    def finish(t):
        z_one(t).wait_send()
        for index in range(3, 7):
            sends(t, index).wait_send()

    loop(BLOCKS, finish)


ANY = pl.BlockSpec(memory_space=pl.ANY)
IN_VMEM = pl.BlockSpec(memory_space=pltpu.VMEM)


def forward(*operands):
    low, full = jnp.bfloat16, jnp.float32
    dma = pltpu.SemaphoreType.DMA
    hbm = [
        ((BLOCKS, WIDE, WIDE), low),
        ((ROWS, WIDE), low),
        ((11, WIDE, ROWS), low),
        ((3, ROWS, WIDE), low),
        ((3, ROWS, WIDE), low),
        ((ROWS, WIDE), low),
        ((2, WIDE, KEYS), low),
        ((4, ROWS, WIDE), low),
        ((4, ROWS, 128), full),
        ((2, ROWS, WIDE), low),
        ((4, ROWS, WIDE), low),
        ((ROWS, WIDE), low),
        ((ROWS, WIDE), low),
        ((8, MOD), full),
        ((8, WIDE), full),
        ((8, WIDE), full),
    ]
    vmem = [
        ((PARTS, WINDOW, WIDE), low),
        ((PARTS, PAIR, WIDE), low),
        ((PARTS, PAIR, WIDE), low),
        ((HELD, LINE, WIDE), low),
        ((2, WIDE, WIDE), low),
        ((ROWS, WIDE), low),
        ((ROWS, WIDE), low),
        ((8, 32, WIDE), low),
        ((ROWS, WIDE), low),
        ((ROWS, WIDE), low),
        ((2, WIDE, ROWS), low),
        ((3, ROWS, WIDE), low),
        ((3, ROWS, WIDE), low),
        ((ROWS, WIDE), low),
        ((2, WIDE, KEYS), low),
        ((4, 2, TEXT, KEYS), low),
        ((8, 32, 128), low),
        ((8, MOD), full),
        ((4, ROWS, WIDE), low),
        ((4, ROWS, 128), full),
        ((2, ROWS, WIDE), low),
        ((ROWS, WIDE), full),
        ((128, 128), full),
        ((ROWS, WIDE), full),
        ((ROWS, WIDE), low),
        ((16, 16, WIDE), low),
        ((ROWS, WIDE), low),
        ((2, ROWS, WIDE), low),
        ((ROWS, WIDE), low),
        ((5, 8, WIDE), full),
        ((6, 8, WIDE), full),
        ((8, WIDE), full),
        ((BLOCKS, WINDOW, WIDE), low),
        ((ROWS, WIDE), low),
        ((WIDE, WIDE), low),
        ((MOD // 8, WIDE), low),
        ((2, L, 4096), low),
        ((TEXT, 4096), low),
        ((32, 128), low),
        ((TEXT, KEYS), low),
        ((4, SHARD, WIDE), full),
    ]
    return pl.pallas_call(
        forward_kernel,
        out_shape=[jax.ShapeDtypeStruct(*shape) for shape in hbm],
        in_specs=[IN_VMEM] * 14 + [ANY] * 5,
        out_specs=[ANY, IN_VMEM] + [ANY] * 14,
        scratch_shapes=[pltpu.VMEM(*shape) for shape in vmem]
        + [
            dma((BLOCKS, 3)), dma((BLOCKS, 3)), dma((BLOCKS, 7)), dma((BLOCKS, 7)), dma((BLOCKS,)), dma((2,)),
            dma((7,)), dma((7,)), dma((7, 2)), dma((7, 2)), dma((7,)), dma((7,)), dma((4,)), dma((4,)),
            dma((6,)), dma((6,)), dma((SAVE_SEMS,)), dma((5,)),
        ],
        compiler_params=pltpu.CompilerParams(
            collective_id=0, has_side_effects=True, vmem_limit_bytes=60 * MIB
        ),
        name="forward",
    )(*operands)


def tn(left, right):
    return lax.dot_general(
        left, right, (((0,), (0,)), ((), ())), preferred_element_type=jnp.float32
    )


def text_heads_backward(h, query, key, value, grad, dquery, dkey, dvalue, bias, mask):
    jobs = chains(h, VIDEOS)
    scores, grads = [], []
    for (lanes, on), rows, keys in jobs:
        low_on = to_low(on)
        scores.append(linear(query[rows, lanes] * low_on, key[lanes, keys]))
        grads.append(linear(grad[rows, lanes] * low_on, value[lanes, keys]))
    probs = soft(jnp.concatenate(scores), bias, mask)
    grad_probs = jnp.concatenate(grads)
    delta = jnp.sum(grad_probs * probs, axis=-1, keepdims=True)
    slopes = split_rows(to_low(probs * (grad_probs - delta)), jobs)
    probs = split_rows(to_low(probs), jobs)
    parts = []
    for slope, prob, ((lanes, on), rows, keys) in zip(slopes, probs, jobs):
        low_on = to_low(on)
        parts.append(
            (
                to_low(nt(slope, key[lanes, keys]) * (on * SCALE)),
                to_low(tn(query[rows, lanes] * low_on, slope) * SCALE),
                to_low(tn(grad[rows, lanes] * low_on, prob)),
            )
        )
    for (by_query, by_key, by_value), ((lanes, on), rows, keys) in zip(parts, jobs):
        dquery[rows, lanes] = dquery[rows, lanes] + by_query
        dkey[lanes, keys] = dkey[lanes, keys] + by_key
        dvalue[lanes, keys] = dvalue[lanes, keys] + by_value


def heads_backward(h, query, key, value, grad, dquery, dkey, dvalue, groups, bias, mask):
    jobs = chains(h, groups)
    scores, grads = [], []
    for (lanes, on), rows, keys in jobs:
        low_on = to_low(on)
        scores.append(nt(query[rows, lanes] * low_on, key[keys, lanes]))
        grads.append(nt(grad[rows, lanes] * low_on, value[keys, lanes]))
    probs = soft(jnp.concatenate(scores), bias, mask)
    grad_probs = jnp.concatenate(grads)
    delta = jnp.sum(grad_probs * probs, axis=-1, keepdims=True)
    slopes = split_rows(to_low(probs * (grad_probs - delta)), jobs)
    probs = split_rows(to_low(probs), jobs)
    parts = []
    for slope, prob, ((lanes, on), rows, keys) in zip(slopes, probs, jobs):
        parts.append(
            (
                to_low(linear(slope, key[keys, lanes]) * (on * SCALE)),
                to_low(tn(slope, query[rows, lanes]) * (on * SCALE)),
                to_low(tn(prob, grad[rows, lanes]) * on),
            )
        )
    for (by_query, by_key, by_value), ((lanes, on), rows, keys) in zip(parts, jobs):
        dquery[rows, lanes] = dquery[rows, lanes] + by_query
        dkey[keys, lanes] = dkey[keys, lanes] + by_key
        dvalue[keys, lanes] = dvalue[keys, lanes] + by_value


def backward_kernel(
    wide, left_i, qkvs_i, qkvt_i, qc_i, mem_i, xhat_i, rstd_i, branch_i, slope_i, gfour_i, cot_i, mods_i, gate_i, gain_i,
    caption_i, seg_in, seg_row, turn, cond_in,
    total, gtok, gain_o, caption_o, mod_o,
    weights, left, right, qkv, xhat, rstd, branch, slope, mods, gain, bias, stream, work, grad, xin, gm, mem, dmem, text, text_at, text_sum, cap, cap_out, cap_in, cap_own, cap_at, mod_out, mod,
    seqs, gains, gain_at, gframe, back,
    s0, r0, s1, r1, s2, r2, k2, s3, pass_in, pass_out, far_in, close, close_in, share,
    in_sem, w_sem, s0_sem, r0_sem, s1_sem, r1_sem, s2_sem, r2_sem, z_send, z_recv, share_sem,
    a_send, a_recv, u_send, u_recv, x_send, x_recv, m_send, m_recv, q_send, q_recv, g_send, g_recv,
    cap_sem, c_send, c_recv, left_sem,
):
    x, c, y, z, x1, y1, x2, y2 = place()
    b = z * 2 + y
    near = [device(x, c, y, (z + k) % 4) for k in (1, 2, 3)]
    first, second, twin = device(x1, c, y1, z), device(x2, c, y2, z), device(x, 1 - c, y, z)
    peers = blk_peers(x, c, b)
    across = [twin, device(1 - x, c, y, z), device(1 - x, 1 - c, y, z)]
    greet(peers + across)

    fetches = {}

    def fetch(name, from_ref, to_ref):
        fetches[name] = pltpu.make_async_copy(from_ref, to_ref, in_sem.at[name])
        fetches[name].start()

    def have(name):
        if name in fetches:
            fetches.pop(name).wait()

    fetch(0, gfour_i, right.at[0])
    for k in range(4):
        fetch(1 + k, left_i.at[k], left.at[k])
    fetch(12, mods_i, mods)
    fetch(13, gain_i, gain)
    fetch(14, slope_i.at[0], slope.at[0])
    fetch(15, slope_i.at[1], slope.at[1])
    fetch(16, xhat_i.at[3], xhat.at[1])
    fetch(17, rstd_i.at[3], rstd.at[1])
    fetch(18, cot_i, xin)
    fetch(19, gate_i, work.at[0:8])

    def weight(block):
        slot = WEIGHT_ORDER.index(block) % 2
        return weights.at[slot]

    def prefetch(at):
        if at < len(WEIGHT_ORDER):
            copy = pltpu.make_async_copy(wide.at[WEIGHT_ORDER[at]], weights.at[at % 2], w_sem.at[at % 2])
            copy.start()
            fetches["w", WEIGHT_ORDER[at]] = copy

    def release(block):
        prefetch(WEIGHT_ORDER.index(block) + 2)

    prefetch(0)
    prefetch(1)

    away = [(1 - x) * 2 + 1 - y, x2 * 2 + y2]
    stay = [x1 * 2 + y1, x * 2 + y]

    def product(t, core, xl):
        rows = pl.ds(pl.multiple_of(line_of(core, xl, 0) * LINE, 16), 2 * LINE)
        return linear(left[left_at(t) % 4, rows, :], right[right_at(t)])

    def left_copy(t):
        return pltpu.make_async_copy(left_i.at[left_at(t)], left.at[left_at(t) % 4], left_sem.at[0])

    def left_next(t):
        return (t >= 4) & (t < BLOCKS) & (left_at(t) != left_at(t - 1))

    def copy0(t, l):
        pair = pl.ds(2 * l, 2)
        return remote(s0.at[t % 2, pair], r0.at[t % 4, pair], s0_sem.at[t % 2, l], r0_sem.at[t % 4, l], twin)

    def copy1(t, l):
        return remote(s1.at[t % 2, away[l]], r1.at[t % 4, l], s1_sem.at[t % 2, l], r1_sem.at[t % 4, l], second)

    def copy2(t):
        return remote(s2.at[t % 2], r2.at[t % 4], s2_sem.at[t % 2], r2_sem.at[t % 4], first)

    beside, opposite = device(x, c, y, z + 1 - 2 * (z % 2)), device(x, c, y, 3 - z)
    middle = (z == 1) | (z == 2)
    near_rows = pl.ds(pl.multiple_of(64 * (z // 2), 16), PAIR)
    far_rows = pl.ds(pl.multiple_of(64 - 64 * (z // 2), 16), PAIR)
    own_rows = pl.ds(pl.multiple_of(32 * (z % 2), 16), WINDOW)
    beside_rows = pl.ds(pl.multiple_of(32 - 32 * (z % 2), 16), WINDOW)

    def z_one(t):
        return remote(s3.at[t % 4, far_rows], pass_in.at[t % 4], z_send.at[0, t % 4], z_recv.at[0, t % 4], beside)

    def z_two(t):
        return remote(pass_out.at[t % 2], far_in.at[t % 4], z_send.at[1, t % 4], z_recv.at[1, t % 4], opposite)

    def z_three(t):
        return remote(
            close.at[t % 2, beside_rows], close_in.at[t % 4], z_send.at[2, t % 4], z_recv.at[2, t % 4], beside
        )

    def share_copy(t):
        return pltpu.make_async_copy(share.at[t % 2], total.at[t], share_sem.at[t % 2])

    def tick(t):
        @pl.when(t >= 10)
        def _():
            now = t - 10
            z_three(now).wait_recv()
            value = wide32(close[now % 2, own_rows]) + wide32(close_in[now % 4])

            @pl.when(jnp.logical_not(middle))
            def _():
                z_one(now).wait_send()

            @pl.when(now >= 2)
            def _():
                share_copy(now - 2).wait()
            share[now % 2] = value
            share_copy(now).start()

        @pl.when((t >= 8) & (t < BLOCKS + 8))
        def _():
            now = t - 8

            @pl.when(now >= 2)
            def _():
                z_three(now - 2).wait_send()

            @pl.when(middle)
            def _():
                z_two(now).wait_recv()
                close[now % 2] = to_low(wide32(s3[now % 4, near_rows]) + wide32(far_in[now % 4]))

            @pl.when(jnp.logical_not(middle))
            def _():
                close[now % 2] = s3[now % 4, near_rows]

            z_three(now).start()

        @pl.when((t >= 7) & (t < BLOCKS + 7) & middle)
        def _():
            now = t - 7
            z_one(now).wait_recv()

            @pl.when(now >= 2)
            def _():
                z_two(now - 2).wait_send()
            pass_out[now % 2] = to_low(wide32(s3[now % 4, far_rows]) + wide32(pass_in[now % 4]))
            z_two(now).start()

        @pl.when((t >= 6) & (t < BLOCKS + 6))
        def _():
            now = t - 6
            copy2(now).wait_recv()
            s3[now % 4] = to_low(k2[now % 2] + wide32(r2[now % 4]))

            @pl.when(jnp.logical_not(middle))
            def _():
                z_one(now).start()

        @pl.when((t >= 4) & (t < BLOCKS + 4))
        def _():
            now = t - 4
            copy1(now, 0).wait_recv()

            @pl.when(now >= 2)
            def _():
                copy2(now - 2).wait_send()
            s2[now % 2] = to_low(wide32(s1[now % 2, stay[0]]) + wide32(r1[now % 4, 0]))
            copy2(now).start()
            copy1(now, 1).wait_recv()
            k2[now % 2] = wide32(s1[now % 2, stay[1]]) + wide32(r1[now % 4, 1])

        @pl.when((t >= 2) & (t < BLOCKS + 2))
        def _():
            now = t - 2

            @pl.when(now >= 2)
            def _():
                for l in range(2):
                    copy1(now - 2, l).wait_send()
            for l in range(2):
                copy0(now, l).wait_recv()
                value = product(now, c, l)
                for part in range(2):
                    line = 2 * l + part
                    summed = value[part * LINE : part * LINE + LINE] + wide32(r0[now % 4, line])
                    s1[now % 2, line] = to_low(summed)
            for l in range(2):
                copy1(now, l).start()

        @pl.when(left_next(t))
        def _():
            left_copy(t).wait()

        @pl.when(t < BLOCKS)
        def _():
            for l in range(2):
                @pl.when(t >= 2)
                def _():
                    copy0(t - 2, l).wait_send()
                value = to_low(product(t, 1 - c, l))
                s0[t % 2, 2 * l] = value[:LINE]
                s0[t % 2, 2 * l + 1] = value[LINE:]
                copy0(t, l).start()

        @pl.when(left_next(t + 1))
        def _():
            left_copy(t + 1).start()

    done = [0]

    def pump(until):
        if until > done[0]:
            start = done[0]
            loop(until - start, lambda i: tick(i + start))
            done[0] = until

    def pick(piece, seg):
        lanes = slice(WIDE * piece, WIDE * piece + WIDE)
        return jnp.where(seg > 0.5, mods[1:2, lanes], mods[0:1, lanes])

    def by_video(piece, value, seg):
        lanes = slice(WIDE * piece, WIDE * piece + WIDE)
        later = jnp.sum(value * seg, axis=0, keepdims=True)
        every = jnp.sum(value, axis=0, keepdims=True)
        gm[0:1, lanes] = gm[0:1, lanes] + (every - later)
        gm[1:2, lanes] = gm[1:2, lanes] + later

    def through(values_at, blocks, emit, grouped=False):
        for n, (values, block) in enumerate(zip(values_at, blocks)):
            have(("w", block))

            def tile(cols, n=n, values=values, block=block):
                part = nt(values[...], weight(block)[cols, :])
                if n > 0:
                    part = part + work[:, cols]
                if n == len(blocks) - 1:
                    xin[:, cols] = to_low(part)
                else:
                    work[:, cols] = part

            each_cols(tile)
            release(block)
        if grouped:
            xin[...] = to_low(linear(regroup(True), xin[...]))
        turn_back(emit)

    def turn_back(emit):
        each_cols(lambda cols: emit(cols, linear(xin[...], turn[:, cols])))

    def emit_work(cols, value):
        work[:, cols] = value

    def emit_grad(cols, value):
        grad[:, cols] = to_low(value)

    def norm_back(grad_in, tilt, at, rows):
        slope_in = grad_in * tilt
        hat = wide32(xhat[at, rows, :])
        first_mean = jnp.mean(slope_in, axis=-1, keepdims=True)
        second_mean = jnp.mean(slope_in * hat, axis=-1, keepdims=True)
        return rstd[at, rows, 0:1] * (slope_in - first_mean - hat * second_mean)

    gm[...] = jnp.zeros_like(gm)
    have(0)
    have(12)
    have(18)
    have(19)
    gm[0:8, 8 * WIDE : 9 * WIDE] = work[0:8]
    stream[...] = wide32(xin[...])
    for k in range(4):
        have(1 + k)
    pump(2)
    for k in range(4):
        have(14 + k % 2 if k < 2 else ("slope", k))
        have(("w", 11 + 2 * k))

        def tile(cols, k=k):
            value = nt(right[0], weight(11 + 2 * k)[cols, :]) * wide32(slope[k % 2, :, cols])
            right[1 + k, :, cols] = to_low(value)

        each_cols(tile)
        release(11 + 2 * k)
        if k < 2:
            copy = pltpu.make_async_copy(slope_i.at[k + 2], slope.at[k % 2], in_sem.at[14 + k])
            copy.start()
            fetches["slope", k + 2] = copy
        have(("w", 10 + 2 * k))

        def tile(cols, k=k):
            part = nt(right[1 + k], weight(10 + 2 * k)[cols, :])
            if k > 0:
                part = part + work[:, cols]
            if k < 3:
                work[:, cols] = part
            else:
                xin[:, cols] = to_low(part)

        each_cols(tile)
        release(10 + 2 * k)
        pump(k + 3)
    turn_back(emit_work)
    have(16)
    have(17)
    fetch(20, qc_i, qkv.at[0])
    fetch(21, mem_i.at[0], mem.at[0])
    fetch(22, mem_i.at[1], mem.at[1])
    fetch(23, xhat_i.at[2], xhat.at[0])
    fetch(24, rstd_i.at[2], rstd.at[0])

    def after_mlp(rows):
        seg = seg_in[0, rows, 0:1]
        value = work[rows, :]
        by_video(6, value, seg)
        by_video(7, value * wide32(xhat[1, rows, :]), seg)
        value = stream[rows, :] + norm_back(value, 1.0 + pick(7, seg), 1, rows)
        stream[rows, :] = value
        right[5, rows, :] = to_low(value)

    each_rows(32, after_mlp)

    fetch(25, xhat_i.at[1], xhat.at[1])
    fetch(26, rstd_i.at[1], rstd.at[1])
    through([right.at[5]], [9], emit_grad)
    right[6] = jnp.zeros_like(right[6])
    dmem[...] = jnp.zeros_like(dmem)
    for name in (13, 20, 21, 22, 23, 24):
        have(name)

    def cross_heads(h):
        text_heads_backward(
            h, qkv.at[0], mem.at[0], mem.at[1], grad, right.at[6], dmem.at[0], dmem.at[1],
            cross_bias(), cross_rows(seg_in),
        )

    for part in range(4):
        loop(2, lambda h: cross_heads(h + 2 * part))
        pump(7 + (part + 1) // 2)

    def dmem_part(zp, yp):
        return dmem.at[zp // 2, pl.ds(pl.multiple_of(TEXT * (zp % 2 * 2 + yp), 16), TEXT)]

    def x_over(zp):
        return remote(dmem_part(zp, 1 - y), text.at[zp], x_send.at[zp], x_recv.at[zp], device(x, c, 1 - y, z))

    def x_copy(k):
        return remote(text.at[(z + k) % 4], text_at.at[k - 1], x_send.at[3 + k], x_recv.at[3 + k], near[k - 1])

    for zp in range(4):
        x_over(zp).start()
    fetch(27, qkvt_i.at[0], qkv.at[0])
    fetch(28, qkvt_i.at[1], qkv.at[1])
    fetch(29, qkvt_i.at[2], qkv.at[2])
    fetch(30, branch_i.at[1], branch)
    through([right.at[6]], [8], emit_work)
    gains[0] = jnp.zeros_like(gains[0])
    have(30)

    def after_cross(rows):
        seg = seg_in[0, rows, 0:1]
        value = work[rows, :]
        gains[0, 0:1, :] = gains[0, 0:1, :] + jnp.sum(value * wide32(xhat[0, rows, :]), axis=0, keepdims=True)
        value = stream[rows, :] + norm_back(value, gain[0:1, :], 0, rows)
        stream[rows, :] = value
        by_video(5, value * wide32(branch[rows, :]), seg)
        right[7, rows, :] = to_low(value * pick(5, seg))

    each_rows(32, after_cross)

    def g_copy(at, to):
        return remote(gains.at[min(at, 3)], gain_at.at[at], g_send.at[at], g_recv.at[at], to)

    g_copy(0, twin).start()
    fetch(31, branch_i.at[0], branch)
    fetch(32, xhat_i.at[0], xhat.at[0])
    fetch(33, rstd_i.at[0], rstd.at[0])
    pump(10)

    through([right.at[7]], [7], emit_grad)
    grad[...] = to_low(linear(regroup(False), grad[...]))
    bias[...] = temporal_bias(seg_in, seg_row)
    for j in range(3):
        right[8 + j] = jnp.zeros_like(right[8 + j])
    for name in (25, 26, 27, 28, 29):
        have(name)

    def temporal_heads(h):
        heads_backward(
            h, qkv.at[0], qkv.at[1], qkv.at[2], grad, right.at[8], right.at[9], right.at[10],
            HALVES, jnp.concatenate([bias[...]] * 4), None,
        )

    loop(4, temporal_heads)
    pump(11)
    g_copy(0, twin).wait_recv()
    gains[1] = gains[0] + gain_at[0]
    g_copy(1, first).start()
    loop(4, lambda h: temporal_heads(h + 4))
    pump(12)
    g_copy(1, first).wait_recv()
    gains[2] = gains[1] + gain_at[1]
    g_copy(2, second).start()
    for zp in range(4):
        x_over(zp).wait_recv()
        text[zp] = to_low(wide32(dmem_part(zp, y)[...]) + wide32(text[zp]))
    for k in (1, 2, 3):
        x_copy(k).start()
    for j in range(3):
        fetch(34 + j, qkvs_i.at[j], qkv.at[j])
    through([right.at[8], right.at[9], right.at[10]], [4, 5, 6], emit_work, True)
    have(31)

    def after_temporal(rows):
        seg = seg_in[0, rows, 0:1]
        value = work[rows, :]
        by_video(3, value, seg)
        by_video(4, value * wide32(xhat[1, rows, :]), seg)
        value = stream[rows, :] + norm_back(value, 1.0 + pick(4, seg), 1, rows)
        stream[rows, :] = value
        by_video(2, value * wide32(branch[rows, :]), seg)
        right[1, rows, :] = to_low(value * pick(2, seg))

    each_rows(32, after_temporal)

    through([right.at[1]], [3], emit_grad)

    def a_copy(k):
        to = (b + k) % 8
        part = grad.at[pl.ds(pl.multiple_of(32 * to, 32), 32)]
        return remote(part, back.at[b], a_send.at[k - 1], a_recv.at[k - 1], peers[k - 1])

    def a_wait(k):
        of = (b + 8 - k) % 8
        remote(grad.at[pl.ds(0, 32)], back.at[of], a_send.at[k - 1], a_recv.at[k - 1], peers[k - 1]).wait_recv()

    for k in (1, 2, 3):
        x_copy(k).wait_recv()
    text_sum[...] = to_low(wide32(text[z]) + wide32(text_at[0]) + wide32(text_at[1]) + wide32(text_at[2]))
    for k in range(1, 8):
        a_copy(k).start()

    def cap_fetch(n):
        quarter = [1 - c, 3 - c, c, 2 + c][n]
        lanes = pl.ds(pl.multiple_of(QUARTER * quarter, 128), QUARTER)
        return pltpu.make_async_copy(caption_i.at[:, :, lanes], cap.at[n % 2], cap_sem.at[n % 2])

    over_x = across[1]
    quarters = [x * 2 + c, (1 - x) * 2 + c, x * 2 + 1 - c, (1 - x) * 2 + 1 - c]

    def c_copy(n):
        from_ref, to_ref, to = (
            (cap_out.at[0], cap_in.at[0], twin),
            (cap_out.at[1], cap_in.at[1], twin),
            (cap_own.at[1 - x], cap_at, over_x),
            (cap_own.at[x], caption_o.at[quarters[0]], over_x),
            (cap_own.at[x], caption_o.at[quarters[0]], twin),
            (caption_o.at[quarters[1]], caption_o.at[quarters[1]], twin),
        )[n]
        return remote(from_ref, to_ref, c_send.at[n], c_recv.at[n], to)

    cap_fetch(0).start()
    cap_fetch(1).start()
    for n in range(4):
        cap_fetch(n).wait()
        part = linear(text_sum[:, 0:L], cap[n % 2, 0]) + linear(text_sum[:, 128 : 128 + L], cap[n % 2, 1])
        if n < 2:
            cap_out[n] = to_low(part)
            c_copy(n).start()
            cap_fetch(n + 2).start()
        else:
            cap_own[n - 2] = to_low(part)
    back[b] = grad[pl.ds(pl.multiple_of(32 * b, 32), 32)]
    pump(13)
    g_copy(2, second).wait_recv()
    gains[3] = gains[2] + gain_at[2]
    for k in (1, 2, 3):
        g_copy(2 + k, near[k - 1]).start()
    for j in range(3):
        right[2 + j] = jnp.zeros_like(right[2 + j])
    for name in (32, 33, 34, 35, 36):
        have(name)
    for k in range(1, 8):
        a_wait(k)
    for k in range(8):
        for f in range(2):
            gframe[128 * f + 16 * k : 128 * f + 16 * k + 16, :] = back[k, 16 * f : 16 * f + 16, :]

    def spatial_heads(h):
        heads_backward(
            h, qkv.at[0], qkv.at[1], qkv.at[2], gframe, right.at[2], right.at[3], right.at[4], HALVES, None, None
        )

    loop(4, spatial_heads)
    pump(14)
    for n in range(2):
        c_copy(n).wait_recv()
        cap_own[n] = to_low(wide32(cap_own[n]) + wide32(cap_in[n]))
    c_copy(2).start()
    loop(4, lambda h: spatial_heads(h + 4))
    pump(15)
    through([right.at[2], right.at[3], right.at[4]], [0, 1, 2], emit_work)
    pump(16)
    for k in range(1, 8):
        a_copy(k).wait_send()

    def after_spatial(i):
        rows = pl.ds(pl.multiple_of(16 * i, 16), 16)
        seg = seg_in[1, rows, 0:1]
        value = work[rows, :]
        by_video(0, value, seg)
        by_video(1, value * wide32(xhat[0, rows, :]), seg)
        value = to_low(norm_back(value, 1.0 + pick(1, seg), 0, rows))
        back[i % 8, pl.ds(pl.multiple_of(16 * (i // 8), 16), 16), :] = value

    loop(16, after_spatial)
    c_copy(2).wait_recv()
    cap_own[x] = to_low(wide32(cap_own[x]) + wide32(cap_at[...]))
    c_copy(3).start()
    c_copy(4).start()
    keep_quarter = pltpu.make_async_copy(cap_own.at[x], caption_o.at[quarters[0]], cap_sem.at[0])
    keep_quarter.start()

    def branch_part(of):
        return branch.at[pl.ds(pl.multiple_of(32 * of, 32), 32)]

    def u_copy(k):
        to = (b + k) % 8
        return remote(back.at[to], branch_part(b), u_send.at[k - 1], u_recv.at[k - 1], peers[k - 1])

    def u_wait(k):
        of = (b + 8 - k) % 8
        remote(back.at[0], branch_part(of), u_send.at[k - 1], u_recv.at[k - 1], peers[k - 1]).wait_recv()

    def m_copy(k):
        to = (b + k) % 8
        return remote(mod_out.at[to], mod.at[b], m_send.at[k - 1], m_recv.at[k - 1], peers[k - 1])

    def m_wait(k):
        of = (b + 8 - k) % 8
        remote(mod_out.at[0], mod.at[of], m_send.at[k - 1], m_recv.at[k - 1], peers[k - 1]).wait_recv()

    for k in range(1, 8):
        u_copy(k).start()
    branch[pl.ds(pl.multiple_of(32 * b, 32), 32), :] = back[b]
    for k in range(8):
        tiles = [
            gm[row : row + 1, 1280 * k + 128 * tile : 1280 * k + 128 * tile + 128]
            for row in range(2)
            for tile in range(MOD_TILES)
        ]
        mod_out[k] = to_low(jnp.concatenate(tiles + [jnp.zeros((32 - 2 * MOD_TILES, 128), jnp.float32)]))
    for k in range(1, 8):
        m_copy(k).start()
    mod[b] = mod_out[b]
    pump(18)
    for k in range(1, 8):
        m_wait(k)
    summed = wide32(mod[0])
    for k in range(1, 8):
        summed = summed + wide32(mod[k])
    own = x * 2 + c
    seqs[own, 0:32] = to_low(summed)
    seqs[own, 32:64] = cond_in[...]
    places = [x * 2 + 1 - c, (1 - x) * 2 + c, (1 - x) * 2 + 1 - c]

    def q_copy(k, at):
        return remote(seqs.at[own], seqs.at[at], q_send.at[k], q_recv.at[k], across[k])

    for k in range(3):
        q_copy(k, own).start()
    for k in range(1, 8):
        u_wait(k)
    xin[...] = to_low(stream[...] + wide32(branch[...]))
    gtok[...] = to_low(linear(swap_rows(), xin[...]))
    for k in (1, 2, 3):
        g_copy(2 + k, near[k - 1]).wait_recv()
    gain_o[...] = gains[3] + gain_at[3] + gain_at[4] + gain_at[5]
    c_copy(3).wait_recv()
    c_copy(5).start()
    pump(BLOCKS + 10)
    c_copy(4).wait_recv()
    c_copy(5).wait_recv()
    for n in range(6):
        c_copy(n).wait_send()
    keep_quarter.wait()
    for k in range(3):
        q_copy(k, places[k]).wait_recv()
    mod_o[...] = seqs[...]

    for now in (BLOCKS - 2, BLOCKS - 1):
        for l in range(2):
            copy0(now, l).wait_send()
            copy1(now, l).wait_send()
        copy2(now).wait_send()
        z_three(now).wait_send()
        share_copy(now).wait()

        @pl.when(middle)
        def _(now=now):
            z_two(now).wait_send()

    for k in range(1, 8):
        u_copy(k).wait_send()
        m_copy(k).wait_send()
        x_over(k - 1).wait_send() if k < 5 else x_copy(k - 4).wait_send()
    for k in range(3):
        q_copy(k, own).wait_send()
    for at, to in enumerate([twin, first, second] + near):
        g_copy(at, to).wait_send()


QUARTER = 1024
WEIGHT_ORDER = (11, 10, 13, 12, 15, 14, 17, 16, 9, 8, 7, 4, 5, 6, 3, 0, 1, 2)


def backward(*operands):
    low, full = jnp.bfloat16, jnp.float32
    dma = pltpu.SemaphoreType.DMA
    outs = [
        ((BLOCKS, WINDOW, WIDE), full),
        ((ROWS, WIDE), low),
        ((8, WIDE), full),
        ((4, TEXT, QUARTER), low),
        ((4, 64, 128), low),
    ]
    vmem = [
        ((2, WIDE, WIDE), low),
        ((4, WIDE, ROWS), low),
        ((11, ROWS, WIDE), low),
        ((3, ROWS, WIDE), low),
        ((2, ROWS, WIDE), low),
        ((2, ROWS, 128), full),
        ((ROWS, WIDE), low),
        ((2, ROWS, WIDE), low),
        ((8, MOD), full),
        ((8, WIDE), full),
        ((128, 128), full),
        ((ROWS, WIDE), full),
        ((ROWS, WIDE), full),
        ((ROWS, WIDE), low),
        ((ROWS, WIDE), low),
        ((8, MOD), full),
        ((2, WIDE, KEYS), low),
        ((2, WIDE, KEYS), low),
        ((4, TEXT, KEYS), low),
        ((3, TEXT, KEYS), low),
        ((TEXT, KEYS), low),
        ((2, 2, L, QUARTER), low),
        ((2, TEXT, QUARTER), low),
        ((2, TEXT, QUARTER), low),
        ((2, TEXT, QUARTER), low),
        ((TEXT, QUARTER), low),
        ((8, 32, 128), low),
        ((8, 32, 128), low),
        ((4, 64, 128), low),
        ((4, 8, WIDE), full),
        ((6, 8, WIDE), full),
        ((ROWS, WIDE), low),
        ((8, 32, WIDE), low),
        ((2, 4, LINE, WIDE), low),
        ((4, 4, LINE, WIDE), low),
        ((2, 4, LINE, WIDE), low),
        ((4, 2, LINE, WIDE), low),
        ((2, LINE, WIDE), low),
        ((4, LINE, WIDE), low),
        ((2, LINE, WIDE), full),
        ((4, LINE, WIDE), low),
        ((4, PAIR, WIDE), low),
        ((2, PAIR, WIDE), low),
        ((4, PAIR, WIDE), low),
        ((2, PAIR, WIDE), low),
        ((4, WINDOW, WIDE), low),
        ((2, WINDOW, WIDE), full),
    ]
    return pl.pallas_call(
        backward_kernel,
        out_shape=[jax.ShapeDtypeStruct(*shape) for shape in outs],
        in_specs=[ANY] * 16 + [IN_VMEM] * 4,
        out_specs=[ANY] + [IN_VMEM] * 2 + [ANY, IN_VMEM],
        scratch_shapes=[pltpu.VMEM(*shape) for shape in vmem]
        + [
            dma((40,)), dma((2,)), dma((2, 4)), dma((4, 4)), dma((2, 2)), dma((4, 2)), dma((2,)), dma((4,)),
            dma((3, 4)), dma((3, 4)), dma((2,)), dma((7,)), dma((7,)), dma((7,)), dma((7,)), dma((7,)), dma((7,)),
            dma((7,)), dma((7,)), dma((3,)), dma((3,)), dma((6,)), dma((6,)), dma((2,)), dma((6,)), dma((6,)), dma((1,)),
        ],
        compiler_params=pltpu.CompilerParams(
            collective_id=1, has_side_effects=True, vmem_limit_bytes=63 * MIB
        ),
        name="backward",
    )(*operands)


def finish_kernel(
    spread, caption_in, mod_in, gain_in,
    ada_o, bias_o, spatial_o, spatial_out_o, temporal_o, temporal_out_o, gain_o, query_o, caption_o, cross_o, hidden_o,
    hidden_out_o,
):
    seq, blk = lax.axis_index("seq"), lax.axis_index("blk")

    def share(t):
        return pltpu.roll(spread[t], (WINDOW - 4 * (blk // 2)) % WINDOW, 0)[0:SHARD]

    for j in range(3):
        lanes = slice(WIDE * j, WIDE * j + WIDE)
        spatial_o[:, lanes] = share(15 + j)
        temporal_o[:, lanes] = share(11 + j)
    spatial_out_o[...] = share(14)
    temporal_out_o[...] = share(10)
    query_o[...] = share(9)
    cross_o[...] = share(8)
    hidden = [share(4 + k) for k in range(4)]
    hidden_o[...] = jnp.zeros_like(hidden_o)
    for k, natural, placed in hidden_places():
        move_lanes(hidden_o, hidden[k], placed, natural, 4 * WIDE)
    for k in range(4):
        hidden_out_o[SHARD * k : SHARD * k + SHARD, :] = share(k)
    gain_o[...] = pltpu.roll(gain_in[...], (WIDE - SHARD * (seq * 8 + blk)) % WIDE, 1)[0:1, 0:SHARD]
    for q in range(4):
        caption_o[:, QUARTER * q : QUARTER * q + QUARTER] = wide32(caption_in[q])
    part = MOD // 8
    mods, conds = [], []
    for pack in range(4):
        rows = wide32(mod_in[pack])
        for video in range(2):
            first = MOD_TILES * video
            mods.append(jnp.concatenate([rows[first + i : first + i + 1] for i in range(MOD_TILES)], axis=1))
            first = 32 + WIDE // 128 * video
            conds.append(jnp.concatenate([rows[first + i : first + i + 1] for i in range(WIDE // 128)], axis=1))
    mods = pltpu.roll(jnp.concatenate(mods), (MOD_WIN - 16 * blk) % MOD_WIN, 1)[:, :part]
    bias_o[...] = jnp.sum(mods, axis=0, keepdims=True)
    ada_o[...] = tn(to_low(mods), to_low(jnp.concatenate(conds)))


def finish(spread, caption, mod, gain):
    full = jnp.float32
    outs = [
        (MOD // 8, WIDE), (1, MOD // 8), (SHARD, 3 * WIDE), (SHARD, WIDE), (SHARD, 3 * WIDE), (SHARD, WIDE),
        (1, SHARD), (SHARD, WIDE), (TEXT, 4 * QUARTER), (SHARD, WIDE), (SHARD, 4 * WIDE), (4 * SHARD, WIDE),
    ]
    return pl.pallas_call(
        finish_kernel,
        out_shape=[jax.ShapeDtypeStruct(shape, full) for shape in outs],
        in_specs=[IN_VMEM] * 4,
        out_specs=[IN_VMEM] * len(outs),
        compiler_params=pltpu.CompilerParams(vmem_limit_bytes=60 * MIB),
        name="finish",
    )(spread, caption, mod, gain)


TURN = np.arange(WIDE)[None, :] == (
    np.arange(WIDE).reshape(2, 2, 4, 2, SHARD).transpose(1, 0, 3, 2, 4).reshape(-1)
)[:, None]


def shards(
    tokens,
    segments,
    timesteps,
    caption,
    cotangent,
    ada_weight,
    ada_bias,
    spatial_in,
    spatial_out,
    temporal_in,
    temporal_out,
    cross_gain,
    cross_query,
    caption_proj,
    cross_out,
    hidden_in,
    hidden_out,
):
    frame_seg = segments[0]
    blk = lax.axis_index("blk")
    conditioning = to_low(jax.nn.silu(time_embedding(timesteps[0], WIDE)))
    cond_in = jnp.pad(conditioning.reshape(2 * WIDE // 128, 128), ((0, 32 - 2 * WIDE // 128), (0, 0)))
    frames = frame_seg.astype(jnp.float32)
    own_frames = lax.dynamic_slice(frames, (2 * blk,), (2,))
    seg_in = jnp.broadcast_to(
        jnp.stack(
            [jnp.repeat(frames, 16), jnp.repeat(own_frames, 128), jnp.tile(jnp.repeat(frames, 8), 2)]
        )[:, :, None],
        (3, ROWS, 128),
    )
    seg_row = jnp.broadcast_to(jnp.repeat(frames, 8)[None], (8, 128))
    turn = jnp.asarray(TURN, jnp.bfloat16)
    wide, out, *kept = forward(
        spatial_in,
        spatial_out,
        temporal_in,
        temporal_out,
        cross_query,
        cross_out,
        hidden_in,
        hidden_out,
        tokens.reshape(ROWS, WIDE),
        jnp.pad(cross_gain[None], ((0, 7), (0, 0))),
        jnp.pad(conditioning, ((0, 14), (0, 0))),
        ada_bias[None],
        seg_in,
        seg_row,
        cotangent.reshape(ROWS, WIDE),
        turn,
        ada_weight.T,
        caption[0],
        caption_proj.T,
    )
    spread, grad_tokens, grad_gain, grad_text, grad_mod = backward(
        wide, *kept, caption[0], seg_in, seg_row, turn, cond_in
    )
    (
        grad_ada,
        grad_bias,
        grad_sin,
        grad_sout,
        grad_tin,
        grad_tout,
        grad_gain,
        grad_query,
        grad_caption,
        grad_cout,
        grad_hin,
        grad_hout,
    ) = finish(spread, grad_text, grad_mod, grad_gain)
    return (
        out.reshape(tokens.shape),
        grad_tokens.reshape(tokens.shape),
        grad_ada.T,
        grad_bias[0],
        grad_sin,
        grad_sout,
        grad_tin,
        grad_tout,
        grad_gain[0],
        grad_query,
        grad_caption.T,
        grad_cout,
        grad_hin,
        grad_hout,
    )


def solution(mesh):
    fast = dict(mesh.shape) == {"seq": 4, "blk": 8}
    return jax.shard_map(
        shards if fast else general_shards,
        mesh=mesh,
        in_specs=(
            P("seq", "blk", None, None),
            P("seq", None),
            P("seq", None),
            P("seq", None, None, None),
            P("seq", "blk", None, None),
            P(None, "blk"),
            P("blk"),
            P(("seq", "blk"), None),
            P(("seq", "blk"), None),
            P(("seq", "blk"), None),
            P(("seq", "blk"), None),
            P(("seq", "blk")),
            P(("seq", "blk"), None),
            P(None, "blk"),
            P(("seq", "blk"), None),
            P(("seq", "blk"), None),
            P(("seq", "blk"), None),
        ),
        out_specs=(
            P("seq", "blk", None, None),
            P("seq", "blk", None, None),
            P(None, "blk"),
            P("blk"),
            P(("seq", "blk"), None),
            P(("seq", "blk"), None),
            P(("seq", "blk"), None),
            P(("seq", "blk"), None),
            P(("seq", "blk")),
            P(("seq", "blk"), None),
            P(None, "blk"),
            P(("seq", "blk"), None),
            P(("seq", "blk"), None),
            P(("seq", "blk"), None),
        ),
        check_vma=False,
    )
```

```python
import math

import jax
import jax.numpy as jnp
import numpy as np
from jax import lax
from jax.experimental import pallas as pl
from jax.experimental.pallas import tpu as pltpu
from jax.sharding import PartitionSpec as P

H = 16
E = 72
L = 120


EPSILON = 1e-06
MASKED = -1e30


def to_low(values):
    return values.astype(jnp.bfloat16)


def linear(left, right):
    return jnp.dot(left, right, preferred_element_type=jnp.float32)


def left_product(left, right):
    return lax.dot_general(
        left, right, (((0,), (0,)), ((), ())), preferred_element_type=jnp.float32
    )


def right_product(left, right):
    return lax.dot_general(
        left, right, (((1,), (1,)), ((), ())), preferred_element_type=jnp.float32
    )


def normalize(values):
    center = values - jnp.mean(values, axis=-1, keepdims=True)
    return center * lax.rsqrt(jnp.mean(center * center, axis=-1, keepdims=True) + EPSILON)


def modulate(values, shift_rows, scale_rows):
    return normalize(values) * (1.0 + scale_rows) + shift_rows


def gain_norm(values, gain_row):
    return normalize(values) * gain_row


def gelu_tanh(values):
    return jax.nn.gelu(values, approximate=True)


def softmax_rows(scores):
    shifted = jnp.exp(scores - jnp.max(scores, axis=-1, keepdims=True))
    return shifted / jnp.sum(shifted, axis=-1, keepdims=True)


def softmax_with_total(scores):
    top = jnp.max(scores, axis=-1, keepdims=True)
    shifted = jnp.exp(scores - top)
    total = jnp.sum(shifted, axis=-1, keepdims=True)
    return (shifted / total, (top + jnp.log(total))[..., 0])


def softmax_back(probs, grad_probs):
    return probs * (grad_probs - jnp.sum(grad_probs * probs, axis=-1, keepdims=True))


def time_embedding(step_ids, model_width):
    half_width = model_width // 2
    frequency = jnp.exp(
        -math.log(10000.0) * jnp.arange(half_width).astype(jnp.float32) / half_width
    )
    angles = step_ids.astype(jnp.float32)[:, None] * frequency[None, :]
    return jnp.concatenate([jnp.cos(angles), jnp.sin(angles)], axis=1)


def general_shards(
    tokens,
    segments,
    timesteps,
    caption,
    cotangent,
    ada_weight,
    ada_bias,
    spatial_in,
    spatial_out,
    temporal_in,
    temporal_out,
    cross_gain,
    cross_query,
    caption_proj,
    cross_out,
    hidden_in,
    hidden_out,
):
    inputs = tokens[0].astype(jnp.float32)
    patch_dev, frames, model_width = inputs.shape
    token_rows = patch_dev * frames
    head_count = H
    head_size = E
    score_scale = E ** (-0.5)
    frame_seg = segments[0]
    step_ids = timesteps[0]
    seg_count, text_len, text_width = caption.shape[1:]
    text_keys = seg_count * text_len
    caption_rows = caption[0].reshape(text_keys, text_width)
    grad_out = cotangent[0].astype(jnp.float32)
    gathered = (
        lax.all_gather(spatial_in, ("seq", "blk"), axis=0, tiled=True),
        lax.all_gather(spatial_out, ("seq", "blk"), axis=0, tiled=True),
        lax.all_gather(temporal_in, ("seq", "blk"), axis=0, tiled=True),
        lax.all_gather(temporal_out, ("seq", "blk"), axis=0, tiled=True),
        lax.all_gather(cross_gain, ("seq", "blk"), axis=0, tiled=True),
        lax.all_gather(cross_query, ("seq", "blk"), axis=0, tiled=True),
        lax.all_gather(cross_out, ("seq", "blk"), axis=0, tiled=True),
        lax.all_gather(hidden_in, ("seq", "blk"), axis=0, tiled=True),
        lax.all_gather(hidden_out, ("seq", "blk"), axis=0, tiled=True),
    )
    (
        wide_sin,
        wide_sout,
        wide_tin,
        wide_tout,
        gain_low,
        wide_query,
        wide_cout,
        wide_hin,
        wide_hout,
    ) = gathered
    gain_row = gain_low.astype(jnp.float32)
    conditioning = to_low(jax.nn.silu(time_embedding(step_ids, model_width)))
    mod_part = to_low(linear(conditioning, ada_weight) + ada_bias.astype(jnp.float32))
    text_part = to_low(linear(caption_rows, caption_proj))
    modulation, memory = (
        lax.all_gather(mod_part, "blk", axis=1, tiled=True),
        lax.all_gather(text_part, "blk", axis=1, tiled=True),
    )
    choose = frame_seg[:, None] == jnp.arange(seg_count, dtype=jnp.int32)[None, :]
    frame_mod = linear(choose.astype(jnp.bfloat16), modulation)
    pieces = [frame_mod[:, index * model_width : (index + 1) * model_width] for index in range(9)]
    (
        shift_one,
        scale_one,
        gate_one,
        shift_two,
        scale_two,
        gate_two,
        shift_three,
        scale_three,
        gate_three,
    ) = pieces
    spatial_input = to_low(modulate(inputs, shift_one, scale_one)).reshape(token_rows, model_width)
    spatial_qkv = to_low(linear(spatial_input, wide_sin)).reshape(
        patch_dev, frames, 3 * model_width
    )
    query_s = spatial_qkv[..., :model_width].reshape(patch_dev, frames, head_count, head_size)
    local_kv = spatial_qkv[..., model_width:]
    whole_kv = lax.all_gather(local_kv, "blk", axis=0, tiled=True)

    def split_kv(both):
        count = both.shape[0]
        return (
            both[..., :model_width].reshape(count, frames, head_count, head_size),
            both[..., model_width:].reshape(count, frames, head_count, head_size),
        )

    def spatial_probs(key_all):
        scores = jnp.einsum("pfhe,qfhe->fhpq", query_s, key_all, preferred_element_type=jnp.float32)
        return softmax_with_total(scores * score_scale)

    key_s, value_s = split_kv(whole_kv)
    probs_s, log_total_s = spatial_probs(key_s)
    probs_s_low = to_low(probs_s)
    attn_s = to_low(
        jnp.einsum(
            "fhpq,qfhe->pfhe", probs_s_low, value_s, preferred_element_type=jnp.float32
        ).reshape(token_rows, model_width)
    )
    branch_s = linear(attn_s, wide_sout).reshape(patch_dev, frames, model_width)
    after_one = inputs + gate_one * branch_s
    temporal_input = to_low(modulate(after_one, shift_two, scale_two)).reshape(
        token_rows, model_width
    )
    temporal_qkv = to_low(linear(temporal_input, wide_tin)).reshape(
        patch_dev, frames, 3, head_count, head_size
    )
    query_t = temporal_qkv[:, :, 0]
    key_t = temporal_qkv[:, :, 1]
    value_t = temporal_qkv[:, :, 2]
    same_seg = frame_seg[:, None] == frame_seg[None, :]
    scores_t = (
        jnp.einsum("pfhe,pghe->phfg", query_t, key_t, preferred_element_type=jnp.float32)
        * score_scale
    )
    probs_t = softmax_rows(jnp.where(same_seg[None, None], scores_t, MASKED))
    probs_t_low = to_low(probs_t)
    attn_t = to_low(
        jnp.einsum(
            "phfg,pghe->pfhe", probs_t_low, value_t, preferred_element_type=jnp.float32
        ).reshape(token_rows, model_width)
    )
    branch_t = linear(attn_t, wide_tout).reshape(patch_dev, frames, model_width)
    after_two = after_one + gate_two * branch_t
    cross_input = to_low(gain_norm(after_two, gain_row)).reshape(token_rows, model_width)
    query_c = to_low(linear(cross_input, wide_query)).reshape(
        patch_dev, frames, head_count, head_size
    )
    key_c = memory[:, :model_width].reshape(text_keys, head_count, head_size)
    value_c = memory[:, model_width:].reshape(text_keys, head_count, head_size)
    key_seg = jnp.arange(text_keys, dtype=jnp.int32) // text_len
    allowed = frame_seg[:, None] == key_seg[None, :]
    scores_c = (
        jnp.einsum("pfhe,khe->pfhk", query_c, key_c, preferred_element_type=jnp.float32)
        * score_scale
    )
    probs_c = softmax_rows(jnp.where(allowed[None, :, None, :], scores_c, MASKED))
    probs_c_low = to_low(probs_c)
    attn_c = to_low(
        jnp.einsum(
            "pfhk,khe->pfhe", probs_c_low, value_c, preferred_element_type=jnp.float32
        ).reshape(token_rows, model_width)
    )
    branch_c = linear(attn_c, wide_cout).reshape(patch_dev, frames, model_width)
    after_three = after_two + branch_c
    mlp_input = to_low(modulate(after_three, shift_three, scale_three)).reshape(
        token_rows, model_width
    )
    pre_act = linear(mlp_input, wide_hin)
    post_act = to_low(gelu_tanh(pre_act))
    branch_m = linear(post_act, wide_hout).reshape(patch_dev, frames, model_width)
    result = after_three + gate_three * branch_m
    grad_gate_three = jnp.sum(grad_out * branch_m, axis=0)
    grad_four = to_low(grad_out * gate_three).reshape(token_rows, model_width)
    grad_hout = left_product(post_act, grad_four)
    grad_post = right_product(grad_four, wide_hout)
    gelu_pull = jax.vjp(gelu_tanh, pre_act)[1]
    grad_pre = to_low(gelu_pull(grad_post)[0])
    grad_hin = left_product(mlp_input, grad_pre)
    grad_mlp_in = right_product(grad_pre, wide_hin).reshape(patch_dev, frames, model_width)
    mlp_pull = jax.vjp(modulate, after_three, shift_three, scale_three)[1]
    back_three, grad_shift_three, grad_scale_three = mlp_pull(grad_mlp_in)
    grad_three = grad_out + back_three
    grad_cross_branch = to_low(grad_three).reshape(token_rows, model_width)
    grad_cout = left_product(attn_c, grad_cross_branch)
    grad_attn_c = to_low(right_product(grad_cross_branch, wide_cout)).reshape(
        patch_dev, frames, head_count, head_size
    )
    grad_probs_c = jnp.einsum(
        "pfhe,khe->pfhk", grad_attn_c, value_c, preferred_element_type=jnp.float32
    )
    grad_scores_c = to_low(softmax_back(probs_c, grad_probs_c))
    grad_query_c = to_low(
        jnp.einsum("pfhk,khe->pfhe", grad_scores_c, key_c, preferred_element_type=jnp.float32)
        * score_scale
    ).reshape(token_rows, model_width)
    grad_key_c = (
        jnp.einsum("pfhk,pfhe->khe", grad_scores_c, query_c, preferred_element_type=jnp.float32)
        * score_scale
    )
    grad_value_c = jnp.einsum(
        "pfhk,pfhe->khe", probs_c_low, grad_attn_c, preferred_element_type=jnp.float32
    )
    grad_memory = jnp.concatenate(
        [grad_key_c.reshape(text_keys, model_width), grad_value_c.reshape(text_keys, model_width)],
        axis=1,
    )
    grad_wquery = left_product(cross_input, grad_query_c)
    grad_cross_in = right_product(grad_query_c, wide_query).reshape(patch_dev, frames, model_width)
    cross_pull = jax.vjp(gain_norm, after_two, gain_row)[1]
    back_two, grad_gain = cross_pull(grad_cross_in)
    grad_two = grad_three + back_two
    grad_gate_two = jnp.sum(grad_two * branch_t, axis=0)
    grad_temporal_branch = to_low(grad_two * gate_two).reshape(token_rows, model_width)
    grad_tout = left_product(attn_t, grad_temporal_branch)
    grad_attn_t = to_low(right_product(grad_temporal_branch, wide_tout)).reshape(
        patch_dev, frames, head_count, head_size
    )
    grad_probs_t = jnp.einsum(
        "pfhe,pghe->phfg", grad_attn_t, value_t, preferred_element_type=jnp.float32
    )
    grad_scores_t = to_low(softmax_back(probs_t, grad_probs_t))
    grad_query_t = (
        jnp.einsum("phfg,pghe->pfhe", grad_scores_t, key_t, preferred_element_type=jnp.float32)
        * score_scale
    )
    grad_key_t = (
        jnp.einsum("phfg,pfhe->pghe", grad_scores_t, query_t, preferred_element_type=jnp.float32)
        * score_scale
    )
    grad_value_t = jnp.einsum(
        "phfg,pfhe->pghe", probs_t_low, grad_attn_t, preferred_element_type=jnp.float32
    )
    grad_qkv_t = to_low(jnp.stack([grad_query_t, grad_key_t, grad_value_t], axis=2)).reshape(
        token_rows, 3 * model_width
    )
    grad_tin = left_product(temporal_input, grad_qkv_t)
    grad_temporal_in = right_product(grad_qkv_t, wide_tin).reshape(patch_dev, frames, model_width)
    temporal_pull = jax.vjp(modulate, after_one, shift_two, scale_two)[1]
    back_one, grad_shift_two, grad_scale_two = temporal_pull(grad_temporal_in)
    grad_one = grad_two + back_one
    grad_gate_one = jnp.sum(grad_one * branch_s, axis=0)
    grad_spatial_branch = to_low(grad_one * gate_one).reshape(token_rows, model_width)
    grad_sout = left_product(attn_s, grad_spatial_branch)
    grad_attn_s = to_low(right_product(grad_spatial_branch, wide_sout)).reshape(
        patch_dev, frames, head_count, head_size
    )
    back_kv = lax.all_gather(local_kv, "blk", axis=0, tiled=True)
    back_key, back_value = split_kv(back_kv)
    back_probs = spatial_probs(back_key)[0]
    back_probs_low = to_low(back_probs)
    grad_probs_s = jnp.einsum(
        "pfhe,qfhe->fhpq", grad_attn_s, back_value, preferred_element_type=jnp.float32
    )
    row_delta = jnp.sum(grad_probs_s * back_probs, axis=-1, keepdims=True)
    grad_scores_s = to_low(back_probs * (grad_probs_s - row_delta))
    grad_query_s = (
        jnp.einsum("fhpq,qfhe->pfhe", grad_scores_s, back_key, preferred_element_type=jnp.float32)
        * score_scale
    )
    count = lax.axis_size("blk") * patch_dev
    grad_key = (
        jnp.einsum("fhpq,pfhe->qfhe", grad_scores_s, query_s, preferred_element_type=jnp.float32)
        * score_scale
    )
    grad_value = jnp.einsum(
        "fhpq,pfhe->qfhe", back_probs_low, grad_attn_s, preferred_element_type=jnp.float32
    )
    grad_kv = to_low(
        lax.psum_scatter(
            jnp.concatenate(
                [
                    grad_key.reshape(count, frames, model_width),
                    grad_value.reshape(count, frames, model_width),
                ],
                axis=2,
            ).astype(jnp.bfloat16),
            "blk",
            scatter_dimension=0,
            tiled=True,
        ).astype(jnp.float32)
    )
    grad_qkv_s = jnp.concatenate(
        [to_low(grad_query_s).reshape(patch_dev, frames, model_width), grad_kv], axis=2
    ).reshape(token_rows, 3 * model_width)
    grad_sin = left_product(spatial_input, grad_qkv_s)
    grad_spatial_in = right_product(grad_qkv_s, wide_sin).reshape(patch_dev, frames, model_width)
    spatial_pull = jax.vjp(modulate, inputs, shift_one, scale_one)[1]
    back_zero, grad_shift_one, grad_scale_one = spatial_pull(grad_spatial_in)
    grad_input = grad_one + back_zero
    grad_frame_mod = jnp.concatenate(
        [
            grad_shift_one,
            grad_scale_one,
            grad_gate_one,
            grad_shift_two,
            grad_scale_two,
            grad_gate_two,
            grad_shift_three,
            grad_scale_three,
            grad_gate_three,
        ],
        axis=1,
    )
    grad_mod_local = lax.dot_general(
        choose.astype(jnp.float32),
        grad_frame_mod,
        (((0,), (0,)), ((), ())),
        precision=lax.Precision.HIGHEST,
    )
    grad_mod_part, grad_memory_part = (
        lax.psum_scatter(
            grad_mod_local.astype(jnp.bfloat16), "blk", scatter_dimension=1, tiled=True
        ).astype(jnp.float32),
        lax.psum_scatter(
            grad_memory.astype(jnp.bfloat16), "blk", scatter_dimension=1, tiled=True
        ).astype(jnp.float32),
    )
    grad_mod_low = to_low(grad_mod_part)
    grad_ada_w = left_product(conditioning, grad_mod_low)
    grad_ada_b = jnp.sum(grad_mod_low.astype(jnp.float32), axis=0)
    grad_caption = left_product(caption_rows, to_low(grad_memory_part))
    grad_ada_w, grad_ada_b, grad_caption = (
        lax.psum(grad_ada_w.astype(jnp.bfloat16), "seq").astype(jnp.float32),
        lax.psum(grad_ada_b.astype(jnp.bfloat16), "seq").astype(jnp.float32),
        lax.psum(grad_caption.astype(jnp.bfloat16), "seq").astype(jnp.float32),
    )
    shares = (
        lax.psum_scatter(grad_sin, ("seq", "blk"), scatter_dimension=0, tiled=True),
        lax.psum_scatter(grad_sout, ("seq", "blk"), scatter_dimension=0, tiled=True),
        lax.psum_scatter(grad_tin, ("seq", "blk"), scatter_dimension=0, tiled=True),
        lax.psum_scatter(grad_tout, ("seq", "blk"), scatter_dimension=0, tiled=True),
        lax.psum_scatter(grad_gain, ("seq", "blk"), scatter_dimension=0, tiled=True),
        lax.psum_scatter(grad_wquery, ("seq", "blk"), scatter_dimension=0, tiled=True),
        lax.psum_scatter(grad_cout, ("seq", "blk"), scatter_dimension=0, tiled=True),
        lax.psum_scatter(grad_hin, ("seq", "blk"), scatter_dimension=0, tiled=True),
        lax.psum_scatter(grad_hout, ("seq", "blk"), scatter_dimension=0, tiled=True),
    )
    (
        share_sin,
        share_sout,
        share_tin,
        share_tout,
        share_gain,
        share_query,
        share_cout,
        share_hin,
        share_hout,
    ) = shares
    return (
        to_low(result)[None],
        to_low(grad_input)[None],
        grad_ada_w,
        grad_ada_b,
        share_sin,
        share_sout,
        share_tin,
        share_tout,
        share_gain,
        share_query,
        grad_caption,
        share_cout,
        share_hin,
        share_hout,
    )


MESH = pl.DeviceIdType.MESH
BLOCKS = 18
LINES = 8
SHARD = 36
LINE = 4 * SHARD
WINDOW = 48
WIDE = LINES * LINE
MIB = 2**20


def place():
    seq = lax.axis_index("seq")
    blk = lax.axis_index("blk")
    x, c = seq // 2, seq % 2
    z, y = blk // 2, blk % 2
    x1, y1 = x + (1 - 2 * x) * (1 - c), y + (1 - 2 * y) * c
    x2, y2 = x + (1 - 2 * x) * c, y + (1 - 2 * y) * (1 - c)
    return x, c, y, z, x1, y1, x2, y2


def device(x, c, y, z):
    return {"seq": x * 2 + c, "blk": z * 2 + y}


def line_of(c, x, y):
    return (c * 2 + x) * 2 + y


def remote(src, dst, send_sem, recv_sem, where):
    return pltpu.make_async_remote_copy(
        src_ref=src,
        dst_ref=dst,
        send_sem=send_sem,
        recv_sem=recv_sem,
        device_id=where,
        device_id_type=MESH,
    )


def greet(others):
    barrier = pltpu.get_barrier_semaphore()
    for other in others:
        pl.semaphore_signal(barrier, inc=1, device_id=other, device_id_type=MESH)
    pl.semaphore_wait(barrier, len(others))


def left_at(t):
    at = jnp.minimum(t, 4)
    for first in (8, 9, 10, 11, 14, 15):
        at = at + jnp.where(t >= first, 1, 0)
    return at


def right_at(t):
    return jnp.where(t < 14, jnp.maximum(t - 3, 0), t - 13)


ROWS = 256
KEYS = 256
TEXT = 288
MOD = 9 * WIDE
MOD_TILES = 11
MOD_WIN = 128 * MOD_TILES
PARTS, HELD, LAST = 6, 4, 10
PAIR = 80
LEFT_SEM, SLOPE_SEM, SAVE_SEMS = 40, 42, 44
TILE = 384
SCALE = E ** (-0.5)


def nt(left, right):
    return lax.dot_general(
        left, right, (((1,), (1,)), ((), ())), preferred_element_type=jnp.float32
    )


def wide32(values):
    return values.astype(jnp.float32)


def loop(count, body):
    def step(index, carry):
        body(index)
        return carry

    lax.fori_loop(0, count, step, 0)


def each_rows(size, body, total=ROWS):
    loop(total // size, lambda i: body(pl.ds(pl.multiple_of(i * size, size), size)))


def each_cols(body):
    loop(WIDE // TILE, lambda i: body(pl.ds(pl.multiple_of(i * TILE, TILE), TILE)))


def swap_rows():
    row = lax.broadcasted_iota(jnp.int32, (ROWS, ROWS), 0)
    col = lax.broadcasted_iota(jnp.int32, (ROWS, ROWS), 1)
    return to_low((((row & 15) << 4) + (row >> 4) == col).astype(jnp.float32))


def head_window(h):
    base = h * E
    start = jnp.minimum(base // 128, 7) * 128
    lane = lax.broadcasted_iota(jnp.int32, (1, 256), 1)
    on = (lane >= base - start) & (lane < base - start + E)
    return pl.ds(pl.multiple_of(start, 128), 256), on.astype(jnp.float32)


def soft(scores, bias, mask):
    scores = scores * SCALE
    if bias is not None:
        scores = scores + bias
    powers = jnp.exp(scores - jnp.max(scores, axis=-1, keepdims=True))
    probs = powers * (1.0 / jnp.sum(powers, axis=-1, keepdims=True))
    return probs if mask is None else probs * mask


def chains(h, groups):
    return [(window, rows, keys) for window in (head_window(h), head_window(h + H // 2)) for rows, keys in groups]


def split_rows(values, jobs):
    start = 0
    parts = []
    for _, rows, _ in jobs:
        size = rows.stop - rows.start
        parts.append(values[start : start + size])
        start += size
    return parts


def heads_forward(h, query, key, value, attn, groups, bias, mask):
    jobs = chains(h, groups)
    scores = [nt(query[rows, lanes] * to_low(on), key[keys, lanes]) for (lanes, on), rows, keys in jobs]
    probs = split_rows(to_low(soft(jnp.concatenate(scores), bias, mask)), jobs)
    parts = [linear(prob, value[keys, lanes]) * on for prob, ((lanes, on), rows, keys) in zip(probs, jobs)]
    for part, ((lanes, on), rows, keys) in zip(parts, jobs):
        attn[rows, lanes] = attn[rows, lanes] + to_low(part)


def text_heads_forward(h, query, key, value, attn, bias, mask):
    jobs = chains(h, VIDEOS)
    scores = [linear(query[rows, lanes] * to_low(on), key[lanes, keys]) for (lanes, on), rows, keys in jobs]
    probs = split_rows(to_low(soft(jnp.concatenate(scores), bias, mask)), jobs)
    parts = [nt(prob, value[lanes, keys]) * on for prob, ((lanes, on), rows, keys) in zip(probs, jobs)]
    for part, ((lanes, on), rows, keys) in zip(parts, jobs):
        attn[rows, lanes] = attn[rows, lanes] + to_low(part)


HALVES = [(slice(0, 128), slice(0, 128)), (slice(128, 256), slice(128, 256))]
VIDEOS = [(slice(0, 144), slice(0, 128)), (slice(112, 256), slice(128, 256))]


def regroup(back):
    row = lax.broadcasted_iota(jnp.int32, (ROWS, ROWS), 0)
    col = lax.broadcasted_iota(jnp.int32, (ROWS, ROWS), 1)
    if back:
        source = (((row >> 3) & 1) << 7) + ((row >> 4) << 3) + (row & 7)
    else:
        source = (((row >> 3) & 15) << 4) + ((row >> 7) << 3) + (row & 7)
    return to_low((source == col).astype(jnp.float32))


def temporal_bias(seg_in, seg_row):
    row = lax.broadcasted_iota(jnp.int32, (128, 128), 0)
    col = lax.broadcasted_iota(jnp.int32, (128, 128), 1)
    allowed = ((row & 7) == (col & 7)) & (seg_in[2, 0:128, 0:1] == seg_row[0:1, 0:128])
    return jnp.where(allowed, 0.0, MASKED)


def cross_bias():
    col = lax.broadcasted_iota(jnp.int32, (1, 128), 1)
    return jnp.where(col < L, 0.0, MASKED)


def cross_rows(seg_in):
    both = [1.0 - seg_in[0, 0:144, 0:1], seg_in[0, 112:256, 0:1]]
    return jnp.concatenate(both + both)


def move_lanes(to, value, from_start, to_start, width):
    left = min(from_start // 128 * 128, value.shape[1] - 256)
    right = min(to_start // 128 * 128, width - 256)
    off = to_start - right
    part = pltpu.roll(value[:, left : left + 256], (off - (from_start - left)) % 256, 1)
    lane = lax.broadcasted_iota(jnp.int32, part.shape, 1)
    lanes = slice(right, right + 256)
    to[:, lanes] = jnp.where((lane >= off) & (lane < off + SHARD), part, to[:, lanes])


def hidden_places():
    places = []
    for d in range(32):
        xp, cp, zp, yp = d // 16, d // 8 % 2, d // 2 % 4, d % 2
        for k in range(4):
            places.append((k, (4 * d + k) * SHARD, (((cp * 2 + xp) * 2 + yp) * 4 + zp) * SHARD))
    return places


def blk_peers(x, c, b):
    return [device(x, c, (b + k) % 2, ((b + k) % 8) // 2) for k in range(1, 8)]


def forward_kernel(
    spatial_in, spatial_out, temporal_in, temporal_out, cross_query, cross_out, hidden_in, hidden_out,
    tok, gain_one, cond, ada_bias, seg_in, seg_row, cot_i, turn_i, ada_i, caption_i, proj_i,
    wide, out, left_o, qkvs_o, qkvt_o, qc_o, mem_o, xhat_o, rstd_o, branch_o, slope_o, gfour_o, cot_o, mods_o, gate_o, gain_o,
    win, pair, far, lines, weights, tokp, cotp, tokf, xin, xp, left, qkvs, qkvt, qc, mem, text, mod, mods, xhat, rstd, branch, branchw, bias,
    stream, attnf, attnp, post, slope, gfour, gains, gain_at, gate,
    src, cot, turn, ada, caption, proj, mod_in, text_in, hidden,
    z_send, z_recv, l_send, l_recv, own_sem, w_sem, t_send, t_recv, a_send, a_recv, m_send, m_recv, x_send, x_recv,
    g_send, g_recv, save_sem, in_sem,
):
    x, c, y, z, x1, y1, x2, y2 = place()
    b = z * 2 + y
    near = [device(x, c, y, (z + k) % 4) for k in (1, 2, 3)]
    beside, across = device(x, c, y, z + 1 - 2 * (z % 2)), device(x, c, y, 3 - z)
    middle = (z == 1) | (z == 2)
    first, second, twin = device(x1, c, y1, z), device(x2, c, y2, z), device(x, 1 - c, y, z)
    peers = blk_peers(x, c, b)
    greet(peers + [device(1 - x, c, y, z), twin])
    mine, line3 = line_of(c, x, y), line_of(c, 1 - x, 1 - y)

    def hops(t, core):
        turn_round = core + (1 - core) * (t % 4 == 2)
        xa, ya = x + (1 - 2 * x) * (1 - turn_round), y + (1 - 2 * y) * turn_round
        xb, yb = x + (1 - 2 * x) * turn_round, y + (1 - 2 * y) * (1 - turn_round)
        return (xa, ya), (xb, yb)

    def z_one(t):
        return remote(src.at[t], win.at[t % PARTS], z_send.at[t, 0], z_recv.at[t, 0], beside)

    def z_two(t):
        return remote(pair.at[t % PARTS], far.at[t % PARTS], z_send.at[t, 1], z_recv.at[t, 1], across)

    def z_three(t):
        return remote(far.at[t % PARTS], far.at[t % PARTS], z_send.at[t, 2], z_recv.at[t, 2], beside)

    def wide_line(t, line):
        return wide.at[t, pl.ds(pl.multiple_of(line * LINE, 16), LINE)]

    def own(t):
        return pltpu.make_async_copy(lines.at[t % HELD], wide_line(t, mine), own_sem.at[t])

    def line_copy(t, to, line, index, where):
        return remote(to, wide_line(t, line), l_send.at[t, index], l_recv.at[t, index], where)

    def sends(t, index):
        (xa, ya), (xb, yb) = hops(t, c)
        one, two = device(xa, c, ya, z), device(xb, c, yb, z)
        line1, line2 = line_of(c, xa, ya), line_of(c, xb, yb)
        line, where = (
            (mine, one), (mine, two), (mine, twin), (line1, two),
            (line1, twin), (line2, twin), (line3, twin),
        )[index]
        from_here = lines.at[t % HELD] if index < 3 else wide_line(t, line)
        return line_copy(t, from_here, line, index, where)

    def arrives(t, line, index):
        line_copy(t, wide_line(t, line), line, index, first).wait_recv()

    def tick(t):
        @pl.when((t >= 6) & (t < BLOCKS + 6))
        def _():
            now = t - 6

            @pl.when(middle)
            def _():
                z_two(now).wait_send()
                z_three(now).wait_send()

            @pl.when(jnp.logical_not(middle))
            def _():
                z_three(now).wait_recv()

            @pl.when(now >= HELD)
            def _():
                for index in range(3):
                    sends(now - HELD, index).wait_send()
                own(now - HELD).wait()

            def line_from(low, high):
                at = now % HELD
                lines[at, 0:64] = low[0:64]
                lines[at, 64:80] = low[64:80] + high[0:16]
                lines[at, 80:144] = high[16:80]

            @pl.when(z < 2)
            def _():
                line_from(pair[now % PARTS], far[now % PARTS])

            @pl.when(z >= 2)
            def _():
                line_from(far[now % PARTS], pair[now % PARTS])

            for index in range(3):
                sends(now, index).start()
            own(now).start()

        @pl.when((t >= 4) & (t < BLOCKS + 4) & middle)
        def _():
            z_two(t - 4).wait_recv()
            z_three(t - 4).start()

        @pl.when((t >= 2) & (t < BLOCKS + 2))
        def _():
            now = t - 2
            z_one(now).wait_recv()

            def pair_from(even, odd):
                at = now % PARTS
                pair[at, 0:32] = even[0:32]
                pair[at, 32:48] = even[32:48] + odd[0:16]
                pair[at, 48:80] = odd[16:48]

            @pl.when(z % 2 == 0)
            def _():
                pair_from(src[now], win[now % PARTS])

            @pl.when(z % 2 == 1)
            def _():
                pair_from(win[now % PARTS], src[now])

            @pl.when(middle)
            def _():
                z_two(now).start()

        @pl.when(t < BLOCKS)
        def _():
            z_one(t).start()

        @pl.when((t >= 8) & (t < BLOCKS + 8))
        def _():
            now = t - 8
            xa, ya = hops(now, c)[0]
            arrives(now, line_of(c, xa, ya), 0)
            for index in (3, 4):
                sends(now, index).start()

        @pl.when(t >= LAST)
        def _():
            now = t - LAST
            xb, yb = hops(now, c)[1]
            arrives(now, line_of(c, xb, yb), 1)
            sends(now, 5).start()
            arrives(now, line3, 3)
            sends(now, 6).start()

    done = [0]

    def pump(until):
        until = min(until, BLOCKS + LAST)
        if until > done[0]:
            start = done[0]
            loop(until - start, lambda i: tick(i + start))
            done[0] = until

    def poke():
        pump(done[0] + 1)

    def load(block):
        pump(block + LAST + 1)
        near_at, far_at = hops(block, 1 - c)
        places = [(x, y), near_at, far_at, (1 - x, 1 - y)]
        for (xl, yl), index in zip(places, (2, 4, 5, 6)):
            arrives(block, line_of(1 - c, xl, yl), index)
        if block >= BLOCKS - HELD:
            own(block).wait()
        copy = pltpu.make_async_copy(wide.at[block], weights.at[block % 2], w_sem.at[block % 2])
        copy.start()
        copy.wait()

    def times(values, block, emit):
        def tile(cols):
            emit(cols, linear(values[...], weights[block % 2, :, cols]))

        each_cols(tile)

    saves = []
    held = {}

    def save(from_ref, to_ref, name=None):
        if name is None:
            name = len(saves)
            saves.append(name)
        held[name] = pltpu.make_async_copy(from_ref, to_ref, save_sem.at[name])
        held[name].start()

    def settle(name):
        if name in held:
            held.pop(name).wait()

    def turned(values, index):
        slot = index % 2
        settle(LEFT_SEM + slot)

        def tile(cols):
            xp[:, cols] = to_low(nt(values[...], turn[cols, :]))
            left[slot, cols, :] = to_low(nt(turn[cols, :], values[...]))

        each_cols(tile)
        save(left.at[slot], left_o.at[index], LEFT_SEM + slot)

    fetches = [
        pltpu.make_async_copy(from_ref, to_ref, in_sem.at[at])
        for at, (from_ref, to_ref) in enumerate(
            ((ada_i, ada), (turn_i, turn), (cot_i, cot), (caption_i, caption), (proj_i, proj))
        )
    ]
    for copy in fetches:
        copy.start()

    def shift(rows, first):
        row = lax.broadcasted_iota(jnp.int32, (WINDOW, rows), 0) - 4 * z
        col = lax.broadcasted_iota(jnp.int32, (WINDOW, rows), 1)
        return to_low(((row >= 0) & (row < SHARD) & (row + first == col)).astype(jnp.float32))

    def window(at, values):
        src[at] = to_low(linear(shift(SHARD, 0), values))

    for j in range(3):
        window(j, spatial_in[:, WIDE * j : WIDE * j + WIDE])
    pump(2)
    window(3, spatial_out[...])
    for j in range(3):
        window(4 + j, temporal_in[:, WIDE * j : WIDE * j + WIDE])
    window(7, temporal_out[...])
    window(8, cross_query[...])
    window(9, cross_out[...])
    pump(4)

    def m_copy(k, at):
        return remote(mod_in, mod.at[at], m_send.at[k - 1], m_recv.at[k - 1], peers[k - 1])

    fetches[0].wait()
    part = wide32(to_low(nt(cond[...], ada[...]) + wide32(ada_bias[...])))[0:8]
    part = jnp.concatenate([part, jnp.zeros((8, MOD_WIN - MOD // 8), jnp.float32)], axis=1)
    part = pltpu.roll(part, 16 * b, 1)
    tiles = [part[row : row + 1, 128 * tile : 128 * tile + 128] for row in range(2) for tile in range(MOD_TILES)]
    mod_in[...] = to_low(jnp.concatenate(tiles + [jnp.zeros((32 - 2 * MOD_TILES, 128), jnp.float32)]))
    for k in range(1, 8):
        m_copy(k, b).start()
    mod[b] = mod_in[...]
    swap = swap_rows()
    tokp[...] = to_low(linear(swap, tok[...]))

    def t_copy(k):
        to = (b + k) % 8
        part = tokp.at[pl.ds(pl.multiple_of(32 * to, 32), 32)]
        return remote(part, tokf.at[b], t_send.at[k - 1], t_recv.at[k - 1], peers[k - 1])

    def t_wait(k):
        of = (b + 8 - k) % 8
        remote(tokp.at[pl.ds(0, 32)], tokf.at[of], t_send.at[k - 1], t_recv.at[k - 1], peers[k - 1]).wait_recv()

    pump(5)
    for k in range(1, 8):
        t_copy(k).start()
    tokf[b] = tokp[pl.ds(pl.multiple_of(32 * b, 32), 32)]

    def g_copy(at, from_at, to):
        return remote(gains.at[from_at], gain_at.at[at], g_send.at[at], g_recv.at[at], to)

    spread = jnp.concatenate([wide32(gain_one[...]), jnp.zeros((8, WIDE - SHARD), jnp.float32)], axis=1)
    gains[0] = pltpu.roll(spread, SHARD * ((x * 2 + c) * 8 + b), 1)
    g_copy(0, 0, twin).start()
    pump(6)
    fetches[2].wait()
    cotp[...] = to_low(linear(swap, cot[...]))
    save(cotp, cot_o)

    def x_copy(k, at):
        return remote(text_in, text.at[at, y], x_send.at[k - 1], x_recv.at[k - 1], near[k - 1])

    def x_over(at):
        return remote(text.at[:, at], text.at[:, at], x_send.at[3], x_recv.at[3], device(x, c, 1 - y, z))

    for k in range(1, 8):
        m_copy(k, (b + 8 - k) % 8).wait_recv()
    mods[...] = jnp.zeros_like(mods)
    for k in range(8):
        part = wide32(mod[k])
        for row in range(2):
            for tile in range(MOD_TILES):
                lanes = slice(1280 * k + 128 * tile, 1280 * k + 128 * tile + 128)
                at = row * MOD_TILES + tile
                mods[row : row + 1, lanes] = mods[row : row + 1, lanes] + part[at : at + 1]
    save(mods, mods_o)
    g_copy(0, 0, twin).wait_recv()
    gains[1] = gains[0] + gain_at[0]
    g_copy(1, 1, first).start()
    pump(7)
    fetches[3].wait()
    fetches[4].wait()
    text_in[...] = jnp.zeros_like(text_in)
    for v in range(2):
        text_in[:, 128 * v : 128 * v + L] = to_low(nt(proj[...], caption[v]))
    for k in (1, 2, 3):
        x_copy(k, z).start()
    text[z, y] = text_in[...]
    pump(8)
    hidden[...] = jnp.zeros_like(hidden)
    for k, natural, placed in hidden_places():
        start = natural // WIDE * WIDE
        move_lanes(hidden.at[k], wide32(hidden_in[:, start : start + WIDE]), natural - start, placed, WIDE)
    for k in range(4):
        window(10 + 2 * k, to_low(hidden[k]))
        src[11 + 2 * k] = to_low(linear(shift(4 * SHARD, SHARD * k), hidden_out[...]))
    fetches[1].wait()

    def pick(piece, seg):
        lanes = slice(WIDE * piece, WIDE * piece + WIDE)
        return jnp.where(seg > 0.5, mods[1:2, lanes], mods[0:1, lanes])

    def normal(values, rows, index):
        center = values - jnp.mean(values, axis=-1, keepdims=True)
        factor = lax.rsqrt(jnp.mean(center * center, axis=-1, keepdims=True) + EPSILON)
        scaled = center * factor
        xhat[index, rows, :] = to_low(scaled)
        rstd[index, rows, :] = jnp.broadcast_to(factor, (factor.shape[0], 128))
        return scaled

    for k in range(1, 8):
        t_wait(k)
    g_copy(1, 1, first).wait_recv()
    gains[2] = gains[1] + gain_at[1]
    g_copy(2, 2, second).start()

    def spatial_rows(i):
        seg = jnp.concatenate([seg_in[1, 0:16, 0:1], seg_in[1, 128:144, 0:1]])
        values = wide32(tokf[i])
        center = values - jnp.mean(values, axis=-1, keepdims=True)
        factor = lax.rsqrt(jnp.mean(center * center, axis=-1, keepdims=True) + EPSILON)
        scaled = center * factor
        ready = to_low(scaled * (1.0 + pick(1, seg)) + pick(0, seg))
        low = to_low(scaled)
        spread = jnp.broadcast_to(factor, (32, 128))
        for f in range(2):
            rows = pl.ds(pl.multiple_of(128 * f + 16 * i, 16), 16)
            part = slice(16 * f, 16 * f + 16)
            xhat[0, rows, :] = low[part]
            rstd[0, rows, :] = spread[part]
            xin[rows, :] = ready[part]

    loop(8, spatial_rows)
    save(xhat.at[0], xhat_o.at[0])
    save(rstd.at[0], rstd_o.at[0])
    turned(xin, 10)
    for j in range(3):
        load(j)

        def emit(cols, value, j=j):
            qkvs[j, :, cols] = to_low(value)

        times(xp, j, emit)
    save(qkvs, qkvs_o)
    g_copy(2, 2, second).wait_recv()
    gains[3] = gains[2] + gain_at[2]
    for k in (1, 2, 3):
        remote(gains.at[3], gain_at.at[2 + k], g_send.at[2 + k], g_recv.at[2 + k], near[k - 1]).start()
    for k in (1, 2, 3):
        x_copy(k, (z + 4 - k) % 4).wait_recv()
    x_over(y).start()
    attnf[...] = jnp.zeros_like(attnf)

    def spatial_heads(h):
        heads_forward(h, qkvs.at[0], qkvs.at[1], qkvs.at[2], attnf, HALVES, None, None)

    loop(4, spatial_heads)
    poke()
    loop(4, lambda h: spatial_heads(h + 4))
    for k in (1, 2, 3):
        remote(gains.at[3], gain_at.at[2 + k], g_send.at[2 + k], g_recv.at[2 + k], near[k - 1]).wait_recv()
    gains[0 + 4] = gains[3] + gain_at[3] + gain_at[4] + gain_at[5]
    save(gains.at[4], gain_o)

    def a_copy(k, f):
        to = (b + k) % 8
        part = attnf.at[pl.ds(pl.multiple_of(128 * f + 16 * to, 16), 16)]
        return remote(part, attnp.at[2 * b + f], a_send.at[k - 1, f], a_recv.at[k - 1, f], peers[k - 1])

    def a_wait(k, f):
        of = (b + 8 - k) % 8
        part = attnf.at[pl.ds(0, 16)]
        remote(part, attnp.at[2 * of + f], a_send.at[k - 1, f], a_recv.at[k - 1, f], peers[k - 1]).wait_recv()

    for k in range(1, 8):
        for f in range(2):
            a_copy(k, f).start()
    for f in range(2):
        attnp[2 * b + f] = attnf[pl.ds(pl.multiple_of(128 * f + 16 * b, 16), 16)]
    poke()
    for k in range(1, 8):
        for f in range(2):
            a_wait(k, f)
    xin[...] = attnp[...].reshape(ROWS, WIDE)
    turned(xin, 9)
    load(3)

    def emit_branch(cols, value):
        branchw[:, cols] = value

    times(xp, 3, emit_branch)

    def after_spatial(rows):
        seg = seg_in[0, rows, 0:1]
        value = branchw[rows, :]
        branch[0, rows, :] = to_low(value)
        value = wide32(tokp[rows, :]) + pick(2, seg) * value
        stream[rows, :] = value
        xin[rows, :] = to_low(normal(value, rows, 1) * (1.0 + pick(4, seg)) + pick(3, seg))

    each_rows(32, after_spatial)
    save(branch.at[0], branch_o.at[0])
    save(xhat.at[1], xhat_o.at[1])
    save(rstd.at[1], rstd_o.at[1])

    for k in range(1, 8):
        for f in range(2):
            a_copy(k, f).wait_send()
    attnf[...] = to_low(linear(regroup(False), xin[...]))
    turned(attnf, 8)
    for j in range(3):
        load(4 + j)

        def emit(cols, value, j=j):
            qkvt[j, :, cols] = to_low(value)

        times(xp, 4 + j, emit)
    save(qkvt, qkvt_o)
    attnf[...] = jnp.zeros_like(attnf)

    bias[...] = temporal_bias(seg_in, seg_row)

    def temporal_heads(h):
        heads_forward(
            h, qkvt.at[0], qkvt.at[1], qkvt.at[2], attnf, HALVES, jnp.concatenate([bias[...]] * 4), None
        )

    loop(4, temporal_heads)
    poke()
    loop(4, lambda h: temporal_heads(h + 4))
    xin[...] = to_low(linear(regroup(True), attnf[...]))
    turned(xin, 7)
    load(7)
    times(xp, 7, emit_branch)

    def after_temporal(rows):
        seg = seg_in[0, rows, 0:1]
        value = branchw[rows, :]
        branch[1, rows, :] = to_low(value)
        value = stream[rows, :] + pick(5, seg) * value
        stream[rows, :] = value
        xin[rows, :] = to_low(normal(value, rows, 2) * gains[4, 0:1, :])

    each_rows(32, after_temporal)
    save(branch.at[1], branch_o.at[1])
    save(xhat.at[2], xhat_o.at[2])
    save(rstd.at[2], rstd_o.at[2])

    turned(xin, 6)
    load(8)

    def emit_query(cols, value):
        qc[:, cols] = to_low(value)

    times(xp, 8, emit_query)
    save(qc, qc_o)
    x_over(1 - y).wait_recv()
    for k in range(8):
        mem[k // 4, TEXT * (k % 4) : TEXT * (k % 4) + TEXT, :] = text[k // 2, k % 2]
    save(mem, mem_o)
    attnf[...] = jnp.zeros_like(attnf)

    def cross_heads(h):
        text_heads_forward(h, qc, mem.at[0], mem.at[1], attnf, cross_bias(), cross_rows(seg_in))

    loop(4, cross_heads)
    poke()
    loop(4, lambda h: cross_heads(h + 4))
    xin[...] = attnf[...]
    turned(xin, 5)
    load(9)
    times(xp, 9, emit_branch)

    def after_cross(rows):
        seg = seg_in[0, rows, 0:1]
        value = stream[rows, :] + branchw[rows, :]
        stream[rows, :] = value
        xin[rows, :] = to_low(normal(value, rows, 3) * (1.0 + pick(7, seg)) + pick(6, seg))
        gfour[rows, :] = to_low(wide32(cotp[rows, :]) * pick(8, seg))

    each_rows(32, after_cross)
    save(xhat.at[3], xhat_o.at[3])
    save(rstd.at[3], rstd_o.at[3])
    save(gfour, gfour_o)

    turned(xin, 4)
    same = (
        lax.broadcasted_iota(jnp.int32, (TILE, TILE), 0) == lax.broadcasted_iota(jnp.int32, (TILE, TILE), 1)
    ).astype(jnp.float32).astype(jnp.bfloat16)
    for k in range(4):
        slot = k % 2
        load(10 + 2 * k)
        settle(SLOPE_SEM + slot)
        settle(LEFT_SEM + slot)

        def emit_hidden(cols, value, slot=slot):
            inner = math.sqrt(2.0 / math.pi) * (value + 0.044715 * value * value * value)
            bent = jnp.tanh(inner)
            half = 0.5 * (1.0 + bent)
            tilt = math.sqrt(2.0 / math.pi) * (1.0 + 3 * 0.044715 * value * value)
            slope[slot, :, cols] = to_low(half + 0.5 * value * (1.0 - bent * bent) * tilt)
            low = to_low(value * half)
            post[:, cols] = low
            left[slot, cols, :] = to_low(nt(same, low))

        times(xp, 10 + 2 * k, emit_hidden)
        save(slope.at[slot], slope_o.at[k], SLOPE_SEM + slot)
        save(left.at[slot], left_o.at[k], LEFT_SEM + slot)
        load(11 + 2 * k)

        def emit_out(cols, value, k=k):
            branchw[:, cols] = value if k == 0 else branchw[:, cols] + value

        times(post, 11 + 2 * k, emit_out)

    gate[...] = jnp.zeros_like(gate)

    def last(rows):
        seg = seg_in[0, rows, 0:1]
        value = branchw[rows, :]
        xin[rows, :] = to_low(stream[rows, :] + pick(8, seg) * value)
        value = wide32(cotp[rows, :]) * value
        later = jnp.sum(value * seg, axis=0, keepdims=True)
        every = jnp.sum(value, axis=0, keepdims=True)
        gate[0:1, :] = gate[0:1, :] + (every - later)
        gate[1:2, :] = gate[1:2, :] + later

    each_rows(32, last)
    save(gate, gate_o)
    out[...] = to_low(linear(swap_rows(), xin[...]))

    for copy in held.values():
        copy.wait()
    for k in range(1, 8):
        t_copy(k).wait_send()
        m_copy(k, b).wait_send()
    for k in (1, 2, 3):
        x_copy(k, z).wait_send()
    x_over(y).wait_send()
    for at, to in ((0, twin), (1, first), (2, second)):
        g_copy(at, at, to).wait_send()
    for k in (1, 2, 3):
        remote(gains.at[3], gain_at.at[2 + k], g_send.at[2 + k], g_recv.at[2 + k], near[k - 1]).wait_send()

    for t in range(BLOCKS - HELD, BLOCKS):
        for index in range(3):
            sends(t, index).wait_send()

    def finish(t):
        z_one(t).wait_send()
        for index in range(3, 7):
            sends(t, index).wait_send()

    loop(BLOCKS, finish)


ANY = pl.BlockSpec(memory_space=pl.ANY)
IN_VMEM = pl.BlockSpec(memory_space=pltpu.VMEM)


def forward(*operands):
    low, full = jnp.bfloat16, jnp.float32
    dma = pltpu.SemaphoreType.DMA
    hbm = [
        ((BLOCKS, WIDE, WIDE), low),
        ((ROWS, WIDE), low),
        ((11, WIDE, ROWS), low),
        ((3, ROWS, WIDE), low),
        ((3, ROWS, WIDE), low),
        ((ROWS, WIDE), low),
        ((2, WIDE, KEYS), low),
        ((4, ROWS, WIDE), low),
        ((4, ROWS, 128), full),
        ((2, ROWS, WIDE), low),
        ((4, ROWS, WIDE), low),
        ((ROWS, WIDE), low),
        ((ROWS, WIDE), low),
        ((8, MOD), full),
        ((8, WIDE), full),
        ((8, WIDE), full),
    ]
    vmem = [
        ((PARTS, WINDOW, WIDE), low),
        ((PARTS, PAIR, WIDE), low),
        ((PARTS, PAIR, WIDE), low),
        ((HELD, LINE, WIDE), low),
        ((2, WIDE, WIDE), low),
        ((ROWS, WIDE), low),
        ((ROWS, WIDE), low),
        ((8, 32, WIDE), low),
        ((ROWS, WIDE), low),
        ((ROWS, WIDE), low),
        ((2, WIDE, ROWS), low),
        ((3, ROWS, WIDE), low),
        ((3, ROWS, WIDE), low),
        ((ROWS, WIDE), low),
        ((2, WIDE, KEYS), low),
        ((4, 2, TEXT, KEYS), low),
        ((8, 32, 128), low),
        ((8, MOD), full),
        ((4, ROWS, WIDE), low),
        ((4, ROWS, 128), full),
        ((2, ROWS, WIDE), low),
        ((ROWS, WIDE), full),
        ((128, 128), full),
        ((ROWS, WIDE), full),
        ((ROWS, WIDE), low),
        ((16, 16, WIDE), low),
        ((ROWS, WIDE), low),
        ((2, ROWS, WIDE), low),
        ((ROWS, WIDE), low),
        ((5, 8, WIDE), full),
        ((6, 8, WIDE), full),
        ((8, WIDE), full),
        ((BLOCKS, WINDOW, WIDE), low),
        ((ROWS, WIDE), low),
        ((WIDE, WIDE), low),
        ((MOD // 8, WIDE), low),
        ((2, L, 4096), low),
        ((TEXT, 4096), low),
        ((32, 128), low),
        ((TEXT, KEYS), low),
        ((4, SHARD, WIDE), full),
    ]
    return pl.pallas_call(
        forward_kernel,
        out_shape=[jax.ShapeDtypeStruct(*shape) for shape in hbm],
        in_specs=[IN_VMEM] * 14 + [ANY] * 5,
        out_specs=[ANY, IN_VMEM] + [ANY] * 14,
        scratch_shapes=[pltpu.VMEM(*shape) for shape in vmem]
        + [
            dma((BLOCKS, 3)), dma((BLOCKS, 3)), dma((BLOCKS, 7)), dma((BLOCKS, 7)), dma((BLOCKS,)), dma((2,)),
            dma((7,)), dma((7,)), dma((7, 2)), dma((7, 2)), dma((7,)), dma((7,)), dma((4,)), dma((4,)),
            dma((6,)), dma((6,)), dma((SAVE_SEMS,)), dma((5,)),
        ],
        compiler_params=pltpu.CompilerParams(
            collective_id=0, has_side_effects=True, vmem_limit_bytes=60 * MIB
        ),
        name="forward",
    )(*operands)


def tn(left, right):
    return lax.dot_general(
        left, right, (((0,), (0,)), ((), ())), preferred_element_type=jnp.float32
    )


def text_heads_backward(h, query, key, value, grad, dquery, dkey, dvalue, bias, mask):
    jobs = chains(h, VIDEOS)
    scores, grads = [], []
    for (lanes, on), rows, keys in jobs:
        low_on = to_low(on)
        scores.append(linear(query[rows, lanes] * low_on, key[lanes, keys]))
        grads.append(linear(grad[rows, lanes] * low_on, value[lanes, keys]))
    probs = soft(jnp.concatenate(scores), bias, mask)
    grad_probs = jnp.concatenate(grads)
    delta = jnp.sum(grad_probs * probs, axis=-1, keepdims=True)
    slopes = split_rows(to_low(probs * (grad_probs - delta)), jobs)
    probs = split_rows(to_low(probs), jobs)
    parts = []
    for slope, prob, ((lanes, on), rows, keys) in zip(slopes, probs, jobs):
        low_on = to_low(on)
        parts.append(
            (
                to_low(nt(slope, key[lanes, keys]) * (on * SCALE)),
                to_low(tn(query[rows, lanes] * low_on, slope) * SCALE),
                to_low(tn(grad[rows, lanes] * low_on, prob)),
            )
        )
    for (by_query, by_key, by_value), ((lanes, on), rows, keys) in zip(parts, jobs):
        dquery[rows, lanes] = dquery[rows, lanes] + by_query
        dkey[lanes, keys] = dkey[lanes, keys] + by_key
        dvalue[lanes, keys] = dvalue[lanes, keys] + by_value


def heads_backward(h, query, key, value, grad, dquery, dkey, dvalue, groups, bias, mask):
    jobs = chains(h, groups)
    scores, grads = [], []
    for (lanes, on), rows, keys in jobs:
        low_on = to_low(on)
        scores.append(nt(query[rows, lanes] * low_on, key[keys, lanes]))
        grads.append(nt(grad[rows, lanes] * low_on, value[keys, lanes]))
    probs = soft(jnp.concatenate(scores), bias, mask)
    grad_probs = jnp.concatenate(grads)
    delta = jnp.sum(grad_probs * probs, axis=-1, keepdims=True)
    slopes = split_rows(to_low(probs * (grad_probs - delta)), jobs)
    probs = split_rows(to_low(probs), jobs)
    parts = []
    for slope, prob, ((lanes, on), rows, keys) in zip(slopes, probs, jobs):
        parts.append(
            (
                to_low(linear(slope, key[keys, lanes]) * (on * SCALE)),
                to_low(tn(slope, query[rows, lanes]) * (on * SCALE)),
                to_low(tn(prob, grad[rows, lanes]) * on),
            )
        )
    for (by_query, by_key, by_value), ((lanes, on), rows, keys) in zip(parts, jobs):
        dquery[rows, lanes] = dquery[rows, lanes] + by_query
        dkey[keys, lanes] = dkey[keys, lanes] + by_key
        dvalue[keys, lanes] = dvalue[keys, lanes] + by_value


def backward_kernel(
    wide, left_i, qkvs_i, qkvt_i, qc_i, mem_i, xhat_i, rstd_i, branch_i, slope_i, gfour_i, cot_i, mods_i, gate_i, gain_i,
    caption_i, seg_in, seg_row, turn, cond_in,
    total, gtok, gain_o, caption_o, mod_o,
    weights, left, right, qkv, xhat, rstd, branch, slope, mods, gain, bias, stream, work, grad, xin, gm, mem, dmem, text, text_at, text_sum, cap, cap_out, cap_in, cap_own, cap_at, mod_out, mod,
    seqs, gains, gain_at, gframe, back,
    s0, r0, s1, r1, s2, r2, k2, s3, pass_in, pass_out, far_in, close, close_in, share,
    in_sem, w_sem, s0_sem, r0_sem, s1_sem, r1_sem, s2_sem, r2_sem, z_send, z_recv, share_sem,
    a_send, a_recv, u_send, u_recv, x_send, x_recv, m_send, m_recv, q_send, q_recv, g_send, g_recv,
    cap_sem, c_send, c_recv, left_sem,
):
    x, c, y, z, x1, y1, x2, y2 = place()
    b = z * 2 + y
    near = [device(x, c, y, (z + k) % 4) for k in (1, 2, 3)]
    first, second, twin = device(x1, c, y1, z), device(x2, c, y2, z), device(x, 1 - c, y, z)
    peers = blk_peers(x, c, b)
    across = [twin, device(1 - x, c, y, z), device(1 - x, 1 - c, y, z)]
    greet(peers + across)

    fetches = {}

    def fetch(name, from_ref, to_ref):
        fetches[name] = pltpu.make_async_copy(from_ref, to_ref, in_sem.at[name])
        fetches[name].start()

    def have(name):
        if name in fetches:
            fetches.pop(name).wait()

    fetch(0, gfour_i, right.at[0])
    for k in range(4):
        fetch(1 + k, left_i.at[k], left.at[k])
    fetch(12, mods_i, mods)
    fetch(13, gain_i, gain)
    fetch(14, slope_i.at[0], slope.at[0])
    fetch(15, slope_i.at[1], slope.at[1])
    fetch(16, xhat_i.at[3], xhat.at[1])
    fetch(17, rstd_i.at[3], rstd.at[1])
    fetch(18, cot_i, xin)
    fetch(19, gate_i, work.at[0:8])

    def weight(block):
        slot = WEIGHT_ORDER.index(block) % 2
        return weights.at[slot]

    def prefetch(at):
        if at < len(WEIGHT_ORDER):
            copy = pltpu.make_async_copy(wide.at[WEIGHT_ORDER[at]], weights.at[at % 2], w_sem.at[at % 2])
            copy.start()
            fetches["w", WEIGHT_ORDER[at]] = copy

    def release(block):
        prefetch(WEIGHT_ORDER.index(block) + 2)

    prefetch(0)
    prefetch(1)

    away = [(1 - x) * 2 + 1 - y, x2 * 2 + y2]
    stay = [x1 * 2 + y1, x * 2 + y]

    def product(t, core, xl):
        rows = pl.ds(pl.multiple_of(line_of(core, xl, 0) * LINE, 16), 2 * LINE)
        return linear(left[left_at(t) % 4, rows, :], right[right_at(t)])

    def left_copy(t):
        return pltpu.make_async_copy(left_i.at[left_at(t)], left.at[left_at(t) % 4], left_sem.at[0])

    def left_next(t):
        return (t >= 4) & (t < BLOCKS) & (left_at(t) != left_at(t - 1))

    def copy0(t, l):
        pair = pl.ds(2 * l, 2)
        return remote(s0.at[t % 2, pair], r0.at[t % 4, pair], s0_sem.at[t % 2, l], r0_sem.at[t % 4, l], twin)

    def copy1(t, l):
        return remote(s1.at[t % 2, away[l]], r1.at[t % 4, l], s1_sem.at[t % 2, l], r1_sem.at[t % 4, l], second)

    def copy2(t):
        return remote(s2.at[t % 2], r2.at[t % 4], s2_sem.at[t % 2], r2_sem.at[t % 4], first)

    beside, opposite = device(x, c, y, z + 1 - 2 * (z % 2)), device(x, c, y, 3 - z)
    middle = (z == 1) | (z == 2)
    near_rows = pl.ds(pl.multiple_of(64 * (z // 2), 16), PAIR)
    far_rows = pl.ds(pl.multiple_of(64 - 64 * (z // 2), 16), PAIR)
    own_rows = pl.ds(pl.multiple_of(32 * (z % 2), 16), WINDOW)
    beside_rows = pl.ds(pl.multiple_of(32 - 32 * (z % 2), 16), WINDOW)

    def z_one(t):
        return remote(s3.at[t % 4, far_rows], pass_in.at[t % 6], z_send.at[0, t % 6], z_recv.at[0, t % 6], beside)

    def z_two(t):
        return remote(pass_out.at[t % 2], far_in.at[t % 4], z_send.at[1, t % 4], z_recv.at[1, t % 4], opposite)

    def z_three(t):
        return remote(
            close.at[t % 2, beside_rows], close_in.at[t % 4], z_send.at[2, t % 4], z_recv.at[2, t % 4], beside
        )

    def share_copy(t):
        return pltpu.make_async_copy(share.at[t % 2], total.at[t], share_sem.at[t % 2])

    def tick(t):
        @pl.when(t >= 12)
        def _():
            now = t - 12
            z_three(now).wait_recv()
            value = wide32(close[now % 2, own_rows]) + wide32(close_in[now % 4])

            @pl.when(now >= 2)
            def _():
                share_copy(now - 2).wait()
            share[now % 2] = value
            share_copy(now).start()

        @pl.when((t >= 10) & (t < BLOCKS + 10))
        def _():
            now = t - 10

            @pl.when(now >= 2)
            def _():
                z_three(now - 2).wait_send()

            @pl.when(middle)
            def _():
                z_two(now).wait_recv()
                close[now % 2] = to_low(wide32(s3[now % 4, near_rows]) + wide32(far_in[now % 4]))

            @pl.when(jnp.logical_not(middle))
            def _():
                close[now % 2] = s3[now % 4, near_rows]
                z_one(now).wait_send()

            z_three(now).start()

        @pl.when((t >= 8) & (t < BLOCKS + 8) & middle)
        def _():
            now = t - 8
            z_one(now).wait_recv()

            @pl.when(now >= 2)
            def _():
                z_two(now - 2).wait_send()
            pass_out[now % 2] = to_low(wide32(s3[now % 4, far_rows]) + wide32(pass_in[now % 6]))
            z_two(now).start()

        @pl.when((t >= 6) & (t < BLOCKS + 6))
        def _():
            now = t - 6
            copy2(now).wait_recv()
            s3[now % 4] = to_low(k2[now % 2] + wide32(r2[now % 4]))

            @pl.when(jnp.logical_not(middle))
            def _():
                z_one(now).start()

        @pl.when((t >= 4) & (t < BLOCKS + 4))
        def _():
            now = t - 4
            copy1(now, 0).wait_recv()

            @pl.when(now >= 2)
            def _():
                copy2(now - 2).wait_send()
            s2[now % 2] = to_low(wide32(s1[now % 2, stay[0]]) + wide32(r1[now % 4, 0]))
            copy2(now).start()
            copy1(now, 1).wait_recv()
            k2[now % 2] = wide32(s1[now % 2, stay[1]]) + wide32(r1[now % 4, 1])

        @pl.when((t >= 2) & (t < BLOCKS + 2))
        def _():
            now = t - 2

            @pl.when(now >= 2)
            def _():
                for l in range(2):
                    copy1(now - 2, l).wait_send()
            for l in range(2):
                copy0(now, l).wait_recv()
                value = product(now, c, l)
                for part in range(2):
                    line = 2 * l + part
                    summed = value[part * LINE : part * LINE + LINE] + wide32(r0[now % 4, line])
                    s1[now % 2, line] = to_low(summed)
            for l in range(2):
                copy1(now, l).start()

        @pl.when(left_next(t))
        def _():
            left_copy(t).wait()

        @pl.when(t < BLOCKS)
        def _():
            for l in range(2):
                @pl.when(t >= 2)
                def _():
                    copy0(t - 2, l).wait_send()
                value = to_low(product(t, 1 - c, l))
                s0[t % 2, 2 * l] = value[:LINE]
                s0[t % 2, 2 * l + 1] = value[LINE:]
                copy0(t, l).start()

        @pl.when(left_next(t + 1))
        def _():
            left_copy(t + 1).start()

    done = [0]

    def pump(until):
        if until > done[0]:
            start = done[0]
            loop(until - start, lambda i: tick(i + start))
            done[0] = until

    def pick(piece, seg):
        lanes = slice(WIDE * piece, WIDE * piece + WIDE)
        return jnp.where(seg > 0.5, mods[1:2, lanes], mods[0:1, lanes])

    def by_video(piece, value, seg):
        lanes = slice(WIDE * piece, WIDE * piece + WIDE)
        later = jnp.sum(value * seg, axis=0, keepdims=True)
        every = jnp.sum(value, axis=0, keepdims=True)
        gm[0:1, lanes] = gm[0:1, lanes] + (every - later)
        gm[1:2, lanes] = gm[1:2, lanes] + later

    def through(values_at, blocks, emit, grouped=False):
        for n, (values, block) in enumerate(zip(values_at, blocks)):
            have(("w", block))

            def tile(cols, n=n, values=values, block=block):
                part = nt(values[...], weight(block)[cols, :])
                if n > 0:
                    part = part + work[:, cols]
                if n == len(blocks) - 1:
                    xin[:, cols] = to_low(part)
                else:
                    work[:, cols] = part

            each_cols(tile)
            release(block)
        if grouped:
            xin[...] = to_low(linear(regroup(True), xin[...]))
        turn_back(emit)

    def turn_back(emit):
        each_cols(lambda cols: emit(cols, linear(xin[...], turn[:, cols])))

    def emit_work(cols, value):
        work[:, cols] = value

    def emit_grad(cols, value):
        grad[:, cols] = to_low(value)

    def norm_back(grad_in, tilt, at, rows):
        slope_in = grad_in * tilt
        hat = wide32(xhat[at, rows, :])
        first_mean = jnp.mean(slope_in, axis=-1, keepdims=True)
        second_mean = jnp.mean(slope_in * hat, axis=-1, keepdims=True)
        return rstd[at, rows, 0:1] * (slope_in - first_mean - hat * second_mean)

    gm[...] = jnp.zeros_like(gm)
    have(0)
    have(12)
    have(18)
    have(19)
    gm[0:8, 8 * WIDE : 9 * WIDE] = work[0:8]
    stream[...] = wide32(xin[...])
    for k in range(4):
        have(1 + k)
    pump(2)
    for k in range(4):
        have(14 + k % 2 if k < 2 else ("slope", k))
        have(("w", 11 + 2 * k))

        def tile(cols, k=k):
            value = nt(right[0], weight(11 + 2 * k)[cols, :]) * wide32(slope[k % 2, :, cols])
            right[1 + k, :, cols] = to_low(value)

        each_cols(tile)
        release(11 + 2 * k)
        if k < 2:
            copy = pltpu.make_async_copy(slope_i.at[k + 2], slope.at[k % 2], in_sem.at[14 + k])
            copy.start()
            fetches["slope", k + 2] = copy
        have(("w", 10 + 2 * k))

        def tile(cols, k=k):
            part = nt(right[1 + k], weight(10 + 2 * k)[cols, :])
            if k > 0:
                part = part + work[:, cols]
            if k < 3:
                work[:, cols] = part
            else:
                xin[:, cols] = to_low(part)

        each_cols(tile)
        release(10 + 2 * k)
        pump(k + 3)
    turn_back(emit_work)
    have(16)
    have(17)
    fetch(20, qc_i, qkv.at[0])
    fetch(21, mem_i.at[0], mem.at[0])
    fetch(22, mem_i.at[1], mem.at[1])
    fetch(23, xhat_i.at[2], xhat.at[0])
    fetch(24, rstd_i.at[2], rstd.at[0])

    def after_mlp(rows):
        seg = seg_in[0, rows, 0:1]
        value = work[rows, :]
        by_video(6, value, seg)
        by_video(7, value * wide32(xhat[1, rows, :]), seg)
        value = stream[rows, :] + norm_back(value, 1.0 + pick(7, seg), 1, rows)
        stream[rows, :] = value
        right[5, rows, :] = to_low(value)

    each_rows(32, after_mlp)

    fetch(25, xhat_i.at[1], xhat.at[1])
    fetch(26, rstd_i.at[1], rstd.at[1])
    through([right.at[5]], [9], emit_grad)
    right[6] = jnp.zeros_like(right[6])
    dmem[...] = jnp.zeros_like(dmem)
    for name in (13, 20, 21, 22, 23, 24):
        have(name)

    def cross_heads(h):
        text_heads_backward(
            h, qkv.at[0], mem.at[0], mem.at[1], grad, right.at[6], dmem.at[0], dmem.at[1],
            cross_bias(), cross_rows(seg_in),
        )

    for part in range(4):
        loop(2, lambda h: cross_heads(h + 2 * part))
        pump(7 + (part + 1) // 2)

    def dmem_part(zp, yp):
        return dmem.at[zp // 2, pl.ds(pl.multiple_of(TEXT * (zp % 2 * 2 + yp), 16), TEXT)]

    def x_over(zp):
        return remote(dmem_part(zp, 1 - y), text.at[zp], x_send.at[zp], x_recv.at[zp], device(x, c, 1 - y, z))

    def x_copy(k):
        return remote(text.at[(z + k) % 4], text_at.at[k - 1], x_send.at[3 + k], x_recv.at[3 + k], near[k - 1])

    for zp in range(4):
        x_over(zp).start()
    fetch(27, qkvt_i.at[0], qkv.at[0])
    fetch(28, qkvt_i.at[1], qkv.at[1])
    fetch(29, qkvt_i.at[2], qkv.at[2])
    fetch(30, branch_i.at[1], branch)
    through([right.at[6]], [8], emit_work)
    gains[0] = jnp.zeros_like(gains[0])
    have(30)

    def after_cross(rows):
        seg = seg_in[0, rows, 0:1]
        value = work[rows, :]
        gains[0, 0:1, :] = gains[0, 0:1, :] + jnp.sum(value * wide32(xhat[0, rows, :]), axis=0, keepdims=True)
        value = stream[rows, :] + norm_back(value, gain[0:1, :], 0, rows)
        stream[rows, :] = value
        by_video(5, value * wide32(branch[rows, :]), seg)
        right[7, rows, :] = to_low(value * pick(5, seg))

    each_rows(32, after_cross)

    def g_copy(at, to):
        return remote(gains.at[min(at, 3)], gain_at.at[at], g_send.at[at], g_recv.at[at], to)

    g_copy(0, twin).start()
    fetch(31, branch_i.at[0], branch)
    fetch(32, xhat_i.at[0], xhat.at[0])
    fetch(33, rstd_i.at[0], rstd.at[0])
    pump(10)

    through([right.at[7]], [7], emit_grad)
    grad[...] = to_low(linear(regroup(False), grad[...]))
    bias[...] = temporal_bias(seg_in, seg_row)
    for j in range(3):
        right[8 + j] = jnp.zeros_like(right[8 + j])
    for name in (25, 26, 27, 28, 29):
        have(name)

    def temporal_heads(h):
        heads_backward(
            h, qkv.at[0], qkv.at[1], qkv.at[2], grad, right.at[8], right.at[9], right.at[10],
            HALVES, jnp.concatenate([bias[...]] * 4), None,
        )

    loop(4, temporal_heads)
    pump(11)
    g_copy(0, twin).wait_recv()
    gains[1] = gains[0] + gain_at[0]
    g_copy(1, first).start()
    loop(4, lambda h: temporal_heads(h + 4))
    pump(12)
    g_copy(1, first).wait_recv()
    gains[2] = gains[1] + gain_at[1]
    g_copy(2, second).start()
    for zp in range(4):
        x_over(zp).wait_recv()
        text[zp] = to_low(wide32(dmem_part(zp, y)[...]) + wide32(text[zp]))
    for k in (1, 2, 3):
        x_copy(k).start()
    for j in range(3):
        fetch(34 + j, qkvs_i.at[j], qkv.at[j])
    through([right.at[8], right.at[9], right.at[10]], [4, 5, 6], emit_work, True)
    have(31)

    def after_temporal(rows):
        seg = seg_in[0, rows, 0:1]
        value = work[rows, :]
        by_video(3, value, seg)
        by_video(4, value * wide32(xhat[1, rows, :]), seg)
        value = stream[rows, :] + norm_back(value, 1.0 + pick(4, seg), 1, rows)
        stream[rows, :] = value
        by_video(2, value * wide32(branch[rows, :]), seg)
        right[1, rows, :] = to_low(value * pick(2, seg))

    each_rows(32, after_temporal)

    through([right.at[1]], [3], emit_grad)

    def a_copy(k):
        to = (b + k) % 8
        part = grad.at[pl.ds(pl.multiple_of(32 * to, 32), 32)]
        return remote(part, back.at[b], a_send.at[k - 1], a_recv.at[k - 1], peers[k - 1])

    def a_wait(k):
        of = (b + 8 - k) % 8
        remote(grad.at[pl.ds(0, 32)], back.at[of], a_send.at[k - 1], a_recv.at[k - 1], peers[k - 1]).wait_recv()

    for k in (1, 2, 3):
        x_copy(k).wait_recv()
    text_sum[...] = to_low(wide32(text[z]) + wide32(text_at[0]) + wide32(text_at[1]) + wide32(text_at[2]))
    for k in range(1, 8):
        a_copy(k).start()

    def cap_fetch(n):
        quarter = [1 - c, 3 - c, c, 2 + c][n]
        lanes = pl.ds(pl.multiple_of(QUARTER * quarter, 128), QUARTER)
        return pltpu.make_async_copy(caption_i.at[:, :, lanes], cap.at[n % 2], cap_sem.at[n % 2])

    over_x = across[1]
    quarters = [x * 2 + c, (1 - x) * 2 + c, x * 2 + 1 - c, (1 - x) * 2 + 1 - c]

    def c_copy(n):
        from_ref, to_ref, to = (
            (cap_out.at[0], cap_in.at[0], twin),
            (cap_out.at[1], cap_in.at[1], twin),
            (cap_own.at[1 - x], cap_at, over_x),
            (cap_own.at[x], caption_o.at[quarters[0]], over_x),
            (cap_own.at[x], caption_o.at[quarters[0]], twin),
            (caption_o.at[quarters[1]], caption_o.at[quarters[1]], twin),
        )[n]
        return remote(from_ref, to_ref, c_send.at[n], c_recv.at[n], to)

    cap_fetch(0).start()
    cap_fetch(1).start()
    for n in range(4):
        cap_fetch(n).wait()
        part = linear(text_sum[:, 0:L], cap[n % 2, 0]) + linear(text_sum[:, 128 : 128 + L], cap[n % 2, 1])
        if n < 2:
            cap_out[n] = to_low(part)
            c_copy(n).start()
            cap_fetch(n + 2).start()
        else:
            cap_own[n - 2] = to_low(part)
    back[b] = grad[pl.ds(pl.multiple_of(32 * b, 32), 32)]
    pump(13)
    g_copy(2, second).wait_recv()
    gains[3] = gains[2] + gain_at[2]
    for k in (1, 2, 3):
        g_copy(2 + k, near[k - 1]).start()
    for j in range(3):
        right[2 + j] = jnp.zeros_like(right[2 + j])
    for name in (32, 33, 34, 35, 36):
        have(name)
    for k in range(1, 8):
        a_wait(k)
    for k in range(8):
        for f in range(2):
            gframe[128 * f + 16 * k : 128 * f + 16 * k + 16, :] = back[k, 16 * f : 16 * f + 16, :]

    def spatial_heads(h):
        heads_backward(
            h, qkv.at[0], qkv.at[1], qkv.at[2], gframe, right.at[2], right.at[3], right.at[4], HALVES, None, None
        )

    loop(4, spatial_heads)
    pump(14)
    for n in range(2):
        c_copy(n).wait_recv()
        cap_own[n] = to_low(wide32(cap_own[n]) + wide32(cap_in[n]))
    c_copy(2).start()
    loop(4, lambda h: spatial_heads(h + 4))
    pump(15)
    through([right.at[2], right.at[3], right.at[4]], [0, 1, 2], emit_work)
    pump(16)
    for k in range(1, 8):
        a_copy(k).wait_send()

    def after_spatial(i):
        rows = pl.ds(pl.multiple_of(16 * i, 16), 16)
        seg = seg_in[1, rows, 0:1]
        value = work[rows, :]
        by_video(0, value, seg)
        by_video(1, value * wide32(xhat[0, rows, :]), seg)
        value = to_low(norm_back(value, 1.0 + pick(1, seg), 0, rows))
        back[i % 8, pl.ds(pl.multiple_of(16 * (i // 8), 16), 16), :] = value

    loop(16, after_spatial)
    c_copy(2).wait_recv()
    cap_own[x] = to_low(wide32(cap_own[x]) + wide32(cap_at[...]))
    c_copy(3).start()
    c_copy(4).start()
    keep_quarter = pltpu.make_async_copy(cap_own.at[x], caption_o.at[quarters[0]], cap_sem.at[0])
    keep_quarter.start()

    def branch_part(of):
        return branch.at[pl.ds(pl.multiple_of(32 * of, 32), 32)]

    def u_copy(k):
        to = (b + k) % 8
        return remote(back.at[to], branch_part(b), u_send.at[k - 1], u_recv.at[k - 1], peers[k - 1])

    def u_wait(k):
        of = (b + 8 - k) % 8
        remote(back.at[0], branch_part(of), u_send.at[k - 1], u_recv.at[k - 1], peers[k - 1]).wait_recv()

    def m_copy(k):
        to = (b + k) % 8
        return remote(mod_out.at[to], mod.at[b], m_send.at[k - 1], m_recv.at[k - 1], peers[k - 1])

    def m_wait(k):
        of = (b + 8 - k) % 8
        remote(mod_out.at[0], mod.at[of], m_send.at[k - 1], m_recv.at[k - 1], peers[k - 1]).wait_recv()

    for k in range(1, 8):
        u_copy(k).start()
    branch[pl.ds(pl.multiple_of(32 * b, 32), 32), :] = back[b]
    for k in range(8):
        tiles = [
            gm[row : row + 1, 1280 * k + 128 * tile : 1280 * k + 128 * tile + 128]
            for row in range(2)
            for tile in range(MOD_TILES)
        ]
        mod_out[k] = to_low(jnp.concatenate(tiles + [jnp.zeros((32 - 2 * MOD_TILES, 128), jnp.float32)]))
    for k in range(1, 8):
        m_copy(k).start()
    mod[b] = mod_out[b]
    pump(18)
    for k in range(1, 8):
        m_wait(k)
    summed = wide32(mod[0])
    for k in range(1, 8):
        summed = summed + wide32(mod[k])
    own = x * 2 + c
    seqs[own, 0:32] = to_low(summed)
    seqs[own, 32:64] = cond_in[...]
    places = [x * 2 + 1 - c, (1 - x) * 2 + c, (1 - x) * 2 + 1 - c]

    def q_copy(k, at):
        return remote(seqs.at[own], seqs.at[at], q_send.at[k], q_recv.at[k], across[k])

    for k in range(3):
        q_copy(k, own).start()
    for k in range(1, 8):
        u_wait(k)
    xin[...] = to_low(stream[...] + wide32(branch[...]))
    gtok[...] = to_low(linear(swap_rows(), xin[...]))
    for k in (1, 2, 3):
        g_copy(2 + k, near[k - 1]).wait_recv()
    gain_o[...] = gains[3] + gain_at[3] + gain_at[4] + gain_at[5]
    c_copy(3).wait_recv()
    c_copy(5).start()
    pump(BLOCKS + 12)
    c_copy(4).wait_recv()
    c_copy(5).wait_recv()
    for n in range(6):
        c_copy(n).wait_send()
    keep_quarter.wait()
    for k in range(3):
        q_copy(k, places[k]).wait_recv()
    mod_o[...] = seqs[...]

    for now in (BLOCKS - 2, BLOCKS - 1):
        for l in range(2):
            copy0(now, l).wait_send()
            copy1(now, l).wait_send()
        copy2(now).wait_send()
        z_three(now).wait_send()
        share_copy(now).wait()

        @pl.when(middle)
        def _(now=now):
            z_two(now).wait_send()

    for k in range(1, 8):
        u_copy(k).wait_send()
        m_copy(k).wait_send()
        x_over(k - 1).wait_send() if k < 5 else x_copy(k - 4).wait_send()
    for k in range(3):
        q_copy(k, own).wait_send()
    for at, to in enumerate([twin, first, second] + near):
        g_copy(at, to).wait_send()


QUARTER = 1024
WEIGHT_ORDER = (11, 10, 13, 12, 15, 14, 17, 16, 9, 8, 7, 4, 5, 6, 3, 0, 1, 2)


def backward(*operands):
    low, full = jnp.bfloat16, jnp.float32
    dma = pltpu.SemaphoreType.DMA
    outs = [
        ((BLOCKS, WINDOW, WIDE), full),
        ((ROWS, WIDE), low),
        ((8, WIDE), full),
        ((4, TEXT, QUARTER), low),
        ((4, 64, 128), low),
    ]
    vmem = [
        ((2, WIDE, WIDE), low),
        ((4, WIDE, ROWS), low),
        ((11, ROWS, WIDE), low),
        ((3, ROWS, WIDE), low),
        ((2, ROWS, WIDE), low),
        ((2, ROWS, 128), full),
        ((ROWS, WIDE), low),
        ((2, ROWS, WIDE), low),
        ((8, MOD), full),
        ((8, WIDE), full),
        ((128, 128), full),
        ((ROWS, WIDE), full),
        ((ROWS, WIDE), full),
        ((ROWS, WIDE), low),
        ((ROWS, WIDE), low),
        ((8, MOD), full),
        ((2, WIDE, KEYS), low),
        ((2, WIDE, KEYS), low),
        ((4, TEXT, KEYS), low),
        ((3, TEXT, KEYS), low),
        ((TEXT, KEYS), low),
        ((2, 2, L, QUARTER), low),
        ((2, TEXT, QUARTER), low),
        ((2, TEXT, QUARTER), low),
        ((2, TEXT, QUARTER), low),
        ((TEXT, QUARTER), low),
        ((8, 32, 128), low),
        ((8, 32, 128), low),
        ((4, 64, 128), low),
        ((4, 8, WIDE), full),
        ((6, 8, WIDE), full),
        ((ROWS, WIDE), low),
        ((8, 32, WIDE), low),
        ((2, 4, LINE, WIDE), low),
        ((4, 4, LINE, WIDE), low),
        ((2, 4, LINE, WIDE), low),
        ((4, 2, LINE, WIDE), low),
        ((2, LINE, WIDE), low),
        ((4, LINE, WIDE), low),
        ((2, LINE, WIDE), full),
        ((4, LINE, WIDE), low),
        ((6, PAIR, WIDE), low),
        ((2, PAIR, WIDE), low),
        ((4, PAIR, WIDE), low),
        ((2, PAIR, WIDE), low),
        ((4, WINDOW, WIDE), low),
        ((2, WINDOW, WIDE), full),
    ]
    return pl.pallas_call(
        backward_kernel,
        out_shape=[jax.ShapeDtypeStruct(*shape) for shape in outs],
        in_specs=[ANY] * 16 + [IN_VMEM] * 4,
        out_specs=[ANY] + [IN_VMEM] * 2 + [ANY, IN_VMEM],
        scratch_shapes=[pltpu.VMEM(*shape) for shape in vmem]
        + [
            dma((40,)), dma((2,)), dma((2, 4)), dma((4, 4)), dma((2, 2)), dma((4, 2)), dma((2,)), dma((4,)),
            dma((3, 6)), dma((3, 6)), dma((2,)), dma((7,)), dma((7,)), dma((7,)), dma((7,)), dma((7,)), dma((7,)),
            dma((7,)), dma((7,)), dma((3,)), dma((3,)), dma((6,)), dma((6,)), dma((2,)), dma((6,)), dma((6,)), dma((1,)),
        ],
        compiler_params=pltpu.CompilerParams(
            collective_id=1, has_side_effects=True, vmem_limit_bytes=63 * MIB
        ),
        name="backward",
    )(*operands)


def finish_kernel(
    spread, caption_in, mod_in, gain_in,
    ada_o, bias_o, spatial_o, spatial_out_o, temporal_o, temporal_out_o, gain_o, query_o, caption_o, cross_o, hidden_o,
    hidden_out_o,
):
    seq, blk = lax.axis_index("seq"), lax.axis_index("blk")

    def share(t):
        return pltpu.roll(spread[t], (WINDOW - 4 * (blk // 2)) % WINDOW, 0)[0:SHARD]

    for j in range(3):
        lanes = slice(WIDE * j, WIDE * j + WIDE)
        spatial_o[:, lanes] = share(15 + j)
        temporal_o[:, lanes] = share(11 + j)
    spatial_out_o[...] = share(14)
    temporal_out_o[...] = share(10)
    query_o[...] = share(9)
    cross_o[...] = share(8)
    hidden = [share(4 + k) for k in range(4)]
    hidden_o[...] = jnp.zeros_like(hidden_o)
    for k, natural, placed in hidden_places():
        move_lanes(hidden_o, hidden[k], placed, natural, 4 * WIDE)
    for k in range(4):
        hidden_out_o[SHARD * k : SHARD * k + SHARD, :] = share(k)
    gain_o[...] = pltpu.roll(gain_in[...], (WIDE - SHARD * (seq * 8 + blk)) % WIDE, 1)[0:1, 0:SHARD]
    for q in range(4):
        caption_o[:, QUARTER * q : QUARTER * q + QUARTER] = wide32(caption_in[q])
    part = MOD // 8
    mods, conds = [], []
    for pack in range(4):
        rows = wide32(mod_in[pack])
        for video in range(2):
            first = MOD_TILES * video
            mods.append(jnp.concatenate([rows[first + i : first + i + 1] for i in range(MOD_TILES)], axis=1))
            first = 32 + WIDE // 128 * video
            conds.append(jnp.concatenate([rows[first + i : first + i + 1] for i in range(WIDE // 128)], axis=1))
    mods = pltpu.roll(jnp.concatenate(mods), (MOD_WIN - 16 * blk) % MOD_WIN, 1)[:, :part]
    bias_o[...] = jnp.sum(mods, axis=0, keepdims=True)
    ada_o[...] = tn(to_low(mods), to_low(jnp.concatenate(conds)))


def finish(spread, caption, mod, gain):
    full = jnp.float32
    outs = [
        (MOD // 8, WIDE), (1, MOD // 8), (SHARD, 3 * WIDE), (SHARD, WIDE), (SHARD, 3 * WIDE), (SHARD, WIDE),
        (1, SHARD), (SHARD, WIDE), (TEXT, 4 * QUARTER), (SHARD, WIDE), (SHARD, 4 * WIDE), (4 * SHARD, WIDE),
    ]
    return pl.pallas_call(
        finish_kernel,
        out_shape=[jax.ShapeDtypeStruct(shape, full) for shape in outs],
        in_specs=[IN_VMEM] * 4,
        out_specs=[IN_VMEM] * len(outs),
        compiler_params=pltpu.CompilerParams(vmem_limit_bytes=60 * MIB),
        name="finish",
    )(spread, caption, mod, gain)


TURN = np.arange(WIDE)[None, :] == (
    np.arange(WIDE).reshape(2, 2, 4, 2, SHARD).transpose(1, 0, 3, 2, 4).reshape(-1)
)[:, None]


def shards(
    tokens,
    segments,
    timesteps,
    caption,
    cotangent,
    ada_weight,
    ada_bias,
    spatial_in,
    spatial_out,
    temporal_in,
    temporal_out,
    cross_gain,
    cross_query,
    caption_proj,
    cross_out,
    hidden_in,
    hidden_out,
):
    frame_seg = segments[0]
    blk = lax.axis_index("blk")
    conditioning = to_low(jax.nn.silu(time_embedding(timesteps[0], WIDE)))
    cond_in = jnp.pad(conditioning.reshape(2 * WIDE // 128, 128), ((0, 32 - 2 * WIDE // 128), (0, 0)))
    frames = frame_seg.astype(jnp.float32)
    own_frames = lax.dynamic_slice(frames, (2 * blk,), (2,))
    seg_in = jnp.broadcast_to(
        jnp.stack(
            [jnp.repeat(frames, 16), jnp.repeat(own_frames, 128), jnp.tile(jnp.repeat(frames, 8), 2)]
        )[:, :, None],
        (3, ROWS, 128),
    )
    seg_row = jnp.broadcast_to(jnp.repeat(frames, 8)[None], (8, 128))
    turn = jnp.asarray(TURN, jnp.bfloat16)
    wide, out, *kept = forward(
        spatial_in,
        spatial_out,
        temporal_in,
        temporal_out,
        cross_query,
        cross_out,
        hidden_in,
        hidden_out,
        tokens.reshape(ROWS, WIDE),
        jnp.pad(cross_gain[None], ((0, 7), (0, 0))),
        jnp.pad(conditioning, ((0, 14), (0, 0))),
        ada_bias[None],
        seg_in,
        seg_row,
        cotangent.reshape(ROWS, WIDE),
        turn,
        ada_weight.T,
        caption[0],
        caption_proj.T,
    )
    spread, grad_tokens, grad_gain, grad_text, grad_mod = backward(
        wide, *kept, caption[0], seg_in, seg_row, turn, cond_in
    )
    (
        grad_ada,
        grad_bias,
        grad_sin,
        grad_sout,
        grad_tin,
        grad_tout,
        grad_gain,
        grad_query,
        grad_caption,
        grad_cout,
        grad_hin,
        grad_hout,
    ) = finish(spread, grad_text, grad_mod, grad_gain)
    return (
        out.reshape(tokens.shape),
        grad_tokens.reshape(tokens.shape),
        grad_ada.T,
        grad_bias[0],
        grad_sin,
        grad_sout,
        grad_tin,
        grad_tout,
        grad_gain[0],
        grad_query,
        grad_caption.T,
        grad_cout,
        grad_hin,
        grad_hout,
    )


def solution(mesh):
    fast = dict(mesh.shape) == {"seq": 4, "blk": 8}
    return jax.shard_map(
        shards if fast else general_shards,
        mesh=mesh,
        in_specs=(
            P("seq", "blk", None, None),
            P("seq", None),
            P("seq", None),
            P("seq", None, None, None),
            P("seq", "blk", None, None),
            P(None, "blk"),
            P("blk"),
            P(("seq", "blk"), None),
            P(("seq", "blk"), None),
            P(("seq", "blk"), None),
            P(("seq", "blk"), None),
            P(("seq", "blk")),
            P(("seq", "blk"), None),
            P(None, "blk"),
            P(("seq", "blk"), None),
            P(("seq", "blk"), None),
            P(("seq", "blk"), None),
        ),
        out_specs=(
            P("seq", "blk", None, None),
            P("seq", "blk", None, None),
            P(None, "blk"),
            P("blk"),
            P(("seq", "blk"), None),
            P(("seq", "blk"), None),
            P(("seq", "blk"), None),
            P(("seq", "blk"), None),
            P(("seq", "blk")),
            P(("seq", "blk"), None),
            P(None, "blk"),
            P(("seq", "blk"), None),
            P(("seq", "blk"), None),
            P(("seq", "blk"), None),
        ),
        check_vma=False,
    )
```

```python
import math

import jax
import jax.numpy as jnp
import numpy as np
from jax import lax
from jax.experimental import pallas as pl
from jax.experimental.pallas import tpu as pltpu
from jax.sharding import PartitionSpec as P

H = 16
E = 72
L = 120


EPSILON = 1e-06
MASKED = -1e30


def to_low(values):
    return values.astype(jnp.bfloat16)


def linear(left, right):
    return jnp.dot(left, right, preferred_element_type=jnp.float32)


def left_product(left, right):
    return lax.dot_general(
        left, right, (((0,), (0,)), ((), ())), preferred_element_type=jnp.float32
    )


def right_product(left, right):
    return lax.dot_general(
        left, right, (((1,), (1,)), ((), ())), preferred_element_type=jnp.float32
    )


def normalize(values):
    center = values - jnp.mean(values, axis=-1, keepdims=True)
    return center * lax.rsqrt(jnp.mean(center * center, axis=-1, keepdims=True) + EPSILON)


def modulate(values, shift_rows, scale_rows):
    return normalize(values) * (1.0 + scale_rows) + shift_rows


def gain_norm(values, gain_row):
    return normalize(values) * gain_row


def gelu_tanh(values):
    return jax.nn.gelu(values, approximate=True)


def softmax_rows(scores):
    shifted = jnp.exp(scores - jnp.max(scores, axis=-1, keepdims=True))
    return shifted / jnp.sum(shifted, axis=-1, keepdims=True)


def softmax_with_total(scores):
    top = jnp.max(scores, axis=-1, keepdims=True)
    shifted = jnp.exp(scores - top)
    total = jnp.sum(shifted, axis=-1, keepdims=True)
    return (shifted / total, (top + jnp.log(total))[..., 0])


def softmax_back(probs, grad_probs):
    return probs * (grad_probs - jnp.sum(grad_probs * probs, axis=-1, keepdims=True))


def time_embedding(step_ids, model_width):
    half_width = model_width // 2
    frequency = jnp.exp(
        -math.log(10000.0) * jnp.arange(half_width).astype(jnp.float32) / half_width
    )
    angles = step_ids.astype(jnp.float32)[:, None] * frequency[None, :]
    return jnp.concatenate([jnp.cos(angles), jnp.sin(angles)], axis=1)


def general_shards(
    tokens,
    segments,
    timesteps,
    caption,
    cotangent,
    ada_weight,
    ada_bias,
    spatial_in,
    spatial_out,
    temporal_in,
    temporal_out,
    cross_gain,
    cross_query,
    caption_proj,
    cross_out,
    hidden_in,
    hidden_out,
):
    inputs = tokens[0].astype(jnp.float32)
    patch_dev, frames, model_width = inputs.shape
    token_rows = patch_dev * frames
    head_count = H
    head_size = E
    score_scale = E ** (-0.5)
    frame_seg = segments[0]
    step_ids = timesteps[0]
    seg_count, text_len, text_width = caption.shape[1:]
    text_keys = seg_count * text_len
    caption_rows = caption[0].reshape(text_keys, text_width)
    grad_out = cotangent[0].astype(jnp.float32)
    gathered = (
        lax.all_gather(spatial_in, ("seq", "blk"), axis=0, tiled=True),
        lax.all_gather(spatial_out, ("seq", "blk"), axis=0, tiled=True),
        lax.all_gather(temporal_in, ("seq", "blk"), axis=0, tiled=True),
        lax.all_gather(temporal_out, ("seq", "blk"), axis=0, tiled=True),
        lax.all_gather(cross_gain, ("seq", "blk"), axis=0, tiled=True),
        lax.all_gather(cross_query, ("seq", "blk"), axis=0, tiled=True),
        lax.all_gather(cross_out, ("seq", "blk"), axis=0, tiled=True),
        lax.all_gather(hidden_in, ("seq", "blk"), axis=0, tiled=True),
        lax.all_gather(hidden_out, ("seq", "blk"), axis=0, tiled=True),
    )
    (
        wide_sin,
        wide_sout,
        wide_tin,
        wide_tout,
        gain_low,
        wide_query,
        wide_cout,
        wide_hin,
        wide_hout,
    ) = gathered
    gain_row = gain_low.astype(jnp.float32)
    conditioning = to_low(jax.nn.silu(time_embedding(step_ids, model_width)))
    mod_part = to_low(linear(conditioning, ada_weight) + ada_bias.astype(jnp.float32))
    text_part = to_low(linear(caption_rows, caption_proj))
    modulation, memory = (
        lax.all_gather(mod_part, "blk", axis=1, tiled=True),
        lax.all_gather(text_part, "blk", axis=1, tiled=True),
    )
    choose = frame_seg[:, None] == jnp.arange(seg_count, dtype=jnp.int32)[None, :]
    frame_mod = linear(choose.astype(jnp.bfloat16), modulation)
    pieces = [frame_mod[:, index * model_width : (index + 1) * model_width] for index in range(9)]
    (
        shift_one,
        scale_one,
        gate_one,
        shift_two,
        scale_two,
        gate_two,
        shift_three,
        scale_three,
        gate_three,
    ) = pieces
    spatial_input = to_low(modulate(inputs, shift_one, scale_one)).reshape(token_rows, model_width)
    spatial_qkv = to_low(linear(spatial_input, wide_sin)).reshape(
        patch_dev, frames, 3 * model_width
    )
    query_s = spatial_qkv[..., :model_width].reshape(patch_dev, frames, head_count, head_size)
    local_kv = spatial_qkv[..., model_width:]
    whole_kv = lax.all_gather(local_kv, "blk", axis=0, tiled=True)

    def split_kv(both):
        count = both.shape[0]
        return (
            both[..., :model_width].reshape(count, frames, head_count, head_size),
            both[..., model_width:].reshape(count, frames, head_count, head_size),
        )

    def spatial_probs(key_all):
        scores = jnp.einsum("pfhe,qfhe->fhpq", query_s, key_all, preferred_element_type=jnp.float32)
        return softmax_with_total(scores * score_scale)

    key_s, value_s = split_kv(whole_kv)
    probs_s, log_total_s = spatial_probs(key_s)
    probs_s_low = to_low(probs_s)
    attn_s = to_low(
        jnp.einsum(
            "fhpq,qfhe->pfhe", probs_s_low, value_s, preferred_element_type=jnp.float32
        ).reshape(token_rows, model_width)
    )
    branch_s = linear(attn_s, wide_sout).reshape(patch_dev, frames, model_width)
    after_one = inputs + gate_one * branch_s
    temporal_input = to_low(modulate(after_one, shift_two, scale_two)).reshape(
        token_rows, model_width
    )
    temporal_qkv = to_low(linear(temporal_input, wide_tin)).reshape(
        patch_dev, frames, 3, head_count, head_size
    )
    query_t = temporal_qkv[:, :, 0]
    key_t = temporal_qkv[:, :, 1]
    value_t = temporal_qkv[:, :, 2]
    same_seg = frame_seg[:, None] == frame_seg[None, :]
    scores_t = (
        jnp.einsum("pfhe,pghe->phfg", query_t, key_t, preferred_element_type=jnp.float32)
        * score_scale
    )
    probs_t = softmax_rows(jnp.where(same_seg[None, None], scores_t, MASKED))
    probs_t_low = to_low(probs_t)
    attn_t = to_low(
        jnp.einsum(
            "phfg,pghe->pfhe", probs_t_low, value_t, preferred_element_type=jnp.float32
        ).reshape(token_rows, model_width)
    )
    branch_t = linear(attn_t, wide_tout).reshape(patch_dev, frames, model_width)
    after_two = after_one + gate_two * branch_t
    cross_input = to_low(gain_norm(after_two, gain_row)).reshape(token_rows, model_width)
    query_c = to_low(linear(cross_input, wide_query)).reshape(
        patch_dev, frames, head_count, head_size
    )
    key_c = memory[:, :model_width].reshape(text_keys, head_count, head_size)
    value_c = memory[:, model_width:].reshape(text_keys, head_count, head_size)
    key_seg = jnp.arange(text_keys, dtype=jnp.int32) // text_len
    allowed = frame_seg[:, None] == key_seg[None, :]
    scores_c = (
        jnp.einsum("pfhe,khe->pfhk", query_c, key_c, preferred_element_type=jnp.float32)
        * score_scale
    )
    probs_c = softmax_rows(jnp.where(allowed[None, :, None, :], scores_c, MASKED))
    probs_c_low = to_low(probs_c)
    attn_c = to_low(
        jnp.einsum(
            "pfhk,khe->pfhe", probs_c_low, value_c, preferred_element_type=jnp.float32
        ).reshape(token_rows, model_width)
    )
    branch_c = linear(attn_c, wide_cout).reshape(patch_dev, frames, model_width)
    after_three = after_two + branch_c
    mlp_input = to_low(modulate(after_three, shift_three, scale_three)).reshape(
        token_rows, model_width
    )
    pre_act = linear(mlp_input, wide_hin)
    post_act = to_low(gelu_tanh(pre_act))
    branch_m = linear(post_act, wide_hout).reshape(patch_dev, frames, model_width)
    result = after_three + gate_three * branch_m
    grad_gate_three = jnp.sum(grad_out * branch_m, axis=0)
    grad_four = to_low(grad_out * gate_three).reshape(token_rows, model_width)
    grad_hout = left_product(post_act, grad_four)
    grad_post = right_product(grad_four, wide_hout)
    gelu_pull = jax.vjp(gelu_tanh, pre_act)[1]
    grad_pre = to_low(gelu_pull(grad_post)[0])
    grad_hin = left_product(mlp_input, grad_pre)
    grad_mlp_in = right_product(grad_pre, wide_hin).reshape(patch_dev, frames, model_width)
    mlp_pull = jax.vjp(modulate, after_three, shift_three, scale_three)[1]
    back_three, grad_shift_three, grad_scale_three = mlp_pull(grad_mlp_in)
    grad_three = grad_out + back_three
    grad_cross_branch = to_low(grad_three).reshape(token_rows, model_width)
    grad_cout = left_product(attn_c, grad_cross_branch)
    grad_attn_c = to_low(right_product(grad_cross_branch, wide_cout)).reshape(
        patch_dev, frames, head_count, head_size
    )
    grad_probs_c = jnp.einsum(
        "pfhe,khe->pfhk", grad_attn_c, value_c, preferred_element_type=jnp.float32
    )
    grad_scores_c = to_low(softmax_back(probs_c, grad_probs_c))
    grad_query_c = to_low(
        jnp.einsum("pfhk,khe->pfhe", grad_scores_c, key_c, preferred_element_type=jnp.float32)
        * score_scale
    ).reshape(token_rows, model_width)
    grad_key_c = (
        jnp.einsum("pfhk,pfhe->khe", grad_scores_c, query_c, preferred_element_type=jnp.float32)
        * score_scale
    )
    grad_value_c = jnp.einsum(
        "pfhk,pfhe->khe", probs_c_low, grad_attn_c, preferred_element_type=jnp.float32
    )
    grad_memory = jnp.concatenate(
        [grad_key_c.reshape(text_keys, model_width), grad_value_c.reshape(text_keys, model_width)],
        axis=1,
    )
    grad_wquery = left_product(cross_input, grad_query_c)
    grad_cross_in = right_product(grad_query_c, wide_query).reshape(patch_dev, frames, model_width)
    cross_pull = jax.vjp(gain_norm, after_two, gain_row)[1]
    back_two, grad_gain = cross_pull(grad_cross_in)
    grad_two = grad_three + back_two
    grad_gate_two = jnp.sum(grad_two * branch_t, axis=0)
    grad_temporal_branch = to_low(grad_two * gate_two).reshape(token_rows, model_width)
    grad_tout = left_product(attn_t, grad_temporal_branch)
    grad_attn_t = to_low(right_product(grad_temporal_branch, wide_tout)).reshape(
        patch_dev, frames, head_count, head_size
    )
    grad_probs_t = jnp.einsum(
        "pfhe,pghe->phfg", grad_attn_t, value_t, preferred_element_type=jnp.float32
    )
    grad_scores_t = to_low(softmax_back(probs_t, grad_probs_t))
    grad_query_t = (
        jnp.einsum("phfg,pghe->pfhe", grad_scores_t, key_t, preferred_element_type=jnp.float32)
        * score_scale
    )
    grad_key_t = (
        jnp.einsum("phfg,pfhe->pghe", grad_scores_t, query_t, preferred_element_type=jnp.float32)
        * score_scale
    )
    grad_value_t = jnp.einsum(
        "phfg,pfhe->pghe", probs_t_low, grad_attn_t, preferred_element_type=jnp.float32
    )
    grad_qkv_t = to_low(jnp.stack([grad_query_t, grad_key_t, grad_value_t], axis=2)).reshape(
        token_rows, 3 * model_width
    )
    grad_tin = left_product(temporal_input, grad_qkv_t)
    grad_temporal_in = right_product(grad_qkv_t, wide_tin).reshape(patch_dev, frames, model_width)
    temporal_pull = jax.vjp(modulate, after_one, shift_two, scale_two)[1]
    back_one, grad_shift_two, grad_scale_two = temporal_pull(grad_temporal_in)
    grad_one = grad_two + back_one
    grad_gate_one = jnp.sum(grad_one * branch_s, axis=0)
    grad_spatial_branch = to_low(grad_one * gate_one).reshape(token_rows, model_width)
    grad_sout = left_product(attn_s, grad_spatial_branch)
    grad_attn_s = to_low(right_product(grad_spatial_branch, wide_sout)).reshape(
        patch_dev, frames, head_count, head_size
    )
    back_kv = lax.all_gather(local_kv, "blk", axis=0, tiled=True)
    back_key, back_value = split_kv(back_kv)
    back_probs = spatial_probs(back_key)[0]
    back_probs_low = to_low(back_probs)
    grad_probs_s = jnp.einsum(
        "pfhe,qfhe->fhpq", grad_attn_s, back_value, preferred_element_type=jnp.float32
    )
    row_delta = jnp.sum(grad_probs_s * back_probs, axis=-1, keepdims=True)
    grad_scores_s = to_low(back_probs * (grad_probs_s - row_delta))
    grad_query_s = (
        jnp.einsum("fhpq,qfhe->pfhe", grad_scores_s, back_key, preferred_element_type=jnp.float32)
        * score_scale
    )
    count = lax.axis_size("blk") * patch_dev
    grad_key = (
        jnp.einsum("fhpq,pfhe->qfhe", grad_scores_s, query_s, preferred_element_type=jnp.float32)
        * score_scale
    )
    grad_value = jnp.einsum(
        "fhpq,pfhe->qfhe", back_probs_low, grad_attn_s, preferred_element_type=jnp.float32
    )
    grad_kv = to_low(
        lax.psum_scatter(
            jnp.concatenate(
                [
                    grad_key.reshape(count, frames, model_width),
                    grad_value.reshape(count, frames, model_width),
                ],
                axis=2,
            ).astype(jnp.bfloat16),
            "blk",
            scatter_dimension=0,
            tiled=True,
        ).astype(jnp.float32)
    )
    grad_qkv_s = jnp.concatenate(
        [to_low(grad_query_s).reshape(patch_dev, frames, model_width), grad_kv], axis=2
    ).reshape(token_rows, 3 * model_width)
    grad_sin = left_product(spatial_input, grad_qkv_s)
    grad_spatial_in = right_product(grad_qkv_s, wide_sin).reshape(patch_dev, frames, model_width)
    spatial_pull = jax.vjp(modulate, inputs, shift_one, scale_one)[1]
    back_zero, grad_shift_one, grad_scale_one = spatial_pull(grad_spatial_in)
    grad_input = grad_one + back_zero
    grad_frame_mod = jnp.concatenate(
        [
            grad_shift_one,
            grad_scale_one,
            grad_gate_one,
            grad_shift_two,
            grad_scale_two,
            grad_gate_two,
            grad_shift_three,
            grad_scale_three,
            grad_gate_three,
        ],
        axis=1,
    )
    grad_mod_local = lax.dot_general(
        choose.astype(jnp.float32),
        grad_frame_mod,
        (((0,), (0,)), ((), ())),
        precision=lax.Precision.HIGHEST,
    )
    grad_mod_part, grad_memory_part = (
        lax.psum_scatter(
            grad_mod_local.astype(jnp.bfloat16), "blk", scatter_dimension=1, tiled=True
        ).astype(jnp.float32),
        lax.psum_scatter(
            grad_memory.astype(jnp.bfloat16), "blk", scatter_dimension=1, tiled=True
        ).astype(jnp.float32),
    )
    grad_mod_low = to_low(grad_mod_part)
    grad_ada_w = left_product(conditioning, grad_mod_low)
    grad_ada_b = jnp.sum(grad_mod_low.astype(jnp.float32), axis=0)
    grad_caption = left_product(caption_rows, to_low(grad_memory_part))
    grad_ada_w, grad_ada_b, grad_caption = (
        lax.psum(grad_ada_w.astype(jnp.bfloat16), "seq").astype(jnp.float32),
        lax.psum(grad_ada_b.astype(jnp.bfloat16), "seq").astype(jnp.float32),
        lax.psum(grad_caption.astype(jnp.bfloat16), "seq").astype(jnp.float32),
    )
    shares = (
        lax.psum_scatter(grad_sin, ("seq", "blk"), scatter_dimension=0, tiled=True),
        lax.psum_scatter(grad_sout, ("seq", "blk"), scatter_dimension=0, tiled=True),
        lax.psum_scatter(grad_tin, ("seq", "blk"), scatter_dimension=0, tiled=True),
        lax.psum_scatter(grad_tout, ("seq", "blk"), scatter_dimension=0, tiled=True),
        lax.psum_scatter(grad_gain, ("seq", "blk"), scatter_dimension=0, tiled=True),
        lax.psum_scatter(grad_wquery, ("seq", "blk"), scatter_dimension=0, tiled=True),
        lax.psum_scatter(grad_cout, ("seq", "blk"), scatter_dimension=0, tiled=True),
        lax.psum_scatter(grad_hin, ("seq", "blk"), scatter_dimension=0, tiled=True),
        lax.psum_scatter(grad_hout, ("seq", "blk"), scatter_dimension=0, tiled=True),
    )
    (
        share_sin,
        share_sout,
        share_tin,
        share_tout,
        share_gain,
        share_query,
        share_cout,
        share_hin,
        share_hout,
    ) = shares
    return (
        to_low(result)[None],
        to_low(grad_input)[None],
        grad_ada_w,
        grad_ada_b,
        share_sin,
        share_sout,
        share_tin,
        share_tout,
        share_gain,
        share_query,
        grad_caption,
        share_cout,
        share_hin,
        share_hout,
    )


MESH = pl.DeviceIdType.MESH
BLOCKS = 18
LINES = 8
SHARD = 36
LINE = 4 * SHARD
WINDOW = 48
WIDE = LINES * LINE
MIB = 2**20


def place():
    seq = lax.axis_index("seq")
    blk = lax.axis_index("blk")
    x, c = seq // 2, seq % 2
    z, y = blk // 2, blk % 2
    x1, y1 = x + (1 - 2 * x) * (1 - c), y + (1 - 2 * y) * c
    x2, y2 = x + (1 - 2 * x) * c, y + (1 - 2 * y) * (1 - c)
    return x, c, y, z, x1, y1, x2, y2


def device(x, c, y, z):
    return {"seq": x * 2 + c, "blk": z * 2 + y}


def line_of(c, x, y):
    return (c * 2 + x) * 2 + y


def remote(src, dst, send_sem, recv_sem, where):
    return pltpu.make_async_remote_copy(
        src_ref=src,
        dst_ref=dst,
        send_sem=send_sem,
        recv_sem=recv_sem,
        device_id=where,
        device_id_type=MESH,
    )


def greet(others):
    barrier = pltpu.get_barrier_semaphore()
    for other in others:
        pl.semaphore_signal(barrier, inc=1, device_id=other, device_id_type=MESH)
    pl.semaphore_wait(barrier, len(others))


def left_at(t):
    at = jnp.minimum(t, 4)
    for first in (8, 9, 10, 11, 14, 15):
        at = at + jnp.where(t >= first, 1, 0)
    return at


def right_at(t):
    return jnp.where(t < 14, jnp.maximum(t - 3, 0), t - 13)


ROWS = 256
KEYS = 256
TEXT = 288
MOD = 9 * WIDE
MOD_TILES = 11
MOD_WIN = 128 * MOD_TILES
PARTS, HELD, LAST = 4, 4, 8
PAIR = 80
LEFT_SEM, SLOPE_SEM, SAVE_SEMS = 40, 42, 44
TILE = 384
SCALE = E ** (-0.5)


def nt(left, right):
    return lax.dot_general(
        left, right, (((1,), (1,)), ((), ())), preferred_element_type=jnp.float32
    )


def wide32(values):
    return values.astype(jnp.float32)


def loop(count, body):
    def step(index, carry):
        body(index)
        return carry

    lax.fori_loop(0, count, step, 0)


def each_rows(size, body, total=ROWS):
    loop(total // size, lambda i: body(pl.ds(pl.multiple_of(i * size, size), size)))


def each_cols(body):
    loop(WIDE // TILE, lambda i: body(pl.ds(pl.multiple_of(i * TILE, TILE), TILE)))


def swap_rows():
    row = lax.broadcasted_iota(jnp.int32, (ROWS, ROWS), 0)
    col = lax.broadcasted_iota(jnp.int32, (ROWS, ROWS), 1)
    return to_low((((row & 15) << 4) + (row >> 4) == col).astype(jnp.float32))


def head_window(h):
    base = h * E
    start = jnp.minimum(base // 128, 7) * 128
    lane = lax.broadcasted_iota(jnp.int32, (1, 256), 1)
    on = (lane >= base - start) & (lane < base - start + E)
    return pl.ds(pl.multiple_of(start, 128), 256), on.astype(jnp.float32)


def soft(scores, bias, mask):
    scores = scores * SCALE
    if bias is not None:
        scores = scores + bias
    powers = jnp.exp(scores - jnp.max(scores, axis=-1, keepdims=True))
    probs = powers * (1.0 / jnp.sum(powers, axis=-1, keepdims=True))
    return probs if mask is None else probs * mask


def chains(h, groups):
    return [(window, rows, keys) for window in (head_window(h), head_window(h + H // 2)) for rows, keys in groups]


def split_rows(values, jobs):
    start = 0
    parts = []
    for _, rows, _ in jobs:
        size = rows.stop - rows.start
        parts.append(values[start : start + size])
        start += size
    return parts


def heads_forward(h, query, key, value, attn, groups, bias, mask):
    jobs = chains(h, groups)
    scores = [nt(query[rows, lanes] * to_low(on), key[keys, lanes]) for (lanes, on), rows, keys in jobs]
    probs = split_rows(to_low(soft(jnp.concatenate(scores), bias, mask)), jobs)
    parts = [linear(prob, value[keys, lanes]) * on for prob, ((lanes, on), rows, keys) in zip(probs, jobs)]
    for part, ((lanes, on), rows, keys) in zip(parts, jobs):
        attn[rows, lanes] = attn[rows, lanes] + to_low(part)


def text_heads_forward(h, query, key, value, attn, bias, mask):
    jobs = chains(h, VIDEOS)
    scores = [linear(query[rows, lanes] * to_low(on), key[lanes, keys]) for (lanes, on), rows, keys in jobs]
    probs = split_rows(to_low(soft(jnp.concatenate(scores), bias, mask)), jobs)
    parts = [nt(prob, value[lanes, keys]) * on for prob, ((lanes, on), rows, keys) in zip(probs, jobs)]
    for part, ((lanes, on), rows, keys) in zip(parts, jobs):
        attn[rows, lanes] = attn[rows, lanes] + to_low(part)


HALVES = [(slice(0, 128), slice(0, 128)), (slice(128, 256), slice(128, 256))]
VIDEOS = [(slice(0, 144), slice(0, 128)), (slice(112, 256), slice(128, 256))]


def regroup(back):
    row = lax.broadcasted_iota(jnp.int32, (ROWS, ROWS), 0)
    col = lax.broadcasted_iota(jnp.int32, (ROWS, ROWS), 1)
    if back:
        source = (((row >> 3) & 1) << 7) + ((row >> 4) << 3) + (row & 7)
    else:
        source = (((row >> 3) & 15) << 4) + ((row >> 7) << 3) + (row & 7)
    return to_low((source == col).astype(jnp.float32))


def temporal_bias(seg_in, seg_row):
    row = lax.broadcasted_iota(jnp.int32, (128, 128), 0)
    col = lax.broadcasted_iota(jnp.int32, (128, 128), 1)
    allowed = ((row & 7) == (col & 7)) & (seg_in[2, 0:128, 0:1] == seg_row[0:1, 0:128])
    return jnp.where(allowed, 0.0, MASKED)


def cross_bias():
    col = lax.broadcasted_iota(jnp.int32, (1, 128), 1)
    return jnp.where(col < L, 0.0, MASKED)


def cross_rows(seg_in):
    both = [1.0 - seg_in[0, 0:144, 0:1], seg_in[0, 112:256, 0:1]]
    return jnp.concatenate(both + both)


def move_lanes(to, value, from_start, to_start, width):
    left = min(from_start // 128 * 128, value.shape[1] - 256)
    right = min(to_start // 128 * 128, width - 256)
    off = to_start - right
    part = pltpu.roll(value[:, left : left + 256], (off - (from_start - left)) % 256, 1)
    lane = lax.broadcasted_iota(jnp.int32, part.shape, 1)
    lanes = slice(right, right + 256)
    to[:, lanes] = jnp.where((lane >= off) & (lane < off + SHARD), part, to[:, lanes])


def hidden_places():
    places = []
    for d in range(32):
        xp, cp, zp, yp = d // 16, d // 8 % 2, d // 2 % 4, d % 2
        for k in range(4):
            places.append((k, (4 * d + k) * SHARD, (((cp * 2 + xp) * 2 + yp) * 4 + zp) * SHARD))
    return places


def blk_peers(x, c, b):
    return [device(x, c, (b + k) % 2, ((b + k) % 8) // 2) for k in range(1, 8)]


def forward_kernel(
    spatial_in, spatial_out, temporal_in, temporal_out, cross_query, cross_out, hidden_in, hidden_out,
    tok, gain_one, cond, ada_bias, seg_in, seg_row, cot_i, turn_i, ada_i, caption_i, proj_i,
    wide, out, left_o, qkvs_o, qkvt_o, qc_o, mem_o, xhat_o, rstd_o, branch_o, slope_o, gfour_o, cot_o, mods_o, gate_o, gain_o,
    win, pair, far, lines, weights, tokp, cotp, tokf, xin, xp, left, qkvs, qkvt, qc, mem, text, mod, mods, xhat, rstd, branch, branchw, bias,
    stream, attnf, attnp, post, slope, gfour, gains, gain_at, gate,
    src, cot, turn, ada, caption, proj, mod_in, text_in, hidden,
    z_send, z_recv, l_send, l_recv, own_sem, w_sem, t_send, t_recv, a_send, a_recv, m_send, m_recv, x_send, x_recv,
    g_send, g_recv, save_sem, in_sem,
):
    x, c, y, z, x1, y1, x2, y2 = place()
    b = z * 2 + y
    near = [device(x, c, y, (z + k) % 4) for k in (1, 2, 3)]
    beside, across = device(x, c, y, z + 1 - 2 * (z % 2)), device(x, c, y, 3 - z)
    middle = (z == 1) | (z == 2)
    first, second, twin = device(x1, c, y1, z), device(x2, c, y2, z), device(x, 1 - c, y, z)
    peers = blk_peers(x, c, b)
    greet(peers + [device(1 - x, c, y, z), twin])
    mine, line3 = line_of(c, x, y), line_of(c, 1 - x, 1 - y)

    def hops(t, core):
        turn_round = core + (1 - core) * (t % 4 == 2)
        xa, ya = x + (1 - 2 * x) * (1 - turn_round), y + (1 - 2 * y) * turn_round
        xb, yb = x + (1 - 2 * x) * turn_round, y + (1 - 2 * y) * (1 - turn_round)
        return (xa, ya), (xb, yb)

    def z_one(t):
        return remote(src.at[t], win.at[t % PARTS], z_send.at[t, 0], z_recv.at[t, 0], beside)

    def z_two(t):
        return remote(pair.at[t % PARTS], far.at[t % PARTS], z_send.at[t, 1], z_recv.at[t, 1], across)

    def z_three(t):
        return remote(far.at[t % PARTS], far.at[t % PARTS], z_send.at[t, 2], z_recv.at[t, 2], beside)

    def wide_line(t, line):
        return wide.at[t, pl.ds(pl.multiple_of(line * LINE, 16), LINE)]

    def own(t):
        return pltpu.make_async_copy(lines.at[t % HELD], wide_line(t, mine), own_sem.at[t])

    def line_copy(t, to, line, index, where):
        return remote(to, wide_line(t, line), l_send.at[t, index], l_recv.at[t, index], where)

    def sends(t, index):
        (xa, ya), (xb, yb) = hops(t, c)
        one, two = device(xa, c, ya, z), device(xb, c, yb, z)
        line1, line2 = line_of(c, xa, ya), line_of(c, xb, yb)
        line, where = (
            (mine, one), (mine, two), (mine, twin), (line1, two),
            (line1, twin), (line2, twin), (line3, twin),
        )[index]
        from_here = lines.at[t % HELD] if index < 3 else wide_line(t, line)
        return line_copy(t, from_here, line, index, where)

    def arrives(t, line, index):
        line_copy(t, wide_line(t, line), line, index, first).wait_recv()

    def tick(t):
        @pl.when((t >= 4) & (t < BLOCKS + 4))
        def _():
            now = t - 4

            @pl.when(middle)
            def _():
                z_two(now).wait_send()
                z_three(now).wait_send()

            @pl.when(jnp.logical_not(middle))
            def _():
                z_three(now).wait_recv()

            @pl.when(now >= HELD)
            def _():
                for index in range(3):
                    sends(now - HELD, index).wait_send()
                own(now - HELD).wait()

            def line_from(low, high):
                at = now % HELD
                lines[at, 0:64] = low[0:64]
                lines[at, 64:80] = low[64:80] + high[0:16]
                lines[at, 80:144] = high[16:80]

            @pl.when(z < 2)
            def _():
                line_from(pair[now % PARTS], far[now % PARTS])

            @pl.when(z >= 2)
            def _():
                line_from(far[now % PARTS], pair[now % PARTS])

            for index in range(3):
                sends(now, index).start()
            own(now).start()

        @pl.when((t >= 2) & (t < BLOCKS + 2) & middle)
        def _():
            z_two(t - 2).wait_recv()
            z_three(t - 2).start()

        @pl.when((t >= 1) & (t < BLOCKS + 1))
        def _():
            now = t - 1
            z_one(now).wait_recv()

            def pair_from(even, odd):
                at = now % PARTS
                pair[at, 0:32] = even[0:32]
                pair[at, 32:48] = even[32:48] + odd[0:16]
                pair[at, 48:80] = odd[16:48]

            @pl.when(z % 2 == 0)
            def _():
                pair_from(src[now], win[now % PARTS])

            @pl.when(z % 2 == 1)
            def _():
                pair_from(win[now % PARTS], src[now])

            @pl.when(middle)
            def _():
                z_two(now).start()

        @pl.when(t < BLOCKS)
        def _():
            z_one(t).start()

        @pl.when((t >= 6) & (t < BLOCKS + 6))
        def _():
            now = t - 6
            xa, ya = hops(now, c)[0]
            arrives(now, line_of(c, xa, ya), 0)
            for index in (3, 4):
                sends(now, index).start()

        @pl.when(t >= LAST)
        def _():
            now = t - LAST
            xb, yb = hops(now, c)[1]
            arrives(now, line_of(c, xb, yb), 1)
            sends(now, 5).start()
            arrives(now, line3, 3)
            sends(now, 6).start()

    done = [0]

    def pump(until):
        until = min(until, BLOCKS + LAST)
        if until > done[0]:
            start = done[0]
            loop(until - start, lambda i: tick(i + start))
            done[0] = until

    def poke():
        pump(done[0] + 1)

    def load(block):
        pump(block + LAST + 1)
        near_at, far_at = hops(block, 1 - c)
        places = [(x, y), near_at, far_at, (1 - x, 1 - y)]
        for (xl, yl), index in zip(places, (2, 4, 5, 6)):
            arrives(block, line_of(1 - c, xl, yl), index)
        if block >= BLOCKS - HELD:
            own(block).wait()
        copy = pltpu.make_async_copy(wide.at[block], weights.at[block % 2], w_sem.at[block % 2])
        copy.start()
        copy.wait()

    def times(values, block, emit):
        def tile(cols):
            emit(cols, linear(values[...], weights[block % 2, :, cols]))

        each_cols(tile)

    saves = []
    held = {}

    def save(from_ref, to_ref, name=None):
        if name is None:
            name = len(saves)
            saves.append(name)
        held[name] = pltpu.make_async_copy(from_ref, to_ref, save_sem.at[name])
        held[name].start()

    def settle(name):
        if name in held:
            held.pop(name).wait()

    def turned(values, index):
        slot = index % 2
        settle(LEFT_SEM + slot)

        def tile(cols):
            xp[:, cols] = to_low(nt(values[...], turn[cols, :]))
            left[slot, cols, :] = to_low(nt(turn[cols, :], values[...]))

        each_cols(tile)
        save(left.at[slot], left_o.at[index], LEFT_SEM + slot)

    fetches = [
        pltpu.make_async_copy(from_ref, to_ref, in_sem.at[at])
        for at, (from_ref, to_ref) in enumerate(
            ((ada_i, ada), (turn_i, turn), (cot_i, cot), (caption_i, caption), (proj_i, proj))
        )
    ]
    for copy in fetches:
        copy.start()

    def shift(rows, first):
        row = lax.broadcasted_iota(jnp.int32, (WINDOW, rows), 0) - 4 * z
        col = lax.broadcasted_iota(jnp.int32, (WINDOW, rows), 1)
        return to_low(((row >= 0) & (row < SHARD) & (row + first == col)).astype(jnp.float32))

    def window(at, values):
        src[at] = to_low(linear(shift(SHARD, 0), values))

    for j in range(3):
        window(j, spatial_in[:, WIDE * j : WIDE * j + WIDE])
    pump(2)
    window(3, spatial_out[...])
    for j in range(3):
        window(4 + j, temporal_in[:, WIDE * j : WIDE * j + WIDE])
    window(7, temporal_out[...])
    window(8, cross_query[...])
    window(9, cross_out[...])
    pump(4)

    def m_copy(k, at):
        return remote(mod_in, mod.at[at], m_send.at[k - 1], m_recv.at[k - 1], peers[k - 1])

    fetches[0].wait()
    part = wide32(to_low(nt(cond[...], ada[...]) + wide32(ada_bias[...])))[0:8]
    part = jnp.concatenate([part, jnp.zeros((8, MOD_WIN - MOD // 8), jnp.float32)], axis=1)
    part = pltpu.roll(part, 16 * b, 1)
    tiles = [part[row : row + 1, 128 * tile : 128 * tile + 128] for row in range(2) for tile in range(MOD_TILES)]
    mod_in[...] = to_low(jnp.concatenate(tiles + [jnp.zeros((32 - 2 * MOD_TILES, 128), jnp.float32)]))
    for k in range(1, 8):
        m_copy(k, b).start()
    mod[b] = mod_in[...]
    swap = swap_rows()
    tokp[...] = to_low(linear(swap, tok[...]))

    def t_copy(k):
        to = (b + k) % 8
        part = tokp.at[pl.ds(pl.multiple_of(32 * to, 32), 32)]
        return remote(part, tokf.at[b], t_send.at[k - 1], t_recv.at[k - 1], peers[k - 1])

    def t_wait(k):
        of = (b + 8 - k) % 8
        remote(tokp.at[pl.ds(0, 32)], tokf.at[of], t_send.at[k - 1], t_recv.at[k - 1], peers[k - 1]).wait_recv()

    pump(5)
    for k in range(1, 8):
        t_copy(k).start()
    tokf[b] = tokp[pl.ds(pl.multiple_of(32 * b, 32), 32)]

    def g_copy(at, from_at, to):
        return remote(gains.at[from_at], gain_at.at[at], g_send.at[at], g_recv.at[at], to)

    spread = jnp.concatenate([wide32(gain_one[...]), jnp.zeros((8, WIDE - SHARD), jnp.float32)], axis=1)
    gains[0] = pltpu.roll(spread, SHARD * ((x * 2 + c) * 8 + b), 1)
    g_copy(0, 0, twin).start()
    pump(6)
    fetches[2].wait()
    cotp[...] = to_low(linear(swap, cot[...]))
    save(cotp, cot_o)

    def x_copy(k, at):
        return remote(text_in, text.at[at, y], x_send.at[k - 1], x_recv.at[k - 1], near[k - 1])

    def x_over(at):
        return remote(text.at[:, at], text.at[:, at], x_send.at[3], x_recv.at[3], device(x, c, 1 - y, z))

    for k in range(1, 8):
        m_copy(k, (b + 8 - k) % 8).wait_recv()
    mods[...] = jnp.zeros_like(mods)
    for k in range(8):
        part = wide32(mod[k])
        for row in range(2):
            for tile in range(MOD_TILES):
                lanes = slice(1280 * k + 128 * tile, 1280 * k + 128 * tile + 128)
                at = row * MOD_TILES + tile
                mods[row : row + 1, lanes] = mods[row : row + 1, lanes] + part[at : at + 1]
    save(mods, mods_o)
    g_copy(0, 0, twin).wait_recv()
    gains[1] = gains[0] + gain_at[0]
    g_copy(1, 1, first).start()
    pump(7)
    fetches[3].wait()
    fetches[4].wait()
    text_in[...] = jnp.zeros_like(text_in)
    for v in range(2):
        text_in[:, 128 * v : 128 * v + L] = to_low(nt(proj[...], caption[v]))
    for k in (1, 2, 3):
        x_copy(k, z).start()
    text[z, y] = text_in[...]
    pump(8)
    hidden[...] = jnp.zeros_like(hidden)
    for k, natural, placed in hidden_places():
        start = natural // WIDE * WIDE
        move_lanes(hidden.at[k], wide32(hidden_in[:, start : start + WIDE]), natural - start, placed, WIDE)
    for k in range(4):
        window(10 + 2 * k, to_low(hidden[k]))
        src[11 + 2 * k] = to_low(linear(shift(4 * SHARD, SHARD * k), hidden_out[...]))
    fetches[1].wait()

    def pick(piece, seg):
        lanes = slice(WIDE * piece, WIDE * piece + WIDE)
        return jnp.where(seg > 0.5, mods[1:2, lanes], mods[0:1, lanes])

    def normal(values, rows, index):
        center = values - jnp.mean(values, axis=-1, keepdims=True)
        factor = lax.rsqrt(jnp.mean(center * center, axis=-1, keepdims=True) + EPSILON)
        scaled = center * factor
        xhat[index, rows, :] = to_low(scaled)
        rstd[index, rows, :] = jnp.broadcast_to(factor, (factor.shape[0], 128))
        return scaled

    for k in range(1, 8):
        t_wait(k)
    g_copy(1, 1, first).wait_recv()
    gains[2] = gains[1] + gain_at[1]
    g_copy(2, 2, second).start()

    def spatial_rows(i):
        seg = jnp.concatenate([seg_in[1, 0:16, 0:1], seg_in[1, 128:144, 0:1]])
        values = wide32(tokf[i])
        center = values - jnp.mean(values, axis=-1, keepdims=True)
        factor = lax.rsqrt(jnp.mean(center * center, axis=-1, keepdims=True) + EPSILON)
        scaled = center * factor
        ready = to_low(scaled * (1.0 + pick(1, seg)) + pick(0, seg))
        low = to_low(scaled)
        spread = jnp.broadcast_to(factor, (32, 128))
        for f in range(2):
            rows = pl.ds(pl.multiple_of(128 * f + 16 * i, 16), 16)
            part = slice(16 * f, 16 * f + 16)
            xhat[0, rows, :] = low[part]
            rstd[0, rows, :] = spread[part]
            xin[rows, :] = ready[part]

    loop(8, spatial_rows)
    save(xhat.at[0], xhat_o.at[0])
    save(rstd.at[0], rstd_o.at[0])
    turned(xin, 10)
    for j in range(3):
        load(j)

        def emit(cols, value, j=j):
            qkvs[j, :, cols] = to_low(value)

        times(xp, j, emit)
    save(qkvs, qkvs_o)
    g_copy(2, 2, second).wait_recv()
    gains[3] = gains[2] + gain_at[2]
    for k in (1, 2, 3):
        remote(gains.at[3], gain_at.at[2 + k], g_send.at[2 + k], g_recv.at[2 + k], near[k - 1]).start()
    for k in (1, 2, 3):
        x_copy(k, (z + 4 - k) % 4).wait_recv()
    x_over(y).start()
    attnf[...] = jnp.zeros_like(attnf)

    def spatial_heads(h):
        heads_forward(h, qkvs.at[0], qkvs.at[1], qkvs.at[2], attnf, HALVES, None, None)

    loop(4, spatial_heads)
    poke()
    loop(4, lambda h: spatial_heads(h + 4))
    for k in (1, 2, 3):
        remote(gains.at[3], gain_at.at[2 + k], g_send.at[2 + k], g_recv.at[2 + k], near[k - 1]).wait_recv()
    gains[0 + 4] = gains[3] + gain_at[3] + gain_at[4] + gain_at[5]
    save(gains.at[4], gain_o)

    def a_copy(k, f):
        to = (b + k) % 8
        part = attnf.at[pl.ds(pl.multiple_of(128 * f + 16 * to, 16), 16)]
        return remote(part, attnp.at[2 * b + f], a_send.at[k - 1, f], a_recv.at[k - 1, f], peers[k - 1])

    def a_wait(k, f):
        of = (b + 8 - k) % 8
        part = attnf.at[pl.ds(0, 16)]
        remote(part, attnp.at[2 * of + f], a_send.at[k - 1, f], a_recv.at[k - 1, f], peers[k - 1]).wait_recv()

    for k in range(1, 8):
        for f in range(2):
            a_copy(k, f).start()
    for f in range(2):
        attnp[2 * b + f] = attnf[pl.ds(pl.multiple_of(128 * f + 16 * b, 16), 16)]
    pump(done[0] + 2)
    for k in range(1, 8):
        for f in range(2):
            a_wait(k, f)
    xin[...] = attnp[...].reshape(ROWS, WIDE)
    turned(xin, 9)
    load(3)

    def emit_branch(cols, value):
        branchw[:, cols] = value

    times(xp, 3, emit_branch)

    def after_spatial(rows):
        seg = seg_in[0, rows, 0:1]
        value = branchw[rows, :]
        branch[0, rows, :] = to_low(value)
        value = wide32(tokp[rows, :]) + pick(2, seg) * value
        stream[rows, :] = value
        xin[rows, :] = to_low(normal(value, rows, 1) * (1.0 + pick(4, seg)) + pick(3, seg))

    each_rows(32, after_spatial)
    save(branch.at[0], branch_o.at[0])
    save(xhat.at[1], xhat_o.at[1])
    save(rstd.at[1], rstd_o.at[1])

    for k in range(1, 8):
        for f in range(2):
            a_copy(k, f).wait_send()
    attnf[...] = to_low(linear(regroup(False), xin[...]))
    turned(attnf, 8)
    for j in range(3):
        load(4 + j)

        def emit(cols, value, j=j):
            qkvt[j, :, cols] = to_low(value)

        times(xp, 4 + j, emit)
    save(qkvt, qkvt_o)
    attnf[...] = jnp.zeros_like(attnf)

    bias[...] = temporal_bias(seg_in, seg_row)

    def temporal_heads(h):
        heads_forward(
            h, qkvt.at[0], qkvt.at[1], qkvt.at[2], attnf, HALVES, jnp.concatenate([bias[...]] * 4), None
        )

    loop(4, temporal_heads)
    poke()
    loop(4, lambda h: temporal_heads(h + 4))
    xin[...] = to_low(linear(regroup(True), attnf[...]))
    turned(xin, 7)
    load(7)
    times(xp, 7, emit_branch)

    def after_temporal(rows):
        seg = seg_in[0, rows, 0:1]
        value = branchw[rows, :]
        branch[1, rows, :] = to_low(value)
        value = stream[rows, :] + pick(5, seg) * value
        stream[rows, :] = value
        xin[rows, :] = to_low(normal(value, rows, 2) * gains[4, 0:1, :])

    each_rows(32, after_temporal)
    save(branch.at[1], branch_o.at[1])
    save(xhat.at[2], xhat_o.at[2])
    save(rstd.at[2], rstd_o.at[2])

    turned(xin, 6)
    load(8)

    def emit_query(cols, value):
        qc[:, cols] = to_low(value)

    times(xp, 8, emit_query)
    save(qc, qc_o)
    x_over(1 - y).wait_recv()
    for k in range(8):
        mem[k // 4, TEXT * (k % 4) : TEXT * (k % 4) + TEXT, :] = text[k // 2, k % 2]
    save(mem, mem_o)
    attnf[...] = jnp.zeros_like(attnf)

    def cross_heads(h):
        text_heads_forward(h, qc, mem.at[0], mem.at[1], attnf, cross_bias(), cross_rows(seg_in))

    loop(4, cross_heads)
    poke()
    loop(4, lambda h: cross_heads(h + 4))
    xin[...] = attnf[...]
    turned(xin, 5)
    load(9)
    times(xp, 9, emit_branch)

    def after_cross(rows):
        seg = seg_in[0, rows, 0:1]
        value = stream[rows, :] + branchw[rows, :]
        stream[rows, :] = value
        xin[rows, :] = to_low(normal(value, rows, 3) * (1.0 + pick(7, seg)) + pick(6, seg))
        gfour[rows, :] = to_low(wide32(cotp[rows, :]) * pick(8, seg))

    each_rows(32, after_cross)
    save(xhat.at[3], xhat_o.at[3])
    save(rstd.at[3], rstd_o.at[3])
    save(gfour, gfour_o)

    turned(xin, 4)
    same = (
        lax.broadcasted_iota(jnp.int32, (TILE, TILE), 0) == lax.broadcasted_iota(jnp.int32, (TILE, TILE), 1)
    ).astype(jnp.float32).astype(jnp.bfloat16)
    for k in range(4):
        slot = k % 2
        load(10 + 2 * k)
        settle(SLOPE_SEM + slot)
        settle(LEFT_SEM + slot)

        def emit_hidden(cols, value, slot=slot):
            inner = math.sqrt(2.0 / math.pi) * (value + 0.044715 * value * value * value)
            bent = jnp.tanh(inner)
            half = 0.5 * (1.0 + bent)
            tilt = math.sqrt(2.0 / math.pi) * (1.0 + 3 * 0.044715 * value * value)
            slope[slot, :, cols] = to_low(half + 0.5 * value * (1.0 - bent * bent) * tilt)
            low = to_low(value * half)
            post[:, cols] = low
            left[slot, cols, :] = to_low(nt(same, low))

        times(xp, 10 + 2 * k, emit_hidden)
        save(slope.at[slot], slope_o.at[k], SLOPE_SEM + slot)
        save(left.at[slot], left_o.at[k], LEFT_SEM + slot)
        load(11 + 2 * k)

        def emit_out(cols, value, k=k):
            branchw[:, cols] = value if k == 0 else branchw[:, cols] + value

        times(post, 11 + 2 * k, emit_out)

    gate[...] = jnp.zeros_like(gate)

    def last(rows):
        seg = seg_in[0, rows, 0:1]
        value = branchw[rows, :]
        xin[rows, :] = to_low(stream[rows, :] + pick(8, seg) * value)
        value = wide32(cotp[rows, :]) * value
        later = jnp.sum(value * seg, axis=0, keepdims=True)
        every = jnp.sum(value, axis=0, keepdims=True)
        gate[0:1, :] = gate[0:1, :] + (every - later)
        gate[1:2, :] = gate[1:2, :] + later

    each_rows(32, last)
    save(gate, gate_o)
    out[...] = to_low(linear(swap_rows(), xin[...]))

    for copy in held.values():
        copy.wait()
    for k in range(1, 8):
        t_copy(k).wait_send()
        m_copy(k, b).wait_send()
    for k in (1, 2, 3):
        x_copy(k, z).wait_send()
    x_over(y).wait_send()
    for at, to in ((0, twin), (1, first), (2, second)):
        g_copy(at, at, to).wait_send()
    for k in (1, 2, 3):
        remote(gains.at[3], gain_at.at[2 + k], g_send.at[2 + k], g_recv.at[2 + k], near[k - 1]).wait_send()

    for t in range(BLOCKS - HELD, BLOCKS):
        for index in range(3):
            sends(t, index).wait_send()

    def finish(t):
        z_one(t).wait_send()
        for index in range(3, 7):
            sends(t, index).wait_send()

    loop(BLOCKS, finish)


ANY = pl.BlockSpec(memory_space=pl.ANY)
IN_VMEM = pl.BlockSpec(memory_space=pltpu.VMEM)


def forward(*operands):
    low, full = jnp.bfloat16, jnp.float32
    dma = pltpu.SemaphoreType.DMA
    hbm = [
        ((BLOCKS, WIDE, WIDE), low),
        ((ROWS, WIDE), low),
        ((11, WIDE, ROWS), low),
        ((3, ROWS, WIDE), low),
        ((3, ROWS, WIDE), low),
        ((ROWS, WIDE), low),
        ((2, WIDE, KEYS), low),
        ((4, ROWS, WIDE), low),
        ((4, ROWS, 128), full),
        ((2, ROWS, WIDE), low),
        ((4, ROWS, WIDE), low),
        ((ROWS, WIDE), low),
        ((ROWS, WIDE), low),
        ((8, MOD), full),
        ((8, WIDE), full),
        ((8, WIDE), full),
    ]
    vmem = [
        ((PARTS, WINDOW, WIDE), low),
        ((PARTS, PAIR, WIDE), low),
        ((PARTS, PAIR, WIDE), low),
        ((HELD, LINE, WIDE), low),
        ((2, WIDE, WIDE), low),
        ((ROWS, WIDE), low),
        ((ROWS, WIDE), low),
        ((8, 32, WIDE), low),
        ((ROWS, WIDE), low),
        ((ROWS, WIDE), low),
        ((2, WIDE, ROWS), low),
        ((3, ROWS, WIDE), low),
        ((3, ROWS, WIDE), low),
        ((ROWS, WIDE), low),
        ((2, WIDE, KEYS), low),
        ((4, 2, TEXT, KEYS), low),
        ((8, 32, 128), low),
        ((8, MOD), full),
        ((4, ROWS, WIDE), low),
        ((4, ROWS, 128), full),
        ((2, ROWS, WIDE), low),
        ((ROWS, WIDE), full),
        ((128, 128), full),
        ((ROWS, WIDE), full),
        ((ROWS, WIDE), low),
        ((16, 16, WIDE), low),
        ((ROWS, WIDE), low),
        ((2, ROWS, WIDE), low),
        ((ROWS, WIDE), low),
        ((5, 8, WIDE), full),
        ((6, 8, WIDE), full),
        ((8, WIDE), full),
        ((BLOCKS, WINDOW, WIDE), low),
        ((ROWS, WIDE), low),
        ((WIDE, WIDE), low),
        ((MOD // 8, WIDE), low),
        ((2, L, 4096), low),
        ((TEXT, 4096), low),
        ((32, 128), low),
        ((TEXT, KEYS), low),
        ((4, SHARD, WIDE), full),
    ]
    return pl.pallas_call(
        forward_kernel,
        out_shape=[jax.ShapeDtypeStruct(*shape) for shape in hbm],
        in_specs=[IN_VMEM] * 14 + [ANY] * 5,
        out_specs=[ANY, IN_VMEM] + [ANY] * 14,
        scratch_shapes=[pltpu.VMEM(*shape) for shape in vmem]
        + [
            dma((BLOCKS, 3)), dma((BLOCKS, 3)), dma((BLOCKS, 7)), dma((BLOCKS, 7)), dma((BLOCKS,)), dma((2,)),
            dma((7,)), dma((7,)), dma((7, 2)), dma((7, 2)), dma((7,)), dma((7,)), dma((4,)), dma((4,)),
            dma((6,)), dma((6,)), dma((SAVE_SEMS,)), dma((5,)),
        ],
        compiler_params=pltpu.CompilerParams(
            collective_id=0, has_side_effects=True, vmem_limit_bytes=60 * MIB
        ),
        name="forward",
    )(*operands)


def tn(left, right):
    return lax.dot_general(
        left, right, (((0,), (0,)), ((), ())), preferred_element_type=jnp.float32
    )


def text_heads_backward(h, query, key, value, grad, dquery, dkey, dvalue, bias, mask):
    jobs = chains(h, VIDEOS)
    scores, grads = [], []
    for (lanes, on), rows, keys in jobs:
        low_on = to_low(on)
        scores.append(linear(query[rows, lanes] * low_on, key[lanes, keys]))
        grads.append(linear(grad[rows, lanes] * low_on, value[lanes, keys]))
    probs = soft(jnp.concatenate(scores), bias, mask)
    grad_probs = jnp.concatenate(grads)
    delta = jnp.sum(grad_probs * probs, axis=-1, keepdims=True)
    slopes = split_rows(to_low(probs * (grad_probs - delta)), jobs)
    probs = split_rows(to_low(probs), jobs)
    parts = []
    for slope, prob, ((lanes, on), rows, keys) in zip(slopes, probs, jobs):
        low_on = to_low(on)
        parts.append(
            (
                to_low(nt(slope, key[lanes, keys]) * (on * SCALE)),
                to_low(tn(query[rows, lanes] * low_on, slope) * SCALE),
                to_low(tn(grad[rows, lanes] * low_on, prob)),
            )
        )
    for (by_query, by_key, by_value), ((lanes, on), rows, keys) in zip(parts, jobs):
        dquery[rows, lanes] = dquery[rows, lanes] + by_query
        dkey[lanes, keys] = dkey[lanes, keys] + by_key
        dvalue[lanes, keys] = dvalue[lanes, keys] + by_value


def heads_backward(h, query, key, value, grad, dquery, dkey, dvalue, groups, bias, mask):
    jobs = chains(h, groups)
    scores, grads = [], []
    for (lanes, on), rows, keys in jobs:
        low_on = to_low(on)
        scores.append(nt(query[rows, lanes] * low_on, key[keys, lanes]))
        grads.append(nt(grad[rows, lanes] * low_on, value[keys, lanes]))
    probs = soft(jnp.concatenate(scores), bias, mask)
    grad_probs = jnp.concatenate(grads)
    delta = jnp.sum(grad_probs * probs, axis=-1, keepdims=True)
    slopes = split_rows(to_low(probs * (grad_probs - delta)), jobs)
    probs = split_rows(to_low(probs), jobs)
    parts = []
    for slope, prob, ((lanes, on), rows, keys) in zip(slopes, probs, jobs):
        parts.append(
            (
                to_low(linear(slope, key[keys, lanes]) * (on * SCALE)),
                to_low(tn(slope, query[rows, lanes]) * (on * SCALE)),
                to_low(tn(prob, grad[rows, lanes]) * on),
            )
        )
    for (by_query, by_key, by_value), ((lanes, on), rows, keys) in zip(parts, jobs):
        dquery[rows, lanes] = dquery[rows, lanes] + by_query
        dkey[keys, lanes] = dkey[keys, lanes] + by_key
        dvalue[keys, lanes] = dvalue[keys, lanes] + by_value


def backward_kernel(
    wide, left_i, qkvs_i, qkvt_i, qc_i, mem_i, xhat_i, rstd_i, branch_i, slope_i, gfour_i, cot_i, mods_i, gate_i, gain_i,
    caption_i, seg_in, seg_row, turn, cond_in,
    total, gtok, gain_o, caption_o, mod_o,
    weights, left, right, qkv, xhat, rstd, branch, slope, mods, gain, bias, stream, work, grad, xin, gm, mem, dmem, text, text_at, text_sum, cap, cap_out, cap_in, cap_own, cap_at, mod_out, mod,
    seqs, gains, gain_at, gframe, back,
    s0, r0, s1, r1, s2, r2, k2, s3, pass_in, pass_out, far_in, close, close_in, share,
    in_sem, w_sem, s0_sem, r0_sem, s1_sem, r1_sem, s2_sem, r2_sem, z_send, z_recv, share_sem,
    a_send, a_recv, u_send, u_recv, x_send, x_recv, m_send, m_recv, q_send, q_recv, g_send, g_recv,
    cap_sem, c_send, c_recv, left_sem,
):
    x, c, y, z, x1, y1, x2, y2 = place()
    b = z * 2 + y
    near = [device(x, c, y, (z + k) % 4) for k in (1, 2, 3)]
    first, second, twin = device(x1, c, y1, z), device(x2, c, y2, z), device(x, 1 - c, y, z)
    peers = blk_peers(x, c, b)
    across = [twin, device(1 - x, c, y, z), device(1 - x, 1 - c, y, z)]
    greet(peers + across)

    fetches = {}

    def fetch(name, from_ref, to_ref):
        fetches[name] = pltpu.make_async_copy(from_ref, to_ref, in_sem.at[name])
        fetches[name].start()

    def have(name):
        if name in fetches:
            fetches.pop(name).wait()

    fetch(0, gfour_i, right.at[0])
    for k in range(4):
        fetch(1 + k, left_i.at[k], left.at[k])
    fetch(12, mods_i, mods)
    fetch(13, gain_i, gain)
    fetch(14, slope_i.at[0], slope.at[0])
    fetch(15, slope_i.at[1], slope.at[1])
    fetch(16, xhat_i.at[3], xhat.at[1])
    fetch(17, rstd_i.at[3], rstd.at[1])
    fetch(18, cot_i, xin)
    fetch(19, gate_i, work.at[0:8])

    def weight(block):
        slot = WEIGHT_ORDER.index(block) % 2
        return weights.at[slot]

    def prefetch(at):
        if at < len(WEIGHT_ORDER):
            copy = pltpu.make_async_copy(wide.at[WEIGHT_ORDER[at]], weights.at[at % 2], w_sem.at[at % 2])
            copy.start()
            fetches["w", WEIGHT_ORDER[at]] = copy

    def release(block):
        prefetch(WEIGHT_ORDER.index(block) + 2)

    prefetch(0)
    prefetch(1)

    away = [(1 - x) * 2 + 1 - y, x2 * 2 + y2]
    stay = [x1 * 2 + y1, x * 2 + y]

    def product(t, core, xl):
        rows = pl.ds(pl.multiple_of(line_of(core, xl, 0) * LINE, 16), 2 * LINE)
        return linear(left[left_at(t) % 4, rows, :], right[right_at(t)])

    def left_copy(t):
        return pltpu.make_async_copy(left_i.at[left_at(t)], left.at[left_at(t) % 4], left_sem.at[0])

    def left_next(t):
        return (t >= 4) & (t < BLOCKS) & (left_at(t) != left_at(t - 1))

    def copy0(t, l):
        pair = pl.ds(2 * l, 2)
        return remote(s0.at[t % 2, pair], r0.at[t % 4, pair], s0_sem.at[t % 2, l], r0_sem.at[t % 4, l], twin)

    def copy1(t, l):
        return remote(s1.at[t % 2, away[l]], r1.at[t % 4, l], s1_sem.at[t % 2, l], r1_sem.at[t % 4, l], second)

    def copy2(t):
        return remote(s2.at[t % 2], r2.at[t % 4], s2_sem.at[t % 2], r2_sem.at[t % 4], first)

    beside, opposite = device(x, c, y, z + 1 - 2 * (z % 2)), device(x, c, y, 3 - z)
    middle = (z == 1) | (z == 2)
    near_rows = pl.ds(pl.multiple_of(64 * (z // 2), 16), PAIR)
    far_rows = pl.ds(pl.multiple_of(64 - 64 * (z // 2), 16), PAIR)
    own_rows = pl.ds(pl.multiple_of(32 * (z % 2), 16), WINDOW)
    beside_rows = pl.ds(pl.multiple_of(32 - 32 * (z % 2), 16), WINDOW)

    def z_one(t):
        return remote(s3.at[t % 4, far_rows], pass_in.at[t % 4], z_send.at[0, t % 4], z_recv.at[0, t % 4], beside)

    def z_two(t):
        return remote(pass_out.at[t % 2], far_in.at[t % 4], z_send.at[1, t % 4], z_recv.at[1, t % 4], opposite)

    def z_three(t):
        return remote(
            close.at[t % 2, beside_rows], close_in.at[t % 4], z_send.at[2, t % 4], z_recv.at[2, t % 4], beside
        )

    def share_copy(t):
        return pltpu.make_async_copy(share.at[t % 2], total.at[t], share_sem.at[t % 2])

    def tick(t):
        @pl.when(t >= 10)
        def _():
            now = t - 10
            z_three(now).wait_recv()
            value = wide32(close[now % 2, own_rows]) + wide32(close_in[now % 4])

            @pl.when(jnp.logical_not(middle))
            def _():
                z_one(now).wait_send()

            @pl.when(now >= 2)
            def _():
                share_copy(now - 2).wait()
            share[now % 2] = value
            share_copy(now).start()

        @pl.when((t >= 8) & (t < BLOCKS + 8))
        def _():
            now = t - 8

            @pl.when(now >= 2)
            def _():
                z_three(now - 2).wait_send()

            @pl.when(middle)
            def _():
                z_two(now).wait_recv()
                close[now % 2] = to_low(wide32(s3[now % 4, near_rows]) + wide32(far_in[now % 4]))

            @pl.when(jnp.logical_not(middle))
            def _():
                close[now % 2] = s3[now % 4, near_rows]

            z_three(now).start()

        @pl.when((t >= 7) & (t < BLOCKS + 7) & middle)
        def _():
            now = t - 7
            z_one(now).wait_recv()

            @pl.when(now >= 2)
            def _():
                z_two(now - 2).wait_send()
            pass_out[now % 2] = to_low(wide32(s3[now % 4, far_rows]) + wide32(pass_in[now % 4]))
            z_two(now).start()

        @pl.when((t >= 6) & (t < BLOCKS + 6))
        def _():
            now = t - 6
            copy2(now).wait_recv()
            s3[now % 4] = to_low(k2[now % 2] + wide32(r2[now % 4]))

            @pl.when(jnp.logical_not(middle))
            def _():
                z_one(now).start()

        @pl.when((t >= 4) & (t < BLOCKS + 4))
        def _():
            now = t - 4
            copy1(now, 0).wait_recv()

            @pl.when(now >= 2)
            def _():
                copy2(now - 2).wait_send()
            s2[now % 2] = to_low(wide32(s1[now % 2, stay[0]]) + wide32(r1[now % 4, 0]))
            copy2(now).start()
            copy1(now, 1).wait_recv()
            k2[now % 2] = wide32(s1[now % 2, stay[1]]) + wide32(r1[now % 4, 1])

        @pl.when((t >= 2) & (t < BLOCKS + 2))
        def _():
            now = t - 2

            @pl.when(now >= 2)
            def _():
                for l in range(2):
                    copy1(now - 2, l).wait_send()
            for l in range(2):
                copy0(now, l).wait_recv()
                value = product(now, c, l)
                for part in range(2):
                    line = 2 * l + part
                    summed = value[part * LINE : part * LINE + LINE] + wide32(r0[now % 4, line])
                    s1[now % 2, line] = to_low(summed)
            for l in range(2):
                copy1(now, l).start()

        @pl.when(left_next(t))
        def _():
            left_copy(t).wait()

        @pl.when(t < BLOCKS)
        def _():
            for l in range(2):
                @pl.when(t >= 2)
                def _():
                    copy0(t - 2, l).wait_send()
                value = to_low(product(t, 1 - c, l))
                s0[t % 2, 2 * l] = value[:LINE]
                s0[t % 2, 2 * l + 1] = value[LINE:]
                copy0(t, l).start()

        @pl.when(left_next(t + 1))
        def _():
            left_copy(t + 1).start()

    done = [0]

    def pump(until):
        if until > done[0]:
            start = done[0]
            loop(until - start, lambda i: tick(i + start))
            done[0] = until

    def pick(piece, seg):
        lanes = slice(WIDE * piece, WIDE * piece + WIDE)
        return jnp.where(seg > 0.5, mods[1:2, lanes], mods[0:1, lanes])

    def by_video(piece, value, seg):
        lanes = slice(WIDE * piece, WIDE * piece + WIDE)
        later = jnp.sum(value * seg, axis=0, keepdims=True)
        every = jnp.sum(value, axis=0, keepdims=True)
        gm[0:1, lanes] = gm[0:1, lanes] + (every - later)
        gm[1:2, lanes] = gm[1:2, lanes] + later

    def through(values_at, blocks, emit, grouped=False):
        for n, (values, block) in enumerate(zip(values_at, blocks)):
            have(("w", block))

            def tile(cols, n=n, values=values, block=block):
                part = nt(values[...], weight(block)[cols, :])
                if n > 0:
                    part = part + work[:, cols]
                if n == len(blocks) - 1:
                    xin[:, cols] = to_low(part)
                else:
                    work[:, cols] = part

            each_cols(tile)
            release(block)
        if grouped:
            xin[...] = to_low(linear(regroup(True), xin[...]))
        turn_back(emit)

    def turn_back(emit):
        each_cols(lambda cols: emit(cols, linear(xin[...], turn[:, cols])))

    def emit_work(cols, value):
        work[:, cols] = value

    def emit_grad(cols, value):
        grad[:, cols] = to_low(value)

    def norm_back(grad_in, tilt, at, rows):
        slope_in = grad_in * tilt
        hat = wide32(xhat[at, rows, :])
        first_mean = jnp.mean(slope_in, axis=-1, keepdims=True)
        second_mean = jnp.mean(slope_in * hat, axis=-1, keepdims=True)
        return rstd[at, rows, 0:1] * (slope_in - first_mean - hat * second_mean)

    gm[...] = jnp.zeros_like(gm)
    have(0)
    have(12)
    have(18)
    have(19)
    gm[0:8, 8 * WIDE : 9 * WIDE] = work[0:8]
    stream[...] = wide32(xin[...])
    for k in range(4):
        have(1 + k)
    pump(2)
    for k in range(4):
        have(14 + k % 2 if k < 2 else ("slope", k))
        have(("w", 11 + 2 * k))

        def tile(cols, k=k):
            value = nt(right[0], weight(11 + 2 * k)[cols, :]) * wide32(slope[k % 2, :, cols])
            right[1 + k, :, cols] = to_low(value)

        each_cols(tile)
        release(11 + 2 * k)
        if k < 2:
            copy = pltpu.make_async_copy(slope_i.at[k + 2], slope.at[k % 2], in_sem.at[14 + k])
            copy.start()
            fetches["slope", k + 2] = copy
        have(("w", 10 + 2 * k))

        def tile(cols, k=k):
            part = nt(right[1 + k], weight(10 + 2 * k)[cols, :])
            if k > 0:
                part = part + work[:, cols]
            if k < 3:
                work[:, cols] = part
            else:
                xin[:, cols] = to_low(part)

        each_cols(tile)
        release(10 + 2 * k)
        pump(k + 3)
    turn_back(emit_work)
    have(16)
    have(17)
    fetch(20, qc_i, qkv.at[0])
    fetch(21, mem_i.at[0], mem.at[0])
    fetch(22, mem_i.at[1], mem.at[1])
    fetch(23, xhat_i.at[2], xhat.at[0])
    fetch(24, rstd_i.at[2], rstd.at[0])

    def after_mlp(rows):
        seg = seg_in[0, rows, 0:1]
        value = work[rows, :]
        by_video(6, value, seg)
        by_video(7, value * wide32(xhat[1, rows, :]), seg)
        value = stream[rows, :] + norm_back(value, 1.0 + pick(7, seg), 1, rows)
        stream[rows, :] = value
        right[5, rows, :] = to_low(value)

    each_rows(32, after_mlp)

    fetch(25, xhat_i.at[1], xhat.at[1])
    fetch(26, rstd_i.at[1], rstd.at[1])
    through([right.at[5]], [9], emit_grad)
    right[6] = jnp.zeros_like(right[6])
    dmem[...] = jnp.zeros_like(dmem)
    for name in (13, 20, 21, 22, 23, 24):
        have(name)

    def cross_heads(h):
        text_heads_backward(
            h, qkv.at[0], mem.at[0], mem.at[1], grad, right.at[6], dmem.at[0], dmem.at[1],
            cross_bias(), cross_rows(seg_in),
        )

    for part in range(4):
        loop(2, lambda h: cross_heads(h + 2 * part))
        pump(7 + (part + 1) // 2)

    def dmem_part(zp, yp):
        return dmem.at[zp // 2, pl.ds(pl.multiple_of(TEXT * (zp % 2 * 2 + yp), 16), TEXT)]

    def x_over(zp):
        return remote(dmem_part(zp, 1 - y), text.at[zp], x_send.at[zp], x_recv.at[zp], device(x, c, 1 - y, z))

    def x_copy(k):
        return remote(text.at[(z + k) % 4], text_at.at[k - 1], x_send.at[3 + k], x_recv.at[3 + k], near[k - 1])

    for zp in range(4):
        x_over(zp).start()
    fetch(27, qkvt_i.at[0], qkv.at[0])
    fetch(28, qkvt_i.at[1], qkv.at[1])
    fetch(29, qkvt_i.at[2], qkv.at[2])
    fetch(30, branch_i.at[1], branch)
    through([right.at[6]], [8], emit_work)
    gains[0] = jnp.zeros_like(gains[0])
    have(30)

    def after_cross(rows):
        seg = seg_in[0, rows, 0:1]
        value = work[rows, :]
        gains[0, 0:1, :] = gains[0, 0:1, :] + jnp.sum(value * wide32(xhat[0, rows, :]), axis=0, keepdims=True)
        value = stream[rows, :] + norm_back(value, gain[0:1, :], 0, rows)
        stream[rows, :] = value
        by_video(5, value * wide32(branch[rows, :]), seg)
        right[7, rows, :] = to_low(value * pick(5, seg))

    each_rows(32, after_cross)

    def g_copy(at, to):
        return remote(gains.at[min(at, 3)], gain_at.at[at], g_send.at[at], g_recv.at[at], to)

    g_copy(0, twin).start()
    fetch(31, branch_i.at[0], branch)
    fetch(32, xhat_i.at[0], xhat.at[0])
    fetch(33, rstd_i.at[0], rstd.at[0])
    pump(10)

    through([right.at[7]], [7], emit_grad)
    grad[...] = to_low(linear(regroup(False), grad[...]))
    bias[...] = temporal_bias(seg_in, seg_row)
    for j in range(3):
        right[8 + j] = jnp.zeros_like(right[8 + j])
    for name in (25, 26, 27, 28, 29):
        have(name)

    def temporal_heads(h):
        heads_backward(
            h, qkv.at[0], qkv.at[1], qkv.at[2], grad, right.at[8], right.at[9], right.at[10],
            HALVES, jnp.concatenate([bias[...]] * 4), None,
        )

    loop(4, temporal_heads)
    pump(11)
    g_copy(0, twin).wait_recv()
    gains[1] = gains[0] + gain_at[0]
    g_copy(1, first).start()
    loop(4, lambda h: temporal_heads(h + 4))
    pump(12)
    g_copy(1, first).wait_recv()
    gains[2] = gains[1] + gain_at[1]
    g_copy(2, second).start()
    for zp in range(4):
        x_over(zp).wait_recv()
        text[zp] = to_low(wide32(dmem_part(zp, y)[...]) + wide32(text[zp]))
    for k in (1, 2, 3):
        x_copy(k).start()
    for j in range(3):
        fetch(34 + j, qkvs_i.at[j], qkv.at[j])
    through([right.at[8], right.at[9], right.at[10]], [4, 5, 6], emit_work, True)
    have(31)

    def after_temporal(rows):
        seg = seg_in[0, rows, 0:1]
        value = work[rows, :]
        by_video(3, value, seg)
        by_video(4, value * wide32(xhat[1, rows, :]), seg)
        value = stream[rows, :] + norm_back(value, 1.0 + pick(4, seg), 1, rows)
        stream[rows, :] = value
        by_video(2, value * wide32(branch[rows, :]), seg)
        right[1, rows, :] = to_low(value * pick(2, seg))

    each_rows(32, after_temporal)

    through([right.at[1]], [3], emit_grad)

    def a_copy(k):
        to = (b + k) % 8
        part = grad.at[pl.ds(pl.multiple_of(32 * to, 32), 32)]
        return remote(part, back.at[b], a_send.at[k - 1], a_recv.at[k - 1], peers[k - 1])

    def a_wait(k):
        of = (b + 8 - k) % 8
        remote(grad.at[pl.ds(0, 32)], back.at[of], a_send.at[k - 1], a_recv.at[k - 1], peers[k - 1]).wait_recv()

    for k in range(1, 8):
        a_copy(k).start()
    pump(13)
    for k in (1, 2, 3):
        x_copy(k).wait_recv()
    text_sum[...] = to_low(wide32(text[z]) + wide32(text_at[0]) + wide32(text_at[1]) + wide32(text_at[2]))

    def cap_fetch(n):
        quarter = [1 - c, 3 - c, c, 2 + c][n]
        lanes = pl.ds(pl.multiple_of(QUARTER * quarter, 128), QUARTER)
        return pltpu.make_async_copy(caption_i.at[:, :, lanes], cap.at[n % 2], cap_sem.at[n % 2])

    over_x = across[1]
    quarters = [x * 2 + c, (1 - x) * 2 + c, x * 2 + 1 - c, (1 - x) * 2 + 1 - c]

    def c_copy(n):
        from_ref, to_ref, to = (
            (cap_out.at[0], cap_in.at[0], twin),
            (cap_out.at[1], cap_in.at[1], twin),
            (cap_own.at[1 - x], cap_at, over_x),
            (cap_own.at[x], caption_o.at[quarters[0]], over_x),
            (cap_own.at[x], caption_o.at[quarters[0]], twin),
            (caption_o.at[quarters[1]], caption_o.at[quarters[1]], twin),
        )[n]
        return remote(from_ref, to_ref, c_send.at[n], c_recv.at[n], to)

    cap_fetch(0).start()
    cap_fetch(1).start()
    for n in range(4):
        cap_fetch(n).wait()
        part = linear(text_sum[:, 0:L], cap[n % 2, 0]) + linear(text_sum[:, 128 : 128 + L], cap[n % 2, 1])
        if n < 2:
            cap_out[n] = to_low(part)
            c_copy(n).start()
            cap_fetch(n + 2).start()
        else:
            cap_own[n - 2] = to_low(part)
    back[b] = grad[pl.ds(pl.multiple_of(32 * b, 32), 32)]
    pump(14)
    g_copy(2, second).wait_recv()
    gains[3] = gains[2] + gain_at[2]
    for k in (1, 2, 3):
        g_copy(2 + k, near[k - 1]).start()
    for j in range(3):
        right[2 + j] = jnp.zeros_like(right[2 + j])
    for name in (32, 33, 34, 35, 36):
        have(name)
    for k in range(1, 8):
        a_wait(k)
    for k in range(8):
        for f in range(2):
            gframe[128 * f + 16 * k : 128 * f + 16 * k + 16, :] = back[k, 16 * f : 16 * f + 16, :]

    def spatial_heads(h):
        heads_backward(
            h, qkv.at[0], qkv.at[1], qkv.at[2], gframe, right.at[2], right.at[3], right.at[4], HALVES, None, None
        )

    loop(4, spatial_heads)
    pump(15)
    for n in range(2):
        c_copy(n).wait_recv()
        cap_own[n] = to_low(wide32(cap_own[n]) + wide32(cap_in[n]))
    c_copy(2).start()
    loop(4, lambda h: spatial_heads(h + 4))
    pump(16)
    through([right.at[2], right.at[3], right.at[4]], [0, 1, 2], emit_work)
    pump(17)
    for k in range(1, 8):
        a_copy(k).wait_send()

    def after_spatial(i):
        rows = pl.ds(pl.multiple_of(16 * i, 16), 16)
        seg = seg_in[1, rows, 0:1]
        value = work[rows, :]
        by_video(0, value, seg)
        by_video(1, value * wide32(xhat[0, rows, :]), seg)
        value = to_low(norm_back(value, 1.0 + pick(1, seg), 0, rows))
        back[i % 8, pl.ds(pl.multiple_of(16 * (i // 8), 16), 16), :] = value

    loop(16, after_spatial)

    def branch_part(of):
        return branch.at[pl.ds(pl.multiple_of(32 * of, 32), 32)]

    def u_copy(k):
        to = (b + k) % 8
        return remote(back.at[to], branch_part(b), u_send.at[k - 1], u_recv.at[k - 1], peers[k - 1])

    def u_wait(k):
        of = (b + 8 - k) % 8
        remote(back.at[0], branch_part(of), u_send.at[k - 1], u_recv.at[k - 1], peers[k - 1]).wait_recv()

    def m_copy(k):
        to = (b + k) % 8
        return remote(mod_out.at[to], mod.at[b], m_send.at[k - 1], m_recv.at[k - 1], peers[k - 1])

    def m_wait(k):
        of = (b + 8 - k) % 8
        remote(mod_out.at[0], mod.at[of], m_send.at[k - 1], m_recv.at[k - 1], peers[k - 1]).wait_recv()

    for k in range(1, 8):
        u_copy(k).start()
    branch[pl.ds(pl.multiple_of(32 * b, 32), 32), :] = back[b]
    for k in range(8):
        tiles = [
            gm[row : row + 1, 1280 * k + 128 * tile : 1280 * k + 128 * tile + 128]
            for row in range(2)
            for tile in range(MOD_TILES)
        ]
        mod_out[k] = to_low(jnp.concatenate(tiles + [jnp.zeros((32 - 2 * MOD_TILES, 128), jnp.float32)]))
    for k in range(1, 8):
        m_copy(k).start()
    mod[b] = mod_out[b]
    pump(18)
    c_copy(2).wait_recv()
    cap_own[x] = to_low(wide32(cap_own[x]) + wide32(cap_at[...]))
    c_copy(3).start()
    c_copy(4).start()
    keep_quarter = pltpu.make_async_copy(cap_own.at[x], caption_o.at[quarters[0]], cap_sem.at[0])
    keep_quarter.start()
    pump(20)
    for k in range(1, 8):
        m_wait(k)
    summed = wide32(mod[0])
    for k in range(1, 8):
        summed = summed + wide32(mod[k])
    own = x * 2 + c
    seqs[own, 0:32] = to_low(summed)
    seqs[own, 32:64] = cond_in[...]
    places = [x * 2 + 1 - c, (1 - x) * 2 + c, (1 - x) * 2 + 1 - c]

    def q_copy(k, at):
        return remote(seqs.at[own], seqs.at[at], q_send.at[k], q_recv.at[k], across[k])

    for k in range(3):
        q_copy(k, own).start()
    pump(22)
    for k in range(1, 8):
        u_wait(k)
    xin[...] = to_low(stream[...] + wide32(branch[...]))
    gtok[...] = to_low(linear(swap_rows(), xin[...]))
    for k in (1, 2, 3):
        g_copy(2 + k, near[k - 1]).wait_recv()
    gain_o[...] = gains[3] + gain_at[3] + gain_at[4] + gain_at[5]
    pump(24)
    c_copy(3).wait_recv()
    c_copy(5).start()
    pump(BLOCKS + 10)
    c_copy(4).wait_recv()
    c_copy(5).wait_recv()
    for n in range(6):
        c_copy(n).wait_send()
    keep_quarter.wait()
    for k in range(3):
        q_copy(k, places[k]).wait_recv()
    mod_o[...] = seqs[...]

    for now in (BLOCKS - 2, BLOCKS - 1):
        for l in range(2):
            copy0(now, l).wait_send()
            copy1(now, l).wait_send()
        copy2(now).wait_send()
        z_three(now).wait_send()
        share_copy(now).wait()

        @pl.when(middle)
        def _(now=now):
            z_two(now).wait_send()

    for k in range(1, 8):
        u_copy(k).wait_send()
        m_copy(k).wait_send()
        x_over(k - 1).wait_send() if k < 5 else x_copy(k - 4).wait_send()
    for k in range(3):
        q_copy(k, own).wait_send()
    for at, to in enumerate([twin, first, second] + near):
        g_copy(at, to).wait_send()


QUARTER = 1024
WEIGHT_ORDER = (11, 10, 13, 12, 15, 14, 17, 16, 9, 8, 7, 4, 5, 6, 3, 0, 1, 2)


def backward(*operands):
    low, full = jnp.bfloat16, jnp.float32
    dma = pltpu.SemaphoreType.DMA
    outs = [
        ((BLOCKS, WINDOW, WIDE), full),
        ((ROWS, WIDE), low),
        ((8, WIDE), full),
        ((4, TEXT, QUARTER), low),
        ((4, 64, 128), low),
    ]
    vmem = [
        ((2, WIDE, WIDE), low),
        ((4, WIDE, ROWS), low),
        ((11, ROWS, WIDE), low),
        ((3, ROWS, WIDE), low),
        ((2, ROWS, WIDE), low),
        ((2, ROWS, 128), full),
        ((ROWS, WIDE), low),
        ((2, ROWS, WIDE), low),
        ((8, MOD), full),
        ((8, WIDE), full),
        ((128, 128), full),
        ((ROWS, WIDE), full),
        ((ROWS, WIDE), full),
        ((ROWS, WIDE), low),
        ((ROWS, WIDE), low),
        ((8, MOD), full),
        ((2, WIDE, KEYS), low),
        ((2, WIDE, KEYS), low),
        ((4, TEXT, KEYS), low),
        ((3, TEXT, KEYS), low),
        ((TEXT, KEYS), low),
        ((2, 2, L, QUARTER), low),
        ((2, TEXT, QUARTER), low),
        ((2, TEXT, QUARTER), low),
        ((2, TEXT, QUARTER), low),
        ((TEXT, QUARTER), low),
        ((8, 32, 128), low),
        ((8, 32, 128), low),
        ((4, 64, 128), low),
        ((4, 8, WIDE), full),
        ((6, 8, WIDE), full),
        ((ROWS, WIDE), low),
        ((8, 32, WIDE), low),
        ((2, 4, LINE, WIDE), low),
        ((4, 4, LINE, WIDE), low),
        ((2, 4, LINE, WIDE), low),
        ((4, 2, LINE, WIDE), low),
        ((2, LINE, WIDE), low),
        ((4, LINE, WIDE), low),
        ((2, LINE, WIDE), full),
        ((4, LINE, WIDE), low),
        ((4, PAIR, WIDE), low),
        ((2, PAIR, WIDE), low),
        ((4, PAIR, WIDE), low),
        ((2, PAIR, WIDE), low),
        ((4, WINDOW, WIDE), low),
        ((2, WINDOW, WIDE), full),
    ]
    return pl.pallas_call(
        backward_kernel,
        out_shape=[jax.ShapeDtypeStruct(*shape) for shape in outs],
        in_specs=[ANY] * 16 + [IN_VMEM] * 4,
        out_specs=[ANY] + [IN_VMEM] * 2 + [ANY, IN_VMEM],
        scratch_shapes=[pltpu.VMEM(*shape) for shape in vmem]
        + [
            dma((40,)), dma((2,)), dma((2, 4)), dma((4, 4)), dma((2, 2)), dma((4, 2)), dma((2,)), dma((4,)),
            dma((3, 4)), dma((3, 4)), dma((2,)), dma((7,)), dma((7,)), dma((7,)), dma((7,)), dma((7,)), dma((7,)),
            dma((7,)), dma((7,)), dma((3,)), dma((3,)), dma((6,)), dma((6,)), dma((2,)), dma((6,)), dma((6,)), dma((1,)),
        ],
        compiler_params=pltpu.CompilerParams(
            collective_id=1, has_side_effects=True, vmem_limit_bytes=63 * MIB
        ),
        name="backward",
    )(*operands)


def finish_kernel(
    spread, caption_in, mod_in, gain_in,
    ada_o, bias_o, spatial_o, spatial_out_o, temporal_o, temporal_out_o, gain_o, query_o, caption_o, cross_o, hidden_o,
    hidden_out_o,
):
    seq, blk = lax.axis_index("seq"), lax.axis_index("blk")

    def share(t):
        return pltpu.roll(spread[t], (WINDOW - 4 * (blk // 2)) % WINDOW, 0)[0:SHARD]

    for j in range(3):
        lanes = slice(WIDE * j, WIDE * j + WIDE)
        spatial_o[:, lanes] = share(15 + j)
        temporal_o[:, lanes] = share(11 + j)
    spatial_out_o[...] = share(14)
    temporal_out_o[...] = share(10)
    query_o[...] = share(9)
    cross_o[...] = share(8)
    hidden = [share(4 + k) for k in range(4)]
    hidden_o[...] = jnp.zeros_like(hidden_o)
    for k, natural, placed in hidden_places():
        move_lanes(hidden_o, hidden[k], placed, natural, 4 * WIDE)
    for k in range(4):
        hidden_out_o[SHARD * k : SHARD * k + SHARD, :] = share(k)
    gain_o[...] = pltpu.roll(gain_in[...], (WIDE - SHARD * (seq * 8 + blk)) % WIDE, 1)[0:1, 0:SHARD]
    for q in range(4):
        caption_o[:, QUARTER * q : QUARTER * q + QUARTER] = wide32(caption_in[q])
    part = MOD // 8
    mods, conds = [], []
    for pack in range(4):
        rows = wide32(mod_in[pack])
        for video in range(2):
            first = MOD_TILES * video
            mods.append(jnp.concatenate([rows[first + i : first + i + 1] for i in range(MOD_TILES)], axis=1))
            first = 32 + WIDE // 128 * video
            conds.append(jnp.concatenate([rows[first + i : first + i + 1] for i in range(WIDE // 128)], axis=1))
    mods = pltpu.roll(jnp.concatenate(mods), (MOD_WIN - 16 * blk) % MOD_WIN, 1)[:, :part]
    bias_o[...] = jnp.sum(mods, axis=0, keepdims=True)
    ada_o[...] = tn(to_low(mods), to_low(jnp.concatenate(conds)))


def finish(spread, caption, mod, gain):
    full = jnp.float32
    outs = [
        (MOD // 8, WIDE), (1, MOD // 8), (SHARD, 3 * WIDE), (SHARD, WIDE), (SHARD, 3 * WIDE), (SHARD, WIDE),
        (1, SHARD), (SHARD, WIDE), (TEXT, 4 * QUARTER), (SHARD, WIDE), (SHARD, 4 * WIDE), (4 * SHARD, WIDE),
    ]
    return pl.pallas_call(
        finish_kernel,
        out_shape=[jax.ShapeDtypeStruct(shape, full) for shape in outs],
        in_specs=[IN_VMEM] * 4,
        out_specs=[IN_VMEM] * len(outs),
        compiler_params=pltpu.CompilerParams(vmem_limit_bytes=60 * MIB),
        name="finish",
    )(spread, caption, mod, gain)


TURN = np.arange(WIDE)[None, :] == (
    np.arange(WIDE).reshape(2, 2, 4, 2, SHARD).transpose(1, 0, 3, 2, 4).reshape(-1)
)[:, None]


def shards(
    tokens,
    segments,
    timesteps,
    caption,
    cotangent,
    ada_weight,
    ada_bias,
    spatial_in,
    spatial_out,
    temporal_in,
    temporal_out,
    cross_gain,
    cross_query,
    caption_proj,
    cross_out,
    hidden_in,
    hidden_out,
):
    frame_seg = segments[0]
    blk = lax.axis_index("blk")
    conditioning = to_low(jax.nn.silu(time_embedding(timesteps[0], WIDE)))
    cond_in = jnp.pad(conditioning.reshape(2 * WIDE // 128, 128), ((0, 32 - 2 * WIDE // 128), (0, 0)))
    frames = frame_seg.astype(jnp.float32)
    own_frames = lax.dynamic_slice(frames, (2 * blk,), (2,))
    seg_in = jnp.broadcast_to(
        jnp.stack(
            [jnp.repeat(frames, 16), jnp.repeat(own_frames, 128), jnp.tile(jnp.repeat(frames, 8), 2)]
        )[:, :, None],
        (3, ROWS, 128),
    )
    seg_row = jnp.broadcast_to(jnp.repeat(frames, 8)[None], (8, 128))
    turn = jnp.asarray(TURN, jnp.bfloat16)
    wide, out, *kept = forward(
        spatial_in,
        spatial_out,
        temporal_in,
        temporal_out,
        cross_query,
        cross_out,
        hidden_in,
        hidden_out,
        tokens.reshape(ROWS, WIDE),
        jnp.pad(cross_gain[None], ((0, 7), (0, 0))),
        jnp.pad(conditioning, ((0, 14), (0, 0))),
        ada_bias[None],
        seg_in,
        seg_row,
        cotangent.reshape(ROWS, WIDE),
        turn,
        ada_weight.T,
        caption[0],
        caption_proj.T,
    )
    spread, grad_tokens, grad_gain, grad_text, grad_mod = backward(
        wide, *kept, caption[0], seg_in, seg_row, turn, cond_in
    )
    (
        grad_ada,
        grad_bias,
        grad_sin,
        grad_sout,
        grad_tin,
        grad_tout,
        grad_gain,
        grad_query,
        grad_caption,
        grad_cout,
        grad_hin,
        grad_hout,
    ) = finish(spread, grad_text, grad_mod, grad_gain)
    return (
        out.reshape(tokens.shape),
        grad_tokens.reshape(tokens.shape),
        grad_ada.T,
        grad_bias[0],
        grad_sin,
        grad_sout,
        grad_tin,
        grad_tout,
        grad_gain[0],
        grad_query,
        grad_caption.T,
        grad_cout,
        grad_hin,
        grad_hout,
    )


def solution(mesh):
    fast = dict(mesh.shape) == {"seq": 4, "blk": 8}
    return jax.shard_map(
        shards if fast else general_shards,
        mesh=mesh,
        in_specs=(
            P("seq", "blk", None, None),
            P("seq", None),
            P("seq", None),
            P("seq", None, None, None),
            P("seq", "blk", None, None),
            P(None, "blk"),
            P("blk"),
            P(("seq", "blk"), None),
            P(("seq", "blk"), None),
            P(("seq", "blk"), None),
            P(("seq", "blk"), None),
            P(("seq", "blk")),
            P(("seq", "blk"), None),
            P(None, "blk"),
            P(("seq", "blk"), None),
            P(("seq", "blk"), None),
            P(("seq", "blk"), None),
        ),
        out_specs=(
            P("seq", "blk", None, None),
            P("seq", "blk", None, None),
            P(None, "blk"),
            P("blk"),
            P(("seq", "blk"), None),
            P(("seq", "blk"), None),
            P(("seq", "blk"), None),
            P(("seq", "blk"), None),
            P(("seq", "blk")),
            P(("seq", "blk"), None),
            P(None, "blk"),
            P(("seq", "blk"), None),
            P(("seq", "blk"), None),
            P(("seq", "blk"), None),
        ),
        check_vma=False,
    )
```

```python
import math

import jax
import jax.numpy as jnp
import numpy as np
from jax import lax
from jax.experimental import pallas as pl
from jax.experimental.pallas import tpu as pltpu
from jax.sharding import PartitionSpec as P

H = 16
E = 72
L = 120


EPSILON = 1e-06
MASKED = -1e30


def to_low(values):
    return values.astype(jnp.bfloat16)


def linear(left, right):
    return jnp.dot(left, right, preferred_element_type=jnp.float32)


def left_product(left, right):
    return lax.dot_general(
        left, right, (((0,), (0,)), ((), ())), preferred_element_type=jnp.float32
    )


def right_product(left, right):
    return lax.dot_general(
        left, right, (((1,), (1,)), ((), ())), preferred_element_type=jnp.float32
    )


def normalize(values):
    center = values - jnp.mean(values, axis=-1, keepdims=True)
    return center * lax.rsqrt(jnp.mean(center * center, axis=-1, keepdims=True) + EPSILON)


def modulate(values, shift_rows, scale_rows):
    return normalize(values) * (1.0 + scale_rows) + shift_rows


def gain_norm(values, gain_row):
    return normalize(values) * gain_row


def gelu_tanh(values):
    return jax.nn.gelu(values, approximate=True)


def softmax_rows(scores):
    shifted = jnp.exp(scores - jnp.max(scores, axis=-1, keepdims=True))
    return shifted / jnp.sum(shifted, axis=-1, keepdims=True)


def softmax_with_total(scores):
    top = jnp.max(scores, axis=-1, keepdims=True)
    shifted = jnp.exp(scores - top)
    total = jnp.sum(shifted, axis=-1, keepdims=True)
    return (shifted / total, (top + jnp.log(total))[..., 0])


def softmax_back(probs, grad_probs):
    return probs * (grad_probs - jnp.sum(grad_probs * probs, axis=-1, keepdims=True))


def time_embedding(step_ids, model_width):
    half_width = model_width // 2
    frequency = jnp.exp(
        -math.log(10000.0) * jnp.arange(half_width).astype(jnp.float32) / half_width
    )
    angles = step_ids.astype(jnp.float32)[:, None] * frequency[None, :]
    return jnp.concatenate([jnp.cos(angles), jnp.sin(angles)], axis=1)


def general_shards(
    tokens,
    segments,
    timesteps,
    caption,
    cotangent,
    ada_weight,
    ada_bias,
    spatial_in,
    spatial_out,
    temporal_in,
    temporal_out,
    cross_gain,
    cross_query,
    caption_proj,
    cross_out,
    hidden_in,
    hidden_out,
):
    inputs = tokens[0].astype(jnp.float32)
    patch_dev, frames, model_width = inputs.shape
    token_rows = patch_dev * frames
    head_count = H
    head_size = E
    score_scale = E ** (-0.5)
    frame_seg = segments[0]
    step_ids = timesteps[0]
    seg_count, text_len, text_width = caption.shape[1:]
    text_keys = seg_count * text_len
    caption_rows = caption[0].reshape(text_keys, text_width)
    grad_out = cotangent[0].astype(jnp.float32)
    gathered = (
        lax.all_gather(spatial_in, ("seq", "blk"), axis=0, tiled=True),
        lax.all_gather(spatial_out, ("seq", "blk"), axis=0, tiled=True),
        lax.all_gather(temporal_in, ("seq", "blk"), axis=0, tiled=True),
        lax.all_gather(temporal_out, ("seq", "blk"), axis=0, tiled=True),
        lax.all_gather(cross_gain, ("seq", "blk"), axis=0, tiled=True),
        lax.all_gather(cross_query, ("seq", "blk"), axis=0, tiled=True),
        lax.all_gather(cross_out, ("seq", "blk"), axis=0, tiled=True),
        lax.all_gather(hidden_in, ("seq", "blk"), axis=0, tiled=True),
        lax.all_gather(hidden_out, ("seq", "blk"), axis=0, tiled=True),
    )
    (
        wide_sin,
        wide_sout,
        wide_tin,
        wide_tout,
        gain_low,
        wide_query,
        wide_cout,
        wide_hin,
        wide_hout,
    ) = gathered
    gain_row = gain_low.astype(jnp.float32)
    conditioning = to_low(jax.nn.silu(time_embedding(step_ids, model_width)))
    mod_part = to_low(linear(conditioning, ada_weight) + ada_bias.astype(jnp.float32))
    text_part = to_low(linear(caption_rows, caption_proj))
    modulation, memory = (
        lax.all_gather(mod_part, "blk", axis=1, tiled=True),
        lax.all_gather(text_part, "blk", axis=1, tiled=True),
    )
    choose = frame_seg[:, None] == jnp.arange(seg_count, dtype=jnp.int32)[None, :]
    frame_mod = linear(choose.astype(jnp.bfloat16), modulation)
    pieces = [frame_mod[:, index * model_width : (index + 1) * model_width] for index in range(9)]
    (
        shift_one,
        scale_one,
        gate_one,
        shift_two,
        scale_two,
        gate_two,
        shift_three,
        scale_three,
        gate_three,
    ) = pieces
    spatial_input = to_low(modulate(inputs, shift_one, scale_one)).reshape(token_rows, model_width)
    spatial_qkv = to_low(linear(spatial_input, wide_sin)).reshape(
        patch_dev, frames, 3 * model_width
    )
    query_s = spatial_qkv[..., :model_width].reshape(patch_dev, frames, head_count, head_size)
    local_kv = spatial_qkv[..., model_width:]
    whole_kv = lax.all_gather(local_kv, "blk", axis=0, tiled=True)

    def split_kv(both):
        count = both.shape[0]
        return (
            both[..., :model_width].reshape(count, frames, head_count, head_size),
            both[..., model_width:].reshape(count, frames, head_count, head_size),
        )

    def spatial_probs(key_all):
        scores = jnp.einsum("pfhe,qfhe->fhpq", query_s, key_all, preferred_element_type=jnp.float32)
        return softmax_with_total(scores * score_scale)

    key_s, value_s = split_kv(whole_kv)
    probs_s, log_total_s = spatial_probs(key_s)
    probs_s_low = to_low(probs_s)
    attn_s = to_low(
        jnp.einsum(
            "fhpq,qfhe->pfhe", probs_s_low, value_s, preferred_element_type=jnp.float32
        ).reshape(token_rows, model_width)
    )
    branch_s = linear(attn_s, wide_sout).reshape(patch_dev, frames, model_width)
    after_one = inputs + gate_one * branch_s
    temporal_input = to_low(modulate(after_one, shift_two, scale_two)).reshape(
        token_rows, model_width
    )
    temporal_qkv = to_low(linear(temporal_input, wide_tin)).reshape(
        patch_dev, frames, 3, head_count, head_size
    )
    query_t = temporal_qkv[:, :, 0]
    key_t = temporal_qkv[:, :, 1]
    value_t = temporal_qkv[:, :, 2]
    same_seg = frame_seg[:, None] == frame_seg[None, :]
    scores_t = (
        jnp.einsum("pfhe,pghe->phfg", query_t, key_t, preferred_element_type=jnp.float32)
        * score_scale
    )
    probs_t = softmax_rows(jnp.where(same_seg[None, None], scores_t, MASKED))
    probs_t_low = to_low(probs_t)
    attn_t = to_low(
        jnp.einsum(
            "phfg,pghe->pfhe", probs_t_low, value_t, preferred_element_type=jnp.float32
        ).reshape(token_rows, model_width)
    )
    branch_t = linear(attn_t, wide_tout).reshape(patch_dev, frames, model_width)
    after_two = after_one + gate_two * branch_t
    cross_input = to_low(gain_norm(after_two, gain_row)).reshape(token_rows, model_width)
    query_c = to_low(linear(cross_input, wide_query)).reshape(
        patch_dev, frames, head_count, head_size
    )
    key_c = memory[:, :model_width].reshape(text_keys, head_count, head_size)
    value_c = memory[:, model_width:].reshape(text_keys, head_count, head_size)
    key_seg = jnp.arange(text_keys, dtype=jnp.int32) // text_len
    allowed = frame_seg[:, None] == key_seg[None, :]
    scores_c = (
        jnp.einsum("pfhe,khe->pfhk", query_c, key_c, preferred_element_type=jnp.float32)
        * score_scale
    )
    probs_c = softmax_rows(jnp.where(allowed[None, :, None, :], scores_c, MASKED))
    probs_c_low = to_low(probs_c)
    attn_c = to_low(
        jnp.einsum(
            "pfhk,khe->pfhe", probs_c_low, value_c, preferred_element_type=jnp.float32
        ).reshape(token_rows, model_width)
    )
    branch_c = linear(attn_c, wide_cout).reshape(patch_dev, frames, model_width)
    after_three = after_two + branch_c
    mlp_input = to_low(modulate(after_three, shift_three, scale_three)).reshape(
        token_rows, model_width
    )
    pre_act = linear(mlp_input, wide_hin)
    post_act = to_low(gelu_tanh(pre_act))
    branch_m = linear(post_act, wide_hout).reshape(patch_dev, frames, model_width)
    result = after_three + gate_three * branch_m
    grad_gate_three = jnp.sum(grad_out * branch_m, axis=0)
    grad_four = to_low(grad_out * gate_three).reshape(token_rows, model_width)
    grad_hout = left_product(post_act, grad_four)
    grad_post = right_product(grad_four, wide_hout)
    gelu_pull = jax.vjp(gelu_tanh, pre_act)[1]
    grad_pre = to_low(gelu_pull(grad_post)[0])
    grad_hin = left_product(mlp_input, grad_pre)
    grad_mlp_in = right_product(grad_pre, wide_hin).reshape(patch_dev, frames, model_width)
    mlp_pull = jax.vjp(modulate, after_three, shift_three, scale_three)[1]
    back_three, grad_shift_three, grad_scale_three = mlp_pull(grad_mlp_in)
    grad_three = grad_out + back_three
    grad_cross_branch = to_low(grad_three).reshape(token_rows, model_width)
    grad_cout = left_product(attn_c, grad_cross_branch)
    grad_attn_c = to_low(right_product(grad_cross_branch, wide_cout)).reshape(
        patch_dev, frames, head_count, head_size
    )
    grad_probs_c = jnp.einsum(
        "pfhe,khe->pfhk", grad_attn_c, value_c, preferred_element_type=jnp.float32
    )
    grad_scores_c = to_low(softmax_back(probs_c, grad_probs_c))
    grad_query_c = to_low(
        jnp.einsum("pfhk,khe->pfhe", grad_scores_c, key_c, preferred_element_type=jnp.float32)
        * score_scale
    ).reshape(token_rows, model_width)
    grad_key_c = (
        jnp.einsum("pfhk,pfhe->khe", grad_scores_c, query_c, preferred_element_type=jnp.float32)
        * score_scale
    )
    grad_value_c = jnp.einsum(
        "pfhk,pfhe->khe", probs_c_low, grad_attn_c, preferred_element_type=jnp.float32
    )
    grad_memory = jnp.concatenate(
        [grad_key_c.reshape(text_keys, model_width), grad_value_c.reshape(text_keys, model_width)],
        axis=1,
    )
    grad_wquery = left_product(cross_input, grad_query_c)
    grad_cross_in = right_product(grad_query_c, wide_query).reshape(patch_dev, frames, model_width)
    cross_pull = jax.vjp(gain_norm, after_two, gain_row)[1]
    back_two, grad_gain = cross_pull(grad_cross_in)
    grad_two = grad_three + back_two
    grad_gate_two = jnp.sum(grad_two * branch_t, axis=0)
    grad_temporal_branch = to_low(grad_two * gate_two).reshape(token_rows, model_width)
    grad_tout = left_product(attn_t, grad_temporal_branch)
    grad_attn_t = to_low(right_product(grad_temporal_branch, wide_tout)).reshape(
        patch_dev, frames, head_count, head_size
    )
    grad_probs_t = jnp.einsum(
        "pfhe,pghe->phfg", grad_attn_t, value_t, preferred_element_type=jnp.float32
    )
    grad_scores_t = to_low(softmax_back(probs_t, grad_probs_t))
    grad_query_t = (
        jnp.einsum("phfg,pghe->pfhe", grad_scores_t, key_t, preferred_element_type=jnp.float32)
        * score_scale
    )
    grad_key_t = (
        jnp.einsum("phfg,pfhe->pghe", grad_scores_t, query_t, preferred_element_type=jnp.float32)
        * score_scale
    )
    grad_value_t = jnp.einsum(
        "phfg,pfhe->pghe", probs_t_low, grad_attn_t, preferred_element_type=jnp.float32
    )
    grad_qkv_t = to_low(jnp.stack([grad_query_t, grad_key_t, grad_value_t], axis=2)).reshape(
        token_rows, 3 * model_width
    )
    grad_tin = left_product(temporal_input, grad_qkv_t)
    grad_temporal_in = right_product(grad_qkv_t, wide_tin).reshape(patch_dev, frames, model_width)
    temporal_pull = jax.vjp(modulate, after_one, shift_two, scale_two)[1]
    back_one, grad_shift_two, grad_scale_two = temporal_pull(grad_temporal_in)
    grad_one = grad_two + back_one
    grad_gate_one = jnp.sum(grad_one * branch_s, axis=0)
    grad_spatial_branch = to_low(grad_one * gate_one).reshape(token_rows, model_width)
    grad_sout = left_product(attn_s, grad_spatial_branch)
    grad_attn_s = to_low(right_product(grad_spatial_branch, wide_sout)).reshape(
        patch_dev, frames, head_count, head_size
    )
    back_kv = lax.all_gather(local_kv, "blk", axis=0, tiled=True)
    back_key, back_value = split_kv(back_kv)
    back_probs = spatial_probs(back_key)[0]
    back_probs_low = to_low(back_probs)
    grad_probs_s = jnp.einsum(
        "pfhe,qfhe->fhpq", grad_attn_s, back_value, preferred_element_type=jnp.float32
    )
    row_delta = jnp.sum(grad_probs_s * back_probs, axis=-1, keepdims=True)
    grad_scores_s = to_low(back_probs * (grad_probs_s - row_delta))
    grad_query_s = (
        jnp.einsum("fhpq,qfhe->pfhe", grad_scores_s, back_key, preferred_element_type=jnp.float32)
        * score_scale
    )
    count = lax.axis_size("blk") * patch_dev
    grad_key = (
        jnp.einsum("fhpq,pfhe->qfhe", grad_scores_s, query_s, preferred_element_type=jnp.float32)
        * score_scale
    )
    grad_value = jnp.einsum(
        "fhpq,pfhe->qfhe", back_probs_low, grad_attn_s, preferred_element_type=jnp.float32
    )
    grad_kv = to_low(
        lax.psum_scatter(
            jnp.concatenate(
                [
                    grad_key.reshape(count, frames, model_width),
                    grad_value.reshape(count, frames, model_width),
                ],
                axis=2,
            ).astype(jnp.bfloat16),
            "blk",
            scatter_dimension=0,
            tiled=True,
        ).astype(jnp.float32)
    )
    grad_qkv_s = jnp.concatenate(
        [to_low(grad_query_s).reshape(patch_dev, frames, model_width), grad_kv], axis=2
    ).reshape(token_rows, 3 * model_width)
    grad_sin = left_product(spatial_input, grad_qkv_s)
    grad_spatial_in = right_product(grad_qkv_s, wide_sin).reshape(patch_dev, frames, model_width)
    spatial_pull = jax.vjp(modulate, inputs, shift_one, scale_one)[1]
    back_zero, grad_shift_one, grad_scale_one = spatial_pull(grad_spatial_in)
    grad_input = grad_one + back_zero
    grad_frame_mod = jnp.concatenate(
        [
            grad_shift_one,
            grad_scale_one,
            grad_gate_one,
            grad_shift_two,
            grad_scale_two,
            grad_gate_two,
            grad_shift_three,
            grad_scale_three,
            grad_gate_three,
        ],
        axis=1,
    )
    grad_mod_local = lax.dot_general(
        choose.astype(jnp.float32),
        grad_frame_mod,
        (((0,), (0,)), ((), ())),
        precision=lax.Precision.HIGHEST,
    )
    grad_mod_part, grad_memory_part = (
        lax.psum_scatter(
            grad_mod_local.astype(jnp.bfloat16), "blk", scatter_dimension=1, tiled=True
        ).astype(jnp.float32),
        lax.psum_scatter(
            grad_memory.astype(jnp.bfloat16), "blk", scatter_dimension=1, tiled=True
        ).astype(jnp.float32),
    )
    grad_mod_low = to_low(grad_mod_part)
    grad_ada_w = left_product(conditioning, grad_mod_low)
    grad_ada_b = jnp.sum(grad_mod_low.astype(jnp.float32), axis=0)
    grad_caption = left_product(caption_rows, to_low(grad_memory_part))
    grad_ada_w, grad_ada_b, grad_caption = (
        lax.psum(grad_ada_w.astype(jnp.bfloat16), "seq").astype(jnp.float32),
        lax.psum(grad_ada_b.astype(jnp.bfloat16), "seq").astype(jnp.float32),
        lax.psum(grad_caption.astype(jnp.bfloat16), "seq").astype(jnp.float32),
    )
    shares = (
        lax.psum_scatter(grad_sin, ("seq", "blk"), scatter_dimension=0, tiled=True),
        lax.psum_scatter(grad_sout, ("seq", "blk"), scatter_dimension=0, tiled=True),
        lax.psum_scatter(grad_tin, ("seq", "blk"), scatter_dimension=0, tiled=True),
        lax.psum_scatter(grad_tout, ("seq", "blk"), scatter_dimension=0, tiled=True),
        lax.psum_scatter(grad_gain, ("seq", "blk"), scatter_dimension=0, tiled=True),
        lax.psum_scatter(grad_wquery, ("seq", "blk"), scatter_dimension=0, tiled=True),
        lax.psum_scatter(grad_cout, ("seq", "blk"), scatter_dimension=0, tiled=True),
        lax.psum_scatter(grad_hin, ("seq", "blk"), scatter_dimension=0, tiled=True),
        lax.psum_scatter(grad_hout, ("seq", "blk"), scatter_dimension=0, tiled=True),
    )
    (
        share_sin,
        share_sout,
        share_tin,
        share_tout,
        share_gain,
        share_query,
        share_cout,
        share_hin,
        share_hout,
    ) = shares
    return (
        to_low(result)[None],
        to_low(grad_input)[None],
        grad_ada_w,
        grad_ada_b,
        share_sin,
        share_sout,
        share_tin,
        share_tout,
        share_gain,
        share_query,
        grad_caption,
        share_cout,
        share_hin,
        share_hout,
    )


MESH = pl.DeviceIdType.MESH
BLOCKS = 18
LINES = 8
SHARD = 36
LINE = 4 * SHARD
WINDOW = 48
WIDE = LINES * LINE
MIB = 2**20


def place():
    seq = lax.axis_index("seq")
    blk = lax.axis_index("blk")
    x, c = seq // 2, seq % 2
    z, y = blk // 2, blk % 2
    x1, y1 = x + (1 - 2 * x) * (1 - c), y + (1 - 2 * y) * c
    x2, y2 = x + (1 - 2 * x) * c, y + (1 - 2 * y) * (1 - c)
    return x, c, y, z, x1, y1, x2, y2


def device(x, c, y, z):
    return {"seq": x * 2 + c, "blk": z * 2 + y}


def line_of(c, x, y):
    return (c * 2 + x) * 2 + y


def remote(src, dst, send_sem, recv_sem, where):
    return pltpu.make_async_remote_copy(
        src_ref=src,
        dst_ref=dst,
        send_sem=send_sem,
        recv_sem=recv_sem,
        device_id=where,
        device_id_type=MESH,
    )


def greet(others):
    barrier = pltpu.get_barrier_semaphore()
    for other in others:
        pl.semaphore_signal(barrier, inc=1, device_id=other, device_id_type=MESH)
    pl.semaphore_wait(barrier, len(others))


def left_at(t):
    at = jnp.minimum(t, 4)
    for first in (8, 9, 10, 11, 14, 15):
        at = at + jnp.where(t >= first, 1, 0)
    return at


def right_at(t):
    return jnp.where(t < 14, jnp.maximum(t - 3, 0), t - 13)


ROWS = 256
KEYS = 256
TEXT = 288
MOD = 9 * WIDE
MOD_TILES = 11
MOD_WIN = 128 * MOD_TILES
PARTS, HELD, LAST = 4, 4, 8
PAIR = 80
LEFT_SEM, SLOPE_SEM, SAVE_SEMS = 40, 42, 44
TILE = 384
SCALE = E ** (-0.5)


def nt(left, right):
    return lax.dot_general(
        left, right, (((1,), (1,)), ((), ())), preferred_element_type=jnp.float32
    )


def wide32(values):
    return values.astype(jnp.float32)


def loop(count, body):
    def step(index, carry):
        body(index)
        return carry

    lax.fori_loop(0, count, step, 0)


def each_rows(size, body, total=ROWS):
    loop(total // size, lambda i: body(pl.ds(pl.multiple_of(i * size, size), size)))


def each_cols(body):
    body(slice(0, 2 * TILE))
    body(slice(2 * TILE, 3 * TILE))


def identity(size):
    row = lax.broadcasted_iota(jnp.int32, (size, size), 0)
    col = lax.broadcasted_iota(jnp.int32, (size, size), 1)
    return to_low((row == col).astype(jnp.float32))


def transposed(same, values, to, start):
    for at in range(0, values.shape[1], TILE):
        to[start + at : start + at + TILE, :] = to_low(nt(same, values[:, at : at + TILE]))


def swap_rows():
    row = lax.broadcasted_iota(jnp.int32, (ROWS, ROWS), 0)
    col = lax.broadcasted_iota(jnp.int32, (ROWS, ROWS), 1)
    return to_low((((row & 15) << 4) + (row >> 4) == col).astype(jnp.float32))


def head_window(h):
    base = h * E
    start = jnp.minimum(base // 128, 7) * 128
    lane = lax.broadcasted_iota(jnp.int32, (1, 256), 1)
    on = (lane >= base - start) & (lane < base - start + E)
    return pl.ds(pl.multiple_of(start, 128), 256), on.astype(jnp.float32)


def soft(scores, bias, mask):
    scores = scores * SCALE
    if bias is not None:
        scores = scores + bias
    powers = jnp.exp(scores - jnp.max(scores, axis=-1, keepdims=True))
    probs = powers * (1.0 / jnp.sum(powers, axis=-1, keepdims=True))
    return probs if mask is None else probs * mask


def chains(h, groups):
    return [(window, rows, keys) for window in (head_window(h), head_window(h + H // 2)) for rows, keys in groups]


def split_rows(values, jobs):
    start = 0
    parts = []
    for _, rows, _ in jobs:
        size = rows.stop - rows.start
        parts.append(values[start : start + size])
        start += size
    return parts


def heads_forward(h, query, key, value, attn, groups, bias, mask):
    jobs = chains(h, groups)
    scores = [nt(query[rows, lanes] * to_low(on), key[keys, lanes]) for (lanes, on), rows, keys in jobs]
    probs = split_rows(to_low(soft(jnp.concatenate(scores), bias, mask)), jobs)
    parts = [linear(prob, value[keys, lanes]) * on for prob, ((lanes, on), rows, keys) in zip(probs, jobs)]
    for part, ((lanes, on), rows, keys) in zip(parts, jobs):
        attn[rows, lanes] = attn[rows, lanes] + to_low(part)


def text_heads_forward(h, query, key, value, attn, bias, mask):
    jobs = chains(h, VIDEOS)
    scores = [linear(query[rows, lanes] * to_low(on), key[lanes, keys]) for (lanes, on), rows, keys in jobs]
    probs = split_rows(to_low(soft(jnp.concatenate(scores), bias, mask)), jobs)
    parts = [nt(prob, value[lanes, keys]) * on for prob, ((lanes, on), rows, keys) in zip(probs, jobs)]
    for part, ((lanes, on), rows, keys) in zip(parts, jobs):
        attn[rows, lanes] = attn[rows, lanes] + to_low(part)


HALVES = [(slice(0, 128), slice(0, 128)), (slice(128, 256), slice(128, 256))]
VIDEOS = [(slice(0, 144), slice(0, 128)), (slice(112, 256), slice(128, 256))]


def regroup(back):
    row = lax.broadcasted_iota(jnp.int32, (ROWS, ROWS), 0)
    col = lax.broadcasted_iota(jnp.int32, (ROWS, ROWS), 1)
    if back:
        source = (((row >> 3) & 1) << 7) + ((row >> 4) << 3) + (row & 7)
    else:
        source = (((row >> 3) & 15) << 4) + ((row >> 7) << 3) + (row & 7)
    return to_low((source == col).astype(jnp.float32))


def temporal_bias(seg_in, seg_row):
    row = lax.broadcasted_iota(jnp.int32, (128, 128), 0)
    col = lax.broadcasted_iota(jnp.int32, (128, 128), 1)
    allowed = ((row & 7) == (col & 7)) & (seg_in[2, 0:128, 0:1] == seg_row[0:1, 0:128])
    return jnp.where(allowed, 0.0, MASKED)


def cross_bias():
    col = lax.broadcasted_iota(jnp.int32, (1, 128), 1)
    return jnp.where(col < L, 0.0, MASKED)


def cross_rows(seg_in):
    both = [1.0 - seg_in[0, 0:144, 0:1], seg_in[0, 112:256, 0:1]]
    return jnp.concatenate(both + both)


def move_lanes(to, value, from_start, to_start, width):
    left = min(from_start // 128 * 128, value.shape[1] - 256)
    right = min(to_start // 128 * 128, width - 256)
    off = to_start - right
    part = pltpu.roll(value[:, left : left + 256], (off - (from_start - left)) % 256, 1)
    lane = lax.broadcasted_iota(jnp.int32, part.shape, 1)
    lanes = slice(right, right + 256)
    to[:, lanes] = jnp.where((lane >= off) & (lane < off + SHARD), part, to[:, lanes])


def hidden_places():
    places = []
    for d in range(32):
        xp, cp, zp, yp = d // 16, d // 8 % 2, d // 2 % 4, d % 2
        for k in range(4):
            places.append((k, (4 * d + k) * SHARD, (((cp * 2 + xp) * 2 + yp) * 4 + zp) * SHARD))
    return places


def blk_peers(x, c, b):
    return [device(x, c, (b + k) % 2, ((b + k) % 8) // 2) for k in range(1, 8)]


def forward_kernel(
    spatial_in, spatial_out, temporal_in, temporal_out, cross_query, cross_out, hidden_in, hidden_out,
    tok, gain_one, cond, ada_bias, seg_in, seg_row, cot_i, turn_i, ada_i, caption_i, proj_i,
    wide, out, left_o, qkvs_o, qkvt_o, qc_o, mem_o, xhat_o, rstd_o, branch_o, slope_o, gfour_o, cot_o, mods_o, gate_o, gain_o,
    win, pair, far, lines, weights, tokp, cotp, tokf, xin, xp, left, qkvs, qkvt, qc, mem, text, mod, mods, xhat, rstd, branch, branchw, bias,
    stream, attnf, attnp, post, slope, gfour, gains, gain_at, gate,
    src, cot, turn, ada, caption, proj, mod_in, text_in, hidden,
    z_send, z_recv, l_send, l_recv, own_sem, w_sem, t_send, t_recv, a_send, a_recv, m_send, m_recv, x_send, x_recv,
    g_send, g_recv, save_sem, in_sem,
):
    x, c, y, z, x1, y1, x2, y2 = place()
    b = z * 2 + y
    near = [device(x, c, y, (z + k) % 4) for k in (1, 2, 3)]
    beside, across = device(x, c, y, z + 1 - 2 * (z % 2)), device(x, c, y, 3 - z)
    middle = (z == 1) | (z == 2)
    first, second, twin = device(x1, c, y1, z), device(x2, c, y2, z), device(x, 1 - c, y, z)
    peers = blk_peers(x, c, b)
    greet(peers + [device(1 - x, c, y, z), twin])
    mine, line3 = line_of(c, x, y), line_of(c, 1 - x, 1 - y)

    def hops(t, core):
        turn_round = core + (1 - core) * (t % 4 == 2)
        xa, ya = x + (1 - 2 * x) * (1 - turn_round), y + (1 - 2 * y) * turn_round
        xb, yb = x + (1 - 2 * x) * turn_round, y + (1 - 2 * y) * (1 - turn_round)
        return (xa, ya), (xb, yb)

    def z_one(t):
        return remote(src.at[t], win.at[t % PARTS], z_send.at[t, 0], z_recv.at[t, 0], beside)

    def z_two(t):
        return remote(pair.at[t % PARTS], far.at[t % PARTS], z_send.at[t, 1], z_recv.at[t, 1], across)

    def z_three(t):
        return remote(far.at[t % PARTS], far.at[t % PARTS], z_send.at[t, 2], z_recv.at[t, 2], beside)

    def wide_line(t, line):
        return wide.at[t, pl.ds(pl.multiple_of(line * LINE, 16), LINE)]

    def own(t):
        return pltpu.make_async_copy(lines.at[t % HELD], wide_line(t, mine), own_sem.at[t])

    def line_copy(t, to, line, index, where):
        return remote(to, wide_line(t, line), l_send.at[t, index], l_recv.at[t, index], where)

    def sends(t, index):
        (xa, ya), (xb, yb) = hops(t, c)
        one, two = device(xa, c, ya, z), device(xb, c, yb, z)
        line1, line2 = line_of(c, xa, ya), line_of(c, xb, yb)
        line, where = (
            (mine, one), (mine, two), (mine, twin), (line1, two),
            (line1, twin), (line2, twin), (line3, twin),
        )[index]
        from_here = lines.at[t % HELD] if index < 3 else wide_line(t, line)
        return line_copy(t, from_here, line, index, where)

    def arrives(t, line, index):
        line_copy(t, wide_line(t, line), line, index, first).wait_recv()

    def tick(t):
        @pl.when((t >= 4) & (t < BLOCKS + 4))
        def _():
            now = t - 4

            @pl.when(middle)
            def _():
                z_two(now).wait_send()
                z_three(now).wait_send()

            @pl.when(jnp.logical_not(middle))
            def _():
                z_three(now).wait_recv()

            @pl.when(now >= HELD)
            def _():
                for index in range(3):
                    sends(now - HELD, index).wait_send()
                own(now - HELD).wait()

            def line_from(low, high):
                at = now % HELD
                lines[at, 0:64] = low[0:64]
                lines[at, 64:80] = low[64:80] + high[0:16]
                lines[at, 80:144] = high[16:80]

            @pl.when(z < 2)
            def _():
                line_from(pair[now % PARTS], far[now % PARTS])

            @pl.when(z >= 2)
            def _():
                line_from(far[now % PARTS], pair[now % PARTS])

            for index in range(3):
                sends(now, index).start()
            own(now).start()

        @pl.when((t >= 2) & (t < BLOCKS + 2) & middle)
        def _():
            z_two(t - 2).wait_recv()
            z_three(t - 2).start()

        @pl.when((t >= 1) & (t < BLOCKS + 1))
        def _():
            now = t - 1
            z_one(now).wait_recv()

            def pair_from(even, odd):
                at = now % PARTS
                pair[at, 0:32] = even[0:32]
                pair[at, 32:48] = even[32:48] + odd[0:16]
                pair[at, 48:80] = odd[16:48]

            @pl.when(z % 2 == 0)
            def _():
                pair_from(src[now], win[now % PARTS])

            @pl.when(z % 2 == 1)
            def _():
                pair_from(win[now % PARTS], src[now])

            @pl.when(middle)
            def _():
                z_two(now).start()

        @pl.when(t < BLOCKS)
        def _():
            z_one(t).start()

        @pl.when((t >= 6) & (t < BLOCKS + 6))
        def _():
            now = t - 6
            xa, ya = hops(now, c)[0]
            arrives(now, line_of(c, xa, ya), 0)
            for index in (3, 4):
                sends(now, index).start()

        @pl.when(t >= LAST)
        def _():
            now = t - LAST
            xb, yb = hops(now, c)[1]
            arrives(now, line_of(c, xb, yb), 1)
            sends(now, 5).start()
            arrives(now, line3, 3)
            sends(now, 6).start()

    done = [0]

    def pump(until):
        until = min(until, BLOCKS + LAST)
        if until > done[0]:
            start = done[0]
            loop(until - start, lambda i: tick(i + start))
            done[0] = until

    def poke():
        pump(done[0] + 1)

    def weight_copy(block):
        return pltpu.make_async_copy(wide.at[block], weights.at[block % 2], w_sem.at[block % 2])

    loaded = set()

    def begin(block):
        if block in loaded:
            return
        loaded.add(block)
        pump(block + LAST + 1)
        near_at, far_at = hops(block, 1 - c)
        places = [(x, y), near_at, far_at, (1 - x, 1 - y)]
        for (xl, yl), index in zip(places, (2, 4, 5, 6)):
            arrives(block, line_of(1 - c, xl, yl), index)
        if block >= BLOCKS - HELD:
            own(block).wait()
        weight_copy(block).start()

    def load(block):
        begin(block)
        weight_copy(block).wait()
        if 3 <= block < BLOCKS - 1:
            begin(block + 1)

    def times(values, block, emit):
        def tile(cols):
            emit(cols, linear(values[...], weights[block % 2, :, cols]))

        each_cols(tile)

    saves = []
    held = {}

    def save(from_ref, to_ref, name=None):
        if name is None:
            name = len(saves)
            saves.append(name)
        held[name] = pltpu.make_async_copy(from_ref, to_ref, save_sem.at[name])
        held[name].start()

    def settle(name):
        if name in held:
            held.pop(name).wait()

    def turned(values, index):
        slot = index % 2
        settle(LEFT_SEM + slot)

        def tile(cols):
            low = to_low(nt(values[...], turn[cols, :]))
            xp[:, cols] = low
            transposed(identity(TILE), low, left.at[slot], cols.start)

        each_cols(tile)
        save(left.at[slot], left_o.at[index], LEFT_SEM + slot)

    fetches = [
        pltpu.make_async_copy(from_ref, to_ref, in_sem.at[at])
        for at, (from_ref, to_ref) in enumerate(
            ((ada_i, ada), (turn_i, turn), (cot_i, cot), (caption_i, caption), (proj_i, proj))
        )
    ]
    for copy in fetches:
        copy.start()

    def shift(rows, first):
        row = lax.broadcasted_iota(jnp.int32, (WINDOW, rows), 0) - 4 * z
        col = lax.broadcasted_iota(jnp.int32, (WINDOW, rows), 1)
        return to_low(((row >= 0) & (row < SHARD) & (row + first == col)).astype(jnp.float32))

    def window(at, values):
        src[at] = to_low(linear(shift(SHARD, 0), values))

    for j in range(3):
        window(j, spatial_in[:, WIDE * j : WIDE * j + WIDE])
    pump(2)
    window(3, spatial_out[...])
    for j in range(3):
        window(4 + j, temporal_in[:, WIDE * j : WIDE * j + WIDE])
    window(7, temporal_out[...])
    window(8, cross_query[...])
    window(9, cross_out[...])
    pump(4)

    def m_copy(k, at):
        return remote(mod_in, mod.at[at], m_send.at[k - 1], m_recv.at[k - 1], peers[k - 1])

    fetches[0].wait()
    part = wide32(to_low(nt(cond[...], ada[...]) + wide32(ada_bias[...])))[0:8]
    part = jnp.concatenate([part, jnp.zeros((8, MOD_WIN - MOD // 8), jnp.float32)], axis=1)
    part = pltpu.roll(part, 16 * b, 1)
    tiles = [part[row : row + 1, 128 * tile : 128 * tile + 128] for row in range(2) for tile in range(MOD_TILES)]
    mod_in[...] = to_low(jnp.concatenate(tiles + [jnp.zeros((32 - 2 * MOD_TILES, 128), jnp.float32)]))
    for k in range(1, 8):
        m_copy(k, b).start()
    mod[b] = mod_in[...]
    swap = swap_rows()
    tokp[...] = to_low(linear(swap, tok[...]))

    def t_copy(k):
        to = (b + k) % 8
        part = tokp.at[pl.ds(pl.multiple_of(32 * to, 32), 32)]
        return remote(part, tokf.at[b], t_send.at[k - 1], t_recv.at[k - 1], peers[k - 1])

    def t_wait(k):
        of = (b + 8 - k) % 8
        remote(tokp.at[pl.ds(0, 32)], tokf.at[of], t_send.at[k - 1], t_recv.at[k - 1], peers[k - 1]).wait_recv()

    pump(5)
    for k in range(1, 8):
        t_copy(k).start()
    tokf[b] = tokp[pl.ds(pl.multiple_of(32 * b, 32), 32)]

    def g_copy(at, from_at, to):
        return remote(gains.at[from_at], gain_at.at[at], g_send.at[at], g_recv.at[at], to)

    spread = jnp.concatenate([wide32(gain_one[...]), jnp.zeros((8, WIDE - SHARD), jnp.float32)], axis=1)
    gains[0] = pltpu.roll(spread, SHARD * ((x * 2 + c) * 8 + b), 1)
    g_copy(0, 0, twin).start()
    pump(6)
    fetches[2].wait()
    cotp[...] = to_low(linear(swap, cot[...]))
    save(cotp, cot_o)

    def x_copy(k, at):
        return remote(text_in, text.at[at, y], x_send.at[k - 1], x_recv.at[k - 1], near[k - 1])

    def x_over(at):
        return remote(text.at[:, at], text.at[:, at], x_send.at[3], x_recv.at[3], device(x, c, 1 - y, z))

    for k in range(1, 8):
        m_copy(k, (b + 8 - k) % 8).wait_recv()
    mods[...] = jnp.zeros_like(mods)
    for k in range(8):
        part = wide32(mod[k])
        for row in range(2):
            for tile in range(MOD_TILES):
                lanes = slice(1280 * k + 128 * tile, 1280 * k + 128 * tile + 128)
                at = row * MOD_TILES + tile
                mods[row : row + 1, lanes] = mods[row : row + 1, lanes] + part[at : at + 1]
    save(mods, mods_o)
    g_copy(0, 0, twin).wait_recv()
    gains[1] = gains[0] + gain_at[0]
    g_copy(1, 1, first).start()
    pump(7)
    fetches[3].wait()
    fetches[4].wait()
    text_in[...] = jnp.zeros_like(text_in)
    for v in range(2):
        text_in[:, 128 * v : 128 * v + L] = to_low(nt(proj[...], caption[v]))
    for k in (1, 2, 3):
        x_copy(k, z).start()
    text[z, y] = text_in[...]
    pump(8)
    hidden[...] = jnp.zeros_like(hidden)
    for k, natural, placed in hidden_places():
        start = natural // WIDE * WIDE
        move_lanes(hidden.at[k], wide32(hidden_in[:, start : start + WIDE]), natural - start, placed, WIDE)
    for k in range(4):
        window(10 + 2 * k, to_low(hidden[k]))
        src[11 + 2 * k] = to_low(linear(shift(4 * SHARD, SHARD * k), hidden_out[...]))
    fetches[1].wait()

    def pick(piece, seg):
        lanes = slice(WIDE * piece, WIDE * piece + WIDE)
        return jnp.where(seg > 0.5, mods[1:2, lanes], mods[0:1, lanes])

    def normal(values, rows, index):
        center = values - jnp.mean(values, axis=-1, keepdims=True)
        factor = lax.rsqrt(jnp.mean(center * center, axis=-1, keepdims=True) + EPSILON)
        scaled = center * factor
        xhat[index, rows, :] = to_low(scaled)
        rstd[index, rows, :] = jnp.broadcast_to(factor, (factor.shape[0], 128))
        return scaled

    for k in range(1, 8):
        t_wait(k)
    g_copy(1, 1, first).wait_recv()
    gains[2] = gains[1] + gain_at[1]
    g_copy(2, 2, second).start()

    def spatial_rows(i):
        seg = jnp.concatenate([seg_in[1, 0:16, 0:1], seg_in[1, 128:144, 0:1]])
        values = wide32(tokf[i])
        center = values - jnp.mean(values, axis=-1, keepdims=True)
        factor = lax.rsqrt(jnp.mean(center * center, axis=-1, keepdims=True) + EPSILON)
        scaled = center * factor
        ready = to_low(scaled * (1.0 + pick(1, seg)) + pick(0, seg))
        low = to_low(scaled)
        spread = jnp.broadcast_to(factor, (32, 128))
        for f in range(2):
            rows = pl.ds(pl.multiple_of(128 * f + 16 * i, 16), 16)
            part = slice(16 * f, 16 * f + 16)
            xhat[0, rows, :] = low[part]
            rstd[0, rows, :] = spread[part]
            xin[rows, :] = ready[part]

    loop(8, spatial_rows)
    save(xhat.at[0], xhat_o.at[0])
    save(rstd.at[0], rstd_o.at[0])
    turned(xin, 10)
    for j in range(3):
        load(j)

        def emit(cols, value, j=j):
            qkvs[j, :, cols] = to_low(value)

        times(xp, j, emit)
    save(qkvs, qkvs_o)
    g_copy(2, 2, second).wait_recv()
    gains[3] = gains[2] + gain_at[2]
    for k in (1, 2, 3):
        remote(gains.at[3], gain_at.at[2 + k], g_send.at[2 + k], g_recv.at[2 + k], near[k - 1]).start()
    for k in (1, 2, 3):
        x_copy(k, (z + 4 - k) % 4).wait_recv()
    x_over(y).start()
    attnf[...] = jnp.zeros_like(attnf)

    def spatial_heads(h):
        heads_forward(h, qkvs.at[0], qkvs.at[1], qkvs.at[2], attnf, HALVES, None, None)

    loop(4, spatial_heads)
    poke()
    loop(4, lambda h: spatial_heads(h + 4))
    for k in (1, 2, 3):
        remote(gains.at[3], gain_at.at[2 + k], g_send.at[2 + k], g_recv.at[2 + k], near[k - 1]).wait_recv()
    gains[0 + 4] = gains[3] + gain_at[3] + gain_at[4] + gain_at[5]
    save(gains.at[4], gain_o)

    def a_copy(k, f):
        to = (b + k) % 8
        part = attnf.at[pl.ds(pl.multiple_of(128 * f + 16 * to, 16), 16)]
        return remote(part, attnp.at[2 * b + f], a_send.at[k - 1, f], a_recv.at[k - 1, f], peers[k - 1])

    def a_wait(k, f):
        of = (b + 8 - k) % 8
        part = attnf.at[pl.ds(0, 16)]
        remote(part, attnp.at[2 * of + f], a_send.at[k - 1, f], a_recv.at[k - 1, f], peers[k - 1]).wait_recv()

    for k in range(1, 8):
        for f in range(2):
            a_copy(k, f).start()
    for f in range(2):
        attnp[2 * b + f] = attnf[pl.ds(pl.multiple_of(128 * f + 16 * b, 16), 16)]
    pump(done[0] + 2)
    for k in range(1, 8):
        for f in range(2):
            a_wait(k, f)
    xin[...] = attnp[...].reshape(ROWS, WIDE)
    turned(xin, 9)
    load(3)

    def emit_branch(cols, value):
        branchw[:, cols] = value

    times(xp, 3, emit_branch)

    def after_spatial(rows):
        seg = seg_in[0, rows, 0:1]
        value = branchw[rows, :]
        branch[0, rows, :] = to_low(value)
        value = wide32(tokp[rows, :]) + pick(2, seg) * value
        stream[rows, :] = value
        xin[rows, :] = to_low(normal(value, rows, 1) * (1.0 + pick(4, seg)) + pick(3, seg))

    each_rows(32, after_spatial)
    save(branch.at[0], branch_o.at[0])
    save(xhat.at[1], xhat_o.at[1])
    save(rstd.at[1], rstd_o.at[1])

    for k in range(1, 8):
        for f in range(2):
            a_copy(k, f).wait_send()
    attnf[...] = to_low(linear(regroup(False), xin[...]))
    turned(attnf, 8)
    for j in range(3):
        load(4 + j)

        def emit(cols, value, j=j):
            qkvt[j, :, cols] = to_low(value)

        times(xp, 4 + j, emit)
    save(qkvt, qkvt_o)
    attnf[...] = jnp.zeros_like(attnf)

    bias[...] = temporal_bias(seg_in, seg_row)

    def temporal_heads(h):
        heads_forward(
            h, qkvt.at[0], qkvt.at[1], qkvt.at[2], attnf, HALVES, jnp.concatenate([bias[...]] * 4), None
        )

    loop(4, temporal_heads)
    poke()
    loop(4, lambda h: temporal_heads(h + 4))
    xin[...] = to_low(linear(regroup(True), attnf[...]))
    turned(xin, 7)
    load(7)
    times(xp, 7, emit_branch)

    def after_temporal(rows):
        seg = seg_in[0, rows, 0:1]
        value = branchw[rows, :]
        branch[1, rows, :] = to_low(value)
        value = stream[rows, :] + pick(5, seg) * value
        stream[rows, :] = value
        xin[rows, :] = to_low(normal(value, rows, 2) * gains[4, 0:1, :])

    each_rows(32, after_temporal)
    save(branch.at[1], branch_o.at[1])
    save(xhat.at[2], xhat_o.at[2])
    save(rstd.at[2], rstd_o.at[2])

    turned(xin, 6)
    load(8)

    def emit_query(cols, value):
        qc[:, cols] = to_low(value)

    times(xp, 8, emit_query)
    save(qc, qc_o)
    x_over(1 - y).wait_recv()
    for k in range(8):
        mem[k // 4, TEXT * (k % 4) : TEXT * (k % 4) + TEXT, :] = text[k // 2, k % 2]
    save(mem, mem_o)
    attnf[...] = jnp.zeros_like(attnf)

    def cross_heads(h):
        text_heads_forward(h, qc, mem.at[0], mem.at[1], attnf, cross_bias(), cross_rows(seg_in))

    loop(4, cross_heads)
    poke()
    loop(4, lambda h: cross_heads(h + 4))
    xin[...] = attnf[...]
    turned(xin, 5)
    load(9)
    times(xp, 9, emit_branch)

    def after_cross(rows):
        seg = seg_in[0, rows, 0:1]
        value = stream[rows, :] + branchw[rows, :]
        stream[rows, :] = value
        xin[rows, :] = to_low(normal(value, rows, 3) * (1.0 + pick(7, seg)) + pick(6, seg))
        gfour[rows, :] = to_low(wide32(cotp[rows, :]) * pick(8, seg))

    each_rows(32, after_cross)
    save(xhat.at[3], xhat_o.at[3])
    save(rstd.at[3], rstd_o.at[3])
    save(gfour, gfour_o)

    turned(xin, 4)
    for k in range(4):
        slot = k % 2
        load(10 + 2 * k)
        settle(SLOPE_SEM + slot)
        settle(LEFT_SEM + slot)

        def emit_hidden(cols, value, slot=slot):
            inner = math.sqrt(2.0 / math.pi) * (value + 0.044715 * value * value * value)
            bent = jnp.tanh(inner)
            half = 0.5 * (1.0 + bent)
            tilt = math.sqrt(2.0 / math.pi) * (1.0 + 3 * 0.044715 * value * value)
            slope[slot, :, cols] = to_low(half + 0.5 * value * (1.0 - bent * bent) * tilt)
            low = to_low(value * half)
            post[:, cols] = low
            transposed(identity(TILE), low, left.at[slot], cols.start)

        times(xp, 10 + 2 * k, emit_hidden)
        save(slope.at[slot], slope_o.at[k], SLOPE_SEM + slot)
        save(left.at[slot], left_o.at[k], LEFT_SEM + slot)
        load(11 + 2 * k)

        def emit_out(cols, value, k=k):
            branchw[:, cols] = value if k == 0 else branchw[:, cols] + value

        times(post, 11 + 2 * k, emit_out)

    gate[...] = jnp.zeros_like(gate)

    def last(rows):
        seg = seg_in[0, rows, 0:1]
        value = branchw[rows, :]
        xin[rows, :] = to_low(stream[rows, :] + pick(8, seg) * value)
        value = wide32(cotp[rows, :]) * value
        later = jnp.sum(value * seg, axis=0, keepdims=True)
        every = jnp.sum(value, axis=0, keepdims=True)
        gate[0:1, :] = gate[0:1, :] + (every - later)
        gate[1:2, :] = gate[1:2, :] + later

    each_rows(32, last)
    save(gate, gate_o)
    out[...] = to_low(linear(swap_rows(), xin[...]))

    for copy in held.values():
        copy.wait()
    for k in range(1, 8):
        t_copy(k).wait_send()
        m_copy(k, b).wait_send()
    for k in (1, 2, 3):
        x_copy(k, z).wait_send()
    x_over(y).wait_send()
    for at, to in ((0, twin), (1, first), (2, second)):
        g_copy(at, at, to).wait_send()
    for k in (1, 2, 3):
        remote(gains.at[3], gain_at.at[2 + k], g_send.at[2 + k], g_recv.at[2 + k], near[k - 1]).wait_send()

    for t in range(BLOCKS - HELD, BLOCKS):
        for index in range(3):
            sends(t, index).wait_send()

    def finish(t):
        z_one(t).wait_send()
        for index in range(3, 7):
            sends(t, index).wait_send()

    loop(BLOCKS, finish)


ANY = pl.BlockSpec(memory_space=pl.ANY)
IN_VMEM = pl.BlockSpec(memory_space=pltpu.VMEM)


def forward(*operands):
    low, full = jnp.bfloat16, jnp.float32
    dma = pltpu.SemaphoreType.DMA
    hbm = [
        ((BLOCKS, WIDE, WIDE), low),
        ((ROWS, WIDE), low),
        ((11, WIDE, ROWS), low),
        ((3, ROWS, WIDE), low),
        ((3, ROWS, WIDE), low),
        ((ROWS, WIDE), low),
        ((2, WIDE, KEYS), low),
        ((4, ROWS, WIDE), low),
        ((4, ROWS, 128), full),
        ((2, ROWS, WIDE), low),
        ((4, ROWS, WIDE), low),
        ((ROWS, WIDE), low),
        ((ROWS, WIDE), low),
        ((8, MOD), full),
        ((8, WIDE), full),
        ((8, WIDE), full),
    ]
    vmem = [
        ((PARTS, WINDOW, WIDE), low),
        ((PARTS, PAIR, WIDE), low),
        ((PARTS, PAIR, WIDE), low),
        ((HELD, LINE, WIDE), low),
        ((2, WIDE, WIDE), low),
        ((ROWS, WIDE), low),
        ((ROWS, WIDE), low),
        ((8, 32, WIDE), low),
        ((ROWS, WIDE), low),
        ((ROWS, WIDE), low),
        ((2, WIDE, ROWS), low),
        ((3, ROWS, WIDE), low),
        ((3, ROWS, WIDE), low),
        ((ROWS, WIDE), low),
        ((2, WIDE, KEYS), low),
        ((4, 2, TEXT, KEYS), low),
        ((8, 32, 128), low),
        ((8, MOD), full),
        ((4, ROWS, WIDE), low),
        ((4, ROWS, 128), full),
        ((2, ROWS, WIDE), low),
        ((ROWS, WIDE), full),
        ((128, 128), full),
        ((ROWS, WIDE), full),
        ((ROWS, WIDE), low),
        ((16, 16, WIDE), low),
        ((ROWS, WIDE), low),
        ((2, ROWS, WIDE), low),
        ((ROWS, WIDE), low),
        ((5, 8, WIDE), full),
        ((6, 8, WIDE), full),
        ((8, WIDE), full),
        ((BLOCKS, WINDOW, WIDE), low),
        ((ROWS, WIDE), low),
        ((WIDE, WIDE), low),
        ((MOD // 8, WIDE), low),
        ((2, L, 4096), low),
        ((TEXT, 4096), low),
        ((32, 128), low),
        ((TEXT, KEYS), low),
        ((4, SHARD, WIDE), full),
    ]
    return pl.pallas_call(
        forward_kernel,
        out_shape=[jax.ShapeDtypeStruct(*shape) for shape in hbm],
        in_specs=[IN_VMEM] * 14 + [ANY] * 5,
        out_specs=[ANY, IN_VMEM] + [ANY] * 14,
        scratch_shapes=[pltpu.VMEM(*shape) for shape in vmem]
        + [
            dma((BLOCKS, 3)), dma((BLOCKS, 3)), dma((BLOCKS, 7)), dma((BLOCKS, 7)), dma((BLOCKS,)), dma((2,)),
            dma((7,)), dma((7,)), dma((7, 2)), dma((7, 2)), dma((7,)), dma((7,)), dma((4,)), dma((4,)),
            dma((6,)), dma((6,)), dma((SAVE_SEMS,)), dma((5,)),
        ],
        compiler_params=pltpu.CompilerParams(
            collective_id=0, has_side_effects=True, vmem_limit_bytes=60 * MIB
        ),
        name="forward",
    )(*operands)


def tn(left, right):
    return lax.dot_general(
        left, right, (((0,), (0,)), ((), ())), preferred_element_type=jnp.float32
    )


def text_heads_backward(h, query, key, value, grad, dquery, dkey, dvalue, bias, mask):
    jobs = chains(h, VIDEOS)
    scores, grads = [], []
    for (lanes, on), rows, keys in jobs:
        low_on = to_low(on)
        scores.append(linear(query[rows, lanes] * low_on, key[lanes, keys]))
        grads.append(linear(grad[rows, lanes] * low_on, value[lanes, keys]))
    probs = soft(jnp.concatenate(scores), bias, mask)
    grad_probs = jnp.concatenate(grads)
    delta = jnp.sum(grad_probs * probs, axis=-1, keepdims=True)
    slopes = split_rows(to_low(probs * (grad_probs - delta)), jobs)
    probs = split_rows(to_low(probs), jobs)
    parts = []
    for slope, prob, ((lanes, on), rows, keys) in zip(slopes, probs, jobs):
        low_on = to_low(on)
        parts.append(
            (
                to_low(nt(slope, key[lanes, keys]) * (on * SCALE)),
                to_low(tn(query[rows, lanes] * low_on, slope) * SCALE),
                to_low(tn(grad[rows, lanes] * low_on, prob)),
            )
        )
    for (by_query, by_key, by_value), ((lanes, on), rows, keys) in zip(parts, jobs):
        dquery[rows, lanes] = dquery[rows, lanes] + by_query
        dkey[lanes, keys] = dkey[lanes, keys] + by_key
        dvalue[lanes, keys] = dvalue[lanes, keys] + by_value


def heads_backward(h, query, key, value, grad, dquery, dkey, dvalue, groups, bias, mask):
    jobs = chains(h, groups)
    scores, grads = [], []
    for (lanes, on), rows, keys in jobs:
        low_on = to_low(on)
        scores.append(nt(query[rows, lanes] * low_on, key[keys, lanes]))
        grads.append(nt(grad[rows, lanes] * low_on, value[keys, lanes]))
    probs = soft(jnp.concatenate(scores), bias, mask)
    grad_probs = jnp.concatenate(grads)
    delta = jnp.sum(grad_probs * probs, axis=-1, keepdims=True)
    slopes = split_rows(to_low(probs * (grad_probs - delta)), jobs)
    probs = split_rows(to_low(probs), jobs)
    parts = []
    for slope, prob, ((lanes, on), rows, keys) in zip(slopes, probs, jobs):
        parts.append(
            (
                to_low(linear(slope, key[keys, lanes]) * (on * SCALE)),
                to_low(tn(slope, query[rows, lanes]) * (on * SCALE)),
                to_low(tn(prob, grad[rows, lanes]) * on),
            )
        )
    for (by_query, by_key, by_value), ((lanes, on), rows, keys) in zip(parts, jobs):
        dquery[rows, lanes] = dquery[rows, lanes] + by_query
        dkey[keys, lanes] = dkey[keys, lanes] + by_key
        dvalue[keys, lanes] = dvalue[keys, lanes] + by_value


def backward_kernel(
    wide, left_i, qkvs_i, qkvt_i, qc_i, mem_i, xhat_i, rstd_i, branch_i, slope_i, gfour_i, cot_i, mods_i, gate_i, gain_i,
    caption_i, seg_in, seg_row, turn, cond_in,
    total, gtok, gain_o, caption_o, mod_o,
    weights, left, right, qkv, xhat, rstd, branch, slope, mods, gain, bias, stream, work, grad, xin, gm, mem, dmem, text, text_at, text_sum, cap, cap_out, cap_in, cap_own, cap_at, mod_out, mod,
    seqs, gains, gain_at, gframe, back,
    s0, r0, s1, r1, s2, r2, k2, s3, pass_in, pass_out, far_in, close, close_in, share,
    in_sem, w_sem, s0_sem, r0_sem, s1_sem, r1_sem, s2_sem, r2_sem, z_send, z_recv, share_sem,
    a_send, a_recv, u_send, u_recv, x_send, x_recv, m_send, m_recv, q_send, q_recv, g_send, g_recv,
    cap_sem, c_send, c_recv, left_sem,
):
    x, c, y, z, x1, y1, x2, y2 = place()
    b = z * 2 + y
    near = [device(x, c, y, (z + k) % 4) for k in (1, 2, 3)]
    first, second, twin = device(x1, c, y1, z), device(x2, c, y2, z), device(x, 1 - c, y, z)
    peers = blk_peers(x, c, b)
    across = [twin, device(1 - x, c, y, z), device(1 - x, 1 - c, y, z)]
    greet(peers + across)

    fetches = {}

    def fetch(name, from_ref, to_ref):
        fetches[name] = pltpu.make_async_copy(from_ref, to_ref, in_sem.at[name])
        fetches[name].start()

    def have(name):
        if name in fetches:
            fetches.pop(name).wait()

    fetch(0, gfour_i, right.at[0])
    for k in range(4):
        fetch(1 + k, left_i.at[k], left.at[k])
    fetch(12, mods_i, mods)
    fetch(13, gain_i, gain)
    fetch(14, slope_i.at[0], slope.at[0])
    fetch(15, slope_i.at[1], slope.at[1])
    fetch(16, xhat_i.at[3], xhat.at[1])
    fetch(17, rstd_i.at[3], rstd.at[1])
    fetch(18, cot_i, xin)
    fetch(19, gate_i, work.at[0:8])

    def weight(block):
        slot = WEIGHT_ORDER.index(block) % 2
        return weights.at[slot]

    def prefetch(at):
        if at < len(WEIGHT_ORDER):
            copy = pltpu.make_async_copy(wide.at[WEIGHT_ORDER[at]], weights.at[at % 2], w_sem.at[at % 2])
            copy.start()
            fetches["w", WEIGHT_ORDER[at]] = copy

    def release(block):
        prefetch(WEIGHT_ORDER.index(block) + 2)

    prefetch(0)
    prefetch(1)

    away = [(1 - x) * 2 + 1 - y, x2 * 2 + y2]
    stay = [x1 * 2 + y1, x * 2 + y]

    def product(t, core, xl):
        rows = pl.ds(pl.multiple_of(line_of(core, xl, 0) * LINE, 16), 2 * LINE)
        return linear(left[left_at(t) % 4, rows, :], right[right_at(t)])

    def left_copy(t):
        return pltpu.make_async_copy(left_i.at[left_at(t)], left.at[left_at(t) % 4], left_sem.at[0])

    def left_next(t):
        return (t >= 4) & (t < BLOCKS) & (left_at(t) != left_at(t - 1))

    def copy0(t, l):
        pair = pl.ds(2 * l, 2)
        return remote(s0.at[t % 2, pair], r0.at[t % 4, pair], s0_sem.at[t % 2, l], r0_sem.at[t % 4, l], twin)

    def copy1(t, l):
        return remote(s1.at[t % 2, away[l]], r1.at[t % 4, l], s1_sem.at[t % 2, l], r1_sem.at[t % 4, l], second)

    def copy2(t):
        return remote(s2.at[t % 2], r2.at[t % 4], s2_sem.at[t % 2], r2_sem.at[t % 4], first)

    beside, opposite = device(x, c, y, z + 1 - 2 * (z % 2)), device(x, c, y, 3 - z)
    middle = (z == 1) | (z == 2)
    near_rows = pl.ds(pl.multiple_of(64 * (z // 2), 16), PAIR)
    far_rows = pl.ds(pl.multiple_of(64 - 64 * (z // 2), 16), PAIR)
    own_rows = pl.ds(pl.multiple_of(32 * (z % 2), 16), WINDOW)
    beside_rows = pl.ds(pl.multiple_of(32 - 32 * (z % 2), 16), WINDOW)

    def z_one(t):
        return remote(s3.at[t % 4, far_rows], pass_in.at[t % 4], z_send.at[0, t % 4], z_recv.at[0, t % 4], beside)

    def z_two(t):
        return remote(pass_out.at[t % 2], far_in.at[t % 4], z_send.at[1, t % 4], z_recv.at[1, t % 4], opposite)

    def z_three(t):
        return remote(
            close.at[t % 2, beside_rows], close_in.at[t % 4], z_send.at[2, t % 4], z_recv.at[2, t % 4], beside
        )

    def share_copy(t):
        return pltpu.make_async_copy(share.at[t % 2], total.at[t], share_sem.at[t % 2])

    def tick(t):
        @pl.when(t >= 10)
        def _():
            now = t - 10
            z_three(now).wait_recv()
            value = wide32(close[now % 2, own_rows]) + wide32(close_in[now % 4])

            @pl.when(jnp.logical_not(middle))
            def _():
                z_one(now).wait_send()

            @pl.when(now >= 2)
            def _():
                share_copy(now - 2).wait()
            share[now % 2] = value
            share_copy(now).start()

        @pl.when((t >= 8) & (t < BLOCKS + 8))
        def _():
            now = t - 8

            @pl.when(now >= 2)
            def _():
                z_three(now - 2).wait_send()

            @pl.when(middle)
            def _():
                z_two(now).wait_recv()
                close[now % 2] = to_low(wide32(s3[now % 4, near_rows]) + wide32(far_in[now % 4]))

            @pl.when(jnp.logical_not(middle))
            def _():
                close[now % 2] = s3[now % 4, near_rows]

            z_three(now).start()

        @pl.when((t >= 7) & (t < BLOCKS + 7) & middle)
        def _():
            now = t - 7
            z_one(now).wait_recv()

            @pl.when(now >= 2)
            def _():
                z_two(now - 2).wait_send()
            pass_out[now % 2] = to_low(wide32(s3[now % 4, far_rows]) + wide32(pass_in[now % 4]))
            z_two(now).start()

        @pl.when((t >= 6) & (t < BLOCKS + 6))
        def _():
            now = t - 6
            copy2(now).wait_recv()
            s3[now % 4] = to_low(k2[now % 2] + wide32(r2[now % 4]))

            @pl.when(jnp.logical_not(middle))
            def _():
                z_one(now).start()

        @pl.when((t >= 4) & (t < BLOCKS + 4))
        def _():
            now = t - 4
            copy1(now, 0).wait_recv()

            @pl.when(now >= 2)
            def _():
                copy2(now - 2).wait_send()
            s2[now % 2] = to_low(wide32(s1[now % 2, stay[0]]) + wide32(r1[now % 4, 0]))
            copy2(now).start()
            copy1(now, 1).wait_recv()
            k2[now % 2] = wide32(s1[now % 2, stay[1]]) + wide32(r1[now % 4, 1])

        @pl.when((t >= 2) & (t < BLOCKS + 2))
        def _():
            now = t - 2

            @pl.when(now >= 2)
            def _():
                for l in range(2):
                    copy1(now - 2, l).wait_send()
            for l in range(2):
                copy0(now, l).wait_recv()
                value = product(now, c, l)
                for part in range(2):
                    line = 2 * l + part
                    summed = value[part * LINE : part * LINE + LINE] + wide32(r0[now % 4, line])
                    s1[now % 2, line] = to_low(summed)
            for l in range(2):
                copy1(now, l).start()

        @pl.when(left_next(t))
        def _():
            left_copy(t).wait()

        @pl.when(t < BLOCKS)
        def _():
            for l in range(2):
                @pl.when(t >= 2)
                def _():
                    copy0(t - 2, l).wait_send()
                value = to_low(product(t, 1 - c, l))
                s0[t % 2, 2 * l] = value[:LINE]
                s0[t % 2, 2 * l + 1] = value[LINE:]
                copy0(t, l).start()

        @pl.when(left_next(t + 1))
        def _():
            left_copy(t + 1).start()

    done = [0]

    def pump(until):
        if until > done[0]:
            start = done[0]
            loop(until - start, lambda i: tick(i + start))
            done[0] = until

    def pick(piece, seg):
        lanes = slice(WIDE * piece, WIDE * piece + WIDE)
        return jnp.where(seg > 0.5, mods[1:2, lanes], mods[0:1, lanes])

    def by_video(piece, value, seg):
        lanes = slice(WIDE * piece, WIDE * piece + WIDE)
        later = jnp.sum(value * seg, axis=0, keepdims=True)
        every = jnp.sum(value, axis=0, keepdims=True)
        gm[0:1, lanes] = gm[0:1, lanes] + (every - later)
        gm[1:2, lanes] = gm[1:2, lanes] + later

    def through(values_at, blocks, emit, grouped=False):
        for n, (values, block) in enumerate(zip(values_at, blocks)):
            have(("w", block))

            def tile(cols, n=n, values=values, block=block):
                part = nt(values[...], weight(block)[cols, :])
                if n > 0:
                    part = part + work[:, cols]
                if n == len(blocks) - 1:
                    xin[:, cols] = to_low(part)
                else:
                    work[:, cols] = part

            each_cols(tile)
            release(block)
        if grouped:
            xin[...] = to_low(linear(regroup(True), xin[...]))
        turn_back(emit)

    def turn_back(emit):
        each_cols(lambda cols: emit(cols, linear(xin[...], turn[:, cols])))

    def emit_work(cols, value):
        work[:, cols] = value

    def emit_grad(cols, value):
        grad[:, cols] = to_low(value)

    def norm_back(grad_in, tilt, at, rows):
        slope_in = grad_in * tilt
        hat = wide32(xhat[at, rows, :])
        first_mean = jnp.mean(slope_in, axis=-1, keepdims=True)
        second_mean = jnp.mean(slope_in * hat, axis=-1, keepdims=True)
        return rstd[at, rows, 0:1] * (slope_in - first_mean - hat * second_mean)

    gm[...] = jnp.zeros_like(gm)
    have(0)
    have(12)
    have(18)
    have(19)
    gm[0:8, 8 * WIDE : 9 * WIDE] = work[0:8]
    stream[...] = wide32(xin[...])
    for k in range(4):
        have(1 + k)
    pump(2)
    for k in range(4):
        have(14 + k % 2 if k < 2 else ("slope", k))
        have(("w", 11 + 2 * k))

        def tile(cols, k=k):
            value = nt(right[0], weight(11 + 2 * k)[cols, :]) * wide32(slope[k % 2, :, cols])
            right[1 + k, :, cols] = to_low(value)

        each_cols(tile)
        release(11 + 2 * k)
        if k < 2:
            copy = pltpu.make_async_copy(slope_i.at[k + 2], slope.at[k % 2], in_sem.at[14 + k])
            copy.start()
            fetches["slope", k + 2] = copy
        have(("w", 10 + 2 * k))

        def tile(cols, k=k):
            part = nt(right[1 + k], weight(10 + 2 * k)[cols, :])
            if k > 0:
                part = part + work[:, cols]
            if k < 3:
                work[:, cols] = part
            else:
                xin[:, cols] = to_low(part)

        each_cols(tile)
        release(10 + 2 * k)
        pump(k + 3)
    turn_back(emit_work)
    have(16)
    have(17)
    fetch(20, qc_i, qkv.at[0])
    fetch(21, mem_i.at[0], mem.at[0])
    fetch(22, mem_i.at[1], mem.at[1])
    fetch(23, xhat_i.at[2], xhat.at[0])
    fetch(24, rstd_i.at[2], rstd.at[0])

    def after_mlp(rows):
        seg = seg_in[0, rows, 0:1]
        value = work[rows, :]
        by_video(6, value, seg)
        by_video(7, value * wide32(xhat[1, rows, :]), seg)
        value = stream[rows, :] + norm_back(value, 1.0 + pick(7, seg), 1, rows)
        stream[rows, :] = value
        right[5, rows, :] = to_low(value)

    each_rows(32, after_mlp)

    fetch(25, xhat_i.at[1], xhat.at[1])
    fetch(26, rstd_i.at[1], rstd.at[1])
    through([right.at[5]], [9], emit_grad)
    right[6] = jnp.zeros_like(right[6])
    dmem[...] = jnp.zeros_like(dmem)
    for name in (13, 20, 21, 22, 23, 24):
        have(name)

    def cross_heads(h):
        text_heads_backward(
            h, qkv.at[0], mem.at[0], mem.at[1], grad, right.at[6], dmem.at[0], dmem.at[1],
            cross_bias(), cross_rows(seg_in),
        )

    for part in range(4):
        loop(2, lambda h: cross_heads(h + 2 * part))
        pump(7 + (part + 1) // 2)

    def dmem_part(zp, yp):
        return dmem.at[zp // 2, pl.ds(pl.multiple_of(TEXT * (zp % 2 * 2 + yp), 16), TEXT)]

    def x_over(zp):
        return remote(dmem_part(zp, 1 - y), text.at[zp], x_send.at[zp], x_recv.at[zp], device(x, c, 1 - y, z))

    def x_copy(k):
        return remote(text.at[(z + k) % 4], text_at.at[k - 1], x_send.at[3 + k], x_recv.at[3 + k], near[k - 1])

    for zp in range(4):
        x_over(zp).start()
    fetch(27, qkvt_i.at[0], qkv.at[0])
    fetch(28, qkvt_i.at[1], qkv.at[1])
    fetch(29, qkvt_i.at[2], qkv.at[2])
    fetch(30, branch_i.at[1], branch)
    through([right.at[6]], [8], emit_work)
    gains[0] = jnp.zeros_like(gains[0])
    have(30)

    def after_cross(rows):
        seg = seg_in[0, rows, 0:1]
        value = work[rows, :]
        gains[0, 0:1, :] = gains[0, 0:1, :] + jnp.sum(value * wide32(xhat[0, rows, :]), axis=0, keepdims=True)
        value = stream[rows, :] + norm_back(value, gain[0:1, :], 0, rows)
        stream[rows, :] = value
        by_video(5, value * wide32(branch[rows, :]), seg)
        right[7, rows, :] = to_low(value * pick(5, seg))

    each_rows(32, after_cross)

    def g_copy(at, to):
        return remote(gains.at[min(at, 3)], gain_at.at[at], g_send.at[at], g_recv.at[at], to)

    g_copy(0, twin).start()
    fetch(31, branch_i.at[0], branch)
    fetch(32, xhat_i.at[0], xhat.at[0])
    fetch(33, rstd_i.at[0], rstd.at[0])
    pump(10)

    through([right.at[7]], [7], emit_grad)
    grad[...] = to_low(linear(regroup(False), grad[...]))
    bias[...] = temporal_bias(seg_in, seg_row)
    for j in range(3):
        right[8 + j] = jnp.zeros_like(right[8 + j])
    for name in (25, 26, 27, 28, 29):
        have(name)

    def temporal_heads(h):
        heads_backward(
            h, qkv.at[0], qkv.at[1], qkv.at[2], grad, right.at[8], right.at[9], right.at[10],
            HALVES, jnp.concatenate([bias[...]] * 4), None,
        )

    loop(4, temporal_heads)
    pump(11)
    g_copy(0, twin).wait_recv()
    gains[1] = gains[0] + gain_at[0]
    g_copy(1, first).start()
    loop(4, lambda h: temporal_heads(h + 4))
    pump(12)
    g_copy(1, first).wait_recv()
    gains[2] = gains[1] + gain_at[1]
    g_copy(2, second).start()
    for zp in range(4):
        x_over(zp).wait_recv()
        text[zp] = to_low(wide32(dmem_part(zp, y)[...]) + wide32(text[zp]))
    for k in (1, 2, 3):
        x_copy(k).start()
    for j in range(3):
        fetch(34 + j, qkvs_i.at[j], qkv.at[j])
    through([right.at[8], right.at[9], right.at[10]], [4, 5, 6], emit_work, True)
    have(31)

    def after_temporal(rows):
        seg = seg_in[0, rows, 0:1]
        value = work[rows, :]
        by_video(3, value, seg)
        by_video(4, value * wide32(xhat[1, rows, :]), seg)
        value = stream[rows, :] + norm_back(value, 1.0 + pick(4, seg), 1, rows)
        stream[rows, :] = value
        by_video(2, value * wide32(branch[rows, :]), seg)
        right[1, rows, :] = to_low(value * pick(2, seg))

    each_rows(32, after_temporal)

    through([right.at[1]], [3], emit_grad)

    def a_copy(k):
        to = (b + k) % 8
        part = grad.at[pl.ds(pl.multiple_of(32 * to, 32), 32)]
        return remote(part, back.at[b], a_send.at[k - 1], a_recv.at[k - 1], peers[k - 1])

    def a_wait(k):
        of = (b + 8 - k) % 8
        remote(grad.at[pl.ds(0, 32)], back.at[of], a_send.at[k - 1], a_recv.at[k - 1], peers[k - 1]).wait_recv()

    for k in range(1, 8):
        a_copy(k).start()
    pump(13)
    for k in (1, 2, 3):
        x_copy(k).wait_recv()
    text_sum[...] = to_low(wide32(text[z]) + wide32(text_at[0]) + wide32(text_at[1]) + wide32(text_at[2]))

    def cap_fetch(n):
        quarter = [1 - c, 3 - c, c, 2 + c][n]
        lanes = pl.ds(pl.multiple_of(QUARTER * quarter, 128), QUARTER)
        return pltpu.make_async_copy(caption_i.at[:, :, lanes], cap.at[n % 2], cap_sem.at[n % 2])

    over_x = across[1]
    quarters = [x * 2 + c, (1 - x) * 2 + c, x * 2 + 1 - c, (1 - x) * 2 + 1 - c]

    def c_copy(n):
        from_ref, to_ref, to = (
            (cap_out.at[0], cap_in.at[0], twin),
            (cap_out.at[1], cap_in.at[1], twin),
            (cap_own.at[1 - x], cap_at, over_x),
            (cap_own.at[x], caption_o.at[quarters[0]], over_x),
            (cap_own.at[x], caption_o.at[quarters[0]], twin),
            (caption_o.at[quarters[1]], caption_o.at[quarters[1]], twin),
        )[n]
        return remote(from_ref, to_ref, c_send.at[n], c_recv.at[n], to)

    cap_fetch(0).start()
    cap_fetch(1).start()
    for n in range(4):
        cap_fetch(n).wait()
        part = linear(text_sum[:, 0:L], cap[n % 2, 0]) + linear(text_sum[:, 128 : 128 + L], cap[n % 2, 1])
        if n < 2:
            cap_out[n] = to_low(part)
            c_copy(n).start()
            cap_fetch(n + 2).start()
        else:
            cap_own[n - 2] = to_low(part)
    back[b] = grad[pl.ds(pl.multiple_of(32 * b, 32), 32)]
    pump(14)
    g_copy(2, second).wait_recv()
    gains[3] = gains[2] + gain_at[2]
    for k in (1, 2, 3):
        g_copy(2 + k, near[k - 1]).start()
    for j in range(3):
        right[2 + j] = jnp.zeros_like(right[2 + j])
    for name in (32, 33, 34, 35, 36):
        have(name)
    for k in range(1, 8):
        a_wait(k)
    for k in range(8):
        for f in range(2):
            gframe[128 * f + 16 * k : 128 * f + 16 * k + 16, :] = back[k, 16 * f : 16 * f + 16, :]

    def spatial_heads(h):
        heads_backward(
            h, qkv.at[0], qkv.at[1], qkv.at[2], gframe, right.at[2], right.at[3], right.at[4], HALVES, None, None
        )

    loop(4, spatial_heads)
    pump(15)
    for n in range(2):
        c_copy(n).wait_recv()
        cap_own[n] = to_low(wide32(cap_own[n]) + wide32(cap_in[n]))
    c_copy(2).start()
    loop(4, lambda h: spatial_heads(h + 4))
    pump(16)
    through([right.at[2], right.at[3], right.at[4]], [0, 1, 2], emit_work)
    pump(17)
    for k in range(1, 8):
        a_copy(k).wait_send()

    def after_spatial(i):
        rows = pl.ds(pl.multiple_of(16 * i, 16), 16)
        seg = seg_in[1, rows, 0:1]
        value = work[rows, :]
        by_video(0, value, seg)
        by_video(1, value * wide32(xhat[0, rows, :]), seg)
        value = to_low(norm_back(value, 1.0 + pick(1, seg), 0, rows))
        back[i % 8, pl.ds(pl.multiple_of(16 * (i // 8), 16), 16), :] = value

    loop(16, after_spatial)

    def branch_part(of):
        return branch.at[pl.ds(pl.multiple_of(32 * of, 32), 32)]

    def u_copy(k):
        to = (b + k) % 8
        return remote(back.at[to], branch_part(b), u_send.at[k - 1], u_recv.at[k - 1], peers[k - 1])

    def u_wait(k):
        of = (b + 8 - k) % 8
        remote(back.at[0], branch_part(of), u_send.at[k - 1], u_recv.at[k - 1], peers[k - 1]).wait_recv()

    def m_copy(k):
        to = (b + k) % 8
        return remote(mod_out.at[to], mod.at[b], m_send.at[k - 1], m_recv.at[k - 1], peers[k - 1])

    def m_wait(k):
        of = (b + 8 - k) % 8
        remote(mod_out.at[0], mod.at[of], m_send.at[k - 1], m_recv.at[k - 1], peers[k - 1]).wait_recv()

    for k in range(1, 8):
        u_copy(k).start()
    branch[pl.ds(pl.multiple_of(32 * b, 32), 32), :] = back[b]
    for k in range(8):
        tiles = [
            gm[row : row + 1, 1280 * k + 128 * tile : 1280 * k + 128 * tile + 128]
            for row in range(2)
            for tile in range(MOD_TILES)
        ]
        mod_out[k] = to_low(jnp.concatenate(tiles + [jnp.zeros((32 - 2 * MOD_TILES, 128), jnp.float32)]))
    for k in range(1, 8):
        m_copy(k).start()
    mod[b] = mod_out[b]
    pump(18)
    c_copy(2).wait_recv()
    cap_own[x] = to_low(wide32(cap_own[x]) + wide32(cap_at[...]))
    c_copy(3).start()
    c_copy(4).start()
    keep_quarter = pltpu.make_async_copy(cap_own.at[x], caption_o.at[quarters[0]], cap_sem.at[0])
    keep_quarter.start()
    pump(20)
    for k in range(1, 8):
        m_wait(k)
    summed = wide32(mod[0])
    for k in range(1, 8):
        summed = summed + wide32(mod[k])
    own = x * 2 + c
    seqs[own, 0:32] = to_low(summed)
    seqs[own, 32:64] = cond_in[...]
    places = [x * 2 + 1 - c, (1 - x) * 2 + c, (1 - x) * 2 + 1 - c]

    def q_copy(k, at):
        return remote(seqs.at[own], seqs.at[at], q_send.at[k], q_recv.at[k], across[k])

    for k in range(3):
        q_copy(k, own).start()
    pump(22)
    for k in range(1, 8):
        u_wait(k)
    xin[...] = to_low(stream[...] + wide32(branch[...]))
    gtok[...] = to_low(linear(swap_rows(), xin[...]))
    for k in (1, 2, 3):
        g_copy(2 + k, near[k - 1]).wait_recv()
    gain_o[...] = gains[3] + gain_at[3] + gain_at[4] + gain_at[5]
    pump(24)
    c_copy(3).wait_recv()
    c_copy(5).start()
    pump(BLOCKS + 10)
    c_copy(4).wait_recv()
    c_copy(5).wait_recv()
    for n in range(6):
        c_copy(n).wait_send()
    keep_quarter.wait()
    for k in range(3):
        q_copy(k, places[k]).wait_recv()
    mod_o[...] = seqs[...]

    for now in (BLOCKS - 2, BLOCKS - 1):
        for l in range(2):
            copy0(now, l).wait_send()
            copy1(now, l).wait_send()
        copy2(now).wait_send()
        z_three(now).wait_send()
        share_copy(now).wait()

        @pl.when(middle)
        def _(now=now):
            z_two(now).wait_send()

    for k in range(1, 8):
        u_copy(k).wait_send()
        m_copy(k).wait_send()
        x_over(k - 1).wait_send() if k < 5 else x_copy(k - 4).wait_send()
    for k in range(3):
        q_copy(k, own).wait_send()
    for at, to in enumerate([twin, first, second] + near):
        g_copy(at, to).wait_send()


QUARTER = 1024
WEIGHT_ORDER = (11, 10, 13, 12, 15, 14, 17, 16, 9, 8, 7, 4, 5, 6, 3, 0, 1, 2)


def backward(*operands):
    low, full = jnp.bfloat16, jnp.float32
    dma = pltpu.SemaphoreType.DMA
    outs = [
        ((BLOCKS, WINDOW, WIDE), full),
        ((ROWS, WIDE), low),
        ((8, WIDE), full),
        ((4, TEXT, QUARTER), low),
        ((4, 64, 128), low),
    ]
    vmem = [
        ((2, WIDE, WIDE), low),
        ((4, WIDE, ROWS), low),
        ((11, ROWS, WIDE), low),
        ((3, ROWS, WIDE), low),
        ((2, ROWS, WIDE), low),
        ((2, ROWS, 128), full),
        ((ROWS, WIDE), low),
        ((2, ROWS, WIDE), low),
        ((8, MOD), full),
        ((8, WIDE), full),
        ((128, 128), full),
        ((ROWS, WIDE), full),
        ((ROWS, WIDE), full),
        ((ROWS, WIDE), low),
        ((ROWS, WIDE), low),
        ((8, MOD), full),
        ((2, WIDE, KEYS), low),
        ((2, WIDE, KEYS), low),
        ((4, TEXT, KEYS), low),
        ((3, TEXT, KEYS), low),
        ((TEXT, KEYS), low),
        ((2, 2, L, QUARTER), low),
        ((2, TEXT, QUARTER), low),
        ((2, TEXT, QUARTER), low),
        ((2, TEXT, QUARTER), low),
        ((TEXT, QUARTER), low),
        ((8, 32, 128), low),
        ((8, 32, 128), low),
        ((4, 64, 128), low),
        ((4, 8, WIDE), full),
        ((6, 8, WIDE), full),
        ((ROWS, WIDE), low),
        ((8, 32, WIDE), low),
        ((2, 4, LINE, WIDE), low),
        ((4, 4, LINE, WIDE), low),
        ((2, 4, LINE, WIDE), low),
        ((4, 2, LINE, WIDE), low),
        ((2, LINE, WIDE), low),
        ((4, LINE, WIDE), low),
        ((2, LINE, WIDE), full),
        ((4, LINE, WIDE), low),
        ((4, PAIR, WIDE), low),
        ((2, PAIR, WIDE), low),
        ((4, PAIR, WIDE), low),
        ((2, PAIR, WIDE), low),
        ((4, WINDOW, WIDE), low),
        ((2, WINDOW, WIDE), full),
    ]
    return pl.pallas_call(
        backward_kernel,
        out_shape=[jax.ShapeDtypeStruct(*shape) for shape in outs],
        in_specs=[ANY] * 16 + [IN_VMEM] * 4,
        out_specs=[ANY] + [IN_VMEM] * 2 + [ANY, IN_VMEM],
        scratch_shapes=[pltpu.VMEM(*shape) for shape in vmem]
        + [
            dma((40,)), dma((2,)), dma((2, 4)), dma((4, 4)), dma((2, 2)), dma((4, 2)), dma((2,)), dma((4,)),
            dma((3, 4)), dma((3, 4)), dma((2,)), dma((7,)), dma((7,)), dma((7,)), dma((7,)), dma((7,)), dma((7,)),
            dma((7,)), dma((7,)), dma((3,)), dma((3,)), dma((6,)), dma((6,)), dma((2,)), dma((6,)), dma((6,)), dma((1,)),
        ],
        compiler_params=pltpu.CompilerParams(
            collective_id=1, has_side_effects=True, vmem_limit_bytes=63 * MIB
        ),
        name="backward",
    )(*operands)


def finish_kernel(
    spread, caption_in, mod_in, gain_in,
    ada_o, bias_o, spatial_o, spatial_out_o, temporal_o, temporal_out_o, gain_o, query_o, caption_o, cross_o, hidden_o,
    hidden_out_o,
):
    seq, blk = lax.axis_index("seq"), lax.axis_index("blk")

    def share(t):
        return pltpu.roll(spread[t], (WINDOW - 4 * (blk // 2)) % WINDOW, 0)[0:SHARD]

    for j in range(3):
        lanes = slice(WIDE * j, WIDE * j + WIDE)
        spatial_o[:, lanes] = share(15 + j)
        temporal_o[:, lanes] = share(11 + j)
    spatial_out_o[...] = share(14)
    temporal_out_o[...] = share(10)
    query_o[...] = share(9)
    cross_o[...] = share(8)
    hidden = [share(4 + k) for k in range(4)]
    hidden_o[...] = jnp.zeros_like(hidden_o)
    for k, natural, placed in hidden_places():
        move_lanes(hidden_o, hidden[k], placed, natural, 4 * WIDE)
    for k in range(4):
        hidden_out_o[SHARD * k : SHARD * k + SHARD, :] = share(k)
    gain_o[...] = pltpu.roll(gain_in[...], (WIDE - SHARD * (seq * 8 + blk)) % WIDE, 1)[0:1, 0:SHARD]
    for q in range(4):
        caption_o[:, QUARTER * q : QUARTER * q + QUARTER] = wide32(caption_in[q])
    part = MOD // 8
    mods, conds = [], []
    for pack in range(4):
        rows = wide32(mod_in[pack])
        for video in range(2):
            first = MOD_TILES * video
            mods.append(jnp.concatenate([rows[first + i : first + i + 1] for i in range(MOD_TILES)], axis=1))
            first = 32 + WIDE // 128 * video
            conds.append(jnp.concatenate([rows[first + i : first + i + 1] for i in range(WIDE // 128)], axis=1))
    mods = pltpu.roll(jnp.concatenate(mods), (MOD_WIN - 16 * blk) % MOD_WIN, 1)[:, :part]
    bias_o[...] = jnp.sum(mods, axis=0, keepdims=True)
    ada_o[...] = tn(to_low(mods), to_low(jnp.concatenate(conds)))


def finish(spread, caption, mod, gain):
    full = jnp.float32
    outs = [
        (MOD // 8, WIDE), (1, MOD // 8), (SHARD, 3 * WIDE), (SHARD, WIDE), (SHARD, 3 * WIDE), (SHARD, WIDE),
        (1, SHARD), (SHARD, WIDE), (TEXT, 4 * QUARTER), (SHARD, WIDE), (SHARD, 4 * WIDE), (4 * SHARD, WIDE),
    ]
    return pl.pallas_call(
        finish_kernel,
        out_shape=[jax.ShapeDtypeStruct(shape, full) for shape in outs],
        in_specs=[IN_VMEM] * 4,
        out_specs=[IN_VMEM] * len(outs),
        compiler_params=pltpu.CompilerParams(vmem_limit_bytes=60 * MIB),
        name="finish",
    )(spread, caption, mod, gain)


TURN = np.arange(WIDE)[None, :] == (
    np.arange(WIDE).reshape(2, 2, 4, 2, SHARD).transpose(1, 0, 3, 2, 4).reshape(-1)
)[:, None]


def shards(
    tokens,
    segments,
    timesteps,
    caption,
    cotangent,
    ada_weight,
    ada_bias,
    spatial_in,
    spatial_out,
    temporal_in,
    temporal_out,
    cross_gain,
    cross_query,
    caption_proj,
    cross_out,
    hidden_in,
    hidden_out,
):
    frame_seg = segments[0]
    blk = lax.axis_index("blk")
    conditioning = to_low(jax.nn.silu(time_embedding(timesteps[0], WIDE)))
    cond_in = jnp.pad(conditioning.reshape(2 * WIDE // 128, 128), ((0, 32 - 2 * WIDE // 128), (0, 0)))
    frames = frame_seg.astype(jnp.float32)
    own_frames = lax.dynamic_slice(frames, (2 * blk,), (2,))
    seg_in = jnp.broadcast_to(
        jnp.stack(
            [jnp.repeat(frames, 16), jnp.repeat(own_frames, 128), jnp.tile(jnp.repeat(frames, 8), 2)]
        )[:, :, None],
        (3, ROWS, 128),
    )
    seg_row = jnp.broadcast_to(jnp.repeat(frames, 8)[None], (8, 128))
    turn = jnp.asarray(TURN, jnp.bfloat16)
    wide, out, *kept = forward(
        spatial_in,
        spatial_out,
        temporal_in,
        temporal_out,
        cross_query,
        cross_out,
        hidden_in,
        hidden_out,
        tokens.reshape(ROWS, WIDE),
        jnp.pad(cross_gain[None], ((0, 7), (0, 0))),
        jnp.pad(conditioning, ((0, 14), (0, 0))),
        ada_bias[None],
        seg_in,
        seg_row,
        cotangent.reshape(ROWS, WIDE),
        turn,
        ada_weight.T,
        caption[0],
        caption_proj.T,
    )
    spread, grad_tokens, grad_gain, grad_text, grad_mod = backward(
        wide, *kept, caption[0], seg_in, seg_row, turn, cond_in
    )
    (
        grad_ada,
        grad_bias,
        grad_sin,
        grad_sout,
        grad_tin,
        grad_tout,
        grad_gain,
        grad_query,
        grad_caption,
        grad_cout,
        grad_hin,
        grad_hout,
    ) = finish(spread, grad_text, grad_mod, grad_gain)
    return (
        out.reshape(tokens.shape),
        grad_tokens.reshape(tokens.shape),
        grad_ada.T,
        grad_bias[0],
        grad_sin,
        grad_sout,
        grad_tin,
        grad_tout,
        grad_gain[0],
        grad_query,
        grad_caption.T,
        grad_cout,
        grad_hin,
        grad_hout,
    )


def solution(mesh):
    fast = dict(mesh.shape) == {"seq": 4, "blk": 8}
    return jax.shard_map(
        shards if fast else general_shards,
        mesh=mesh,
        in_specs=(
            P("seq", "blk", None, None),
            P("seq", None),
            P("seq", None),
            P("seq", None, None, None),
            P("seq", "blk", None, None),
            P(None, "blk"),
            P("blk"),
            P(("seq", "blk"), None),
            P(("seq", "blk"), None),
            P(("seq", "blk"), None),
            P(("seq", "blk"), None),
            P(("seq", "blk")),
            P(("seq", "blk"), None),
            P(None, "blk"),
            P(("seq", "blk"), None),
            P(("seq", "blk"), None),
            P(("seq", "blk"), None),
        ),
        out_specs=(
            P("seq", "blk", None, None),
            P("seq", "blk", None, None),
            P(None, "blk"),
            P("blk"),
            P(("seq", "blk"), None),
            P(("seq", "blk"), None),
            P(("seq", "blk"), None),
            P(("seq", "blk"), None),
            P(("seq", "blk")),
            P(("seq", "blk"), None),
            P(None, "blk"),
            P(("seq", "blk"), None),
            P(("seq", "blk"), None),
            P(("seq", "blk"), None),
        ),
        check_vma=False,
    )
```

```python
import math

import jax
import jax.numpy as jnp
import numpy as np
from jax import lax
from jax.experimental import pallas as pl
from jax.experimental.pallas import tpu as pltpu
from jax.sharding import PartitionSpec as P

H = 16
E = 72
L = 120


EPSILON = 1e-06
MASKED = -1e30


def to_low(values):
    return values.astype(jnp.bfloat16)


def linear(left, right):
    return jnp.dot(left, right, preferred_element_type=jnp.float32)


def left_product(left, right):
    return lax.dot_general(
        left, right, (((0,), (0,)), ((), ())), preferred_element_type=jnp.float32
    )


def right_product(left, right):
    return lax.dot_general(
        left, right, (((1,), (1,)), ((), ())), preferred_element_type=jnp.float32
    )


def normalize(values):
    center = values - jnp.mean(values, axis=-1, keepdims=True)
    return center * lax.rsqrt(jnp.mean(center * center, axis=-1, keepdims=True) + EPSILON)


def modulate(values, shift_rows, scale_rows):
    return normalize(values) * (1.0 + scale_rows) + shift_rows


def gain_norm(values, gain_row):
    return normalize(values) * gain_row


def gelu_tanh(values):
    return jax.nn.gelu(values, approximate=True)


def softmax_rows(scores):
    shifted = jnp.exp(scores - jnp.max(scores, axis=-1, keepdims=True))
    return shifted / jnp.sum(shifted, axis=-1, keepdims=True)


def softmax_with_total(scores):
    top = jnp.max(scores, axis=-1, keepdims=True)
    shifted = jnp.exp(scores - top)
    total = jnp.sum(shifted, axis=-1, keepdims=True)
    return (shifted / total, (top + jnp.log(total))[..., 0])


def softmax_back(probs, grad_probs):
    return probs * (grad_probs - jnp.sum(grad_probs * probs, axis=-1, keepdims=True))


def time_embedding(step_ids, model_width):
    half_width = model_width // 2
    frequency = jnp.exp(
        -math.log(10000.0) * jnp.arange(half_width).astype(jnp.float32) / half_width
    )
    angles = step_ids.astype(jnp.float32)[:, None] * frequency[None, :]
    return jnp.concatenate([jnp.cos(angles), jnp.sin(angles)], axis=1)


def general_shards(
    tokens,
    segments,
    timesteps,
    caption,
    cotangent,
    ada_weight,
    ada_bias,
    spatial_in,
    spatial_out,
    temporal_in,
    temporal_out,
    cross_gain,
    cross_query,
    caption_proj,
    cross_out,
    hidden_in,
    hidden_out,
):
    inputs = tokens[0].astype(jnp.float32)
    patch_dev, frames, model_width = inputs.shape
    token_rows = patch_dev * frames
    head_count = H
    head_size = E
    score_scale = E ** (-0.5)
    frame_seg = segments[0]
    step_ids = timesteps[0]
    seg_count, text_len, text_width = caption.shape[1:]
    text_keys = seg_count * text_len
    caption_rows = caption[0].reshape(text_keys, text_width)
    grad_out = cotangent[0].astype(jnp.float32)
    gathered = (
        lax.all_gather(spatial_in, ("seq", "blk"), axis=0, tiled=True),
        lax.all_gather(spatial_out, ("seq", "blk"), axis=0, tiled=True),
        lax.all_gather(temporal_in, ("seq", "blk"), axis=0, tiled=True),
        lax.all_gather(temporal_out, ("seq", "blk"), axis=0, tiled=True),
        lax.all_gather(cross_gain, ("seq", "blk"), axis=0, tiled=True),
        lax.all_gather(cross_query, ("seq", "blk"), axis=0, tiled=True),
        lax.all_gather(cross_out, ("seq", "blk"), axis=0, tiled=True),
        lax.all_gather(hidden_in, ("seq", "blk"), axis=0, tiled=True),
        lax.all_gather(hidden_out, ("seq", "blk"), axis=0, tiled=True),
    )
    (
        wide_sin,
        wide_sout,
        wide_tin,
        wide_tout,
        gain_low,
        wide_query,
        wide_cout,
        wide_hin,
        wide_hout,
    ) = gathered
    gain_row = gain_low.astype(jnp.float32)
    conditioning = to_low(jax.nn.silu(time_embedding(step_ids, model_width)))
    mod_part = to_low(linear(conditioning, ada_weight) + ada_bias.astype(jnp.float32))
    text_part = to_low(linear(caption_rows, caption_proj))
    modulation, memory = (
        lax.all_gather(mod_part, "blk", axis=1, tiled=True),
        lax.all_gather(text_part, "blk", axis=1, tiled=True),
    )
    choose = frame_seg[:, None] == jnp.arange(seg_count, dtype=jnp.int32)[None, :]
    frame_mod = linear(choose.astype(jnp.bfloat16), modulation)
    pieces = [frame_mod[:, index * model_width : (index + 1) * model_width] for index in range(9)]
    (
        shift_one,
        scale_one,
        gate_one,
        shift_two,
        scale_two,
        gate_two,
        shift_three,
        scale_three,
        gate_three,
    ) = pieces
    spatial_input = to_low(modulate(inputs, shift_one, scale_one)).reshape(token_rows, model_width)
    spatial_qkv = to_low(linear(spatial_input, wide_sin)).reshape(
        patch_dev, frames, 3 * model_width
    )
    query_s = spatial_qkv[..., :model_width].reshape(patch_dev, frames, head_count, head_size)
    local_kv = spatial_qkv[..., model_width:]
    whole_kv = lax.all_gather(local_kv, "blk", axis=0, tiled=True)

    def split_kv(both):
        count = both.shape[0]
        return (
            both[..., :model_width].reshape(count, frames, head_count, head_size),
            both[..., model_width:].reshape(count, frames, head_count, head_size),
        )

    def spatial_probs(key_all):
        scores = jnp.einsum("pfhe,qfhe->fhpq", query_s, key_all, preferred_element_type=jnp.float32)
        return softmax_with_total(scores * score_scale)

    key_s, value_s = split_kv(whole_kv)
    probs_s, log_total_s = spatial_probs(key_s)
    probs_s_low = to_low(probs_s)
    attn_s = to_low(
        jnp.einsum(
            "fhpq,qfhe->pfhe", probs_s_low, value_s, preferred_element_type=jnp.float32
        ).reshape(token_rows, model_width)
    )
    branch_s = linear(attn_s, wide_sout).reshape(patch_dev, frames, model_width)
    after_one = inputs + gate_one * branch_s
    temporal_input = to_low(modulate(after_one, shift_two, scale_two)).reshape(
        token_rows, model_width
    )
    temporal_qkv = to_low(linear(temporal_input, wide_tin)).reshape(
        patch_dev, frames, 3, head_count, head_size
    )
    query_t = temporal_qkv[:, :, 0]
    key_t = temporal_qkv[:, :, 1]
    value_t = temporal_qkv[:, :, 2]
    same_seg = frame_seg[:, None] == frame_seg[None, :]
    scores_t = (
        jnp.einsum("pfhe,pghe->phfg", query_t, key_t, preferred_element_type=jnp.float32)
        * score_scale
    )
    probs_t = softmax_rows(jnp.where(same_seg[None, None], scores_t, MASKED))
    probs_t_low = to_low(probs_t)
    attn_t = to_low(
        jnp.einsum(
            "phfg,pghe->pfhe", probs_t_low, value_t, preferred_element_type=jnp.float32
        ).reshape(token_rows, model_width)
    )
    branch_t = linear(attn_t, wide_tout).reshape(patch_dev, frames, model_width)
    after_two = after_one + gate_two * branch_t
    cross_input = to_low(gain_norm(after_two, gain_row)).reshape(token_rows, model_width)
    query_c = to_low(linear(cross_input, wide_query)).reshape(
        patch_dev, frames, head_count, head_size
    )
    key_c = memory[:, :model_width].reshape(text_keys, head_count, head_size)
    value_c = memory[:, model_width:].reshape(text_keys, head_count, head_size)
    key_seg = jnp.arange(text_keys, dtype=jnp.int32) // text_len
    allowed = frame_seg[:, None] == key_seg[None, :]
    scores_c = (
        jnp.einsum("pfhe,khe->pfhk", query_c, key_c, preferred_element_type=jnp.float32)
        * score_scale
    )
    probs_c = softmax_rows(jnp.where(allowed[None, :, None, :], scores_c, MASKED))
    probs_c_low = to_low(probs_c)
    attn_c = to_low(
        jnp.einsum(
            "pfhk,khe->pfhe", probs_c_low, value_c, preferred_element_type=jnp.float32
        ).reshape(token_rows, model_width)
    )
    branch_c = linear(attn_c, wide_cout).reshape(patch_dev, frames, model_width)
    after_three = after_two + branch_c
    mlp_input = to_low(modulate(after_three, shift_three, scale_three)).reshape(
        token_rows, model_width
    )
    pre_act = linear(mlp_input, wide_hin)
    post_act = to_low(gelu_tanh(pre_act))
    branch_m = linear(post_act, wide_hout).reshape(patch_dev, frames, model_width)
    result = after_three + gate_three * branch_m
    grad_gate_three = jnp.sum(grad_out * branch_m, axis=0)
    grad_four = to_low(grad_out * gate_three).reshape(token_rows, model_width)
    grad_hout = left_product(post_act, grad_four)
    grad_post = right_product(grad_four, wide_hout)
    gelu_pull = jax.vjp(gelu_tanh, pre_act)[1]
    grad_pre = to_low(gelu_pull(grad_post)[0])
    grad_hin = left_product(mlp_input, grad_pre)
    grad_mlp_in = right_product(grad_pre, wide_hin).reshape(patch_dev, frames, model_width)
    mlp_pull = jax.vjp(modulate, after_three, shift_three, scale_three)[1]
    back_three, grad_shift_three, grad_scale_three = mlp_pull(grad_mlp_in)
    grad_three = grad_out + back_three
    grad_cross_branch = to_low(grad_three).reshape(token_rows, model_width)
    grad_cout = left_product(attn_c, grad_cross_branch)
    grad_attn_c = to_low(right_product(grad_cross_branch, wide_cout)).reshape(
        patch_dev, frames, head_count, head_size
    )
    grad_probs_c = jnp.einsum(
        "pfhe,khe->pfhk", grad_attn_c, value_c, preferred_element_type=jnp.float32
    )
    grad_scores_c = to_low(softmax_back(probs_c, grad_probs_c))
    grad_query_c = to_low(
        jnp.einsum("pfhk,khe->pfhe", grad_scores_c, key_c, preferred_element_type=jnp.float32)
        * score_scale
    ).reshape(token_rows, model_width)
    grad_key_c = (
        jnp.einsum("pfhk,pfhe->khe", grad_scores_c, query_c, preferred_element_type=jnp.float32)
        * score_scale
    )
    grad_value_c = jnp.einsum(
        "pfhk,pfhe->khe", probs_c_low, grad_attn_c, preferred_element_type=jnp.float32
    )
    grad_memory = jnp.concatenate(
        [grad_key_c.reshape(text_keys, model_width), grad_value_c.reshape(text_keys, model_width)],
        axis=1,
    )
    grad_wquery = left_product(cross_input, grad_query_c)
    grad_cross_in = right_product(grad_query_c, wide_query).reshape(patch_dev, frames, model_width)
    cross_pull = jax.vjp(gain_norm, after_two, gain_row)[1]
    back_two, grad_gain = cross_pull(grad_cross_in)
    grad_two = grad_three + back_two
    grad_gate_two = jnp.sum(grad_two * branch_t, axis=0)
    grad_temporal_branch = to_low(grad_two * gate_two).reshape(token_rows, model_width)
    grad_tout = left_product(attn_t, grad_temporal_branch)
    grad_attn_t = to_low(right_product(grad_temporal_branch, wide_tout)).reshape(
        patch_dev, frames, head_count, head_size
    )
    grad_probs_t = jnp.einsum(
        "pfhe,pghe->phfg", grad_attn_t, value_t, preferred_element_type=jnp.float32
    )
    grad_scores_t = to_low(softmax_back(probs_t, grad_probs_t))
    grad_query_t = (
        jnp.einsum("phfg,pghe->pfhe", grad_scores_t, key_t, preferred_element_type=jnp.float32)
        * score_scale
    )
    grad_key_t = (
        jnp.einsum("phfg,pfhe->pghe", grad_scores_t, query_t, preferred_element_type=jnp.float32)
        * score_scale
    )
    grad_value_t = jnp.einsum(
        "phfg,pfhe->pghe", probs_t_low, grad_attn_t, preferred_element_type=jnp.float32
    )
    grad_qkv_t = to_low(jnp.stack([grad_query_t, grad_key_t, grad_value_t], axis=2)).reshape(
        token_rows, 3 * model_width
    )
    grad_tin = left_product(temporal_input, grad_qkv_t)
    grad_temporal_in = right_product(grad_qkv_t, wide_tin).reshape(patch_dev, frames, model_width)
    temporal_pull = jax.vjp(modulate, after_one, shift_two, scale_two)[1]
    back_one, grad_shift_two, grad_scale_two = temporal_pull(grad_temporal_in)
    grad_one = grad_two + back_one
    grad_gate_one = jnp.sum(grad_one * branch_s, axis=0)
    grad_spatial_branch = to_low(grad_one * gate_one).reshape(token_rows, model_width)
    grad_sout = left_product(attn_s, grad_spatial_branch)
    grad_attn_s = to_low(right_product(grad_spatial_branch, wide_sout)).reshape(
        patch_dev, frames, head_count, head_size
    )
    back_kv = lax.all_gather(local_kv, "blk", axis=0, tiled=True)
    back_key, back_value = split_kv(back_kv)
    back_probs = spatial_probs(back_key)[0]
    back_probs_low = to_low(back_probs)
    grad_probs_s = jnp.einsum(
        "pfhe,qfhe->fhpq", grad_attn_s, back_value, preferred_element_type=jnp.float32
    )
    row_delta = jnp.sum(grad_probs_s * back_probs, axis=-1, keepdims=True)
    grad_scores_s = to_low(back_probs * (grad_probs_s - row_delta))
    grad_query_s = (
        jnp.einsum("fhpq,qfhe->pfhe", grad_scores_s, back_key, preferred_element_type=jnp.float32)
        * score_scale
    )
    count = lax.axis_size("blk") * patch_dev
    grad_key = (
        jnp.einsum("fhpq,pfhe->qfhe", grad_scores_s, query_s, preferred_element_type=jnp.float32)
        * score_scale
    )
    grad_value = jnp.einsum(
        "fhpq,pfhe->qfhe", back_probs_low, grad_attn_s, preferred_element_type=jnp.float32
    )
    grad_kv = to_low(
        lax.psum_scatter(
            jnp.concatenate(
                [
                    grad_key.reshape(count, frames, model_width),
                    grad_value.reshape(count, frames, model_width),
                ],
                axis=2,
            ).astype(jnp.bfloat16),
            "blk",
            scatter_dimension=0,
            tiled=True,
        ).astype(jnp.float32)
    )
    grad_qkv_s = jnp.concatenate(
        [to_low(grad_query_s).reshape(patch_dev, frames, model_width), grad_kv], axis=2
    ).reshape(token_rows, 3 * model_width)
    grad_sin = left_product(spatial_input, grad_qkv_s)
    grad_spatial_in = right_product(grad_qkv_s, wide_sin).reshape(patch_dev, frames, model_width)
    spatial_pull = jax.vjp(modulate, inputs, shift_one, scale_one)[1]
    back_zero, grad_shift_one, grad_scale_one = spatial_pull(grad_spatial_in)
    grad_input = grad_one + back_zero
    grad_frame_mod = jnp.concatenate(
        [
            grad_shift_one,
            grad_scale_one,
            grad_gate_one,
            grad_shift_two,
            grad_scale_two,
            grad_gate_two,
            grad_shift_three,
            grad_scale_three,
            grad_gate_three,
        ],
        axis=1,
    )
    grad_mod_local = lax.dot_general(
        choose.astype(jnp.float32),
        grad_frame_mod,
        (((0,), (0,)), ((), ())),
        precision=lax.Precision.HIGHEST,
    )
    grad_mod_part, grad_memory_part = (
        lax.psum_scatter(
            grad_mod_local.astype(jnp.bfloat16), "blk", scatter_dimension=1, tiled=True
        ).astype(jnp.float32),
        lax.psum_scatter(
            grad_memory.astype(jnp.bfloat16), "blk", scatter_dimension=1, tiled=True
        ).astype(jnp.float32),
    )
    grad_mod_low = to_low(grad_mod_part)
    grad_ada_w = left_product(conditioning, grad_mod_low)
    grad_ada_b = jnp.sum(grad_mod_low.astype(jnp.float32), axis=0)
    grad_caption = left_product(caption_rows, to_low(grad_memory_part))
    grad_ada_w, grad_ada_b, grad_caption = (
        lax.psum(grad_ada_w.astype(jnp.bfloat16), "seq").astype(jnp.float32),
        lax.psum(grad_ada_b.astype(jnp.bfloat16), "seq").astype(jnp.float32),
        lax.psum(grad_caption.astype(jnp.bfloat16), "seq").astype(jnp.float32),
    )
    shares = (
        lax.psum_scatter(grad_sin, ("seq", "blk"), scatter_dimension=0, tiled=True),
        lax.psum_scatter(grad_sout, ("seq", "blk"), scatter_dimension=0, tiled=True),
        lax.psum_scatter(grad_tin, ("seq", "blk"), scatter_dimension=0, tiled=True),
        lax.psum_scatter(grad_tout, ("seq", "blk"), scatter_dimension=0, tiled=True),
        lax.psum_scatter(grad_gain, ("seq", "blk"), scatter_dimension=0, tiled=True),
        lax.psum_scatter(grad_wquery, ("seq", "blk"), scatter_dimension=0, tiled=True),
        lax.psum_scatter(grad_cout, ("seq", "blk"), scatter_dimension=0, tiled=True),
        lax.psum_scatter(grad_hin, ("seq", "blk"), scatter_dimension=0, tiled=True),
        lax.psum_scatter(grad_hout, ("seq", "blk"), scatter_dimension=0, tiled=True),
    )
    (
        share_sin,
        share_sout,
        share_tin,
        share_tout,
        share_gain,
        share_query,
        share_cout,
        share_hin,
        share_hout,
    ) = shares
    return (
        to_low(result)[None],
        to_low(grad_input)[None],
        grad_ada_w,
        grad_ada_b,
        share_sin,
        share_sout,
        share_tin,
        share_tout,
        share_gain,
        share_query,
        grad_caption,
        share_cout,
        share_hin,
        share_hout,
    )


MESH = pl.DeviceIdType.MESH
BLOCKS = 18
LINES = 8
SHARD = 36
LINE = 4 * SHARD
WINDOW = 48
WIDE = LINES * LINE
MIB = 2**20


def place():
    seq = lax.axis_index("seq")
    blk = lax.axis_index("blk")
    x, c = seq // 2, seq % 2
    z, y = blk // 2, blk % 2
    x1, y1 = x + (1 - 2 * x) * (1 - c), y + (1 - 2 * y) * c
    x2, y2 = x + (1 - 2 * x) * c, y + (1 - 2 * y) * (1 - c)
    return x, c, y, z, x1, y1, x2, y2


def device(x, c, y, z):
    return {"seq": x * 2 + c, "blk": z * 2 + y}


def line_of(c, x, y):
    return (c * 2 + x) * 2 + y


def remote(src, dst, send_sem, recv_sem, where):
    return pltpu.make_async_remote_copy(
        src_ref=src,
        dst_ref=dst,
        send_sem=send_sem,
        recv_sem=recv_sem,
        device_id=where,
        device_id_type=MESH,
    )


def greet(others):
    barrier = pltpu.get_barrier_semaphore()
    for other in others:
        pl.semaphore_signal(barrier, inc=1, device_id=other, device_id_type=MESH)
    pl.semaphore_wait(barrier, len(others))


def left_at(t):
    at = jnp.minimum(t, 4)
    for first in (8, 9, 10, 11, 14, 15):
        at = at + jnp.where(t >= first, 1, 0)
    return at


def right_at(t):
    return jnp.where(t < 14, jnp.maximum(t - 3, 0), t - 13)


ROWS = 256
KEYS = 256
TEXT = 288
MOD = 9 * WIDE
MOD_TILES = 11
MOD_WIN = 128 * MOD_TILES
PARTS, HELD, LAST = 4, 4, 8
PAIR = 80
LEFT_SEM, SLOPE_SEM, SAVE_SEMS = 40, 42, 44
TILE = 384
SCALE = E ** (-0.5)


def nt(left, right):
    return lax.dot_general(
        left, right, (((1,), (1,)), ((), ())), preferred_element_type=jnp.float32
    )


def wide32(values):
    return values.astype(jnp.float32)


def loop(count, body):
    def step(index, carry):
        body(index)
        return carry

    lax.fori_loop(0, count, step, 0)


def each_rows(size, body, total=ROWS):
    loop(total // size, lambda i: body(pl.ds(pl.multiple_of(i * size, size), size)))


def each_cols(body):
    body(slice(0, 2 * TILE))
    body(slice(2 * TILE, 3 * TILE))


def identity(size):
    row = lax.broadcasted_iota(jnp.int32, (size, size), 0)
    col = lax.broadcasted_iota(jnp.int32, (size, size), 1)
    return to_low((row == col).astype(jnp.float32))


def transposed(same, values, to, start):
    for at in range(0, values.shape[1], TILE):
        to[start + at : start + at + TILE, :] = to_low(nt(same, values[:, at : at + TILE]))


def swap_rows():
    row = lax.broadcasted_iota(jnp.int32, (ROWS, ROWS), 0)
    col = lax.broadcasted_iota(jnp.int32, (ROWS, ROWS), 1)
    return to_low((((row & 15) << 4) + (row >> 4) == col).astype(jnp.float32))


def head_window(h):
    base = h * E
    start = jnp.minimum(base // 128, 7) * 128
    lane = lax.broadcasted_iota(jnp.int32, (1, 256), 1)
    on = (lane >= base - start) & (lane < base - start + E)
    return pl.ds(pl.multiple_of(start, 128), 256), on.astype(jnp.float32)


def soft(scores, bias, mask):
    scores = scores * SCALE
    if bias is not None:
        scores = scores + bias
    powers = jnp.exp(scores - jnp.max(scores, axis=-1, keepdims=True))
    probs = powers * (1.0 / jnp.sum(powers, axis=-1, keepdims=True))
    return probs if mask is None else probs * mask


def chains(h, groups, heads=2):
    windows = [head_window(h + H // heads * i) for i in range(heads)]
    return [(window, rows, keys) for window in windows for rows, keys in groups]


def split_rows(values, jobs):
    start = 0
    parts = []
    for _, rows, _ in jobs:
        size = rows.stop - rows.start
        parts.append(values[start : start + size])
        start += size
    return parts


def heads_forward(h, query, key, value, attn, groups, bias, mask):
    jobs = chains(h, groups, 4)
    scores = [nt(query[rows, lanes] * to_low(on), key[keys, lanes]) for (lanes, on), rows, keys in jobs]
    probs = split_rows(to_low(soft(jnp.concatenate(scores), bias, mask)), jobs)
    parts = [linear(prob, value[keys, lanes]) * on for prob, ((lanes, on), rows, keys) in zip(probs, jobs)]
    for part, ((lanes, on), rows, keys) in zip(parts, jobs):
        attn[rows, lanes] = attn[rows, lanes] + to_low(part)


def text_heads_forward(h, query, key, value, attn, bias, mask):
    jobs = chains(h, VIDEOS, 4)
    scores = [linear(query[rows, lanes] * to_low(on), key[lanes, keys]) for (lanes, on), rows, keys in jobs]
    probs = split_rows(to_low(soft(jnp.concatenate(scores), bias, mask)), jobs)
    parts = [nt(prob, value[lanes, keys]) * on for prob, ((lanes, on), rows, keys) in zip(probs, jobs)]
    for part, ((lanes, on), rows, keys) in zip(parts, jobs):
        attn[rows, lanes] = attn[rows, lanes] + to_low(part)


HALVES = [(slice(0, 128), slice(0, 128)), (slice(128, 256), slice(128, 256))]
VIDEOS = [(slice(0, 144), slice(0, 128)), (slice(112, 256), slice(128, 256))]


def regroup(back):
    row = lax.broadcasted_iota(jnp.int32, (ROWS, ROWS), 0)
    col = lax.broadcasted_iota(jnp.int32, (ROWS, ROWS), 1)
    if back:
        source = (((row >> 3) & 1) << 7) + ((row >> 4) << 3) + (row & 7)
    else:
        source = (((row >> 3) & 15) << 4) + ((row >> 7) << 3) + (row & 7)
    return to_low((source == col).astype(jnp.float32))


def temporal_bias(seg_in, seg_row):
    row = lax.broadcasted_iota(jnp.int32, (128, 128), 0)
    col = lax.broadcasted_iota(jnp.int32, (128, 128), 1)
    allowed = ((row & 7) == (col & 7)) & (seg_in[2, 0:128, 0:1] == seg_row[0:1, 0:128])
    return jnp.where(allowed, 0.0, MASKED)


def cross_bias():
    col = lax.broadcasted_iota(jnp.int32, (1, 128), 1)
    return jnp.where(col < L, 0.0, MASKED)


def cross_rows(seg_in, heads=2):
    both = [1.0 - seg_in[0, 0:144, 0:1], seg_in[0, 112:256, 0:1]]
    return jnp.concatenate(both * heads)


def move_lanes(to, value, from_start, to_start, width):
    left = min(from_start // 128 * 128, value.shape[1] - 256)
    right = min(to_start // 128 * 128, width - 256)
    off = to_start - right
    part = pltpu.roll(value[:, left : left + 256], (off - (from_start - left)) % 256, 1)
    lane = lax.broadcasted_iota(jnp.int32, part.shape, 1)
    lanes = slice(right, right + 256)
    to[:, lanes] = jnp.where((lane >= off) & (lane < off + SHARD), part, to[:, lanes])


def hidden_places():
    places = []
    for d in range(32):
        xp, cp, zp, yp = d // 16, d // 8 % 2, d // 2 % 4, d % 2
        for k in range(4):
            places.append((k, (4 * d + k) * SHARD, (((cp * 2 + xp) * 2 + yp) * 4 + zp) * SHARD))
    return places


def blk_peers(x, c, b):
    return [device(x, c, (b + k) % 2, ((b + k) % 8) // 2) for k in range(1, 8)]


def forward_kernel(
    spatial_in, spatial_out, temporal_in, temporal_out, cross_query, cross_out, hidden_in, hidden_out,
    tok, gain_one, cond, ada_bias, seg_in, seg_row, cot_i, turn_i, ada_i, caption_i, proj_i,
    wide, out, left_o, qkvs_o, qkvt_o, qc_o, mem_o, xhat_o, rstd_o, branch_o, slope_o, gfour_o, cot_o, mods_o, gate_o, gain_o,
    win, pair, far, lines, weights, tokp, cotp, tokf, xin, xp, left, qkvs, qkvt, qc, mem, text, mod, mods, xhat, rstd, branch, branchw, bias,
    stream, attnf, attnp, post, slope, gfour, gains, gain_at, gate,
    src, cot, turn, ada, caption, proj, mod_in, text_in, hidden,
    z_send, z_recv, l_send, l_recv, own_sem, w_sem, t_send, t_recv, a_send, a_recv, m_send, m_recv, x_send, x_recv,
    g_send, g_recv, save_sem, in_sem,
):
    x, c, y, z, x1, y1, x2, y2 = place()
    b = z * 2 + y
    near = [device(x, c, y, (z + k) % 4) for k in (1, 2, 3)]
    beside, across = device(x, c, y, z + 1 - 2 * (z % 2)), device(x, c, y, 3 - z)
    middle = (z == 1) | (z == 2)
    first, second, twin = device(x1, c, y1, z), device(x2, c, y2, z), device(x, 1 - c, y, z)
    peers = blk_peers(x, c, b)
    greet(peers + [device(1 - x, c, y, z), twin])
    mine, line3 = line_of(c, x, y), line_of(c, 1 - x, 1 - y)

    def hops(t, core):
        turn_round = core + (1 - core) * (t % 4 == 2)
        xa, ya = x + (1 - 2 * x) * (1 - turn_round), y + (1 - 2 * y) * turn_round
        xb, yb = x + (1 - 2 * x) * turn_round, y + (1 - 2 * y) * (1 - turn_round)
        return (xa, ya), (xb, yb)

    def z_one(t):
        return remote(src.at[t], win.at[t % PARTS], z_send.at[t, 0], z_recv.at[t, 0], beside)

    def z_two(t):
        return remote(pair.at[t % PARTS], far.at[t % PARTS], z_send.at[t, 1], z_recv.at[t, 1], across)

    def z_three(t):
        return remote(far.at[t % PARTS], far.at[t % PARTS], z_send.at[t, 2], z_recv.at[t, 2], beside)

    def wide_line(t, line):
        return wide.at[t, pl.ds(pl.multiple_of(line * LINE, 16), LINE)]

    def own(t):
        return pltpu.make_async_copy(lines.at[t % HELD], wide_line(t, mine), own_sem.at[t])

    def line_copy(t, to, line, index, where):
        return remote(to, wide_line(t, line), l_send.at[t, index], l_recv.at[t, index], where)

    def sends(t, index):
        (xa, ya), (xb, yb) = hops(t, c)
        one, two = device(xa, c, ya, z), device(xb, c, yb, z)
        line1, line2 = line_of(c, xa, ya), line_of(c, xb, yb)
        line, where = (
            (mine, one), (mine, two), (mine, twin), (line1, two),
            (line1, twin), (line2, twin), (line3, twin),
        )[index]
        from_here = lines.at[t % HELD] if index < 3 else wide_line(t, line)
        return line_copy(t, from_here, line, index, where)

    def arrives(t, line, index):
        line_copy(t, wide_line(t, line), line, index, first).wait_recv()

    def tick(t):
        @pl.when((t >= 4) & (t < BLOCKS + 4))
        def _():
            now = t - 4

            @pl.when(middle)
            def _():
                z_two(now).wait_send()
                z_three(now).wait_send()

            @pl.when(jnp.logical_not(middle))
            def _():
                z_three(now).wait_recv()

            @pl.when(now >= HELD)
            def _():
                for index in range(3):
                    sends(now - HELD, index).wait_send()
                own(now - HELD).wait()

            def line_from(low, high):
                at = now % HELD
                lines[at, 0:64] = low[0:64]
                lines[at, 64:80] = low[64:80] + high[0:16]
                lines[at, 80:144] = high[16:80]

            @pl.when(z < 2)
            def _():
                line_from(pair[now % PARTS], far[now % PARTS])

            @pl.when(z >= 2)
            def _():
                line_from(far[now % PARTS], pair[now % PARTS])

            for index in range(3):
                sends(now, index).start()
            own(now).start()

        @pl.when((t >= 2) & (t < BLOCKS + 2) & middle)
        def _():
            z_two(t - 2).wait_recv()
            z_three(t - 2).start()

        @pl.when((t >= 1) & (t < BLOCKS + 1))
        def _():
            now = t - 1
            z_one(now).wait_recv()

            def pair_from(even, odd):
                at = now % PARTS
                pair[at, 0:32] = even[0:32]
                pair[at, 32:48] = even[32:48] + odd[0:16]
                pair[at, 48:80] = odd[16:48]

            @pl.when(z % 2 == 0)
            def _():
                pair_from(src[now], win[now % PARTS])

            @pl.when(z % 2 == 1)
            def _():
                pair_from(win[now % PARTS], src[now])

            @pl.when(middle)
            def _():
                z_two(now).start()

        @pl.when(t < BLOCKS)
        def _():
            z_one(t).start()

        @pl.when((t >= 6) & (t < BLOCKS + 6))
        def _():
            now = t - 6
            xa, ya = hops(now, c)[0]
            arrives(now, line_of(c, xa, ya), 0)
            for index in (3, 4):
                sends(now, index).start()

        @pl.when(t >= LAST)
        def _():
            now = t - LAST
            xb, yb = hops(now, c)[1]
            arrives(now, line_of(c, xb, yb), 1)
            sends(now, 5).start()
            arrives(now, line3, 3)
            sends(now, 6).start()

    done = [0]

    def pump(until):
        until = min(until, BLOCKS + LAST)
        if until > done[0]:
            start = done[0]
            loop(until - start, lambda i: tick(i + start))
            done[0] = until

    def poke():
        pump(done[0] + 1)

    def weight_copy(block):
        return pltpu.make_async_copy(wide.at[block], weights.at[block % 2], w_sem.at[block % 2])

    loaded = set()

    def begin(block):
        if block in loaded:
            return
        loaded.add(block)
        pump(block + LAST + 1)
        near_at, far_at = hops(block, 1 - c)
        places = [(x, y), near_at, far_at, (1 - x, 1 - y)]
        for (xl, yl), index in zip(places, (2, 4, 5, 6)):
            arrives(block, line_of(1 - c, xl, yl), index)
        if block >= BLOCKS - HELD:
            own(block).wait()
        weight_copy(block).start()

    def load(block):
        begin(block)
        weight_copy(block).wait()
        if 3 <= block < BLOCKS - 1:
            begin(block + 1)

    def times(values, block, emit):
        def tile(cols):
            emit(cols, linear(values[...], weights[block % 2, :, cols]))

        each_cols(tile)

    saves = []
    held = {}

    def save(from_ref, to_ref, name=None):
        if name is None:
            name = len(saves)
            saves.append(name)
        held[name] = pltpu.make_async_copy(from_ref, to_ref, save_sem.at[name])
        held[name].start()

    def settle(name):
        if name in held:
            held.pop(name).wait()

    def turned(values, index):
        slot = index % 2
        settle(LEFT_SEM + slot)

        def tile(cols):
            low = to_low(nt(values[...], turn[cols, :]))
            xp[:, cols] = low
            transposed(identity(TILE), low, left.at[slot], cols.start)

        each_cols(tile)
        save(left.at[slot], left_o.at[index], LEFT_SEM + slot)

    fetches = [
        pltpu.make_async_copy(from_ref, to_ref, in_sem.at[at])
        for at, (from_ref, to_ref) in enumerate(
            ((ada_i, ada), (turn_i, turn), (cot_i, cot), (caption_i, caption), (proj_i, proj))
        )
    ]
    for copy in fetches:
        copy.start()

    def shift(rows, first):
        row = lax.broadcasted_iota(jnp.int32, (WINDOW, rows), 0) - 4 * z
        col = lax.broadcasted_iota(jnp.int32, (WINDOW, rows), 1)
        return to_low(((row >= 0) & (row < SHARD) & (row + first == col)).astype(jnp.float32))

    def window(at, values):
        src[at] = to_low(linear(shift(SHARD, 0), values))

    for j in range(3):
        window(j, spatial_in[:, WIDE * j : WIDE * j + WIDE])
    pump(2)
    window(3, spatial_out[...])
    for j in range(3):
        window(4 + j, temporal_in[:, WIDE * j : WIDE * j + WIDE])
    window(7, temporal_out[...])
    window(8, cross_query[...])
    window(9, cross_out[...])
    pump(4)

    def m_copy(k, at):
        return remote(mod_in, mod.at[at], m_send.at[k - 1], m_recv.at[k - 1], peers[k - 1])

    fetches[0].wait()
    part = wide32(to_low(nt(cond[...], ada[...]) + wide32(ada_bias[...])))[0:8]
    part = jnp.concatenate([part, jnp.zeros((8, MOD_WIN - MOD // 8), jnp.float32)], axis=1)
    part = pltpu.roll(part, 16 * b, 1)
    tiles = [part[row : row + 1, 128 * tile : 128 * tile + 128] for row in range(2) for tile in range(MOD_TILES)]
    mod_in[...] = to_low(jnp.concatenate(tiles + [jnp.zeros((32 - 2 * MOD_TILES, 128), jnp.float32)]))
    for k in range(1, 8):
        m_copy(k, b).start()
    mod[b] = mod_in[...]
    swap = swap_rows()
    tokp[...] = to_low(linear(swap, tok[...]))

    def t_copy(k):
        to = (b + k) % 8
        part = tokp.at[pl.ds(pl.multiple_of(32 * to, 32), 32)]
        return remote(part, tokf.at[b], t_send.at[k - 1], t_recv.at[k - 1], peers[k - 1])

    def t_wait(k):
        of = (b + 8 - k) % 8
        remote(tokp.at[pl.ds(0, 32)], tokf.at[of], t_send.at[k - 1], t_recv.at[k - 1], peers[k - 1]).wait_recv()

    pump(5)
    for k in range(1, 8):
        t_copy(k).start()
    tokf[b] = tokp[pl.ds(pl.multiple_of(32 * b, 32), 32)]

    def g_copy(at, from_at, to):
        return remote(gains.at[from_at], gain_at.at[at], g_send.at[at], g_recv.at[at], to)

    spread = jnp.concatenate([wide32(gain_one[...]), jnp.zeros((8, WIDE - SHARD), jnp.float32)], axis=1)
    gains[0] = pltpu.roll(spread, SHARD * ((x * 2 + c) * 8 + b), 1)
    g_copy(0, 0, twin).start()
    pump(6)
    fetches[2].wait()
    cotp[...] = to_low(linear(swap, cot[...]))
    save(cotp, cot_o)

    def x_copy(k, at):
        return remote(text_in, text.at[at, y], x_send.at[k - 1], x_recv.at[k - 1], near[k - 1])

    def x_over(at):
        return remote(text.at[:, at], text.at[:, at], x_send.at[3], x_recv.at[3], device(x, c, 1 - y, z))

    for k in range(1, 8):
        m_copy(k, (b + 8 - k) % 8).wait_recv()
    mods[...] = jnp.zeros_like(mods)
    for k in range(8):
        part = wide32(mod[k])
        for row in range(2):
            for tile in range(MOD_TILES):
                lanes = slice(1280 * k + 128 * tile, 1280 * k + 128 * tile + 128)
                at = row * MOD_TILES + tile
                mods[row : row + 1, lanes] = mods[row : row + 1, lanes] + part[at : at + 1]
    save(mods, mods_o)
    g_copy(0, 0, twin).wait_recv()
    gains[1] = gains[0] + gain_at[0]
    g_copy(1, 1, first).start()
    pump(7)
    fetches[3].wait()
    fetches[4].wait()
    text_in[...] = jnp.zeros_like(text_in)
    for v in range(2):
        text_in[:, 128 * v : 128 * v + L] = to_low(nt(proj[...], caption[v]))
    for k in (1, 2, 3):
        x_copy(k, z).start()
    text[z, y] = text_in[...]
    pump(8)
    hidden[...] = jnp.zeros_like(hidden)
    for k, natural, placed in hidden_places():
        start = natural // WIDE * WIDE
        move_lanes(hidden.at[k], wide32(hidden_in[:, start : start + WIDE]), natural - start, placed, WIDE)
    for k in range(4):
        window(10 + 2 * k, to_low(hidden[k]))
        src[11 + 2 * k] = to_low(linear(shift(4 * SHARD, SHARD * k), hidden_out[...]))
    fetches[1].wait()

    def pick(piece, seg):
        lanes = slice(WIDE * piece, WIDE * piece + WIDE)
        return jnp.where(seg > 0.5, mods[1:2, lanes], mods[0:1, lanes])

    def normal(values, rows, index):
        center = values - jnp.mean(values, axis=-1, keepdims=True)
        factor = lax.rsqrt(jnp.mean(center * center, axis=-1, keepdims=True) + EPSILON)
        scaled = center * factor
        xhat[index, rows, :] = to_low(scaled)
        rstd[index, rows, :] = jnp.broadcast_to(factor, (factor.shape[0], 128))
        return scaled

    for k in range(1, 8):
        t_wait(k)
    g_copy(1, 1, first).wait_recv()
    gains[2] = gains[1] + gain_at[1]
    g_copy(2, 2, second).start()

    def spatial_rows(i):
        seg = jnp.concatenate([seg_in[1, 0:16, 0:1], seg_in[1, 128:144, 0:1]])
        values = wide32(tokf[i])
        center = values - jnp.mean(values, axis=-1, keepdims=True)
        factor = lax.rsqrt(jnp.mean(center * center, axis=-1, keepdims=True) + EPSILON)
        scaled = center * factor
        ready = to_low(scaled * (1.0 + pick(1, seg)) + pick(0, seg))
        low = to_low(scaled)
        spread = jnp.broadcast_to(factor, (32, 128))
        for f in range(2):
            rows = pl.ds(pl.multiple_of(128 * f + 16 * i, 16), 16)
            part = slice(16 * f, 16 * f + 16)
            xhat[0, rows, :] = low[part]
            rstd[0, rows, :] = spread[part]
            xin[rows, :] = ready[part]

    loop(8, spatial_rows)
    save(xhat.at[0], xhat_o.at[0])
    save(rstd.at[0], rstd_o.at[0])
    turned(xin, 10)
    for j in range(3):
        load(j)

        def emit(cols, value, j=j):
            qkvs[j, :, cols] = to_low(value)

        times(xp, j, emit)
    save(qkvs, qkvs_o)
    g_copy(2, 2, second).wait_recv()
    gains[3] = gains[2] + gain_at[2]
    for k in (1, 2, 3):
        remote(gains.at[3], gain_at.at[2 + k], g_send.at[2 + k], g_recv.at[2 + k], near[k - 1]).start()
    for k in (1, 2, 3):
        x_copy(k, (z + 4 - k) % 4).wait_recv()
    x_over(y).start()
    attnf[...] = jnp.zeros_like(attnf)

    def spatial_heads(h):
        heads_forward(h, qkvs.at[0], qkvs.at[1], qkvs.at[2], attnf, HALVES, None, None)

    loop(2, spatial_heads)
    poke()
    loop(2, lambda h: spatial_heads(h + 2))
    for k in (1, 2, 3):
        remote(gains.at[3], gain_at.at[2 + k], g_send.at[2 + k], g_recv.at[2 + k], near[k - 1]).wait_recv()
    gains[0 + 4] = gains[3] + gain_at[3] + gain_at[4] + gain_at[5]
    save(gains.at[4], gain_o)

    def a_copy(k, f):
        to = (b + k) % 8
        part = attnf.at[pl.ds(pl.multiple_of(128 * f + 16 * to, 16), 16)]
        return remote(part, attnp.at[2 * b + f], a_send.at[k - 1, f], a_recv.at[k - 1, f], peers[k - 1])

    def a_wait(k, f):
        of = (b + 8 - k) % 8
        part = attnf.at[pl.ds(0, 16)]
        remote(part, attnp.at[2 * of + f], a_send.at[k - 1, f], a_recv.at[k - 1, f], peers[k - 1]).wait_recv()

    for k in range(1, 8):
        for f in range(2):
            a_copy(k, f).start()
    for f in range(2):
        attnp[2 * b + f] = attnf[pl.ds(pl.multiple_of(128 * f + 16 * b, 16), 16)]
    pump(done[0] + 2)
    for k in range(1, 8):
        for f in range(2):
            a_wait(k, f)
    xin[...] = attnp[...].reshape(ROWS, WIDE)
    turned(xin, 9)
    load(3)

    def emit_branch(cols, value):
        branchw[:, cols] = value

    times(xp, 3, emit_branch)

    def after_spatial(rows):
        seg = seg_in[0, rows, 0:1]
        value = branchw[rows, :]
        branch[0, rows, :] = to_low(value)
        value = wide32(tokp[rows, :]) + pick(2, seg) * value
        stream[rows, :] = value
        xin[rows, :] = to_low(normal(value, rows, 1) * (1.0 + pick(4, seg)) + pick(3, seg))

    each_rows(64, after_spatial)
    save(branch.at[0], branch_o.at[0])
    save(xhat.at[1], xhat_o.at[1])
    save(rstd.at[1], rstd_o.at[1])

    for k in range(1, 8):
        for f in range(2):
            a_copy(k, f).wait_send()
    attnf[...] = to_low(linear(regroup(False), xin[...]))
    turned(attnf, 8)
    for j in range(3):
        load(4 + j)

        def emit(cols, value, j=j):
            qkvt[j, :, cols] = to_low(value)

        times(xp, 4 + j, emit)
    save(qkvt, qkvt_o)
    attnf[...] = jnp.zeros_like(attnf)

    bias[...] = temporal_bias(seg_in, seg_row)

    def temporal_heads(h):
        heads_forward(
            h, qkvt.at[0], qkvt.at[1], qkvt.at[2], attnf, HALVES, jnp.concatenate([bias[...]] * 8), None
        )

    loop(2, temporal_heads)
    poke()
    loop(2, lambda h: temporal_heads(h + 2))
    xin[...] = to_low(linear(regroup(True), attnf[...]))
    turned(xin, 7)
    load(7)
    times(xp, 7, emit_branch)

    def after_temporal(rows):
        seg = seg_in[0, rows, 0:1]
        value = branchw[rows, :]
        branch[1, rows, :] = to_low(value)
        value = stream[rows, :] + pick(5, seg) * value
        stream[rows, :] = value
        xin[rows, :] = to_low(normal(value, rows, 2) * gains[4, 0:1, :])

    each_rows(64, after_temporal)
    save(branch.at[1], branch_o.at[1])
    save(xhat.at[2], xhat_o.at[2])
    save(rstd.at[2], rstd_o.at[2])

    turned(xin, 6)
    load(8)

    def emit_query(cols, value):
        qc[:, cols] = to_low(value)

    times(xp, 8, emit_query)
    save(qc, qc_o)
    x_over(1 - y).wait_recv()
    for k in range(8):
        mem[k // 4, TEXT * (k % 4) : TEXT * (k % 4) + TEXT, :] = text[k // 2, k % 2]
    save(mem, mem_o)
    attnf[...] = jnp.zeros_like(attnf)

    def cross_heads(h):
        text_heads_forward(h, qc, mem.at[0], mem.at[1], attnf, cross_bias(), cross_rows(seg_in, 4))

    loop(2, cross_heads)
    poke()
    loop(2, lambda h: cross_heads(h + 2))
    xin[...] = attnf[...]
    turned(xin, 5)
    load(9)
    times(xp, 9, emit_branch)

    def after_cross(rows):
        seg = seg_in[0, rows, 0:1]
        value = stream[rows, :] + branchw[rows, :]
        stream[rows, :] = value
        xin[rows, :] = to_low(normal(value, rows, 3) * (1.0 + pick(7, seg)) + pick(6, seg))
        gfour[rows, :] = to_low(wide32(cotp[rows, :]) * pick(8, seg))

    each_rows(64, after_cross)
    save(xhat.at[3], xhat_o.at[3])
    save(rstd.at[3], rstd_o.at[3])
    save(gfour, gfour_o)

    turned(xin, 4)
    for k in range(4):
        slot = k % 2
        load(10 + 2 * k)
        settle(SLOPE_SEM + slot)
        settle(LEFT_SEM + slot)

        def emit_hidden(cols, value, slot=slot):
            inner = math.sqrt(2.0 / math.pi) * (value + 0.044715 * value * value * value)
            bent = jnp.tanh(inner)
            half = 0.5 * (1.0 + bent)
            tilt = math.sqrt(2.0 / math.pi) * (1.0 + 3 * 0.044715 * value * value)
            slope[slot, :, cols] = to_low(half + 0.5 * value * (1.0 - bent * bent) * tilt)
            low = to_low(value * half)
            post[:, cols] = low
            transposed(identity(TILE), low, left.at[slot], cols.start)

        times(xp, 10 + 2 * k, emit_hidden)
        save(slope.at[slot], slope_o.at[k], SLOPE_SEM + slot)
        save(left.at[slot], left_o.at[k], LEFT_SEM + slot)
        load(11 + 2 * k)

        def emit_out(cols, value, k=k):
            branchw[:, cols] = value if k == 0 else branchw[:, cols] + value

        times(post, 11 + 2 * k, emit_out)

    gate[...] = jnp.zeros_like(gate)

    def last(rows):
        seg = seg_in[0, rows, 0:1]
        value = branchw[rows, :]
        xin[rows, :] = to_low(stream[rows, :] + pick(8, seg) * value)
        value = wide32(cotp[rows, :]) * value
        later = jnp.sum(value * seg, axis=0, keepdims=True)
        every = jnp.sum(value, axis=0, keepdims=True)
        gate[0:1, :] = gate[0:1, :] + (every - later)
        gate[1:2, :] = gate[1:2, :] + later

    each_rows(64, last)
    save(gate, gate_o)
    out[...] = to_low(linear(swap_rows(), xin[...]))

    for copy in held.values():
        copy.wait()
    for k in range(1, 8):
        t_copy(k).wait_send()
        m_copy(k, b).wait_send()
    for k in (1, 2, 3):
        x_copy(k, z).wait_send()
    x_over(y).wait_send()
    for at, to in ((0, twin), (1, first), (2, second)):
        g_copy(at, at, to).wait_send()
    for k in (1, 2, 3):
        remote(gains.at[3], gain_at.at[2 + k], g_send.at[2 + k], g_recv.at[2 + k], near[k - 1]).wait_send()

    for t in range(BLOCKS - HELD, BLOCKS):
        for index in range(3):
            sends(t, index).wait_send()

    def finish(t):
        z_one(t).wait_send()
        for index in range(3, 7):
            sends(t, index).wait_send()

    loop(BLOCKS, finish)


ANY = pl.BlockSpec(memory_space=pl.ANY)
IN_VMEM = pl.BlockSpec(memory_space=pltpu.VMEM)


def forward(*operands):
    low, full = jnp.bfloat16, jnp.float32
    dma = pltpu.SemaphoreType.DMA
    hbm = [
        ((BLOCKS, WIDE, WIDE), low),
        ((ROWS, WIDE), low),
        ((11, WIDE, ROWS), low),
        ((3, ROWS, WIDE), low),
        ((3, ROWS, WIDE), low),
        ((ROWS, WIDE), low),
        ((2, WIDE, KEYS), low),
        ((4, ROWS, WIDE), low),
        ((4, ROWS, 128), full),
        ((2, ROWS, WIDE), low),
        ((4, ROWS, WIDE), low),
        ((ROWS, WIDE), low),
        ((ROWS, WIDE), low),
        ((8, MOD), full),
        ((8, WIDE), full),
        ((8, WIDE), full),
    ]
    vmem = [
        ((PARTS, WINDOW, WIDE), low),
        ((PARTS, PAIR, WIDE), low),
        ((PARTS, PAIR, WIDE), low),
        ((HELD, LINE, WIDE), low),
        ((2, WIDE, WIDE), low),
        ((ROWS, WIDE), low),
        ((ROWS, WIDE), low),
        ((8, 32, WIDE), low),
        ((ROWS, WIDE), low),
        ((ROWS, WIDE), low),
        ((2, WIDE, ROWS), low),
        ((3, ROWS, WIDE), low),
        ((3, ROWS, WIDE), low),
        ((ROWS, WIDE), low),
        ((2, WIDE, KEYS), low),
        ((4, 2, TEXT, KEYS), low),
        ((8, 32, 128), low),
        ((8, MOD), full),
        ((4, ROWS, WIDE), low),
        ((4, ROWS, 128), full),
        ((2, ROWS, WIDE), low),
        ((ROWS, WIDE), full),
        ((128, 128), full),
        ((ROWS, WIDE), full),
        ((ROWS, WIDE), low),
        ((16, 16, WIDE), low),
        ((ROWS, WIDE), low),
        ((2, ROWS, WIDE), low),
        ((ROWS, WIDE), low),
        ((5, 8, WIDE), full),
        ((6, 8, WIDE), full),
        ((8, WIDE), full),
        ((BLOCKS, WINDOW, WIDE), low),
        ((ROWS, WIDE), low),
        ((WIDE, WIDE), low),
        ((MOD // 8, WIDE), low),
        ((2, L, 4096), low),
        ((TEXT, 4096), low),
        ((32, 128), low),
        ((TEXT, KEYS), low),
        ((4, SHARD, WIDE), full),
    ]
    return pl.pallas_call(
        forward_kernel,
        out_shape=[jax.ShapeDtypeStruct(*shape) for shape in hbm],
        in_specs=[IN_VMEM] * 14 + [ANY] * 5,
        out_specs=[ANY, IN_VMEM] + [ANY] * 14,
        scratch_shapes=[pltpu.VMEM(*shape) for shape in vmem]
        + [
            dma((BLOCKS, 3)), dma((BLOCKS, 3)), dma((BLOCKS, 7)), dma((BLOCKS, 7)), dma((BLOCKS,)), dma((2,)),
            dma((7,)), dma((7,)), dma((7, 2)), dma((7, 2)), dma((7,)), dma((7,)), dma((4,)), dma((4,)),
            dma((6,)), dma((6,)), dma((SAVE_SEMS,)), dma((5,)),
        ],
        compiler_params=pltpu.CompilerParams(
            collective_id=0, has_side_effects=True, vmem_limit_bytes=60 * MIB
        ),
        name="forward",
    )(*operands)


def tn(left, right):
    return lax.dot_general(
        left, right, (((0,), (0,)), ((), ())), preferred_element_type=jnp.float32
    )


def text_heads_backward(h, query, key, value, grad, dquery, dkey, dvalue, bias, mask):
    jobs = chains(h, VIDEOS)
    scores, grads = [], []
    for (lanes, on), rows, keys in jobs:
        low_on = to_low(on)
        scores.append(linear(query[rows, lanes] * low_on, key[lanes, keys]))
        grads.append(linear(grad[rows, lanes] * low_on, value[lanes, keys]))
    probs = soft(jnp.concatenate(scores), bias, mask)
    grad_probs = jnp.concatenate(grads)
    delta = jnp.sum(grad_probs * probs, axis=-1, keepdims=True)
    slopes = split_rows(to_low(probs * (grad_probs - delta)), jobs)
    probs = split_rows(to_low(probs), jobs)
    parts = []
    for slope, prob, ((lanes, on), rows, keys) in zip(slopes, probs, jobs):
        low_on = to_low(on)
        parts.append(
            (
                to_low(nt(slope, key[lanes, keys]) * (on * SCALE)),
                to_low(tn(query[rows, lanes] * low_on, slope) * SCALE),
                to_low(tn(grad[rows, lanes] * low_on, prob)),
            )
        )
    for (by_query, by_key, by_value), ((lanes, on), rows, keys) in zip(parts, jobs):
        dquery[rows, lanes] = dquery[rows, lanes] + by_query
        dkey[lanes, keys] = dkey[lanes, keys] + by_key
        dvalue[lanes, keys] = dvalue[lanes, keys] + by_value


def heads_backward(h, query, key, value, grad, dquery, dkey, dvalue, groups, bias, mask):
    jobs = chains(h, groups)
    scores, grads = [], []
    for (lanes, on), rows, keys in jobs:
        low_on = to_low(on)
        scores.append(nt(query[rows, lanes] * low_on, key[keys, lanes]))
        grads.append(nt(grad[rows, lanes] * low_on, value[keys, lanes]))
    probs = soft(jnp.concatenate(scores), bias, mask)
    grad_probs = jnp.concatenate(grads)
    delta = jnp.sum(grad_probs * probs, axis=-1, keepdims=True)
    slopes = split_rows(to_low(probs * (grad_probs - delta)), jobs)
    probs = split_rows(to_low(probs), jobs)
    parts = []
    for slope, prob, ((lanes, on), rows, keys) in zip(slopes, probs, jobs):
        parts.append(
            (
                to_low(linear(slope, key[keys, lanes]) * (on * SCALE)),
                to_low(tn(slope, query[rows, lanes]) * (on * SCALE)),
                to_low(tn(prob, grad[rows, lanes]) * on),
            )
        )
    for (by_query, by_key, by_value), ((lanes, on), rows, keys) in zip(parts, jobs):
        dquery[rows, lanes] = dquery[rows, lanes] + by_query
        dkey[keys, lanes] = dkey[keys, lanes] + by_key
        dvalue[keys, lanes] = dvalue[keys, lanes] + by_value


def backward_kernel(
    wide, left_i, qkvs_i, qkvt_i, qc_i, mem_i, xhat_i, rstd_i, branch_i, slope_i, gfour_i, cot_i, mods_i, gate_i, gain_i,
    caption_i, seg_in, seg_row, turn, cond_in,
    total, gtok, gain_o, caption_o, mod_o,
    weights, left, right, qkv, xhat, rstd, branch, slope, mods, gain, bias, stream, work, grad, xin, gm, mem, dmem, text, text_at, text_sum, cap, cap_out, cap_in, cap_own, cap_at, mod_out, mod,
    seqs, gains, gain_at, gframe, back,
    s0, r0, s1, r1, s2, r2, k2, s3, pass_in, pass_out, far_in, close, close_in, share,
    in_sem, w_sem, s0_sem, r0_sem, s1_sem, r1_sem, s2_sem, r2_sem, z_send, z_recv, share_sem,
    a_send, a_recv, u_send, u_recv, x_send, x_recv, m_send, m_recv, q_send, q_recv, g_send, g_recv,
    cap_sem, c_send, c_recv, left_sem,
):
    x, c, y, z, x1, y1, x2, y2 = place()
    b = z * 2 + y
    near = [device(x, c, y, (z + k) % 4) for k in (1, 2, 3)]
    first, second, twin = device(x1, c, y1, z), device(x2, c, y2, z), device(x, 1 - c, y, z)
    peers = blk_peers(x, c, b)
    across = [twin, device(1 - x, c, y, z), device(1 - x, 1 - c, y, z)]
    greet(peers + across)

    fetches = {}

    def fetch(name, from_ref, to_ref):
        fetches[name] = pltpu.make_async_copy(from_ref, to_ref, in_sem.at[name])
        fetches[name].start()

    def have(name):
        if name in fetches:
            fetches.pop(name).wait()

    fetch(0, gfour_i, right.at[0])
    for k in range(4):
        fetch(1 + k, left_i.at[k], left.at[k])
    fetch(12, mods_i, mods)
    fetch(13, gain_i, gain)
    fetch(14, slope_i.at[0], slope.at[0])
    fetch(15, slope_i.at[1], slope.at[1])
    fetch(16, xhat_i.at[3], xhat.at[1])
    fetch(17, rstd_i.at[3], rstd.at[1])
    fetch(18, cot_i, xin)
    fetch(19, gate_i, work.at[0:8])

    def weight(block):
        slot = WEIGHT_ORDER.index(block) % 2
        return weights.at[slot]

    def prefetch(at):
        if at < len(WEIGHT_ORDER):
            copy = pltpu.make_async_copy(wide.at[WEIGHT_ORDER[at]], weights.at[at % 2], w_sem.at[at % 2])
            copy.start()
            fetches["w", WEIGHT_ORDER[at]] = copy

    def release(block):
        prefetch(WEIGHT_ORDER.index(block) + 2)

    prefetch(0)
    prefetch(1)

    away = [(1 - x) * 2 + 1 - y, x2 * 2 + y2]
    stay = [x1 * 2 + y1, x * 2 + y]

    def product(t, core, xl):
        rows = pl.ds(pl.multiple_of(line_of(core, xl, 0) * LINE, 16), 2 * LINE)
        return linear(left[left_at(t) % 4, rows, :], right[right_at(t)])

    def left_copy(t):
        return pltpu.make_async_copy(left_i.at[left_at(t)], left.at[left_at(t) % 4], left_sem.at[0])

    def left_next(t):
        return (t >= 4) & (t < BLOCKS) & (left_at(t) != left_at(t - 1))

    def copy0(t, l):
        pair = pl.ds(2 * l, 2)
        return remote(s0.at[t % 2, pair], r0.at[t % 4, pair], s0_sem.at[t % 2, l], r0_sem.at[t % 4, l], twin)

    def copy1(t, l):
        return remote(s1.at[t % 2, away[l]], r1.at[t % 4, l], s1_sem.at[t % 2, l], r1_sem.at[t % 4, l], second)

    def copy2(t):
        return remote(s2.at[t % 2], r2.at[t % 4], s2_sem.at[t % 2], r2_sem.at[t % 4], first)

    beside, opposite = device(x, c, y, z + 1 - 2 * (z % 2)), device(x, c, y, 3 - z)
    middle = (z == 1) | (z == 2)
    near_rows = pl.ds(pl.multiple_of(64 * (z // 2), 16), PAIR)
    far_rows = pl.ds(pl.multiple_of(64 - 64 * (z // 2), 16), PAIR)
    own_rows = pl.ds(pl.multiple_of(32 * (z % 2), 16), WINDOW)
    beside_rows = pl.ds(pl.multiple_of(32 - 32 * (z % 2), 16), WINDOW)

    def z_one(t):
        return remote(s3.at[t % 4, far_rows], pass_in.at[t % 4], z_send.at[0, t % 4], z_recv.at[0, t % 4], beside)

    def z_two(t):
        return remote(pass_out.at[t % 2], far_in.at[t % 4], z_send.at[1, t % 4], z_recv.at[1, t % 4], opposite)

    def z_three(t):
        return remote(
            close.at[t % 2, beside_rows], close_in.at[t % 4], z_send.at[2, t % 4], z_recv.at[2, t % 4], beside
        )

    def share_copy(t):
        return pltpu.make_async_copy(share.at[t % 2], total.at[t], share_sem.at[t % 2])

    def tick(t):
        @pl.when(t >= 10)
        def _():
            now = t - 10
            z_three(now).wait_recv()
            value = wide32(close[now % 2, own_rows]) + wide32(close_in[now % 4])

            @pl.when(jnp.logical_not(middle))
            def _():
                z_one(now).wait_send()

            @pl.when(now >= 2)
            def _():
                share_copy(now - 2).wait()
            share[now % 2] = value
            share_copy(now).start()

        @pl.when((t >= 8) & (t < BLOCKS + 8))
        def _():
            now = t - 8

            @pl.when(now >= 2)
            def _():
                z_three(now - 2).wait_send()

            @pl.when(middle)
            def _():
                z_two(now).wait_recv()
                close[now % 2] = to_low(wide32(s3[now % 4, near_rows]) + wide32(far_in[now % 4]))

            @pl.when(jnp.logical_not(middle))
            def _():
                close[now % 2] = s3[now % 4, near_rows]

            z_three(now).start()

        @pl.when((t >= 7) & (t < BLOCKS + 7) & middle)
        def _():
            now = t - 7
            z_one(now).wait_recv()

            @pl.when(now >= 2)
            def _():
                z_two(now - 2).wait_send()
            pass_out[now % 2] = to_low(wide32(s3[now % 4, far_rows]) + wide32(pass_in[now % 4]))
            z_two(now).start()

        @pl.when((t >= 6) & (t < BLOCKS + 6))
        def _():
            now = t - 6
            copy2(now).wait_recv()
            s3[now % 4] = to_low(k2[now % 2] + wide32(r2[now % 4]))

            @pl.when(jnp.logical_not(middle))
            def _():
                z_one(now).start()

        @pl.when((t >= 4) & (t < BLOCKS + 4))
        def _():
            now = t - 4
            copy1(now, 0).wait_recv()

            @pl.when(now >= 2)
            def _():
                copy2(now - 2).wait_send()
            s2[now % 2] = to_low(wide32(s1[now % 2, stay[0]]) + wide32(r1[now % 4, 0]))
            copy2(now).start()
            copy1(now, 1).wait_recv()
            k2[now % 2] = wide32(s1[now % 2, stay[1]]) + wide32(r1[now % 4, 1])

        @pl.when((t >= 2) & (t < BLOCKS + 2))
        def _():
            now = t - 2

            @pl.when(now >= 2)
            def _():
                for l in range(2):
                    copy1(now - 2, l).wait_send()
            for l in range(2):
                copy0(now, l).wait_recv()
                value = product(now, c, l)
                for part in range(2):
                    line = 2 * l + part
                    summed = value[part * LINE : part * LINE + LINE] + wide32(r0[now % 4, line])
                    s1[now % 2, line] = to_low(summed)
            for l in range(2):
                copy1(now, l).start()

        @pl.when(left_next(t))
        def _():
            left_copy(t).wait()

        @pl.when(t < BLOCKS)
        def _():
            for l in range(2):
                @pl.when(t >= 2)
                def _():
                    copy0(t - 2, l).wait_send()
                value = to_low(product(t, 1 - c, l))
                s0[t % 2, 2 * l] = value[:LINE]
                s0[t % 2, 2 * l + 1] = value[LINE:]
                copy0(t, l).start()

        @pl.when(left_next(t + 1))
        def _():
            left_copy(t + 1).start()

    done = [0]

    def pump(until):
        if until > done[0]:
            start = done[0]
            loop(until - start, lambda i: tick(i + start))
            done[0] = until

    def pick(piece, seg):
        lanes = slice(WIDE * piece, WIDE * piece + WIDE)
        return jnp.where(seg > 0.5, mods[1:2, lanes], mods[0:1, lanes])

    def by_video(piece, value, seg):
        lanes = slice(WIDE * piece, WIDE * piece + WIDE)
        later = jnp.sum(value * seg, axis=0, keepdims=True)
        every = jnp.sum(value, axis=0, keepdims=True)
        gm[0:1, lanes] = gm[0:1, lanes] + (every - later)
        gm[1:2, lanes] = gm[1:2, lanes] + later

    def through(values_at, blocks, emit, grouped=False):
        for n, (values, block) in enumerate(zip(values_at, blocks)):
            have(("w", block))

            def tile(cols, n=n, values=values, block=block):
                part = nt(values[...], weight(block)[cols, :])
                if n > 0:
                    part = part + work[:, cols]
                if n == len(blocks) - 1:
                    xin[:, cols] = to_low(part)
                else:
                    work[:, cols] = part

            each_cols(tile)
            release(block)
        if grouped:
            xin[...] = to_low(linear(regroup(True), xin[...]))
        turn_back(emit)

    def turn_back(emit):
        each_cols(lambda cols: emit(cols, linear(xin[...], turn[:, cols])))

    def emit_work(cols, value):
        work[:, cols] = value

    def emit_grad(cols, value):
        grad[:, cols] = to_low(value)

    def norm_back(grad_in, tilt, at, rows):
        slope_in = grad_in * tilt
        hat = wide32(xhat[at, rows, :])
        first_mean = jnp.mean(slope_in, axis=-1, keepdims=True)
        second_mean = jnp.mean(slope_in * hat, axis=-1, keepdims=True)
        return rstd[at, rows, 0:1] * (slope_in - first_mean - hat * second_mean)

    gm[...] = jnp.zeros_like(gm)
    have(0)
    have(12)
    have(18)
    have(19)
    gm[0:8, 8 * WIDE : 9 * WIDE] = work[0:8]
    stream[...] = wide32(xin[...])
    for k in range(4):
        have(1 + k)
    pump(2)
    for k in range(4):
        have(14 + k % 2 if k < 2 else ("slope", k))
        have(("w", 11 + 2 * k))

        def tile(cols, k=k):
            value = nt(right[0], weight(11 + 2 * k)[cols, :]) * wide32(slope[k % 2, :, cols])
            right[1 + k, :, cols] = to_low(value)

        each_cols(tile)
        release(11 + 2 * k)
        if k < 2:
            copy = pltpu.make_async_copy(slope_i.at[k + 2], slope.at[k % 2], in_sem.at[14 + k])
            copy.start()
            fetches["slope", k + 2] = copy
        have(("w", 10 + 2 * k))

        def tile(cols, k=k):
            part = nt(right[1 + k], weight(10 + 2 * k)[cols, :])
            if k > 0:
                part = part + work[:, cols]
            if k < 3:
                work[:, cols] = part
            else:
                xin[:, cols] = to_low(part)

        each_cols(tile)
        release(10 + 2 * k)
        pump(k + 3)
    turn_back(emit_work)
    have(16)
    have(17)
    fetch(20, qc_i, qkv.at[0])
    fetch(21, mem_i.at[0], mem.at[0])
    fetch(22, mem_i.at[1], mem.at[1])
    fetch(23, xhat_i.at[2], xhat.at[0])
    fetch(24, rstd_i.at[2], rstd.at[0])

    def after_mlp(rows):
        seg = seg_in[0, rows, 0:1]
        value = work[rows, :]
        by_video(6, value, seg)
        by_video(7, value * wide32(xhat[1, rows, :]), seg)
        value = stream[rows, :] + norm_back(value, 1.0 + pick(7, seg), 1, rows)
        stream[rows, :] = value
        right[5, rows, :] = to_low(value)

    each_rows(32, after_mlp)

    fetch(25, xhat_i.at[1], xhat.at[1])
    fetch(26, rstd_i.at[1], rstd.at[1])
    through([right.at[5]], [9], emit_grad)
    right[6] = jnp.zeros_like(right[6])
    dmem[...] = jnp.zeros_like(dmem)
    for name in (13, 20, 21, 22, 23, 24):
        have(name)

    def cross_heads(h):
        text_heads_backward(
            h, qkv.at[0], mem.at[0], mem.at[1], grad, right.at[6], dmem.at[0], dmem.at[1],
            cross_bias(), cross_rows(seg_in),
        )

    for part in range(4):
        loop(2, lambda h: cross_heads(h + 2 * part))
        pump(7 + (part + 1) // 2)

    def dmem_part(zp, yp):
        return dmem.at[zp // 2, pl.ds(pl.multiple_of(TEXT * (zp % 2 * 2 + yp), 16), TEXT)]

    def x_over(zp):
        return remote(dmem_part(zp, 1 - y), text.at[zp], x_send.at[zp], x_recv.at[zp], device(x, c, 1 - y, z))

    def x_copy(k):
        return remote(text.at[(z + k) % 4], text_at.at[k - 1], x_send.at[3 + k], x_recv.at[3 + k], near[k - 1])

    for zp in range(4):
        x_over(zp).start()
    fetch(27, qkvt_i.at[0], qkv.at[0])
    fetch(28, qkvt_i.at[1], qkv.at[1])
    fetch(29, qkvt_i.at[2], qkv.at[2])
    fetch(30, branch_i.at[1], branch)
    through([right.at[6]], [8], emit_work)
    gains[0] = jnp.zeros_like(gains[0])
    have(30)

    def after_cross(rows):
        seg = seg_in[0, rows, 0:1]
        value = work[rows, :]
        gains[0, 0:1, :] = gains[0, 0:1, :] + jnp.sum(value * wide32(xhat[0, rows, :]), axis=0, keepdims=True)
        value = stream[rows, :] + norm_back(value, gain[0:1, :], 0, rows)
        stream[rows, :] = value
        by_video(5, value * wide32(branch[rows, :]), seg)
        right[7, rows, :] = to_low(value * pick(5, seg))

    each_rows(32, after_cross)

    def g_copy(at, to):
        return remote(gains.at[min(at, 3)], gain_at.at[at], g_send.at[at], g_recv.at[at], to)

    g_copy(0, twin).start()
    fetch(31, branch_i.at[0], branch)
    fetch(32, xhat_i.at[0], xhat.at[0])
    fetch(33, rstd_i.at[0], rstd.at[0])
    pump(10)

    through([right.at[7]], [7], emit_grad)
    grad[...] = to_low(linear(regroup(False), grad[...]))
    bias[...] = temporal_bias(seg_in, seg_row)
    for j in range(3):
        right[8 + j] = jnp.zeros_like(right[8 + j])
    for name in (25, 26, 27, 28, 29):
        have(name)

    def temporal_heads(h):
        heads_backward(
            h, qkv.at[0], qkv.at[1], qkv.at[2], grad, right.at[8], right.at[9], right.at[10],
            HALVES, jnp.concatenate([bias[...]] * 4), None,
        )

    loop(4, temporal_heads)
    pump(11)
    g_copy(0, twin).wait_recv()
    gains[1] = gains[0] + gain_at[0]
    g_copy(1, first).start()
    loop(4, lambda h: temporal_heads(h + 4))
    pump(12)
    g_copy(1, first).wait_recv()
    gains[2] = gains[1] + gain_at[1]
    g_copy(2, second).start()
    for zp in range(4):
        x_over(zp).wait_recv()
        text[zp] = to_low(wide32(dmem_part(zp, y)[...]) + wide32(text[zp]))
    for k in (1, 2, 3):
        x_copy(k).start()
    for j in range(3):
        fetch(34 + j, qkvs_i.at[j], qkv.at[j])
    through([right.at[8], right.at[9], right.at[10]], [4, 5, 6], emit_work, True)
    have(31)

    def after_temporal(rows):
        seg = seg_in[0, rows, 0:1]
        value = work[rows, :]
        by_video(3, value, seg)
        by_video(4, value * wide32(xhat[1, rows, :]), seg)
        value = stream[rows, :] + norm_back(value, 1.0 + pick(4, seg), 1, rows)
        stream[rows, :] = value
        by_video(2, value * wide32(branch[rows, :]), seg)
        right[1, rows, :] = to_low(value * pick(2, seg))

    each_rows(32, after_temporal)

    through([right.at[1]], [3], emit_grad)

    def a_copy(k):
        to = (b + k) % 8
        part = grad.at[pl.ds(pl.multiple_of(32 * to, 32), 32)]
        return remote(part, back.at[b], a_send.at[k - 1], a_recv.at[k - 1], peers[k - 1])

    def a_wait(k):
        of = (b + 8 - k) % 8
        remote(grad.at[pl.ds(0, 32)], back.at[of], a_send.at[k - 1], a_recv.at[k - 1], peers[k - 1]).wait_recv()

    for k in range(1, 8):
        a_copy(k).start()
    pump(13)
    for k in (1, 2, 3):
        x_copy(k).wait_recv()
    text_sum[...] = to_low(wide32(text[z]) + wide32(text_at[0]) + wide32(text_at[1]) + wide32(text_at[2]))

    def cap_fetch(n):
        quarter = [1 - c, 3 - c, c, 2 + c][n]
        lanes = pl.ds(pl.multiple_of(QUARTER * quarter, 128), QUARTER)
        return pltpu.make_async_copy(caption_i.at[:, :, lanes], cap.at[n % 2], cap_sem.at[n % 2])

    over_x = across[1]
    quarters = [x * 2 + c, (1 - x) * 2 + c, x * 2 + 1 - c, (1 - x) * 2 + 1 - c]

    def c_copy(n):
        from_ref, to_ref, to = (
            (cap_out.at[0], cap_in.at[0], twin),
            (cap_out.at[1], cap_in.at[1], twin),
            (cap_own.at[1 - x], cap_at, over_x),
            (cap_own.at[x], caption_o.at[quarters[0]], over_x),
            (cap_own.at[x], caption_o.at[quarters[0]], twin),
            (caption_o.at[quarters[1]], caption_o.at[quarters[1]], twin),
        )[n]
        return remote(from_ref, to_ref, c_send.at[n], c_recv.at[n], to)

    cap_fetch(0).start()
    cap_fetch(1).start()
    for n in range(4):
        cap_fetch(n).wait()
        part = linear(text_sum[:, 0:L], cap[n % 2, 0]) + linear(text_sum[:, 128 : 128 + L], cap[n % 2, 1])
        if n < 2:
            cap_out[n] = to_low(part)
            c_copy(n).start()
            cap_fetch(n + 2).start()
        else:
            cap_own[n - 2] = to_low(part)
    back[b] = grad[pl.ds(pl.multiple_of(32 * b, 32), 32)]
    pump(14)
    g_copy(2, second).wait_recv()
    gains[3] = gains[2] + gain_at[2]
    for k in (1, 2, 3):
        g_copy(2 + k, near[k - 1]).start()
    for j in range(3):
        right[2 + j] = jnp.zeros_like(right[2 + j])
    for name in (32, 33, 34, 35, 36):
        have(name)
    for k in range(1, 8):
        a_wait(k)
    for k in range(8):
        for f in range(2):
            gframe[128 * f + 16 * k : 128 * f + 16 * k + 16, :] = back[k, 16 * f : 16 * f + 16, :]

    def spatial_heads(h):
        heads_backward(
            h, qkv.at[0], qkv.at[1], qkv.at[2], gframe, right.at[2], right.at[3], right.at[4], HALVES, None, None
        )

    loop(4, spatial_heads)
    pump(15)
    for n in range(2):
        c_copy(n).wait_recv()
        cap_own[n] = to_low(wide32(cap_own[n]) + wide32(cap_in[n]))
    c_copy(2).start()
    loop(4, lambda h: spatial_heads(h + 4))
    pump(16)
    through([right.at[2], right.at[3], right.at[4]], [0, 1, 2], emit_work)
    pump(17)
    for k in range(1, 8):
        a_copy(k).wait_send()

    def after_spatial(i):
        rows = pl.ds(pl.multiple_of(16 * i, 16), 16)
        seg = seg_in[1, rows, 0:1]
        value = work[rows, :]
        by_video(0, value, seg)
        by_video(1, value * wide32(xhat[0, rows, :]), seg)
        value = to_low(norm_back(value, 1.0 + pick(1, seg), 0, rows))
        back[i % 8, pl.ds(pl.multiple_of(16 * (i // 8), 16), 16), :] = value

    loop(16, after_spatial)

    def branch_part(of):
        return branch.at[pl.ds(pl.multiple_of(32 * of, 32), 32)]

    def u_copy(k):
        to = (b + k) % 8
        return remote(back.at[to], branch_part(b), u_send.at[k - 1], u_recv.at[k - 1], peers[k - 1])

    def u_wait(k):
        of = (b + 8 - k) % 8
        remote(back.at[0], branch_part(of), u_send.at[k - 1], u_recv.at[k - 1], peers[k - 1]).wait_recv()

    def m_copy(k):
        to = (b + k) % 8
        return remote(mod_out.at[to], mod.at[b], m_send.at[k - 1], m_recv.at[k - 1], peers[k - 1])

    def m_wait(k):
        of = (b + 8 - k) % 8
        remote(mod_out.at[0], mod.at[of], m_send.at[k - 1], m_recv.at[k - 1], peers[k - 1]).wait_recv()

    for k in range(1, 8):
        u_copy(k).start()
    branch[pl.ds(pl.multiple_of(32 * b, 32), 32), :] = back[b]
    for k in range(8):
        tiles = [
            gm[row : row + 1, 1280 * k + 128 * tile : 1280 * k + 128 * tile + 128]
            for row in range(2)
            for tile in range(MOD_TILES)
        ]
        mod_out[k] = to_low(jnp.concatenate(tiles + [jnp.zeros((32 - 2 * MOD_TILES, 128), jnp.float32)]))
    for k in range(1, 8):
        m_copy(k).start()
    mod[b] = mod_out[b]
    pump(18)
    c_copy(2).wait_recv()
    cap_own[x] = to_low(wide32(cap_own[x]) + wide32(cap_at[...]))
    c_copy(3).start()
    c_copy(4).start()
    keep_quarter = pltpu.make_async_copy(cap_own.at[x], caption_o.at[quarters[0]], cap_sem.at[0])
    keep_quarter.start()
    pump(20)
    for k in range(1, 8):
        m_wait(k)
    summed = wide32(mod[0])
    for k in range(1, 8):
        summed = summed + wide32(mod[k])
    own = x * 2 + c
    seqs[own, 0:32] = to_low(summed)
    seqs[own, 32:64] = cond_in[...]
    places = [x * 2 + 1 - c, (1 - x) * 2 + c, (1 - x) * 2 + 1 - c]

    def q_copy(k, at):
        return remote(seqs.at[own], seqs.at[at], q_send.at[k], q_recv.at[k], across[k])

    for k in range(3):
        q_copy(k, own).start()
    pump(22)
    for k in range(1, 8):
        u_wait(k)
    xin[...] = to_low(stream[...] + wide32(branch[...]))
    gtok[...] = to_low(linear(swap_rows(), xin[...]))
    for k in (1, 2, 3):
        g_copy(2 + k, near[k - 1]).wait_recv()
    gain_o[...] = gains[3] + gain_at[3] + gain_at[4] + gain_at[5]
    pump(24)
    c_copy(3).wait_recv()
    c_copy(5).start()
    pump(BLOCKS + 10)
    c_copy(4).wait_recv()
    c_copy(5).wait_recv()
    for n in range(6):
        c_copy(n).wait_send()
    keep_quarter.wait()
    for k in range(3):
        q_copy(k, places[k]).wait_recv()
    mod_o[...] = seqs[...]

    for now in (BLOCKS - 2, BLOCKS - 1):
        for l in range(2):
            copy0(now, l).wait_send()
            copy1(now, l).wait_send()
        copy2(now).wait_send()
        z_three(now).wait_send()
        share_copy(now).wait()

        @pl.when(middle)
        def _(now=now):
            z_two(now).wait_send()

    for k in range(1, 8):
        u_copy(k).wait_send()
        m_copy(k).wait_send()
        x_over(k - 1).wait_send() if k < 5 else x_copy(k - 4).wait_send()
    for k in range(3):
        q_copy(k, own).wait_send()
    for at, to in enumerate([twin, first, second] + near):
        g_copy(at, to).wait_send()


QUARTER = 1024
WEIGHT_ORDER = (11, 10, 13, 12, 15, 14, 17, 16, 9, 8, 7, 4, 5, 6, 3, 0, 1, 2)


def backward(*operands):
    low, full = jnp.bfloat16, jnp.float32
    dma = pltpu.SemaphoreType.DMA
    outs = [
        ((BLOCKS, WINDOW, WIDE), full),
        ((ROWS, WIDE), low),
        ((8, WIDE), full),
        ((4, TEXT, QUARTER), low),
        ((4, 64, 128), low),
    ]
    vmem = [
        ((2, WIDE, WIDE), low),
        ((4, WIDE, ROWS), low),
        ((11, ROWS, WIDE), low),
        ((3, ROWS, WIDE), low),
        ((2, ROWS, WIDE), low),
        ((2, ROWS, 128), full),
        ((ROWS, WIDE), low),
        ((2, ROWS, WIDE), low),
        ((8, MOD), full),
        ((8, WIDE), full),
        ((128, 128), full),
        ((ROWS, WIDE), full),
        ((ROWS, WIDE), full),
        ((ROWS, WIDE), low),
        ((ROWS, WIDE), low),
        ((8, MOD), full),
        ((2, WIDE, KEYS), low),
        ((2, WIDE, KEYS), low),
        ((4, TEXT, KEYS), low),
        ((3, TEXT, KEYS), low),
        ((TEXT, KEYS), low),
        ((2, 2, L, QUARTER), low),
        ((2, TEXT, QUARTER), low),
        ((2, TEXT, QUARTER), low),
        ((2, TEXT, QUARTER), low),
        ((TEXT, QUARTER), low),
        ((8, 32, 128), low),
        ((8, 32, 128), low),
        ((4, 64, 128), low),
        ((4, 8, WIDE), full),
        ((6, 8, WIDE), full),
        ((ROWS, WIDE), low),
        ((8, 32, WIDE), low),
        ((2, 4, LINE, WIDE), low),
        ((4, 4, LINE, WIDE), low),
        ((2, 4, LINE, WIDE), low),
        ((4, 2, LINE, WIDE), low),
        ((2, LINE, WIDE), low),
        ((4, LINE, WIDE), low),
        ((2, LINE, WIDE), full),
        ((4, LINE, WIDE), low),
        ((4, PAIR, WIDE), low),
        ((2, PAIR, WIDE), low),
        ((4, PAIR, WIDE), low),
        ((2, PAIR, WIDE), low),
        ((4, WINDOW, WIDE), low),
        ((2, WINDOW, WIDE), full),
    ]
    return pl.pallas_call(
        backward_kernel,
        out_shape=[jax.ShapeDtypeStruct(*shape) for shape in outs],
        in_specs=[ANY] * 16 + [IN_VMEM] * 4,
        out_specs=[ANY] + [IN_VMEM] * 2 + [ANY, IN_VMEM],
        scratch_shapes=[pltpu.VMEM(*shape) for shape in vmem]
        + [
            dma((40,)), dma((2,)), dma((2, 4)), dma((4, 4)), dma((2, 2)), dma((4, 2)), dma((2,)), dma((4,)),
            dma((3, 4)), dma((3, 4)), dma((2,)), dma((7,)), dma((7,)), dma((7,)), dma((7,)), dma((7,)), dma((7,)),
            dma((7,)), dma((7,)), dma((3,)), dma((3,)), dma((6,)), dma((6,)), dma((2,)), dma((6,)), dma((6,)), dma((1,)),
        ],
        compiler_params=pltpu.CompilerParams(
            collective_id=1, has_side_effects=True, vmem_limit_bytes=63 * MIB
        ),
        name="backward",
    )(*operands)


def finish_kernel(
    spread, caption_in, mod_in, gain_in,
    ada_o, bias_o, spatial_o, spatial_out_o, temporal_o, temporal_out_o, gain_o, query_o, caption_o, cross_o, hidden_o,
    hidden_out_o,
):
    seq, blk = lax.axis_index("seq"), lax.axis_index("blk")

    def share(t):
        return pltpu.roll(spread[t], (WINDOW - 4 * (blk // 2)) % WINDOW, 0)[0:SHARD]

    for j in range(3):
        lanes = slice(WIDE * j, WIDE * j + WIDE)
        spatial_o[:, lanes] = share(15 + j)
        temporal_o[:, lanes] = share(11 + j)
    spatial_out_o[...] = share(14)
    temporal_out_o[...] = share(10)
    query_o[...] = share(9)
    cross_o[...] = share(8)
    hidden = [share(4 + k) for k in range(4)]
    hidden_o[...] = jnp.zeros_like(hidden_o)
    for k, natural, placed in hidden_places():
        move_lanes(hidden_o, hidden[k], placed, natural, 4 * WIDE)
    for k in range(4):
        hidden_out_o[SHARD * k : SHARD * k + SHARD, :] = share(k)
    gain_o[...] = pltpu.roll(gain_in[...], (WIDE - SHARD * (seq * 8 + blk)) % WIDE, 1)[0:1, 0:SHARD]
    for q in range(4):
        caption_o[:, QUARTER * q : QUARTER * q + QUARTER] = wide32(caption_in[q])
    part = MOD // 8
    mods, conds = [], []
    for pack in range(4):
        rows = wide32(mod_in[pack])
        for video in range(2):
            first = MOD_TILES * video
            mods.append(jnp.concatenate([rows[first + i : first + i + 1] for i in range(MOD_TILES)], axis=1))
            first = 32 + WIDE // 128 * video
            conds.append(jnp.concatenate([rows[first + i : first + i + 1] for i in range(WIDE // 128)], axis=1))
    mods = pltpu.roll(jnp.concatenate(mods), (MOD_WIN - 16 * blk) % MOD_WIN, 1)[:, :part]
    bias_o[...] = jnp.sum(mods, axis=0, keepdims=True)
    ada_o[...] = tn(to_low(mods), to_low(jnp.concatenate(conds)))


def finish(spread, caption, mod, gain):
    full = jnp.float32
    outs = [
        (MOD // 8, WIDE), (1, MOD // 8), (SHARD, 3 * WIDE), (SHARD, WIDE), (SHARD, 3 * WIDE), (SHARD, WIDE),
        (1, SHARD), (SHARD, WIDE), (TEXT, 4 * QUARTER), (SHARD, WIDE), (SHARD, 4 * WIDE), (4 * SHARD, WIDE),
    ]
    return pl.pallas_call(
        finish_kernel,
        out_shape=[jax.ShapeDtypeStruct(shape, full) for shape in outs],
        in_specs=[IN_VMEM] * 4,
        out_specs=[IN_VMEM] * len(outs),
        compiler_params=pltpu.CompilerParams(vmem_limit_bytes=60 * MIB),
        name="finish",
    )(spread, caption, mod, gain)


TURN = np.arange(WIDE)[None, :] == (
    np.arange(WIDE).reshape(2, 2, 4, 2, SHARD).transpose(1, 0, 3, 2, 4).reshape(-1)
)[:, None]


def shards(
    tokens,
    segments,
    timesteps,
    caption,
    cotangent,
    ada_weight,
    ada_bias,
    spatial_in,
    spatial_out,
    temporal_in,
    temporal_out,
    cross_gain,
    cross_query,
    caption_proj,
    cross_out,
    hidden_in,
    hidden_out,
):
    frame_seg = segments[0]
    blk = lax.axis_index("blk")
    conditioning = to_low(jax.nn.silu(time_embedding(timesteps[0], WIDE)))
    cond_in = jnp.pad(conditioning.reshape(2 * WIDE // 128, 128), ((0, 32 - 2 * WIDE // 128), (0, 0)))
    frames = frame_seg.astype(jnp.float32)
    own_frames = lax.dynamic_slice(frames, (2 * blk,), (2,))
    seg_in = jnp.broadcast_to(
        jnp.stack(
            [jnp.repeat(frames, 16), jnp.repeat(own_frames, 128), jnp.tile(jnp.repeat(frames, 8), 2)]
        )[:, :, None],
        (3, ROWS, 128),
    )
    seg_row = jnp.broadcast_to(jnp.repeat(frames, 8)[None], (8, 128))
    turn = jnp.asarray(TURN, jnp.bfloat16)
    wide, out, *kept = forward(
        spatial_in,
        spatial_out,
        temporal_in,
        temporal_out,
        cross_query,
        cross_out,
        hidden_in,
        hidden_out,
        tokens.reshape(ROWS, WIDE),
        jnp.pad(cross_gain[None], ((0, 7), (0, 0))),
        jnp.pad(conditioning, ((0, 14), (0, 0))),
        ada_bias[None],
        seg_in,
        seg_row,
        cotangent.reshape(ROWS, WIDE),
        turn,
        ada_weight.T,
        caption[0],
        caption_proj.T,
    )
    spread, grad_tokens, grad_gain, grad_text, grad_mod = backward(
        wide, *kept, caption[0], seg_in, seg_row, turn, cond_in
    )
    (
        grad_ada,
        grad_bias,
        grad_sin,
        grad_sout,
        grad_tin,
        grad_tout,
        grad_gain,
        grad_query,
        grad_caption,
        grad_cout,
        grad_hin,
        grad_hout,
    ) = finish(spread, grad_text, grad_mod, grad_gain)
    return (
        out.reshape(tokens.shape),
        grad_tokens.reshape(tokens.shape),
        grad_ada.T,
        grad_bias[0],
        grad_sin,
        grad_sout,
        grad_tin,
        grad_tout,
        grad_gain[0],
        grad_query,
        grad_caption.T,
        grad_cout,
        grad_hin,
        grad_hout,
    )


def solution(mesh):
    fast = dict(mesh.shape) == {"seq": 4, "blk": 8}
    return jax.shard_map(
        shards if fast else general_shards,
        mesh=mesh,
        in_specs=(
            P("seq", "blk", None, None),
            P("seq", None),
            P("seq", None),
            P("seq", None, None, None),
            P("seq", "blk", None, None),
            P(None, "blk"),
            P("blk"),
            P(("seq", "blk"), None),
            P(("seq", "blk"), None),
            P(("seq", "blk"), None),
            P(("seq", "blk"), None),
            P(("seq", "blk")),
            P(("seq", "blk"), None),
            P(None, "blk"),
            P(("seq", "blk"), None),
            P(("seq", "blk"), None),
            P(("seq", "blk"), None),
        ),
        out_specs=(
            P("seq", "blk", None, None),
            P("seq", "blk", None, None),
            P(None, "blk"),
            P("blk"),
            P(("seq", "blk"), None),
            P(("seq", "blk"), None),
            P(("seq", "blk"), None),
            P(("seq", "blk"), None),
            P(("seq", "blk")),
            P(("seq", "blk"), None),
            P(None, "blk"),
            P(("seq", "blk"), None),
            P(("seq", "blk"), None),
            P(("seq", "blk"), None),
        ),
        check_vma=False,
    )
```
